32 devices in a mesh: section: 2 (over core), fsdp: 16 (over z, y, x).
Axes of the slice: x: 2, y: 2, z: 4, core: 2. Of those that a mesh axis runs over, the one named last changes fastest.
Arguments:
- images: bfloat16 [2, 96, 197, 384], P(None, 'fsdp'), may hold values from -6 to 6
- cotangent: bfloat16 [2, 96, 197, 384], P(None, 'fsdp'), may hold values from -6 to 6
- counts: int32 [2, 16], P(None, 'fsdp'), may hold values from 1 to 6, 72 in all within a row
- ln1_gain: bfloat16 [2, 384], P('section', 'fsdp'), may hold values from 0.099609375 to 1.8984375
- ln1_bias: bfloat16 [2, 384], P('section', 'fsdp'), may hold values from -1.75 to 1.75
- w_qkv: bfloat16 [2, 384, 1152], P('section', 'fsdp'), may hold values from -0.4375 to 0.4375
- b_qv: bfloat16 [2, 768], P('section', 'fsdp'), may hold values from -3 to 3
- w_out: bfloat16 [2, 384, 384], P('section', 'fsdp'), may hold values from -0.875 to 0.875
- b_out: bfloat16 [2, 384], P('section', 'fsdp'), may hold values from -3 to 3
- ln2_gain: bfloat16 [2, 384], P('section', 'fsdp'), may hold values from 0.099609375 to 1.8984375
- ln2_bias: bfloat16 [2, 384], P('section', 'fsdp'), may hold values from -1.75 to 1.75
- w_up: bfloat16 [2, 384, 1536], P('section', 'fsdp'), may hold values from -0.3125 to 0.3125
- b_up: bfloat16 [2, 1536], P('section', 'fsdp'), may hold values from -3 to 3
- w_down: bfloat16 [2, 1536, 384], P('section', 'fsdp'), may hold values from -0.15625 to 0.15625
- b_down: bfloat16 [2, 384], P('section', 'fsdp'), may hold values from -3 to 3
Outputs:
- acts: bfloat16 [2, 2, 96, 197, 384], P('section', None, 'fsdp')
- in_grads: bfloat16 [2, 2, 96, 197, 384], P('section', None, 'fsdp')
- grad_ln1_gain: float32 [2, 384], P('section', 'fsdp')
- grad_ln1_bias: float32 [2, 384], P('section', 'fsdp')
- grad_w_qkv: float32 [2, 384, 1152], P('section', 'fsdp')
- grad_b_qv: float32 [2, 768], P('section', 'fsdp')
- grad_w_out: float32 [2, 384, 384], P('section', 'fsdp')
- grad_b_out: float32 [2, 384], P('section', 'fsdp')
- grad_ln2_gain: float32 [2, 384], P('section', 'fsdp')
- grad_ln2_bias: float32 [2, 384], P('section', 'fsdp')
- grad_w_up: float32 [2, 384, 1536], P('section', 'fsdp')
- grad_b_up: float32 [2, 1536], P('section', 'fsdp')
- grad_w_down: float32 [2, 1536, 384], P('section', 'fsdp')
- grad_b_down: float32 [2, 384], P('section', 'fsdp')
The draws below stay inside these ranges and needn't reach their ends.
Inputs may be any that keep to these rules, and one draw needn't show every extreme that they name: counts[m, d] of the 6 image slots of fsdp index d in micro-batch m hold images, the first ones; each micro-batch holds 72 images, and in each some index holds 6.
All inputs are finite; a program needn't handle non-finite values. No bound on the sum of `counts` on one device may be relied on, other than what follows from the above.
Results may differ from the reference program's by a relative error of at most 0.02.
The reference program's roundings to bfloat16 on the way count: a program that leaves them out, or rounds other values in their place, can miss the bound.
Values may be sent and summed in bfloat16 or wider, within the bound.
A program may use at most 256 MiB of HBM per device.

```python
import math
import jax
import jax.numpy as jnp
import numpy as np
from jax import lax

D = 384
H = 6
HD = 64
FF = 1536
SEQ = 197
MB = 2
SLOTS = 6
IMAGES = 96
IMAGES_MB = 72
N_FSDP = 16


def block_scale(key, dims, cuts, least, largest):
    level = 1.0
    for position, shards_of in cuts:
        draws = jax.random.uniform(jax.random.fold_in(jax.random.fold_in(key, 6), position), (shards_of,), jnp.float32, least / len(cuts), largest / len(cuts))
        level = level * jnp.repeat(jnp.exp(draws), dims[position] // shards_of).reshape((-1,) + (1,) * (len(dims) - 1 - position))
    return level


def split_up(number_of, total, bound, lean):
    portions = [(1 << 20) // math.isqrt(standing ** lean) + 1 for standing in range(2, number_of + 1)]
    surplus, given = total - bound - (number_of - 1), [1] * (number_of - 1)
    while surplus > 0:
        movable = [i for i in range(number_of - 1) if given[i] < bound]
        pool, budget = sum([portions[i] for i in movable]), surplus
        for i in movable:
            more = min(bound - given[i], max(1, budget * portions[i] // pool), surplus)
            given[i] = given[i] + more
            surplus = surplus - more
    return np.array([bound] + given)


def uneven_parts(stream_key, count, total, most, skew):
    if count == 2:
        one = jax.random.randint(stream_key, (), max(1, total - most), min(most, total - 1) + 1)
        return jnp.stack([one, total - one])
    sizes = jnp.asarray(split_up(count, total, most, skew), jnp.int32)
    couples = (count - 1) // 2
    source_of, sink = sizes[1:1 + 2 * couples:2], sizes[2:2 + 2 * couples:2]
    margin = jnp.minimum(source_of - 1, most - sink)
    passed = jax.random.randint(jax.random.fold_in(stream_key, 1), (couples,), 0, 1 << 20) % (margin + 1)
    sizes = sizes.at[1:1 + 2 * couples:2].set(source_of - passed).at[2:2 + 2 * couples:2].set(sink + passed)
    return sizes[jax.random.permutation(jax.random.fold_in(stream_key, 2), count)]


def bell_draw(rng, extent, scale, limit, cuts=(), kind=jnp.bfloat16):
    drawn = scale * jax.random.normal(rng, extent, jnp.float32)
    if cuts:
        drawn = drawn * block_scale(rng, extent, cuts, -0.22, 0.18)
    return jnp.clip(drawn, -limit, limit).astype(kind)


def setup_inputs(seed: int = 0) -> dict:
    seeds = jax.random.split(jax.random.key(seed), 16)
    images = bell_draw(seeds[0], (MB, IMAGES, SEQ, D), 1.0, 6.0, ((1, 16),))
    cotangent = bell_draw(seeds[1], (MB, IMAGES, SEQ, D), 1.0, 6.0, ((1, 16),))
    counts = jax.vmap(lambda own: uneven_parts(own, N_FSDP, IMAGES_MB, SLOTS, 0))(jax.random.split(seeds[2], MB)).reshape((MB, N_FSDP)).astype(jnp.int32)
    ln1_gain = jnp.clip(1.0 + 0.18 * jax.random.normal(seeds[3], (2, D), jnp.float32), 0.099609375, 1.8984375).astype(jnp.bfloat16)
    ln1_bias = bell_draw(seeds[4], (2, D), 0.3, 1.75, ((0, 2), (1, 16)))
    w_qkv = bell_draw(seeds[5], (2, D, 3 * D), (D // 2) ** -0.5, 0.4375, ((0, 2), (1, 16)))
    b_qv = bell_draw(seeds[6], (2, 2 * D), 0.5, 3.0, ((0, 2), (1, 16)))
    w_out = bell_draw(seeds[7], (2, D, D), (D // 8) ** -0.5, 0.875, ((0, 2), (1, 16)))
    b_out = bell_draw(seeds[8], (2, D), 0.5, 3.0, ((0, 2), (1, 16)))
    ln2_gain = jnp.clip(1.0 + 0.18 * jax.random.normal(seeds[9], (2, D), jnp.float32), 0.099609375, 1.8984375).astype(jnp.bfloat16)
    ln2_bias = bell_draw(seeds[10], (2, D), 0.3, 1.75, ((0, 2), (1, 16)))
    w_up = bell_draw(seeds[11], (2, D, FF), D ** -0.5, 0.3125, ((0, 2), (1, 16)))
    b_up = bell_draw(seeds[12], (2, FF), 0.5, 3.0, ((0, 2), (1, 16)))
    w_down = bell_draw(seeds[13], (2, FF, D), FF ** -0.5, 0.15625, ((0, 2), (1, 16)))
    b_down = bell_draw(seeds[14], (2, D), 0.5, 3.0, ((0, 2), (1, 16)))
    return {"images": images, "cotangent": cotangent, "counts": counts, "ln1_gain": ln1_gain, "ln1_bias": ln1_bias, "w_qkv": w_qkv, "b_qv": b_qv, "w_out": w_out, "b_out": b_out, "ln2_gain": ln2_gain, "ln2_bias": ln2_bias, "w_up": w_up, "b_up": b_up, "w_down": w_down, "b_down": b_down}


@jax.custom_vjp
def low(v):
    return lax.optimization_barrier(v.astype(jnp.bfloat16)).astype(jnp.float32)

@jax.custom_vjp
def low_back(v):
    return v

def low_keep(v):
    return (low(v), None)

def low_pass(kept, grad):
    return (grad,)

def back_keep(v):
    return (v, None)

def back_low(kept, grad):
    return (low(grad),)
low.defvjp(low_keep, low_pass)
low_back.defvjp(back_keep, back_low)
EPS = 1e-06
HIGH = lax.Precision.HIGHEST

def layer_norm(values, gain, shift):
    center = values - lax.optimization_barrier(jnp.mean(values, axis=-1, keepdims=True))
    spread = lax.optimization_barrier(jnp.mean(center * center, axis=-1, keepdims=True))
    return center * lax.rsqrt(spread + EPS) * gain + shift

def encoder_block(params, group):
    gain_one, shift_one, w_qkv, b_qv, w_out, b_out, gain_two, shift_two, w_up, b_up, w_down, b_down = params
    normed = low(layer_norm(group, gain_one, shift_one))
    mixed = jnp.einsum('sqd,de->sqe', normed, w_qkv, precision=HIGH)
    query = low(low_back(mixed[..., :D] + b_qv[:D])).reshape(SLOTS, SEQ, H, HD)
    keys = low(low_back(mixed[..., D:2 * D])).reshape(SLOTS, SEQ, H, HD)
    values = low(low_back(mixed[..., 2 * D:] + b_qv[D:])).reshape(SLOTS, SEQ, H, HD)
    scores = low_back(jnp.einsum('sqhd,skhd->shqk', query, keys, precision=HIGH))
    probs = low(jax.nn.softmax(scores * HD ** (-0.5), axis=-1))
    context = jnp.einsum('shqk,skhd->sqhd', probs, values, precision=HIGH).reshape(SLOTS, SEQ, D)
    context = low(low_back(context))
    after = group + low_back(jnp.einsum('sqd,de->sqe', context, w_out, precision=HIGH) + b_out)
    normed_two = low(layer_norm(after, gain_two, shift_two))
    pre = low_back(jnp.einsum('sqd,de->sqe', normed_two, w_up, precision=HIGH) + b_up)
    hidden = low(jax.nn.gelu(pre, approximate=False))
    return after + low_back(jnp.einsum('sqe,ed->sqd', hidden, w_down, precision=HIGH) + b_down)

def reference(images, cotangent, counts, ln1_gain, ln1_bias, w_qkv, b_qv, w_out, b_out, ln2_gain, ln2_bias, w_up, b_up, w_down, b_down):
    weights = tuple((p.astype(jnp.float32) for p in (ln1_gain, ln1_bias, w_qkv, b_qv, w_out, b_out, ln2_gain, ln2_bias, w_up, b_up, w_down, b_down)))
    groups = images.astype(jnp.float32).reshape(MB * N_FSDP, SLOTS, SEQ, D)
    backs = cotangent.astype(jnp.float32).reshape(MB * N_FSDP, SLOTS, SEQ, D)
    live = counts.reshape(MB * N_FSDP).astype(jnp.int32)
    bump = jnp.zeros_like(groups)

    def forward(weights, groups, bump):
        first_params = tuple((p[0] for p in weights))
        second_params = tuple((p[1] for p in weights))

        def one_group(item):
            group, extra, count = item
            mask = (jnp.arange(SLOTS, dtype=jnp.int32) < count).astype(jnp.float32)[:, None, None]
            handed = low(low_back(mask * encoder_block(first_params, group))) + extra
            final = mask * encoder_block(second_params, handed)
            return (handed, final)
        return lax.map(jax.checkpoint(one_group), (groups, bump, live))
    (handed, final), pullback = jax.vjp(forward, weights, groups, bump)
    grad_weights, grad_groups, grad_bump = pullback((jnp.zeros_like(handed), backs))
    acts = jnp.stack([handed, final]).reshape(2, MB, N_FSDP * SLOTS, SEQ, D).astype(jnp.bfloat16)
    in_grads = jnp.stack([grad_groups, grad_bump]).reshape(2, MB, N_FSDP * SLOTS, SEQ, D).astype(jnp.bfloat16)
    return (acts, in_grads, grad_weights[0], grad_weights[1], grad_weights[2], grad_weights[3], grad_weights[4], grad_weights[5], grad_weights[6], grad_weights[7], grad_weights[8], grad_weights[9], grad_weights[10], grad_weights[11])
```

```python
import functools

import jax
import jax.numpy as jnp
from jax import lax
from jax.experimental import pallas as pl
from jax.experimental.pallas import tpu as pltpu
from jax.sharding import PartitionSpec as P

HEADS = 6
EPS = 1e-06
F32 = jnp.float32
LOW = jnp.bfloat16

G1, S1, BO, G2, S2, BD, BQ, BV, BU = 0, 1, 2, 3, 4, 5, 6, 7, 8
TABLE = 16


def mm(left, right):
    return jnp.dot(left, right, preferred_element_type=F32)


def mm_right(left, right):
    return lax.dot_general(left, right, (((1,), (1,)), ((), ())), preferred_element_type=F32)


def mm_left(left, right):
    return lax.dot_general(left, right, (((0,), (0,)), ((), ())), preferred_element_type=F32)


def normal_parts(pre):
    decay = jnp.exp2(pre * pre * (-0.5 * 1.4426950408889634))
    t = 1.0 / (1.0 + (0.3275911 * 0.7071067811865476) * jnp.abs(pre))
    poly = 0.5 * 1.061405429
    for term in (-1.453152027, 1.421413741, -0.284496736, 0.254829592):
        poly = poly * t + 0.5 * term
    tail = poly * t * decay
    phi = jnp.where(pre < 0.0, tail, 1.0 - tail)
    slope = phi + pre * (decay * 0.3989422804014327)
    return phi, slope


def normalize(value):
    center = value - jnp.mean(value, axis=-1, keepdims=True)
    rstd = lax.rsqrt(jnp.mean(center * center, axis=-1, keepdims=True) + EPS)
    return center * rstd, rstd


def normalize_back(d_hat, hat, rstd):
    mean_one = jnp.mean(d_hat, axis=-1, keepdims=True)
    mean_two = jnp.mean(d_hat * hat, axis=-1, keepdims=True)
    return rstd * (d_hat - mean_one - hat * mean_two)


def colsum(value):
    return jnp.sum(value, axis=0, keepdims=True)


def compute_kernel(
    dims,
    x_ref, ct_ref, mask_ref, wqkv, wout, wup, wdown, table,
    act_ref, ing_ref, gqkv, gout, gup, gdown, gtable,
    hat1, nrm1, qkv, prob, ctx, hat2, nrm2, hid, slope, rstds,
    nrm1b, qkvb, ctxb, nrm2b, hidb, dpreb, probb, slopeb, dal, left_t, hat1b, hat2b,
):
    slots, length, rows, width, ff, head_dim = dims
    pairs = width // 128
    scale = head_dim ** -0.5
    lane = lax.broadcasted_iota(jnp.int32, (1, 128), 1)
    half = [(lane < head_dim).astype(LOW), (lane >= head_dim).astype(LOW)]
    half_f = [(lane < head_dim).astype(F32), (lane >= head_dim).astype(F32)]
    key_pad = jnp.where(lax.broadcasted_iota(jnp.int32, (1, rows), 1) < length, 0.0, -1e30).astype(F32)
    chunk = 256
    chunks = ff // chunk

    def vec(s, r):
        return table[s, r : r + 1, :]

    def up_bias(s, c):
        first = c * chunk
        row, col = first // width, first % width
        if col + chunk <= width:
            return table[s, BU + row : BU + row + 1, col : col + chunk]
        a = table[s, BU + row : BU + row + 1, col:width]
        b = table[s, BU + row + 1 : BU + row + 2, 0 : chunk - (width - col)]
        return jnp.concatenate([a, b], axis=1)

    gtable[...] = jnp.zeros_like(gtable)

    def add_vec(s, r, value):
        gtable[s, r : r + 1, :] += value

    def add_up_bias(s, c, value):
        first = c * chunk
        row, col = first // width, first % width
        if col + chunk <= width:
            gtable[s, BU + row : BU + row + 1, col : col + chunk] += value
        else:
            cut = width - col
            gtable[s, BU + row : BU + row + 1, col:width] += value[:, :cut]
            gtable[s, BU + row + 1 : BU + row + 2, 0 : chunk - cut] += value[:, cut:]

    def attn_forward(s, x, rd, srd, hat_ref, nrm_ref, qkv_ref, prob_ref, ctx_ref, pi):
        hat, rstd = normalize(x)
        hat_ref[srd, :] = hat.astype(LOW)
        nrm = (hat * vec(s, G1) + vec(s, S1)).astype(LOW)
        nrm_ref[rd, :] = nrm
        q = (mm(nrm, wqkv[s, :, 0:width]) + vec(s, BQ)).astype(LOW)
        k = mm(nrm, wqkv[s, :, width : 2 * width]).astype(LOW)
        v = (mm(nrm, wqkv[s, :, 2 * width :]) + vec(s, BV)).astype(LOW)
        qkv_ref[rd, 0:width] = q
        qkv_ref[rd, width : 2 * width] = k
        qkv_ref[rd, 2 * width :] = v
        parts = []
        for p in range(pairs):
            cols = slice(128 * p, 128 * p + 128)
            total = None
            for j in range(2):
                scores = mm_right(q[:, cols], k[:, cols] * half[j]) + key_pad
                top = jnp.max(scores, axis=-1, keepdims=True)
                e = jnp.exp2((scores - top) * (scale * 1.4426950408889634))
                pr = (e * (1.0 / jnp.sum(e, axis=-1, keepdims=True))).astype(LOW)
                prob_ref[pi, 2 * p + j] = pr
                part = mm(pr, v[:, cols] * half[j])
                total = part if total is None else total + part
            parts.append(total.astype(LOW))
        context = jnp.concatenate(parts, axis=1)
        ctx_ref[rd, :] = context
        after = x + mm(context, wout[s]) + vec(s, BO)
        return after, rstd

    def ff_forward(s, after, rd, srd, hat_ref, nrm_ref, hid_ref, slope_ref):
        hat, rstd = normalize(after)
        hat_ref[srd, :] = hat.astype(LOW)
        nrm = (hat * vec(s, G2) + vec(s, S2)).astype(LOW)
        nrm_ref[rd, :] = nrm
        total = after + vec(s, BD)
        for c in range(chunks):
            cols = slice(chunk * c, chunk * c + chunk)
            pre = mm(nrm, wup[s, :, cols]) + up_bias(s, c)
            phi, slo = normal_parts(pre)
            h = (pre * phi).astype(LOW)
            hid_ref[rd, cols] = h
            slope_ref[srd, cols] = slo.astype(LOW)
            total = total + mm(h, wdown[s, cols, :])
        return total, rstd

    def ff_backward(s, g, rd, srd, hat_ref, slope_ref, dpre_ref, rstd):
        g_low = g.astype(LOW)
        add_vec(s, BD, colsum(g_low.astype(F32)))
        d_nrm = None
        for c in range(chunks):
            cols = slice(chunk * c, chunk * c + chunk)
            d_hid = mm_right(g_low, wdown[s, cols, :])
            d_pre = (d_hid * slope_ref[srd, cols].astype(F32)).astype(LOW)
            dpre_ref[rd, cols] = d_pre
            add_up_bias(s, c, colsum(d_pre.astype(F32)))
            part = mm_right(d_pre, wup[s, :, cols])
            d_nrm = part if d_nrm is None else d_nrm + part
        hat = hat_ref[srd, :].astype(F32)
        add_vec(s, G2, colsum(d_nrm * hat))
        add_vec(s, S2, colsum(d_nrm))
        return g + normalize_back(d_nrm * vec(s, G2), hat, rstd)

    def attn_backward(s, d_after, rd, srd, hat_ref, qkv_ref, prob_ref, ctx_ref, pi, rstd):
        low = d_after.astype(LOW)
        dal[rd, :] = low
        add_vec(s, BO, colsum(low.astype(F32)))
        d_ctx = mm_right(low, wout[s]).astype(LOW)
        dq, dk, dv = [], [], []
        for p in range(pairs):
            cols = slice(128 * p, 128 * p + 128)
            q = qkv_ref[rd, 128 * p : 128 * p + 128]
            k = qkv_ref[rd, width + 128 * p : width + 128 * p + 128]
            v = qkv_ref[rd, 2 * width + 128 * p : 2 * width + 128 * p + 128]
            dc = d_ctx[:, cols]
            both = dc.astype(F32) * ctx_ref[rd, cols].astype(F32)
            sums = [None, None, None]
            for j in range(2):
                pr = prob_ref[pi, 2 * p + j]
                delta = jnp.sum(both * half_f[j], axis=-1, keepdims=True)
                d_prob = mm_right(dc, v * half[j])
                ds = (pr.astype(F32) * (d_prob - delta)).astype(LOW)
                new = [mm(ds, k * half[j]), mm_left(ds, q * half[j]), mm_left(pr, dc * half[j])]
                sums = [b if a is None else a + b for a, b in zip(sums, new)]
            dq.append((sums[0] * scale).astype(LOW))
            dk.append((sums[1] * scale).astype(LOW))
            dv.append(sums[2].astype(LOW))
        d_mixed = jnp.concatenate(dq + dk + dv, axis=1)
        qkv_ref[rd, :] = d_mixed
        add_vec(s, BQ, colsum(d_mixed[:, 0:width].astype(F32)))
        add_vec(s, BV, colsum(d_mixed[:, 2 * width :].astype(F32)))
        d_nrm = mm_right(d_mixed, wqkv[s])
        hat = hat_ref[srd, :].astype(F32)
        add_vec(s, G1, colsum(d_nrm * hat))
        add_vec(s, S1, colsum(d_nrm))
        return d_after + normalize_back(d_nrm * vec(s, G1), hat, rstd)

    def weight_grads(s, g_ref, hid_ref, nrm2_ref, dpre_ref, ctx_ref, nrm1_ref, dmix_ref):
        left_t[...] = g_ref[...].T

        @pl.loop(0, chunks)
        def down(c):
            cols = pl.ds(pl.multiple_of(c * chunk, chunk), chunk)
            gdown[s, cols, :] = mm(left_t[...], hid_ref[:, cols]).T.astype(LOW)

        left_t[...] = nrm2_ref[...].T

        @pl.loop(0, chunks)
        def up(c):
            cols = pl.ds(pl.multiple_of(c * chunk, chunk), chunk)
            gup[s, :, cols] = mm(left_t[...], dpre_ref[:, cols]).astype(LOW)

        left_t[...] = ctx_ref[...].T
        gout[s] = mm(left_t[...], dal[...]).astype(LOW)
        left_t[...] = nrm1_ref[...].T

        @pl.loop(0, 3)
        def three(c):
            cols = pl.ds(pl.multiple_of(c * width, 128), width)
            gqkv[s, :, cols] = mm(left_t[...], dmix_ref[:, cols]).astype(LOW)

    def rows_of(i):
        return pl.ds(pl.multiple_of(i * rows, 16), rows)

    here = pl.ds(0, rows)

    @pl.loop(0, slots)
    def forward_one(i):
        rd = rows_of(i)
        after, rstd1 = attn_forward(0, x_ref[rd, :].astype(F32), rd, rd, hat1, nrm1, qkv, prob, ctx, i)
        out, rstd2 = ff_forward(0, after, rd, rd, hat2, nrm2, hid, slope)
        act_ref[0, rd, :] = (mask_ref[rd, :] * out).astype(LOW)
        rstds[rd, 0:1] = rstd1
        rstds[rd, 1:2] = rstd2

    @pl.loop(0, slots)
    def both_two(i):
        rd = rows_of(i)
        x = act_ref[0, rd, :].astype(F32)
        after, rstd1 = attn_forward(1, x, rd, here, hat1b, nrm1b, qkvb, probb, ctxb, 0)
        out, rstd2 = ff_forward(1, after, rd, here, hat2b, nrm2b, hidb, slopeb)
        act_ref[1, rd, :] = (mask_ref[rd, :] * out).astype(LOW)
        g = ct_ref[rd, :].astype(F32)
        d_after = ff_backward(1, g, rd, here, hat2b, slopeb, dpreb, rstd2)
        d_in = attn_backward(1, d_after, rd, here, hat1b, qkvb, probb, ctxb, 0, rstd1)
        ing_ref[1, rd, :] = d_in.astype(LOW)

    weight_grads(1, ct_ref, hidb, nrm2b, dpreb, ctxb, nrm1b, qkvb)

    @pl.loop(0, slots)
    def backward_one(i):
        rd = rows_of(i)
        g = mask_ref[rd, :] * ing_ref[1, rd, :].astype(F32)
        nrm1b[rd, :] = g.astype(LOW)
        d_after = ff_backward(0, g, rd, rd, hat2, slope, slope, rstds[rd, 1:2])
        d_in = attn_backward(0, d_after, rd, rd, hat1, qkv, prob, ctx, i, rstds[rd, 0:1])
        ing_ref[0, rd, :] = d_in.astype(LOW)

    weight_grads(0, nrm1b, hid, nrm2, slope, ctx, nrm1, qkv)


def to_rows(value, rows):
    slots, length, width = value.shape
    return jnp.pad(value, ((0, 0), (0, rows - length), (0, 0))).reshape(slots * rows, width)


def local(
    images, cotangent, counts,
    ln1_gain, ln1_bias, w_qkv, b_qv, w_out, b_out, ln2_gain, ln2_bias, w_up, b_up, w_down, b_down,
):
    micro_count, slots, length, width = images.shape
    ff = w_up.shape[2]
    rows = -(-length // 16) * 16
    n = lax.axis_size("fsdp")
    core = lax.axis_index("section")
    me = lax.axis_index("fsdp")

    def mine(value):
        return lax.dynamic_index_in_dim(value, core, 0, keepdims=False)

    live = jnp.arange(slots, dtype=jnp.int32) < mine(counts)[0]
    valid = (live[:, None] & (jnp.arange(rows) < length)[None, :]).reshape(slots * rows, 1)
    mask = valid.astype(F32)
    x = to_rows(mine(images), rows)
    ct = jnp.where(valid, to_rows(mine(cotangent), rows), 0).astype(LOW)

    lines = []
    for vector in (ln1_gain, ln1_bias, b_out, ln2_gain, ln2_bias, b_down, b_qv, b_up):
        part = vector.shape[1]
        full = part * n
        line = lax.dynamic_update_slice(jnp.zeros((1, full), LOW), vector, (0, part * me))
        lines.append(line.reshape(-1, width))
    table = jnp.concatenate(lines, axis=0)
    table = jnp.pad(table, ((0, TABLE - table.shape[0]), (0, 0)))
    table = lax.all_gather(lax.psum(table.astype(F32), "fsdp"), "section", axis=0)

    def whole(value):
        return lax.all_gather(lax.all_gather(value[0], "fsdp", axis=0, tiled=True), "section", axis=0)

    weights = [whole(w) for w in (w_qkv, w_out, w_up, w_down)]
    total = slots * rows
    head_dim = width // HEADS

    def vm(shape, kind=LOW):
        return pltpu.VMEM(shape, kind)

    outs = [
        ((2, total, width), LOW), ((2, total, width), LOW),
        ((2, width, 3 * width), LOW), ((2, width, width), LOW), ((2, width, ff), LOW), ((2, ff, width), LOW),
        ((2, TABLE, width), F32),
    ]
    scratch = [
        vm((total, width)), vm((total, width)), vm((total, 3 * width)), vm((slots, HEADS, rows, rows)),
        vm((total, width)), vm((total, width)), vm((total, width)), vm((total, ff)), vm((total, ff)),
        vm((total, 2), F32),
        vm((total, width)), vm((total, 3 * width)), vm((total, width)), vm((total, width)), vm((total, ff)),
        vm((total, ff)), vm((1, HEADS, rows, rows)), vm((rows, ff)), vm((total, width)), vm((width, total)),
    ]
    dims = (slots, length, rows, width, ff, head_dim)
    acts, ings, gqkv, gout, gup, gdown, gtable = pl.pallas_call(
        functools.partial(compute_kernel, dims),
        out_shape=[jax.ShapeDtypeStruct(*o) for o in outs],
        in_specs=[pl.BlockSpec(memory_space=pltpu.VMEM)] * 8,
        out_specs=[pl.BlockSpec(memory_space=pltpu.VMEM)] * len(outs),
        scratch_shapes=scratch + [vm((rows, width)), vm((rows, width))],
        compiler_params=pltpu.CompilerParams(vmem_limit_bytes=63 << 20),
    )(x, ct, mask, *weights, table)

    def other(value):
        return lax.all_to_all(
            value.reshape(2, slots, rows, width)[:, :, :length], "section", split_axis=0, concat_axis=0, tiled=True
        )

    def share(grad):
        grad = lax.psum_scatter(grad, "section", scatter_dimension=0, tiled=True)
        return lax.psum_scatter(grad, "fsdp", scatter_dimension=1, tiled=True).astype(F32)

    gtable = lax.psum_scatter(gtable, "section", scatter_dimension=0, tiled=True)
    gtable = lax.psum(gtable, "fsdp")[0]

    def vector(row, like):
        part = like.shape[1]
        count = part * n // width
        flat = gtable[row : row + count].reshape(1, part * n)
        return lax.dynamic_slice(flat, (0, part * me), (1, part))

    return (
        other(acts)[None], other(ings)[None],
        vector(G1, ln1_gain), vector(S1, ln1_bias), share(gqkv), vector(BQ, b_qv), share(gout), vector(BO, b_out),
        vector(G2, ln2_gain), vector(S2, ln2_bias), share(gup), vector(BU, b_up), share(gdown), vector(BD, b_down),
    )


def solution(mesh):
    split = P("section", "fsdp")
    cube = P("section", "fsdp", None)
    image = P(None, "fsdp", None, None)
    result = P("section", None, "fsdp", None, None)
    params = (split, split, cube, split, cube, split, split, split, cube, split, cube, split)
    return jax.shard_map(
        local,
        mesh=mesh,
        in_specs=(image, image, P(None, "fsdp")) + params,
        out_specs=(result, result) + params,
        check_vma=False,
    )
```

```python
import functools
import math

import jax
import jax.numpy as jnp
from jax import lax
from jax.experimental import pallas as pl
from jax.experimental.pallas import tpu as pltpu
from jax.sharding import PartitionSpec as P

HEADS = 6
EPS = 1e-06
F32 = jnp.float32
LOW = jnp.bfloat16

G1, S1, BO, G2, S2, BD, BQ, BV, BU = 0, 1, 2, 3, 4, 5, 6, 7, 8
TABLE = 16
ATT, UP, DOWN = 0, 1, 2


def radices(n):
    rest = max(r for r in range(1, n + 1) if r * r * r <= n and n % (r * r) == 0)
    return n // (rest * rest), rest


def mm(left, right):
    return jnp.dot(left, right, preferred_element_type=F32)


def mm_right(left, right):
    return lax.dot_general(left, right, (((1,), (1,)), ((), ())), preferred_element_type=F32)


def mm_left(left, right):
    return lax.dot_general(left, right, (((0,), (0,)), ((), ())), preferred_element_type=F32)


def normal_parts(pre):
    decay = jnp.exp2(pre * pre * (-0.5 * 1.4426950408889634))
    t = 1.0 / (1.0 + (0.3275911 * 0.7071067811865476) * jnp.abs(pre))
    poly = 0.5 * 1.061405429
    for term in (-1.453152027, 1.421413741, -0.284496736, 0.254829592):
        poly = poly * t + 0.5 * term
    tail = poly * t * decay
    phi = jnp.where(pre < 0.0, tail, 1.0 - tail)
    slope = phi + pre * (decay * 0.3989422804014327)
    return phi, slope


def normalize(value):
    mean = jnp.mean(value, axis=-1, keepdims=True)
    center = value - mean
    rstd = lax.rsqrt(jnp.mean(center * center, axis=-1, keepdims=True) + EPS)
    return center * rstd, rstd, mean


def normalize_back(d_hat, hat, rstd):
    mean_one = jnp.mean(d_hat, axis=-1, keepdims=True)
    mean_two = jnp.mean(d_hat * hat, axis=-1, keepdims=True)
    return rstd * (d_hat - mean_one - hat * mean_two)


def colsum(value):
    return jnp.sum(value, axis=0, keepdims=True)


def whole_kernel(dims, *refs):
    slots, length, rows, width, ff, head_dim, n = dims
    (
        x_ref, ct_ref, live_ref, pack_a, pack_u, pack_d,
        act_out, ing_out, o_qkv, o_out, o_up, o_down, o_vec, hid_far, slope_far,
        wqkv, wout, wup, wdown, table, gtable,
        act, ing, after_ref, nrm1, qkv, prob, ctx, hat2, nrm2, rstds,
        hid, slope,
        nrm1b, qkvb, ctxb, nrm2b, probb, hat2b, dal, low_g, left_t,
        s_a, s_u, s_d, r0_a, r0_u, r0_d, r1_a, r1_u, r1_d, r2_a, r2_u, r2_d, r3_a, r3_u, r3_d,
        t_a, t_u, t_d, f_a, f_u, f_d,
        ship_s, ship_r, far_s, ag0_s, ag0_r, ag1_s, ag1_r, ag2_s, ag2_r, ag3_s, ag3_r, ag4_s, ag4_r,
        rs0_s, rs0_r, rs1_s, rs1_r, rs2_s, rs2_r, rs3_s, rs3_r, rs4_s, rs4_r, credit,
    ) = refs
    pack = (pack_a, pack_u, pack_d)
    stage = (s_a, s_u, s_d)
    r0, r1, r2, r3 = (r0_a, r0_u, r0_d), (r1_a, r1_u, r1_d), (r2_a, r2_u, r2_d), (r3_a, r3_u, r3_d)
    leaving, final = (t_a, t_u, t_d), (f_a, f_u, f_d)

    first, rest = radices(n)
    unit = width // n
    core = lax.axis_index("section")
    me = lax.axis_index("fsdp")
    dig_a, dig_b, dig_c = me // (rest * rest), (me // rest) % rest, me % rest
    dig_three, dig_two = dig_c + core * (dig_b - dig_c), dig_b + core * (dig_c - dig_b)
    step_three, step_two = 1 + core * (rest - 1), rest - core * (rest - 1)
    pos = (dig_three * rest + dig_two) * first + dig_a
    pos_other = (dig_two * rest + dig_three) * first + dig_a
    sibling = {"section": 1 - core}

    def place(half, j):
        a, b, c = j // (rest * rest), (j // rest) % rest, j % rest
        return ((c * rest + b) if half == 0 else (b * rest + c)) * first + a

    def peer_first(t):
        return {"fsdp": me + ((dig_a + t) % first - dig_a) * (rest * rest)}

    def peer_two(t):
        return {"fsdp": me + ((dig_two + t) % rest - dig_two) * step_two}

    def peer_three(t):
        return {"fsdp": me + ((dig_three + t) % rest - dig_three) * step_three}

    def remote(src, dst, s_sem, r_sem, device):
        return pltpu.make_async_remote_copy(
            src_ref=src, dst_ref=dst, send_sem=s_sem, recv_sem=r_sem, device_id=device,
            device_id_type=pl.DeviceIdType.MESH,
        )

    def slab_two(three, two):
        return pl.ds((three * rest + two) * first, first)

    def slab_three(three):
        return pl.ds(three * rest * first, rest * first)

    def ag0_copy(g):
        return remote(pack[g].at[1 - core], stage[g].at[core, 1 - core, pos_other], ag0_s.at[g], ag0_r.at[g], sibling)

    def ag1_copy(b, g, t):
        ref = stage[g].at[b, core, pos]
        return remote(ref, ref, ag1_s.at[3 * b + g, t - 1], ag1_r.at[3 * b + g, t - 1], peer_first(t))

    def ag2_copy(b, g, t):
        ref = stage[g].at[b, core, slab_two(dig_three, dig_two)]
        return remote(ref, ref, ag2_s.at[3 * b + g, t - 1], ag2_r.at[3 * b + g, t - 1], peer_two(t))

    def ag3_copy(b, g, t):
        ref = stage[g].at[b, core, slab_three(dig_three)]
        return remote(ref, ref, ag3_s.at[3 * b + g, t - 1], ag3_r.at[3 * b + g, t - 1], peer_three(t))

    def ag4_copy(b, g, t):
        ref = stage[g].at[b, core, slab_three((dig_three + rest - t) % rest)]
        return remote(ref, ref, ag4_s.at[3 * b + g, t], ag4_r.at[3 * b + g, t], sibling)

    def ag4_landing(b, g, t):
        ref = stage[g].at[b, 1 - core, slab_three((dig_two + rest - t) % rest)]
        return remote(ref, ref, ag4_s.at[3 * b + g, t], ag4_r.at[3 * b + g, t], sibling)

    def ag0(g):
        ag0_copy(g).start()
        stage[g][core, core, pos] = pack[g][core]

    def ag1(b, g):
        @pl.when(core != b)
        def _():
            ag0_copy(g).wait_recv()

        for t in range(1, first):
            ag1_copy(b, g, t).start()

    def ag2(b, g):
        for t in range(1, first):
            ag1_copy(b, g, t).wait_recv()
        for t in range(1, rest):
            ag2_copy(b, g, t).start()

    def ag3(b, g):
        for t in range(1, rest):
            ag2_copy(b, g, t).wait_recv()
        for t in range(1, rest):
            ag3_copy(b, g, t).start()
        ag4_copy(b, g, 0).start()

    def ag4(b, g):
        for t in range(1, rest):
            ag3_copy(b, g, t).wait_recv()
            ag4_copy(b, g, t).start()

    def ag5(b, g):
        for t in range(rest):
            ag4_landing(b, g, t).wait_recv()
        lay_out(b, g)

    def ag_sent(b, g):
        for t in range(1, first):
            ag1_copy(b, g, t).wait_send()
        for t in range(1, rest):
            ag2_copy(b, g, t).wait_send()
            ag3_copy(b, g, t).wait_send()
        for t in range(rest):
            ag4_copy(b, g, t).wait_send()

    def lay_out(b, g):
        if g == DOWN:
            for j in range(n):
                for half in range(2):
                    begin = 4 * unit * j + 2 * unit * half
                    wdown[b, begin : begin + 2 * unit, :] = s_d[b, half, place(half, j)]
            return
        skip = TABLE if g == ATT else 0
        together = 16 // math.gcd(unit, 16)
        for half in range(2):
            for j in range(0, n, together):
                pieces = [stage[g][b, half, place(half, j + i)].astype(F32) for i in range(together)]
                for sub in range(2):
                    low = skip + sub * unit
                    block = jnp.concatenate([piece[low : low + unit] for piece in pieces], axis=0).astype(LOW)
                    part = 2 * half + sub
                    down = slice(unit * j, unit * (j + together))
                    if g == UP:
                        wup[b, down, part * width : (part + 1) * width] = block
                    elif part == 3:
                        wout[b, down, :] = block
                    else:
                        wqkv[b, down, part * width : (part + 1) * width] = block
            if g == ATT:
                total = s_a[b, half, 0][0:TABLE].astype(F32)
                for j in range(1, n):
                    total = total + s_a[b, half, j][0:TABLE].astype(F32)
                table[b, 8 * half : 8 * half + 8, :] = total[0:8]

    def rs0_copy(b, g):
        return remote(stage[g].at[b, 1 - core], r0[g], rs0_s.at[3 * b + g], rs0_r.at[3 * b + g], sibling)

    def rs1_copy(b, g, t):
        return remote(
            stage[g].at[b, core, slab_three((dig_three + t) % rest)], r1[g].at[b, t - 1],
            rs1_s.at[3 * b + g, t - 1], rs1_r.at[3 * b + g, t - 1], peer_three(t),
        )

    def rs2_copy(b, g, t):
        return remote(
            stage[g].at[b, core, slab_two(dig_three, (dig_two + t) % rest)], r2[g].at[b, t - 1],
            rs2_s.at[3 * b + g, t - 1], rs2_r.at[3 * b + g, t - 1], peer_two(t),
        )

    def rs3_copy(b, g, t):
        there = (dig_three * rest + dig_two) * first + (dig_a + t) % first
        return remote(
            stage[g].at[b, core, there], r3[g].at[b, t - 1],
            rs3_s.at[3 * b + g, t - 1], rs3_r.at[3 * b + g, t - 1], peer_first(t),
        )

    def rs4_copy(b, g):
        return remote(leaving[g], final[g].at[core], rs4_s.at[g], rs4_r.at[g], sibling)

    def rs0(b, g):
        if b == 0:
            pl.semaphore_wait(credit.at[g], 1)
        rs0_copy(b, g).start()

    def rs1(b, g):
        rs0_copy(b, g).wait_recv()

        @pl.loop(0, n)
        def _(p):
            stage[g][b, core, p] = stage[g][b, core, p] + r0[g][p]

        if b == 1:
            pl.semaphore_signal(credit.at[g], inc=1, device_id=sibling, device_id_type=pl.DeviceIdType.MESH)
        for t in range(1, rest):
            rs1_copy(b, g, t).start()

    def rs2(b, g):
        for t in range(1, rest):
            rs1_copy(b, g, t).wait_recv()

        @pl.loop(0, rest * first)
        def _(p):
            at = dig_three * rest * first + p
            total = stage[g][b, core, at].astype(F32)
            for t in range(1, rest):
                total = total + r1[g][b, t - 1, p].astype(F32)
            stage[g][b, core, at] = total.astype(LOW)

        for t in range(1, rest):
            rs2_copy(b, g, t).start()

    def rs3(b, g):
        for t in range(1, rest):
            rs2_copy(b, g, t).wait_recv()

        @pl.loop(0, first)
        def _(p):
            at = (dig_three * rest + dig_two) * first + p
            total = stage[g][b, core, at].astype(F32)
            for t in range(1, rest):
                total = total + r2[g][b, t - 1, p].astype(F32)
            stage[g][b, core, at] = total.astype(LOW)

        for t in range(1, first):
            rs3_copy(b, g, t).start()

    def rs4(b, g):
        for t in range(1, first):
            rs3_copy(b, g, t).wait_recv()
        total = stage[g][b, core, pos].astype(F32)
        for t in range(1, first):
            total = total + r3[g][b, t - 1].astype(F32)

        @pl.when(core == b)
        def _():
            final[g][core] = total

        @pl.when(core != b)
        def _():
            leaving[g][...] = total
            rs4_copy(b, g).start()

    def rs_sent(b, g):
        rs0_copy(b, g).wait_send()
        for t in range(1, rest):
            rs1_copy(b, g, t).wait_send()
            rs2_copy(b, g, t).wait_send()
        for t in range(1, first):
            rs3_copy(b, g, t).wait_send()

    def rows_of(i):
        return pl.ds(pl.multiple_of(i * rows, 16), rows)

    def ship_parts(kind, b, i):
        src, out = ((act, act_out), (ing, ing_out))[kind]
        q = 2 * kind + b
        rd = rows_of(i)
        near = pltpu.make_async_copy(src.at[rd], out.at[core, rd], ship_s.at[q, i])
        far = remote(src.at[rd], out.at[core, rd], ship_s.at[q, i], ship_r.at[q, i], sibling)
        return near, far

    def ship(kind, b, i):
        near, far = ship_parts(kind, b, i)

        @pl.when(core == b)
        def _():
            near.start()

        @pl.when(core != b)
        def _():
            far.start()

    def shipped(kind, b, i):
        near, far = ship_parts(kind, b, i)

        @pl.when(core == b)
        def _():
            near.wait()

        @pl.when(core != b)
        def _():
            far.wait_send()

    def landed(kind, b, i):
        out = (act_out, ing_out)[kind]
        q = 2 * kind + b
        ref = out.at[1 - core, rows_of(i)]

        @pl.when(core == b)
        def _():
            remote(ref, ref, ship_s.at[q, i], ship_r.at[q, i], sibling).wait_recv()

    def far_copy(which, i, back):
        near, far = ((hid, hid_far), (slope, slope_far))[which]
        near, far = near.at[rows_of(i)], far.at[rows_of(i)]
        src, dst = (far, near) if back else (near, far)
        return pltpu.make_async_copy(src, dst, far_s.at[2 * int(back) + which, i])

    pairs = width // 128
    scale = head_dim ** -0.5
    lane = lax.broadcasted_iota(jnp.int32, (1, 128), 1)
    half_low = [(lane < head_dim).astype(LOW), (lane >= head_dim).astype(LOW)]
    half_f = [(lane < head_dim).astype(F32), (lane >= head_dim).astype(F32)]
    key_pad = jnp.where(lax.broadcasted_iota(jnp.int32, (1, rows), 1) < length, 0.0, -1e30).astype(F32)
    chunk = 256
    chunks = ff // chunk

    def vec(s, r):
        return table[s, r : r + 1, :]

    def up_bias(s, c):
        begin = c * chunk
        row, col = begin // width, begin % width
        if col + chunk <= width:
            return table[s, BU + row : BU + row + 1, col : col + chunk]
        a = table[s, BU + row : BU + row + 1, col:width]
        b = table[s, BU + row + 1 : BU + row + 2, 0 : chunk - (width - col)]
        return jnp.concatenate([a, b], axis=1)

    def add_vec(s, r, value):
        gtable[s, r : r + 1, :] += value

    def add_up_bias(s, c, value):
        begin = c * chunk
        row, col = begin // width, begin % width
        if col + chunk <= width:
            gtable[s, BU + row : BU + row + 1, col : col + chunk] += value
        else:
            cut = width - col
            gtable[s, BU + row : BU + row + 1, col:width] += value[:, :cut]
            gtable[s, BU + row + 1 : BU + row + 2, 0 : chunk - cut] += value[:, cut:]

    def attn_forward(s, x, rd, nrm_ref, qkv_ref, prob_ref, ctx_ref, pi):
        hat, rstd, mean = normalize(x)
        nrm = (hat * vec(s, G1) + vec(s, S1)).astype(LOW)
        nrm_ref[rd, :] = nrm
        q = (mm(nrm, wqkv[s, :, 0:width]) + vec(s, BQ)).astype(LOW)
        k = mm(nrm, wqkv[s, :, width : 2 * width]).astype(LOW)
        v = (mm(nrm, wqkv[s, :, 2 * width :]) + vec(s, BV)).astype(LOW)
        qkv_ref[rd, 0:width] = q
        qkv_ref[rd, width : 2 * width] = k
        qkv_ref[rd, 2 * width :] = v
        parts = []
        for p in range(pairs):
            cols = slice(128 * p, 128 * p + 128)
            total = None
            for j in range(2):
                scores = mm_right(q[:, cols], k[:, cols] * half_low[j]) + key_pad
                top = jnp.max(scores, axis=-1, keepdims=True)
                e = jnp.exp2((scores - top) * (scale * 1.4426950408889634))
                pr = (e * (1.0 / jnp.sum(e, axis=-1, keepdims=True))).astype(LOW)
                prob_ref[pi, 2 * p + j] = pr
                part = mm(pr, v[:, cols] * half_low[j])
                total = part if total is None else total + part
            parts.append(total.astype(LOW))
        context = jnp.concatenate(parts, axis=1)
        ctx_ref[rd, :] = context
        return x + mm(context, wout[s]) + vec(s, BO), rstd, mean

    def ff_forward(s, after, rd, srd, hat_ref, nrm_ref):
        hat, rstd, _ = normalize(after)
        hat_ref[srd, :] = hat.astype(LOW)
        nrm = (hat * vec(s, G2) + vec(s, S2)).astype(LOW)
        nrm_ref[rd, :] = nrm
        total = after + vec(s, BD)
        for c in range(chunks):
            cols = slice(chunk * c, chunk * c + chunk)
            pre = mm(nrm, wup[s, :, cols]) + up_bias(s, c)
            phi, slo = normal_parts(pre)
            h = (pre * phi).astype(LOW)
            hid[rd, cols] = h
            slope[rd, cols] = slo.astype(LOW)
            total = total + mm(h, wdown[s, cols, :])
        return total, rstd

    def ff_backward(s, g, rd, srd, hat_ref, rstd):
        g_low = g.astype(LOW)
        low_g[rd, :] = g_low
        add_vec(s, BD, colsum(g_low.astype(F32)))
        d_nrm = None
        for c in range(chunks):
            cols = slice(chunk * c, chunk * c + chunk)
            d_hid = mm_right(g_low, wdown[s, cols, :])
            d_pre = (d_hid * slope[rd, cols].astype(F32)).astype(LOW)
            slope[rd, cols] = d_pre
            add_up_bias(s, c, colsum(d_pre.astype(F32)))
            part = mm_right(d_pre, wup[s, :, cols])
            d_nrm = part if d_nrm is None else d_nrm + part
        hat = hat_ref[srd, :].astype(F32)
        add_vec(s, G2, colsum(d_nrm * hat))
        add_vec(s, S2, colsum(d_nrm))
        d_after = g + normalize_back(d_nrm * vec(s, G2), hat, rstd)
        low = d_after.astype(LOW)
        dal[rd, :] = low
        add_vec(s, BO, colsum(low.astype(F32)))
        return d_after

    def attn_backward(s, d_after, rd, x, mean, rstd, qkv_ref, prob_ref, ctx_ref, pi):
        d_ctx = mm_right(d_after.astype(LOW), wout[s]).astype(LOW)
        dq, dk, dv = [], [], []
        for p in range(pairs):
            cols = slice(128 * p, 128 * p + 128)
            q = qkv_ref[rd, 128 * p : 128 * p + 128]
            k = qkv_ref[rd, width + 128 * p : width + 128 * p + 128]
            v = qkv_ref[rd, 2 * width + 128 * p : 2 * width + 128 * p + 128]
            dc = d_ctx[:, cols]
            both = dc.astype(F32) * ctx_ref[rd, cols].astype(F32)
            sums = [None, None, None]
            for j in range(2):
                pr = prob_ref[pi, 2 * p + j]
                delta = jnp.sum(both * half_f[j], axis=-1, keepdims=True)
                d_prob = mm_right(dc, v * half_low[j])
                ds = (pr.astype(F32) * (d_prob - delta)).astype(LOW)
                new = [mm(ds, k * half_low[j]), mm_left(ds, q * half_low[j]), mm_left(pr, dc * half_low[j])]
                sums = [b if a is None else a + b for a, b in zip(sums, new)]
            dq.append((sums[0] * scale).astype(LOW))
            dk.append((sums[1] * scale).astype(LOW))
            dv.append(sums[2].astype(LOW))
        d_mixed = jnp.concatenate(dq + dk + dv, axis=1)
        qkv_ref[rd, :] = d_mixed
        add_vec(s, BQ, colsum(d_mixed[:, 0:width].astype(F32)))
        add_vec(s, BV, colsum(d_mixed[:, 2 * width :].astype(F32)))
        d_nrm = mm_right(d_mixed, wqkv[s])
        hat = (x - mean) * rstd
        add_vec(s, G1, colsum(d_nrm * hat))
        add_vec(s, S1, colsum(d_nrm))
        return d_after + normalize_back(d_nrm * vec(s, G1), hat, rstd)

    def grads_down(s):
        left_t[...] = low_g[...].T

        @pl.loop(0, 4)
        def _(c):
            cols = pl.ds(pl.multiple_of(c * width, 128), width)
            block = mm(left_t[...], hid[:, cols]).T
            for i in range(n // 4):
                for half in range(2):
                    begin = 4 * unit * i + 2 * unit * half
                    s_d[s, half, place(half, c * (n // 4) + i)] = block[begin : begin + 2 * unit].astype(LOW)

    def pair_out(ref, s, half, skip, one, two):
        for j in range(n):
            down = slice(unit * j, unit * (j + 1))
            piece = jnp.concatenate([one[down], two[down]], axis=0).astype(LOW)
            ref[s, half, place(half, j), skip : skip + 2 * unit] = piece

    def grads_up(s):
        left_t[...] = nrm2_of[s][...].T
        for half in range(2):
            one, two = [
                mm(left_t[...], slope[:, part * width : (part + 1) * width]) for part in (2 * half, 2 * half + 1)
            ]
            pair_out(s_u, s, half, 0, one, two)

    def grads_attn(s):
        ctx_s, nrm_s, mix_s = ((ctx, nrm1, qkv), (ctxb, nrm1b, qkvb))[s]
        left_t[...] = ctx_s[...].T
        four = mm(left_t[...], dal[...])
        left_t[...] = nrm_s[...].T
        three = mm(left_t[...], mix_s[:, 2 * width :])
        pair_out(s_a, s, 1, TABLE, three, four)
        one = mm(left_t[...], mix_s[:, 0:width])
        two = mm(left_t[...], mix_s[:, width : 2 * width])
        pair_out(s_a, s, 0, TABLE, one, two)
        for half in range(2):
            lines = gtable[s, 8 * half : 8 * half + 8, :]
            lines = jnp.concatenate([lines, jnp.zeros_like(lines)], axis=0).astype(LOW)
            for j in range(n):
                s_a[s, half, j, 0:TABLE] = lines

    nrm2_of = (nrm2, nrm2b)
    here = pl.ds(0, rows)

    barrier = pltpu.get_barrier_semaphore()
    greeted = [sibling] + [peer_first(t) for t in range(1, first)]
    greeted += [f(t) for f in (peer_two, peer_three) for t in range(1, rest)]
    for device in greeted:
        pl.semaphore_signal(barrier, inc=1, device_id=device, device_id_type=pl.DeviceIdType.MESH)
    pl.semaphore_wait(barrier, len(greeted))

    for g in (ATT, UP, DOWN):
        ag0(g)
    gtable[...] = jnp.zeros_like(gtable)
    ag1(0, ATT)
    ag2(0, ATT)
    ag1(0, UP)
    ag3(0, ATT)
    ag4(0, ATT)
    ag2(0, UP)
    ag1(0, DOWN)
    ag5(0, ATT)

    def events(i, table_of):
        for at, todo in table_of.items():
            @pl.when(i == at)
            def _():
                for f, b, g in todo:
                    f(b, g)

    @pl.loop(0, slots)
    def attn_one(i):
        events(i, {
            1: [(ag3, 0, UP)],
            2: [(ag4, 0, UP), (ag2, 0, DOWN), (ag1, 1, ATT)],
            3: [(ag3, 0, DOWN)],
            4: [(ag4, 0, DOWN), (ag2, 1, ATT), (ag1, 1, UP)],
            5: [(ag3, 1, ATT)],
        })
        rd = rows_of(i)
        after, rstd1, mean1 = attn_forward(0, x_ref[rd, :].astype(F32), rd, nrm1, qkv, prob, ctx, i)
        after_ref[rd, :] = after
        rstds[rd, 0:1] = rstd1
        rstds[rd, 2:3] = mean1

    ag5(0, UP)
    ag5(0, DOWN)
    ag4(1, ATT)
    ag2(1, UP)
    ag1(1, DOWN)

    @pl.loop(0, slots)
    def ff_one(i):
        events(i, {
            1: [(ag3, 1, UP)],
            2: [(ag4, 1, UP), (ag2, 1, DOWN)],
            3: [(ag3, 1, DOWN)],
            5: [(ag4, 1, DOWN)],
        })
        rd = rows_of(i)
        out, rstd2 = ff_forward(0, after_ref[rd, :], rd, rd, hat2, nrm2)
        far_copy(0, i, False).start()
        far_copy(1, i, False).start()
        act[rd, :] = (live_ref[pl.ds(i, 1), :] * out).astype(LOW)
        rstds[rd, 1:2] = rstd2
        ship(0, 0, i)

    for g in (ATT, UP, DOWN):
        ag5(1, g)

    @pl.loop(0, slots)
    def both_two(i):
        rd = rows_of(i)
        x = act[rd, :].astype(F32)
        after, rstd1, mean1 = attn_forward(1, x, rd, nrm1b, qkvb, probb, ctxb, 0)
        far_copy(0, i, False).wait()
        far_copy(1, i, False).wait()
        out, rstd2 = ff_forward(1, after, rd, here, hat2b, nrm2b)
        shipped(0, 0, i)
        act[rd, :] = (live_ref[pl.ds(i, 1), :] * out).astype(LOW)
        ship(0, 1, i)
        g = live_ref[pl.ds(i, 1), :] * ct_ref[rd, :].astype(F32)
        d_after = ff_backward(1, g, rd, here, hat2b, rstd2)
        d_in = attn_backward(1, d_after, rd, x, mean1, rstd1, qkvb, probb, ctxb, 0)
        ing[rd, :] = d_in.astype(LOW)
        ship(1, 1, i)

    for b in range(2):
        for g in (ATT, UP, DOWN):
            ag_sent(b, g)
    for g in (ATT, UP, DOWN):
        ag0_copy(g).wait_send()

    grads_down(1)
    rs0(1, DOWN)

    @pl.loop(0, slots)
    def hid_back(i):
        far_copy(0, i, True).start()

    grads_up(1)
    rs0(1, UP)

    @pl.loop(0, slots)
    def slope_back(i):
        far_copy(1, i, True).start()

    rs1(1, DOWN)
    grads_attn(1)
    rs0(1, ATT)
    rs1(1, UP)
    rs2(1, DOWN)

    @pl.loop(0, slots)
    def ff_back_one(i):
        events(i, {
            1: [(rs1, 1, ATT), (rs2, 1, UP), (rs3, 1, DOWN)],
            3: [(rs2, 1, ATT), (rs3, 1, UP), (rs4, 1, DOWN)],
            5: [(rs3, 1, ATT), (rs4, 1, UP)],
        })
        rd = rows_of(i)
        far_copy(1, i, True).wait()
        g = live_ref[pl.ds(i, 1), :] * ing[rd, :].astype(F32)
        after_ref[rd, :] = ff_backward(0, g, rd, rd, hat2, rstds[rd, 1:2])

    @pl.loop(0, slots)
    def hid_is_back(i):
        far_copy(0, i, True).wait()

    grads_down(0)
    rs0(0, DOWN)
    rs4(1, ATT)
    grads_up(0)
    rs0(0, UP)
    rs1(0, DOWN)

    @pl.loop(0, slots)
    def attn_back_one(i):
        events(i, {
            0: [(rs1, 0, UP)],
            1: [(rs2, 0, DOWN)],
            2: [(rs2, 0, UP), (rs3, 0, DOWN)],
            4: [(rs3, 0, UP)],
        })
        rd = rows_of(i)
        x = x_ref[rd, :].astype(F32)
        d_in = attn_backward(0, after_ref[rd, :], rd, x, rstds[rd, 2:3], rstds[rd, 0:1], qkv, prob, ctx, i)
        shipped(1, 1, i)
        ing[rd, :] = d_in.astype(LOW)
        ship(1, 0, i)

    grads_attn(0)
    rs0(0, ATT)
    rs1(0, ATT)
    for g in (UP, DOWN):
        @pl.when(core == 0)
        def _():
            rs4_copy(1, g).wait_send()

        rs4(0, g)
    rs2(0, ATT)
    rs3(0, ATT)

    @pl.loop(0, slots)
    def all_out(i):
        shipped(0, 1, i)
        shipped(1, 0, i)
        for kind in range(2):
            for b in range(2):
                landed(kind, b, i)

    @pl.when(core == 0)
    def _():
        rs4_copy(1, ATT).wait_send()

    rs4(0, ATT)

    for g in (DOWN, UP, ATT):
        rs_sent(0, g)
        rs_sent(1, g)
        ref = final[g].at[1 - core]
        remote(ref, ref, rs4_s.at[g], rs4_r.at[g], sibling).wait_recv()

        @pl.when(core == 1)
        def _():
            rs4_copy(0, g).wait_send()

    for half in range(2):
        o_down[2 * unit * half : 2 * unit * (half + 1), :] = f_d[half]
        for sub in range(2):
            part = 2 * half + sub
            cols = slice(part * width, (part + 1) * width)
            o_up[:, cols] = f_u[half, unit * sub : unit * (sub + 1), :]
            piece = f_a[half, TABLE + unit * sub : TABLE + unit * (sub + 1), :]
            if part == 3:
                o_out[...] = piece
            else:
                o_qkv[:, cols] = piece
        o_vec[8 * half : 8 * half + 8, :] = f_a[half, 0:8, :]


def to_rows(value, rows):
    slots, length, width = value.shape
    return jnp.pad(value, ((0, 0), (0, rows - length), (0, 0))).reshape(slots * rows, width)


def local(
    images, cotangent, counts,
    ln1_gain, ln1_bias, w_qkv, b_qv, w_out, b_out, ln2_gain, ln2_bias, w_up, b_up, w_down, b_down,
):
    micro_count, slots, length, width = images.shape
    ff = w_up.shape[2]
    rows = -(-length // 16) * 16
    n = lax.axis_size("fsdp")
    core = lax.axis_index("section")
    me = lax.axis_index("fsdp")
    unit = width // n
    first, rest = radices(n)

    def mine(value):
        return lax.dynamic_index_in_dim(value, core, 0, keepdims=False)

    live = (jnp.arange(slots, dtype=jnp.int32) < mine(counts)[0]).astype(F32)
    live = jnp.broadcast_to(jnp.pad(live, (0, -slots % 8))[:, None], (slots + -slots % 8, width))
    x = to_rows(mine(images), rows)
    ct = to_rows(mine(cotangent), rows)

    lines = []
    for vector in (ln1_gain, ln1_bias, b_out, ln2_gain, ln2_bias, b_down, b_qv, b_up):
        part = vector.shape[1]
        full = part * n
        line = lax.dynamic_update_slice(jnp.zeros((1, full), LOW), vector, (0, part * me))
        lines.append(line.reshape(-1, width))
    lines = jnp.concatenate(lines, axis=0)
    lines = jnp.pad(lines, ((0, 16 - lines.shape[0]), (0, 0))).reshape(2, 8, width)
    lines = jnp.pad(lines, ((0, 0), (0, TABLE - 8), (0, 0)))

    def by_columns(value):
        return value[0].reshape(unit, 2, 2, width).transpose(1, 2, 0, 3).reshape(2, 2 * unit, width)

    pack_a = jnp.concatenate([lines, by_columns(jnp.concatenate([w_qkv, w_out], axis=2))], axis=1)
    pack_u = by_columns(w_up)
    pack_d = w_down.reshape(2, 2 * unit, width)

    total = slots * rows
    head_dim = width // HEADS

    def vm(*shape, kind=LOW):
        return pltpu.VMEM(shape, kind)

    tall = [TABLE + 2 * unit, 2 * unit, 2 * unit]
    dma = lambda *shape: pltpu.SemaphoreType.DMA(shape)
    outs = [
        ((2, total, width), LOW), ((2, total, width), LOW),
        ((unit, 3 * width), F32), ((unit, width), F32), ((unit, ff), F32), ((4 * unit, width), F32),
        ((TABLE, width), F32), ((total, ff), LOW), ((total, ff), LOW),
    ]
    scratch = [
        vm(2, width, 3 * width), vm(2, width, width), vm(2, width, ff), vm(2, ff, width),
        vm(2, TABLE, width, kind=F32), vm(2, TABLE, width, kind=F32),
        vm(total, width), vm(total, width), vm(total, width, kind=F32),
        vm(total, width), vm(total, 3 * width), vm(slots, HEADS, rows, rows), vm(total, width),
        vm(total, width), vm(total, width), vm(total, 3, kind=F32),
        vm(total, ff), vm(total, ff),
        vm(total, width), vm(total, 3 * width), vm(total, width), vm(total, width), vm(1, HEADS, rows, rows),
        vm(rows, width), vm(total, width), vm(total, width), vm(width, total),
    ]
    scratch += [vm(2, 2, n, r, width) for r in tall]
    scratch += [vm(n, r, width) for r in tall]
    scratch += [vm(2, rest - 1, rest * first, r, width) for r in tall]
    scratch += [vm(2, rest - 1, first, r, width) for r in tall]
    scratch += [vm(2, first - 1, r, width) for r in tall]
    scratch += [vm(r, width, kind=F32) for r in tall]
    scratch += [vm(2, r, width, kind=F32) for r in tall]
    scratch += [dma(4, slots), dma(4, slots), dma(4, slots), dma(3), dma(3)]
    scratch += [dma(6, first - 1)] * 2 + [dma(6, rest - 1)] * 4 + [dma(6, rest)] * 2
    scratch += [dma(6)] * 2 + [dma(6, rest - 1)] * 4 + [dma(6, first - 1)] * 2 + [dma(3)] * 2
    scratch += [pltpu.SemaphoreType.REGULAR((3,))]
    dims = (slots, length, rows, width, ff, head_dim, n)
    vmem = pl.BlockSpec(memory_space=pltpu.VMEM)
    hbm = pl.BlockSpec(memory_space=pltpu.HBM)
    acts, ings, gqkv, gout, gup, gdown, gtable, _, _ = pl.pallas_call(
        functools.partial(whole_kernel, dims),
        out_shape=[jax.ShapeDtypeStruct(*o) for o in outs],
        in_specs=[vmem] * 6,
        out_specs=[hbm, hbm] + [vmem] * 5 + [hbm, hbm],
        scratch_shapes=scratch,
        compiler_params=pltpu.CompilerParams(
            vmem_limit_bytes=63 << 20, collective_id=0, has_side_effects=True
        ),
    )(x, ct, live, pack_a, pack_u, pack_d)

    def images_of(value):
        return value.reshape(1, 2, slots, rows, width)[:, :, :, :length]

    def vector(row, like):
        part = like.shape[1]
        count = part * n // width
        flat = gtable[row : row + count].reshape(1, part * n)
        return lax.dynamic_slice(flat, (0, part * me), (1, part))

    return (
        images_of(acts), images_of(ings),
        vector(G1, ln1_gain), vector(S1, ln1_bias), gqkv[None], vector(BQ, b_qv), gout[None], vector(BO, b_out),
        vector(G2, ln2_gain), vector(S2, ln2_bias), gup[None], vector(BU, b_up), gdown[None], vector(BD, b_down),
    )


def solution(mesh):
    split = P("section", "fsdp")
    cube = P("section", "fsdp", None)
    image = P(None, "fsdp", None, None)
    result = P("section", None, "fsdp", None, None)
    params = (split, split, cube, split, cube, split, split, split, cube, split, cube, split)
    return jax.shard_map(
        local,
        mesh=mesh,
        in_specs=(image, image, P(None, "fsdp")) + params,
        out_specs=(result, result) + params,
        check_vma=False,
    )
```

```python
import functools
import math

import jax
import jax.numpy as jnp
from jax import lax
from jax.experimental import pallas as pl
from jax.experimental.pallas import tpu as pltpu
from jax.sharding import PartitionSpec as P

HEADS = 6
EPS = 1e-06
F32 = jnp.float32
LOW = jnp.bfloat16

G1, S1, BO, G2, S2, BD, BQ, BV, BU = 0, 1, 2, 3, 4, 5, 6, 7, 8
TABLE = 16
ATT, UP, DOWN = 0, 1, 2


def radices(n):
    rest = max(r for r in range(1, n + 1) if r * r * r <= n and n % (r * r) == 0)
    return n // (rest * rest), rest


def mm(left, right):
    return jnp.dot(left, right, preferred_element_type=F32)


def mm_right(left, right):
    return lax.dot_general(left, right, (((1,), (1,)), ((), ())), preferred_element_type=F32)


def mm_left(left, right):
    return lax.dot_general(left, right, (((0,), (0,)), ((), ())), preferred_element_type=F32)


def normal_parts(pre):
    decay = jnp.exp2(pre * pre * (-0.5 * 1.4426950408889634))
    t = 1.0 / (1.0 + (0.3275911 * 0.7071067811865476) * jnp.abs(pre))
    poly = 0.5 * 1.061405429
    for term in (-1.453152027, 1.421413741, -0.284496736, 0.254829592):
        poly = poly * t + 0.5 * term
    tail = poly * t * decay
    phi = jnp.where(pre < 0.0, tail, 1.0 - tail)
    slope = phi + pre * (decay * 0.3989422804014327)
    return phi, slope


def normalize(value):
    mean = jnp.mean(value, axis=-1, keepdims=True)
    center = value - mean
    rstd = lax.rsqrt(jnp.mean(center * center, axis=-1, keepdims=True) + EPS)
    return center * rstd, rstd, mean


def normalize_back(d_hat, hat, rstd):
    mean_one = jnp.mean(d_hat, axis=-1, keepdims=True)
    mean_two = jnp.mean(d_hat * hat, axis=-1, keepdims=True)
    return rstd * (d_hat - mean_one - hat * mean_two)


def colsum(value):
    return jnp.sum(value, axis=0, keepdims=True)


def whole_kernel(dims, *refs):
    slots, length, rows, width, ff, head_dim, n = dims
    (
        images, cotangent, counts, v_g1, v_s1, v_bo, v_g2, v_s2, v_bd, v_qv, v_up, a_qkv, a_out, a_up, a_down,
        act_out, ing_out, f_a, f_u, f_d, hid_far, slope_far,
        x_ref, ct_ref, arrived, pack_a, pack_u, pack_d,
        wqkv, wout, wup, wdown, table, gtable,
        act, ing, after_ref, nrm1, qkv, prob, ctx, hat2, nrm2, rstds,
        hid, slope,
        nrm1b, qkvb, ctxb, nrm2b, probb, hat2b, dal, low_g, left_t,
        s_a, s_u, s_d, r0_a, r0_u, r0_d, r1_a, r1_u, r1_d, r2_a, r2_u, r2_d, r3_a, r3_u, r3_d,
        t_a, t_u, t_d, in_s, ship_s, ship_r, far_s, ag0_s, ag0_r, ag1_s, ag1_r, ag2_s, ag2_r, ag3_s, ag3_r, ag4_s, ag4_r,
        rs0_s, rs0_r, rs1_s, rs1_r, rs2_s, rs2_r, rs3_s, rs3_r, rs4_s, rs4_r, credit,
    ) = refs
    pack = (pack_a, pack_u, pack_d)
    stage = (s_a, s_u, s_d)
    r0, r1, r2, r3 = (r0_a, r0_u, r0_d), (r1_a, r1_u, r1_d), (r2_a, r2_u, r2_d), (r3_a, r3_u, r3_d)
    leaving, final = (t_a, t_u, t_d), (f_a, f_u, f_d)

    first, rest = radices(n)
    unit = width // n
    core = lax.axis_index("section")
    me = lax.axis_index("fsdp")
    dig_a, dig_b, dig_c = me // (rest * rest), (me // rest) % rest, me % rest
    dig_three, dig_two = dig_c + core * (dig_b - dig_c), dig_b + core * (dig_c - dig_b)
    step_three, step_two = 1 + core * (rest - 1), rest - core * (rest - 1)
    pos = (dig_three * rest + dig_two) * first + dig_a
    pos_other = (dig_two * rest + dig_three) * first + dig_a
    sibling = {"section": 1 - core}

    def place(half, j):
        a, b, c = j // (rest * rest), (j // rest) % rest, j % rest
        return ((c * rest + b) if half == 0 else (b * rest + c)) * first + a

    def peer_first(t):
        return {"fsdp": me + ((dig_a + t) % first - dig_a) * (rest * rest)}

    def peer_two(t):
        return {"fsdp": me + ((dig_two + t) % rest - dig_two) * step_two}

    def peer_three(t):
        return {"fsdp": me + ((dig_three + t) % rest - dig_three) * step_three}

    def remote(src, dst, s_sem, r_sem, device):
        return pltpu.make_async_remote_copy(
            src_ref=src, dst_ref=dst, send_sem=s_sem, recv_sem=r_sem, device_id=device,
            device_id_type=pl.DeviceIdType.MESH,
        )

    def slab_two(three, two):
        return pl.ds((three * rest + two) * first, first)

    def slab_three(three):
        return pl.ds(three * rest * first, rest * first)

    def spread(vector, rows_to):
        part = vector.shape[1]
        lanes = lax.broadcasted_iota(jnp.int32, (part, part * n), 1)
        here = lax.broadcasted_iota(jnp.int32, (part, part * n), 0) + part * me
        line = mm(vector[...], jnp.where(lanes == here, 1.0, 0.0).astype(LOW))
        return [line[:, width * i : width * (i + 1)] for i in range(rows_to)]

    def pack_own():
        lines = []
        for vector in (v_g1, v_s1, v_bo, v_g2, v_s2, v_bd):
            lines += spread(vector, 1)
        lines += spread(v_qv, 2) + spread(v_up, 4)
        blank = jnp.zeros((1, width), F32)
        lines += [blank] * (16 - len(lines))
        for half in range(2):
            top = jnp.concatenate(lines[8 * half : 8 * half + 8] + [blank] * (TABLE - 8), axis=0)
            pack_a[half, 0:TABLE, :] = top.astype(LOW)
            for ref, skip in ((pack_a, TABLE), (pack_u, 0)):
                both = []
                for part in (2 * half, 2 * half + 1):
                    if ref is pack_u:
                        both.append(a_up[0, :, part * width : (part + 1) * width])
                    elif part == 3:
                        both.append(a_out[0])
                    else:
                        both.append(a_qkv[0, :, part * width : (part + 1) * width])
                both = jnp.concatenate([value.astype(F32) for value in both], axis=0)
                ref[half, skip : skip + 2 * unit, :] = both.astype(LOW)
            pack_d[half] = a_down[0, 2 * unit * half : 2 * unit * (half + 1), :]

    def ag0_copy(g):
        return remote(pack[g].at[1 - core], stage[g].at[core, 1 - core, pos_other], ag0_s.at[g], ag0_r.at[g], sibling)

    def ag1_copy(b, g, t):
        ref = stage[g].at[b, core, pos]
        return remote(ref, ref, ag1_s.at[3 * b + g, t - 1], ag1_r.at[3 * b + g, t - 1], peer_first(t))

    def ag2_copy(b, g, t):
        ref = stage[g].at[b, core, slab_two(dig_three, dig_two)]
        return remote(ref, ref, ag2_s.at[3 * b + g, t - 1], ag2_r.at[3 * b + g, t - 1], peer_two(t))

    def ag3_copy(b, g, t):
        ref = stage[g].at[b, core, slab_three(dig_three)]
        return remote(ref, ref, ag3_s.at[3 * b + g, t - 1], ag3_r.at[3 * b + g, t - 1], peer_three(t))

    def ag4_copy(b, g, t):
        ref = stage[g].at[b, core, slab_three((dig_three + rest - t) % rest)]
        return remote(ref, ref, ag4_s.at[3 * b + g, t], ag4_r.at[3 * b + g, t], sibling)

    def ag4_landing(b, g, t):
        ref = stage[g].at[b, 1 - core, slab_three((dig_two + rest - t) % rest)]
        return remote(ref, ref, ag4_s.at[3 * b + g, t], ag4_r.at[3 * b + g, t], sibling)

    def ag0(g):
        ag0_copy(g).start()
        stage[g][core, core, pos] = pack[g][core]

    def ag1(b, g):
        @pl.when(core != b)
        def _():
            ag0_copy(g).wait_recv()

        for t in range(1, first):
            ag1_copy(b, g, t).start()

    def ag2(b, g):
        for t in range(1, first):
            ag1_copy(b, g, t).wait_recv()
        for t in range(1, rest):
            ag2_copy(b, g, t).start()

    def ag3(b, g):
        for t in range(1, rest):
            ag2_copy(b, g, t).wait_recv()
        for t in range(1, rest):
            ag3_copy(b, g, t).start()
        ag4_copy(b, g, 0).start()

    def ag4(b, g):
        for t in range(1, rest):
            ag3_copy(b, g, t).wait_recv()
            ag4_copy(b, g, t).start()

    def ag5(b, g):
        for t in range(rest):
            ag4_landing(b, g, t).wait_recv()
        lay_out(b, g)

    def ag_sent(b, g):
        for t in range(1, first):
            ag1_copy(b, g, t).wait_send()
        for t in range(1, rest):
            ag2_copy(b, g, t).wait_send()
            ag3_copy(b, g, t).wait_send()
        for t in range(rest):
            ag4_copy(b, g, t).wait_send()

    def lay_out(b, g):
        if g == DOWN:
            for j in range(n):
                for half in range(2):
                    begin = 4 * unit * j + 2 * unit * half
                    wdown[b, begin : begin + 2 * unit, :] = s_d[b, half, place(half, j)]
            return
        skip = TABLE if g == ATT else 0
        together = 16 // math.gcd(unit, 16)
        for half in range(2):
            for j in range(0, n, together):
                pieces = [stage[g][b, half, place(half, j + i)].astype(F32) for i in range(together)]
                for sub in range(2):
                    low = skip + sub * unit
                    block = jnp.concatenate([piece[low : low + unit] for piece in pieces], axis=0).astype(LOW)
                    part = 2 * half + sub
                    down = slice(unit * j, unit * (j + together))
                    if g == UP:
                        wup[b, down, part * width : (part + 1) * width] = block
                    elif part == 3:
                        wout[b, down, :] = block
                    else:
                        wqkv[b, down, part * width : (part + 1) * width] = block
            if g == ATT:
                total = s_a[b, half, 0][0:TABLE].astype(F32)
                for j in range(1, n):
                    total = total + s_a[b, half, j][0:TABLE].astype(F32)
                table[b, 8 * half : 8 * half + 8, :] = total[0:8]

    def rs0_copy(b, g):
        return remote(stage[g].at[b, 1 - core], r0[g], rs0_s.at[3 * b + g], rs0_r.at[3 * b + g], sibling)

    def rs1_copy(b, g, t):
        return remote(
            stage[g].at[b, core, slab_three((dig_three + t) % rest)], r1[g].at[b, t - 1],
            rs1_s.at[3 * b + g, t - 1], rs1_r.at[3 * b + g, t - 1], peer_three(t),
        )

    def rs2_copy(b, g, t):
        return remote(
            stage[g].at[b, core, slab_two(dig_three, (dig_two + t) % rest)], r2[g].at[b, t - 1],
            rs2_s.at[3 * b + g, t - 1], rs2_r.at[3 * b + g, t - 1], peer_two(t),
        )

    def rs3_copy(b, g, t):
        there = (dig_three * rest + dig_two) * first + (dig_a + t) % first
        return remote(
            stage[g].at[b, core, there], r3[g].at[b, t - 1],
            rs3_s.at[3 * b + g, t - 1], rs3_r.at[3 * b + g, t - 1], peer_first(t),
        )

    def rs4_copy(b, g):
        return remote(leaving[g], final[g].at[core], rs4_s.at[g], rs4_r.at[g], sibling)

    def rs0(b, g):
        if b == 0:
            pl.semaphore_wait(credit.at[g], 1)
        rs0_copy(b, g).start()

    def rs1(b, g):
        rs0_copy(b, g).wait_recv()

        @pl.loop(0, n)
        def _(p):
            stage[g][b, core, p] = stage[g][b, core, p] + r0[g][p]

        if b == 1:
            pl.semaphore_signal(credit.at[g], inc=1, device_id=sibling, device_id_type=pl.DeviceIdType.MESH)
        for t in range(1, rest):
            rs1_copy(b, g, t).start()

    def rs2(b, g):
        for t in range(1, rest):
            rs1_copy(b, g, t).wait_recv()

        @pl.loop(0, rest * first)
        def _(p):
            at = dig_three * rest * first + p
            total = stage[g][b, core, at].astype(F32)
            for t in range(1, rest):
                total = total + r1[g][b, t - 1, p].astype(F32)
            stage[g][b, core, at] = total.astype(LOW)

        for t in range(1, rest):
            rs2_copy(b, g, t).start()

    def rs3(b, g):
        for t in range(1, rest):
            rs2_copy(b, g, t).wait_recv()

        @pl.loop(0, first)
        def _(p):
            at = (dig_three * rest + dig_two) * first + p
            total = stage[g][b, core, at].astype(F32)
            for t in range(1, rest):
                total = total + r2[g][b, t - 1, p].astype(F32)
            stage[g][b, core, at] = total.astype(LOW)

        for t in range(1, first):
            rs3_copy(b, g, t).start()

    def rs4(b, g):
        for t in range(1, first):
            rs3_copy(b, g, t).wait_recv()
        total = stage[g][b, core, pos].astype(F32)
        for t in range(1, first):
            total = total + r3[g][b, t - 1].astype(F32)

        @pl.when(core == b)
        def _():
            final[g][core] = total

        @pl.when(core != b)
        def _():
            leaving[g][...] = total
            rs4_copy(b, g).start()

    def rs_sent(b, g):
        rs0_copy(b, g).wait_send()
        for t in range(1, rest):
            rs1_copy(b, g, t).wait_send()
            rs2_copy(b, g, t).wait_send()
        for t in range(1, first):
            rs3_copy(b, g, t).wait_send()

    def rows_of(i):
        return pl.ds(pl.multiple_of(i * rows, 16), rows)

    def ship_parts(kind, b, i):
        src, out = ((act, act_out), (ing, ing_out))[kind]
        q = 2 * kind + b
        rd = rows_of(i)
        near = pltpu.make_async_copy(src.at[rd], out.at[core, rd], ship_s.at[q, i])
        far = remote(src.at[rd], out.at[core, rd], ship_s.at[q, i], ship_r.at[q, i], sibling)
        return near, far

    def ship(kind, b, i):
        near, far = ship_parts(kind, b, i)

        @pl.when(core == b)
        def _():
            near.start()

        @pl.when(core != b)
        def _():
            far.start()

    def shipped(kind, b, i):
        near, far = ship_parts(kind, b, i)

        @pl.when(core == b)
        def _():
            near.wait()

        @pl.when(core != b)
        def _():
            far.wait_send()

    def landed(kind, b, i):
        out = (act_out, ing_out)[kind]
        q = 2 * kind + b
        ref = out.at[1 - core, rows_of(i)]

        @pl.when(core == b)
        def _():
            remote(ref, ref, ship_s.at[q, i], ship_r.at[q, i], sibling).wait_recv()

    def live(i):
        return jnp.where(i < counts[core, 0], 1.0, 0.0).astype(F32)

    def take_in(source, target):
        def coming(i):
            return pltpu.make_async_copy(source.at[core, i], arrived.at[i % 2], in_s.at[i % 2])

        coming(0).start()
        target[...] = jnp.zeros_like(target)
        for i in range(slots):
            if i + 1 < slots:
                coming(i + 1).start()
            coming(i).wait()
            target[pl.ds(rows * i, length), :] = arrived[i % 2]

    def far_copy(which, i, back):
        near, far = ((hid, hid_far), (slope, slope_far))[which]
        near, far = near.at[rows_of(i)], far.at[rows_of(i)]
        src, dst = (far, near) if back else (near, far)
        return pltpu.make_async_copy(src, dst, far_s.at[2 * int(back) + which, i])

    pairs = width // 128
    scale = head_dim ** -0.5
    lane = lax.broadcasted_iota(jnp.int32, (1, 128), 1)
    half_low = [(lane < head_dim).astype(LOW), (lane >= head_dim).astype(LOW)]
    half_f = [(lane < head_dim).astype(F32), (lane >= head_dim).astype(F32)]
    key_pad = jnp.where(lax.broadcasted_iota(jnp.int32, (1, rows), 1) < length, 0.0, -1e30).astype(F32)
    chunk = 256
    chunks = ff // chunk

    def vec(s, r):
        return table[s, r : r + 1, :]

    def up_bias(s, c):
        begin = c * chunk
        row, col = begin // width, begin % width
        if col + chunk <= width:
            return table[s, BU + row : BU + row + 1, col : col + chunk]
        a = table[s, BU + row : BU + row + 1, col:width]
        b = table[s, BU + row + 1 : BU + row + 2, 0 : chunk - (width - col)]
        return jnp.concatenate([a, b], axis=1)

    def add_vec(s, r, value):
        gtable[s, r : r + 1, :] += value

    def add_up_bias(s, c, value):
        begin = c * chunk
        row, col = begin // width, begin % width
        if col + chunk <= width:
            gtable[s, BU + row : BU + row + 1, col : col + chunk] += value
        else:
            cut = width - col
            gtable[s, BU + row : BU + row + 1, col:width] += value[:, :cut]
            gtable[s, BU + row + 1 : BU + row + 2, 0 : chunk - cut] += value[:, cut:]

    def attn_forward(s, x, rd, nrm_ref, qkv_ref, prob_ref, ctx_ref, pi):
        hat, rstd, mean = normalize(x)
        nrm = (hat * vec(s, G1) + vec(s, S1)).astype(LOW)
        nrm_ref[rd, :] = nrm
        q = (mm(nrm, wqkv[s, :, 0:width]) + vec(s, BQ)).astype(LOW)
        k = mm(nrm, wqkv[s, :, width : 2 * width]).astype(LOW)
        v = (mm(nrm, wqkv[s, :, 2 * width :]) + vec(s, BV)).astype(LOW)
        qkv_ref[rd, 0:width] = q
        qkv_ref[rd, width : 2 * width] = k
        qkv_ref[rd, 2 * width :] = v
        parts = []
        for p in range(pairs):
            cols = slice(128 * p, 128 * p + 128)
            total = None
            for j in range(2):
                scores = mm_right(q[:, cols], k[:, cols] * half_low[j]) + key_pad
                top = jnp.max(scores, axis=-1, keepdims=True)
                e = jnp.exp2((scores - top) * (scale * 1.4426950408889634))
                pr = (e * (1.0 / jnp.sum(e, axis=-1, keepdims=True))).astype(LOW)
                prob_ref[pi, 2 * p + j] = pr
                part = mm(pr, v[:, cols] * half_low[j])
                total = part if total is None else total + part
            parts.append(total.astype(LOW))
        context = jnp.concatenate(parts, axis=1)
        ctx_ref[rd, :] = context
        return x + mm(context, wout[s]) + vec(s, BO), rstd, mean

    def ff_forward(s, after, rd, srd, hat_ref, nrm_ref):
        hat, rstd, _ = normalize(after)
        hat_ref[srd, :] = hat.astype(LOW)
        nrm = (hat * vec(s, G2) + vec(s, S2)).astype(LOW)
        nrm_ref[rd, :] = nrm
        total = after + vec(s, BD)
        for c in range(chunks):
            cols = slice(chunk * c, chunk * c + chunk)
            pre = mm(nrm, wup[s, :, cols]) + up_bias(s, c)
            phi, slo = normal_parts(pre)
            h = (pre * phi).astype(LOW)
            hid[rd, cols] = h
            slope[rd, cols] = slo.astype(LOW)
            total = total + mm(h, wdown[s, cols, :])
        return total, rstd

    def ff_backward(s, g, rd, srd, hat_ref, rstd):
        g_low = g.astype(LOW)
        low_g[rd, :] = g_low
        add_vec(s, BD, colsum(g_low.astype(F32)))
        d_nrm = None
        for c in range(chunks):
            cols = slice(chunk * c, chunk * c + chunk)
            d_hid = mm_right(g_low, wdown[s, cols, :])
            d_pre = (d_hid * slope[rd, cols].astype(F32)).astype(LOW)
            slope[rd, cols] = d_pre
            add_up_bias(s, c, colsum(d_pre.astype(F32)))
            part = mm_right(d_pre, wup[s, :, cols])
            d_nrm = part if d_nrm is None else d_nrm + part
        hat = hat_ref[srd, :].astype(F32)
        add_vec(s, G2, colsum(d_nrm * hat))
        add_vec(s, S2, colsum(d_nrm))
        d_after = g + normalize_back(d_nrm * vec(s, G2), hat, rstd)
        low = d_after.astype(LOW)
        dal[rd, :] = low
        add_vec(s, BO, colsum(low.astype(F32)))
        return d_after

    def attn_backward(s, d_after, rd, x, mean, rstd, qkv_ref, prob_ref, ctx_ref, pi):
        d_ctx = mm_right(d_after.astype(LOW), wout[s]).astype(LOW)
        dq, dk, dv = [], [], []
        for p in range(pairs):
            cols = slice(128 * p, 128 * p + 128)
            q = qkv_ref[rd, 128 * p : 128 * p + 128]
            k = qkv_ref[rd, width + 128 * p : width + 128 * p + 128]
            v = qkv_ref[rd, 2 * width + 128 * p : 2 * width + 128 * p + 128]
            dc = d_ctx[:, cols]
            both = dc.astype(F32) * ctx_ref[rd, cols].astype(F32)
            sums = [None, None, None]
            for j in range(2):
                pr = prob_ref[pi, 2 * p + j]
                delta = jnp.sum(both * half_f[j], axis=-1, keepdims=True)
                d_prob = mm_right(dc, v * half_low[j])
                ds = (pr.astype(F32) * (d_prob - delta)).astype(LOW)
                new = [mm(ds, k * half_low[j]), mm_left(ds, q * half_low[j]), mm_left(pr, dc * half_low[j])]
                sums = [b if a is None else a + b for a, b in zip(sums, new)]
            dq.append((sums[0] * scale).astype(LOW))
            dk.append((sums[1] * scale).astype(LOW))
            dv.append(sums[2].astype(LOW))
        d_mixed = jnp.concatenate(dq + dk + dv, axis=1)
        qkv_ref[rd, :] = d_mixed
        add_vec(s, BQ, colsum(d_mixed[:, 0:width].astype(F32)))
        add_vec(s, BV, colsum(d_mixed[:, 2 * width :].astype(F32)))
        d_nrm = mm_right(d_mixed, wqkv[s])
        hat = (x - mean) * rstd
        add_vec(s, G1, colsum(d_nrm * hat))
        add_vec(s, S1, colsum(d_nrm))
        return d_after + normalize_back(d_nrm * vec(s, G1), hat, rstd)

    def grads_down(s):
        left_t[...] = low_g[...].T

        @pl.loop(0, 4)
        def _(c):
            cols = pl.ds(pl.multiple_of(c * width, 128), width)
            block = mm(left_t[...], hid[:, cols]).T
            for i in range(n // 4):
                for half in range(2):
                    begin = 4 * unit * i + 2 * unit * half
                    s_d[s, half, place(half, c * (n // 4) + i)] = block[begin : begin + 2 * unit].astype(LOW)

    def pair_out(ref, s, half, skip, one, two):
        for j in range(n):
            down = slice(unit * j, unit * (j + 1))
            piece = jnp.concatenate([one[down], two[down]], axis=0).astype(LOW)
            ref[s, half, place(half, j), skip : skip + 2 * unit] = piece

    def grads_up(s):
        left_t[...] = nrm2_of[s][...].T
        for half in range(2):
            one, two = [
                mm(left_t[...], slope[:, part * width : (part + 1) * width]) for part in (2 * half, 2 * half + 1)
            ]
            pair_out(s_u, s, half, 0, one, two)

    def grads_attn(s):
        ctx_s, nrm_s, mix_s = ((ctx, nrm1, qkv), (ctxb, nrm1b, qkvb))[s]
        left_t[...] = ctx_s[...].T
        four = mm(left_t[...], dal[...])
        left_t[...] = nrm_s[...].T
        three = mm(left_t[...], mix_s[:, 2 * width :])
        pair_out(s_a, s, 1, TABLE, three, four)
        one = mm(left_t[...], mix_s[:, 0:width])
        two = mm(left_t[...], mix_s[:, width : 2 * width])
        pair_out(s_a, s, 0, TABLE, one, two)
        for half in range(2):
            lines = gtable[s, 8 * half : 8 * half + 8, :]
            lines = jnp.concatenate([lines, jnp.zeros_like(lines)], axis=0).astype(LOW)
            for j in range(n):
                s_a[s, half, j, 0:TABLE] = lines

    nrm2_of = (nrm2, nrm2b)
    here = pl.ds(0, rows)

    barrier = pltpu.get_barrier_semaphore()
    greeted = [sibling] + [peer_first(t) for t in range(1, first)]
    greeted += [f(t) for f in (peer_two, peer_three) for t in range(1, rest)]
    for device in greeted:
        pl.semaphore_signal(barrier, inc=1, device_id=device, device_id_type=pl.DeviceIdType.MESH)
    pack_own()
    pl.semaphore_wait(barrier, len(greeted))

    for g in (ATT, UP, DOWN):
        ag0(g)
    ag1(0, ATT)
    gtable[...] = jnp.zeros_like(gtable)
    take_in(images, x_ref)
    ag2(0, ATT)
    ag1(0, UP)
    take_in(cotangent, ct_ref)
    ag3(0, ATT)
    ag2(0, UP)
    ag1(0, DOWN)
    ag4(0, ATT)
    ag3(0, UP)
    ag2(0, DOWN)
    ag1(1, ATT)
    ag5(0, ATT)

    def events(i, table_of):
        for at, todo in table_of.items():
            @pl.when(i == at)
            def _():
                for f, b, g in todo:
                    f(b, g)

    @pl.loop(0, slots)
    def attn_one(i):
        events(i, {
            2: [(ag4, 0, UP), (ag3, 0, DOWN), (ag2, 1, ATT), (ag1, 1, UP)],
            5: [(ag4, 0, DOWN), (ag3, 1, ATT), (ag2, 1, UP), (ag1, 1, DOWN)],
        })
        rd = rows_of(i)
        after, rstd1, mean1 = attn_forward(0, x_ref[rd, :].astype(F32), rd, nrm1, qkv, prob, ctx, i)
        after_ref[rd, :] = after
        rstds[rd, 0:1] = rstd1
        rstds[rd, 2:3] = mean1

    ag5(0, UP)
    ag5(0, DOWN)

    @pl.loop(0, slots)
    def ff_one(i):
        events(i, {
            2: [(ag4, 1, ATT), (ag3, 1, UP), (ag2, 1, DOWN)],
            5: [(ag4, 1, UP), (ag3, 1, DOWN)],
        })
        rd = rows_of(i)
        out, rstd2 = ff_forward(0, after_ref[rd, :], rd, rd, hat2, nrm2)
        far_copy(0, i, False).start()
        far_copy(1, i, False).start()
        act[rd, :] = (live(i) * out).astype(LOW)
        rstds[rd, 1:2] = rstd2
        ship(0, 0, i)

    ag4(1, DOWN)
    for g in (ATT, UP, DOWN):
        ag5(1, g)

    @pl.loop(0, slots)
    def both_two(i):
        rd = rows_of(i)
        x = act[rd, :].astype(F32)
        after, rstd1, mean1 = attn_forward(1, x, rd, nrm1b, qkvb, probb, ctxb, 0)
        far_copy(0, i, False).wait()
        far_copy(1, i, False).wait()
        out, rstd2 = ff_forward(1, after, rd, here, hat2b, nrm2b)
        shipped(0, 0, i)
        act[rd, :] = (live(i) * out).astype(LOW)
        ship(0, 1, i)
        g = live(i) * ct_ref[rd, :].astype(F32)
        d_after = ff_backward(1, g, rd, here, hat2b, rstd2)
        d_in = attn_backward(1, d_after, rd, x, mean1, rstd1, qkvb, probb, ctxb, 0)
        ing[rd, :] = d_in.astype(LOW)
        ship(1, 1, i)

    for b in range(2):
        for g in (ATT, UP, DOWN):
            ag_sent(b, g)
    for g in (ATT, UP, DOWN):
        ag0_copy(g).wait_send()

    grads_down(1)
    rs0(1, DOWN)

    @pl.loop(0, slots)
    def hid_back(i):
        far_copy(0, i, True).start()

    grads_up(1)
    rs0(1, UP)

    @pl.loop(0, slots)
    def slope_back(i):
        far_copy(1, i, True).start()

    rs1(1, DOWN)
    grads_attn(1)
    rs0(1, ATT)
    rs1(1, UP)
    rs2(1, DOWN)

    @pl.loop(0, slots)
    def ff_back_one(i):
        events(i, {
            1: [(rs1, 1, ATT)],
            2: [(rs2, 1, UP), (rs3, 1, DOWN)],
            4: [(rs2, 1, ATT), (rs3, 1, UP), (rs4, 1, DOWN)],
        })
        rd = rows_of(i)
        far_copy(1, i, True).wait()
        g = live(i) * ing[rd, :].astype(F32)
        after_ref[rd, :] = ff_backward(0, g, rd, rd, hat2, rstds[rd, 1:2])

    @pl.loop(0, slots)
    def hid_is_back(i):
        far_copy(0, i, True).wait()

    grads_down(0)
    rs0(0, DOWN)
    rs3(1, ATT)
    rs4(1, UP)
    grads_up(0)
    rs0(0, UP)
    rs1(0, DOWN)

    @pl.loop(0, slots)
    def attn_back_one(i):
        events(i, {
            0: [(rs1, 0, UP)],
            1: [(rs4, 1, ATT)],
            2: [(rs2, 0, DOWN)],
            3: [(rs2, 0, UP), (rs3, 0, DOWN)],
            5: [(rs3, 0, UP)],
        })
        rd = rows_of(i)
        x = x_ref[rd, :].astype(F32)
        d_in = attn_backward(0, after_ref[rd, :], rd, x, rstds[rd, 2:3], rstds[rd, 0:1], qkv, prob, ctx, i)
        shipped(1, 1, i)
        ing[rd, :] = d_in.astype(LOW)
        ship(1, 0, i)

    grads_attn(0)
    rs0(0, ATT)
    rs1(0, ATT)
    for g in (UP, DOWN):
        @pl.when(core == 0)
        def _():
            rs4_copy(1, g).wait_send()

        rs4(0, g)
    rs2(0, ATT)
    rs3(0, ATT)

    @pl.loop(0, slots)
    def all_out(i):
        shipped(0, 1, i)
        shipped(1, 0, i)
        for kind in range(2):
            for b in range(2):
                landed(kind, b, i)

    @pl.when(core == 0)
    def _():
        rs4_copy(1, ATT).wait_send()

    rs4(0, ATT)

    for g in (DOWN, UP, ATT):
        rs_sent(0, g)
        rs_sent(1, g)
        ref = final[g].at[1 - core]
        remote(ref, ref, rs4_s.at[g], rs4_r.at[g], sibling).wait_recv()

        @pl.when(core == 1)
        def _():
            rs4_copy(0, g).wait_send()


def output_kernel(
    n, f_a, f_u, f_d,
    o_g1, o_s1, o_qkv, o_qv, o_out, o_bo, o_g2, o_s2, o_up, o_bu, o_down, o_bd,
):
    unit, width = o_out.shape[1:]
    me = lax.axis_index("fsdp")
    for half in range(2):
        o_down[0, 2 * unit * half : 2 * unit * (half + 1), :] = f_d[half]
        for sub in range(2):
            part = 2 * half + sub
            cols = slice(part * width, (part + 1) * width)
            o_up[0, :, cols] = f_u[half, unit * sub : unit * (sub + 1), :]
            piece = f_a[half, TABLE + unit * sub : TABLE + unit * (sub + 1), :]
            if part == 3:
                o_out[0] = piece
            else:
                o_qkv[0, :, cols] = piece
    table = jnp.concatenate([f_a[0, 0:8, :], f_a[1, 0:8, :]], axis=0)
    for row, out in (
        (G1, o_g1), (S1, o_s1), (BO, o_bo), (G2, o_g2), (S2, o_s2), (BD, o_bd), (BQ, o_qv), (BU, o_bu)
    ):
        part = out.shape[1]
        total = None
        for i in range(part * n // width):
            lanes = lax.broadcasted_iota(jnp.int32, (width, part), 0) + width * i
            here = lax.broadcasted_iota(jnp.int32, (width, part), 1) + part * me
            pick = jnp.where(lanes == here, 1.0, 0.0).astype(F32)
            value = jnp.dot(
                table[row + i : row + i + 1], pick, preferred_element_type=F32, precision=lax.Precision.HIGHEST
            )
            total = value if total is None else total + value
        out[...] = total


def local(
    images, cotangent, counts,
    ln1_gain, ln1_bias, w_qkv, b_qv, w_out, b_out, ln2_gain, ln2_bias, w_up, b_up, w_down, b_down,
):
    micro_count, slots, length, width = images.shape
    ff = w_up.shape[2]
    rows = -(-length // 16) * 16
    n = lax.axis_size("fsdp")
    unit = width // n
    first, rest = radices(n)
    total = slots * rows
    head_dim = width // HEADS

    def vm(*shape, kind=LOW):
        return pltpu.VMEM(shape, kind)

    tall = [TABLE + 2 * unit, 2 * unit, 2 * unit]
    dma = lambda *shape: pltpu.SemaphoreType.DMA(shape)
    outs = [((2, total, width), LOW), ((2, total, width), LOW)]
    outs += [((2, r, width), F32) for r in tall] + [((total, ff), LOW), ((total, ff), LOW)]
    scratch = [
        vm(total, width), vm(total, width), vm(2, length, width),
        vm(2, TABLE + 2 * unit, width), vm(2, 2 * unit, width), vm(2, 2 * unit, width),
        vm(2, width, 3 * width), vm(2, width, width), vm(2, width, ff), vm(2, ff, width),
        vm(2, TABLE, width, kind=F32), vm(2, TABLE, width, kind=F32),
        vm(total, width), vm(total, width), vm(total, width, kind=F32),
        vm(total, width), vm(total, 3 * width), vm(slots, HEADS, rows, rows), vm(total, width),
        vm(total, width), vm(total, width), vm(total, 3, kind=F32),
        vm(total, ff), vm(total, ff),
        vm(total, width), vm(total, 3 * width), vm(total, width), vm(total, width), vm(1, HEADS, rows, rows),
        vm(rows, width), vm(total, width), vm(total, width), vm(width, total),
    ]
    scratch += [vm(2, 2, n, r, width) for r in tall]
    scratch += [vm(n, r, width) for r in tall]
    scratch += [vm(2, rest - 1, rest * first, r, width) for r in tall]
    scratch += [vm(2, rest - 1, first, r, width) for r in tall]
    scratch += [vm(2, first - 1, r, width) for r in tall]
    scratch += [vm(r, width, kind=F32) for r in tall]
    scratch += [dma(2), dma(4, slots), dma(4, slots), dma(4, slots), dma(3), dma(3)]
    scratch += [dma(6, first - 1)] * 2 + [dma(6, rest - 1)] * 4 + [dma(6, rest)] * 2
    scratch += [dma(6)] * 2 + [dma(6, rest - 1)] * 4 + [dma(6, first - 1)] * 2 + [dma(3)] * 2
    scratch += [pltpu.SemaphoreType.REGULAR((3,))]
    dims = (slots, length, rows, width, ff, head_dim, n)
    vmem = pl.BlockSpec(memory_space=pltpu.VMEM)
    hbm = pl.BlockSpec(memory_space=pltpu.HBM)
    acts, ings, f_a, f_u, f_d, _, _ = pl.pallas_call(
        functools.partial(whole_kernel, dims),
        out_shape=[jax.ShapeDtypeStruct(*o) for o in outs],
        in_specs=[hbm, hbm, pl.BlockSpec(memory_space=pltpu.SMEM)] + [vmem] * 12,
        out_specs=[hbm, hbm] + [vmem] * 3 + [hbm, hbm],
        scratch_shapes=scratch,
        compiler_params=pltpu.CompilerParams(
            vmem_limit_bytes=(64 << 20) - (96 << 10), collective_id=0, has_side_effects=True
        ),
    )(
        images, cotangent, counts, ln1_gain, ln1_bias, b_out, ln2_gain, ln2_bias, b_down, b_qv, b_up,
        w_qkv, w_out, w_up, w_down,
    )

    params = (
        ln1_gain, ln1_bias, w_qkv, b_qv, w_out, b_out, ln2_gain, ln2_bias, w_up, b_up, w_down, b_down
    )
    grads = pl.pallas_call(
        functools.partial(output_kernel, n),
        out_shape=[jax.ShapeDtypeStruct(p.shape, F32) for p in params],
        in_specs=[vmem] * 3,
        out_specs=[vmem] * len(params),
    )(f_a, f_u, f_d)

    def images_of(value):
        return value.reshape(1, 2, slots, rows, width)[:, :, :, :length]

    return (images_of(acts), images_of(ings), *grads)


def solution(mesh):
    split = P("section", "fsdp")
    cube = P("section", "fsdp", None)
    image = P(None, "fsdp", None, None)
    result = P("section", None, "fsdp", None, None)
    params = (split, split, cube, split, cube, split, split, split, cube, split, cube, split)
    return jax.shard_map(
        local,
        mesh=mesh,
        in_specs=(image, image, P(None, "fsdp")) + params,
        out_specs=(result, result) + params,
        check_vma=False,
    )
```

```python
import functools
import math

import jax
import jax.numpy as jnp
from jax import lax
from jax.experimental import pallas as pl
from jax.experimental.pallas import tpu as pltpu
from jax.sharding import PartitionSpec as P

HEADS = 6
EPS = 1e-06
F32 = jnp.float32
LOW = jnp.bfloat16

G1, S1, BO, G2, S2, BD, BQ, BV, BU = 0, 1, 2, 3, 4, 5, 6, 7, 8
TABLE = 16
ATT, UP, DOWN, TAB = 0, 1, 2, 3


def radices(n):
    rest = max(r for r in range(1, n + 1) if r * r * r <= n and n % (r * r) == 0)
    return n // (rest * rest), rest


def mm(left, right):
    return jnp.dot(left, right, preferred_element_type=F32)


def mm_right(left, right):
    return lax.dot_general(left, right, (((1,), (1,)), ((), ())), preferred_element_type=F32)


def mm_left(left, right):
    return lax.dot_general(left, right, (((0,), (0,)), ((), ())), preferred_element_type=F32)


def normal_parts(pre):
    decay = jnp.exp2(pre * pre * (-0.5 * 1.4426950408889634))
    t = 1.0 / (1.0 + (0.3275911 * 0.7071067811865476) * jnp.abs(pre))
    poly = 0.5 * 1.061405429
    for term in (-1.453152027, 1.421413741, -0.284496736, 0.254829592):
        poly = poly * t + 0.5 * term
    tail = poly * t * decay
    phi = jnp.where(pre < 0.0, tail, 1.0 - tail)
    slope = phi + pre * (decay * 0.3989422804014327)
    return phi, slope


def normalize(value):
    mean = jnp.mean(value, axis=-1, keepdims=True)
    center = value - mean
    rstd = lax.rsqrt(jnp.mean(center * center, axis=-1, keepdims=True) + EPS)
    return center * rstd, rstd, mean


def normalize_back(d_hat, hat, rstd):
    mean_one = jnp.mean(d_hat, axis=-1, keepdims=True)
    mean_two = jnp.mean(d_hat * hat, axis=-1, keepdims=True)
    return rstd * (d_hat - mean_one - hat * mean_two)


def colsum(value):
    return jnp.sum(value, axis=0, keepdims=True)


def whole_kernel(dims, *refs):
    slots, length, rows, width, ff, head_dim, n = dims
    (
        images, cotangent, counts, v_g1, v_s1, v_bo, v_g2, v_s2, v_bd, v_qv, v_up, a_qkv, a_out, a_up, a_down,
        act_out, ing_out, f_a, f_u, f_d, f_t, hid_far, slope_far,
        x_ref, ct_ref, arrived, pack_a, pack_u, pack_d, pack_t,
        wqkv, wout, wup, wdown, table, gtable, rep_one, rep_two, rep_four,
        act, out_two, ing, after_ref, nrm1, qkv, prob, ctx, hat2, nrm2, rstds,
        hid, slope,
        nrm1b, qkvb, ctxb, nrm2b, probb, hat2b, dal, low_g, left_t,
        s_a, s_u, s_d, s_t, r0_a, r0_u, r0_d, r0_t, r1_a, r1_u, r1_d, r1_t, r2_a, r2_u, r2_d, r2_t,
        r3_a, r3_u, r3_d, r3_t,
        in_s, ship_s, ship_r, far_s, ag1_s, ag1_r, ag2_s, ag2_r, ag3_s, ag3_r, ag4_s, ag4_r,
        rs0_s, rs0_r, rs1_s, rs1_r, rs2_s, rs2_r, rs3_s, rs3_r, credit,
    ) = refs
    groups = (ATT, UP, DOWN, TAB)
    pack = (pack_a, pack_u, pack_d, pack_t)
    stage = (s_a, s_u, s_d, s_t)
    r0, r1, r2 = (r0_a, r0_u, r0_d, r0_t), (r1_a, r1_u, r1_d, r1_t), (r2_a, r2_u, r2_d, r2_t)
    r3, final = (r3_a, r3_u, r3_d, r3_t), (f_a, f_u, f_d, f_t)

    first, rest = radices(n)
    unit = width // n
    core = lax.axis_index("section")
    me = lax.axis_index("fsdp")
    dig_a, dig_b, dig_c = me // (rest * rest), (me // rest) % rest, me % rest
    dig_three, dig_two = dig_c + core * (dig_b - dig_c), dig_b + core * (dig_c - dig_b)
    step_three, step_two = 1 + core * (rest - 1), rest - core * (rest - 1)
    pos = (dig_three * rest + dig_two) * first + dig_a
    pos_of = ((dig_c * rest + dig_b) * first + dig_a, (dig_b * rest + dig_c) * first + dig_a)
    sibling = {"section": 1 - core}

    def place(half, j):
        a, b, c = j // (rest * rest), (j // rest) % rest, j % rest
        return ((c * rest + b) if half == 0 else (b * rest + c)) * first + a

    def peer_first(t):
        return {"fsdp": me + ((dig_a + t) % first - dig_a) * (rest * rest)}

    def peer_two(t):
        return {"fsdp": me + ((dig_two + t) % rest - dig_two) * step_two}

    def peer_three(t):
        return {"fsdp": me + ((dig_three + t) % rest - dig_three) * step_three}

    def remote(src, dst, s_sem, r_sem, device):
        return pltpu.make_async_remote_copy(
            src_ref=src, dst_ref=dst, send_sem=s_sem, recv_sem=r_sem, device_id=device,
            device_id_type=pl.DeviceIdType.MESH,
        )

    def slab_two(three, two):
        return pl.ds((three * rest + two) * first, first)

    def slab_three(three):
        return pl.ds(three * rest * first, rest * first)

    def fill_repeats():
        for ref in (rep_one, rep_two, rep_four):
            part = ref.shape[0]
            lanes = lax.broadcasted_iota(jnp.int32, ref.shape, 1).astype(F32)
            line = lax.broadcasted_iota(jnp.int32, ref.shape, 0).astype(F32)
            rest_of = lanes - part * jnp.floor((lanes + 0.5) * (1.0 / part))
            ref[...] = jnp.where(jnp.abs(rest_of - line) < 0.5, 1.0, 0.0).astype(LOW)

    def own_lanes(part):
        shape = (n, part * n)
        lanes = lax.broadcasted_iota(jnp.int32, shape, 1)
        begin = lax.broadcasted_iota(jnp.int32, shape, 0) * part
        return (lanes >= begin) & (lanes < begin + part)

    shares = (
        ((G1, unit, rep_one), (S1, unit, rep_one), (BO, unit, rep_one), (G2, unit, rep_one), (S2, unit, rep_one),
         (BD, unit, rep_one), (BQ, 2 * unit, rep_two)),
        ((BU, 4 * unit, rep_four),),
    )

    def table_in(b):
        for half in range(2):
            lines = jnp.concatenate([s_t[b, half, place(half, j)] for j in range(n)], axis=0)
            begin = 0
            for row, part, ref in shares[half]:
                spread = mm(lines[:, begin : begin + part].astype(LOW), ref[...])
                line = colsum(jnp.where(own_lanes(part), spread, 0.0))
                for i in range(part * n // width):
                    table[b, row + i : row + i + 1, :] = line[:, width * i : width * (i + 1)]
                begin += part

    def table_out(b):
        for half in range(2):
            parts, begin = [], 0
            for row, part, ref in shares[half]:
                count = part * n // width
                line = jnp.concatenate([gtable[b, row + i : row + i + 1, :] for i in range(count)], axis=1)
                parts.append(mm_right(jnp.where(own_lanes(part), line, 0.0).astype(LOW), ref[...]))
                begin += part
            parts.append(jnp.zeros((n, width - begin), F32))
            lines = jnp.concatenate(parts, axis=1)
            for j in range(n):
                s_t[b, half, place(half, j)] = lines[j : j + 1]

    def pack_own():
        for half in range(2):
            vectors = ((v_g1, v_s1, v_bo, v_g2, v_s2, v_bd, v_qv), (v_up,))[half]
            lines = [vector[...].astype(F32) for vector in vectors]
            lines.append(jnp.zeros((1, width - sum(line.shape[1] for line in lines)), F32))
            pack_t[half] = jnp.concatenate(lines, axis=1)
            for ref in (pack_a, pack_u):
                both = []
                for part in (2 * half, 2 * half + 1):
                    if ref is pack_u:
                        both.append(a_up[0, :, part * width : (part + 1) * width])
                    elif part == 3:
                        both.append(a_out[0])
                    else:
                        both.append(a_qkv[0, :, part * width : (part + 1) * width])
                ref[half] = jnp.concatenate([value.astype(F32) for value in both], axis=0).astype(LOW)
            pack_d[half] = a_down[0, 2 * unit * half : 2 * unit * (half + 1), :]

    def at(b, g):
        return len(groups) * b + g

    def ag1_copy(b, g, half, t):
        device = {"section": half, **peer_first(t)} if t else sibling
        return remote(
            pack[g].at[half], stage[g].at[b, half, pos_of[half]],
            ag1_s.at[g, half, t], ag1_r.at[at(b, g), t], device,
        )

    def ag1_landing(b, g, t):
        ref = stage[g].at[b, core, (dig_three * rest + dig_two) * first + (dig_a + first - t) % first]
        return remote(ref, ref, ag1_s.at[g, 0, t], ag1_r.at[at(b, g), t], sibling)

    def ag2_copy(b, g, t):
        ref = stage[g].at[b, core, slab_two(dig_three, dig_two)]
        return remote(ref, ref, ag2_s.at[at(b, g), t - 1], ag2_r.at[at(b, g), t - 1], peer_two(t))

    def ag3_copy(b, g, t):
        ref = stage[g].at[b, core, slab_three(dig_three)]
        return remote(ref, ref, ag3_s.at[at(b, g), t - 1], ag3_r.at[at(b, g), t - 1], peer_three(t))

    def ag4_copy(b, g, t):
        ref = stage[g].at[b, core, slab_three((dig_three + rest - t) % rest)]
        return remote(ref, ref, ag4_s.at[at(b, g), t], ag4_r.at[at(b, g), t], sibling)

    def ag4_landing(b, g, t):
        ref = stage[g].at[b, 1 - core, slab_three((dig_two + rest - t) % rest)]
        return remote(ref, ref, ag4_s.at[at(b, g), t], ag4_r.at[at(b, g), t], sibling)

    def ag1(b, g):
        @pl.when(core == b)
        def _():
            for t in range(1, first):
                for half in range(2):
                    ag1_copy(b, g, half, t).start()
            ag1_copy(b, g, 1 - b, 0).start()
            stage[g][b, b, pos] = pack[g][b]

    def ag2(b, g):
        for t in range(1, first):
            ag1_landing(b, g, t).wait_recv()

        @pl.when(core != b)
        def _():
            ag1_landing(b, g, 0).wait_recv()

        for t in range(1, rest):
            ag2_copy(b, g, t).start()

    def ag3(b, g):
        for t in range(1, rest):
            ag2_copy(b, g, t).wait_recv()
        for t in range(1, rest):
            ag3_copy(b, g, t).start()
        ag4_copy(b, g, 0).start()

    def ag4(b, g):
        for t in range(1, rest):
            ag3_copy(b, g, t).wait_recv()
            ag4_copy(b, g, t).start()

    def ag5(b, g):
        for t in range(rest):
            ag4_landing(b, g, t).wait_recv()
        lay_out(b, g)

    def ag_sent(b, g):
        @pl.when(core == b)
        def _():
            for t in range(1, first):
                for half in range(2):
                    ag1_copy(b, g, half, t).wait_send()
            ag1_copy(b, g, 1 - b, 0).wait_send()

        for t in range(1, rest):
            ag2_copy(b, g, t).wait_send()
            ag3_copy(b, g, t).wait_send()
        for t in range(rest):
            ag4_copy(b, g, t).wait_send()

    def lay_out(b, g):
        if g == TAB:
            table_in(b)
            return
        if g == DOWN:
            for j in range(n):
                for half in range(2):
                    begin = 4 * unit * j + 2 * unit * half
                    wdown[b, begin : begin + 2 * unit, :] = s_d[b, half, place(half, j)]
            return
        together = 16 // math.gcd(unit, 16)
        for half in range(2):
            for j in range(0, n, together):
                pieces = [stage[g][b, half, place(half, j + i)].astype(F32) for i in range(together)]
                for sub in range(2):
                    low = sub * unit
                    block = jnp.concatenate([piece[low : low + unit] for piece in pieces], axis=0).astype(LOW)
                    part = 2 * half + sub
                    down = slice(unit * j, unit * (j + together))
                    if g == UP:
                        wup[b, down, part * width : (part + 1) * width] = block
                    elif part == 3:
                        wout[b, down, :] = block
                    else:
                        wqkv[b, down, part * width : (part + 1) * width] = block

    def rs0_copy(b, g):
        return remote(stage[g].at[b, 1 - core], r0[g], rs0_s.at[at(b, g)], rs0_r.at[at(b, g)], sibling)

    def rs1_copy(b, g, t):
        return remote(
            stage[g].at[b, core, slab_three((dig_three + t) % rest)], r1[g].at[b, t - 1],
            rs1_s.at[at(b, g), t - 1], rs1_r.at[at(b, g), t - 1], peer_three(t),
        )

    def rs2_copy(b, g, t):
        return remote(
            stage[g].at[b, core, slab_two(dig_three, (dig_two + t) % rest)], r2[g].at[b, t - 1],
            rs2_s.at[at(b, g), t - 1], rs2_r.at[at(b, g), t - 1], peer_two(t),
        )

    def rs3_copy(b, g, t):
        there = (dig_three * rest + dig_two) * first + (dig_a + t) % first
        device = {"section": b, **peer_first(t)} if t else sibling
        return remote(
            stage[g].at[b, core, there], r3[g].at[core, t], rs3_s.at[at(b, g), t], rs3_r.at[g, core, t], device
        )

    def rs0(b, g):
        if b == 0:
            pl.semaphore_wait(credit.at[g], 1)
        rs0_copy(b, g).start()

    def rs1(b, g):
        rs0_copy(b, g).wait_recv()

        @pl.loop(0, n)
        def _(p):
            stage[g][b, core, p] = stage[g][b, core, p] + r0[g][p]

        if b == 1:
            pl.semaphore_signal(credit.at[g], inc=1, device_id=sibling, device_id_type=pl.DeviceIdType.MESH)
        for t in range(1, rest):
            rs1_copy(b, g, t).start()

    def rs2(b, g):
        for t in range(1, rest):
            rs1_copy(b, g, t).wait_recv()

        @pl.loop(0, rest * first)
        def _(p):
            here = dig_three * rest * first + p
            total = stage[g][b, core, here].astype(F32)
            for t in range(1, rest):
                total = total + r1[g][b, t - 1, p].astype(F32)
            stage[g][b, core, here] = total.astype(stage[g].dtype)

        for t in range(1, rest):
            rs2_copy(b, g, t).start()

    def rs3(b, g):
        for t in range(1, rest):
            rs2_copy(b, g, t).wait_recv()

        @pl.loop(0, first)
        def _(p):
            here = (dig_three * rest + dig_two) * first + p
            total = stage[g][b, core, here].astype(F32)
            for t in range(1, rest):
                total = total + r2[g][b, t - 1, p].astype(F32)
            stage[g][b, core, here] = total.astype(stage[g].dtype)

        for t in range(1, first):
            rs3_copy(b, g, t).start()

        @pl.when(core != b)
        def _():
            rs3_copy(b, g, 0).start()

    def rs4(b, g):
        @pl.when(core == b)
        def _():
            for half in range(2):
                begin = int(half == b)
                for t in range(begin, first):
                    ref = r3[g].at[half, t]
                    remote(ref, ref, rs3_s.at[at(b, g), t], rs3_r.at[g, half, t], sibling).wait_recv()
                total = stage[g][b, b, pos].astype(F32) if half == b else None
                for t in range(begin, first):
                    value = r3[g][half, t].astype(F32)
                    total = value if total is None else total + value
                final[g][half] = total

    def rs_sent(b, g):
        rs0_copy(b, g).wait_send()
        for t in range(1, rest):
            rs1_copy(b, g, t).wait_send()
            rs2_copy(b, g, t).wait_send()
        for t in range(1, first):
            rs3_copy(b, g, t).wait_send()

        @pl.when(core != b)
        def _():
            rs3_copy(b, g, 0).wait_send()

    def rows_of(i):
        return pl.ds(pl.multiple_of(i * rows, 16), rows)

    def ship_parts(kind, b, i):
        src, out = ((out_two if b else act, act_out), (ing, ing_out))[kind]
        q = 2 * kind + b
        rd = rows_of(i)
        near = pltpu.make_async_copy(src.at[rd], out.at[core, rd], ship_s.at[q, i])
        far = remote(src.at[rd], out.at[core, rd], ship_s.at[q, i], ship_r.at[q, i], sibling)
        return near, far

    def ship(kind, b, i):
        near, far = ship_parts(kind, b, i)

        @pl.when(core == b)
        def _():
            near.start()

        @pl.when(core != b)
        def _():
            far.start()

    def shipped(kind, b, i):
        near, far = ship_parts(kind, b, i)

        @pl.when(core == b)
        def _():
            near.wait()

        @pl.when(core != b)
        def _():
            far.wait_send()

    def landed(kind, b, i):
        out = (act_out, ing_out)[kind]
        q = 2 * kind + b
        ref = out.at[1 - core, rows_of(i)]

        @pl.when(core == b)
        def _():
            remote(ref, ref, ship_s.at[q, i], ship_r.at[q, i], sibling).wait_recv()

    def live(i):
        return jnp.where(i < counts[0, core], 1.0, 0.0).astype(F32)

    def take_in(source, target):
        def coming(i):
            return pltpu.make_async_copy(source.at[core, i], arrived.at[i % 2], in_s.at[i % 2])

        coming(0).start()
        target[...] = jnp.zeros_like(target)
        for i in range(slots):
            if i + 1 < slots:
                coming(i + 1).start()
            coming(i).wait()
            target[pl.ds(rows * i, length), :] = arrived[i % 2]

    def far_copy(which, i, back):
        near, far = ((hid, hid_far), (slope, slope_far))[which]
        near, far = near.at[rows_of(i)], far.at[rows_of(i)]
        src, dst = (far, near) if back else (near, far)
        return pltpu.make_async_copy(src, dst, far_s.at[2 * int(back) + which, i])

    pairs = width // 128
    scale = head_dim ** -0.5
    lane = lax.broadcasted_iota(jnp.int32, (1, 128), 1)
    half_low = [(lane < head_dim).astype(LOW), (lane >= head_dim).astype(LOW)]
    half_f = [(lane < head_dim).astype(F32), (lane >= head_dim).astype(F32)]
    key_pad = jnp.where(lax.broadcasted_iota(jnp.int32, (1, rows), 1) < length, 0.0, -1e30).astype(F32)
    chunk = 256
    chunks = ff // chunk

    def vec(s, r):
        return table[s, r : r + 1, :]

    def up_bias(s, c):
        begin = c * chunk
        row, col = begin // width, begin % width
        if col + chunk <= width:
            return table[s, BU + row : BU + row + 1, col : col + chunk]
        a = table[s, BU + row : BU + row + 1, col:width]
        b = table[s, BU + row + 1 : BU + row + 2, 0 : chunk - (width - col)]
        return jnp.concatenate([a, b], axis=1)

    def add_vec(s, r, value):
        gtable[s, r : r + 1, :] += value

    def add_up_bias(s, c, value):
        begin = c * chunk
        row, col = begin // width, begin % width
        if col + chunk <= width:
            gtable[s, BU + row : BU + row + 1, col : col + chunk] += value
        else:
            cut = width - col
            gtable[s, BU + row : BU + row + 1, col:width] += value[:, :cut]
            gtable[s, BU + row + 1 : BU + row + 2, 0 : chunk - cut] += value[:, cut:]

    def attn_forward(s, x, hat, rd, nrm_ref, qkv_ref, prob_ref, ctx_ref, pi):
        nrm = (hat * vec(s, G1) + vec(s, S1)).astype(LOW)
        nrm_ref[rd, :] = nrm
        q = (mm(nrm, wqkv[s, :, 0:width]) + vec(s, BQ)).astype(LOW)
        k = mm(nrm, wqkv[s, :, width : 2 * width]).astype(LOW)
        v = (mm(nrm, wqkv[s, :, 2 * width :]) + vec(s, BV)).astype(LOW)
        qkv_ref[rd, 0:width] = q
        qkv_ref[rd, width : 2 * width] = k
        qkv_ref[rd, 2 * width :] = v
        parts = []
        for p in range(pairs):
            cols = slice(128 * p, 128 * p + 128)
            total = None
            for j in range(2):
                scores = mm_right(q[:, cols], k[:, cols] * half_low[j]) + key_pad
                top = jnp.max(scores, axis=-1, keepdims=True)
                e = jnp.exp2((scores - top) * (scale * 1.4426950408889634))
                pr = (e * (1.0 / jnp.sum(e, axis=-1, keepdims=True))).astype(LOW)
                prob_ref[pi, 2 * p + j] = pr
                part = mm(pr, v[:, cols] * half_low[j])
                total = part if total is None else total + part
            parts.append(total.astype(LOW))
        context = jnp.concatenate(parts, axis=1)
        ctx_ref[rd, :] = context
        return x + mm(context, wout[s]) + vec(s, BO)

    def ff_forward(s, after, rd, srd, hat_ref, nrm_ref):
        hat, rstd, _ = normalize(after)
        hat_ref[srd, :] = hat.astype(LOW)
        nrm = (hat * vec(s, G2) + vec(s, S2)).astype(LOW)
        nrm_ref[rd, :] = nrm
        total = after + vec(s, BD)
        for c in range(chunks):
            cols = slice(chunk * c, chunk * c + chunk)
            pre = mm(nrm, wup[s, :, cols]) + up_bias(s, c)
            phi, slo = normal_parts(pre)
            h = (pre * phi).astype(LOW)
            hid[rd, cols] = h
            slope[rd, cols] = slo.astype(LOW)
            total = total + mm(h, wdown[s, cols, :])
        return total, rstd

    def ff_backward(s, g, rd, srd, hat_ref, rstd):
        g_low = g.astype(LOW)
        low_g[rd, :] = g_low
        add_vec(s, BD, colsum(g_low.astype(F32)))
        d_nrm = None
        for c in range(chunks):
            cols = slice(chunk * c, chunk * c + chunk)
            d_hid = mm_right(g_low, wdown[s, cols, :])
            d_pre = (d_hid * slope[rd, cols].astype(F32)).astype(LOW)
            slope[rd, cols] = d_pre
            add_up_bias(s, c, colsum(d_pre.astype(F32)))
            part = mm_right(d_pre, wup[s, :, cols])
            d_nrm = part if d_nrm is None else d_nrm + part
        hat = hat_ref[srd, :].astype(F32)
        add_vec(s, G2, colsum(d_nrm * hat))
        add_vec(s, S2, colsum(d_nrm))
        d_after = g + normalize_back(d_nrm * vec(s, G2), hat, rstd)
        low = d_after.astype(LOW)
        dal[rd, :] = low
        add_vec(s, BO, colsum(low.astype(F32)))
        return d_after

    def attn_backward(s, rd, qkv_ref, prob_ref, ctx_ref, pi):
        d_ctx = mm_right(dal[rd, :], wout[s]).astype(LOW)
        dq, dk, dv = [], [], []
        for p in range(pairs):
            cols = slice(128 * p, 128 * p + 128)
            q = qkv_ref[rd, 128 * p : 128 * p + 128]
            k = qkv_ref[rd, width + 128 * p : width + 128 * p + 128]
            v = qkv_ref[rd, 2 * width + 128 * p : 2 * width + 128 * p + 128]
            dc = d_ctx[:, cols]
            both = dc.astype(F32) * ctx_ref[rd, cols].astype(F32)
            sums = [None, None, None]
            for j in range(2):
                pr = prob_ref[pi, 2 * p + j]
                delta = jnp.sum(both * half_f[j], axis=-1, keepdims=True)
                d_prob = mm_right(dc, v * half_low[j])
                ds = (pr.astype(F32) * (d_prob - delta)).astype(LOW)
                new = [mm(ds, k * half_low[j]), mm_left(ds, q * half_low[j]), mm_left(pr, dc * half_low[j])]
                sums = [b if a is None else a + b for a, b in zip(sums, new)]
            dq.append((sums[0] * scale).astype(LOW))
            dk.append((sums[1] * scale).astype(LOW))
            dv.append(sums[2].astype(LOW))
        d_mixed = jnp.concatenate(dq + dk + dv, axis=1)
        qkv_ref[rd, :] = d_mixed
        add_vec(s, BQ, colsum(d_mixed[:, 0:width].astype(F32)))
        add_vec(s, BV, colsum(d_mixed[:, 2 * width :].astype(F32)))

    def input_backward(s, d_after, rd, x, mean, rstd, qkv_ref):
        d_nrm = mm_right(qkv_ref[rd, :], wqkv[s])
        hat = (x - mean) * rstd
        add_vec(s, G1, colsum(d_nrm * hat))
        add_vec(s, S1, colsum(d_nrm))
        return d_after + normalize_back(d_nrm * vec(s, G1), hat, rstd)

    def grads_down(s):
        left_t[...] = low_g[...].T

        @pl.loop(0, 4)
        def _(c):
            cols = pl.ds(pl.multiple_of(c * width, 128), width)
            block = mm(left_t[...], hid[:, cols]).T
            for i in range(n // 4):
                for half in range(2):
                    begin = 4 * unit * i + 2 * unit * half
                    s_d[s, half, place(half, c * (n // 4) + i)] = block[begin : begin + 2 * unit].astype(LOW)

    def pair_out(ref, s, half, one, two):
        for j in range(n):
            down = slice(unit * j, unit * (j + 1))
            piece = jnp.concatenate([one[down], two[down]], axis=0).astype(LOW)
            ref[s, half, place(half, j)] = piece

    def grads_up(s):
        left_t[...] = nrm2_of[s][...].T
        for half in range(2):
            one, two = [
                mm(left_t[...], slope[:, part * width : (part + 1) * width]) for part in (2 * half, 2 * half + 1)
            ]
            pair_out(s_u, s, half, one, two)

    def grads_attn(s):
        ctx_s, nrm_s, mix_s = ((ctx, nrm1, qkv), (ctxb, nrm1b, qkvb))[s]
        left_t[...] = ctx_s[...].T
        four = mm(left_t[...], dal[...])
        left_t[...] = nrm_s[...].T
        three = mm(left_t[...], mix_s[:, 2 * width :])
        pair_out(s_a, s, 1, three, four)
        one = mm(left_t[...], mix_s[:, 0:width])
        two = mm(left_t[...], mix_s[:, width : 2 * width])
        pair_out(s_a, s, 0, one, two)

    nrm2_of = (nrm2, nrm2b)
    here = pl.ds(0, rows)

    barrier = pltpu.get_barrier_semaphore()
    greeted = [sibling]
    greeted += [{"section": half, **peer_first(t)} for t in range(1, first) for half in range(2)]
    greeted += [f(t) for f in (peer_two, peer_three) for t in range(1, rest)]
    for device in greeted:
        pl.semaphore_signal(barrier, inc=1, device_id=device, device_id_type=pl.DeviceIdType.MESH)
    pack_own()
    pl.semaphore_wait(barrier, len(greeted))

    def run(*todo):
        for f, b, g in todo:
            f(b, g)

    def events(i, table_of):
        for when, todo in table_of.items():
            @pl.when(i == when)
            def _():
                run(*todo)

    run((ag1, 0, TAB), (ag1, 0, ATT))
    fill_repeats()
    gtable[...] = jnp.zeros_like(gtable)
    take_in(images, x_ref)
    run((ag2, 0, TAB), (ag2, 0, ATT), (ag1, 0, UP))

    @pl.loop(0, slots)
    def norm_one(i):
        rd = rows_of(i)
        hat, rstd, mean = normalize(x_ref[rd, :].astype(F32))
        after_ref[rd, :] = hat
        rstds[rd, 0:1] = rstd
        rstds[rd, 2:3] = mean

    run((ag3, 0, TAB), (ag3, 0, ATT), (ag2, 0, UP), (ag1, 0, DOWN))
    take_in(cotangent, ct_ref)
    run((ag4, 0, TAB), (ag4, 0, ATT), (ag3, 0, UP), (ag2, 0, DOWN), (ag1, 1, TAB), (ag1, 1, ATT))
    run((ag5, 0, TAB), (ag5, 0, ATT))

    @pl.loop(0, slots)
    def attn_one(i):
        events(i, {
            2: [(ag4, 0, UP), (ag3, 0, DOWN), (ag2, 1, TAB), (ag2, 1, ATT), (ag1, 1, UP)],
            5: [(ag4, 0, DOWN), (ag3, 1, TAB), (ag3, 1, ATT), (ag2, 1, UP), (ag1, 1, DOWN)],
        })
        rd = rows_of(i)
        x = x_ref[rd, :].astype(F32)
        after_ref[rd, :] = attn_forward(0, x, after_ref[rd, :], rd, nrm1, qkv, prob, ctx, i)

    run((ag5, 0, UP), (ag5, 0, DOWN))

    @pl.loop(0, slots)
    def ff_one(i):
        events(i, {
            2: [(ag4, 1, TAB), (ag4, 1, ATT), (ag3, 1, UP), (ag2, 1, DOWN)],
        })
        rd = rows_of(i)
        out, rstd2 = ff_forward(0, after_ref[rd, :], rd, rd, hat2, nrm2)
        far_copy(0, i, False).start()
        far_copy(1, i, False).start()
        act[rd, :] = (live(i) * out).astype(LOW)
        rstds[rd, 1:2] = rstd2
        ship(0, 0, i)

    run((ag4, 1, UP), (ag3, 1, DOWN), (ag5, 1, TAB), (ag5, 1, ATT))

    @pl.loop(0, slots)
    def attn_two(i):
        events(i, {3: [(ag4, 1, DOWN)]})
        rd = rows_of(i)
        x = act[rd, :].astype(F32)
        hat, rstd, mean = normalize(x)
        rstds[rd, 3:4] = rstd
        rstds[rd, 4:5] = mean
        after_ref[rd, :] = attn_forward(1, x, hat, rd, nrm1b, qkvb, probb, ctxb, i)

    run((ag5, 1, UP), (ag5, 1, DOWN))

    @pl.loop(0, slots)
    def ff_two(i):
        rd = rows_of(i)
        far_copy(0, i, False).wait()
        far_copy(1, i, False).wait()
        out, rstd2 = ff_forward(1, after_ref[rd, :], rd, here, hat2b, nrm2b)
        out_two[rd, :] = (live(i) * out).astype(LOW)
        ship(0, 1, i)
        g = live(i) * ct_ref[rd, :].astype(F32)
        after_ref[rd, :] = ff_backward(1, g, rd, here, hat2b, rstd2)

    for b in range(2):
        for g in groups:
            ag_sent(b, g)

    grads_down(1)
    run((rs0, 1, DOWN))

    @pl.loop(0, slots)
    def hid_back(i):
        far_copy(0, i, True).start()

    grads_up(1)
    run((rs0, 1, UP), (rs1, 1, DOWN))

    @pl.loop(0, slots)
    def slope_back(i):
        far_copy(1, i, True).start()

    @pl.loop(0, slots)
    def attn_back_two(i):
        events(i, {
            0: [(rs1, 1, UP)],
            1: [(rs2, 1, DOWN)],
            2: [(rs2, 1, UP), (rs3, 1, DOWN)],
            4: [(rs3, 1, UP), (rs4, 1, DOWN)],
        })
        rd = rows_of(i)
        attn_backward(1, rd, qkvb, probb, ctxb, i)
        x = act[rd, :].astype(F32)
        d_in = input_backward(1, after_ref[rd, :], rd, x, rstds[rd, 4:5], rstds[rd, 3:4], qkvb)
        ing[rd, :] = d_in.astype(LOW)
        ship(1, 1, i)

    grads_attn(1)
    table_out(1)
    run((rs0, 1, ATT), (rs0, 1, TAB), (rs4, 1, UP))

    @pl.loop(0, slots)
    def ff_back_one(i):
        events(i, {
            1: [(rs1, 1, ATT), (rs1, 1, TAB)],
            3: [(rs2, 1, ATT), (rs2, 1, TAB)],
            5: [(rs3, 1, ATT), (rs3, 1, TAB)],
        })
        rd = rows_of(i)
        far_copy(1, i, True).wait()
        g = live(i) * ing[rd, :].astype(F32)
        after_ref[rd, :] = ff_backward(0, g, rd, rd, hat2, rstds[rd, 1:2])

    @pl.loop(0, slots)
    def hid_is_back(i):
        far_copy(0, i, True).wait()

    grads_down(0)
    run((rs0, 0, DOWN), (rs4, 1, ATT), (rs4, 1, TAB))
    grads_up(0)
    run((rs0, 0, UP), (rs1, 0, DOWN))

    @pl.loop(0, slots)
    def attn_back_one(i):
        events(i, {
            0: [(rs1, 0, UP)],
            2: [(rs2, 0, DOWN)],
            3: [(rs2, 0, UP), (rs3, 0, DOWN)],
            5: [(rs3, 0, UP), (rs4, 0, DOWN)],
        })
        attn_backward(0, rows_of(i), qkv, prob, ctx, i)

    grads_attn(0)
    run((rs0, 0, ATT), (rs4, 0, UP))

    @pl.loop(0, slots)
    def input_one(i):
        events(i, {2: [(rs1, 0, ATT)], 5: [(rs2, 0, ATT)]})
        rd = rows_of(i)
        x = x_ref[rd, :].astype(F32)
        d_in = input_backward(0, after_ref[rd, :], rd, x, rstds[rd, 2:3], rstds[rd, 0:1], qkv)
        shipped(1, 1, i)
        ing[rd, :] = d_in.astype(LOW)
        ship(1, 0, i)

    table_out(0)
    run((rs0, 0, TAB), (rs1, 0, TAB), (rs3, 0, ATT), (rs2, 0, TAB), (rs3, 0, TAB))

    @pl.loop(0, slots)
    def all_out(i):
        shipped(0, 0, i)
        shipped(0, 1, i)
        shipped(1, 0, i)
        for kind in range(2):
            for b in range(2):
                landed(kind, b, i)

    run((rs4, 0, ATT), (rs4, 0, TAB))
    for b in range(2):
        for g in groups:
            rs_sent(b, g)


def output_kernel(
    f_a, f_u, f_d, f_t, o_g1, o_s1, o_qkv, o_qv, o_out, o_bo, o_g2, o_s2, o_up, o_bu, o_down, o_bd
):
    unit, width = o_out.shape[1:]
    for half in range(2):
        o_down[0, 2 * unit * half : 2 * unit * (half + 1), :] = f_d[half]
        for sub in range(2):
            part = 2 * half + sub
            cols = slice(part * width, (part + 1) * width)
            o_up[0, :, cols] = f_u[half, unit * sub : unit * (sub + 1), :]
            piece = f_a[half, unit * sub : unit * (sub + 1), :]
            if part == 3:
                o_out[0] = piece
            else:
                o_qkv[0, :, cols] = piece
    begin = 0
    for out in (o_g1, o_s1, o_bo, o_g2, o_s2, o_bd, o_qv):
        part = out.shape[1]
        out[...] = f_t[0, :, begin : begin + part]
        begin += part
    o_bu[...] = f_t[1, :, 0 : o_bu.shape[1]]


def local(
    images, cotangent, counts,
    ln1_gain, ln1_bias, w_qkv, b_qv, w_out, b_out, ln2_gain, ln2_bias, w_up, b_up, w_down, b_down,
):
    micro_count, slots, length, width = images.shape
    ff = w_up.shape[2]
    rows = -(-length // 16) * 16
    n = lax.axis_size("fsdp")
    unit = width // n
    first, rest = radices(n)
    total = slots * rows
    head_dim = width // HEADS

    def vm(*shape, kind=LOW):
        return pltpu.VMEM(shape, kind)

    tall = [(2 * unit, LOW)] * 3 + [(1, F32)]
    dma = lambda *shape: pltpu.SemaphoreType.DMA(shape)
    outs = [((2, total, width), LOW), ((2, total, width), LOW)]
    outs += [((2, r, width), F32) for r, _ in tall] + [((total, ff), LOW), ((total, ff), LOW)]
    scratch = [
        vm(total, width), vm(total, width), vm(2, length, width), *[vm(2, r, width, kind=kind) for r, kind in tall],
        vm(2, width, 3 * width), vm(2, width, width), vm(2, width, ff), vm(2, ff, width),
        vm(2, TABLE, width, kind=F32), vm(2, TABLE, width, kind=F32),
        vm(unit, width), vm(2 * unit, 2 * width), vm(4 * unit, 4 * width),
        vm(total, width), vm(total, width), vm(total, width), vm(total, width, kind=F32),
        vm(total, width), vm(total, 3 * width), vm(slots, HEADS, rows, rows), vm(total, width),
        vm(total, width), vm(total, width), vm(total, 5, kind=F32),
        vm(total, ff), vm(total, ff),
        vm(total, width), vm(total, 3 * width), vm(total, width), vm(total, width), vm(slots, HEADS, rows, rows),
        vm(rows, width), vm(total, width), vm(total, width), vm(width, total),
    ]
    scratch += [vm(2, 2, n, r, width, kind=kind) for r, kind in tall]
    scratch += [vm(n, r, width, kind=kind) for r, kind in tall]
    scratch += [vm(2, rest - 1, rest * first, r, width, kind=kind) for r, kind in tall]
    scratch += [vm(2, rest - 1, first, r, width, kind=kind) for r, kind in tall]
    scratch += [vm(2, first, r, width, kind=kind) for r, kind in tall]
    scratch += [dma(2), dma(4, slots), dma(4, slots), dma(4, slots)]
    scratch += [dma(4, 2, first), dma(8, first)] + [dma(8, rest - 1)] * 4 + [dma(8, rest)] * 2
    scratch += [dma(8)] * 2 + [dma(8, rest - 1)] * 4 + [dma(8, first), dma(4, 2, first)]
    scratch += [pltpu.SemaphoreType.REGULAR((4,))]
    dims = (slots, length, rows, width, ff, head_dim, n)
    vmem = pl.BlockSpec(memory_space=pltpu.VMEM)
    hbm = pl.BlockSpec(memory_space=pltpu.HBM)
    acts, ings, f_a, f_u, f_d, f_t, _, _ = pl.pallas_call(
        functools.partial(whole_kernel, dims),
        out_shape=[jax.ShapeDtypeStruct(*o) for o in outs],
        in_specs=[hbm, hbm, pl.BlockSpec(memory_space=pltpu.SMEM)] + [vmem] * 12,
        out_specs=[hbm, hbm] + [vmem] * 4 + [hbm, hbm],
        scratch_shapes=scratch,
        compiler_params=pltpu.CompilerParams(
            vmem_limit_bytes=(64 << 20) - (96 << 10), collective_id=0, has_side_effects=True
        ),
    )(
        images, cotangent, counts.T, ln1_gain, ln1_bias, b_out, ln2_gain, ln2_bias, b_down, b_qv, b_up,
        w_qkv, w_out, w_up, w_down,
    )

    params = (
        ln1_gain, ln1_bias, w_qkv, b_qv, w_out, b_out, ln2_gain, ln2_bias, w_up, b_up, w_down, b_down
    )
    grads = pl.pallas_call(
        output_kernel,
        out_shape=[jax.ShapeDtypeStruct(p.shape, F32) for p in params],
        in_specs=[vmem] * 4,
        out_specs=[vmem] * len(params),
    )(f_a, f_u, f_d, f_t)

    def images_of(value):
        return value.reshape(1, 2, slots, rows, width)[:, :, :, :length]

    return (images_of(acts), images_of(ings), *grads)


def solution(mesh):
    split = P("section", "fsdp")
    cube = P("section", "fsdp", None)
    image = P(None, "fsdp", None, None)
    result = P("section", None, "fsdp", None, None)
    params = (split, split, cube, split, cube, split, split, split, cube, split, cube, split)
    return jax.shard_map(
        local,
        mesh=mesh,
        in_specs=(image, image, P(None, "fsdp")) + params,
        out_specs=(result, result) + params,
        check_vma=False,
    )
```

```python
import functools
import math

import jax
import jax.numpy as jnp
from jax import lax
from jax.experimental import pallas as pl
from jax.experimental.pallas import tpu as pltpu
from jax.sharding import PartitionSpec as P

HEADS = 6
EPS = 1e-06
F32 = jnp.float32
LOW = jnp.bfloat16

G1, S1, BO, G2, S2, BD, BQ, BV, BU = 0, 1, 2, 3, 4, 5, 6, 7, 8
TABLE = 16
ATT, UP, DOWN, TAB = 0, 1, 2, 3


def radices(n):
    rest = max(r for r in range(1, n + 1) if r * r * r <= n and n % (r * r) == 0)
    return n // (rest * rest), rest


def mm(left, right):
    return jnp.dot(left, right, preferred_element_type=F32)


def mm_right(left, right):
    return lax.dot_general(left, right, (((1,), (1,)), ((), ())), preferred_element_type=F32)


def mm_left(left, right):
    return lax.dot_general(left, right, (((0,), (0,)), ((), ())), preferred_element_type=F32)


def normal_parts(pre):
    decay = jnp.exp2(pre * pre * (-0.5 * 1.4426950408889634))
    t = 1.0 / (1.0 + (0.3275911 * 0.7071067811865476) * jnp.abs(pre))
    poly = 0.5 * 1.061405429
    for term in (-1.453152027, 1.421413741, -0.284496736, 0.254829592):
        poly = poly * t + 0.5 * term
    tail = poly * t * decay
    phi = jnp.where(pre < 0.0, tail, 1.0 - tail)
    slope = phi + pre * (decay * 0.3989422804014327)
    return phi, slope


def normalize(value):
    mean = jnp.mean(value, axis=-1, keepdims=True)
    center = value - mean
    rstd = lax.rsqrt(jnp.mean(center * center, axis=-1, keepdims=True) + EPS)
    return center * rstd, rstd, mean


def normalize_back(d_hat, hat, rstd):
    mean_one = jnp.mean(d_hat, axis=-1, keepdims=True)
    mean_two = jnp.mean(d_hat * hat, axis=-1, keepdims=True)
    return rstd * (d_hat - mean_one - hat * mean_two)


def colsum(value):
    return jnp.sum(value, axis=0, keepdims=True)


def whole_kernel(dims, *refs):
    slots, length, rows, width, ff, head_dim, n = dims
    (
        images, cotangent, counts, v_g1, v_s1, v_bo, v_g2, v_s2, v_bd, v_qv, v_up, a_qkv, a_out, a_up, a_down,
        act_out, ing_out, f_a, f_u, f_d, f_t, hid_far, slope_far,
        x_ref, x_in, ct_in, pack_a, pack_u, pack_d, pack_t,
        wqkv, wout, wup, wdown, table, gtable, rep_one, rep_two, rep_four,
        act, out_two, ing, after_ref, nrm1, qkv, prob, ctx, hat2, nrm2, rstds,
        hid, slope,
        nrm1b, qkvb, ctxb, nrm2b, probb, hat2b, dal, low_g, left_t,
        s_a, s_u, s_d, s_t, r0_a, r0_u, r0_d, r0_t, r1_a, r1_u, r1_d, r1_t, r2_a, r2_u, r2_d, r2_t,
        r3_a, r3_u, r3_d, r3_t,
        in_s, ship_s, ship_r, far_s, ag1_s, ag1_r, ag2_s, ag2_r, ag3_s, ag3_r, ag4_s, ag4_r,
        rs0_s, rs0_r, rs1_s, rs1_r, rs2_s, rs2_r, rs3_s, rs3_r, credit,
    ) = refs
    groups = (ATT, UP, DOWN, TAB)
    pack = (pack_a, pack_u, pack_d, pack_t)
    stage = (s_a, s_u, s_d, s_t)
    r0, r1, r2 = (r0_a, r0_u, r0_d, r0_t), (r1_a, r1_u, r1_d, r1_t), (r2_a, r2_u, r2_d, r2_t)
    r3, final = (r3_a, r3_u, r3_d, r3_t), (f_a, f_u, f_d, f_t)

    first, rest = radices(n)
    unit = width // n
    core = lax.axis_index("section")
    me = lax.axis_index("fsdp")
    dig_a, dig_b, dig_c = me // (rest * rest), (me // rest) % rest, me % rest
    dig_three, dig_two = dig_c + core * (dig_b - dig_c), dig_b + core * (dig_c - dig_b)
    step_three, step_two = 1 + core * (rest - 1), rest - core * (rest - 1)
    pos = (dig_three * rest + dig_two) * first + dig_a
    pos_of = ((dig_c * rest + dig_b) * first + dig_a, (dig_b * rest + dig_c) * first + dig_a)
    sibling = {"section": 1 - core}

    def place(half, j):
        a, b, c = j // (rest * rest), (j // rest) % rest, j % rest
        return ((c * rest + b) if half == 0 else (b * rest + c)) * first + a

    def peer_first(t):
        return {"fsdp": me + ((dig_a + t) % first - dig_a) * (rest * rest)}

    def peer_two(t):
        return {"fsdp": me + ((dig_two + t) % rest - dig_two) * step_two}

    def peer_three(t):
        return {"fsdp": me + ((dig_three + t) % rest - dig_three) * step_three}

    def remote(src, dst, s_sem, r_sem, device):
        return pltpu.make_async_remote_copy(
            src_ref=src, dst_ref=dst, send_sem=s_sem, recv_sem=r_sem, device_id=device,
            device_id_type=pl.DeviceIdType.MESH,
        )

    def slab_two(three, two):
        return pl.ds((three * rest + two) * first, first)

    def slab_three(three):
        return pl.ds(three * rest * first, rest * first)

    def fill_repeats():
        for ref in (rep_one, rep_two, rep_four):
            part = ref.shape[0]
            lanes = lax.broadcasted_iota(jnp.int32, ref.shape, 1).astype(F32)
            line = lax.broadcasted_iota(jnp.int32, ref.shape, 0).astype(F32)
            rest_of = lanes - part * jnp.floor((lanes + 0.5) * (1.0 / part))
            ref[...] = jnp.where(jnp.abs(rest_of - line) < 0.5, 1.0, 0.0).astype(LOW)

    def own_lanes(part):
        shape = (n, part * n)
        lanes = lax.broadcasted_iota(jnp.int32, shape, 1)
        begin = lax.broadcasted_iota(jnp.int32, shape, 0) * part
        return (lanes >= begin) & (lanes < begin + part)

    shares = (
        ((G1, unit, rep_one), (S1, unit, rep_one), (BO, unit, rep_one), (G2, unit, rep_one), (S2, unit, rep_one),
         (BD, unit, rep_one), (BQ, 2 * unit, rep_two)),
        ((BU, 4 * unit, rep_four),),
    )

    def table_in(b):
        for half in range(2):
            lines = jnp.concatenate([s_t[b, half, place(half, j)] for j in range(n)], axis=0)
            begin = 0
            for row, part, ref in shares[half]:
                spread = mm(lines[:, begin : begin + part].astype(LOW), ref[...])
                line = colsum(jnp.where(own_lanes(part), spread, 0.0))
                for i in range(part * n // width):
                    table[b, row + i : row + i + 1, :] = line[:, width * i : width * (i + 1)]
                begin += part

    def table_out(b):
        for half in range(2):
            parts, begin = [], 0
            for row, part, ref in shares[half]:
                count = part * n // width
                line = jnp.concatenate([gtable[b, row + i : row + i + 1, :] for i in range(count)], axis=1)
                parts.append(mm_right(jnp.where(own_lanes(part), line, 0.0).astype(LOW), ref[...]))
                begin += part
            parts.append(jnp.zeros((n, width - begin), F32))
            lines = jnp.concatenate(parts, axis=1)
            for j in range(n):
                s_t[b, half, place(half, j)] = lines[j : j + 1]

    def pack_own():
        for half in range(2):
            vectors = ((v_g1, v_s1, v_bo, v_g2, v_s2, v_bd, v_qv), (v_up,))[half]
            lines = [vector[...].astype(F32) for vector in vectors]
            lines.append(jnp.zeros((1, width - sum(line.shape[1] for line in lines)), F32))
            pack_t[half] = jnp.concatenate(lines, axis=1)
            for ref in (pack_a, pack_u):
                both = []
                for part in (2 * half, 2 * half + 1):
                    if ref is pack_u:
                        both.append(a_up[0, :, part * width : (part + 1) * width])
                    elif part == 3:
                        both.append(a_out[0])
                    else:
                        both.append(a_qkv[0, :, part * width : (part + 1) * width])
                ref[half] = jnp.concatenate([value.astype(F32) for value in both], axis=0).astype(LOW)
            pack_d[half] = a_down[0, 2 * unit * half : 2 * unit * (half + 1), :]

    def at(b, g):
        return len(groups) * b + g

    def ag1_copy(b, g, half, t):
        device = {"section": half, **peer_first(t)} if t else sibling
        return remote(
            pack[g].at[half], stage[g].at[b, half, pos_of[half]],
            ag1_s.at[g, half, t], ag1_r.at[at(b, g), t], device,
        )

    def ag1_landing(b, g, t):
        ref = stage[g].at[b, core, (dig_three * rest + dig_two) * first + (dig_a + first - t) % first]
        return remote(ref, ref, ag1_s.at[g, 0, t], ag1_r.at[at(b, g), t], sibling)

    def ag2_copy(b, g, t):
        ref = stage[g].at[b, core, slab_two(dig_three, dig_two)]
        return remote(ref, ref, ag2_s.at[at(b, g), t - 1], ag2_r.at[at(b, g), t - 1], peer_two(t))

    def ag3_copy(b, g, t):
        ref = stage[g].at[b, core, slab_three(dig_three)]
        return remote(ref, ref, ag3_s.at[at(b, g), t - 1], ag3_r.at[at(b, g), t - 1], peer_three(t))

    def ag4_copy(b, g, t):
        ref = stage[g].at[b, core, slab_three((dig_three + rest - t) % rest)]
        return remote(ref, ref, ag4_s.at[at(b, g), t], ag4_r.at[at(b, g), t], sibling)

    def ag4_landing(b, g, t):
        ref = stage[g].at[b, 1 - core, slab_three((dig_two + rest - t) % rest)]
        return remote(ref, ref, ag4_s.at[at(b, g), t], ag4_r.at[at(b, g), t], sibling)

    def ag1(b, g):
        @pl.when(core == b)
        def _():
            for t in range(1, first):
                for half in range(2):
                    ag1_copy(b, g, half, t).start()
            ag1_copy(b, g, 1 - b, 0).start()
            stage[g][b, b, pos] = pack[g][b]

    def ag2(b, g):
        for t in range(1, first):
            ag1_landing(b, g, t).wait_recv()

        @pl.when(core != b)
        def _():
            ag1_landing(b, g, 0).wait_recv()

        for t in range(1, rest):
            ag2_copy(b, g, t).start()

    def ag3(b, g):
        for t in range(1, rest):
            ag2_copy(b, g, t).wait_recv()
        for t in range(1, rest):
            ag3_copy(b, g, t).start()
        ag4_copy(b, g, 0).start()

    def ag4(b, g):
        for t in range(1, rest):
            ag3_copy(b, g, t).wait_recv()
            ag4_copy(b, g, t).start()

    def ag5(b, g):
        for t in range(rest):
            ag4_landing(b, g, t).wait_recv()
        lay_out(b, g)

    def ag_sent(b, g):
        @pl.when(core == b)
        def _():
            for t in range(1, first):
                for half in range(2):
                    ag1_copy(b, g, half, t).wait_send()
            ag1_copy(b, g, 1 - b, 0).wait_send()

        for t in range(1, rest):
            ag2_copy(b, g, t).wait_send()
            ag3_copy(b, g, t).wait_send()
        for t in range(rest):
            ag4_copy(b, g, t).wait_send()

    def lay_out(b, g):
        if g == TAB:
            table_in(b)
            return
        if g == DOWN:
            for j in range(n):
                for half in range(2):
                    begin = 4 * unit * j + 2 * unit * half
                    wdown[b, begin : begin + 2 * unit, :] = s_d[b, half, place(half, j)]
            return
        together = 16 // math.gcd(unit, 16)
        for half in range(2):
            for j in range(0, n, together):
                pieces = [stage[g][b, half, place(half, j + i)].astype(F32) for i in range(together)]
                for sub in range(2):
                    low = sub * unit
                    block = jnp.concatenate([piece[low : low + unit] for piece in pieces], axis=0).astype(LOW)
                    part = 2 * half + sub
                    down = slice(unit * j, unit * (j + together))
                    if g == UP:
                        wup[b, down, part * width : (part + 1) * width] = block
                    elif part == 3:
                        wout[b, down, :] = block
                    else:
                        wqkv[b, down, part * width : (part + 1) * width] = block

    def rs0_copy(b, g):
        return remote(stage[g].at[b, 1 - core], r0[g], rs0_s.at[at(b, g)], rs0_r.at[at(b, g)], sibling)

    def rs1_copy(b, g, t):
        return remote(
            stage[g].at[b, core, slab_three((dig_three + t) % rest)], r1[g].at[b, t - 1],
            rs1_s.at[at(b, g), t - 1], rs1_r.at[at(b, g), t - 1], peer_three(t),
        )

    def rs2_copy(b, g, t):
        return remote(
            stage[g].at[b, core, slab_two(dig_three, (dig_two + t) % rest)], r2[g].at[b, t - 1],
            rs2_s.at[at(b, g), t - 1], rs2_r.at[at(b, g), t - 1], peer_two(t),
        )

    def rs3_copy(b, g, t):
        there = (dig_three * rest + dig_two) * first + (dig_a + t) % first
        device = {"section": b, **peer_first(t)} if t else sibling
        return remote(
            stage[g].at[b, core, there], r3[g].at[core, t], rs3_s.at[at(b, g), t], rs3_r.at[g, core, t], device
        )

    def rs0(b, g):
        if b == 0:
            pl.semaphore_wait(credit.at[g], 1)
        rs0_copy(b, g).start()

    def rs1(b, g):
        rs0_copy(b, g).wait_recv()

        @pl.loop(0, n)
        def _(p):
            stage[g][b, core, p] = stage[g][b, core, p] + r0[g][p]

        if b == 1:
            pl.semaphore_signal(credit.at[g], inc=1, device_id=sibling, device_id_type=pl.DeviceIdType.MESH)
        for t in range(1, rest):
            rs1_copy(b, g, t).start()

    def rs2(b, g):
        for t in range(1, rest):
            rs1_copy(b, g, t).wait_recv()

        @pl.loop(0, rest * first)
        def _(p):
            here = dig_three * rest * first + p
            total = stage[g][b, core, here].astype(F32)
            for t in range(1, rest):
                total = total + r1[g][b, t - 1, p].astype(F32)
            stage[g][b, core, here] = total.astype(stage[g].dtype)

        for t in range(1, rest):
            rs2_copy(b, g, t).start()

    def rs3(b, g):
        for t in range(1, rest):
            rs2_copy(b, g, t).wait_recv()

        @pl.loop(0, first)
        def _(p):
            here = (dig_three * rest + dig_two) * first + p
            total = stage[g][b, core, here].astype(F32)
            for t in range(1, rest):
                total = total + r2[g][b, t - 1, p].astype(F32)
            stage[g][b, core, here] = total.astype(stage[g].dtype)

        for t in range(1, first):
            rs3_copy(b, g, t).start()

        @pl.when(core != b)
        def _():
            rs3_copy(b, g, 0).start()

    def rs4(b, g):
        @pl.when(core == b)
        def _():
            for half in range(2):
                begin = int(half == b)
                for t in range(begin, first):
                    ref = r3[g].at[half, t]
                    remote(ref, ref, rs3_s.at[at(b, g), t], rs3_r.at[g, half, t], sibling).wait_recv()
                total = stage[g][b, b, pos].astype(F32) if half == b else None
                for t in range(begin, first):
                    value = r3[g][half, t].astype(F32)
                    total = value if total is None else total + value
                final[g][half] = total

    def rs_sent(b, g):
        rs0_copy(b, g).wait_send()
        for t in range(1, rest):
            rs1_copy(b, g, t).wait_send()
            rs2_copy(b, g, t).wait_send()
        for t in range(1, first):
            rs3_copy(b, g, t).wait_send()

        @pl.when(core != b)
        def _():
            rs3_copy(b, g, 0).wait_send()

    def rows_of(i):
        return pl.ds(pl.multiple_of(i * rows, 16), rows)

    def ship_parts(kind, b, i):
        src, out = ((out_two if b else act, act_out), (ing, ing_out))[kind]
        q = 2 * kind + b
        rd = rows_of(i)
        near = pltpu.make_async_copy(src.at[rd], out.at[core, rd], ship_s.at[q, i])
        far = remote(src.at[rd], out.at[core, rd], ship_s.at[q, i], ship_r.at[q, i], sibling)
        return near, far

    def ship(kind, b, i):
        near, far = ship_parts(kind, b, i)

        @pl.when(core == b)
        def _():
            near.start()

        @pl.when(core != b)
        def _():
            far.start()

    def shipped(kind, b, i):
        near, far = ship_parts(kind, b, i)

        @pl.when(core == b)
        def _():
            near.wait()

        @pl.when(core != b)
        def _():
            far.wait_send()

    def landed(kind, b, i):
        out = (act_out, ing_out)[kind]
        q = 2 * kind + b
        ref = out.at[1 - core, rows_of(i)]

        @pl.when(core == b)
        def _():
            remote(ref, ref, ship_s.at[q, i], ship_r.at[q, i], sibling).wait_recv()

    def live(i):
        return jnp.where(i < counts[0, core], 1.0, 0.0).astype(F32)

    def coming(which, i):
        source, target = ((images, x_in), (cotangent, ct_in))[which]
        return pltpu.make_async_copy(source.at[core, i], target.at[i], in_s.at[which, i])

    def far_copy(which, i, back):
        near, far = ((hid, hid_far), (slope, slope_far))[which]
        near, far = near.at[rows_of(i)], far.at[rows_of(i)]
        src, dst = (far, near) if back else (near, far)
        return pltpu.make_async_copy(src, dst, far_s.at[2 * int(back) + which, i])

    pairs = width // 128
    scale = head_dim ** -0.5
    lane = lax.broadcasted_iota(jnp.int32, (1, 128), 1)
    half_low = [(lane < head_dim).astype(LOW), (lane >= head_dim).astype(LOW)]
    half_f = [(lane < head_dim).astype(F32), (lane >= head_dim).astype(F32)]
    key_pad = jnp.where(lax.broadcasted_iota(jnp.int32, (1, rows), 1) < length, 0.0, -1e30).astype(F32)
    chunk = 256
    chunks = ff // chunk

    def vec(s, r):
        return table[s, r : r + 1, :]

    def up_bias(s, c):
        begin = c * chunk
        row, col = begin // width, begin % width
        if col + chunk <= width:
            return table[s, BU + row : BU + row + 1, col : col + chunk]
        a = table[s, BU + row : BU + row + 1, col:width]
        b = table[s, BU + row + 1 : BU + row + 2, 0 : chunk - (width - col)]
        return jnp.concatenate([a, b], axis=1)

    def add_vec(s, r, value):
        gtable[s, r : r + 1, :] += value

    def add_up_bias(s, c, value):
        begin = c * chunk
        row, col = begin // width, begin % width
        if col + chunk <= width:
            gtable[s, BU + row : BU + row + 1, col : col + chunk] += value
        else:
            cut = width - col
            gtable[s, BU + row : BU + row + 1, col:width] += value[:, :cut]
            gtable[s, BU + row + 1 : BU + row + 2, 0 : chunk - cut] += value[:, cut:]

    def attn_forward(s, x, hat, rd, nrm_ref, qkv_ref, prob_ref, ctx_ref, pi):
        nrm = (hat * vec(s, G1) + vec(s, S1)).astype(LOW)
        nrm_ref[rd, :] = nrm
        q = (mm(nrm, wqkv[s, :, 0:width]) + vec(s, BQ)).astype(LOW)
        k = mm(nrm, wqkv[s, :, width : 2 * width]).astype(LOW)
        v = (mm(nrm, wqkv[s, :, 2 * width :]) + vec(s, BV)).astype(LOW)
        qkv_ref[rd, 0:width] = q
        qkv_ref[rd, width : 2 * width] = k
        qkv_ref[rd, 2 * width :] = v
        parts = []
        for p in range(pairs):
            cols = slice(128 * p, 128 * p + 128)
            total = None
            for j in range(2):
                scores = mm_right(q[:, cols], k[:, cols] * half_low[j]) + key_pad
                top = jnp.max(scores, axis=-1, keepdims=True)
                e = jnp.exp2((scores - top) * (scale * 1.4426950408889634))
                pr = (e * (1.0 / jnp.sum(e, axis=-1, keepdims=True))).astype(LOW)
                prob_ref[pi, 2 * p + j] = pr
                part = mm(pr, v[:, cols] * half_low[j])
                total = part if total is None else total + part
            parts.append(total.astype(LOW))
        context = jnp.concatenate(parts, axis=1)
        ctx_ref[rd, :] = context
        return x + mm(context, wout[s]) + vec(s, BO)

    def ff_forward(s, after, rd, srd, hat_ref, nrm_ref):
        hat, rstd, _ = normalize(after)
        hat_ref[srd, :] = hat.astype(LOW)
        nrm = (hat * vec(s, G2) + vec(s, S2)).astype(LOW)
        nrm_ref[rd, :] = nrm
        total = after + vec(s, BD)
        for c in range(chunks):
            cols = slice(chunk * c, chunk * c + chunk)
            pre = mm(nrm, wup[s, :, cols]) + up_bias(s, c)
            phi, slo = normal_parts(pre)
            h = (pre * phi).astype(LOW)
            hid[rd, cols] = h
            slope[rd, cols] = slo.astype(LOW)
            total = total + mm(h, wdown[s, cols, :])
        return total, rstd

    def ff_backward(s, g, rd, srd, hat_ref, rstd):
        g_low = g.astype(LOW)
        add_vec(s, BD, colsum(g_low.astype(F32)))
        d_nrm = None
        for c in range(chunks):
            cols = slice(chunk * c, chunk * c + chunk)
            d_hid = mm_right(g_low, wdown[s, cols, :])
            d_pre = (d_hid * slope[rd, cols].astype(F32)).astype(LOW)
            slope[rd, cols] = d_pre
            add_up_bias(s, c, colsum(d_pre.astype(F32)))
            part = mm_right(d_pre, wup[s, :, cols])
            d_nrm = part if d_nrm is None else d_nrm + part
        hat = hat_ref[srd, :].astype(F32)
        add_vec(s, G2, colsum(d_nrm * hat))
        add_vec(s, S2, colsum(d_nrm))
        d_after = g + normalize_back(d_nrm * vec(s, G2), hat, rstd)
        low = d_after.astype(LOW)
        dal[rd, :] = low
        add_vec(s, BO, colsum(low.astype(F32)))
        return d_after

    def attn_backward(s, rd, qkv_ref, prob_ref, ctx_ref, pi):
        d_ctx = mm_right(dal[rd, :], wout[s]).astype(LOW)
        dq, dk, dv = [], [], []
        for p in range(pairs):
            cols = slice(128 * p, 128 * p + 128)
            q = qkv_ref[rd, 128 * p : 128 * p + 128]
            k = qkv_ref[rd, width + 128 * p : width + 128 * p + 128]
            v = qkv_ref[rd, 2 * width + 128 * p : 2 * width + 128 * p + 128]
            dc = d_ctx[:, cols]
            both = dc.astype(F32) * ctx_ref[rd, cols].astype(F32)
            sums = [None, None, None]
            for j in range(2):
                pr = prob_ref[pi, 2 * p + j]
                delta = jnp.sum(both * half_f[j], axis=-1, keepdims=True)
                d_prob = mm_right(dc, v * half_low[j])
                ds = (pr.astype(F32) * (d_prob - delta)).astype(LOW)
                new = [mm(ds, k * half_low[j]), mm_left(ds, q * half_low[j]), mm_left(pr, dc * half_low[j])]
                sums = [b if a is None else a + b for a, b in zip(sums, new)]
            dq.append((sums[0] * scale).astype(LOW))
            dk.append((sums[1] * scale).astype(LOW))
            dv.append(sums[2].astype(LOW))
        d_mixed = jnp.concatenate(dq + dk + dv, axis=1)
        qkv_ref[rd, :] = d_mixed
        add_vec(s, BQ, colsum(d_mixed[:, 0:width].astype(F32)))
        add_vec(s, BV, colsum(d_mixed[:, 2 * width :].astype(F32)))

    def input_backward(s, d_after, rd, x, mean, rstd, qkv_ref):
        d_nrm = mm_right(qkv_ref[rd, :], wqkv[s])
        hat = (x - mean) * rstd
        add_vec(s, G1, colsum(d_nrm * hat))
        add_vec(s, S1, colsum(d_nrm))
        return d_after + normalize_back(d_nrm * vec(s, G1), hat, rstd)

    def grads_down(s):
        left_t[...] = low_g[...].T

        @pl.loop(0, 4)
        def _(c):
            cols = pl.ds(pl.multiple_of(c * width, 128), width)
            block = mm(left_t[...], hid[:, cols]).T
            for i in range(n // 4):
                for half in range(2):
                    begin = 4 * unit * i + 2 * unit * half
                    s_d[s, half, place(half, c * (n // 4) + i)] = block[begin : begin + 2 * unit].astype(LOW)

    def pair_out(ref, s, half, one, two):
        for j in range(n):
            down = slice(unit * j, unit * (j + 1))
            piece = jnp.concatenate([one[down], two[down]], axis=0).astype(LOW)
            ref[s, half, place(half, j)] = piece

    def grads_up(s):
        left_t[...] = nrm2_of[s][...].T
        for half in range(2):
            one, two = [
                mm(left_t[...], slope[:, part * width : (part + 1) * width]) for part in (2 * half, 2 * half + 1)
            ]
            pair_out(s_u, s, half, one, two)

    def grads_attn(s):
        ctx_s, nrm_s, mix_s = ((ctx, nrm1, qkv), (ctxb, nrm1b, qkvb))[s]
        left_t[...] = ctx_s[...].T
        four = mm(left_t[...], dal[...])
        left_t[...] = nrm_s[...].T
        three = mm(left_t[...], mix_s[:, 2 * width :])
        pair_out(s_a, s, 1, three, four)
        one = mm(left_t[...], mix_s[:, 0:width])
        two = mm(left_t[...], mix_s[:, width : 2 * width])
        pair_out(s_a, s, 0, one, two)

    nrm2_of = (nrm2, nrm2b)
    here = pl.ds(0, rows)

    barrier = pltpu.get_barrier_semaphore()
    greeted = [sibling]
    greeted += [{"section": half, **peer_first(t)} for t in range(1, first) for half in range(2)]
    greeted += [f(t) for f in (peer_two, peer_three) for t in range(1, rest)]
    for device in greeted:
        pl.semaphore_signal(barrier, inc=1, device_id=device, device_id_type=pl.DeviceIdType.MESH)
    pack_own()
    pl.semaphore_wait(barrier, len(greeted))

    def run(*todo):
        for f, b, g in todo:
            f(b, g)

    def events(i, table_of):
        for when, todo in table_of.items():
            @pl.when(i == when)
            def _():
                run(*todo)

    run((ag1, 0, TAB), (ag1, 0, ATT))
    for which in range(2):
        for i in range(slots):
            coming(which, i).start()
    fill_repeats()
    gtable[...] = jnp.zeros_like(gtable)
    low_g[...] = jnp.zeros_like(low_g)
    x_ref[...] = jnp.zeros_like(x_ref)
    run((ag2, 0, TAB), (ag2, 0, ATT), (ag1, 0, UP), (ag1, 0, DOWN))

    @pl.loop(0, slots)
    def norm_one(i):
        rd = rows_of(i)
        coming(0, i).wait()
        x_ref[pl.ds(pl.multiple_of(i * rows, 16), length), :] = x_in[i]
        hat, rstd, mean = normalize(x_ref[rd, :].astype(F32))
        after_ref[rd, :] = hat
        rstds[rd, 0:1] = rstd
        rstds[rd, 2:3] = mean

    run((ag3, 0, TAB), (ag3, 0, ATT), (ag2, 0, UP), (ag1, 1, TAB), (ag1, 1, ATT))
    run((ag2, 0, DOWN), (ag1, 1, UP), (ag1, 1, DOWN))
    run((ag4, 0, TAB), (ag4, 0, ATT), (ag3, 0, UP), (ag5, 0, TAB), (ag5, 0, ATT))

    @pl.loop(0, slots)
    def attn_one(i):
        events(i, {
            0: [(ag3, 0, DOWN), (ag2, 1, TAB), (ag2, 1, ATT)],
            3: [(ag4, 0, UP), (ag2, 1, UP)],
            5: [(ag4, 0, DOWN)],
        })
        rd = rows_of(i)
        x = x_ref[rd, :].astype(F32)
        after_ref[rd, :] = attn_forward(0, x, after_ref[rd, :], rd, nrm1, qkv, prob, ctx, i)

    run((ag3, 1, TAB), (ag3, 1, ATT), (ag5, 0, UP), (ag5, 0, DOWN))

    @pl.loop(0, slots)
    def ff_one(i):
        events(i, {
            0: [(ag3, 1, UP), (ag2, 1, DOWN)],
            3: [(ag4, 1, TAB), (ag4, 1, ATT)],
            5: [(ag4, 1, UP)],
        })
        rd = rows_of(i)
        out, rstd2 = ff_forward(0, after_ref[rd, :], rd, rd, hat2, nrm2)
        far_copy(0, i, False).start()
        far_copy(1, i, False).start()
        act[rd, :] = (live(i) * out).astype(LOW)
        rstds[rd, 1:2] = rstd2
        ship(0, 0, i)

    run((ag3, 1, DOWN), (ag5, 1, TAB), (ag5, 1, ATT))

    @pl.loop(0, slots)
    def attn_two(i):
        events(i, {5: [(ag4, 1, DOWN)]})
        rd = rows_of(i)
        x = act[rd, :].astype(F32)
        hat, rstd, mean = normalize(x)
        rstds[rd, 3:4] = rstd
        rstds[rd, 4:5] = mean
        after_ref[rd, :] = attn_forward(1, x, hat, rd, nrm1b, qkvb, probb, ctxb, i)

    run((ag5, 1, UP), (ag5, 1, DOWN))

    @pl.loop(0, slots)
    def ff_two(i):
        rd = rows_of(i)
        far_copy(0, i, False).wait()
        far_copy(1, i, False).wait()
        out, rstd2 = ff_forward(1, after_ref[rd, :], rd, here, hat2b, nrm2b)
        out_two[rd, :] = (live(i) * out).astype(LOW)
        ship(0, 1, i)
        coming(1, i).wait()
        g = live(i) * ct_in[i].astype(F32)
        low_g[pl.ds(pl.multiple_of(i * rows, 16), length), :] = g.astype(LOW)
        g = low_g[rd, :].astype(F32)
        after_ref[rd, :] = ff_backward(1, g, rd, here, hat2b, rstd2)

    for b in range(2):
        for g in groups:
            ag_sent(b, g)

    grads_down(1)
    run((rs0, 1, DOWN))

    @pl.loop(0, slots)
    def hid_back(i):
        far_copy(0, i, True).start()

    grads_up(1)
    run((rs0, 1, UP), (rs1, 1, DOWN))

    @pl.loop(0, slots)
    def slope_back(i):
        far_copy(1, i, True).start()

    @pl.loop(0, slots)
    def attn_back_two(i):
        events(i, {
            1: [(rs1, 1, UP)],
            2: [(rs2, 1, DOWN)],
            3: [(rs2, 1, UP)],
            4: [(rs3, 1, DOWN)],
            5: [(rs3, 1, UP)],
        })
        rd = rows_of(i)
        attn_backward(1, rd, qkvb, probb, ctxb, i)
        x = act[rd, :].astype(F32)
        d_in = input_backward(1, after_ref[rd, :], rd, x, rstds[rd, 4:5], rstds[rd, 3:4], qkvb)
        ing[rd, :] = d_in.astype(LOW)
        ship(1, 1, i)

    grads_attn(1)
    table_out(1)
    run((rs0, 1, ATT), (rs0, 1, TAB), (rs4, 1, DOWN))

    @pl.loop(0, slots)
    def ff_back_one(i):
        events(i, {
            2: [(rs1, 1, ATT), (rs1, 1, TAB), (rs4, 1, UP)],
            5: [(rs2, 1, ATT), (rs2, 1, TAB)],
        })
        rd = rows_of(i)
        far_copy(1, i, True).wait()
        g = live(i) * ing[rd, :].astype(F32)
        low_g[rd, :] = g.astype(LOW)
        after_ref[rd, :] = ff_backward(0, g, rd, rd, hat2, rstds[rd, 1:2])

    @pl.loop(0, slots)
    def hid_is_back(i):
        far_copy(0, i, True).wait()

    grads_down(0)
    run((rs0, 0, DOWN), (rs3, 1, ATT), (rs3, 1, TAB))
    grads_up(0)
    run((rs0, 0, UP), (rs1, 0, DOWN))

    @pl.loop(0, slots)
    def attn_back_one(i):
        events(i, {
            1: [(rs1, 0, UP), (rs4, 1, ATT), (rs4, 1, TAB)],
            3: [(rs2, 0, DOWN)],
            4: [(rs2, 0, UP)],
            5: [(rs3, 0, DOWN)],
        })
        attn_backward(0, rows_of(i), qkv, prob, ctx, i)

    grads_attn(0)
    run((rs0, 0, ATT), (rs3, 0, UP))

    @pl.loop(0, slots)
    def input_one(i):
        events(i, {3: [(rs1, 0, ATT)], 5: [(rs4, 0, DOWN)]})
        rd = rows_of(i)
        x = x_ref[rd, :].astype(F32)
        d_in = input_backward(0, after_ref[rd, :], rd, x, rstds[rd, 2:3], rstds[rd, 0:1], qkv)
        shipped(1, 1, i)
        ing[rd, :] = d_in.astype(LOW)
        ship(1, 0, i)

    table_out(0)
    run((rs0, 0, TAB), (rs2, 0, ATT), (rs1, 0, TAB), (rs4, 0, UP), (rs3, 0, ATT), (rs2, 0, TAB), (rs3, 0, TAB))

    @pl.loop(0, slots)
    def all_out(i):
        shipped(0, 0, i)
        shipped(0, 1, i)
        shipped(1, 0, i)
        for kind in range(2):
            for b in range(2):
                landed(kind, b, i)

    run((rs4, 0, ATT), (rs4, 0, TAB))
    for b in range(2):
        for g in groups:
            rs_sent(b, g)


def output_kernel(
    f_a, f_u, f_d, f_t, o_g1, o_s1, o_qkv, o_qv, o_out, o_bo, o_g2, o_s2, o_up, o_bu, o_down, o_bd
):
    unit, width = o_out.shape[1:]
    for half in range(2):
        o_down[0, 2 * unit * half : 2 * unit * (half + 1), :] = f_d[half]
        for sub in range(2):
            part = 2 * half + sub
            cols = slice(part * width, (part + 1) * width)
            o_up[0, :, cols] = f_u[half, unit * sub : unit * (sub + 1), :]
            piece = f_a[half, unit * sub : unit * (sub + 1), :]
            if part == 3:
                o_out[0] = piece
            else:
                o_qkv[0, :, cols] = piece
    begin = 0
    for out in (o_g1, o_s1, o_bo, o_g2, o_s2, o_bd, o_qv):
        part = out.shape[1]
        out[...] = f_t[0, :, begin : begin + part]
        begin += part
    o_bu[...] = f_t[1, :, 0 : o_bu.shape[1]]


def local(
    images, cotangent, counts,
    ln1_gain, ln1_bias, w_qkv, b_qv, w_out, b_out, ln2_gain, ln2_bias, w_up, b_up, w_down, b_down,
):
    micro_count, slots, length, width = images.shape
    ff = w_up.shape[2]
    rows = -(-length // 16) * 16
    n = lax.axis_size("fsdp")
    unit = width // n
    first, rest = radices(n)
    total = slots * rows
    head_dim = width // HEADS

    def vm(*shape, kind=LOW):
        return pltpu.VMEM(shape, kind)

    tall = [(2 * unit, LOW)] * 3 + [(1, F32)]
    dma = lambda *shape: pltpu.SemaphoreType.DMA(shape)
    outs = [((2, total, width), LOW), ((2, total, width), LOW)]
    outs += [((2, r, width), F32) for r, _ in tall] + [((total, ff), LOW), ((total, ff), LOW)]
    scratch = [
        vm(total, width), vm(slots, length, width), vm(slots, length, width), *[vm(2, r, width, kind=kind) for r, kind in tall],
        vm(2, width, 3 * width), vm(2, width, width), vm(2, width, ff), vm(2, ff, width),
        vm(2, TABLE, width, kind=F32), vm(2, TABLE, width, kind=F32),
        vm(unit, width), vm(2 * unit, 2 * width), vm(4 * unit, 4 * width),
        vm(total, width), vm(total, width), vm(total, width), vm(total, width, kind=F32),
        vm(total, width), vm(total, 3 * width), vm(slots, HEADS, rows, rows), vm(total, width),
        vm(total, width), vm(total, width), vm(total, 5, kind=F32),
        vm(total, ff), vm(total, ff),
        vm(total, width), vm(total, 3 * width), vm(total, width), vm(total, width), vm(slots, HEADS, rows, rows),
        vm(rows, width), vm(total, width), vm(total, width), vm(width, total),
    ]
    scratch += [vm(2, 2, n, r, width, kind=kind) for r, kind in tall]
    scratch += [vm(n, r, width, kind=kind) for r, kind in tall]
    scratch += [vm(2, rest - 1, rest * first, r, width, kind=kind) for r, kind in tall]
    scratch += [vm(2, rest - 1, first, r, width, kind=kind) for r, kind in tall]
    scratch += [vm(2, first, r, width, kind=kind) for r, kind in tall]
    scratch += [dma(2, slots), dma(4, slots), dma(4, slots), dma(4, slots)]
    scratch += [dma(4, 2, first), dma(8, first)] + [dma(8, rest - 1)] * 4 + [dma(8, rest)] * 2
    scratch += [dma(8)] * 2 + [dma(8, rest - 1)] * 4 + [dma(8, first), dma(4, 2, first)]
    scratch += [pltpu.SemaphoreType.REGULAR((4,))]
    dims = (slots, length, rows, width, ff, head_dim, n)
    vmem = pl.BlockSpec(memory_space=pltpu.VMEM)
    hbm = pl.BlockSpec(memory_space=pltpu.HBM)
    acts, ings, f_a, f_u, f_d, f_t, _, _ = pl.pallas_call(
        functools.partial(whole_kernel, dims),
        out_shape=[jax.ShapeDtypeStruct(*o) for o in outs],
        in_specs=[hbm, hbm, pl.BlockSpec(memory_space=pltpu.SMEM)] + [vmem] * 12,
        out_specs=[hbm, hbm] + [vmem] * 4 + [hbm, hbm],
        scratch_shapes=scratch,
        compiler_params=pltpu.CompilerParams(
            vmem_limit_bytes=(64 << 20) - (96 << 10), collective_id=0, has_side_effects=True
        ),
    )(
        images, cotangent, counts.T, ln1_gain, ln1_bias, b_out, ln2_gain, ln2_bias, b_down, b_qv, b_up,
        w_qkv, w_out, w_up, w_down,
    )

    params = (
        ln1_gain, ln1_bias, w_qkv, b_qv, w_out, b_out, ln2_gain, ln2_bias, w_up, b_up, w_down, b_down
    )
    grads = pl.pallas_call(
        output_kernel,
        out_shape=[jax.ShapeDtypeStruct(p.shape, F32) for p in params],
        in_specs=[vmem] * 4,
        out_specs=[vmem] * len(params),
    )(f_a, f_u, f_d, f_t)

    def images_of(value):
        return value.reshape(1, 2, slots, rows, width)[:, :, :, :length]

    return (images_of(acts), images_of(ings), *grads)


def solution(mesh):
    split = P("section", "fsdp")
    cube = P("section", "fsdp", None)
    image = P(None, "fsdp", None, None)
    result = P("section", None, "fsdp", None, None)
    params = (split, split, cube, split, cube, split, split, split, cube, split, cube, split)
    return jax.shard_map(
        local,
        mesh=mesh,
        in_specs=(image, image, P(None, "fsdp")) + params,
        out_specs=(result, result) + params,
        check_vma=False,
    )
```

```python
import functools
import math

import jax
import jax.numpy as jnp
from jax import lax
from jax.experimental import pallas as pl
from jax.experimental.pallas import tpu as pltpu
from jax.sharding import PartitionSpec as P

HEADS = 6
EPS = 1e-06
F32 = jnp.float32
LOW = jnp.bfloat16

G1, S1, BO, G2, S2, BD, BQ, BV, BU = 0, 1, 2, 3, 4, 5, 6, 7, 8
TABLE = 16
TOGETHER = 2
ATT, UP, DOWN, TAB = 0, 1, 2, 3


def radices(n):
    rest = max(r for r in range(1, n + 1) if r * r * r <= n and n % (r * r) == 0)
    return n // (rest * rest), rest


def mm(left, right):
    return jnp.dot(left, right, preferred_element_type=F32)


def mm_right(left, right):
    return lax.dot_general(left, right, (((1,), (1,)), ((), ())), preferred_element_type=F32)


def mm_left(left, right):
    return lax.dot_general(left, right, (((0,), (0,)), ((), ())), preferred_element_type=F32)


def normal_parts(pre):
    decay = jnp.exp2(pre * pre * (-0.5 * 1.4426950408889634))
    t = 1.0 / (1.0 + (0.3275911 * 0.7071067811865476) * jnp.abs(pre))
    poly = 0.5 * 1.061405429
    for term in (-1.453152027, 1.421413741, -0.284496736, 0.254829592):
        poly = poly * t + 0.5 * term
    tail = poly * t * decay
    phi = jnp.where(pre < 0.0, tail, 1.0 - tail)
    slope = phi + pre * (decay * 0.3989422804014327)
    return phi, slope


def normalize(value):
    mean = jnp.mean(value, axis=-1, keepdims=True)
    center = value - mean
    rstd = lax.rsqrt(jnp.mean(center * center, axis=-1, keepdims=True) + EPS)
    return center * rstd, rstd, mean


def normalize_back(d_hat, hat, rstd):
    mean_one = jnp.mean(d_hat, axis=-1, keepdims=True)
    mean_two = jnp.mean(d_hat * hat, axis=-1, keepdims=True)
    return rstd * (d_hat - mean_one - hat * mean_two)


def colsum(value):
    return jnp.sum(value, axis=0, keepdims=True)


def whole_kernel(dims, *refs):
    slots, length, rows, width, ff, head_dim, n = dims
    (
        images, cotangent, counts, v_g1, v_s1, v_bo, v_g2, v_s2, v_bd, v_qv, v_up, a_qkv, a_out, a_up, a_down,
        act_out, ing_out, f_a, f_u, f_d, f_t, hid_far, slope_far,
        x_ref, x_in, ct_in, pack_a, pack_u, pack_d, pack_t,
        wqkv, wout, wup, wdown, table, gtable, rep_one, rep_two, rep_four,
        act, out_two, ing, after_ref, nrm1, qkv, prob, ctx, hat2, nrm2, rstds,
        hid, slope,
        nrm1b, qkvb, ctxb, nrm2b, probb, hat2b, dal, low_g, left_t,
        s_a, s_u, s_d, s_t, r0_a, r0_u, r0_d, r0_t, r1_a, r1_u, r1_d, r1_t, r2_a, r2_u, r2_d, r2_t,
        r3_a, r3_u, r3_d, r3_t,
        in_s, ship_s, ship_r, far_s, ag1_s, ag1_r, ag2_s, ag2_r, ag3_s, ag3_r, ag4_s, ag4_r,
        rs0_s, rs0_r, rs1_s, rs1_r, rs2_s, rs2_r, rs3_s, rs3_r, credit,
    ) = refs
    groups = (ATT, UP, DOWN, TAB)
    pack = (pack_a, pack_u, pack_d, pack_t)
    stage = (s_a, s_u, s_d, s_t)
    r0, r1, r2 = (r0_a, r0_u, r0_d, r0_t), (r1_a, r1_u, r1_d, r1_t), (r2_a, r2_u, r2_d, r2_t)
    r3, final = (r3_a, r3_u, r3_d, r3_t), (f_a, f_u, f_d, f_t)

    first, rest = radices(n)
    unit = width // n
    core = lax.axis_index("section")
    me = lax.axis_index("fsdp")
    dig_a, dig_b, dig_c = me // (rest * rest), (me // rest) % rest, me % rest
    dig_three, dig_two = dig_c + core * (dig_b - dig_c), dig_b + core * (dig_c - dig_b)
    step_three, step_two = 1 + core * (rest - 1), rest - core * (rest - 1)
    pos = (dig_three * rest + dig_two) * first + dig_a
    pos_of = ((dig_c * rest + dig_b) * first + dig_a, (dig_b * rest + dig_c) * first + dig_a)
    sibling = {"section": 1 - core}

    def place(half, j):
        a, b, c = j // (rest * rest), (j // rest) % rest, j % rest
        return ((c * rest + b) if half == 0 else (b * rest + c)) * first + a

    def peer_first(t):
        return {"fsdp": me + ((dig_a + t) % first - dig_a) * (rest * rest)}

    def peer_two(t):
        return {"fsdp": me + ((dig_two + t) % rest - dig_two) * step_two}

    def peer_three(t):
        return {"fsdp": me + ((dig_three + t) % rest - dig_three) * step_three}

    def remote(src, dst, s_sem, r_sem, device):
        return pltpu.make_async_remote_copy(
            src_ref=src, dst_ref=dst, send_sem=s_sem, recv_sem=r_sem, device_id=device,
            device_id_type=pl.DeviceIdType.MESH,
        )

    def slab_two(three, two):
        return pl.ds((three * rest + two) * first, first)

    def slab_three(three):
        return pl.ds(three * rest * first, rest * first)

    def fill_repeats():
        for ref in (rep_one, rep_two, rep_four):
            part = ref.shape[0]
            lanes = lax.broadcasted_iota(jnp.int32, ref.shape, 1).astype(F32)
            line = lax.broadcasted_iota(jnp.int32, ref.shape, 0).astype(F32)
            rest_of = lanes - part * jnp.floor((lanes + 0.5) * (1.0 / part))
            ref[...] = jnp.where(jnp.abs(rest_of - line) < 0.5, 1.0, 0.0).astype(LOW)

    def own_lanes(part):
        shape = (n, part * n)
        lanes = lax.broadcasted_iota(jnp.int32, shape, 1)
        begin = lax.broadcasted_iota(jnp.int32, shape, 0) * part
        return (lanes >= begin) & (lanes < begin + part)

    shares = (
        ((G1, unit, rep_one), (S1, unit, rep_one), (BO, unit, rep_one), (G2, unit, rep_one), (S2, unit, rep_one),
         (BD, unit, rep_one), (BQ, 2 * unit, rep_two)),
        ((BU, 4 * unit, rep_four),),
    )

    def table_in(b):
        for half in range(2):
            lines = jnp.concatenate([s_t[b, half, place(half, j)] for j in range(n)], axis=0)
            begin = 0
            for row, part, ref in shares[half]:
                spread = mm(lines[:, begin : begin + part].astype(LOW), ref[...])
                line = colsum(jnp.where(own_lanes(part), spread, 0.0))
                for i in range(part * n // width):
                    table[b, row + i : row + i + 1, :] = line[:, width * i : width * (i + 1)]
                begin += part

    def table_out(b):
        for half in range(2):
            parts, begin = [], 0
            for row, part, ref in shares[half]:
                count = part * n // width
                line = jnp.concatenate([gtable[b, row + i : row + i + 1, :] for i in range(count)], axis=1)
                parts.append(mm_right(jnp.where(own_lanes(part), line, 0.0).astype(LOW), ref[...]))
                begin += part
            parts.append(jnp.zeros((n, width - begin), F32))
            lines = jnp.concatenate(parts, axis=1)
            for j in range(n):
                s_t[b, half, place(half, j)] = lines[j : j + 1]

    def pack_own():
        for half in range(2):
            vectors = ((v_g1, v_s1, v_bo, v_g2, v_s2, v_bd, v_qv), (v_up,))[half]
            lines = [vector[...].astype(F32) for vector in vectors]
            lines.append(jnp.zeros((1, width - sum(line.shape[1] for line in lines)), F32))
            pack_t[half] = jnp.concatenate(lines, axis=1)
            for ref in (pack_a, pack_u):
                both = []
                for part in (2 * half, 2 * half + 1):
                    if ref is pack_u:
                        both.append(a_up[0, :, part * width : (part + 1) * width])
                    elif part == 3:
                        both.append(a_out[0])
                    else:
                        both.append(a_qkv[0, :, part * width : (part + 1) * width])
                ref[half] = jnp.concatenate([value.astype(F32) for value in both], axis=0).astype(LOW)
            pack_d[half] = a_down[0, 2 * unit * half : 2 * unit * (half + 1), :]

    def at(b, g):
        return len(groups) * b + g

    def ag1_copy(b, g, half, t):
        device = {"section": half, **peer_first(t)} if t else sibling
        return remote(
            pack[g].at[half], stage[g].at[b, half, pos_of[half]],
            ag1_s.at[g, half, t], ag1_r.at[at(b, g), t], device,
        )

    def ag1_landing(b, g, t):
        ref = stage[g].at[b, core, (dig_three * rest + dig_two) * first + (dig_a + first - t) % first]
        return remote(ref, ref, ag1_s.at[g, 0, t], ag1_r.at[at(b, g), t], sibling)

    def ag2_copy(b, g, t):
        ref = stage[g].at[b, core, slab_two(dig_three, dig_two)]
        return remote(ref, ref, ag2_s.at[at(b, g), t - 1], ag2_r.at[at(b, g), t - 1], peer_two(t))

    def ag3_copy(b, g, t):
        ref = stage[g].at[b, core, slab_three(dig_three)]
        return remote(ref, ref, ag3_s.at[at(b, g), t - 1], ag3_r.at[at(b, g), t - 1], peer_three(t))

    def ag4_copy(b, g, t):
        ref = stage[g].at[b, core, slab_three((dig_three + rest - t) % rest)]
        return remote(ref, ref, ag4_s.at[at(b, g), t], ag4_r.at[at(b, g), t], sibling)

    def ag4_landing(b, g, t):
        ref = stage[g].at[b, 1 - core, slab_three((dig_two + rest - t) % rest)]
        return remote(ref, ref, ag4_s.at[at(b, g), t], ag4_r.at[at(b, g), t], sibling)

    def ag1(b, g):
        @pl.when(core == b)
        def _():
            for t in range(1, first):
                for half in range(2):
                    ag1_copy(b, g, half, t).start()
            ag1_copy(b, g, 1 - b, 0).start()
            stage[g][b, b, pos] = pack[g][b]

    def ag2(b, g):
        for t in range(1, first):
            ag1_landing(b, g, t).wait_recv()

        @pl.when(core != b)
        def _():
            ag1_landing(b, g, 0).wait_recv()

        for t in range(1, rest):
            ag2_copy(b, g, t).start()

    def ag3(b, g):
        for t in range(1, rest):
            ag2_copy(b, g, t).wait_recv()
        for t in range(1, rest):
            ag3_copy(b, g, t).start()
        ag4_copy(b, g, 0).start()

    def ag4(b, g):
        for t in range(1, rest):
            ag3_copy(b, g, t).wait_recv()
            ag4_copy(b, g, t).start()

    def ag5(b, g):
        for t in range(rest):
            ag4_landing(b, g, t).wait_recv()
        lay_out(b, g)

    def ag_sent(b, g):
        @pl.when(core == b)
        def _():
            for t in range(1, first):
                for half in range(2):
                    ag1_copy(b, g, half, t).wait_send()
            ag1_copy(b, g, 1 - b, 0).wait_send()

        for t in range(1, rest):
            ag2_copy(b, g, t).wait_send()
            ag3_copy(b, g, t).wait_send()
        for t in range(rest):
            ag4_copy(b, g, t).wait_send()

    def lay_out(b, g):
        if g == TAB:
            table_in(b)
            return
        if g == DOWN:
            for j in range(n):
                for half in range(2):
                    begin = 4 * unit * j + 2 * unit * half
                    wdown[b, begin : begin + 2 * unit, :] = s_d[b, half, place(half, j)]
            return
        together = 16 // math.gcd(unit, 16)
        for half in range(2):
            for j in range(0, n, together):
                pieces = [stage[g][b, half, place(half, j + i)].astype(F32) for i in range(together)]
                for sub in range(2):
                    low = sub * unit
                    block = jnp.concatenate([piece[low : low + unit] for piece in pieces], axis=0).astype(LOW)
                    part = 2 * half + sub
                    down = slice(unit * j, unit * (j + together))
                    if g == UP:
                        wup[b, down, part * width : (part + 1) * width] = block
                    elif part == 3:
                        wout[b, down, :] = block
                    else:
                        wqkv[b, down, part * width : (part + 1) * width] = block

    def rs0_copy(b, g):
        return remote(stage[g].at[b, 1 - core], r0[g], rs0_s.at[at(b, g)], rs0_r.at[at(b, g)], sibling)

    def rs1_copy(b, g, t):
        return remote(
            stage[g].at[b, core, slab_three((dig_three + t) % rest)], r1[g].at[t - 1],
            rs1_s.at[at(b, g), t - 1], rs1_r.at[at(b, g), t - 1], peer_three(t),
        )

    def rs2_copy(b, g, t):
        return remote(
            stage[g].at[b, core, slab_two(dig_three, (dig_two + t) % rest)], r2[g].at[b, t - 1],
            rs2_s.at[at(b, g), t - 1], rs2_r.at[at(b, g), t - 1], peer_two(t),
        )

    def rs3_copy(b, g, t):
        there = (dig_three * rest + dig_two) * first + (dig_a + t) % first
        device = {"section": b, **peer_first(t)} if t else sibling
        return remote(
            stage[g].at[b, core, there], r3[g].at[core, t], rs3_s.at[at(b, g), t], rs3_r.at[g, core, t], device
        )

    def rs0(b, g):
        if b == 0:
            pl.semaphore_wait(credit.at[0, g], 1)
        rs0_copy(b, g).start()

    def rs1(b, g):
        rs0_copy(b, g).wait_recv()

        @pl.loop(0, n)
        def _(p):
            stage[g][b, core, p] = stage[g][b, core, p] + r0[g][p]

        if b == 1:
            pl.semaphore_signal(credit.at[0, g], inc=1, device_id=sibling, device_id_type=pl.DeviceIdType.MESH)
        elif rest > 1:
            pl.semaphore_wait(credit.at[1, g], rest - 1)
        for t in range(1, rest):
            rs1_copy(b, g, t).start()

    def rs2(b, g):
        for t in range(1, rest):
            rs1_copy(b, g, t).wait_recv()

        @pl.loop(0, rest * first)
        def _(p):
            here = dig_three * rest * first + p
            total = stage[g][b, core, here].astype(F32)
            for t in range(1, rest):
                total = total + r1[g][t - 1, p].astype(F32)
            stage[g][b, core, here] = total.astype(stage[g].dtype)

        for t in range(1, rest):
            if b == 1:
                pl.semaphore_signal(
                    credit.at[1, g], inc=1, device_id=peer_three(t), device_id_type=pl.DeviceIdType.MESH
                )
            rs2_copy(b, g, t).start()

    def rs3(b, g):
        for t in range(1, rest):
            rs2_copy(b, g, t).wait_recv()

        @pl.loop(0, first)
        def _(p):
            here = (dig_three * rest + dig_two) * first + p
            total = stage[g][b, core, here].astype(F32)
            for t in range(1, rest):
                total = total + r2[g][b, t - 1, p].astype(F32)
            stage[g][b, core, here] = total.astype(stage[g].dtype)

        for t in range(1, first):
            rs3_copy(b, g, t).start()

        @pl.when(core != b)
        def _():
            rs3_copy(b, g, 0).start()

    def rs4(b, g):
        @pl.when(core == b)
        def _():
            for half in range(2):
                begin = int(half == b)
                for t in range(begin, first):
                    ref = r3[g].at[half, t]
                    remote(ref, ref, rs3_s.at[at(b, g), t], rs3_r.at[g, half, t], sibling).wait_recv()
                total = stage[g][b, b, pos].astype(F32) if half == b else None
                for t in range(begin, first):
                    value = r3[g][half, t].astype(F32)
                    total = value if total is None else total + value
                final[g][half] = total

    def rs_sent(b, g):
        rs0_copy(b, g).wait_send()
        for t in range(1, rest):
            rs1_copy(b, g, t).wait_send()
            rs2_copy(b, g, t).wait_send()
        for t in range(1, first):
            rs3_copy(b, g, t).wait_send()

        @pl.when(core != b)
        def _():
            rs3_copy(b, g, 0).wait_send()

    def rows_of(i, images_too=1):
        return pl.ds(pl.multiple_of(i * rows, 16), images_too * rows)

    many = TOGETHER if slots % TOGETHER == 0 else 1
    steps = slots // many

    def step_rows(i):
        return rows_of(i * many, many)

    def ship_parts(kind, b, i):
        src, out = ((out_two if b else act, act_out), (ing, ing_out))[kind]
        q = 2 * kind + b
        rd = rows_of(i)
        near = pltpu.make_async_copy(src.at[rd], out.at[core, rd], ship_s.at[q, i])
        far = remote(src.at[rd], out.at[core, rd], ship_s.at[q, i], ship_r.at[q, i], sibling)
        return near, far

    def ship(kind, b, i):
        near, far = ship_parts(kind, b, i)

        @pl.when(core == b)
        def _():
            near.start()

        @pl.when(core != b)
        def _():
            far.start()

    def shipped(kind, b, i):
        near, far = ship_parts(kind, b, i)

        @pl.when(core == b)
        def _():
            near.wait()

        @pl.when(core != b)
        def _():
            far.wait_send()

    def landed(kind, b, i):
        out = (act_out, ing_out)[kind]
        q = 2 * kind + b
        ref = out.at[1 - core, rows_of(i)]

        @pl.when(core == b)
        def _():
            remote(ref, ref, ship_s.at[q, i], ship_r.at[q, i], sibling).wait_recv()

    def live(i):
        return jnp.where(i < counts[0, core], 1.0, 0.0).astype(F32)

    def only_live(i, value):
        parts = [value[rows * m : rows * (m + 1)] * live(i * many + m) for m in range(many)]
        return jnp.concatenate(parts, axis=0)

    def coming(which, i):
        source, target = ((images, x_in), (cotangent, ct_in))[which]
        return pltpu.make_async_copy(source.at[core, i], target.at[i], in_s.at[which, i])

    def far_copy(which, i, back):
        near, far = ((hid, hid_far), (slope, slope_far))[which]
        near, far = near.at[rows_of(i)], far.at[rows_of(i)]
        src, dst = (far, near) if back else (near, far)
        return pltpu.make_async_copy(src, dst, far_s.at[2 * int(back) + which, i])

    pairs = width // 128
    scale = head_dim ** -0.5
    lane = lax.broadcasted_iota(jnp.int32, (1, 128), 1)
    half_low = [(lane < head_dim).astype(LOW), (lane >= head_dim).astype(LOW)]
    half_f = [(lane < head_dim).astype(F32), (lane >= head_dim).astype(F32)]
    key_pad = jnp.where(lax.broadcasted_iota(jnp.int32, (1, rows), 1) < length, 0.0, -1e30).astype(F32)
    chunk = 256
    chunks = ff // chunk

    def vec(s, r):
        return table[s, r : r + 1, :]

    def up_bias(s, c):
        begin = c * chunk
        row, col = begin // width, begin % width
        if col + chunk <= width:
            return table[s, BU + row : BU + row + 1, col : col + chunk]
        a = table[s, BU + row : BU + row + 1, col:width]
        b = table[s, BU + row + 1 : BU + row + 2, 0 : chunk - (width - col)]
        return jnp.concatenate([a, b], axis=1)

    def add_vec(s, r, value):
        gtable[s, r : r + 1, :] += value

    def add_up_bias(s, c, value):
        begin = c * chunk
        row, col = begin // width, begin % width
        if col + chunk <= width:
            gtable[s, BU + row : BU + row + 1, col : col + chunk] += value
        else:
            cut = width - col
            gtable[s, BU + row : BU + row + 1, col:width] += value[:, :cut]
            gtable[s, BU + row + 1 : BU + row + 2, 0 : chunk - cut] += value[:, cut:]

    def attn_forward(s, x, hat, i, nrm_ref, qkv_ref, prob_ref, ctx_ref):
        rd = step_rows(i)
        nrm = (hat * vec(s, G1) + vec(s, S1)).astype(LOW)
        nrm_ref[rd, :] = nrm
        q = (mm(nrm, wqkv[s, :, 0:width]) + vec(s, BQ)).astype(LOW)
        k = mm(nrm, wqkv[s, :, width : 2 * width]).astype(LOW)
        v = (mm(nrm, wqkv[s, :, 2 * width :]) + vec(s, BV)).astype(LOW)
        qkv_ref[rd, 0:width] = q
        qkv_ref[rd, width : 2 * width] = k
        qkv_ref[rd, 2 * width :] = v
        images_out = []
        for m in range(many):
            mine = slice(rows * m, rows * (m + 1))
            parts = []
            for p in range(pairs):
                cols = slice(128 * p, 128 * p + 128)
                total = None
                for j in range(2):
                    scores = mm_right(q[mine, cols], k[mine, cols] * half_low[j]) + key_pad
                    top = jnp.max(scores, axis=-1, keepdims=True)
                    e = jnp.exp2((scores - top) * (scale * 1.4426950408889634))
                    pr = (e * (1.0 / jnp.sum(e, axis=-1, keepdims=True))).astype(LOW)
                    prob_ref[i * many + m, 2 * p + j] = pr
                    part = mm(pr, v[mine, cols] * half_low[j])
                    total = part if total is None else total + part
                parts.append(total.astype(LOW))
            images_out.append(jnp.concatenate(parts, axis=1))
        context = jnp.concatenate(images_out, axis=0)
        ctx_ref[rd, :] = context
        return x + mm(context, wout[s]) + vec(s, BO)

    def ff_forward(s, after, rd, srd, hat_ref, nrm_ref):
        hat, rstd, _ = normalize(after)
        hat_ref[srd, :] = hat.astype(LOW)
        nrm = (hat * vec(s, G2) + vec(s, S2)).astype(LOW)
        nrm_ref[rd, :] = nrm
        total = after + vec(s, BD)
        for c in range(chunks):
            cols = slice(chunk * c, chunk * c + chunk)
            pre = mm(nrm, wup[s, :, cols]) + up_bias(s, c)
            phi, slo = normal_parts(pre)
            h = (pre * phi).astype(LOW)
            hid[rd, cols] = h
            slope[rd, cols] = slo.astype(LOW)
            total = total + mm(h, wdown[s, cols, :])
        return total, rstd

    def ff_backward(s, g, rd, srd, hat_ref, rstd):
        g_low = g.astype(LOW)
        add_vec(s, BD, colsum(g_low.astype(F32)))
        d_nrm = None
        for c in range(chunks):
            cols = slice(chunk * c, chunk * c + chunk)
            d_hid = mm_right(g_low, wdown[s, cols, :])
            d_pre = (d_hid * slope[rd, cols].astype(F32)).astype(LOW)
            slope[rd, cols] = d_pre
            add_up_bias(s, c, colsum(d_pre.astype(F32)))
            part = mm_right(d_pre, wup[s, :, cols])
            d_nrm = part if d_nrm is None else d_nrm + part
        hat = hat_ref[srd, :].astype(F32)
        add_vec(s, G2, colsum(d_nrm * hat))
        add_vec(s, S2, colsum(d_nrm))
        d_after = g + normalize_back(d_nrm * vec(s, G2), hat, rstd)
        low = d_after.astype(LOW)
        dal[rd, :] = low
        add_vec(s, BO, colsum(low.astype(F32)))
        return d_after

    def attn_backward(s, i, qkv_ref, prob_ref, ctx_ref):
        d_context = mm_right(dal[step_rows(i), :], wout[s]).astype(LOW)
        for m in range(many):
            rd = rows_of(i * many + m)
            d_ctx = d_context[rows * m : rows * (m + 1)]
            dq, dk, dv = [], [], []
            for p in range(pairs):
                cols = slice(128 * p, 128 * p + 128)
                q = qkv_ref[rd, 128 * p : 128 * p + 128]
                k = qkv_ref[rd, width + 128 * p : width + 128 * p + 128]
                v = qkv_ref[rd, 2 * width + 128 * p : 2 * width + 128 * p + 128]
                dc = d_ctx[:, cols]
                both = dc.astype(F32) * ctx_ref[rd, cols].astype(F32)
                sums = [None, None, None]
                for j in range(2):
                    pr = prob_ref[i * many + m, 2 * p + j]
                    delta = jnp.sum(both * half_f[j], axis=-1, keepdims=True)
                    d_prob = mm_right(dc, v * half_low[j])
                    ds = (pr.astype(F32) * (d_prob - delta)).astype(LOW)
                    new = [mm(ds, k * half_low[j]), mm_left(ds, q * half_low[j]), mm_left(pr, dc * half_low[j])]
                    sums = [b if a is None else a + b for a, b in zip(sums, new)]
                dq.append((sums[0] * scale).astype(LOW))
                dk.append((sums[1] * scale).astype(LOW))
                dv.append(sums[2].astype(LOW))
            d_mixed = jnp.concatenate(dq + dk + dv, axis=1)
            qkv_ref[rd, :] = d_mixed
            add_vec(s, BQ, colsum(d_mixed[:, 0:width].astype(F32)))
            add_vec(s, BV, colsum(d_mixed[:, 2 * width :].astype(F32)))

    def input_backward(s, d_after, rd, x, mean, rstd, qkv_ref):
        d_nrm = mm_right(qkv_ref[rd, :], wqkv[s])
        hat = (x - mean) * rstd
        add_vec(s, G1, colsum(d_nrm * hat))
        add_vec(s, S1, colsum(d_nrm))
        return d_after + normalize_back(d_nrm * vec(s, G1), hat, rstd)

    def grads_down(s):
        left_t[...] = low_g[...].T

        @pl.loop(0, 4)
        def _(c):
            cols = pl.ds(pl.multiple_of(c * width, 128), width)
            block = mm(left_t[...], hid[:, cols]).T
            for i in range(n // 4):
                for half in range(2):
                    begin = 4 * unit * i + 2 * unit * half
                    s_d[s, half, place(half, c * (n // 4) + i)] = block[begin : begin + 2 * unit].astype(LOW)

    def pair_out(ref, s, half, one, two):
        for j in range(n):
            down = slice(unit * j, unit * (j + 1))
            piece = jnp.concatenate([one[down], two[down]], axis=0).astype(LOW)
            ref[s, half, place(half, j)] = piece

    def grads_up(s):
        left_t[...] = nrm2_of[s][...].T
        for half in range(2):
            one, two = [
                mm(left_t[...], slope[:, part * width : (part + 1) * width]) for part in (2 * half, 2 * half + 1)
            ]
            pair_out(s_u, s, half, one, two)

    def grads_attn(s):
        ctx_s, nrm_s, mix_s = ((ctx, nrm1, qkv), (ctxb, nrm1b, qkvb))[s]
        left_t[...] = ctx_s[...].T
        four = mm(left_t[...], dal[...])
        left_t[...] = nrm_s[...].T
        three = mm(left_t[...], mix_s[:, 2 * width :])
        pair_out(s_a, s, 1, three, four)
        one = mm(left_t[...], mix_s[:, 0:width])
        two = mm(left_t[...], mix_s[:, width : 2 * width])
        pair_out(s_a, s, 0, one, two)

    nrm2_of = (nrm2, nrm2b)
    here = pl.ds(0, many * rows)

    barrier = pltpu.get_barrier_semaphore()
    greeted = [sibling]
    greeted += [{"section": half, **peer_first(t)} for t in range(1, first) for half in range(2)]
    greeted += [f(t) for f in (peer_two, peer_three) for t in range(1, rest)]
    for device in greeted:
        pl.semaphore_signal(barrier, inc=1, device_id=device, device_id_type=pl.DeviceIdType.MESH)
    pack_own()
    pl.semaphore_wait(barrier, len(greeted))

    def run(*todo):
        for f, b, g in todo:
            f(b, g)

    def events(i, table_of):
        for when, todo in table_of.items():
            @pl.when(i == when)
            def _():
                run(*todo)

    run((ag1, 0, TAB), (ag1, 0, ATT))
    for which in range(2):
        for i in range(slots):
            coming(which, i).start()
    fill_repeats()
    gtable[...] = jnp.zeros_like(gtable)
    low_g[...] = jnp.zeros_like(low_g)
    x_ref[...] = jnp.zeros_like(x_ref)
    run((ag2, 0, TAB), (ag2, 0, ATT), (ag1, 0, UP), (ag1, 0, DOWN))

    @pl.loop(0, steps)
    def norm_one(i):
        for m in range(many):
            coming(0, i * many + m).wait()
            x_ref[pl.ds(pl.multiple_of((i * many + m) * rows, 16), length), :] = x_in[i * many + m]
        rd = step_rows(i)
        hat, rstd, mean = normalize(x_ref[rd, :].astype(F32))
        after_ref[rd, :] = hat
        rstds[rd, 0:1] = rstd
        rstds[rd, 2:3] = mean

    run((ag3, 0, TAB), (ag3, 0, ATT), (ag2, 0, UP), (ag1, 1, TAB), (ag1, 1, ATT))
    run((ag2, 0, DOWN), (ag1, 1, UP), (ag1, 1, DOWN))
    run((ag4, 0, TAB), (ag4, 0, ATT), (ag3, 0, UP), (ag5, 0, TAB), (ag5, 0, ATT))

    @pl.loop(0, steps)
    def attn_one(i):
        events(i, {
            0: [(ag3, 0, DOWN), (ag2, 1, TAB), (ag2, 1, ATT)],
            1: [(ag4, 0, UP), (ag2, 1, UP)],
            2: [(ag4, 0, DOWN)],
        })
        rd = step_rows(i)
        x = x_ref[rd, :].astype(F32)
        after_ref[rd, :] = attn_forward(0, x, after_ref[rd, :], i, nrm1, qkv, prob, ctx)

    run((ag3, 1, TAB), (ag3, 1, ATT), (ag5, 0, UP), (ag5, 0, DOWN))

    @pl.loop(0, steps)
    def ff_one(i):
        events(i, {
            0: [(ag3, 1, UP), (ag2, 1, DOWN)],
            1: [(ag4, 1, TAB), (ag4, 1, ATT)],
            2: [(ag4, 1, UP)],
        })
        rd = step_rows(i)
        out, rstd2 = ff_forward(0, after_ref[rd, :], rd, rd, hat2, nrm2)
        act[rd, :] = only_live(i, out).astype(LOW)
        rstds[rd, 1:2] = rstd2
        for m in range(many):
            far_copy(0, i * many + m, False).start()
            far_copy(1, i * many + m, False).start()
            ship(0, 0, i * many + m)

    run((ag3, 1, DOWN), (ag5, 1, TAB), (ag5, 1, ATT))

    @pl.loop(0, steps)
    def attn_two(i):
        events(i, {2: [(ag4, 1, DOWN)]})
        rd = step_rows(i)
        x = act[rd, :].astype(F32)
        hat, rstd, mean = normalize(x)
        rstds[rd, 3:4] = rstd
        rstds[rd, 4:5] = mean
        after_ref[rd, :] = attn_forward(1, x, hat, i, nrm1b, qkvb, probb, ctxb)

    run((ag5, 1, UP), (ag5, 1, DOWN))

    @pl.loop(0, steps)
    def ff_two(i):
        rd = step_rows(i)
        for m in range(many):
            far_copy(0, i * many + m, False).wait()
            far_copy(1, i * many + m, False).wait()
            coming(1, i * many + m).wait()
            g = live(i * many + m) * ct_in[i * many + m].astype(F32)
            low_g[pl.ds(pl.multiple_of((i * many + m) * rows, 16), length), :] = g.astype(LOW)
        out, rstd2 = ff_forward(1, after_ref[rd, :], rd, here, hat2b, nrm2b)
        out_two[rd, :] = only_live(i, out).astype(LOW)
        for m in range(many):
            ship(0, 1, i * many + m)
        after_ref[rd, :] = ff_backward(1, low_g[rd, :].astype(F32), rd, here, hat2b, rstd2)

    for b in range(2):
        for g in groups:
            ag_sent(b, g)

    grads_down(1)
    run((rs0, 1, DOWN))

    @pl.loop(0, slots)
    def hid_back(i):
        far_copy(0, i, True).start()

    grads_up(1)
    run((rs0, 1, UP), (rs1, 1, DOWN))

    @pl.loop(0, slots)
    def slope_back(i):
        far_copy(1, i, True).start()

    @pl.loop(0, steps)
    def attn_back_two(i):
        events(i, {
            1: [(rs1, 1, UP), (rs2, 1, DOWN)],
            2: [(rs2, 1, UP), (rs3, 1, DOWN)],
        })
        rd = step_rows(i)
        attn_backward(1, i, qkvb, probb, ctxb)
        x = act[rd, :].astype(F32)
        d_in = input_backward(1, after_ref[rd, :], rd, x, rstds[rd, 4:5], rstds[rd, 3:4], qkvb)
        ing[rd, :] = d_in.astype(LOW)
        for m in range(many):
            ship(1, 1, i * many + m)

    grads_attn(1)
    table_out(1)
    run((rs0, 1, ATT), (rs0, 1, TAB), (rs3, 1, UP), (rs4, 1, DOWN))

    @pl.loop(0, steps)
    def ff_back_one(i):
        events(i, {1: [(rs1, 1, ATT), (rs1, 1, TAB)], 2: [(rs4, 1, UP)]})
        rd = step_rows(i)
        for m in range(many):
            far_copy(1, i * many + m, True).wait()
        g = only_live(i, ing[rd, :].astype(F32))
        low_g[rd, :] = g.astype(LOW)
        after_ref[rd, :] = ff_backward(0, g, rd, rd, hat2, rstds[rd, 1:2])

    @pl.loop(0, slots)
    def hid_is_back(i):
        far_copy(0, i, True).wait()

    run((rs2, 1, ATT), (rs2, 1, TAB))
    grads_down(0)
    run((rs0, 0, DOWN))
    grads_up(0)
    run((rs0, 0, UP), (rs1, 0, DOWN), (rs3, 1, ATT), (rs3, 1, TAB))

    @pl.loop(0, steps)
    def attn_back_one(i):
        events(i, {
            1: [(rs1, 0, UP), (rs2, 0, DOWN), (rs4, 1, ATT), (rs4, 1, TAB)],
            2: [(rs2, 0, UP), (rs3, 0, DOWN)],
        })
        attn_backward(0, i, qkv, prob, ctx)

    grads_attn(0)
    run((rs0, 0, ATT), (rs3, 0, UP))

    @pl.loop(0, steps)
    def input_one(i):
        events(i, {2: [(rs1, 0, ATT), (rs4, 0, DOWN)]})
        rd = step_rows(i)
        x = x_ref[rd, :].astype(F32)
        d_in = input_backward(0, after_ref[rd, :], rd, x, rstds[rd, 2:3], rstds[rd, 0:1], qkv)
        for m in range(many):
            shipped(1, 1, i * many + m)
        ing[rd, :] = d_in.astype(LOW)
        for m in range(many):
            ship(1, 0, i * many + m)

    table_out(0)
    run((rs0, 0, TAB), (rs2, 0, ATT), (rs1, 0, TAB), (rs4, 0, UP), (rs3, 0, ATT), (rs2, 0, TAB), (rs3, 0, TAB))

    @pl.loop(0, slots)
    def all_out(i):
        shipped(0, 0, i)
        shipped(0, 1, i)
        shipped(1, 0, i)
        for kind in range(2):
            for b in range(2):
                landed(kind, b, i)

    run((rs4, 0, ATT), (rs4, 0, TAB))
    for b in range(2):
        for g in groups:
            rs_sent(b, g)


def output_kernel(
    f_a, f_u, f_d, f_t, o_g1, o_s1, o_qkv, o_qv, o_out, o_bo, o_g2, o_s2, o_up, o_bu, o_down, o_bd
):
    unit, width = o_out.shape[1:]
    for half in range(2):
        o_down[0, 2 * unit * half : 2 * unit * (half + 1), :] = f_d[half]
        for sub in range(2):
            part = 2 * half + sub
            cols = slice(part * width, (part + 1) * width)
            o_up[0, :, cols] = f_u[half, unit * sub : unit * (sub + 1), :]
            piece = f_a[half, unit * sub : unit * (sub + 1), :]
            if part == 3:
                o_out[0] = piece
            else:
                o_qkv[0, :, cols] = piece
    begin = 0
    for out in (o_g1, o_s1, o_bo, o_g2, o_s2, o_bd, o_qv):
        part = out.shape[1]
        out[...] = f_t[0, :, begin : begin + part]
        begin += part
    o_bu[...] = f_t[1, :, 0 : o_bu.shape[1]]


def local(
    images, cotangent, counts,
    ln1_gain, ln1_bias, w_qkv, b_qv, w_out, b_out, ln2_gain, ln2_bias, w_up, b_up, w_down, b_down,
):
    micro_count, slots, length, width = images.shape
    ff = w_up.shape[2]
    rows = -(-length // 16) * 16
    n = lax.axis_size("fsdp")
    unit = width // n
    first, rest = radices(n)
    total = slots * rows
    head_dim = width // HEADS

    def vm(*shape, kind=LOW):
        return pltpu.VMEM(shape, kind)

    tall = [(2 * unit, LOW)] * 3 + [(1, F32)]
    dma = lambda *shape: pltpu.SemaphoreType.DMA(shape)
    outs = [((2, total, width), LOW), ((2, total, width), LOW)]
    outs += [((2, r, width), F32) for r, _ in tall] + [((total, ff), LOW), ((total, ff), LOW)]
    scratch = [
        vm(total, width), vm(slots, length, width), vm(slots, length, width), *[vm(2, r, width, kind=kind) for r, kind in tall],
        vm(2, width, 3 * width), vm(2, width, width), vm(2, width, ff), vm(2, ff, width),
        vm(2, TABLE, width, kind=F32), vm(2, TABLE, width, kind=F32),
        vm(unit, width), vm(2 * unit, 2 * width), vm(4 * unit, 4 * width),
        vm(total, width), vm(total, width), vm(total, width), vm(total, width, kind=F32),
        vm(total, width), vm(total, 3 * width), vm(slots, HEADS, rows, rows), vm(total, width),
        vm(total, width), vm(total, width), vm(total, 5, kind=F32),
        vm(total, ff), vm(total, ff),
        vm(total, width), vm(total, 3 * width), vm(total, width), vm(total, width), vm(slots, HEADS, rows, rows),
        vm(TOGETHER * rows, width), vm(total, width), vm(total, width), vm(width, total),
    ]
    scratch += [vm(2, 2, n, r, width, kind=kind) for r, kind in tall]
    scratch += [vm(n, r, width, kind=kind) for r, kind in tall]
    scratch += [vm(rest - 1, rest * first, r, width, kind=kind) for r, kind in tall]
    scratch += [vm(2, rest - 1, first, r, width, kind=kind) for r, kind in tall]
    scratch += [vm(2, first, r, width, kind=kind) for r, kind in tall]
    scratch += [dma(2, slots), dma(4, slots), dma(4, slots), dma(4, slots)]
    scratch += [dma(4, 2, first), dma(8, first)] + [dma(8, rest - 1)] * 4 + [dma(8, rest)] * 2
    scratch += [dma(8)] * 2 + [dma(8, rest - 1)] * 4 + [dma(8, first), dma(4, 2, first)]
    scratch += [pltpu.SemaphoreType.REGULAR((2, 4))]
    dims = (slots, length, rows, width, ff, head_dim, n)
    vmem = pl.BlockSpec(memory_space=pltpu.VMEM)
    hbm = pl.BlockSpec(memory_space=pltpu.HBM)
    acts, ings, f_a, f_u, f_d, f_t, _, _ = pl.pallas_call(
        functools.partial(whole_kernel, dims),
        out_shape=[jax.ShapeDtypeStruct(*o) for o in outs],
        in_specs=[hbm, hbm, pl.BlockSpec(memory_space=pltpu.SMEM)] + [vmem] * 12,
        out_specs=[hbm, hbm] + [vmem] * 4 + [hbm, hbm],
        scratch_shapes=scratch,
        compiler_params=pltpu.CompilerParams(
            vmem_limit_bytes=(64 << 20) - (96 << 10), collective_id=0, has_side_effects=True
        ),
    )(
        images, cotangent, counts.T, ln1_gain, ln1_bias, b_out, ln2_gain, ln2_bias, b_down, b_qv, b_up,
        w_qkv, w_out, w_up, w_down,
    )

    params = (
        ln1_gain, ln1_bias, w_qkv, b_qv, w_out, b_out, ln2_gain, ln2_bias, w_up, b_up, w_down, b_down
    )
    grads = pl.pallas_call(
        output_kernel,
        out_shape=[jax.ShapeDtypeStruct(p.shape, F32) for p in params],
        in_specs=[vmem] * 4,
        out_specs=[vmem] * len(params),
    )(f_a, f_u, f_d, f_t)

    def images_of(value):
        return value.reshape(1, 2, slots, rows, width)[:, :, :, :length]

    return (images_of(acts), images_of(ings), *grads)


def solution(mesh):
    split = P("section", "fsdp")
    cube = P("section", "fsdp", None)
    image = P(None, "fsdp", None, None)
    result = P("section", None, "fsdp", None, None)
    params = (split, split, cube, split, cube, split, split, split, cube, split, cube, split)
    return jax.shard_map(
        local,
        mesh=mesh,
        in_specs=(image, image, P(None, "fsdp")) + params,
        out_specs=(result, result) + params,
        check_vma=False,
    )
```

```python
import functools
import math

import jax
import jax.numpy as jnp
from jax import lax
from jax.experimental import pallas as pl
from jax.experimental.pallas import tpu as pltpu
from jax.sharding import PartitionSpec as P

HEADS = 6
EPS = 1e-06
F32 = jnp.float32
LOW = jnp.bfloat16

G1, S1, BO, G2, S2, BD, BQ, BV, BU = 0, 1, 2, 3, 4, 5, 6, 7, 8
TABLE = 16
TOGETHER = 2
ATT, UP, DOWN, TAB = 0, 1, 2, 3


def radices(n):
    rest = max(r for r in range(1, n + 1) if r * r * r <= n and n % (r * r) == 0)
    return n // (rest * rest), rest


def mm(left, right):
    return jnp.dot(left, right, preferred_element_type=F32)


def mm_right(left, right):
    return lax.dot_general(left, right, (((1,), (1,)), ((), ())), preferred_element_type=F32)


def mm_left(left, right):
    return lax.dot_general(left, right, (((0,), (0,)), ((), ())), preferred_element_type=F32)


def normal_parts(pre):
    decay = jnp.exp2(pre * pre * (-0.5 * 1.4426950408889634))
    t = 1.0 / (1.0 + (0.3275911 * 0.7071067811865476) * jnp.abs(pre))
    poly = 0.5 * 1.061405429
    for term in (-1.453152027, 1.421413741, -0.284496736, 0.254829592):
        poly = poly * t + 0.5 * term
    tail = poly * t * decay
    phi = jnp.where(pre < 0.0, tail, 1.0 - tail)
    slope = phi + pre * (decay * 0.3989422804014327)
    return phi, slope


def normalize(value):
    mean = jnp.mean(value, axis=-1, keepdims=True)
    center = value - mean
    rstd = lax.rsqrt(jnp.mean(center * center, axis=-1, keepdims=True) + EPS)
    return center * rstd, rstd, mean


def normalize_back(d_hat, hat, rstd):
    mean_one = jnp.mean(d_hat, axis=-1, keepdims=True)
    mean_two = jnp.mean(d_hat * hat, axis=-1, keepdims=True)
    return rstd * (d_hat - mean_one - hat * mean_two)


def colsum(value):
    return jnp.sum(value, axis=0, keepdims=True)


def whole_kernel(dims, *refs):
    slots, length, rows, width, ff, head_dim, n = dims
    (
        images, cotangent, counts, v_g1, v_s1, v_bo, v_g2, v_s2, v_bd, v_qv, v_up, a_qkv, a_out, a_up, a_down,
        act_out, ing_out, f_a, f_u, f_d, f_t, hid_far, slope_far,
        xs, io_one, io_two, pack_a, pack_u, pack_d, pack_t,
        wqkv, wout, wup, wdown, table, gtable, rep_one, rep_two, rep_four,
        after_ref, nrm1, qkv, prob, ctx, hat2, nrm2, rstds, hid, slope, dal, low_g, left_t,
        s_a, s_u, s_d, s_t, r0_a, r0_u, r0_d, r0_t, r1_a, r1_u, r1_d, r1_t, r2_a, r2_u, r2_d, r2_t,
        r3_a, r3_u, r3_d, r3_t,
        in_s, ship_s, ship_r, far_s, ag1_s, ag1_r, ag2_s, ag2_r, ag3_s, ag3_r, ag4_s, ag4_r,
        rs0_s, rs0_r, rs1_s, rs1_r, rs2_s, rs2_r, rs3_s, rs3_r, credit,
    ) = refs
    groups = (ATT, UP, DOWN, TAB)
    pack = (pack_a, pack_u, pack_d, pack_t)
    stage = (s_a, s_u, s_d, s_t)
    r0, r1, r2 = (r0_a, r0_u, r0_d, r0_t), (r1_a, r1_u, r1_d, r1_t), (r2_a, r2_u, r2_d, r2_t)
    r3, final = (r3_a, r3_u, r3_d, r3_t), (f_a, f_u, f_d, f_t)

    first, rest = radices(n)
    unit = width // n
    core = lax.axis_index("section")
    me = lax.axis_index("fsdp")
    dig_a, dig_b, dig_c = me // (rest * rest), (me // rest) % rest, me % rest
    dig_three, dig_two = dig_c + core * (dig_b - dig_c), dig_b + core * (dig_c - dig_b)
    step_three, step_two = 1 + core * (rest - 1), rest - core * (rest - 1)
    pos = (dig_three * rest + dig_two) * first + dig_a
    pos_of = ((dig_c * rest + dig_b) * first + dig_a, (dig_b * rest + dig_c) * first + dig_a)
    sibling = {"section": 1 - core}

    def place(half, j):
        a, b, c = j // (rest * rest), (j // rest) % rest, j % rest
        return ((c * rest + b) if half == 0 else (b * rest + c)) * first + a

    def peer_first(t):
        return {"fsdp": me + ((dig_a + t) % first - dig_a) * (rest * rest)}

    def peer_two(t):
        return {"fsdp": me + ((dig_two + t) % rest - dig_two) * step_two}

    def peer_three(t):
        return {"fsdp": me + ((dig_three + t) % rest - dig_three) * step_three}

    def remote(src, dst, s_sem, r_sem, device):
        return pltpu.make_async_remote_copy(
            src_ref=src, dst_ref=dst, send_sem=s_sem, recv_sem=r_sem, device_id=device,
            device_id_type=pl.DeviceIdType.MESH,
        )

    def slab_two(three, two):
        return pl.ds((three * rest + two) * first, first)

    def slab_three(three):
        return pl.ds(three * rest * first, rest * first)

    def fill_repeats():
        for ref in (rep_one, rep_two, rep_four):
            part = ref.shape[0]
            lanes = lax.broadcasted_iota(jnp.int32, ref.shape, 1).astype(F32)
            line = lax.broadcasted_iota(jnp.int32, ref.shape, 0).astype(F32)
            rest_of = lanes - part * jnp.floor((lanes + 0.5) * (1.0 / part))
            ref[...] = jnp.where(jnp.abs(rest_of - line) < 0.5, 1.0, 0.0).astype(LOW)

    def own_lanes(part):
        shape = (n, part * n)
        lanes = lax.broadcasted_iota(jnp.int32, shape, 1)
        begin = lax.broadcasted_iota(jnp.int32, shape, 0) * part
        return (lanes >= begin) & (lanes < begin + part)

    shares = (
        ((G1, unit, rep_one), (S1, unit, rep_one), (BO, unit, rep_one), (G2, unit, rep_one), (S2, unit, rep_one),
         (BD, unit, rep_one), (BQ, 2 * unit, rep_two)),
        ((BU, 4 * unit, rep_four),),
    )

    def table_in(b):
        for half in range(2):
            lines = jnp.concatenate([s_t[b, half, place(half, j)] for j in range(n)], axis=0)
            begin = 0
            for row, part, ref in shares[half]:
                spread = mm(lines[:, begin : begin + part].astype(LOW), ref[...])
                line = colsum(jnp.where(own_lanes(part), spread, 0.0))
                for i in range(part * n // width):
                    table[b, row + i : row + i + 1, :] = line[:, width * i : width * (i + 1)]
                begin += part

    def table_out(b):
        for half in range(2):
            parts, begin = [], 0
            for row, part, ref in shares[half]:
                count = part * n // width
                line = jnp.concatenate([gtable[b, row + i : row + i + 1, :] for i in range(count)], axis=1)
                parts.append(mm_right(jnp.where(own_lanes(part), line, 0.0).astype(LOW), ref[...]))
                begin += part
            parts.append(jnp.zeros((n, width - begin), F32))
            lines = jnp.concatenate(parts, axis=1)
            for j in range(n):
                s_t[b, half, place(half, j)] = lines[j : j + 1]

    def pack_own():
        for half in range(2):
            vectors = ((v_g1, v_s1, v_bo, v_g2, v_s2, v_bd, v_qv), (v_up,))[half]
            lines = [vector[...].astype(F32) for vector in vectors]
            lines.append(jnp.zeros((1, width - sum(line.shape[1] for line in lines)), F32))
            pack_t[half] = jnp.concatenate(lines, axis=1)
            for ref in (pack_a, pack_u):
                both = []
                for part in (2 * half, 2 * half + 1):
                    if ref is pack_u:
                        both.append(a_up[0, :, part * width : (part + 1) * width])
                    elif part == 3:
                        both.append(a_out[0])
                    else:
                        both.append(a_qkv[0, :, part * width : (part + 1) * width])
                ref[half] = jnp.concatenate([value.astype(F32) for value in both], axis=0).astype(LOW)
            pack_d[half] = a_down[0, 2 * unit * half : 2 * unit * (half + 1), :]

    def at(b, g):
        return len(groups) * b + g

    def ag1_copy(b, g, half, t):
        device = {"section": half, **peer_first(t)} if t else sibling
        return remote(
            pack[g].at[half], stage[g].at[b, half, pos_of[half]],
            ag1_s.at[g, half, t], ag1_r.at[at(b, g), t], device,
        )

    def ag1_landing(b, g, t):
        ref = stage[g].at[b, core, (dig_three * rest + dig_two) * first + (dig_a + first - t) % first]
        return remote(ref, ref, ag1_s.at[g, 0, t], ag1_r.at[at(b, g), t], sibling)

    def ag2_copy(b, g, t):
        ref = stage[g].at[b, core, slab_two(dig_three, dig_two)]
        return remote(ref, ref, ag2_s.at[at(b, g), t - 1], ag2_r.at[at(b, g), t - 1], peer_two(t))

    def ag3_copy(b, g, t):
        ref = stage[g].at[b, core, slab_three(dig_three)]
        return remote(ref, ref, ag3_s.at[at(b, g), t - 1], ag3_r.at[at(b, g), t - 1], peer_three(t))

    def ag4_copy(b, g, t):
        ref = stage[g].at[b, core, slab_three((dig_three + rest - t) % rest)]
        return remote(ref, ref, ag4_s.at[at(b, g), t], ag4_r.at[at(b, g), t], sibling)

    def ag4_landing(b, g, t):
        ref = stage[g].at[b, 1 - core, slab_three((dig_two + rest - t) % rest)]
        return remote(ref, ref, ag4_s.at[at(b, g), t], ag4_r.at[at(b, g), t], sibling)

    def ag1(b, g):
        @pl.when(core == b)
        def _():
            for t in range(1, first):
                for half in range(2):
                    ag1_copy(b, g, half, t).start()
            ag1_copy(b, g, 1 - b, 0).start()
            stage[g][b, b, pos] = pack[g][b]

    def ag2(b, g):
        for t in range(1, first):
            ag1_landing(b, g, t).wait_recv()

        @pl.when(core != b)
        def _():
            ag1_landing(b, g, 0).wait_recv()

        for t in range(1, rest):
            ag2_copy(b, g, t).start()

    def ag3(b, g):
        for t in range(1, rest):
            ag2_copy(b, g, t).wait_recv()
        for t in range(1, rest):
            ag3_copy(b, g, t).start()
        ag4_copy(b, g, 0).start()

    def ag4(b, g):
        for t in range(1, rest):
            ag3_copy(b, g, t).wait_recv()
            ag4_copy(b, g, t).start()

    def ag5(b, g):
        for t in range(rest):
            ag4_landing(b, g, t).wait_recv()
        lay_out(b, g)

    def ag_sent(b, g):
        @pl.when(core == b)
        def _():
            for t in range(1, first):
                for half in range(2):
                    ag1_copy(b, g, half, t).wait_send()
            ag1_copy(b, g, 1 - b, 0).wait_send()

        for t in range(1, rest):
            ag2_copy(b, g, t).wait_send()
            ag3_copy(b, g, t).wait_send()
        for t in range(rest):
            ag4_copy(b, g, t).wait_send()

    def lay_out(b, g):
        if g == TAB:
            table_in(b)
            return
        if g == DOWN:
            for j in range(n):
                for half in range(2):
                    begin = 4 * unit * j + 2 * unit * half
                    wdown[b, begin : begin + 2 * unit, :] = s_d[b, half, place(half, j)]
            return
        together = 16 // math.gcd(unit, 16)
        for half in range(2):
            for j in range(0, n, together):
                pieces = [stage[g][b, half, place(half, j + i)].astype(F32) for i in range(together)]
                for sub in range(2):
                    low = sub * unit
                    block = jnp.concatenate([piece[low : low + unit] for piece in pieces], axis=0).astype(LOW)
                    part = 2 * half + sub
                    down = slice(unit * j, unit * (j + together))
                    if g == UP:
                        wup[b, down, part * width : (part + 1) * width] = block
                    elif part == 3:
                        wout[b, down, :] = block
                    else:
                        wqkv[b, down, part * width : (part + 1) * width] = block

    def rs0_copy(b, g):
        return remote(stage[g].at[b, 1 - core], r0[g], rs0_s.at[at(b, g)], rs0_r.at[at(b, g)], sibling)

    def rs1_copy(b, g, t):
        return remote(
            stage[g].at[b, core, slab_three((dig_three + t) % rest)], r1[g].at[t - 1],
            rs1_s.at[at(b, g), t - 1], rs1_r.at[at(b, g), t - 1], peer_three(t),
        )

    def rs2_copy(b, g, t):
        return remote(
            stage[g].at[b, core, slab_two(dig_three, (dig_two + t) % rest)], r2[g].at[b, t - 1],
            rs2_s.at[at(b, g), t - 1], rs2_r.at[at(b, g), t - 1], peer_two(t),
        )

    def rs3_copy(b, g, t):
        there = (dig_three * rest + dig_two) * first + (dig_a + t) % first
        device = {"section": b, **peer_first(t)} if t else sibling
        return remote(
            stage[g].at[b, core, there], r3[g].at[core, t], rs3_s.at[at(b, g), t], rs3_r.at[g, core, t], device
        )

    def rs0(b, g):
        @pl.when(b == 0)
        def _():
            pl.semaphore_wait(credit.at[0, g], 1)

        rs0_copy(b, g).start()

    def rs1(b, g):
        rs0_copy(b, g).wait_recv()

        @pl.loop(0, n)
        def _(p):
            stage[g][b, core, p] = stage[g][b, core, p] + r0[g][p]

        @pl.when(b == 1)
        def _():
            pl.semaphore_signal(credit.at[0, g], inc=1, device_id=sibling, device_id_type=pl.DeviceIdType.MESH)

        if rest > 1:
            @pl.when(b == 0)
            def _():
                pl.semaphore_wait(credit.at[1, g], rest - 1)

        for t in range(1, rest):
            rs1_copy(b, g, t).start()

    def rs2(b, g):
        for t in range(1, rest):
            rs1_copy(b, g, t).wait_recv()

        @pl.loop(0, rest * first)
        def _(p):
            here = dig_three * rest * first + p
            total = stage[g][b, core, here].astype(F32)
            for t in range(1, rest):
                total = total + r1[g][t - 1, p].astype(F32)
            stage[g][b, core, here] = total.astype(stage[g].dtype)

        for t in range(1, rest):
            @pl.when(b == 1)
            def _():
                pl.semaphore_signal(
                    credit.at[1, g], inc=1, device_id=peer_three(t), device_id_type=pl.DeviceIdType.MESH
                )

            rs2_copy(b, g, t).start()

    def rs3(b, g):
        for t in range(1, rest):
            rs2_copy(b, g, t).wait_recv()

        @pl.loop(0, first)
        def _(p):
            here = (dig_three * rest + dig_two) * first + p
            total = stage[g][b, core, here].astype(F32)
            for t in range(1, rest):
                total = total + r2[g][b, t - 1, p].astype(F32)
            stage[g][b, core, here] = total.astype(stage[g].dtype)

        for t in range(1, first):
            rs3_copy(b, g, t).start()

        @pl.when(core != b)
        def _():
            rs3_copy(b, g, 0).start()

    def rs4(b, g):
        @pl.when(core == b)
        def _():
            for own in (True, False):
                half = core if own else 1 - core
                begin = int(own)
                for t in range(begin, first):
                    ref = r3[g].at[half, t]
                    remote(ref, ref, rs3_s.at[at(b, g), t], rs3_r.at[g, half, t], sibling).wait_recv()
                total = stage[g][b, core, pos].astype(F32) if own else None
                for t in range(begin, first):
                    value = r3[g][half, t].astype(F32)
                    total = value if total is None else total + value
                final[g][half] = total

    def rs_sent(b, g):
        rs0_copy(b, g).wait_send()
        for t in range(1, rest):
            rs1_copy(b, g, t).wait_send()
            rs2_copy(b, g, t).wait_send()
        for t in range(1, first):
            rs3_copy(b, g, t).wait_send()

        @pl.when(core != b)
        def _():
            rs3_copy(b, g, 0).wait_send()

    def rows_of(i, images_too=1):
        return pl.ds(pl.multiple_of(i * rows, 16), images_too * rows)

    many = TOGETHER if slots % TOGETHER == 0 else 1
    steps = slots // many

    def step_rows(i):
        return rows_of(i * many, many)

    def ship_parts(kind, b, i):
        src, out = ((io_one, act_out), (io_two, ing_out))[kind]
        q = 2 * kind + b
        near = pltpu.make_async_copy(src.at[i], out.at[core, i], ship_s.at[q, i])
        far = remote(src.at[i], out.at[core, i], ship_s.at[q, i], ship_r.at[q, i], sibling)
        return near, far

    def ship(kind, b, i):
        near, far = ship_parts(kind, b, i)

        @pl.when(core == b)
        def _():
            near.start()

        @pl.when(core != b)
        def _():
            far.start()

    def shipped(kind, b, i):
        near, far = ship_parts(kind, b, i)

        @pl.when(core == b)
        def _():
            near.wait()

        @pl.when(core != b)
        def _():
            far.wait_send()

    def landed(kind, b, i):
        out = (act_out, ing_out)[kind]
        q = 2 * kind + b
        ref = out.at[1 - core, i]

        @pl.when(core == b)
        def _():
            remote(ref, ref, ship_s.at[q, i], ship_r.at[q, i], sibling).wait_recv()

    def live(i):
        return jnp.where(i < counts[0, core], 1.0, 0.0).astype(F32)

    def only_live(i, value):
        parts = [value[rows * m : rows * (m + 1)] * live(i * many + m) for m in range(many)]
        return jnp.concatenate(parts, axis=0)

    def coming(which, i):
        source, target = ((images, io_one), (cotangent, io_two))[which]
        return pltpu.make_async_copy(source.at[core, i], target.at[i], in_s.at[which, i])

    def far_copy(which, i, back):
        near, far = ((hid, hid_far), (slope, slope_far))[which]
        near, far = near.at[rows_of(i)], far.at[rows_of(i)]
        src, dst = (far, near) if back else (near, far)
        return pltpu.make_async_copy(src, dst, far_s.at[2 * int(back) + which, i])

    pairs = width // 128
    scale = head_dim ** -0.5
    lane = lax.broadcasted_iota(jnp.int32, (1, 128), 1)
    half_low = [(lane < head_dim).astype(LOW), (lane >= head_dim).astype(LOW)]
    half_f = [(lane < head_dim).astype(F32), (lane >= head_dim).astype(F32)]
    key_pad = jnp.where(lax.broadcasted_iota(jnp.int32, (1, rows), 1) < length, 0.0, -1e30).astype(F32)
    chunk = 256
    chunks = ff // chunk

    def vec(s, r):
        return table[s, r : r + 1, :]

    def up_bias(s, c):
        begin = c * chunk
        row, col = begin // width, begin % width
        if col + chunk <= width:
            return table[s, BU + row : BU + row + 1, col : col + chunk]
        a = table[s, BU + row : BU + row + 1, col:width]
        b = table[s, BU + row + 1 : BU + row + 2, 0 : chunk - (width - col)]
        return jnp.concatenate([a, b], axis=1)

    def add_vec(s, r, value):
        gtable[s, r : r + 1, :] += value

    def add_up_bias(s, c, value):
        begin = c * chunk
        row, col = begin // width, begin % width
        if col + chunk <= width:
            gtable[s, BU + row : BU + row + 1, col : col + chunk] += value
        else:
            cut = width - col
            gtable[s, BU + row : BU + row + 1, col:width] += value[:, :cut]
            gtable[s, BU + row + 1 : BU + row + 2, 0 : chunk - cut] += value[:, cut:]

    def attn_forward(s, x, hat, i):
        rd = step_rows(i)
        nrm_ref, qkv_ref, prob_ref, ctx_ref = nrm1.at[s], qkv.at[s], prob.at[s], ctx.at[s]
        nrm = (hat * vec(s, G1) + vec(s, S1)).astype(LOW)
        nrm_ref[rd, :] = nrm
        q = (mm(nrm, wqkv[s, :, 0:width]) + vec(s, BQ)).astype(LOW)
        k = mm(nrm, wqkv[s, :, width : 2 * width]).astype(LOW)
        v = (mm(nrm, wqkv[s, :, 2 * width :]) + vec(s, BV)).astype(LOW)
        qkv_ref[rd, 0:width] = q
        qkv_ref[rd, width : 2 * width] = k
        qkv_ref[rd, 2 * width :] = v
        images_out = []
        for m in range(many):
            mine = slice(rows * m, rows * (m + 1))
            parts = []
            for p in range(pairs):
                cols = slice(128 * p, 128 * p + 128)
                total = None
                for j in range(2):
                    scores = mm_right(q[mine, cols], k[mine, cols] * half_low[j]) + key_pad
                    top = jnp.max(scores, axis=-1, keepdims=True)
                    e = jnp.exp2((scores - top) * (scale * 1.4426950408889634))
                    pr = (e * (1.0 / jnp.sum(e, axis=-1, keepdims=True))).astype(LOW)
                    prob_ref[i * many + m, 2 * p + j] = pr
                    part = mm(pr, v[mine, cols] * half_low[j])
                    total = part if total is None else total + part
                parts.append(total.astype(LOW))
            images_out.append(jnp.concatenate(parts, axis=1))
        context = jnp.concatenate(images_out, axis=0)
        ctx_ref[rd, :] = context
        return x + mm(context, wout[s]) + vec(s, BO)

    def ff_forward(s, after, rd):
        nrm_ref = nrm2.at[s]
        hat, rstd, _ = normalize(after)
        hat2[s, rd, :] = hat.astype(LOW)
        nrm = (hat * vec(s, G2) + vec(s, S2)).astype(LOW)
        nrm_ref[rd, :] = nrm
        total = after + vec(s, BD)
        for c in range(chunks):
            cols = slice(chunk * c, chunk * c + chunk)
            pre = mm(nrm, wup[s, :, cols]) + up_bias(s, c)
            phi, slo = normal_parts(pre)
            h = (pre * phi).astype(LOW)
            hid[rd, cols] = h
            slope[rd, cols] = slo.astype(LOW)
            total = total + mm(h, wdown[s, cols, :])
        return total, rstd

    def ff_backward(s, g, rd, rstd):
        g_low = g.astype(LOW)
        add_vec(s, BD, colsum(g_low.astype(F32)))
        d_nrm = None
        for c in range(chunks):
            cols = slice(chunk * c, chunk * c + chunk)
            d_hid = mm_right(g_low, wdown[s, cols, :])
            d_pre = (d_hid * slope[rd, cols].astype(F32)).astype(LOW)
            slope[rd, cols] = d_pre
            add_up_bias(s, c, colsum(d_pre.astype(F32)))
            part = mm_right(d_pre, wup[s, :, cols])
            d_nrm = part if d_nrm is None else d_nrm + part
        hat = hat2[s, rd, :].astype(F32)
        add_vec(s, G2, colsum(d_nrm * hat))
        add_vec(s, S2, colsum(d_nrm))
        d_after = g + normalize_back(d_nrm * vec(s, G2), hat, rstd)
        low = d_after.astype(LOW)
        dal[rd, :] = low
        add_vec(s, BO, colsum(low.astype(F32)))
        return d_after

    def attn_backward(s, i):
        qkv_ref, prob_ref, ctx_ref = qkv.at[s], prob.at[s], ctx.at[s]
        d_context = mm_right(dal[step_rows(i), :], wout[s]).astype(LOW)
        for m in range(many):
            rd = rows_of(i * many + m)
            d_ctx = d_context[rows * m : rows * (m + 1)]
            dq, dk, dv = [], [], []
            for p in range(pairs):
                cols = slice(128 * p, 128 * p + 128)
                q = qkv_ref[rd, 128 * p : 128 * p + 128]
                k = qkv_ref[rd, width + 128 * p : width + 128 * p + 128]
                v = qkv_ref[rd, 2 * width + 128 * p : 2 * width + 128 * p + 128]
                dc = d_ctx[:, cols]
                both = dc.astype(F32) * ctx_ref[rd, cols].astype(F32)
                sums = [None, None, None]
                for j in range(2):
                    pr = prob_ref[i * many + m, 2 * p + j]
                    delta = jnp.sum(both * half_f[j], axis=-1, keepdims=True)
                    d_prob = mm_right(dc, v * half_low[j])
                    ds = (pr.astype(F32) * (d_prob - delta)).astype(LOW)
                    new = [mm(ds, k * half_low[j]), mm_left(ds, q * half_low[j]), mm_left(pr, dc * half_low[j])]
                    sums = [b if a is None else a + b for a, b in zip(sums, new)]
                dq.append((sums[0] * scale).astype(LOW))
                dk.append((sums[1] * scale).astype(LOW))
                dv.append(sums[2].astype(LOW))
            d_mixed = jnp.concatenate(dq + dk + dv, axis=1)
            qkv_ref[rd, :] = d_mixed
            add_vec(s, BQ, colsum(d_mixed[:, 0:width].astype(F32)))
            add_vec(s, BV, colsum(d_mixed[:, 2 * width :].astype(F32)))

    def input_backward(s, d_after, rd, x, mean, rstd):
        d_nrm = mm_right(qkv[s, rd, :], wqkv[s])
        hat = (x - mean) * rstd
        add_vec(s, G1, colsum(d_nrm * hat))
        add_vec(s, S1, colsum(d_nrm))
        return d_after + normalize_back(d_nrm * vec(s, G1), hat, rstd)

    def grads_down(s):
        left_t[...] = low_g[...].T

        @pl.loop(0, 4)
        def _(c):
            cols = pl.ds(pl.multiple_of(c * width, 128), width)
            block = mm(left_t[...], hid[:, cols]).T
            for i in range(n // 4):
                for half in range(2):
                    begin = 4 * unit * i + 2 * unit * half
                    s_d[s, half, place(half, c * (n // 4) + i)] = block[begin : begin + 2 * unit].astype(LOW)

    def pair_out(ref, s, half, one, two):
        for j in range(n):
            down = slice(unit * j, unit * (j + 1))
            piece = jnp.concatenate([one[down], two[down]], axis=0).astype(LOW)
            ref[s, half, place(half, j)] = piece

    def grads_up(s):
        left_t[...] = nrm2[s].T
        for half in range(2):
            one, two = [
                mm(left_t[...], slope[:, part * width : (part + 1) * width]) for part in (2 * half, 2 * half + 1)
            ]
            pair_out(s_u, s, half, one, two)

    def grads_attn(s):
        mix_s = qkv.at[s]
        left_t[...] = ctx[s].T
        four = mm(left_t[...], dal[...])
        left_t[...] = nrm1[s].T
        three = mm(left_t[...], mix_s[:, 2 * width :])
        pair_out(s_a, s, 1, three, four)
        one = mm(left_t[...], mix_s[:, 0:width])
        two = mm(left_t[...], mix_s[:, width : 2 * width])
        pair_out(s_a, s, 0, one, two)

    barrier = pltpu.get_barrier_semaphore()
    greeted = [sibling]
    greeted += [{"section": half, **peer_first(t)} for t in range(1, first) for half in range(2)]
    greeted += [f(t) for f in (peer_two, peer_three) for t in range(1, rest)]
    for device in greeted:
        pl.semaphore_signal(barrier, inc=1, device_id=device, device_id_type=pl.DeviceIdType.MESH)
    pack_own()
    pl.semaphore_wait(barrier, len(greeted))

    def run(*todo):
        for f, b, g in todo:
            f(b, g)

    def events(i, table_of):
        for when, todo in table_of.items():
            @pl.when(i == when // many)
            def _():
                run(*todo)

    def both(f, b, g):
        return [(f, b, g), (f, b, TAB)]

    def take(i, m):
        return pl.ds(pl.multiple_of((i * many + m) * rows, 16), length)

    run(*both(ag1, 0, ATT))
    for which in range(2):
        for i in range(slots):
            coming(which, i).start()
    fill_repeats()
    gtable[...] = jnp.zeros_like(gtable)
    low_g[...] = jnp.zeros_like(low_g)
    xs[0] = jnp.zeros_like(low_g)
    run(*both(ag2, 0, ATT), (ag1, 0, UP), (ag1, 0, DOWN))

    def first_norm(s, rd, x):
        hat, rstd, mean = normalize(x)
        after_ref[rd, :] = hat
        rstds[s, rd, 0:1] = rstd
        rstds[s, rd, 2:3] = mean

    @pl.loop(0, steps)
    def norm_one(i):
        for m in range(many):
            coming(0, i * many + m).wait()
            xs[0, take(i, m), :] = io_one[i * many + m]
        rd = step_rows(i)
        first_norm(0, rd, xs[0, rd, :].astype(F32))

    run(*both(ag3, 0, ATT), (ag2, 0, UP), *both(ag1, 1, ATT), (ag2, 0, DOWN), (ag1, 1, UP), (ag1, 1, DOWN))
    run(*both(ag4, 0, ATT), (ag3, 0, UP), *both(ag5, 0, ATT))

    @pl.loop(0, 2)
    def forward(s):
        @pl.loop(0, steps)
        def attention(i):
            @pl.when(s == 0)
            def _():
                events(i, {
                    0: [(ag3, 0, DOWN), *both(ag2, 1, ATT)],
                    3: [(ag4, 0, UP), (ag2, 1, UP)],
                    5: [(ag4, 0, DOWN)],
                })

            @pl.when(s == 1)
            def _():
                events(i, {5: [(ag4, 1, DOWN)]})

            rd = step_rows(i)
            after_ref[rd, :] = attn_forward(s, xs[s, rd, :].astype(F32), after_ref[rd, :], i)

        @pl.when(s == 0)
        def _():
            run(*both(ag3, 1, ATT), (ag5, 0, UP), (ag5, 0, DOWN))

        @pl.when(s == 1)
        def _():
            run((ag5, 1, UP), (ag5, 1, DOWN))

        @pl.loop(0, steps)
        def feed_forward(i):
            @pl.when(s == 0)
            def _():
                events(i, {0: [(ag3, 1, UP), (ag2, 1, DOWN)], 3: both(ag4, 1, ATT), 5: [(ag4, 1, UP)]})

            rd = step_rows(i)

            @pl.when(s == 1)
            def _():
                for m in range(many):
                    far_copy(0, i * many + m, False).wait()
                    far_copy(1, i * many + m, False).wait()
                    shipped(0, 0, i * many + m)

            out, rstd2 = ff_forward(s, after_ref[rd, :], rd)
            rstds[s, rd, 1:2] = rstd2
            out = only_live(i, out)
            for m in range(many):
                io_one[i * many + m] = out[rows * m : rows * m + length].astype(LOW)
                ship(0, s, i * many + m)

            @pl.when(s == 0)
            def _():
                for m in range(many):
                    far_copy(0, i * many + m, False).start()
                    far_copy(1, i * many + m, False).start()
                low = out.astype(LOW)
                xs[1, rd, :] = low
                first_norm(1, rd, low.astype(F32))

        @pl.when(s == 0)
        def _():
            run((ag3, 1, DOWN), *both(ag5, 1, ATT))

    for b in range(2):
        for g in groups:
            ag_sent(b, g)

    @pl.loop(0, 2)
    def backward(turn):
        s = 1 - turn

        @pl.loop(0, steps)
        def feed_forward(i):
            @pl.when(s == 0)
            def _():
                events(i, {2: [(rs1, 1, TAB)], 4: [(rs4, 1, UP)]})
                for m in range(many):
                    far_copy(1, i * many + m, True).wait()

            @pl.when(s == 1)
            def _():
                for m in range(many):
                    coming(1, i * many + m).wait()

            rd = step_rows(i)
            for m in range(many):
                g = live(i * many + m) * io_two[i * many + m].astype(F32)
                low_g[take(i, m), :] = g.astype(LOW)
            after_ref[rd, :] = ff_backward(s, low_g[rd, :].astype(F32), rd, rstds[s, rd, 1:2])

        @pl.when(s == 0)
        def _():
            for i in range(slots):
                far_copy(0, i, True).wait()
            run(*both(rs2, 1, ATT))

        grads_down(s)
        run((rs0, s, DOWN))

        @pl.when(s == 1)
        def _():
            for i in range(slots):
                far_copy(0, i, True).start()

        grads_up(s)
        run((rs0, s, UP), (rs1, s, DOWN))

        @pl.when(s == 1)
        def _():
            for i in range(slots):
                far_copy(1, i, True).start()

        @pl.when(s == 0)
        def _():
            run(*both(rs3, 1, ATT))

        @pl.loop(0, steps)
        def attention(i):
            events(i, {2: [(rs1, s, UP), (rs2, s, DOWN)], 4: [(rs2, s, UP), (rs3, s, DOWN)]})

            @pl.when(s == 0)
            def _():
                events(i, {2: both(rs4, 1, ATT)})

            attn_backward(s, i)

        grads_attn(s)
        run((rs0, s, ATT), (rs3, s, UP))

        @pl.loop(0, steps)
        def to_input(i):
            events(i, {4: [(rs1, s, ATT), (rs4, s, DOWN)]})
            rd = step_rows(i)
            x = xs[s, rd, :].astype(F32)
            d_in = input_backward(s, after_ref[rd, :], rd, x, rstds[s, rd, 2:3], rstds[s, rd, 0:1])
            for m in range(many):
                @pl.when(s == 0)
                def _():
                    shipped(1, 1, i * many + m)

                io_two[i * many + m] = d_in[rows * m : rows * m + length].astype(LOW)
                ship(1, s, i * many + m)

        table_out(s)
        run((rs0, s, TAB))

    run((rs2, 0, ATT), (rs1, 0, TAB), (rs4, 0, UP), (rs3, 0, ATT), (rs2, 0, TAB), (rs3, 0, TAB))

    @pl.loop(0, slots)
    def all_out(i):
        shipped(0, 1, i)
        shipped(1, 0, i)
        for kind in range(2):
            for b in range(2):
                landed(kind, b, i)

    run(*both(rs4, 0, ATT))
    for b in range(2):
        for g in groups:
            rs_sent(b, g)


def output_kernel(
    f_a, f_u, f_d, f_t, o_g1, o_s1, o_qkv, o_qv, o_out, o_bo, o_g2, o_s2, o_up, o_bu, o_down, o_bd
):
    unit, width = o_out.shape[1:]
    for half in range(2):
        o_down[0, 2 * unit * half : 2 * unit * (half + 1), :] = f_d[half]
        for sub in range(2):
            part = 2 * half + sub
            cols = slice(part * width, (part + 1) * width)
            o_up[0, :, cols] = f_u[half, unit * sub : unit * (sub + 1), :]
            piece = f_a[half, unit * sub : unit * (sub + 1), :]
            if part == 3:
                o_out[0] = piece
            else:
                o_qkv[0, :, cols] = piece
    begin = 0
    for out in (o_g1, o_s1, o_bo, o_g2, o_s2, o_bd, o_qv):
        part = out.shape[1]
        out[...] = f_t[0, :, begin : begin + part]
        begin += part
    o_bu[...] = f_t[1, :, 0 : o_bu.shape[1]]


def local(
    images, cotangent, counts,
    ln1_gain, ln1_bias, w_qkv, b_qv, w_out, b_out, ln2_gain, ln2_bias, w_up, b_up, w_down, b_down,
):
    micro_count, slots, length, width = images.shape
    ff = w_up.shape[2]
    rows = -(-length // 16) * 16
    n = lax.axis_size("fsdp")
    unit = width // n
    first, rest = radices(n)
    total = slots * rows
    head_dim = width // HEADS

    def vm(*shape, kind=LOW):
        return pltpu.VMEM(shape, kind)

    tall = [(2 * unit, LOW)] * 3 + [(1, F32)]
    dma = lambda *shape: pltpu.SemaphoreType.DMA(shape)
    outs = [((2, slots, length, width), LOW), ((2, slots, length, width), LOW)]
    outs += [((2, r, width), F32) for r, _ in tall] + [((total, ff), LOW), ((total, ff), LOW)]
    scratch = [
        vm(2, total, width), vm(slots, length, width), vm(slots, length, width),
        *[vm(2, r, width, kind=kind) for r, kind in tall],
        vm(2, width, 3 * width), vm(2, width, width), vm(2, width, ff), vm(2, ff, width),
        vm(2, TABLE, width, kind=F32), vm(2, TABLE, width, kind=F32),
        vm(unit, width), vm(2 * unit, 2 * width), vm(4 * unit, 4 * width),
        vm(total, width, kind=F32), vm(2, total, width), vm(2, total, 3 * width), vm(2, slots, HEADS, rows, rows),
        vm(2, total, width), vm(2, total, width), vm(2, total, width), vm(2, total, 3, kind=F32),
        vm(total, ff), vm(total, ff), vm(total, width), vm(total, width), vm(width, total),
    ]
    scratch += [vm(2, 2, n, r, width, kind=kind) for r, kind in tall]
    scratch += [vm(n, r, width, kind=kind) for r, kind in tall]
    scratch += [vm(rest - 1, rest * first, r, width, kind=kind) for r, kind in tall]
    scratch += [vm(2, rest - 1, first, r, width, kind=kind) for r, kind in tall]
    scratch += [vm(2, first, r, width, kind=kind) for r, kind in tall]
    scratch += [dma(2, slots), dma(4, slots), dma(4, slots), dma(4, slots)]
    scratch += [dma(4, 2, first), dma(8, first)] + [dma(8, rest - 1)] * 4 + [dma(8, rest)] * 2
    scratch += [dma(8)] * 2 + [dma(8, rest - 1)] * 4 + [dma(8, first), dma(4, 2, first)]
    scratch += [pltpu.SemaphoreType.REGULAR((2, 4))]
    dims = (slots, length, rows, width, ff, head_dim, n)
    vmem = pl.BlockSpec(memory_space=pltpu.VMEM)
    hbm = pl.BlockSpec(memory_space=pltpu.HBM)
    acts, ings, f_a, f_u, f_d, f_t, _, _ = pl.pallas_call(
        functools.partial(whole_kernel, dims),
        out_shape=[jax.ShapeDtypeStruct(*o) for o in outs],
        in_specs=[hbm, hbm, pl.BlockSpec(memory_space=pltpu.SMEM)] + [vmem] * 12,
        out_specs=[hbm, hbm] + [vmem] * 4 + [hbm, hbm],
        scratch_shapes=scratch,
        compiler_params=pltpu.CompilerParams(
            vmem_limit_bytes=(64 << 20) - (96 << 10), collective_id=0, has_side_effects=True
        ),
    )(
        images, cotangent, counts.T, ln1_gain, ln1_bias, b_out, ln2_gain, ln2_bias, b_down, b_qv, b_up,
        w_qkv, w_out, w_up, w_down,
    )

    params = (
        ln1_gain, ln1_bias, w_qkv, b_qv, w_out, b_out, ln2_gain, ln2_bias, w_up, b_up, w_down, b_down
    )
    grads = pl.pallas_call(
        output_kernel,
        out_shape=[jax.ShapeDtypeStruct(p.shape, F32) for p in params],
        in_specs=[vmem] * 4,
        out_specs=[vmem] * len(params),
    )(f_a, f_u, f_d, f_t)

    return (acts[None], ings[None], *grads)


def solution(mesh):
    split = P("section", "fsdp")
    cube = P("section", "fsdp", None)
    image = P(None, "fsdp", None, None)
    result = P("section", None, "fsdp", None, None)
    params = (split, split, cube, split, cube, split, split, split, cube, split, cube, split)
    return jax.shard_map(
        local,
        mesh=mesh,
        in_specs=(image, image, P(None, "fsdp")) + params,
        out_specs=(result, result) + params,
        check_vma=False,
    )
```

```python
import functools
import math

import jax
import jax.numpy as jnp
from jax import lax
from jax.experimental import pallas as pl
from jax.experimental.pallas import tpu as pltpu
from jax.sharding import PartitionSpec as P

HEADS = 6
EPS = 1e-06
F32 = jnp.float32
LOW = jnp.bfloat16

G1, S1, BO, G2, S2, BD, BQ, BV, BU = 0, 1, 2, 3, 4, 5, 6, 7, 8
TABLE = 16
TOGETHER, TOGETHER_ROWS = 2, 3
ATT, UP, DOWN, TAB = 0, 1, 2, 3


def radices(n):
    rest = max(r for r in range(1, n + 1) if r * r * r <= n and n % (r * r) == 0)
    return n // (rest * rest), rest


def mm(left, right):
    return jnp.dot(left, right, preferred_element_type=F32)


def mm_right(left, right):
    return lax.dot_general(left, right, (((1,), (1,)), ((), ())), preferred_element_type=F32)


def mm_left(left, right):
    return lax.dot_general(left, right, (((0,), (0,)), ((), ())), preferred_element_type=F32)


def normal_parts(pre):
    decay = jnp.exp2(pre * pre * (-0.5 * 1.4426950408889634))
    t = 1.0 / (1.0 + (0.3275911 * 0.7071067811865476) * jnp.abs(pre))
    poly = 0.5 * 1.061405429
    for term in (-1.453152027, 1.421413741, -0.284496736, 0.254829592):
        poly = poly * t + 0.5 * term
    tail = poly * t * decay
    phi = jnp.where(pre < 0.0, tail, 1.0 - tail)
    slope = phi + pre * (decay * 0.3989422804014327)
    return phi, slope


def normalize(value):
    mean = jnp.mean(value, axis=-1, keepdims=True)
    center = value - mean
    rstd = lax.rsqrt(jnp.mean(center * center, axis=-1, keepdims=True) + EPS)
    return center * rstd, rstd, mean


def normalize_back(d_hat, hat, rstd):
    mean_one = jnp.mean(d_hat, axis=-1, keepdims=True)
    mean_two = jnp.mean(d_hat * hat, axis=-1, keepdims=True)
    return rstd * (d_hat - mean_one - hat * mean_two)


def colsum(value):
    return jnp.sum(value, axis=0, keepdims=True)


def whole_kernel(dims, *refs):
    slots, length, rows, width, ff, head_dim, n = dims
    (
        images, cotangent, counts, v_g1, v_s1, v_bo, v_g2, v_s2, v_bd, v_qv, v_up, a_qkv, a_out, a_up, a_down,
        act_out, ing_out, f_a, f_u, f_d, f_t, hid_far, slope_far,
        xs, raw, io_one, io_two, pack_a, pack_u, pack_d, pack_t,
        wqkv, wout, wup, wdown, table, gtable, rep_one, rep_two, rep_four,
        after_ref, nrm1, qkv, prob, ctx, hat2, nrm2, rstds, hid, slope, dal, low_g, left_t,
        s_a, s_u, s_d, s_t, r0_a, r0_u, r0_d, r0_t, r1_a, r1_u, r1_d, r1_t, r2_u, r2_d,
        r3_a, r3_u, r3_d, r3_t,
        in_s, ship_s, ship_r, far_s, ag1_s, ag1_r, ag2_s, ag2_r, ag3_s, ag3_r, ag4_s, ag4_r,
        rs0_s, rs0_r, rs1_s, rs1_r, rs2_s, rs2_r, rs3_s, rs3_r, credit,
    ) = refs
    groups = (ATT, UP, DOWN, TAB)
    pack = (pack_a, pack_u, pack_d, pack_t)
    stage = (s_a, s_u, s_d, s_t)
    r0, r1, r2 = (r0_a, r0_u, r0_d, r0_t), (r1_a, r1_u, r1_d, r1_t), (None, r2_u, r2_d, None)
    r3, final = (r3_a, r3_u, r3_d, r3_t), (f_a, f_u, f_d, f_t)

    first, rest = radices(n)
    unit = width // n
    core = lax.axis_index("section")
    me = lax.axis_index("fsdp")
    dig_a, dig_b, dig_c = me // (rest * rest), (me // rest) % rest, me % rest
    dig_three, dig_two = dig_c + core * (dig_b - dig_c), dig_b + core * (dig_c - dig_b)
    step_three, step_two = 1 + core * (rest - 1), rest - core * (rest - 1)
    pos = (dig_three * rest + dig_two) * first + dig_a
    pos_of = ((dig_c * rest + dig_b) * first + dig_a, (dig_b * rest + dig_c) * first + dig_a)
    sibling = {"section": 1 - core}

    def place(half, j):
        a, b, c = j // (rest * rest), (j // rest) % rest, j % rest
        return ((c * rest + b) if half == 0 else (b * rest + c)) * first + a

    def peer_first(t):
        return {"fsdp": me + ((dig_a + t) % first - dig_a) * (rest * rest)}

    def peer_two(t):
        return {"fsdp": me + ((dig_two + t) % rest - dig_two) * step_two}

    def peer_three(t):
        return {"fsdp": me + ((dig_three + t) % rest - dig_three) * step_three}

    def peer_plane(three, two):
        here = ((dig_three + three) % rest - dig_three) * step_three
        return {"fsdp": me + here + ((dig_two + two) % rest - dig_two) * step_two}

    plane = [(three, two) for three in range(rest) for two in range(rest) if three or two]

    def remote(src, dst, s_sem, r_sem, device):
        return pltpu.make_async_remote_copy(
            src_ref=src, dst_ref=dst, send_sem=s_sem, recv_sem=r_sem, device_id=device,
            device_id_type=pl.DeviceIdType.MESH,
        )

    def slab_two(three, two):
        return pl.ds((three * rest + two) * first, first)

    def slab_three(three):
        return pl.ds(three * rest * first, rest * first)

    def fill_repeats():
        for ref in (rep_one, rep_two, rep_four):
            part = ref.shape[0]
            lanes = lax.broadcasted_iota(jnp.int32, ref.shape, 1).astype(F32)
            line = lax.broadcasted_iota(jnp.int32, ref.shape, 0).astype(F32)
            rest_of = lanes - part * jnp.floor((lanes + 0.5) * (1.0 / part))
            ref[...] = jnp.where(jnp.abs(rest_of - line) < 0.5, 1.0, 0.0).astype(LOW)

    def own_lanes(part):
        shape = (n, part * n)
        lanes = lax.broadcasted_iota(jnp.int32, shape, 1)
        begin = lax.broadcasted_iota(jnp.int32, shape, 0) * part
        return (lanes >= begin) & (lanes < begin + part)

    shares = (
        ((G1, unit, rep_one), (S1, unit, rep_one), (BO, unit, rep_one), (G2, unit, rep_one), (S2, unit, rep_one),
         (BD, unit, rep_one), (BQ, 2 * unit, rep_two)),
        ((BU, 4 * unit, rep_four),),
    )

    def table_in(b):
        for half in range(2):
            lines = jnp.concatenate([s_t[b, half, place(half, j)] for j in range(n)], axis=0)
            begin = 0
            for row, part, ref in shares[half]:
                spread = mm(lines[:, begin : begin + part].astype(LOW), ref[...])
                line = colsum(jnp.where(own_lanes(part), spread, 0.0))
                for i in range(part * n // width):
                    table[b, row + i : row + i + 1, :] = line[:, width * i : width * (i + 1)]
                begin += part

    def table_out(b):
        for half in range(2):
            parts, begin = [], 0
            for row, part, ref in shares[half]:
                count = part * n // width
                line = jnp.concatenate([gtable[b, row + i : row + i + 1, :] for i in range(count)], axis=1)
                parts.append(mm_right(jnp.where(own_lanes(part), line, 0.0).astype(LOW), ref[...]))
                begin += part
            parts.append(jnp.zeros((n, width - begin), F32))
            lines = jnp.concatenate(parts, axis=1)
            for j in range(n):
                s_t[b, half, place(half, j)] = lines[j : j + 1]

    def pack_own():
        for half in range(2):
            vectors = ((v_g1, v_s1, v_bo, v_g2, v_s2, v_bd, v_qv), (v_up,))[half]
            lines = [vector[...].astype(F32) for vector in vectors]
            lines.append(jnp.zeros((1, width - sum(line.shape[1] for line in lines)), F32))
            pack_t[half] = jnp.concatenate(lines, axis=1)
            for ref in (pack_a, pack_u):
                both = []
                for part in (2 * half, 2 * half + 1):
                    if ref is pack_u:
                        both.append(a_up[0, :, part * width : (part + 1) * width])
                    elif part == 3:
                        both.append(a_out[0])
                    else:
                        both.append(a_qkv[0, :, part * width : (part + 1) * width])
                ref[half] = jnp.concatenate([value.astype(F32) for value in both], axis=0).astype(LOW)
            pack_d[half] = a_down[0, 2 * unit * half : 2 * unit * (half + 1), :]

    def at(b, g):
        return len(groups) * b + g

    def ag1_copy(b, g, half, t):
        device = {"section": half, **peer_first(t)} if t else sibling
        return remote(
            pack[g].at[half], stage[g].at[b, half, pos_of[half]],
            ag1_s.at[g, half, t], ag1_r.at[at(b, g), t], device,
        )

    def ag1_landing(b, g, t):
        ref = stage[g].at[b, core, (dig_three * rest + dig_two) * first + (dig_a + first - t) % first]
        return remote(ref, ref, ag1_s.at[g, 0, t], ag1_r.at[at(b, g), t], sibling)

    def ag2_copy(b, g, t):
        ref = stage[g].at[b, core, slab_two(dig_three, dig_two)]
        return remote(ref, ref, ag2_s.at[at(b, g), t - 1], ag2_r.at[at(b, g), t - 1], peer_two(t))

    def ag3_copy(b, g, t):
        ref = stage[g].at[b, core, slab_three(dig_three)]
        return remote(ref, ref, ag3_s.at[at(b, g), t - 1], ag3_r.at[at(b, g), t - 1], peer_three(t))

    def ag4_copy(b, g, t):
        ref = stage[g].at[b, core, slab_three((dig_three + rest - t) % rest)]
        return remote(ref, ref, ag4_s.at[at(b, g), t], ag4_r.at[at(b, g), t], sibling)

    def ag4_landing(b, g, t):
        ref = stage[g].at[b, 1 - core, slab_three((dig_two + rest - t) % rest)]
        return remote(ref, ref, ag4_s.at[at(b, g), t], ag4_r.at[at(b, g), t], sibling)

    def ag1(b, g):
        @pl.when(core == b)
        def _():
            for t in range(1, first):
                for half in range(2):
                    ag1_copy(b, g, half, t).start()
            ag1_copy(b, g, 1 - b, 0).start()
            stage[g][b, b, pos] = pack[g][b]

    def ag2(b, g):
        for t in range(1, first):
            ag1_landing(b, g, t).wait_recv()

        @pl.when(core != b)
        def _():
            ag1_landing(b, g, 0).wait_recv()

        for t in range(1, rest):
            ag2_copy(b, g, t).start()

    def ag3(b, g):
        for t in range(1, rest):
            ag2_copy(b, g, t).wait_recv()
        for t in range(1, rest):
            ag3_copy(b, g, t).start()
        ag4_copy(b, g, 0).start()

    def ag4(b, g):
        for t in range(1, rest):
            ag3_copy(b, g, t).wait_recv()
            ag4_copy(b, g, t).start()

    def ag5(b, g):
        for t in range(rest):
            ag4_landing(b, g, t).wait_recv()
        lay_out(b, g)

    def ag_sent(b, g):
        @pl.when(core == b)
        def _():
            for t in range(1, first):
                for half in range(2):
                    ag1_copy(b, g, half, t).wait_send()
            ag1_copy(b, g, 1 - b, 0).wait_send()

        for t in range(1, rest):
            ag2_copy(b, g, t).wait_send()
            ag3_copy(b, g, t).wait_send()
        for t in range(rest):
            ag4_copy(b, g, t).wait_send()

    def lay_out(b, g):
        if g == TAB:
            table_in(b)
            return
        if g == DOWN:
            for j in range(n):
                for half in range(2):
                    begin = 4 * unit * j + 2 * unit * half
                    wdown[b, begin : begin + 2 * unit, :] = s_d[b, half, place(half, j)]
            return
        together = 16 // math.gcd(unit, 16)
        for half in range(2):
            for j in range(0, n, together):
                pieces = [stage[g][b, half, place(half, j + i)].astype(F32) for i in range(together)]
                for sub in range(2):
                    low = sub * unit
                    block = jnp.concatenate([piece[low : low + unit] for piece in pieces], axis=0).astype(LOW)
                    part = 2 * half + sub
                    down = slice(unit * j, unit * (j + together))
                    if g == UP:
                        wup[b, down, part * width : (part + 1) * width] = block
                    elif part == 3:
                        wout[b, down, :] = block
                    else:
                        wqkv[b, down, part * width : (part + 1) * width] = block

    def rs0_copy(b, g):
        return remote(stage[g].at[b, 1 - core], r0[g], rs0_s.at[at(b, g)], rs0_r.at[at(b, g)], sibling)

    def rs1_copy(b, g, t):
        return remote(
            stage[g].at[b, core, slab_three((dig_three + t) % rest)], r1[g].at[t - 1],
            rs1_s.at[at(b, g), t - 1], rs1_r.at[at(b, g), t - 1], peer_three(t),
        )

    def rs2_copy(b, g, t):
        return remote(
            stage[g].at[b, core, slab_two(dig_three, (dig_two + t) % rest)], r2[g].at[b, t - 1],
            rs2_s.at[at(b, g), t - 1], rs2_r.at[at(b, g), t - 1], peer_two(t),
        )

    def rs3_copy(b, g, t):
        there = (dig_three * rest + dig_two) * first + (dig_a + t) % first
        device = {"section": b, **peer_first(t)} if t else sibling
        return remote(
            stage[g].at[b, core, there], r3[g].at[core, t], rs3_s.at[at(b, g), t], rs3_r.at[g, core, t], device
        )

    def plane_copy(b, g, t):
        three, two = plane[t]
        return remote(
            stage[g].at[b, core, slab_two((dig_three + three) % rest, (dig_two + two) % rest)], r1[g].at[t],
            rs1_s.at[at(b, g), t], rs1_r.at[at(b, g), t], peer_plane(three, two),
        )

    def rs0(b, g):
        @pl.when(b == 0)
        def _():
            pl.semaphore_wait(credit.at[0, g], 1)

        rs0_copy(b, g).start()

    def rs1(b, g):
        rs0_copy(b, g).wait_recv()

        @pl.loop(0, n)
        def _(p):
            stage[g][b, core, p] = stage[g][b, core, p] + r0[g][p]

        @pl.when(b == 1)
        def _():
            pl.semaphore_signal(credit.at[0, g], inc=1, device_id=sibling, device_id_type=pl.DeviceIdType.MESH)

        direct = g in (ATT, TAB)
        if rest > 1:
            @pl.when(b == 0)
            def _():
                pl.semaphore_wait(credit.at[1, g], len(plane) if direct else rest - 1)

        if direct:
            for t in range(len(plane)):
                plane_copy(b, g, t).start()
            return
        for t in range(1, rest):
            rs1_copy(b, g, t).start()

    def rs2(b, g):
        for t in range(1, rest):
            rs1_copy(b, g, t).wait_recv()

        @pl.loop(0, rest * first)
        def _(p):
            here = dig_three * rest * first + p
            total = stage[g][b, core, here].astype(F32)
            for t in range(1, rest):
                total = total + r1[g][t - 1, p].astype(F32)
            stage[g][b, core, here] = total.astype(stage[g].dtype)

        for t in range(1, rest):
            @pl.when(b == 1)
            def _():
                pl.semaphore_signal(
                    credit.at[1, g], inc=1, device_id=peer_three(t), device_id_type=pl.DeviceIdType.MESH
                )

            rs2_copy(b, g, t).start()

    def rs3(b, g):
        direct = g in (ATT, TAB)
        copies = [plane_copy(b, g, t) for t in range(len(plane))] if direct else [
            rs2_copy(b, g, t) for t in range(1, rest)
        ]
        landing = r1[g] if direct else r2[g].at[b]
        for copy in copies:
            copy.wait_recv()

        @pl.loop(0, first)
        def _(p):
            here = (dig_three * rest + dig_two) * first + p
            total = stage[g][b, core, here].astype(F32)
            for t in range(len(copies)):
                total = total + landing[t, p].astype(F32)
            stage[g][b, core, here] = total.astype(stage[g].dtype)

        if direct:
            @pl.when(b == 1)
            def _():
                for three, two in plane:
                    pl.semaphore_signal(
                        credit.at[1, g], inc=1, device_id=peer_plane(three, two),
                        device_id_type=pl.DeviceIdType.MESH,
                    )


        for t in range(1, first):
            rs3_copy(b, g, t).start()

        @pl.when(core != b)
        def _():
            rs3_copy(b, g, 0).start()

    def rs4(b, g):
        @pl.when(core == b)
        def _():
            for own in (True, False):
                half = core if own else 1 - core
                begin = int(own)
                for t in range(begin, first):
                    ref = r3[g].at[half, t]
                    remote(ref, ref, rs3_s.at[at(b, g), t], rs3_r.at[g, half, t], sibling).wait_recv()
                total = stage[g][b, core, pos].astype(F32) if own else None
                for t in range(begin, first):
                    value = r3[g][half, t].astype(F32)
                    total = value if total is None else total + value
                final[g][half] = total

    def rs_sent(b, g):
        rs0_copy(b, g).wait_send()
        if g in (ATT, TAB):
            for t in range(len(plane)):
                plane_copy(b, g, t).wait_send()
        else:
            for t in range(1, rest):
                rs1_copy(b, g, t).wait_send()
                rs2_copy(b, g, t).wait_send()
        for t in range(1, first):
            rs3_copy(b, g, t).wait_send()

        @pl.when(core != b)
        def _():
            rs3_copy(b, g, 0).wait_send()

    def rows_of(i, images_too=1):
        return pl.ds(pl.multiple_of(i * rows, 16), images_too * rows)

    few = TOGETHER if slots % TOGETHER == 0 else 1
    many = TOGETHER_ROWS if slots % TOGETHER_ROWS == 0 else 1

    def step_rows(i, count):
        return rows_of(i * count, count)

    def ship_parts(kind, b, i):
        src, out = ((io_one, act_out), (io_two, ing_out))[kind]
        q = 2 * kind + b
        near = pltpu.make_async_copy(src.at[i], out.at[core, i], ship_s.at[q, i])
        far = remote(src.at[i], out.at[core, i], ship_s.at[q, i], ship_r.at[q, i], sibling)
        return near, far

    def ship(kind, b, i):
        near, far = ship_parts(kind, b, i)

        @pl.when(core == b)
        def _():
            near.start()

        @pl.when(core != b)
        def _():
            far.start()

    def shipped(kind, b, i):
        near, far = ship_parts(kind, b, i)

        @pl.when(core == b)
        def _():
            near.wait()

        @pl.when(core != b)
        def _():
            far.wait_send()

    def landed(kind, b, i):
        out = (act_out, ing_out)[kind]
        q = 2 * kind + b
        ref = out.at[1 - core, i]

        @pl.when(core == b)
        def _():
            remote(ref, ref, ship_s.at[q, i], ship_r.at[q, i], sibling).wait_recv()

    def live(i):
        return jnp.where(i < counts[0, core], 1.0, 0.0).astype(F32)

    def only_live(i, value, count):
        parts = [value[rows * m : rows * (m + 1)] * live(i * count + m) for m in range(count)]
        return jnp.concatenate(parts, axis=0)

    def coming(which, i):
        slot = (which * slots + i) % raw.shape[0]
        return pltpu.make_async_copy((images, cotangent)[which].at[i], raw.at[slot], in_s.at[which, i])

    def take_in(which, i):
        coming(which, i).wait()
        both = raw[(which * slots + i) % raw.shape[0]].astype(F32)
        (io_one, io_two)[which][i] = jnp.where(core == 0, both[:, 0, :], both[:, 1, :]).astype(LOW)

    def far_copy(which, i, back):
        near, far = ((hid, hid_far), (slope, slope_far))[which]
        near, far = near.at[rows_of(i)], far.at[rows_of(i)]
        src, dst = (far, near) if back else (near, far)
        return pltpu.make_async_copy(src, dst, far_s.at[2 * int(back) + which, i])

    pairs = width // 128
    scale = head_dim ** -0.5
    lane = lax.broadcasted_iota(jnp.int32, (1, 128), 1)
    half_low = [(lane < head_dim).astype(LOW), (lane >= head_dim).astype(LOW)]
    half_f = [(lane < head_dim).astype(F32), (lane >= head_dim).astype(F32)]
    key_pad = jnp.where(lax.broadcasted_iota(jnp.int32, (1, rows), 1) < length, 0.0, -1e30).astype(F32)
    chunk = 256
    chunks = ff // chunk

    def vec(s, r):
        return table[s, r : r + 1, :]

    def up_bias(s, c):
        begin = c * chunk
        row, col = begin // width, begin % width
        if col + chunk <= width:
            return table[s, BU + row : BU + row + 1, col : col + chunk]
        a = table[s, BU + row : BU + row + 1, col:width]
        b = table[s, BU + row + 1 : BU + row + 2, 0 : chunk - (width - col)]
        return jnp.concatenate([a, b], axis=1)

    def add_vec(s, r, value):
        gtable[s, r : r + 1, :] += value

    def add_up_bias(s, c, value):
        begin = c * chunk
        row, col = begin // width, begin % width
        if col + chunk <= width:
            gtable[s, BU + row : BU + row + 1, col : col + chunk] += value
        else:
            cut = width - col
            gtable[s, BU + row : BU + row + 1, col:width] += value[:, :cut]
            gtable[s, BU + row + 1 : BU + row + 2, 0 : chunk - cut] += value[:, cut:]

    def attn_forward(s, x, hat, i):
        rd = step_rows(i, few)
        nrm_ref, qkv_ref, prob_ref, ctx_ref = nrm1.at[s], qkv.at[s], prob.at[s], ctx.at[s]
        nrm = (hat * vec(s, G1) + vec(s, S1)).astype(LOW)
        nrm_ref[rd, :] = nrm
        mixed = mm(nrm, wqkv[s])
        q = (mixed[:, 0:width] + vec(s, BQ)).astype(LOW)
        k = mixed[:, width : 2 * width].astype(LOW)
        v = (mixed[:, 2 * width :] + vec(s, BV)).astype(LOW)
        qkv_ref[rd, 0:width] = q
        qkv_ref[rd, width : 2 * width] = k
        qkv_ref[rd, 2 * width :] = v
        images_out = []
        for m in range(few):
            mine = slice(rows * m, rows * (m + 1))
            parts = []
            for p in range(pairs):
                cols = slice(128 * p, 128 * p + 128)
                total = None
                for j in range(2):
                    scores = mm_right(q[mine, cols], k[mine, cols] * half_low[j]) + key_pad
                    top = jnp.max(scores, axis=-1, keepdims=True)
                    e = jnp.exp2((scores - top) * (scale * 1.4426950408889634))
                    pr = (e * (1.0 / jnp.sum(e, axis=-1, keepdims=True))).astype(LOW)
                    prob_ref[i * few + m, 2 * p + j] = pr
                    part = mm(pr, v[mine, cols] * half_low[j])
                    total = part if total is None else total + part
                parts.append(total.astype(LOW))
            images_out.append(jnp.concatenate(parts, axis=1))
        context = jnp.concatenate(images_out, axis=0)
        ctx_ref[rd, :] = context
        return x + mm(context, wout[s]) + vec(s, BO)

    def ff_forward(s, after, rd):
        nrm_ref = nrm2.at[s]
        hat, rstd, _ = normalize(after)
        hat2[s, rd, :] = hat.astype(LOW)
        nrm = (hat * vec(s, G2) + vec(s, S2)).astype(LOW)
        nrm_ref[rd, :] = nrm
        total = after + vec(s, BD)
        for c in range(chunks):
            cols = slice(chunk * c, chunk * c + chunk)
            pre = mm(nrm, wup[s, :, cols]) + up_bias(s, c)
            phi, slo = normal_parts(pre)
            h = (pre * phi).astype(LOW)
            hid[rd, cols] = h
            slope[rd, cols] = slo.astype(LOW)
            total = total + mm(h, wdown[s, cols, :])
        return total, rstd

    def ff_backward(s, g, rd, rstd):
        g_low = g.astype(LOW)
        add_vec(s, BD, colsum(g_low.astype(F32)))
        d_nrm = None
        for c in range(chunks):
            cols = slice(chunk * c, chunk * c + chunk)
            d_hid = mm_right(g_low, wdown[s, cols, :])
            d_pre = (d_hid * slope[rd, cols].astype(F32)).astype(LOW)
            slope[rd, cols] = d_pre
            add_up_bias(s, c, colsum(d_pre.astype(F32)))
            part = mm_right(d_pre, wup[s, :, cols])
            d_nrm = part if d_nrm is None else d_nrm + part
        hat = hat2[s, rd, :].astype(F32)
        add_vec(s, G2, colsum(d_nrm * hat))
        add_vec(s, S2, colsum(d_nrm))
        d_after = g + normalize_back(d_nrm * vec(s, G2), hat, rstd)
        low = d_after.astype(LOW)
        dal[rd, :] = low
        add_vec(s, BO, colsum(low.astype(F32)))
        return d_after

    def attn_backward(s, i):
        qkv_ref, prob_ref, ctx_ref = qkv.at[s], prob.at[s], ctx.at[s]
        d_context = mm_right(dal[step_rows(i, few), :], wout[s]).astype(LOW)
        for m in range(few):
            rd = rows_of(i * few + m)
            d_ctx = d_context[rows * m : rows * (m + 1)]
            dq, dk, dv = [], [], []
            for p in range(pairs):
                cols = slice(128 * p, 128 * p + 128)
                q = qkv_ref[rd, 128 * p : 128 * p + 128]
                k = qkv_ref[rd, width + 128 * p : width + 128 * p + 128]
                v = qkv_ref[rd, 2 * width + 128 * p : 2 * width + 128 * p + 128]
                dc = d_ctx[:, cols]
                both = dc.astype(F32) * ctx_ref[rd, cols].astype(F32)
                sums = [None, None, None]
                for j in range(2):
                    pr = prob_ref[i * few + m, 2 * p + j]
                    delta = jnp.sum(both * half_f[j], axis=-1, keepdims=True)
                    d_prob = mm_right(dc, v * half_low[j])
                    ds = (pr.astype(F32) * (d_prob - delta)).astype(LOW)
                    new = [mm(ds, k * half_low[j]), mm_left(ds, q * half_low[j]), mm_left(pr, dc * half_low[j])]
                    sums = [b if a is None else a + b for a, b in zip(sums, new)]
                dq.append((sums[0] * scale).astype(LOW))
                dk.append((sums[1] * scale).astype(LOW))
                dv.append(sums[2].astype(LOW))
            d_mixed = jnp.concatenate(dq + dk + dv, axis=1)
            qkv_ref[rd, :] = d_mixed
            add_vec(s, BQ, colsum(d_mixed[:, 0:width].astype(F32)))
            add_vec(s, BV, colsum(d_mixed[:, 2 * width :].astype(F32)))

    def input_backward(s, d_after, rd, x, mean, rstd):
        d_nrm = mm_right(qkv[s, rd, :], wqkv[s])
        hat = (x - mean) * rstd
        add_vec(s, G1, colsum(d_nrm * hat))
        add_vec(s, S1, colsum(d_nrm))
        return d_after + normalize_back(d_nrm * vec(s, G1), hat, rstd)

    def grads_down(s):
        left_t[...] = low_g[...].T

        @pl.loop(0, 4)
        def _(c):
            cols = pl.ds(pl.multiple_of(c * width, 128), width)
            block = mm(left_t[...], hid[:, cols]).T
            for i in range(n // 4):
                for half in range(2):
                    begin = 4 * unit * i + 2 * unit * half
                    s_d[s, half, place(half, c * (n // 4) + i)] = block[begin : begin + 2 * unit].astype(LOW)

    def pair_out(ref, s, half, one, two):
        for j in range(n):
            down = slice(unit * j, unit * (j + 1))
            piece = jnp.concatenate([one[down], two[down]], axis=0).astype(LOW)
            ref[s, half, place(half, j)] = piece

    def grads_up(s):
        left_t[...] = nrm2[s].T
        for half in range(2):
            one, two = [
                mm(left_t[...], slope[:, part * width : (part + 1) * width]) for part in (2 * half, 2 * half + 1)
            ]
            pair_out(s_u, s, half, one, two)

    def grads_attn(s):
        mix_s = qkv.at[s]
        left_t[...] = ctx[s].T
        four = mm(left_t[...], dal[...])
        left_t[...] = nrm1[s].T
        three = mm(left_t[...], mix_s[:, 2 * width :])
        pair_out(s_a, s, 1, three, four)
        one = mm(left_t[...], mix_s[:, 0:width])
        two = mm(left_t[...], mix_s[:, width : 2 * width])
        pair_out(s_a, s, 0, one, two)

    barrier = pltpu.get_barrier_semaphore()
    greeted = [sibling]
    greeted += [{"section": half, **peer_first(t)} for t in range(1, first) for half in range(2)]
    greeted += [peer_plane(three, two) for three, two in plane]
    for device in greeted:
        pl.semaphore_signal(barrier, inc=1, device_id=device, device_id_type=pl.DeviceIdType.MESH)
    pack_own()
    pl.semaphore_wait(barrier, len(greeted))

    def run(*todo):
        for f, b, g in todo:
            f(b, g)

    def events(i, table_of):
        for when, todo in table_of.items():
            @pl.when(i == when)
            def _():
                run(*todo)

    def both(f, b, g):
        return [(f, b, g), (f, b, TAB)]

    def take(i, m):
        return pl.ds(pl.multiple_of((i * many + m) * rows, 16), length)

    ahead = raw.shape[0]
    run(*both(ag1, 0, ATT))
    for i in range(ahead):
        coming(0, i).start()
    fill_repeats()
    gtable[...] = jnp.zeros_like(gtable)
    low_g[...] = jnp.zeros_like(low_g)
    xs[0] = jnp.zeros_like(low_g)

    @pl.loop(0, slots)
    def images_in(i):
        take_in(0, i)

        @pl.when(i + ahead < slots)
        def _():
            coming(0, i + ahead).start()

        @pl.when(i + ahead >= slots)
        def _():
            coming(1, i + ahead - slots).start()

        @pl.when(i == 3)
        def _():
            run(*both(ag2, 0, ATT), (ag1, 0, UP), (ag1, 0, DOWN))

    def first_norm(s, rd, x):
        hat, rstd, mean = normalize(x)
        after_ref[rd, :] = hat
        rstds[s, rd, 0:1] = rstd
        rstds[s, rd, 2:3] = mean

    @pl.loop(0, slots // many)
    def norm_one(i):
        for m in range(many):
            xs[0, take(i, m), :] = io_one[i * many + m]
        rd = step_rows(i, many)
        first_norm(0, rd, xs[0, rd, :].astype(F32))

    run(*both(ag3, 0, ATT), (ag2, 0, UP), *both(ag1, 1, ATT), (ag2, 0, DOWN), (ag1, 1, UP), (ag1, 1, DOWN))

    @pl.loop(0, slots)
    def cotangents_in(i):
        take_in(1, i)

        @pl.when(i + ahead < slots)
        def _():
            coming(1, i + ahead).start()

    run(*both(ag4, 0, ATT), (ag3, 0, UP), *both(ag5, 0, ATT))

    @pl.loop(0, 2)
    def forward(s):
        @pl.loop(0, slots // few)
        def attention(i):
            @pl.when(s == 0)
            def _():
                events(i, {
                    0: [(ag3, 0, DOWN), *both(ag2, 1, ATT)],
                    1: [(ag4, 0, UP), (ag2, 1, UP)],
                    2: [(ag4, 0, DOWN)],
                })

            @pl.when(s == 1)
            def _():
                events(i, {2: [(ag4, 1, DOWN)]})

            rd = step_rows(i, few)
            after_ref[rd, :] = attn_forward(s, xs[s, rd, :].astype(F32), after_ref[rd, :], i)

        @pl.when(s == 0)
        def _():
            run(*both(ag3, 1, ATT), (ag5, 0, UP), (ag5, 0, DOWN))

        @pl.when(s == 1)
        def _():
            run((ag5, 1, UP), (ag5, 1, DOWN))

        @pl.loop(0, slots // many)
        def feed_forward(i):
            @pl.when(s == 0)
            def _():
                events(i, {0: [(ag3, 1, UP), (ag2, 1, DOWN)], 1: both(ag4, 1, ATT)})

            rd = step_rows(i, many)

            @pl.when(s == 1)
            def _():
                for m in range(many):
                    far_copy(0, i * many + m, False).wait()
                    far_copy(1, i * many + m, False).wait()
                    shipped(0, 0, i * many + m)

            out, rstd2 = ff_forward(s, after_ref[rd, :], rd)
            rstds[s, rd, 1:2] = rstd2
            out = only_live(i, out, many)
            for m in range(many):
                io_one[i * many + m] = out[rows * m : rows * m + length].astype(LOW)
                ship(0, s, i * many + m)

            @pl.when(s == 0)
            def _():
                for m in range(many):
                    far_copy(0, i * many + m, False).start()
                    far_copy(1, i * many + m, False).start()
                low = out.astype(LOW)
                xs[1, rd, :] = low
                first_norm(1, rd, low.astype(F32))

        @pl.when(s == 0)
        def _():
            run((ag4, 1, UP), (ag3, 1, DOWN), *both(ag5, 1, ATT))

    for b in range(2):
        for g in groups:
            ag_sent(b, g)

    @pl.loop(0, 2)
    def backward(turn):
        s = 1 - turn

        @pl.loop(0, slots // many)
        def feed_forward(i):
            @pl.when(s == 0)
            def _():
                events(i, {1: [(rs1, 1, TAB), (rs4, 1, UP)]})
                for m in range(many):
                    far_copy(1, i * many + m, True).wait()

            rd = step_rows(i, many)
            for m in range(many):
                g = live(i * many + m) * io_two[i * many + m].astype(F32)
                low_g[take(i, m), :] = g.astype(LOW)
            after_ref[rd, :] = ff_backward(s, low_g[rd, :].astype(F32), rd, rstds[s, rd, 1:2])

        @pl.when(s == 0)
        def _():
            for i in range(slots):
                far_copy(0, i, True).wait()
            run((rs3, 1, ATT))

        grads_down(s)
        run((rs0, s, DOWN))

        @pl.when(s == 1)
        def _():
            for i in range(slots):
                far_copy(0, i, True).start()

        grads_up(s)
        run((rs0, s, UP), (rs1, s, DOWN))

        @pl.when(s == 1)
        def _():
            for i in range(slots):
                far_copy(1, i, True).start()

        @pl.when(s == 0)
        def _():
            run((rs3, 1, TAB))

        @pl.loop(0, slots // few)
        def attention(i):
            events(i, {1: [(rs1, s, UP), (rs2, s, DOWN)], 2: [(rs2, s, UP), (rs3, s, DOWN)]})

            @pl.when(s == 0)
            def _():
                events(i, {1: both(rs4, 1, ATT)})

            attn_backward(s, i)

        grads_attn(s)
        run((rs0, s, ATT), (rs3, s, UP))

        @pl.loop(0, slots // many)
        def to_input(i):
            events(i, {1: [(rs1, s, ATT), (rs4, s, DOWN)]})
            rd = step_rows(i, many)
            x = xs[s, rd, :].astype(F32)
            d_in = input_backward(s, after_ref[rd, :], rd, x, rstds[s, rd, 2:3], rstds[s, rd, 0:1])
            for m in range(many):
                @pl.when(s == 0)
                def _():
                    shipped(1, 1, i * many + m)

                io_two[i * many + m] = d_in[rows * m : rows * m + length].astype(LOW)
                ship(1, s, i * many + m)

        table_out(s)
        run((rs0, s, TAB))

    run((rs4, 0, UP), (rs1, 0, TAB), (rs3, 0, ATT), (rs3, 0, TAB))

    @pl.loop(0, slots)
    def all_out(i):
        shipped(0, 1, i)
        shipped(1, 0, i)
        for kind in range(2):
            for b in range(2):
                landed(kind, b, i)

    run(*both(rs4, 0, ATT))
    for b in range(2):
        for g in groups:
            rs_sent(b, g)


def output_kernel(
    f_a, f_u, f_d, f_t, o_g1, o_s1, o_qkv, o_qv, o_out, o_bo, o_g2, o_s2, o_up, o_bu, o_down, o_bd
):
    unit, width = o_out.shape[1:]
    for half in range(2):
        o_down[0, 2 * unit * half : 2 * unit * (half + 1), :] = f_d[half]
        for sub in range(2):
            part = 2 * half + sub
            cols = slice(part * width, (part + 1) * width)
            o_up[0, :, cols] = f_u[half, unit * sub : unit * (sub + 1), :]
            piece = f_a[half, unit * sub : unit * (sub + 1), :]
            if part == 3:
                o_out[0] = piece
            else:
                o_qkv[0, :, cols] = piece
    begin = 0
    for out in (o_g1, o_s1, o_bo, o_g2, o_s2, o_bd, o_qv):
        part = out.shape[1]
        out[...] = f_t[0, :, begin : begin + part]
        begin += part
    o_bu[...] = f_t[1, :, 0 : o_bu.shape[1]]


def local(
    images, cotangent, counts,
    ln1_gain, ln1_bias, w_qkv, b_qv, w_out, b_out, ln2_gain, ln2_bias, w_up, b_up, w_down, b_down,
):
    micro_count, slots, length, width = images.shape
    ff = w_up.shape[2]
    rows = -(-length // 16) * 16
    n = lax.axis_size("fsdp")
    unit = width // n
    first, rest = radices(n)
    total = slots * rows
    head_dim = width // HEADS

    def vm(*shape, kind=LOW):
        return pltpu.VMEM(shape, kind)

    tall = [(2 * unit, LOW)] * 3 + [(1, F32)]
    dma = lambda *shape: pltpu.SemaphoreType.DMA(shape)
    outs = [((2, slots, length, width), LOW), ((2, slots, length, width), LOW)]
    outs += [((2, r, width), F32) for r, _ in tall] + [((total, ff), LOW), ((total, ff), LOW)]
    scratch = [
        vm(2, total, width), vm(3, length, 2, width), vm(slots, length, width), vm(slots, length, width),
        *[vm(2, r, width, kind=kind) for r, kind in tall],
        vm(2, width, 3 * width), vm(2, width, width), vm(2, width, ff), vm(2, ff, width),
        vm(2, TABLE, width, kind=F32), vm(2, TABLE, width, kind=F32),
        vm(unit, width), vm(2 * unit, 2 * width), vm(4 * unit, 4 * width),
        vm(total, width, kind=F32), vm(2, total, width), vm(2, total, 3 * width), vm(2, slots, HEADS, rows, rows),
        vm(2, total, width), vm(2, total, width), vm(2, total, width), vm(2, total, 3, kind=F32),
        vm(total, ff), vm(total, ff), vm(total, width), vm(total, width), vm(width, total),
    ]
    scratch += [vm(2, 2, n, r, width, kind=kind) for r, kind in tall]
    scratch += [vm(n, r, width, kind=kind) for r, kind in tall]
    plane = rest * rest - 1
    for g, (r, kind) in enumerate(tall):
        direct = g in (ATT, TAB)
        scratch.append(vm(*((plane, first) if direct else (rest - 1, rest * first)), r, width, kind=kind))
    scratch += [vm(2, rest - 1, first, *tall[g][:1], width) for g in (UP, DOWN)]
    scratch += [vm(2, first, r, width, kind=kind) for r, kind in tall]
    scratch += [dma(2, slots), dma(4, slots), dma(4, slots), dma(4, slots)]
    scratch += [dma(4, 2, first), dma(8, first)] + [dma(8, rest - 1)] * 4 + [dma(8, rest)] * 2
    scratch += [dma(8)] * 2 + [dma(8, plane)] * 2 + [dma(8, rest - 1)] * 2 + [dma(8, first), dma(4, 2, first)]
    scratch += [pltpu.SemaphoreType.REGULAR((2, 4))]
    dims = (slots, length, rows, width, ff, head_dim, n)
    vmem = pl.BlockSpec(memory_space=pltpu.VMEM)
    hbm = pl.BlockSpec(memory_space=pltpu.HBM)
    acts, ings, f_a, f_u, f_d, f_t, _, _ = pl.pallas_call(
        functools.partial(whole_kernel, dims),
        out_shape=[jax.ShapeDtypeStruct(*o) for o in outs],
        in_specs=[hbm, hbm, pl.BlockSpec(memory_space=pltpu.SMEM)] + [vmem] * 12,
        out_specs=[hbm, hbm] + [vmem] * 4 + [hbm, hbm],
        scratch_shapes=scratch,
        compiler_params=pltpu.CompilerParams(
            vmem_limit_bytes=(64 << 20) - (96 << 10), collective_id=0, has_side_effects=True
        ),
    )(
        images.transpose(1, 2, 0, 3), cotangent.transpose(1, 2, 0, 3), counts.T, ln1_gain, ln1_bias, b_out, ln2_gain, ln2_bias, b_down, b_qv, b_up,
        w_qkv, w_out, w_up, w_down,
    )

    params = (
        ln1_gain, ln1_bias, w_qkv, b_qv, w_out, b_out, ln2_gain, ln2_bias, w_up, b_up, w_down, b_down
    )
    grads = pl.pallas_call(
        output_kernel,
        out_shape=[jax.ShapeDtypeStruct(p.shape, F32) for p in params],
        in_specs=[vmem] * 4,
        out_specs=[vmem] * len(params),
    )(f_a, f_u, f_d, f_t)

    return (acts[None], ings[None], *grads)


def solution(mesh):
    split = P("section", "fsdp")
    cube = P("section", "fsdp", None)
    image = P(None, "fsdp", None, None)
    result = P("section", None, "fsdp", None, None)
    params = (split, split, cube, split, cube, split, split, split, cube, split, cube, split)
    return jax.shard_map(
        local,
        mesh=mesh,
        in_specs=(image, image, P(None, "fsdp")) + params,
        out_specs=(result, result) + params,
        check_vma=False,
    )
```

```python
import functools
import math

import jax
import jax.numpy as jnp
from jax import lax
from jax.experimental import pallas as pl
from jax.experimental.pallas import tpu as pltpu
from jax.sharding import PartitionSpec as P

HEADS = 6
EPS = 1e-06
F32 = jnp.float32
LOW = jnp.bfloat16

G1, S1, BO, G2, S2, BD, BQ, BV, BU = 0, 1, 2, 3, 4, 5, 6, 7, 8
TABLE = 16
TOGETHER, TOGETHER_ROWS = 2, 3
ATT, UP, DOWN, TAB = 0, 1, 2, 3


def radices(n):
    rest = max(r for r in range(1, n + 1) if r * r * r <= n and n % (r * r) == 0)
    return n // (rest * rest), rest


def mm(left, right):
    return jnp.dot(left, right, preferred_element_type=F32)


def mm_right(left, right):
    return lax.dot_general(left, right, (((1,), (1,)), ((), ())), preferred_element_type=F32)


def mm_left(left, right):
    return lax.dot_general(left, right, (((0,), (0,)), ((), ())), preferred_element_type=F32)


def normal_parts(pre):
    phi = 0.5 + 0.5 * lax.erf(pre * 0.7071067811865476)
    density = jnp.exp2(pre * pre * (-0.5 * 1.4426950408889634)) * 0.3989422804014327
    return phi, phi + pre * density


def normalize(value):
    mean = jnp.mean(value, axis=-1, keepdims=True)
    center = value - mean
    rstd = lax.rsqrt(jnp.mean(center * center, axis=-1, keepdims=True) + EPS)
    return center * rstd, rstd, mean


def normalize_back(d_hat, hat, rstd):
    mean_one = jnp.mean(d_hat, axis=-1, keepdims=True)
    mean_two = jnp.mean(d_hat * hat, axis=-1, keepdims=True)
    return rstd * (d_hat - mean_one - hat * mean_two)


def colsum(value):
    return jnp.sum(value, axis=0, keepdims=True)


def whole_kernel(dims, *refs):
    slots, length, rows, width, ff, head_dim, n = dims
    (
        images, cotangent, counts, v_g1, v_s1, v_bo, v_g2, v_s2, v_bd, v_qv, v_up, a_qkv, a_out, a_up, a_down,
        act_out, ing_out, f_a, f_u, f_d, f_t, hid_far, slope_far,
        xs, raw, io_one, io_two, pack_a, pack_u, pack_d, pack_t,
        wqkv, wout, wup, wdown, table, gtable, rep_one, rep_two, rep_four,
        after_ref, nrm1, qkv, prob, overs, ctx, hat2, nrm2, rstds, hid, slope, dal, low_g, left_t,
        s_a, s_u, s_d, s_t, r0_a, r0_u, r0_d, r0_t, r1_a, r1_u, r1_d, r1_t, r2_u, r2_d,
        r3_a, r3_u, r3_d, r3_t,
        in_s, ship_s, ship_r, far_s, ag1_s, ag1_r, ag2_s, ag2_r, ag3_s, ag3_r, ag4_s, ag4_r,
        rs0_s, rs0_r, rs1_s, rs1_r, rs2_s, rs2_r, rs3_s, rs3_r, credit,
    ) = refs
    groups = (ATT, UP, DOWN, TAB)
    pack = (pack_a, pack_u, pack_d, pack_t)
    stage = (s_a, s_u, s_d, s_t)
    r0, r1, r2 = (r0_a, r0_u, r0_d, r0_t), (r1_a, r1_u, r1_d, r1_t), (None, r2_u, r2_d, None)
    r3, final = (r3_a, r3_u, r3_d, r3_t), (f_a, f_u, f_d, f_t)

    first, rest = radices(n)
    unit = width // n
    core = lax.axis_index("section")
    me = lax.axis_index("fsdp")
    dig_a, dig_b, dig_c = me // (rest * rest), (me // rest) % rest, me % rest
    dig_three, dig_two = dig_c + core * (dig_b - dig_c), dig_b + core * (dig_c - dig_b)
    step_three, step_two = 1 + core * (rest - 1), rest - core * (rest - 1)
    pos = (dig_three * rest + dig_two) * first + dig_a
    pos_of = ((dig_c * rest + dig_b) * first + dig_a, (dig_b * rest + dig_c) * first + dig_a)
    sibling = {"section": 1 - core}

    def place(half, j):
        a, b, c = j // (rest * rest), (j // rest) % rest, j % rest
        return ((c * rest + b) if half == 0 else (b * rest + c)) * first + a

    def peer_first(t):
        return {"fsdp": me + ((dig_a + t) % first - dig_a) * (rest * rest)}

    def peer_two(t):
        return {"fsdp": me + ((dig_two + t) % rest - dig_two) * step_two}

    def peer_three(t):
        return {"fsdp": me + ((dig_three + t) % rest - dig_three) * step_three}

    def peer_plane(three, two):
        here = ((dig_three + three) % rest - dig_three) * step_three
        return {"fsdp": me + here + ((dig_two + two) % rest - dig_two) * step_two}

    plane = [(three, two) for three in range(rest) for two in range(rest) if three or two]

    def remote(src, dst, s_sem, r_sem, device):
        return pltpu.make_async_remote_copy(
            src_ref=src, dst_ref=dst, send_sem=s_sem, recv_sem=r_sem, device_id=device,
            device_id_type=pl.DeviceIdType.MESH,
        )

    def slab_two(three, two):
        return pl.ds((three * rest + two) * first, first)

    def slab_three(three):
        return pl.ds(three * rest * first, rest * first)

    def fill_repeats():
        for ref in (rep_one, rep_two, rep_four):
            part = ref.shape[0]
            lanes = lax.broadcasted_iota(jnp.int32, ref.shape, 1).astype(F32)
            line = lax.broadcasted_iota(jnp.int32, ref.shape, 0).astype(F32)
            rest_of = lanes - part * jnp.floor((lanes + 0.5) * (1.0 / part))
            ref[...] = jnp.where(jnp.abs(rest_of - line) < 0.5, 1.0, 0.0).astype(LOW)

    def own_lanes(part):
        shape = (n, part * n)
        lanes = lax.broadcasted_iota(jnp.int32, shape, 1)
        begin = lax.broadcasted_iota(jnp.int32, shape, 0) * part
        return (lanes >= begin) & (lanes < begin + part)

    shares = (
        ((G1, unit, rep_one), (S1, unit, rep_one), (BO, unit, rep_one), (G2, unit, rep_one), (S2, unit, rep_one),
         (BD, unit, rep_one), (BQ, 2 * unit, rep_two)),
        ((BU, 4 * unit, rep_four),),
    )

    def table_in(b):
        for half in range(2):
            lines = jnp.concatenate([s_t[b, half, place(half, j)] for j in range(n)], axis=0)
            begin = 0
            for row, part, ref in shares[half]:
                spread = mm(lines[:, begin : begin + part].astype(LOW), ref[...])
                line = colsum(jnp.where(own_lanes(part), spread, 0.0))
                for i in range(part * n // width):
                    table[b, row + i : row + i + 1, :] = line[:, width * i : width * (i + 1)]
                begin += part

    def table_out(b):
        for half in range(2):
            parts, begin = [], 0
            for row, part, ref in shares[half]:
                count = part * n // width
                line = jnp.concatenate([gtable[b, row + i : row + i + 1, :] for i in range(count)], axis=1)
                parts.append(mm_right(jnp.where(own_lanes(part), line, 0.0).astype(LOW), ref[...]))
                begin += part
            parts.append(jnp.zeros((n, width - begin), F32))
            lines = jnp.concatenate(parts, axis=1)
            for j in range(n):
                s_t[b, half, place(half, j)] = lines[j : j + 1]

    def pack_own():
        for half in range(2):
            vectors = ((v_g1, v_s1, v_bo, v_g2, v_s2, v_bd, v_qv), (v_up,))[half]
            lines = [vector[...].astype(F32) for vector in vectors]
            lines.append(jnp.zeros((1, width - sum(line.shape[1] for line in lines)), F32))
            pack_t[half] = jnp.concatenate(lines, axis=1)
            for ref in (pack_a, pack_u):
                both = []
                for part in (2 * half, 2 * half + 1):
                    if ref is pack_u:
                        both.append(a_up[0, :, part * width : (part + 1) * width])
                    elif part == 3:
                        both.append(a_out[0])
                    else:
                        both.append(a_qkv[0, :, part * width : (part + 1) * width])
                ref[half] = jnp.concatenate([value.astype(F32) for value in both], axis=0).astype(LOW)
            pack_d[half] = a_down[0, 2 * unit * half : 2 * unit * (half + 1), :]

    def at(b, g):
        return len(groups) * b + g

    def ag1_copy(b, g, half, t):
        device = {"section": half, **peer_first(t)} if t else sibling
        return remote(
            pack[g].at[half], stage[g].at[b, half, pos_of[half]],
            ag1_s.at[g, half, t], ag1_r.at[at(b, g), t], device,
        )

    def ag1_landing(b, g, t):
        ref = stage[g].at[b, core, (dig_three * rest + dig_two) * first + (dig_a + first - t) % first]
        return remote(ref, ref, ag1_s.at[g, 0, t], ag1_r.at[at(b, g), t], sibling)

    def ag2_copy(b, g, t):
        ref = stage[g].at[b, core, slab_two(dig_three, dig_two)]
        return remote(ref, ref, ag2_s.at[at(b, g), t - 1], ag2_r.at[at(b, g), t - 1], peer_two(t))

    def ag3_copy(b, g, t):
        ref = stage[g].at[b, core, slab_three(dig_three)]
        return remote(ref, ref, ag3_s.at[at(b, g), t - 1], ag3_r.at[at(b, g), t - 1], peer_three(t))

    def ag4_copy(b, g, t):
        ref = stage[g].at[b, core, slab_three((dig_three + rest - t) % rest)]
        return remote(ref, ref, ag4_s.at[at(b, g), t], ag4_r.at[at(b, g), t], sibling)

    def ag4_landing(b, g, t):
        ref = stage[g].at[b, 1 - core, slab_three((dig_two + rest - t) % rest)]
        return remote(ref, ref, ag4_s.at[at(b, g), t], ag4_r.at[at(b, g), t], sibling)

    def ag1(b, g):
        @pl.when(core == b)
        def _():
            for t in range(1, first):
                for half in range(2):
                    ag1_copy(b, g, half, t).start()
            ag1_copy(b, g, 1 - b, 0).start()
            stage[g][b, b, pos] = pack[g][b]

    def ag2(b, g):
        for t in range(1, first):
            ag1_landing(b, g, t).wait_recv()

        @pl.when(core != b)
        def _():
            ag1_landing(b, g, 0).wait_recv()

        for t in range(1, rest):
            ag2_copy(b, g, t).start()

    def ag3(b, g):
        for t in range(1, rest):
            ag2_copy(b, g, t).wait_recv()
        for t in range(1, rest):
            ag3_copy(b, g, t).start()
        ag4_copy(b, g, 0).start()

    def ag4(b, g):
        for t in range(1, rest):
            ag3_copy(b, g, t).wait_recv()
            ag4_copy(b, g, t).start()

    def ag5(b, g):
        for t in range(rest):
            ag4_landing(b, g, t).wait_recv()
        lay_out(b, g)

    def ag_sent(b, g):
        @pl.when(core == b)
        def _():
            for t in range(1, first):
                for half in range(2):
                    ag1_copy(b, g, half, t).wait_send()
            ag1_copy(b, g, 1 - b, 0).wait_send()

        for t in range(1, rest):
            ag2_copy(b, g, t).wait_send()
            ag3_copy(b, g, t).wait_send()
        for t in range(rest):
            ag4_copy(b, g, t).wait_send()

    def lay_out(b, g):
        if g == TAB:
            table_in(b)
            return
        if g == DOWN:
            for j in range(n):
                for half in range(2):
                    begin = 4 * unit * j + 2 * unit * half
                    wdown[b, begin : begin + 2 * unit, :] = s_d[b, half, place(half, j)]
            return
        together = 16 // math.gcd(unit, 16)
        for half in range(2):
            for j in range(0, n, together):
                pieces = [stage[g][b, half, place(half, j + i)].astype(F32) for i in range(together)]
                for sub in range(2):
                    low = sub * unit
                    block = jnp.concatenate([piece[low : low + unit] for piece in pieces], axis=0).astype(LOW)
                    part = 2 * half + sub
                    down = slice(unit * j, unit * (j + together))
                    if g == UP:
                        wup[b, down, part * width : (part + 1) * width] = block
                    elif part == 3:
                        wout[b, down, :] = block
                    else:
                        wqkv[b, down, part * width : (part + 1) * width] = block

    def rs0_copy(b, g):
        return remote(stage[g].at[b, 1 - core], r0[g], rs0_s.at[at(b, g)], rs0_r.at[at(b, g)], sibling)

    def rs1_copy(b, g, t):
        return remote(
            stage[g].at[b, core, slab_three((dig_three + t) % rest)], r1[g].at[t - 1],
            rs1_s.at[at(b, g), t - 1], rs1_r.at[at(b, g), t - 1], peer_three(t),
        )

    def rs2_copy(b, g, t):
        return remote(
            stage[g].at[b, core, slab_two(dig_three, (dig_two + t) % rest)], r2[g].at[b, t - 1],
            rs2_s.at[at(b, g), t - 1], rs2_r.at[at(b, g), t - 1], peer_two(t),
        )

    def rs3_copy(b, g, t):
        there = (dig_three * rest + dig_two) * first + (dig_a + t) % first
        device = {"section": b, **peer_first(t)} if t else sibling
        return remote(
            stage[g].at[b, core, there], r3[g].at[core, t], rs3_s.at[at(b, g), t], rs3_r.at[g, core, t], device
        )

    def plane_copy(b, g, t):
        three, two = plane[t]
        return remote(
            stage[g].at[b, core, slab_two((dig_three + three) % rest, (dig_two + two) % rest)], r1[g].at[t],
            rs1_s.at[at(b, g), t], rs1_r.at[at(b, g), t], peer_plane(three, two),
        )

    def rs0(b, g):
        @pl.when(b == 0)
        def _():
            pl.semaphore_wait(credit.at[0, g], 1)

        rs0_copy(b, g).start()

    def rs1(b, g):
        rs0_copy(b, g).wait_recv()

        @pl.loop(0, n)
        def _(p):
            stage[g][b, core, p] = stage[g][b, core, p] + r0[g][p]

        @pl.when(b == 1)
        def _():
            pl.semaphore_signal(credit.at[0, g], inc=1, device_id=sibling, device_id_type=pl.DeviceIdType.MESH)

        direct = g in (ATT, TAB)
        if rest > 1:
            @pl.when(b == 0)
            def _():
                pl.semaphore_wait(credit.at[1, g], len(plane) if direct else rest - 1)

        if direct:
            for t in range(len(plane)):
                plane_copy(b, g, t).start()
            return
        for t in range(1, rest):
            rs1_copy(b, g, t).start()

    def rs2(b, g):
        for t in range(1, rest):
            rs1_copy(b, g, t).wait_recv()

        @pl.loop(0, rest * first)
        def _(p):
            here = dig_three * rest * first + p
            total = stage[g][b, core, here].astype(F32)
            for t in range(1, rest):
                total = total + r1[g][t - 1, p].astype(F32)
            stage[g][b, core, here] = total.astype(stage[g].dtype)

        for t in range(1, rest):
            @pl.when(b == 1)
            def _():
                pl.semaphore_signal(
                    credit.at[1, g], inc=1, device_id=peer_three(t), device_id_type=pl.DeviceIdType.MESH
                )

            rs2_copy(b, g, t).start()

    def rs3(b, g):
        direct = g in (ATT, TAB)
        copies = [plane_copy(b, g, t) for t in range(len(plane))] if direct else [
            rs2_copy(b, g, t) for t in range(1, rest)
        ]
        landing = r1[g] if direct else r2[g].at[b]
        for copy in copies:
            copy.wait_recv()

        @pl.loop(0, first)
        def _(p):
            here = (dig_three * rest + dig_two) * first + p
            total = stage[g][b, core, here].astype(F32)
            for t in range(len(copies)):
                total = total + landing[t, p].astype(F32)
            stage[g][b, core, here] = total.astype(stage[g].dtype)

        if direct:
            @pl.when(b == 1)
            def _():
                for three, two in plane:
                    pl.semaphore_signal(
                        credit.at[1, g], inc=1, device_id=peer_plane(three, two),
                        device_id_type=pl.DeviceIdType.MESH,
                    )


        for t in range(1, first):
            rs3_copy(b, g, t).start()

        @pl.when(core != b)
        def _():
            rs3_copy(b, g, 0).start()

    def rs4(b, g):
        @pl.when(core == b)
        def _():
            for own in (True, False):
                half = core if own else 1 - core
                begin = int(own)
                for t in range(begin, first):
                    ref = r3[g].at[half, t]
                    remote(ref, ref, rs3_s.at[at(b, g), t], rs3_r.at[g, half, t], sibling).wait_recv()
                total = stage[g][b, core, pos].astype(F32) if own else None
                for t in range(begin, first):
                    value = r3[g][half, t].astype(F32)
                    total = value if total is None else total + value
                final[g][half] = total

    def rs_sent(b, g):
        rs0_copy(b, g).wait_send()
        if g in (ATT, TAB):
            for t in range(len(plane)):
                plane_copy(b, g, t).wait_send()
        else:
            for t in range(1, rest):
                rs1_copy(b, g, t).wait_send()
                rs2_copy(b, g, t).wait_send()
        for t in range(1, first):
            rs3_copy(b, g, t).wait_send()

        @pl.when(core != b)
        def _():
            rs3_copy(b, g, 0).wait_send()

    def rows_of(i, images_too=1):
        return pl.ds(pl.multiple_of(i * rows, 16), images_too * rows)

    few = TOGETHER if slots % TOGETHER == 0 else 1
    many = TOGETHER_ROWS if slots % TOGETHER_ROWS == 0 else 1

    def step_rows(i, count):
        return rows_of(i * count, count)

    def ship_parts(kind, b, i):
        src, out = ((io_one, act_out), (io_two, ing_out))[kind]
        q = 2 * kind + b
        near = pltpu.make_async_copy(src.at[i], out.at[core, i], ship_s.at[q, i])
        far = remote(src.at[i], out.at[core, i], ship_s.at[q, i], ship_r.at[q, i], sibling)
        return near, far

    def ship(kind, b, i):
        near, far = ship_parts(kind, b, i)

        @pl.when(core == b)
        def _():
            near.start()

        @pl.when(core != b)
        def _():
            far.start()

    def shipped(kind, b, i):
        near, far = ship_parts(kind, b, i)

        @pl.when(core == b)
        def _():
            near.wait()

        @pl.when(core != b)
        def _():
            far.wait_send()

    def landed(kind, b, i):
        out = (act_out, ing_out)[kind]
        q = 2 * kind + b
        ref = out.at[1 - core, i]

        @pl.when(core == b)
        def _():
            remote(ref, ref, ship_s.at[q, i], ship_r.at[q, i], sibling).wait_recv()

    def live(i):
        return jnp.where(i < counts[0, core], 1.0, 0.0).astype(F32)

    def only_live(i, value, count):
        parts = [value[rows * m : rows * (m + 1)] * live(i * count + m) for m in range(count)]
        return jnp.concatenate(parts, axis=0)

    def coming(which, i):
        slot = (which * slots + i) % raw.shape[0]
        return pltpu.make_async_copy((images, cotangent)[which].at[i], raw.at[slot], in_s.at[which, i])

    def take_in(which, i):
        coming(which, i).wait()
        both = raw[(which * slots + i) % raw.shape[0]].astype(F32)
        (io_one, io_two)[which][i] = jnp.where(core == 0, both[:, 0, :], both[:, 1, :]).astype(LOW)

    def far_copy(which, i, back):
        near, far = ((hid, hid_far), (slope, slope_far))[which]
        near, far = near.at[rows_of(i)], far.at[rows_of(i)]
        src, dst = (far, near) if back else (near, far)
        return pltpu.make_async_copy(src, dst, far_s.at[2 * int(back) + which, i])

    pairs = width // 128
    scale = head_dim ** -0.5
    lane = lax.broadcasted_iota(jnp.int32, (1, 128), 1)
    half_low = [(lane < head_dim).astype(LOW), (lane >= head_dim).astype(LOW)]
    half_f = [(lane < head_dim).astype(F32), (lane >= head_dim).astype(F32)]
    token = lax.broadcasted_iota(jnp.int32, (rows, 128), 0) < length
    half_valid = [jnp.where(token, half_f[j], 0.0).astype(LOW) for j in range(2)]
    valid = jnp.where(token, 1.0, 0.0).astype(F32)
    chunk = 256
    chunks = ff // chunk

    def vec(s, r):
        return table[s, r : r + 1, :]

    def up_bias(s, c):
        begin = c * chunk
        row, col = begin // width, begin % width
        if col + chunk <= width:
            return table[s, BU + row : BU + row + 1, col : col + chunk]
        a = table[s, BU + row : BU + row + 1, col:width]
        b = table[s, BU + row + 1 : BU + row + 2, 0 : chunk - (width - col)]
        return jnp.concatenate([a, b], axis=1)

    def add_vec(s, r, value):
        gtable[s, r : r + 1, :] += value

    def add_up_bias(s, c, value):
        begin = c * chunk
        row, col = begin // width, begin % width
        if col + chunk <= width:
            gtable[s, BU + row : BU + row + 1, col : col + chunk] += value
        else:
            cut = width - col
            gtable[s, BU + row : BU + row + 1, col:width] += value[:, :cut]
            gtable[s, BU + row + 1 : BU + row + 2, 0 : chunk - cut] += value[:, cut:]

    def attn_forward(s, x, hat, i):
        rd = step_rows(i, few)
        nrm_ref, qkv_ref, prob_ref, ctx_ref = nrm1.at[s], qkv.at[s], prob.at[s], ctx.at[s]
        nrm = (hat * vec(s, G1) + vec(s, S1)).astype(LOW)
        nrm_ref[rd, :] = nrm
        mixed = mm(nrm, wqkv[s])
        q = (mixed[:, 0:width] + vec(s, BQ)).astype(LOW)
        k = mixed[:, width : 2 * width].astype(LOW)
        v = (mixed[:, 2 * width :] + vec(s, BV)).astype(LOW)
        qkv_ref[rd, 0:width] = q
        qkv_ref[rd, width : 2 * width] = k
        qkv_ref[rd, 2 * width :] = v
        images_out = []
        for m in range(few):
            mine = slice(rows * m, rows * (m + 1))
            parts = []
            for p in range(pairs):
                cols = slice(128 * p, 128 * p + 128)
                total = None
                for j in range(2):
                    scores = mm_right(q[mine, cols], k[mine, cols] * half_low[j])
                    top = jnp.max(scores, axis=-1, keepdims=True)
                    e = jnp.exp2((scores - top) * (scale * 1.4426950408889634)).astype(LOW)
                    prob_ref[i * few + m, 2 * p + j] = e
                    part = mm(e, jnp.concatenate([v[mine, cols] * half_valid[j], half_valid[j]], axis=1))
                    total = part if total is None else total + part
                over = 1.0 / total[:, 128:]
                overs[s, rows_of(i * few + m), cols] = over.astype(LOW)
                parts.append((total[:, :128] * over).astype(LOW))
            images_out.append(jnp.concatenate(parts, axis=1))
        context = jnp.concatenate(images_out, axis=0)
        ctx_ref[rd, :] = context
        return x + mm(context, wout[s]) + vec(s, BO)

    def ff_forward(s, after, rd):
        nrm_ref = nrm2.at[s]
        hat, rstd, _ = normalize(after)
        hat2[s, rd, :] = hat.astype(LOW)
        nrm = (hat * vec(s, G2) + vec(s, S2)).astype(LOW)
        nrm_ref[rd, :] = nrm
        total = after + vec(s, BD)
        for c in range(chunks):
            cols = slice(chunk * c, chunk * c + chunk)
            pre = mm(nrm, wup[s, :, cols]) + up_bias(s, c)
            phi, slo = normal_parts(pre)
            h = (pre * phi).astype(LOW)
            hid[rd, cols] = h
            slope[rd, cols] = slo.astype(LOW)
            total = total + mm(h, wdown[s, cols, :])
        return total, rstd

    def ff_backward(s, g, rd, rstd):
        g_low = g.astype(LOW)
        add_vec(s, BD, colsum(g_low.astype(F32)))
        d_nrm = None
        for c in range(chunks):
            cols = slice(chunk * c, chunk * c + chunk)
            d_hid = mm_right(g_low, wdown[s, cols, :])
            d_pre = (d_hid * slope[rd, cols].astype(F32)).astype(LOW)
            slope[rd, cols] = d_pre
            add_up_bias(s, c, colsum(d_pre.astype(F32)))
            part = mm_right(d_pre, wup[s, :, cols])
            d_nrm = part if d_nrm is None else d_nrm + part
        hat = hat2[s, rd, :].astype(F32)
        add_vec(s, G2, colsum(d_nrm * hat))
        add_vec(s, S2, colsum(d_nrm))
        d_after = g + normalize_back(d_nrm * vec(s, G2), hat, rstd)
        low = d_after.astype(LOW)
        dal[rd, :] = low
        add_vec(s, BO, colsum(low.astype(F32)))
        return d_after

    def attn_backward(s, i):
        qkv_ref, prob_ref, ctx_ref = qkv.at[s], prob.at[s], ctx.at[s]
        rd = step_rows(i, few)
        d_context = mm_right(dal[rd, :], wout[s])
        d_context = (d_context * overs[s, rd, :].astype(F32)).astype(LOW)
        for m in range(few):
            rd = rows_of(i * few + m)
            d_ctx = d_context[rows * m : rows * (m + 1)]
            dq, dk, dv = [], [], []
            for p in range(pairs):
                cols = slice(128 * p, 128 * p + 128)
                q = qkv_ref[rd, 128 * p : 128 * p + 128]
                k = qkv_ref[rd, width + 128 * p : width + 128 * p + 128]
                v = qkv_ref[rd, 2 * width + 128 * p : 2 * width + 128 * p + 128]
                dc = d_ctx[:, cols]
                both = dc.astype(F32) * ctx_ref[rd, cols].astype(F32)
                sums = [None, None, None]
                for j in range(2):
                    e = prob_ref[i * few + m, 2 * p + j]
                    delta = jnp.sum(both * half_f[j], axis=-1, keepdims=True)
                    d_prob = mm_right(dc, v * half_low[j])
                    ds = (e.astype(F32) * (d_prob - delta)).astype(LOW)
                    new = [mm(ds, k * half_valid[j]), mm_left(ds, q * half_low[j]), mm_left(e, dc * half_low[j])]
                    sums = [b if a is None else a + b for a, b in zip(sums, new)]
                dq.append((sums[0] * scale).astype(LOW))
                dk.append((sums[1] * (valid * scale)).astype(LOW))
                dv.append((sums[2] * valid).astype(LOW))
            d_mixed = jnp.concatenate(dq + dk + dv, axis=1)
            qkv_ref[rd, :] = d_mixed
            add_vec(s, BQ, colsum(d_mixed[:, 0:width].astype(F32)))
            add_vec(s, BV, colsum(d_mixed[:, 2 * width :].astype(F32)))

    def input_backward(s, d_after, rd, x, mean, rstd):
        d_nrm = mm_right(qkv[s, rd, :], wqkv[s])
        hat = (x - mean) * rstd
        add_vec(s, G1, colsum(d_nrm * hat))
        add_vec(s, S1, colsum(d_nrm))
        return d_after + normalize_back(d_nrm * vec(s, G1), hat, rstd)

    def grads_down(s):
        left_t[...] = low_g[...].T

        @pl.loop(0, 4)
        def _(c):
            cols = pl.ds(pl.multiple_of(c * width, 128), width)
            block = mm(left_t[...], hid[:, cols]).T
            for i in range(n // 4):
                for half in range(2):
                    begin = 4 * unit * i + 2 * unit * half
                    s_d[s, half, place(half, c * (n // 4) + i)] = block[begin : begin + 2 * unit].astype(LOW)

    def pair_out(ref, s, half, one, two):
        for j in range(n):
            down = slice(unit * j, unit * (j + 1))
            piece = jnp.concatenate([one[down], two[down]], axis=0).astype(LOW)
            ref[s, half, place(half, j)] = piece

    def grads_up(s):
        left_t[...] = nrm2[s].T
        for half in range(2):
            one, two = [
                mm(left_t[...], slope[:, part * width : (part + 1) * width]) for part in (2 * half, 2 * half + 1)
            ]
            pair_out(s_u, s, half, one, two)

    def grads_attn(s):
        mix_s = qkv.at[s]
        left_t[...] = ctx[s].T
        four = mm(left_t[...], dal[...])
        left_t[...] = nrm1[s].T
        three = mm(left_t[...], mix_s[:, 2 * width :])
        pair_out(s_a, s, 1, three, four)
        one = mm(left_t[...], mix_s[:, 0:width])
        two = mm(left_t[...], mix_s[:, width : 2 * width])
        pair_out(s_a, s, 0, one, two)

    barrier = pltpu.get_barrier_semaphore()
    greeted = [sibling]
    greeted += [{"section": half, **peer_first(t)} for t in range(1, first) for half in range(2)]
    greeted += [peer_plane(three, two) for three, two in plane]
    for device in greeted:
        pl.semaphore_signal(barrier, inc=1, device_id=device, device_id_type=pl.DeviceIdType.MESH)
    pack_own()
    pl.semaphore_wait(barrier, len(greeted))

    def run(*todo):
        for f, b, g in todo:
            f(b, g)

    def events(i, table_of):
        for when, todo in table_of.items():
            @pl.when(i == when)
            def _():
                run(*todo)

    def both(f, b, g):
        return [(f, b, g), (f, b, TAB)]

    def take(i, m):
        return pl.ds(pl.multiple_of((i * many + m) * rows, 16), length)

    ahead = raw.shape[0]
    run(*both(ag1, 0, ATT))
    for i in range(ahead):
        coming(0, i).start()
    fill_repeats()
    gtable[...] = jnp.zeros_like(gtable)
    low_g[...] = jnp.zeros_like(low_g)
    xs[0] = jnp.zeros_like(low_g)

    @pl.loop(0, slots)
    def images_in(i):
        take_in(0, i)

        @pl.when(i + ahead < slots)
        def _():
            coming(0, i + ahead).start()

        @pl.when(i + ahead >= slots)
        def _():
            coming(1, i + ahead - slots).start()

        @pl.when(i == 3)
        def _():
            run(*both(ag2, 0, ATT), (ag1, 0, UP), (ag1, 0, DOWN))

    def statistic(s, rd, which):
        return jnp.where(s == 0, rstds[rd, which : which + 1], rstds[rd, 3 + which : 4 + which])

    def first_norm(s, rd, x):
        hat, rstd, mean = normalize(x)
        after_ref[rd, :] = hat
        rstds[rd, 3 * s : 3 * s + 1] = rstd
        rstds[rd, 3 * s + 2 : 3 * s + 3] = mean

    @pl.loop(0, slots // many)
    def norm_one(i):
        for m in range(many):
            xs[0, take(i, m), :] = io_one[i * many + m]
        rd = step_rows(i, many)
        x = xs[0, rd, :].astype(F32)
        token_rows = lax.broadcasted_iota(jnp.int32, (rows, width), 0) < length
        parts = [x[rows * m : rows * (m + 1)] for m in range(many)]
        x = jnp.concatenate([jnp.where(token_rows, part, part[0:1]) for part in parts], axis=0)
        xs[0, rd, :] = x.astype(LOW)
        first_norm(0, rd, x)

    run(*both(ag3, 0, ATT), (ag2, 0, UP), *both(ag1, 1, ATT), (ag2, 0, DOWN), (ag1, 1, UP), (ag1, 1, DOWN))

    @pl.loop(0, slots)
    def cotangents_in(i):
        take_in(1, i)

        @pl.when(i + ahead < slots)
        def _():
            coming(1, i + ahead).start()

    run(*both(ag4, 0, ATT), (ag3, 0, UP), *both(ag5, 0, ATT))

    @pl.loop(0, 2)
    def forward(s):
        @pl.loop(0, slots // few)
        def attention(i):
            @pl.when(s == 0)
            def _():
                events(i, {
                    0: [(ag3, 0, DOWN), *both(ag2, 1, ATT)],
                    1: [(ag4, 0, UP), (ag2, 1, UP)],
                    2: [(ag4, 0, DOWN)],
                })

            @pl.when(s == 1)
            def _():
                events(i, {2: [(ag4, 1, DOWN)]})

            rd = step_rows(i, few)
            after_ref[rd, :] = attn_forward(s, xs[s, rd, :].astype(F32), after_ref[rd, :], i)

        @pl.when(s == 0)
        def _():
            run(*both(ag3, 1, ATT), (ag5, 0, UP), (ag5, 0, DOWN))

        @pl.when(s == 1)
        def _():
            run((ag5, 1, UP), (ag5, 1, DOWN))

        @pl.loop(0, slots // many)
        def feed_forward(i):
            @pl.when(s == 0)
            def _():
                events(i, {0: [(ag3, 1, UP), (ag2, 1, DOWN)], 1: both(ag4, 1, ATT)})

            rd = step_rows(i, many)

            @pl.when(s == 1)
            def _():
                for m in range(many):
                    far_copy(0, i * many + m, False).wait()
                    far_copy(1, i * many + m, False).wait()
                    shipped(0, 0, i * many + m)

            out, rstd2 = ff_forward(s, after_ref[rd, :], rd)
            for block in range(2):
                @pl.when(s == block)
                def _():
                    rstds[rd, 3 * block + 1 : 3 * block + 2] = rstd2

            out = only_live(i, out, many)
            for m in range(many):
                io_one[i * many + m] = out[rows * m : rows * m + length].astype(LOW)
                ship(0, s, i * many + m)

            @pl.when(s == 0)
            def _():
                for m in range(many):
                    far_copy(0, i * many + m, False).start()
                    far_copy(1, i * many + m, False).start()
                low = out.astype(LOW)
                xs[1, rd, :] = low
                first_norm(1, rd, low.astype(F32))

        @pl.when(s == 0)
        def _():
            run((ag4, 1, UP), (ag3, 1, DOWN), *both(ag5, 1, ATT))

    for b in range(2):
        for g in groups:
            ag_sent(b, g)

    @pl.loop(0, 2)
    def backward(turn):
        s = 1 - turn

        @pl.loop(0, slots // many)
        def feed_forward(i):
            @pl.when(s == 0)
            def _():
                events(i, {1: [(rs1, 1, TAB), (rs4, 1, UP)]})
                for m in range(many):
                    far_copy(1, i * many + m, True).wait()

            rd = step_rows(i, many)
            for m in range(many):
                g = live(i * many + m) * io_two[i * many + m].astype(F32)
                low_g[take(i, m), :] = g.astype(LOW)
            after_ref[rd, :] = ff_backward(s, low_g[rd, :].astype(F32), rd, statistic(s, rd, 1))

        @pl.when(s == 0)
        def _():
            for i in range(slots):
                far_copy(0, i, True).wait()
            run((rs3, 1, ATT))

        grads_down(s)
        run((rs0, s, DOWN))

        @pl.when(s == 1)
        def _():
            for i in range(slots):
                far_copy(0, i, True).start()

        grads_up(s)
        run((rs0, s, UP), (rs1, s, DOWN))

        @pl.when(s == 1)
        def _():
            for i in range(slots):
                far_copy(1, i, True).start()

        @pl.when(s == 0)
        def _():
            run((rs3, 1, TAB))

        @pl.loop(0, slots // few)
        def attention(i):
            events(i, {1: [(rs1, s, UP), (rs2, s, DOWN)], 2: [(rs2, s, UP), (rs3, s, DOWN)]})

            @pl.when(s == 0)
            def _():
                events(i, {1: both(rs4, 1, ATT)})

            attn_backward(s, i)

        grads_attn(s)
        run((rs0, s, ATT), (rs3, s, UP))

        @pl.loop(0, slots // many)
        def to_input(i):
            events(i, {1: [(rs1, s, ATT), (rs4, s, DOWN)]})
            rd = step_rows(i, many)
            x = xs[s, rd, :].astype(F32)
            d_in = input_backward(s, after_ref[rd, :], rd, x, statistic(s, rd, 2), statistic(s, rd, 0))
            for m in range(many):
                @pl.when(s == 0)
                def _():
                    shipped(1, 1, i * many + m)

                io_two[i * many + m] = d_in[rows * m : rows * m + length].astype(LOW)
                ship(1, s, i * many + m)

        table_out(s)
        run((rs0, s, TAB))

    run((rs4, 0, UP), (rs1, 0, TAB), (rs3, 0, ATT), (rs3, 0, TAB))

    @pl.loop(0, slots)
    def all_out(i):
        shipped(0, 1, i)
        shipped(1, 0, i)
        for kind in range(2):
            for b in range(2):
                landed(kind, b, i)

    run(*both(rs4, 0, ATT))
    for b in range(2):
        for g in groups:
            rs_sent(b, g)


def output_kernel(
    f_a, f_u, f_d, f_t, o_g1, o_s1, o_qkv, o_qv, o_out, o_bo, o_g2, o_s2, o_up, o_bu, o_down, o_bd
):
    unit, width = o_out.shape[1:]
    for half in range(2):
        o_down[0, 2 * unit * half : 2 * unit * (half + 1), :] = f_d[half]
        for sub in range(2):
            part = 2 * half + sub
            cols = slice(part * width, (part + 1) * width)
            o_up[0, :, cols] = f_u[half, unit * sub : unit * (sub + 1), :]
            piece = f_a[half, unit * sub : unit * (sub + 1), :]
            if part == 3:
                o_out[0] = piece
            else:
                o_qkv[0, :, cols] = piece
    begin = 0
    for out in (o_g1, o_s1, o_bo, o_g2, o_s2, o_bd, o_qv):
        part = out.shape[1]
        out[...] = f_t[0, :, begin : begin + part]
        begin += part
    o_bu[...] = f_t[1, :, 0 : o_bu.shape[1]]


def local(
    images, cotangent, counts,
    ln1_gain, ln1_bias, w_qkv, b_qv, w_out, b_out, ln2_gain, ln2_bias, w_up, b_up, w_down, b_down,
):
    micro_count, slots, length, width = images.shape
    ff = w_up.shape[2]
    rows = -(-length // 16) * 16
    n = lax.axis_size("fsdp")
    unit = width // n
    first, rest = radices(n)
    total = slots * rows
    head_dim = width // HEADS

    def vm(*shape, kind=LOW):
        return pltpu.VMEM(shape, kind)

    tall = [(2 * unit, LOW)] * 3 + [(1, F32)]
    dma = lambda *shape: pltpu.SemaphoreType.DMA(shape)
    outs = [((2, slots, length, width), LOW), ((2, slots, length, width), LOW)]
    outs += [((2, r, width), F32) for r, _ in tall] + [((total, ff), LOW), ((total, ff), LOW)]
    scratch = [
        vm(2, total, width), vm(3, length, 2, width), vm(slots, length, width), vm(slots, length, width),
        *[vm(2, r, width, kind=kind) for r, kind in tall],
        vm(2, width, 3 * width), vm(2, width, width), vm(2, width, ff), vm(2, ff, width),
        vm(2, TABLE, width, kind=F32), vm(2, TABLE, width, kind=F32),
        vm(unit, width), vm(2 * unit, 2 * width), vm(4 * unit, 4 * width),
        vm(total, width, kind=F32), vm(2, total, width), vm(2, total, 3 * width), vm(2, slots, HEADS, rows, rows),
        vm(2, total, width),
        vm(2, total, width), vm(2, total, width), vm(2, total, width), vm(total, 6, kind=F32),
        vm(total, ff), vm(total, ff), vm(total, width), vm(total, width), vm(width, total),
    ]
    scratch += [vm(2, 2, n, r, width, kind=kind) for r, kind in tall]
    scratch += [vm(n, r, width, kind=kind) for r, kind in tall]
    plane = rest * rest - 1
    for g, (r, kind) in enumerate(tall):
        direct = g in (ATT, TAB)
        scratch.append(vm(*((plane, first) if direct else (rest - 1, rest * first)), r, width, kind=kind))
    scratch += [vm(2, rest - 1, first, *tall[g][:1], width) for g in (UP, DOWN)]
    scratch += [vm(2, first, r, width, kind=kind) for r, kind in tall]
    scratch += [dma(2, slots), dma(4, slots), dma(4, slots), dma(4, slots)]
    scratch += [dma(4, 2, first), dma(8, first)] + [dma(8, rest - 1)] * 4 + [dma(8, rest)] * 2
    scratch += [dma(8)] * 2 + [dma(8, plane)] * 2 + [dma(8, rest - 1)] * 2 + [dma(8, first), dma(4, 2, first)]
    scratch += [pltpu.SemaphoreType.REGULAR((2, 4))]
    dims = (slots, length, rows, width, ff, head_dim, n)
    vmem = pl.BlockSpec(memory_space=pltpu.VMEM)
    hbm = pl.BlockSpec(memory_space=pltpu.HBM)
    acts, ings, f_a, f_u, f_d, f_t, _, _ = pl.pallas_call(
        functools.partial(whole_kernel, dims),
        out_shape=[jax.ShapeDtypeStruct(*o) for o in outs],
        in_specs=[hbm, hbm, pl.BlockSpec(memory_space=pltpu.SMEM)] + [vmem] * 12,
        out_specs=[hbm, hbm] + [vmem] * 4 + [hbm, hbm],
        scratch_shapes=scratch,
        compiler_params=pltpu.CompilerParams(
            vmem_limit_bytes=(64 << 20) - (96 << 10), collective_id=0, has_side_effects=True
        ),
    )(
        images.transpose(1, 2, 0, 3), cotangent.transpose(1, 2, 0, 3), counts.T, ln1_gain, ln1_bias, b_out, ln2_gain, ln2_bias, b_down, b_qv, b_up,
        w_qkv, w_out, w_up, w_down,
    )

    params = (
        ln1_gain, ln1_bias, w_qkv, b_qv, w_out, b_out, ln2_gain, ln2_bias, w_up, b_up, w_down, b_down
    )
    grads = pl.pallas_call(
        output_kernel,
        out_shape=[jax.ShapeDtypeStruct(p.shape, F32) for p in params],
        in_specs=[vmem] * 4,
        out_specs=[vmem] * len(params),
    )(f_a, f_u, f_d, f_t)

    return (acts[None], ings[None], *grads)


def solution(mesh):
    split = P("section", "fsdp")
    cube = P("section", "fsdp", None)
    image = P(None, "fsdp", None, None)
    result = P("section", None, "fsdp", None, None)
    params = (split, split, cube, split, cube, split, split, split, cube, split, cube, split)
    return jax.shard_map(
        local,
        mesh=mesh,
        in_specs=(image, image, P(None, "fsdp")) + params,
        out_specs=(result, result) + params,
        check_vma=False,
    )
```

```python
import functools
import math

import jax
import jax.numpy as jnp
from jax import lax
from jax.experimental import pallas as pl
from jax.experimental.pallas import tpu as pltpu
from jax.sharding import PartitionSpec as P

HEADS = 6
EPS = 1e-06
F32 = jnp.float32
LOW = jnp.bfloat16

G1, S1, BO, G2, S2, BD, BQ, BV, BU = 0, 1, 2, 3, 4, 5, 6, 7, 8
TABLE = 16
TOGETHER, TOGETHER_ROWS = 2, 3
ATT, UP, DOWN, TAB = 0, 1, 2, 3


def radices(n):
    rest = max(r for r in range(1, n + 1) if r * r * r <= n and n % (r * r) == 0)
    return n // (rest * rest), rest


def mm(left, right):
    return jnp.dot(left, right, preferred_element_type=F32)


def mm_right(left, right):
    return lax.dot_general(left, right, (((1,), (1,)), ((), ())), preferred_element_type=F32)


def mm_left(left, right):
    return lax.dot_general(left, right, (((0,), (0,)), ((), ())), preferred_element_type=F32)


def normal_parts(pre):
    phi = 0.5 + 0.5 * lax.erf(pre * 0.7071067811865476)
    density = jnp.exp2(pre * pre * (-0.5 * 1.4426950408889634)) * 0.3989422804014327
    return phi, phi + pre * density


def normalize(value):
    mean = jnp.mean(value, axis=-1, keepdims=True)
    center = value - mean
    rstd = lax.rsqrt(jnp.mean(center * center, axis=-1, keepdims=True) + EPS)
    return center * rstd, rstd, mean


def normalize_back(d_hat, hat, rstd):
    mean_one = jnp.mean(d_hat, axis=-1, keepdims=True)
    mean_two = jnp.mean(d_hat * hat, axis=-1, keepdims=True)
    return rstd * (d_hat - mean_one - hat * mean_two)


def colsum(value):
    return jnp.sum(value, axis=0, keepdims=True)


def whole_kernel(dims, *refs):
    slots, length, rows, width, ff, head_dim, n = dims
    (
        images, cotangent, counts, v_g1, v_s1, v_bo, v_g2, v_s2, v_bd, v_qv, v_up, a_qkv, a_out, a_up, a_down,
        act_out, ing_out, f_a, f_u, f_d, f_t, hid_far, slope_far,
        xs, raw, io_one, io_two, pack_a, pack_u, pack_d, pack_t,
        wqkv, wout, wup, wdown, table, gtable, rep_one, rep_two, rep_four,
        after_ref, nrm1, qkv, prob, overs, ctx, hat2, rstds, hid, slope, dal, low_g, left_t,
        s_a, s_u, s_d, s_t, r0_a, r0_u, r0_d, r0_t, r1_a, r1_u, r1_d, r1_t, r2_u, r2_d,
        r3_a, r3_u, r3_d, r3_t,
        in_s, ship_s, ship_r, far_s, ag1_s, ag1_r, ag2_s, ag2_r, ag3_s, ag3_r, ag4_s, ag4_r,
        rs0_s, rs0_r, rs1_s, rs1_r, rs2_s, rs2_r, rs3_s, rs3_r, credit,
    ) = refs
    groups = (ATT, UP, DOWN, TAB)
    pack = (pack_a, pack_u, pack_d, pack_t)
    stage = (s_a, s_u, s_d, s_t)
    r0, r1, r2 = (r0_a, r0_u, r0_d, r0_t), (r1_a, r1_u, r1_d, r1_t), (None, r2_u, r2_d, None)
    r3, final = (r3_a, r3_u, r3_d, r3_t), (f_a, f_u, f_d, f_t)

    first, rest = radices(n)
    unit = width // n
    core = lax.axis_index("section")
    me = lax.axis_index("fsdp")
    dig_a, dig_b, dig_c = me // (rest * rest), (me // rest) % rest, me % rest
    dig_three, dig_two = dig_c + core * (dig_b - dig_c), dig_b + core * (dig_c - dig_b)
    step_three, step_two = 1 + core * (rest - 1), rest - core * (rest - 1)
    pos = (dig_three * rest + dig_two) * first + dig_a
    pos_of = ((dig_c * rest + dig_b) * first + dig_a, (dig_b * rest + dig_c) * first + dig_a)
    sibling = {"section": 1 - core}

    def place(half, j):
        a, b, c = j // (rest * rest), (j // rest) % rest, j % rest
        return ((c * rest + b) if half == 0 else (b * rest + c)) * first + a

    def peer_first(t):
        return {"fsdp": me + ((dig_a + t) % first - dig_a) * (rest * rest)}

    def peer_two(t):
        return {"fsdp": me + ((dig_two + t) % rest - dig_two) * step_two}

    def peer_three(t):
        return {"fsdp": me + ((dig_three + t) % rest - dig_three) * step_three}

    def peer_plane(three, two):
        here = ((dig_three + three) % rest - dig_three) * step_three
        return {"fsdp": me + here + ((dig_two + two) % rest - dig_two) * step_two}

    plane = [(three, two) for three in range(rest) for two in range(rest) if three or two]

    def remote(src, dst, s_sem, r_sem, device):
        return pltpu.make_async_remote_copy(
            src_ref=src, dst_ref=dst, send_sem=s_sem, recv_sem=r_sem, device_id=device,
            device_id_type=pl.DeviceIdType.MESH,
        )

    def slab_two(three, two):
        return pl.ds((three * rest + two) * first, first)

    def slab_three(three):
        return pl.ds(three * rest * first, rest * first)

    def fill_repeats():
        for ref in (rep_one, rep_two, rep_four):
            part = ref.shape[0]
            lanes = lax.broadcasted_iota(jnp.int32, ref.shape, 1).astype(F32)
            line = lax.broadcasted_iota(jnp.int32, ref.shape, 0).astype(F32)
            rest_of = lanes - part * jnp.floor((lanes + 0.5) * (1.0 / part))
            ref[...] = jnp.where(jnp.abs(rest_of - line) < 0.5, 1.0, 0.0).astype(LOW)

    def own_lanes(part):
        shape = (n, part * n)
        lanes = lax.broadcasted_iota(jnp.int32, shape, 1)
        begin = lax.broadcasted_iota(jnp.int32, shape, 0) * part
        return (lanes >= begin) & (lanes < begin + part)

    shares = (
        ((G1, unit, rep_one), (S1, unit, rep_one), (BO, unit, rep_one), (G2, unit, rep_one), (S2, unit, rep_one),
         (BD, unit, rep_one), (BQ, 2 * unit, rep_two)),
        ((BU, 4 * unit, rep_four),),
    )

    def table_in(b):
        for half in range(2):
            lines = jnp.concatenate([s_t[b, half, place(half, j)] for j in range(n)], axis=0)
            begin = 0
            for row, part, ref in shares[half]:
                spread = mm(lines[:, begin : begin + part].astype(LOW), ref[...])
                line = colsum(jnp.where(own_lanes(part), spread, 0.0))
                for i in range(part * n // width):
                    table[b, row + i : row + i + 1, :] = line[:, width * i : width * (i + 1)]
                begin += part

    def table_out(b):
        for half in range(2):
            parts, begin = [], 0
            for row, part, ref in shares[half]:
                count = part * n // width
                line = jnp.concatenate([gtable[b, row + i : row + i + 1, :] for i in range(count)], axis=1)
                parts.append(mm_right(jnp.where(own_lanes(part), line, 0.0).astype(LOW), ref[...]))
                begin += part
            parts.append(jnp.zeros((n, width - begin), F32))
            lines = jnp.concatenate(parts, axis=1)
            for j in range(n):
                s_t[b, half, place(half, j)] = lines[j : j + 1]

    def pack_own():
        for half in range(2):
            vectors = ((v_g1, v_s1, v_bo, v_g2, v_s2, v_bd, v_qv), (v_up,))[half]
            lines = [vector[...].astype(F32) for vector in vectors]
            lines.append(jnp.zeros((1, width - sum(line.shape[1] for line in lines)), F32))
            pack_t[half] = jnp.concatenate(lines, axis=1)
            for ref in (pack_a, pack_u):
                both = []
                for part in (2 * half, 2 * half + 1):
                    if ref is pack_u:
                        both.append(a_up[0, :, part * width : (part + 1) * width])
                    elif part == 3:
                        both.append(a_out[0])
                    else:
                        both.append(a_qkv[0, :, part * width : (part + 1) * width])
                ref[half] = jnp.concatenate([value.astype(F32) for value in both], axis=0).astype(LOW)
            pack_d[half] = a_down[0, 2 * unit * half : 2 * unit * (half + 1), :]

    def at(b, g):
        return len(groups) * b + g

    def ag1_copy(b, g, half, t):
        device = {"section": half, **peer_first(t)} if t else sibling
        return remote(
            pack[g].at[half], stage[g].at[b, half, pos_of[half]],
            ag1_s.at[g, half, t], ag1_r.at[at(b, g), t], device,
        )

    def ag1_landing(b, g, t):
        ref = stage[g].at[b, core, (dig_three * rest + dig_two) * first + (dig_a + first - t) % first]
        return remote(ref, ref, ag1_s.at[g, 0, t], ag1_r.at[at(b, g), t], sibling)

    def ag2_copy(b, g, t):
        ref = stage[g].at[b, core, slab_two(dig_three, dig_two)]
        return remote(ref, ref, ag2_s.at[at(b, g), t - 1], ag2_r.at[at(b, g), t - 1], peer_two(t))

    def ag3_copy(b, g, t):
        ref = stage[g].at[b, core, slab_three(dig_three)]
        return remote(ref, ref, ag3_s.at[at(b, g), t - 1], ag3_r.at[at(b, g), t - 1], peer_three(t))

    def ag4_copy(b, g, t):
        ref = stage[g].at[b, core, slab_three((dig_three + rest - t) % rest)]
        return remote(ref, ref, ag4_s.at[at(b, g), t], ag4_r.at[at(b, g), t], sibling)

    def ag4_landing(b, g, t):
        ref = stage[g].at[b, 1 - core, slab_three((dig_two + rest - t) % rest)]
        return remote(ref, ref, ag4_s.at[at(b, g), t], ag4_r.at[at(b, g), t], sibling)

    def ag1(b, g):
        @pl.when(core == b)
        def _():
            for t in range(1, first):
                for half in range(2):
                    ag1_copy(b, g, half, t).start()
            ag1_copy(b, g, 1 - b, 0).start()
            stage[g][b, b, pos] = pack[g][b]

    def ag2(b, g):
        for t in range(1, first):
            ag1_landing(b, g, t).wait_recv()

        @pl.when(core != b)
        def _():
            ag1_landing(b, g, 0).wait_recv()

        for t in range(1, rest):
            ag2_copy(b, g, t).start()

    def ag3(b, g):
        for t in range(1, rest):
            ag2_copy(b, g, t).wait_recv()
        for t in range(1, rest):
            ag3_copy(b, g, t).start()
        ag4_copy(b, g, 0).start()

    def ag4(b, g):
        for t in range(1, rest):
            ag3_copy(b, g, t).wait_recv()
            ag4_copy(b, g, t).start()

    def ag5(b, g):
        for t in range(rest):
            ag4_landing(b, g, t).wait_recv()
        lay_out(b, g)

    def ag_sent(b, g):
        @pl.when(core == b)
        def _():
            for t in range(1, first):
                for half in range(2):
                    ag1_copy(b, g, half, t).wait_send()
            ag1_copy(b, g, 1 - b, 0).wait_send()

        for t in range(1, rest):
            ag2_copy(b, g, t).wait_send()
            ag3_copy(b, g, t).wait_send()
        for t in range(rest):
            ag4_copy(b, g, t).wait_send()

    def lay_out(b, g):
        if g == TAB:
            table_in(b)
            return
        if g == DOWN:
            for j in range(n):
                for half in range(2):
                    begin = 4 * unit * j + 2 * unit * half
                    wdown[b, begin : begin + 2 * unit, :] = s_d[b, half, place(half, j)]
            return
        together = 16 // math.gcd(unit, 16)
        for half in range(2):
            for j in range(0, n, together):
                pieces = [stage[g][b, half, place(half, j + i)].astype(F32) for i in range(together)]
                for sub in range(2):
                    low = sub * unit
                    block = jnp.concatenate([piece[low : low + unit] for piece in pieces], axis=0).astype(LOW)
                    part = 2 * half + sub
                    down = slice(unit * j, unit * (j + together))
                    if g == UP:
                        wup[b, down, part * width : (part + 1) * width] = block
                    elif part == 3:
                        wout[b, down, :] = block
                    else:
                        wqkv[b, down, part * width : (part + 1) * width] = block

    def rs0_copy(b, g):
        return remote(stage[g].at[b, 1 - core], r0[g], rs0_s.at[at(b, g)], rs0_r.at[at(b, g)], sibling)

    def rs1_copy(b, g, t):
        return remote(
            stage[g].at[b, core, slab_three((dig_three + t) % rest)], r1[g].at[t - 1],
            rs1_s.at[at(b, g), t - 1], rs1_r.at[at(b, g), t - 1], peer_three(t),
        )

    def rs2_copy(b, g, t):
        return remote(
            stage[g].at[b, core, slab_two(dig_three, (dig_two + t) % rest)], r2[g].at[b, t - 1],
            rs2_s.at[at(b, g), t - 1], rs2_r.at[at(b, g), t - 1], peer_two(t),
        )

    def rs3_copy(b, g, t):
        there = (dig_three * rest + dig_two) * first + (dig_a + t) % first
        device = {"section": b, **peer_first(t)} if t else sibling
        return remote(
            stage[g].at[b, core, there], r3[g].at[core, t], rs3_s.at[at(b, g), t], rs3_r.at[g, core, t], device
        )

    def plane_copy(b, g, t):
        three, two = plane[t]
        return remote(
            stage[g].at[b, core, slab_two((dig_three + three) % rest, (dig_two + two) % rest)], r1[g].at[t],
            rs1_s.at[at(b, g), t], rs1_r.at[at(b, g), t], peer_plane(three, two),
        )

    def rs0(b, g):
        @pl.when(b == 0)
        def _():
            pl.semaphore_wait(credit.at[0, g], 1)

        rs0_copy(b, g).start()

    def rs1(b, g):
        rs0_copy(b, g).wait_recv()

        @pl.loop(0, n)
        def _(p):
            stage[g][b, core, p] = stage[g][b, core, p] + r0[g][p]

        @pl.when(b == 1)
        def _():
            pl.semaphore_signal(credit.at[0, g], inc=1, device_id=sibling, device_id_type=pl.DeviceIdType.MESH)

        direct = g in (ATT, TAB)
        if rest > 1:
            @pl.when(b == 0)
            def _():
                pl.semaphore_wait(credit.at[1, g], len(plane) if direct else rest - 1)

        if direct:
            for t in range(len(plane)):
                plane_copy(b, g, t).start()
            return
        for t in range(1, rest):
            rs1_copy(b, g, t).start()

    def rs2(b, g):
        for t in range(1, rest):
            rs1_copy(b, g, t).wait_recv()

        @pl.loop(0, rest * first)
        def _(p):
            here = dig_three * rest * first + p
            total = stage[g][b, core, here].astype(F32)
            for t in range(1, rest):
                total = total + r1[g][t - 1, p].astype(F32)
            stage[g][b, core, here] = total.astype(stage[g].dtype)

        for t in range(1, rest):
            @pl.when(b == 1)
            def _():
                pl.semaphore_signal(
                    credit.at[1, g], inc=1, device_id=peer_three(t), device_id_type=pl.DeviceIdType.MESH
                )

            rs2_copy(b, g, t).start()

    def rs3(b, g):
        direct = g in (ATT, TAB)
        copies = [plane_copy(b, g, t) for t in range(len(plane))] if direct else [
            rs2_copy(b, g, t) for t in range(1, rest)
        ]
        landing = r1[g] if direct else r2[g].at[b]
        for copy in copies:
            copy.wait_recv()

        @pl.loop(0, first)
        def _(p):
            here = (dig_three * rest + dig_two) * first + p
            total = stage[g][b, core, here].astype(F32)
            for t in range(len(copies)):
                total = total + landing[t, p].astype(F32)
            stage[g][b, core, here] = total.astype(stage[g].dtype)

        if direct:
            @pl.when(b == 1)
            def _():
                for three, two in plane:
                    pl.semaphore_signal(
                        credit.at[1, g], inc=1, device_id=peer_plane(three, two),
                        device_id_type=pl.DeviceIdType.MESH,
                    )


        for t in range(1, first):
            rs3_copy(b, g, t).start()

        @pl.when(core != b)
        def _():
            rs3_copy(b, g, 0).start()

    def rs4(b, g):
        @pl.when(core == b)
        def _():
            for own in (True, False):
                half = core if own else 1 - core
                begin = int(own)
                for t in range(begin, first):
                    ref = r3[g].at[half, t]
                    remote(ref, ref, rs3_s.at[at(b, g), t], rs3_r.at[g, half, t], sibling).wait_recv()
                total = stage[g][b, core, pos].astype(F32) if own else None
                for t in range(begin, first):
                    value = r3[g][half, t].astype(F32)
                    total = value if total is None else total + value
                final[g][half] = total

    def rs_sent(b, g):
        rs0_copy(b, g).wait_send()
        if g in (ATT, TAB):
            for t in range(len(plane)):
                plane_copy(b, g, t).wait_send()
        else:
            for t in range(1, rest):
                rs1_copy(b, g, t).wait_send()
                rs2_copy(b, g, t).wait_send()
        for t in range(1, first):
            rs3_copy(b, g, t).wait_send()

        @pl.when(core != b)
        def _():
            rs3_copy(b, g, 0).wait_send()

    def rows_of(i, images_too=1):
        return pl.ds(pl.multiple_of(i * rows, 16), images_too * rows)

    few = TOGETHER if slots % TOGETHER == 0 else 1
    many = TOGETHER_ROWS if slots % TOGETHER_ROWS == 0 else 1

    def step_rows(i, count):
        return rows_of(i * count, count)

    def ship_parts(kind, b, i):
        src, out = ((io_one, act_out), (io_two, ing_out))[kind]
        q = 2 * kind + b
        near = pltpu.make_async_copy(src.at[i], out.at[core, i], ship_s.at[q, i])
        far = remote(src.at[i], out.at[core, i], ship_s.at[q, i], ship_r.at[q, i], sibling)
        return near, far

    def ship(kind, b, i):
        near, far = ship_parts(kind, b, i)

        @pl.when(core == b)
        def _():
            near.start()

        @pl.when(core != b)
        def _():
            far.start()

    def shipped(kind, b, i):
        near, far = ship_parts(kind, b, i)

        @pl.when(core == b)
        def _():
            near.wait()

        @pl.when(core != b)
        def _():
            far.wait_send()

    def landed(kind, b, i):
        out = (act_out, ing_out)[kind]
        q = 2 * kind + b
        ref = out.at[1 - core, i]

        @pl.when(core == b)
        def _():
            remote(ref, ref, ship_s.at[q, i], ship_r.at[q, i], sibling).wait_recv()

    def live(i):
        return jnp.where(i < counts[0, core], 1.0, 0.0).astype(F32)

    def only_live(i, value, count):
        parts = [value[rows * m : rows * (m + 1)] * live(i * count + m) for m in range(count)]
        return jnp.concatenate(parts, axis=0)

    def coming(which, i):
        slot = (which * slots + i) % raw.shape[0]
        return pltpu.make_async_copy((images, cotangent)[which].at[i], raw.at[slot], in_s.at[which, i])

    def take_in(which, i):
        coming(which, i).wait()
        both = raw[(which * slots + i) % raw.shape[0]].astype(F32)
        (io_one, io_two)[which][i] = jnp.where(core == 0, both[:, 0, :], both[:, 1, :]).astype(LOW)

    def far_copy(which, i, back):
        near, far = ((hid, hid_far), (slope, slope_far))[which]
        near, far = near.at[rows_of(i)], far.at[rows_of(i)]
        src, dst = (far, near) if back else (near, far)
        return pltpu.make_async_copy(src, dst, far_s.at[2 * int(back) + which, i])

    pairs = width // 128
    scale = head_dim ** -0.5
    lane = lax.broadcasted_iota(jnp.int32, (1, 128), 1)
    half_low = [(lane < head_dim).astype(LOW), (lane >= head_dim).astype(LOW)]
    half_f = [(lane < head_dim).astype(F32), (lane >= head_dim).astype(F32)]
    token = lax.broadcasted_iota(jnp.int32, (rows, 128), 0) < length
    half_valid = [jnp.where(token, half_f[j], 0.0).astype(LOW) for j in range(2)]
    valid_lanes = jnp.where(lax.broadcasted_iota(jnp.int32, (1, rows), 1) < length, 1.0, 0.0).astype(F32)
    spare = -rows % 128
    chunk = 2 * width
    chunks = ff // chunk

    def vec(s, r):
        return table[s, r : r + 1, :]

    def up_bias(s, c):
        begin = c * chunk
        row, col = begin // width, begin % width
        if col + chunk <= width:
            return table[s, BU + row : BU + row + 1, col : col + chunk]
        a = table[s, BU + row : BU + row + 1, col:width]
        b = table[s, BU + row + 1 : BU + row + 2, 0 : chunk - (width - col)]
        return jnp.concatenate([a, b], axis=1)

    def add_vec(s, r, value):
        gtable[s, r : r + 1, :] += value

    def add_up_bias(s, c, value):
        begin = c * chunk
        row, col = begin // width, begin % width
        if col + chunk <= width:
            gtable[s, BU + row : BU + row + 1, col : col + chunk] += value
        else:
            cut = width - col
            gtable[s, BU + row : BU + row + 1, col:width] += value[:, :cut]
            gtable[s, BU + row + 1 : BU + row + 2, 0 : chunk - cut] += value[:, cut:]

    def attn_forward(s, x, hat, i):
        rd = step_rows(i, few)
        nrm_ref, qkv_ref, prob_ref, ctx_ref = nrm1.at[s], qkv.at[s], prob.at[s], ctx.at[s]
        nrm = (hat * vec(s, G1) + vec(s, S1)).astype(LOW)
        nrm_ref[rd, :] = nrm
        mixed = mm(nrm, wqkv[s])
        q = (mixed[:, 0:width] + vec(s, BQ)).astype(LOW)
        k = mixed[:, width : 2 * width].astype(LOW)
        v = (mixed[:, 2 * width :] + vec(s, BV)).astype(LOW)
        qkv_ref[rd, 0:width] = q
        qkv_ref[rd, width : 2 * width] = k
        qkv_ref[rd, 2 * width :] = v
        images_out = []
        for m in range(few):
            mine = slice(rows * m, rows * (m + 1))
            parts = []
            for p in range(pairs):
                cols = slice(128 * p, 128 * p + 128)
                weights, sides = [], []
                for j in range(2):
                    keys = k[mine, cols] * half_low[j]
                    keys = jnp.concatenate([keys, keys[rows - spare :]], axis=0)
                    scores = mm_right(q[mine, cols], keys)
                    top = jnp.max(scores, axis=-1, keepdims=True)
                    e = jnp.exp2((scores - top) * (scale * 1.4426950408889634)).astype(LOW)
                    prob_ref[i * few + m, 2 * p + j] = e[:, :rows]
                    weights.append(e)
                    sides.append(jnp.concatenate([v[mine, cols] * half_valid[j], half_valid[j]], axis=1))
                    sides.append(jnp.zeros((spare, 256), LOW))
                total = mm(jnp.concatenate(weights, axis=1), jnp.concatenate(sides, axis=0))
                over = 1.0 / total[:, 128:]
                overs[s, rows_of(i * few + m), cols] = over.astype(LOW)
                parts.append((total[:, :128] * over).astype(LOW))
            images_out.append(jnp.concatenate(parts, axis=1))
        context = jnp.concatenate(images_out, axis=0)
        ctx_ref[rd, :] = context
        return x + mm(context, wout[s]) + vec(s, BO)

    def ff_forward(s, after, rd):
        hat, rstd, _ = normalize(after)
        hat2[s, rd, :] = hat.astype(LOW)
        nrm = (hat * vec(s, G2) + vec(s, S2)).astype(LOW)
        total = after + vec(s, BD)
        for c in range(chunks):
            cols = slice(chunk * c, chunk * c + chunk)
            pre = mm(nrm, wup[s, :, cols]) + up_bias(s, c)
            phi, slo = normal_parts(pre)
            h = (pre * phi).astype(LOW)
            hid[rd, cols] = h
            slope[rd, cols] = slo.astype(LOW)
            total = total + mm(h, wdown[s, cols, :])
        return total, rstd

    def ff_backward(s, g, rd, rstd):
        g_low = g.astype(LOW)
        add_vec(s, BD, colsum(g_low.astype(F32)))
        d_nrm = None
        for c in range(chunks):
            cols = slice(chunk * c, chunk * c + chunk)
            d_hid = mm_right(g_low, wdown[s, cols, :])
            d_pre = (d_hid * slope[rd, cols].astype(F32)).astype(LOW)
            slope[rd, cols] = d_pre
            add_up_bias(s, c, colsum(d_pre.astype(F32)))
            part = mm_right(d_pre, wup[s, :, cols])
            d_nrm = part if d_nrm is None else d_nrm + part
        hat = hat2[s, rd, :].astype(F32)
        add_vec(s, G2, colsum(d_nrm * hat))
        add_vec(s, S2, colsum(d_nrm))
        d_after = g + normalize_back(d_nrm * vec(s, G2), hat, rstd)
        low = d_after.astype(LOW)
        dal[rd, :] = low
        add_vec(s, BO, colsum(low.astype(F32)))
        return d_after

    def attn_backward(s, i):
        qkv_ref, prob_ref, ctx_ref = qkv.at[s], prob.at[s], ctx.at[s]
        rd = step_rows(i, few)
        d_context = mm_right(dal[rd, :], wout[s])
        d_context = (d_context * overs[s, rd, :].astype(F32)).astype(LOW)
        for m in range(few):
            rd = rows_of(i * few + m)
            d_ctx = d_context[rows * m : rows * (m + 1)]
            dq, dk, dv = [], [], []
            for p in range(pairs):
                cols = slice(128 * p, 128 * p + 128)
                q = qkv_ref[rd, 128 * p : 128 * p + 128]
                k = qkv_ref[rd, width + 128 * p : width + 128 * p + 128]
                v = qkv_ref[rd, 2 * width + 128 * p : 2 * width + 128 * p + 128]
                dc = d_ctx[:, cols]
                both = dc.astype(F32) * ctx_ref[rd, cols].astype(F32)
                q_t, dc_t = q.T, dc.T
                to_q, to_k, to_v = None, [], []
                for j in range(2):
                    e = prob_ref[i * few + m, 2 * p + j]
                    delta = jnp.sum(both * half_f[j], axis=-1, keepdims=True)
                    d_prob = mm_right(dc, v * half_low[j])
                    ds = (e.astype(F32) * (d_prob - delta)).astype(LOW)
                    part = mm(ds, k * half_valid[j])
                    to_q = part if to_q is None else to_q + part
                    head = slice(head_dim * j, head_dim * (j + 1))
                    to_k.append(mm(q_t[head], ds))
                    to_v.append(mm(dc_t[head], e))
                dq.append((to_q * scale).astype(LOW))
                dk.append((jnp.concatenate(to_k, axis=0) * (valid_lanes * scale)).astype(LOW).T)
                dv.append((jnp.concatenate(to_v, axis=0) * valid_lanes).astype(LOW).T)
            d_mixed = jnp.concatenate(dq + dk + dv, axis=1)
            qkv_ref[rd, :] = d_mixed
            add_vec(s, BQ, colsum(d_mixed[:, 0:width].astype(F32)))
            add_vec(s, BV, colsum(d_mixed[:, 2 * width :].astype(F32)))

    def input_backward(s, d_after, rd, x, mean, rstd):
        d_nrm = mm_right(qkv[s, rd, :], wqkv[s])
        hat = (x - mean) * rstd
        add_vec(s, G1, colsum(d_nrm * hat))
        add_vec(s, S1, colsum(d_nrm))
        return d_after + normalize_back(d_nrm * vec(s, G1), hat, rstd)

    def grads_down(s):
        left_t[...] = low_g[...].T

        @pl.loop(0, 2)
        def _(c):
            cols = pl.ds(pl.multiple_of(c * 2 * width, 128), 2 * width)
            block = mm(left_t[...], hid[:, cols]).T
            for i in range(n // 2):
                for half in range(2):
                    begin = 4 * unit * i + 2 * unit * half
                    s_d[s, half, place(half, c * (n // 2) + i)] = block[begin : begin + 2 * unit].astype(LOW)

    def pair_out(ref, s, half, one, two):
        for j in range(n):
            down = slice(unit * j, unit * (j + 1))
            piece = jnp.concatenate([one[down], two[down]], axis=0).astype(LOW)
            ref[s, half, place(half, j)] = piece

    def grads_up(s):
        left_t[...] = (hat2[s].astype(F32) * vec(s, G2) + vec(s, S2)).astype(LOW).T
        for half in range(2):
            both = mm(left_t[...], slope[:, 2 * half * width : 2 * (half + 1) * width])
            pair_out(s_u, s, half, both[:, :width], both[:, width:])

    def grads_attn(s):
        mix_s = qkv.at[s]
        left_t[...] = ctx[s].T
        four = mm(left_t[...], dal[...])
        left_t[...] = nrm1[s].T
        three = mm(left_t[...], mix_s[:, 2 * width :])
        pair_out(s_a, s, 1, three, four)
        both = mm(left_t[...], mix_s[:, 0 : 2 * width])
        pair_out(s_a, s, 0, both[:, :width], both[:, width:])

    barrier = pltpu.get_barrier_semaphore()
    greeted = [sibling]
    greeted += [{"section": half, **peer_first(t)} for t in range(1, first) for half in range(2)]
    greeted += [peer_plane(three, two) for three, two in plane]
    for device in greeted:
        pl.semaphore_signal(barrier, inc=1, device_id=device, device_id_type=pl.DeviceIdType.MESH)
    pack_own()
    pl.semaphore_wait(barrier, len(greeted))

    def run(*todo):
        for f, b, g in todo:
            f(b, g)

    def events(i, table_of):
        for when, todo in table_of.items():
            @pl.when(i == when)
            def _():
                run(*todo)

    def both(f, b, g):
        return [(f, b, g), (f, b, TAB)]

    def take(i, m):
        return pl.ds(pl.multiple_of((i * many + m) * rows, 16), length)

    ahead = raw.shape[0]
    run(*both(ag1, 0, ATT))
    for i in range(ahead):
        coming(0, i).start()
    fill_repeats()
    gtable[...] = jnp.zeros_like(gtable)
    low_g[...] = jnp.zeros_like(low_g)
    xs[0] = jnp.zeros_like(low_g)

    @pl.loop(0, slots)
    def images_in(i):
        take_in(0, i)

        @pl.when(i + ahead < slots)
        def _():
            coming(0, i + ahead).start()

        @pl.when(i + ahead >= slots)
        def _():
            coming(1, i + ahead - slots).start()

        @pl.when(i == 3)
        def _():
            run(*both(ag2, 0, ATT), (ag1, 0, UP), (ag1, 0, DOWN))

    def statistic(s, rd, which):
        return jnp.where(s == 0, rstds[rd, which : which + 1], rstds[rd, 3 + which : 4 + which])

    def first_norm(s, rd, x):
        hat, rstd, mean = normalize(x)
        after_ref[rd, :] = hat
        rstds[rd, 3 * s : 3 * s + 1] = rstd
        rstds[rd, 3 * s + 2 : 3 * s + 3] = mean

    @pl.loop(0, slots // many)
    def norm_one(i):
        for m in range(many):
            xs[0, take(i, m), :] = io_one[i * many + m]
        rd = step_rows(i, many)
        x = xs[0, rd, :].astype(F32)
        token_rows = lax.broadcasted_iota(jnp.int32, (rows, width), 0) < length
        parts = [x[rows * m : rows * (m + 1)] for m in range(many)]
        x = jnp.concatenate([jnp.where(token_rows, part, part[0:1]) for part in parts], axis=0)
        xs[0, rd, :] = x.astype(LOW)
        first_norm(0, rd, x)

    run(*both(ag3, 0, ATT), (ag2, 0, UP), *both(ag1, 1, ATT), (ag2, 0, DOWN), (ag1, 1, UP), (ag1, 1, DOWN))

    @pl.loop(0, slots)
    def cotangents_in(i):
        take_in(1, i)

        @pl.when(i + ahead < slots)
        def _():
            coming(1, i + ahead).start()

    run(*both(ag4, 0, ATT), (ag3, 0, UP), *both(ag5, 0, ATT))

    @pl.loop(0, 2)
    def forward(s):
        @pl.loop(0, slots // few)
        def attention(i):
            @pl.when(s == 0)
            def _():
                events(i, {
                    0: [(ag3, 0, DOWN), *both(ag2, 1, ATT)],
                    1: [(ag4, 0, UP), (ag2, 1, UP)],
                    2: [(ag4, 0, DOWN)],
                })

            @pl.when(s == 1)
            def _():
                events(i, {2: [(ag4, 1, DOWN)]})

            rd = step_rows(i, few)
            after_ref[rd, :] = attn_forward(s, xs[s, rd, :].astype(F32), after_ref[rd, :], i)

        @pl.when(s == 0)
        def _():
            run(*both(ag3, 1, ATT), (ag5, 0, UP), (ag5, 0, DOWN))

        @pl.when(s == 1)
        def _():
            run((ag5, 1, UP), (ag5, 1, DOWN))

        @pl.loop(0, slots // many)
        def feed_forward(i):
            @pl.when(s == 0)
            def _():
                events(i, {0: [(ag3, 1, UP), (ag2, 1, DOWN)], 1: both(ag4, 1, ATT)})

            rd = step_rows(i, many)

            @pl.when(s == 1)
            def _():
                for m in range(many):
                    far_copy(0, i * many + m, False).wait()
                    far_copy(1, i * many + m, False).wait()
                    shipped(0, 0, i * many + m)

            out, rstd2 = ff_forward(s, after_ref[rd, :], rd)
            for block in range(2):
                @pl.when(s == block)
                def _():
                    rstds[rd, 3 * block + 1 : 3 * block + 2] = rstd2

            out = only_live(i, out, many)
            for m in range(many):
                io_one[i * many + m] = out[rows * m : rows * m + length].astype(LOW)
                ship(0, s, i * many + m)

            @pl.when(s == 0)
            def _():
                for m in range(many):
                    far_copy(0, i * many + m, False).start()
                    far_copy(1, i * many + m, False).start()
                low = out.astype(LOW)
                xs[1, rd, :] = low
                first_norm(1, rd, low.astype(F32))

        @pl.when(s == 0)
        def _():
            run((ag4, 1, UP), (ag3, 1, DOWN), *both(ag5, 1, ATT))

    for b in range(2):
        for g in groups:
            ag_sent(b, g)

    @pl.loop(0, 2)
    def backward(turn):
        s = 1 - turn

        @pl.loop(0, slots // many)
        def feed_forward(i):
            @pl.when(s == 0)
            def _():
                events(i, {1: [(rs1, 1, TAB), (rs4, 1, UP)]})
                for m in range(many):
                    far_copy(1, i * many + m, True).wait()

            rd = step_rows(i, many)
            for m in range(many):
                g = live(i * many + m) * io_two[i * many + m].astype(F32)
                low_g[take(i, m), :] = g.astype(LOW)
            after_ref[rd, :] = ff_backward(s, low_g[rd, :].astype(F32), rd, statistic(s, rd, 1))

        @pl.when(s == 0)
        def _():
            for i in range(slots):
                far_copy(0, i, True).wait()
            run((rs3, 1, ATT))

        grads_down(s)
        run((rs0, s, DOWN))

        @pl.when(s == 1)
        def _():
            for i in range(slots):
                far_copy(0, i, True).start()

        grads_up(s)
        run((rs0, s, UP), (rs1, s, DOWN))

        @pl.when(s == 1)
        def _():
            for i in range(slots):
                far_copy(1, i, True).start()

        @pl.when(s == 0)
        def _():
            run((rs3, 1, TAB))

        @pl.loop(0, slots // few)
        def attention(i):
            events(i, {1: [(rs1, s, UP), (rs2, s, DOWN)], 2: [(rs2, s, UP), (rs3, s, DOWN)]})

            @pl.when(s == 0)
            def _():
                events(i, {1: both(rs4, 1, ATT)})

            attn_backward(s, i)

        grads_attn(s)
        run((rs0, s, ATT), (rs3, s, UP))

        @pl.loop(0, slots // many)
        def to_input(i):
            events(i, {1: [(rs1, s, ATT), (rs4, s, DOWN)]})
            rd = step_rows(i, many)
            x = xs[s, rd, :].astype(F32)
            d_in = input_backward(s, after_ref[rd, :], rd, x, statistic(s, rd, 2), statistic(s, rd, 0))
            for m in range(many):
                @pl.when(s == 0)
                def _():
                    shipped(1, 1, i * many + m)

                io_two[i * many + m] = d_in[rows * m : rows * m + length].astype(LOW)
                ship(1, s, i * many + m)

        table_out(s)
        run((rs0, s, TAB))

    run((rs4, 0, UP), (rs1, 0, TAB), (rs3, 0, ATT), (rs3, 0, TAB))

    @pl.loop(0, slots)
    def all_out(i):
        shipped(0, 1, i)
        shipped(1, 0, i)
        for kind in range(2):
            for b in range(2):
                landed(kind, b, i)

    run(*both(rs4, 0, ATT))
    for b in range(2):
        for g in groups:
            rs_sent(b, g)


def output_kernel(
    f_a, f_u, f_d, f_t, o_g1, o_s1, o_qkv, o_qv, o_out, o_bo, o_g2, o_s2, o_up, o_bu, o_down, o_bd
):
    unit, width = o_out.shape[1:]
    for half in range(2):
        o_down[0, 2 * unit * half : 2 * unit * (half + 1), :] = f_d[half]
        for sub in range(2):
            part = 2 * half + sub
            cols = slice(part * width, (part + 1) * width)
            o_up[0, :, cols] = f_u[half, unit * sub : unit * (sub + 1), :]
            piece = f_a[half, unit * sub : unit * (sub + 1), :]
            if part == 3:
                o_out[0] = piece
            else:
                o_qkv[0, :, cols] = piece
    begin = 0
    for out in (o_g1, o_s1, o_bo, o_g2, o_s2, o_bd, o_qv):
        part = out.shape[1]
        out[...] = f_t[0, :, begin : begin + part]
        begin += part
    o_bu[...] = f_t[1, :, 0 : o_bu.shape[1]]


def local(
    images, cotangent, counts,
    ln1_gain, ln1_bias, w_qkv, b_qv, w_out, b_out, ln2_gain, ln2_bias, w_up, b_up, w_down, b_down,
):
    micro_count, slots, length, width = images.shape
    ff = w_up.shape[2]
    rows = -(-length // 16) * 16
    n = lax.axis_size("fsdp")
    unit = width // n
    first, rest = radices(n)
    total = slots * rows
    head_dim = width // HEADS

    def vm(*shape, kind=LOW):
        return pltpu.VMEM(shape, kind)

    tall = [(2 * unit, LOW)] * 3 + [(1, F32)]
    dma = lambda *shape: pltpu.SemaphoreType.DMA(shape)
    outs = [((2, slots, length, width), LOW), ((2, slots, length, width), LOW)]
    outs += [((2, r, width), F32) for r, _ in tall] + [((total, ff), LOW), ((total, ff), LOW)]
    scratch = [
        vm(2, total, width), vm(3, length, 2, width), vm(slots, length, width), vm(slots, length, width),
        *[vm(2, r, width, kind=kind) for r, kind in tall],
        vm(2, width, 3 * width), vm(2, width, width), vm(2, width, ff), vm(2, ff, width),
        vm(2, TABLE, width, kind=F32), vm(2, TABLE, width, kind=F32),
        vm(unit, width), vm(2 * unit, 2 * width), vm(4 * unit, 4 * width),
        vm(total, width, kind=F32), vm(2, total, width), vm(2, total, 3 * width), vm(2, slots, HEADS, rows, rows),
        vm(2, total, width),
        vm(2, total, width), vm(2, total, width), vm(total, 6, kind=F32),
        vm(total, ff), vm(total, ff), vm(total, width), vm(total, width), vm(width, total),
    ]
    scratch += [vm(2, 2, n, r, width, kind=kind) for r, kind in tall]
    scratch += [vm(n, r, width, kind=kind) for r, kind in tall]
    plane = rest * rest - 1
    for g, (r, kind) in enumerate(tall):
        direct = g in (ATT, TAB)
        scratch.append(vm(*((plane, first) if direct else (rest - 1, rest * first)), r, width, kind=kind))
    scratch += [vm(2, rest - 1, first, *tall[g][:1], width) for g in (UP, DOWN)]
    scratch += [vm(2, first, r, width, kind=kind) for r, kind in tall]
    scratch += [dma(2, slots), dma(4, slots), dma(4, slots), dma(4, slots)]
    scratch += [dma(4, 2, first), dma(8, first)] + [dma(8, rest - 1)] * 4 + [dma(8, rest)] * 2
    scratch += [dma(8)] * 2 + [dma(8, plane)] * 2 + [dma(8, rest - 1)] * 2 + [dma(8, first), dma(4, 2, first)]
    scratch += [pltpu.SemaphoreType.REGULAR((2, 4))]
    dims = (slots, length, rows, width, ff, head_dim, n)
    vmem = pl.BlockSpec(memory_space=pltpu.VMEM)
    hbm = pl.BlockSpec(memory_space=pltpu.HBM)
    acts, ings, f_a, f_u, f_d, f_t, _, _ = pl.pallas_call(
        functools.partial(whole_kernel, dims),
        out_shape=[jax.ShapeDtypeStruct(*o) for o in outs],
        in_specs=[hbm, hbm, pl.BlockSpec(memory_space=pltpu.SMEM)] + [vmem] * 12,
        out_specs=[hbm, hbm] + [vmem] * 4 + [hbm, hbm],
        scratch_shapes=scratch,
        compiler_params=pltpu.CompilerParams(
            vmem_limit_bytes=(64 << 20) - (96 << 10), collective_id=0, has_side_effects=True
        ),
    )(
        images.transpose(1, 2, 0, 3), cotangent.transpose(1, 2, 0, 3), counts.T, ln1_gain, ln1_bias, b_out, ln2_gain, ln2_bias, b_down, b_qv, b_up,
        w_qkv, w_out, w_up, w_down,
    )

    params = (
        ln1_gain, ln1_bias, w_qkv, b_qv, w_out, b_out, ln2_gain, ln2_bias, w_up, b_up, w_down, b_down
    )
    grads = pl.pallas_call(
        output_kernel,
        out_shape=[jax.ShapeDtypeStruct(p.shape, F32) for p in params],
        in_specs=[vmem] * 4,
        out_specs=[vmem] * len(params),
    )(f_a, f_u, f_d, f_t)

    return (acts[None], ings[None], *grads)


def solution(mesh):
    split = P("section", "fsdp")
    cube = P("section", "fsdp", None)
    image = P(None, "fsdp", None, None)
    result = P("section", None, "fsdp", None, None)
    params = (split, split, cube, split, cube, split, split, split, cube, split, cube, split)
    return jax.shard_map(
        local,
        mesh=mesh,
        in_specs=(image, image, P(None, "fsdp")) + params,
        out_specs=(result, result) + params,
        check_vma=False,
    )
```

```python
import functools
import math

import jax
import jax.numpy as jnp
from jax import lax
from jax.experimental import pallas as pl
from jax.experimental.pallas import tpu as pltpu
from jax.sharding import PartitionSpec as P

HEADS = 6
EPS = 1e-06
F32 = jnp.float32
LOW = jnp.bfloat16

G1, S1, BO, G2, S2, BD, BQ, BV, BU = 0, 1, 2, 3, 4, 5, 6, 7, 8
TABLE = 16
TOGETHER, TOGETHER_ROWS = 2, 3
ATT, UP, DOWN, TAB = 0, 1, 2, 3


def radices(n):
    rest = max(r for r in range(1, n + 1) if r * r * r <= n and n % (r * r) == 0)
    return n // (rest * rest), rest


def mm(left, right):
    return jnp.dot(left, right, preferred_element_type=F32)


def mm_right(left, right):
    return lax.dot_general(left, right, (((1,), (1,)), ((), ())), preferred_element_type=F32)


def mm_left(left, right):
    return lax.dot_general(left, right, (((0,), (0,)), ((), ())), preferred_element_type=F32)


def normal_parts(pre):
    phi = 0.5 + 0.5 * lax.erf(pre * 0.7071067811865476)
    density = jnp.exp2(pre * pre * (-0.5 * 1.4426950408889634)) * 0.3989422804014327
    return phi, phi + pre * density


def normalize(value):
    mean = jnp.mean(value, axis=-1, keepdims=True)
    center = value - mean
    rstd = lax.rsqrt(jnp.mean(center * center, axis=-1, keepdims=True) + EPS)
    return center * rstd, rstd, mean


def normalize_back(d_hat, hat, rstd):
    mean_one = jnp.mean(d_hat, axis=-1, keepdims=True)
    mean_two = jnp.mean(d_hat * hat, axis=-1, keepdims=True)
    return rstd * (d_hat - mean_one - hat * mean_two)


def colsum(value):
    return jnp.sum(value, axis=0, keepdims=True)


def whole_kernel(dims, *refs):
    slots, length, rows, width, ff, head_dim, n = dims
    (
        images, cotangent, counts, v_g1, v_s1, v_bo, v_g2, v_s2, v_bd, v_qv, v_up, a_qkv, a_out, a_up, a_down,
        act_fin, ing_fin, f_a, f_u, f_d, f_t, hid_far, slope_far, act_out, ing_out,
        xs, raw, io_one, io_two, pack_a, pack_u, pack_d, pack_t,
        wqkv, wout, wup, wdown, table, gtable, rep_one, rep_two, rep_four,
        after_ref, nrm1, qkv, prob, overs, ctx, hat2, rstds, hid, slope, dal, low_g, left_t,
        s_a, s_u, s_d, s_t, r0_a, r0_u, r0_d, r0_t, r1_a, r1_u, r1_d, r1_t, r2_u, r2_d,
        r3_a, r3_u, r3_d, r3_t,
        in_s, weave_in, weave_out, ship_s, ship_r, far_s, ag1_s, ag1_r, ag2_s, ag2_r, ag3_s, ag3_r, ag4_s, ag4_r,
        rs0_s, rs0_r, rs1_s, rs1_r, rs2_s, rs2_r, rs3_s, rs3_r, credit,
    ) = refs
    groups = (ATT, UP, DOWN, TAB)
    pack = (pack_a, pack_u, pack_d, pack_t)
    stage = (s_a, s_u, s_d, s_t)
    r0, r1, r2 = (r0_a, r0_u, r0_d, r0_t), (r1_a, r1_u, r1_d, r1_t), (None, r2_u, r2_d, None)
    r3, final = (r3_a, r3_u, r3_d, r3_t), (f_a, f_u, f_d, f_t)

    first, rest = radices(n)
    unit = width // n
    core = lax.axis_index("section")
    me = lax.axis_index("fsdp")
    dig_a, dig_b, dig_c = me // (rest * rest), (me // rest) % rest, me % rest
    dig_three, dig_two = dig_c + core * (dig_b - dig_c), dig_b + core * (dig_c - dig_b)
    step_three, step_two = 1 + core * (rest - 1), rest - core * (rest - 1)
    pos = (dig_three * rest + dig_two) * first + dig_a
    pos_of = ((dig_c * rest + dig_b) * first + dig_a, (dig_b * rest + dig_c) * first + dig_a)
    sibling = {"section": 1 - core}

    def place(half, j):
        a, b, c = j // (rest * rest), (j // rest) % rest, j % rest
        return ((c * rest + b) if half == 0 else (b * rest + c)) * first + a

    def peer_first(t):
        return {"fsdp": me + ((dig_a + t) % first - dig_a) * (rest * rest)}

    def peer_two(t):
        return {"fsdp": me + ((dig_two + t) % rest - dig_two) * step_two}

    def peer_three(t):
        return {"fsdp": me + ((dig_three + t) % rest - dig_three) * step_three}

    def peer_plane(three, two):
        here = ((dig_three + three) % rest - dig_three) * step_three
        return {"fsdp": me + here + ((dig_two + two) % rest - dig_two) * step_two}

    plane = [(three, two) for three in range(rest) for two in range(rest) if three or two]

    def remote(src, dst, s_sem, r_sem, device):
        return pltpu.make_async_remote_copy(
            src_ref=src, dst_ref=dst, send_sem=s_sem, recv_sem=r_sem, device_id=device,
            device_id_type=pl.DeviceIdType.MESH,
        )

    def slab_two(three, two):
        return pl.ds((three * rest + two) * first, first)

    def slab_three(three):
        return pl.ds(three * rest * first, rest * first)

    def fill_repeats():
        for ref in (rep_one, rep_two, rep_four):
            part = ref.shape[0]
            lanes = lax.broadcasted_iota(jnp.int32, ref.shape, 1).astype(F32)
            line = lax.broadcasted_iota(jnp.int32, ref.shape, 0).astype(F32)
            rest_of = lanes - part * jnp.floor((lanes + 0.5) * (1.0 / part))
            ref[...] = jnp.where(jnp.abs(rest_of - line) < 0.5, 1.0, 0.0).astype(LOW)

    def own_lanes(part):
        shape = (n, part * n)
        lanes = lax.broadcasted_iota(jnp.int32, shape, 1)
        begin = lax.broadcasted_iota(jnp.int32, shape, 0) * part
        return (lanes >= begin) & (lanes < begin + part)

    shares = (
        ((G1, unit, rep_one), (S1, unit, rep_one), (BO, unit, rep_one), (G2, unit, rep_one), (S2, unit, rep_one),
         (BD, unit, rep_one), (BQ, 2 * unit, rep_two)),
        ((BU, 4 * unit, rep_four),),
    )

    def table_in(b):
        for half in range(2):
            lines = jnp.concatenate([s_t[b, half, place(half, j)] for j in range(n)], axis=0)
            begin = 0
            for row, part, ref in shares[half]:
                spread = mm(lines[:, begin : begin + part].astype(LOW), ref[...])
                line = colsum(jnp.where(own_lanes(part), spread, 0.0))
                for i in range(part * n // width):
                    table[b, row + i : row + i + 1, :] = line[:, width * i : width * (i + 1)]
                begin += part

    def table_out(b):
        for half in range(2):
            parts, begin = [], 0
            for row, part, ref in shares[half]:
                count = part * n // width
                line = jnp.concatenate([gtable[b, row + i : row + i + 1, :] for i in range(count)], axis=1)
                parts.append(mm_right(jnp.where(own_lanes(part), line, 0.0).astype(LOW), ref[...]))
                begin += part
            parts.append(jnp.zeros((n, width - begin), F32))
            lines = jnp.concatenate(parts, axis=1)
            for j in range(n):
                s_t[b, half, place(half, j)] = lines[j : j + 1]

    def pack_own():
        for half in range(2):
            vectors = ((v_g1, v_s1, v_bo, v_g2, v_s2, v_bd, v_qv), (v_up,))[half]
            lines = [vector[...].astype(F32) for vector in vectors]
            lines.append(jnp.zeros((1, width - sum(line.shape[1] for line in lines)), F32))
            pack_t[half] = jnp.concatenate(lines, axis=1)
            for ref in (pack_a, pack_u):
                both = []
                for part in (2 * half, 2 * half + 1):
                    if ref is pack_u:
                        both.append(a_up[0, :, part * width : (part + 1) * width])
                    elif part == 3:
                        both.append(a_out[0])
                    else:
                        both.append(a_qkv[0, :, part * width : (part + 1) * width])
                ref[half] = jnp.concatenate([value.astype(F32) for value in both], axis=0).astype(LOW)
            pack_d[half] = a_down[0, 2 * unit * half : 2 * unit * (half + 1), :]

    def at(b, g):
        return len(groups) * b + g

    def ag1_copy(b, g, half, t):
        device = {"section": half, **peer_first(t)} if t else sibling
        return remote(
            pack[g].at[half], stage[g].at[b, half, pos_of[half]],
            ag1_s.at[g, half, t], ag1_r.at[at(b, g), t], device,
        )

    def ag1_landing(b, g, t):
        ref = stage[g].at[b, core, (dig_three * rest + dig_two) * first + (dig_a + first - t) % first]
        return remote(ref, ref, ag1_s.at[g, 0, t], ag1_r.at[at(b, g), t], sibling)

    def ag2_copy(b, g, t):
        ref = stage[g].at[b, core, slab_two(dig_three, dig_two)]
        return remote(ref, ref, ag2_s.at[at(b, g), t - 1], ag2_r.at[at(b, g), t - 1], peer_two(t))

    def ag3_copy(b, g, t):
        ref = stage[g].at[b, core, slab_three(dig_three)]
        return remote(ref, ref, ag3_s.at[at(b, g), t - 1], ag3_r.at[at(b, g), t - 1], peer_three(t))

    def ag4_copy(b, g, t):
        ref = stage[g].at[b, core, slab_three((dig_three + rest - t) % rest)]
        return remote(ref, ref, ag4_s.at[at(b, g), t], ag4_r.at[at(b, g), t], sibling)

    def ag4_landing(b, g, t):
        ref = stage[g].at[b, 1 - core, slab_three((dig_two + rest - t) % rest)]
        return remote(ref, ref, ag4_s.at[at(b, g), t], ag4_r.at[at(b, g), t], sibling)

    def ag1(b, g):
        @pl.when(core == b)
        def _():
            for t in range(1, first):
                for half in range(2):
                    ag1_copy(b, g, half, t).start()
            ag1_copy(b, g, 1 - b, 0).start()
            stage[g][b, b, pos] = pack[g][b]

    def ag2(b, g):
        for t in range(1, first):
            ag1_landing(b, g, t).wait_recv()

        @pl.when(core != b)
        def _():
            ag1_landing(b, g, 0).wait_recv()

        for t in range(1, rest):
            ag2_copy(b, g, t).start()

    def ag3(b, g):
        for t in range(1, rest):
            ag2_copy(b, g, t).wait_recv()
        for t in range(1, rest):
            ag3_copy(b, g, t).start()
        ag4_copy(b, g, 0).start()

    def ag4(b, g):
        for t in range(1, rest):
            ag3_copy(b, g, t).wait_recv()
            ag4_copy(b, g, t).start()

    def ag5(b, g):
        for t in range(rest):
            ag4_landing(b, g, t).wait_recv()
        lay_out(b, g)

    def ag_sent(b, g):
        @pl.when(core == b)
        def _():
            for t in range(1, first):
                for half in range(2):
                    ag1_copy(b, g, half, t).wait_send()
            ag1_copy(b, g, 1 - b, 0).wait_send()

        for t in range(1, rest):
            ag2_copy(b, g, t).wait_send()
            ag3_copy(b, g, t).wait_send()
        for t in range(rest):
            ag4_copy(b, g, t).wait_send()

    def lay_out(b, g):
        if g == TAB:
            table_in(b)
            return
        if g == DOWN:
            for j in range(n):
                for half in range(2):
                    begin = 4 * unit * j + 2 * unit * half
                    wdown[b, begin : begin + 2 * unit, :] = s_d[b, half, place(half, j)]
            return
        together = 16 // math.gcd(unit, 16)
        for half in range(2):
            for j in range(0, n, together):
                pieces = [stage[g][b, half, place(half, j + i)].astype(F32) for i in range(together)]
                for sub in range(2):
                    low = sub * unit
                    block = jnp.concatenate([piece[low : low + unit] for piece in pieces], axis=0).astype(LOW)
                    part = 2 * half + sub
                    down = slice(unit * j, unit * (j + together))
                    if g == UP:
                        wup[b, down, part * width : (part + 1) * width] = block
                    elif part == 3:
                        wout[b, down, :] = block
                    else:
                        wqkv[b, down, part * width : (part + 1) * width] = block

    def rs0_copy(b, g):
        return remote(stage[g].at[b, 1 - core], r0[g], rs0_s.at[at(b, g)], rs0_r.at[at(b, g)], sibling)

    def rs1_copy(b, g, t):
        return remote(
            stage[g].at[b, core, slab_three((dig_three + t) % rest)], r1[g].at[t - 1],
            rs1_s.at[at(b, g), t - 1], rs1_r.at[at(b, g), t - 1], peer_three(t),
        )

    def rs2_copy(b, g, t):
        return remote(
            stage[g].at[b, core, slab_two(dig_three, (dig_two + t) % rest)], r2[g].at[b, t - 1],
            rs2_s.at[at(b, g), t - 1], rs2_r.at[at(b, g), t - 1], peer_two(t),
        )

    def rs3_copy(b, g, t):
        there = (dig_three * rest + dig_two) * first + (dig_a + t) % first
        device = {"section": b, **peer_first(t)} if t else sibling
        return remote(
            stage[g].at[b, core, there], r3[g].at[core, t], rs3_s.at[at(b, g), t], rs3_r.at[g, core, t], device
        )

    def plane_copy(b, g, t):
        three, two = plane[t]
        return remote(
            stage[g].at[b, core, slab_two((dig_three + three) % rest, (dig_two + two) % rest)], r1[g].at[t],
            rs1_s.at[at(b, g), t], rs1_r.at[at(b, g), t], peer_plane(three, two),
        )

    def rs0(b, g):
        @pl.when(b == 0)
        def _():
            pl.semaphore_wait(credit.at[0, g], 1)

        rs0_copy(b, g).start()

    def rs1(b, g):
        rs0_copy(b, g).wait_recv()

        @pl.loop(0, n)
        def _(p):
            stage[g][b, core, p] = stage[g][b, core, p] + r0[g][p]

        @pl.when(b == 1)
        def _():
            pl.semaphore_signal(credit.at[0, g], inc=1, device_id=sibling, device_id_type=pl.DeviceIdType.MESH)

        direct = g in (ATT, TAB)
        if rest > 1:
            @pl.when(b == 0)
            def _():
                pl.semaphore_wait(credit.at[1, g], len(plane) if direct else rest - 1)

        if direct:
            for t in range(len(plane)):
                plane_copy(b, g, t).start()
            return
        for t in range(1, rest):
            rs1_copy(b, g, t).start()

    def rs2(b, g):
        for t in range(1, rest):
            rs1_copy(b, g, t).wait_recv()

        @pl.loop(0, rest * first)
        def _(p):
            here = dig_three * rest * first + p
            total = stage[g][b, core, here].astype(F32)
            for t in range(1, rest):
                total = total + r1[g][t - 1, p].astype(F32)
            stage[g][b, core, here] = total.astype(stage[g].dtype)

        for t in range(1, rest):
            @pl.when(b == 1)
            def _():
                pl.semaphore_signal(
                    credit.at[1, g], inc=1, device_id=peer_three(t), device_id_type=pl.DeviceIdType.MESH
                )

            rs2_copy(b, g, t).start()

    def rs3(b, g):
        direct = g in (ATT, TAB)
        copies = [plane_copy(b, g, t) for t in range(len(plane))] if direct else [
            rs2_copy(b, g, t) for t in range(1, rest)
        ]
        landing = r1[g] if direct else r2[g].at[b]
        for copy in copies:
            copy.wait_recv()

        @pl.loop(0, first)
        def _(p):
            here = (dig_three * rest + dig_two) * first + p
            total = stage[g][b, core, here].astype(F32)
            for t in range(len(copies)):
                total = total + landing[t, p].astype(F32)
            stage[g][b, core, here] = total.astype(stage[g].dtype)

        if direct:
            @pl.when(b == 1)
            def _():
                for three, two in plane:
                    pl.semaphore_signal(
                        credit.at[1, g], inc=1, device_id=peer_plane(three, two),
                        device_id_type=pl.DeviceIdType.MESH,
                    )


        for t in range(1, first):
            rs3_copy(b, g, t).start()

        @pl.when(core != b)
        def _():
            rs3_copy(b, g, 0).start()

    def rs4(b, g):
        @pl.when(core == b)
        def _():
            for own in (True, False):
                half = core if own else 1 - core
                begin = int(own)
                for t in range(begin, first):
                    ref = r3[g].at[half, t]
                    remote(ref, ref, rs3_s.at[at(b, g), t], rs3_r.at[g, half, t], sibling).wait_recv()
                total = stage[g][b, core, pos].astype(F32) if own else None
                for t in range(begin, first):
                    value = r3[g][half, t].astype(F32)
                    total = value if total is None else total + value
                final[g][half] = total

    def rs_sent(b, g):
        rs0_copy(b, g).wait_send()
        if g in (ATT, TAB):
            for t in range(len(plane)):
                plane_copy(b, g, t).wait_send()
        else:
            for t in range(1, rest):
                rs1_copy(b, g, t).wait_send()
                rs2_copy(b, g, t).wait_send()
        for t in range(1, first):
            rs3_copy(b, g, t).wait_send()

        @pl.when(core != b)
        def _():
            rs3_copy(b, g, 0).wait_send()

    def rows_of(i, images_too=1):
        return pl.ds(pl.multiple_of(i * rows, 16), images_too * rows)

    few = TOGETHER if slots % TOGETHER == 0 else 1
    many = TOGETHER_ROWS if slots % TOGETHER_ROWS == 0 else 1

    def step_rows(i, count):
        return rows_of(i * count, count)

    def ship_parts(kind, b, i):
        src, out = ((io_one, act_out), (io_two, ing_out))[kind]
        q = 2 * kind + b
        near = pltpu.make_async_copy(src.at[i], out.at[core, i], ship_s.at[q, i])
        far = remote(src.at[i], out.at[core, i], ship_s.at[q, i], ship_r.at[q, i], sibling)
        return near, far

    def ship(kind, b, i):
        near, far = ship_parts(kind, b, i)

        @pl.when(core == b)
        def _():
            near.start()

        @pl.when(core != b)
        def _():
            far.start()

    def shipped(kind, b, i):
        near, far = ship_parts(kind, b, i)

        @pl.when(core == b)
        def _():
            near.wait()

        @pl.when(core != b)
        def _():
            far.wait_send()

    def landed(kind, b, i):
        out = (act_out, ing_out)[kind]
        q = 2 * kind + b
        ref = out.at[1 - core, i]

        @pl.when(core == b)
        def _():
            remote(ref, ref, ship_s.at[q, i], ship_r.at[q, i], sibling).wait_recv()

    def live(i):
        return jnp.where(i < counts[0, core], 1.0, 0.0).astype(F32)

    def only_live(i, value, count):
        parts = [value[rows * m : rows * (m + 1)] * live(i * count + m) for m in range(count)]
        return jnp.concatenate(parts, axis=0)

    def coming(which, i):
        slot = (which * slots + i) % raw.shape[0]
        return pltpu.make_async_copy((images, cotangent)[which].at[i], raw.at[slot], in_s.at[which, i])

    def take_in(which, i):
        coming(which, i).wait()
        both = raw[(which * slots + i) % raw.shape[0]].astype(F32)
        (io_one, io_two)[which][i] = jnp.where(core == 0, both[:, 0, :], both[:, 1, :]).astype(LOW)

    def weave(kind):
        source, target = ((act_out, act_fin), (ing_out, ing_fin))[kind]
        ring = raw.shape[0]

        def fetch(i, m):
            return pltpu.make_async_copy(source.at[m, i], io_one.at[2 * (i % ring) + m], weave_in.at[kind, m, i])

        def leave(i):
            return pltpu.make_async_copy(raw.at[i % ring], target.at[i], weave_out.at[kind, i])

        for i in range(min(ring - 1, slots)):
            for m in range(2):
                fetch(i, m).start()

        @pl.loop(0, slots)
        def _(i):
            @pl.when(i + ring - 1 < slots)
            def _():
                for m in range(2):
                    fetch(i + ring - 1, m).start()

            @pl.when(i >= ring)
            def _():
                leave(i - ring).wait()

            for m in range(2):
                fetch(i, m).wait()
                raw[i % ring, :, m, :] = io_one[2 * (i % ring) + m]
            leave(i).start()

        for i in range(max(slots - ring, 0), slots):
            leave(i).wait()

    def far_copy(which, i, back):
        near, far = ((hid, hid_far), (slope, slope_far))[which]
        near, far = near.at[rows_of(i)], far.at[rows_of(i)]
        src, dst = (far, near) if back else (near, far)
        return pltpu.make_async_copy(src, dst, far_s.at[2 * int(back) + which, i])

    pairs = width // 128
    scale = head_dim ** -0.5
    lane = lax.broadcasted_iota(jnp.int32, (1, 128), 1)
    half_low = [(lane < head_dim).astype(LOW), (lane >= head_dim).astype(LOW)]
    half_f = [(lane < head_dim).astype(F32), (lane >= head_dim).astype(F32)]
    token = lax.broadcasted_iota(jnp.int32, (rows, 128), 0) < length
    half_valid = [jnp.where(token, half_f[j], 0.0).astype(LOW) for j in range(2)]
    valid_lanes = jnp.where(lax.broadcasted_iota(jnp.int32, (1, rows), 1) < length, 1.0, 0.0).astype(F32)
    spare = -rows % 128
    chunk = 2 * width
    chunks = ff // chunk

    def vec(s, r):
        return table[s, r : r + 1, :]

    def up_bias(s, c):
        begin = c * chunk
        row, col = begin // width, begin % width
        if col + chunk <= width:
            return table[s, BU + row : BU + row + 1, col : col + chunk]
        a = table[s, BU + row : BU + row + 1, col:width]
        b = table[s, BU + row + 1 : BU + row + 2, 0 : chunk - (width - col)]
        return jnp.concatenate([a, b], axis=1)

    def add_vec(s, r, value):
        gtable[s, r : r + 1, :] += value

    def add_up_bias(s, c, value):
        begin = c * chunk
        row, col = begin // width, begin % width
        if col + chunk <= width:
            gtable[s, BU + row : BU + row + 1, col : col + chunk] += value
        else:
            cut = width - col
            gtable[s, BU + row : BU + row + 1, col:width] += value[:, :cut]
            gtable[s, BU + row + 1 : BU + row + 2, 0 : chunk - cut] += value[:, cut:]

    def attn_forward(s, x, hat, i):
        rd = step_rows(i, few)
        nrm_ref, qkv_ref, prob_ref, ctx_ref = nrm1.at[s], qkv.at[s], prob.at[s], ctx.at[s]
        nrm = (hat * vec(s, G1) + vec(s, S1)).astype(LOW)
        nrm_ref[rd, :] = nrm
        mixed = mm(nrm, wqkv[s])
        q = (mixed[:, 0:width] + vec(s, BQ)).astype(LOW)
        k = mixed[:, width : 2 * width].astype(LOW)
        v = (mixed[:, 2 * width :] + vec(s, BV)).astype(LOW)
        qkv_ref[rd, 0:width] = q
        qkv_ref[rd, width : 2 * width] = k
        qkv_ref[rd, 2 * width :] = v
        images_out = []
        for m in range(few):
            mine = slice(rows * m, rows * (m + 1))
            parts = []
            for p in range(pairs):
                cols = slice(128 * p, 128 * p + 128)
                weights, sides = [], []
                for j in range(2):
                    keys = k[mine, cols] * half_low[j]
                    keys = jnp.concatenate([keys, keys[rows - spare :]], axis=0)
                    scores = mm_right(q[mine, cols], keys)
                    top = jnp.max(scores, axis=-1, keepdims=True)
                    e = jnp.exp2((scores - top) * (scale * 1.4426950408889634)).astype(LOW)
                    prob_ref[i * few + m, 2 * p + j] = e[:, :rows]
                    weights.append(e)
                    sides.append(jnp.concatenate([v[mine, cols] * half_valid[j], half_valid[j]], axis=1))
                    sides.append(jnp.zeros((spare, 256), LOW))
                total = mm(jnp.concatenate(weights, axis=1), jnp.concatenate(sides, axis=0))
                over = 1.0 / total[:, 128:]
                overs[s, rows_of(i * few + m), cols] = over.astype(LOW)
                parts.append((total[:, :128] * over).astype(LOW))
            images_out.append(jnp.concatenate(parts, axis=1))
        context = jnp.concatenate(images_out, axis=0)
        ctx_ref[rd, :] = context
        return x + mm(context, wout[s]) + vec(s, BO)

    def ff_forward(s, after, rd):
        hat, rstd, _ = normalize(after)
        hat2[s, rd, :] = hat.astype(LOW)
        nrm = (hat * vec(s, G2) + vec(s, S2)).astype(LOW)
        total = after + vec(s, BD)
        for c in range(chunks):
            cols = slice(chunk * c, chunk * c + chunk)
            pre = mm(nrm, wup[s, :, cols]) + up_bias(s, c)
            phi, slo = normal_parts(pre)
            h = (pre * phi).astype(LOW)
            hid[rd, cols] = h
            slope[rd, cols] = slo.astype(LOW)
            total = total + mm(h, wdown[s, cols, :])
        return total, rstd

    def ff_backward(s, g, rd, rstd):
        g_low = g.astype(LOW)
        add_vec(s, BD, colsum(g_low.astype(F32)))
        d_nrm = None
        for c in range(chunks):
            cols = slice(chunk * c, chunk * c + chunk)
            d_hid = mm_right(g_low, wdown[s, cols, :])
            d_pre = (d_hid * slope[rd, cols].astype(F32)).astype(LOW)
            slope[rd, cols] = d_pre
            add_up_bias(s, c, colsum(d_pre.astype(F32)))
            part = mm_right(d_pre, wup[s, :, cols])
            d_nrm = part if d_nrm is None else d_nrm + part
        hat = hat2[s, rd, :].astype(F32)
        add_vec(s, G2, colsum(d_nrm * hat))
        add_vec(s, S2, colsum(d_nrm))
        d_after = g + normalize_back(d_nrm * vec(s, G2), hat, rstd)
        low = d_after.astype(LOW)
        dal[rd, :] = low
        add_vec(s, BO, colsum(low.astype(F32)))
        return d_after

    def attn_backward(s, i):
        qkv_ref, prob_ref, ctx_ref = qkv.at[s], prob.at[s], ctx.at[s]
        rd = step_rows(i, few)
        d_context = mm_right(dal[rd, :], wout[s])
        d_context = (d_context * overs[s, rd, :].astype(F32)).astype(LOW)
        for m in range(few):
            rd = rows_of(i * few + m)
            d_ctx = d_context[rows * m : rows * (m + 1)]
            dq, dk, dv = [], [], []
            for p in range(pairs):
                cols = slice(128 * p, 128 * p + 128)
                q = qkv_ref[rd, 128 * p : 128 * p + 128]
                k = qkv_ref[rd, width + 128 * p : width + 128 * p + 128]
                v = qkv_ref[rd, 2 * width + 128 * p : 2 * width + 128 * p + 128]
                dc = d_ctx[:, cols]
                both = dc.astype(F32) * ctx_ref[rd, cols].astype(F32)
                q_t, dc_t = q.T, dc.T
                to_q, to_k, to_v = None, [], []
                for j in range(2):
                    e = prob_ref[i * few + m, 2 * p + j]
                    delta = jnp.sum(both * half_f[j], axis=-1, keepdims=True)
                    d_prob = mm_right(dc, v * half_low[j])
                    ds = (e.astype(F32) * (d_prob - delta)).astype(LOW)
                    part = mm(ds, k * half_valid[j])
                    to_q = part if to_q is None else to_q + part
                    head = slice(head_dim * j, head_dim * (j + 1))
                    to_k.append(mm(q_t[head], ds))
                    to_v.append(mm(dc_t[head], e))
                dq.append((to_q * scale).astype(LOW))
                dk.append((jnp.concatenate(to_k, axis=0) * (valid_lanes * scale)).astype(LOW).T)
                dv.append((jnp.concatenate(to_v, axis=0) * valid_lanes).astype(LOW).T)
            d_mixed = jnp.concatenate(dq + dk + dv, axis=1)
            qkv_ref[rd, :] = d_mixed
            add_vec(s, BQ, colsum(d_mixed[:, 0:width].astype(F32)))
            add_vec(s, BV, colsum(d_mixed[:, 2 * width :].astype(F32)))

    def input_backward(s, d_after, rd, x, mean, rstd):
        d_nrm = mm_right(qkv[s, rd, :], wqkv[s])
        hat = (x - mean) * rstd
        add_vec(s, G1, colsum(d_nrm * hat))
        add_vec(s, S1, colsum(d_nrm))
        return d_after + normalize_back(d_nrm * vec(s, G1), hat, rstd)

    def grads_down(s):
        left_t[...] = low_g[...].T

        @pl.loop(0, 2)
        def _(c):
            cols = pl.ds(pl.multiple_of(c * 2 * width, 128), 2 * width)
            block = mm(left_t[...], hid[:, cols]).T
            for i in range(n // 2):
                for half in range(2):
                    begin = 4 * unit * i + 2 * unit * half
                    s_d[s, half, place(half, c * (n // 2) + i)] = block[begin : begin + 2 * unit].astype(LOW)

    def pair_out(ref, s, half, one, two):
        for j in range(n):
            down = slice(unit * j, unit * (j + 1))
            piece = jnp.concatenate([one[down], two[down]], axis=0).astype(LOW)
            ref[s, half, place(half, j)] = piece

    def grads_up(s):
        left_t[...] = (hat2[s].astype(F32) * vec(s, G2) + vec(s, S2)).astype(LOW).T
        for half in range(2):
            both = mm(left_t[...], slope[:, 2 * half * width : 2 * (half + 1) * width])
            pair_out(s_u, s, half, both[:, :width], both[:, width:])

    def grads_attn(s):
        mix_s = qkv.at[s]
        left_t[...] = ctx[s].T
        four = mm(left_t[...], dal[...])
        left_t[...] = nrm1[s].T
        three = mm(left_t[...], mix_s[:, 2 * width :])
        pair_out(s_a, s, 1, three, four)
        both = mm(left_t[...], mix_s[:, 0 : 2 * width])
        pair_out(s_a, s, 0, both[:, :width], both[:, width:])

    barrier = pltpu.get_barrier_semaphore()
    greeted = [sibling]
    greeted += [{"section": half, **peer_first(t)} for t in range(1, first) for half in range(2)]
    greeted += [peer_plane(three, two) for three, two in plane]
    for device in greeted:
        pl.semaphore_signal(barrier, inc=1, device_id=device, device_id_type=pl.DeviceIdType.MESH)
    pack_own()
    pl.semaphore_wait(barrier, len(greeted))

    def run(*todo):
        for f, b, g in todo:
            f(b, g)

    def events(i, table_of):
        for when, todo in table_of.items():
            @pl.when(i == when)
            def _():
                run(*todo)

    def both(f, b, g):
        return [(f, b, g), (f, b, TAB)]

    def take(i, m):
        return pl.ds(pl.multiple_of((i * many + m) * rows, 16), length)

    ahead = raw.shape[0]
    run(*both(ag1, 0, ATT))
    for i in range(ahead):
        coming(0, i).start()
    fill_repeats()
    gtable[...] = jnp.zeros_like(gtable)
    low_g[...] = jnp.zeros_like(low_g)
    xs[0] = jnp.zeros_like(low_g)

    @pl.loop(0, slots)
    def images_in(i):
        take_in(0, i)

        @pl.when(i + ahead < slots)
        def _():
            coming(0, i + ahead).start()

        @pl.when(i + ahead >= slots)
        def _():
            coming(1, i + ahead - slots).start()

        @pl.when(i == 3)
        def _():
            run(*both(ag2, 0, ATT), (ag1, 0, UP), (ag1, 0, DOWN))

    def statistic(s, rd, which):
        return jnp.where(s == 0, rstds[rd, which : which + 1], rstds[rd, 3 + which : 4 + which])

    def first_norm(s, rd, x):
        hat, rstd, mean = normalize(x)
        after_ref[rd, :] = hat
        rstds[rd, 3 * s : 3 * s + 1] = rstd
        rstds[rd, 3 * s + 2 : 3 * s + 3] = mean

    @pl.loop(0, slots // many)
    def norm_one(i):
        for m in range(many):
            xs[0, take(i, m), :] = io_one[i * many + m]
        rd = step_rows(i, many)
        x = xs[0, rd, :].astype(F32)
        token_rows = lax.broadcasted_iota(jnp.int32, (rows, width), 0) < length
        parts = [x[rows * m : rows * (m + 1)] for m in range(many)]
        x = jnp.concatenate([jnp.where(token_rows, part, part[0:1]) for part in parts], axis=0)
        xs[0, rd, :] = x.astype(LOW)
        first_norm(0, rd, x)

    run(*both(ag3, 0, ATT), (ag2, 0, UP), *both(ag1, 1, ATT), (ag2, 0, DOWN), (ag1, 1, UP), (ag1, 1, DOWN))

    @pl.loop(0, slots)
    def cotangents_in(i):
        take_in(1, i)

        @pl.when(i + ahead < slots)
        def _():
            coming(1, i + ahead).start()

    run(*both(ag4, 0, ATT), (ag3, 0, UP), *both(ag5, 0, ATT))

    @pl.loop(0, 2)
    def forward(s):
        @pl.loop(0, slots // few)
        def attention(i):
            @pl.when(s == 0)
            def _():
                events(i, {
                    0: [(ag3, 0, DOWN), *both(ag2, 1, ATT)],
                    1: [(ag4, 0, UP), (ag2, 1, UP)],
                    2: [(ag4, 0, DOWN)],
                })

            @pl.when(s == 1)
            def _():
                events(i, {2: [(ag4, 1, DOWN)]})

            rd = step_rows(i, few)
            after_ref[rd, :] = attn_forward(s, xs[s, rd, :].astype(F32), after_ref[rd, :], i)

        @pl.when(s == 0)
        def _():
            run(*both(ag3, 1, ATT), (ag5, 0, UP), (ag5, 0, DOWN))

        @pl.when(s == 1)
        def _():
            run((ag5, 1, UP), (ag5, 1, DOWN))

        @pl.loop(0, slots // many)
        def feed_forward(i):
            @pl.when(s == 0)
            def _():
                events(i, {0: [(ag3, 1, UP), (ag2, 1, DOWN)], 1: both(ag4, 1, ATT)})

            rd = step_rows(i, many)

            @pl.when(s == 1)
            def _():
                for m in range(many):
                    far_copy(0, i * many + m, False).wait()
                    far_copy(1, i * many + m, False).wait()
                    shipped(0, 0, i * many + m)

            out, rstd2 = ff_forward(s, after_ref[rd, :], rd)
            for block in range(2):
                @pl.when(s == block)
                def _():
                    rstds[rd, 3 * block + 1 : 3 * block + 2] = rstd2

            out = only_live(i, out, many)
            for m in range(many):
                io_one[i * many + m] = out[rows * m : rows * m + length].astype(LOW)
                ship(0, s, i * many + m)

            @pl.when(s == 0)
            def _():
                for m in range(many):
                    far_copy(0, i * many + m, False).start()
                    far_copy(1, i * many + m, False).start()
                low = out.astype(LOW)
                xs[1, rd, :] = low
                first_norm(1, rd, low.astype(F32))

        @pl.when(s == 0)
        def _():
            run((ag4, 1, UP), (ag3, 1, DOWN), *both(ag5, 1, ATT))

    for b in range(2):
        for g in groups:
            ag_sent(b, g)

    @pl.loop(0, 2)
    def backward(turn):
        s = 1 - turn

        @pl.loop(0, slots // many)
        def feed_forward(i):
            @pl.when(s == 0)
            def _():
                events(i, {1: [(rs1, 1, TAB), (rs4, 1, UP)]})
                for m in range(many):
                    far_copy(1, i * many + m, True).wait()

            rd = step_rows(i, many)
            for m in range(many):
                g = live(i * many + m) * io_two[i * many + m].astype(F32)
                low_g[take(i, m), :] = g.astype(LOW)
            after_ref[rd, :] = ff_backward(s, low_g[rd, :].astype(F32), rd, statistic(s, rd, 1))

        @pl.when(s == 0)
        def _():
            for i in range(slots):
                far_copy(0, i, True).wait()
            run((rs3, 1, ATT))

        grads_down(s)
        run((rs0, s, DOWN))

        @pl.when(s == 1)
        def _():
            for i in range(slots):
                far_copy(0, i, True).start()

        grads_up(s)
        run((rs0, s, UP), (rs1, s, DOWN))

        @pl.when(s == 1)
        def _():
            for i in range(slots):
                far_copy(1, i, True).start()

        @pl.when(s == 0)
        def _():
            run((rs3, 1, TAB))

        @pl.loop(0, slots // few)
        def attention(i):
            events(i, {1: [(rs1, s, UP), (rs2, s, DOWN)], 2: [(rs2, s, UP), (rs3, s, DOWN)]})

            @pl.when(s == 0)
            def _():
                events(i, {1: both(rs4, 1, ATT)})

            attn_backward(s, i)

        grads_attn(s)
        run((rs0, s, ATT), (rs3, s, UP))

        @pl.loop(0, slots // many)
        def to_input(i):
            events(i, {1: [(rs1, s, ATT), (rs4, s, DOWN)]})
            rd = step_rows(i, many)
            x = xs[s, rd, :].astype(F32)
            d_in = input_backward(s, after_ref[rd, :], rd, x, statistic(s, rd, 2), statistic(s, rd, 0))
            for m in range(many):
                @pl.when(s == 0)
                def _():
                    shipped(1, 1, i * many + m)

                io_two[i * many + m] = d_in[rows * m : rows * m + length].astype(LOW)
                ship(1, s, i * many + m)

        table_out(s)
        run((rs0, s, TAB))

    run((rs4, 0, UP), (rs1, 0, TAB))

    @pl.loop(0, slots)
    def acts_out(i):
        shipped(0, 1, i)
        for b in range(2):
            landed(0, b, i)

    weave(0)
    run((rs3, 0, ATT), (rs3, 0, TAB))

    @pl.loop(0, slots)
    def ings_out(i):
        shipped(1, 0, i)
        for b in range(2):
            landed(1, b, i)

    weave(1)
    run(*both(rs4, 0, ATT))
    for b in range(2):
        for g in groups:
            rs_sent(b, g)


def output_kernel(
    acts, ings, f_a, f_u, f_d, f_t, o_acts, o_ings, o_g1, o_s1, o_qkv, o_qv, o_out, o_bo, o_g2, o_s2, o_up, o_bu, o_down, o_bd, sems
):
    copies = [
        pltpu.make_async_copy(source.at[i], target.at[i], sems.at[which, i])
        for which, (source, target) in enumerate(((acts, o_acts), (ings, o_ings)))
        for i in range(acts.shape[0])
    ]
    for copy in copies:
        copy.start()
    unit, width = o_out.shape[1:]
    for half in range(2):
        o_down[0, 2 * unit * half : 2 * unit * (half + 1), :] = f_d[half]
        for sub in range(2):
            part = 2 * half + sub
            cols = slice(part * width, (part + 1) * width)
            o_up[0, :, cols] = f_u[half, unit * sub : unit * (sub + 1), :]
            piece = f_a[half, unit * sub : unit * (sub + 1), :]
            if part == 3:
                o_out[0] = piece
            else:
                o_qkv[0, :, cols] = piece
    begin = 0
    for out in (o_g1, o_s1, o_bo, o_g2, o_s2, o_bd, o_qv):
        part = out.shape[1]
        out[...] = f_t[0, :, begin : begin + part]
        begin += part
    o_bu[...] = f_t[1, :, 0 : o_bu.shape[1]]
    for copy in copies:
        copy.wait()


def local(
    images, cotangent, counts,
    ln1_gain, ln1_bias, w_qkv, b_qv, w_out, b_out, ln2_gain, ln2_bias, w_up, b_up, w_down, b_down,
):
    micro_count, slots, length, width = images.shape
    ff = w_up.shape[2]
    rows = -(-length // 16) * 16
    n = lax.axis_size("fsdp")
    unit = width // n
    first, rest = radices(n)
    total = slots * rows
    head_dim = width // HEADS

    def vm(*shape, kind=LOW):
        return pltpu.VMEM(shape, kind)

    tall = [(2 * unit, LOW)] * 3 + [(1, F32)]
    dma = lambda *shape: pltpu.SemaphoreType.DMA(shape)
    outs = [((slots, length, 2, width), LOW)] * 2
    outs += [((2, r, width), F32) for r, _ in tall] + [((total, ff), LOW)] * 2 + [((2, slots, length, width), LOW)] * 2
    scratch = [
        vm(2, total, width), vm(3, length, 2, width), vm(slots, length, width), vm(slots, length, width),
        *[vm(2, r, width, kind=kind) for r, kind in tall],
        vm(2, width, 3 * width), vm(2, width, width), vm(2, width, ff), vm(2, ff, width),
        vm(2, TABLE, width, kind=F32), vm(2, TABLE, width, kind=F32),
        vm(unit, width), vm(2 * unit, 2 * width), vm(4 * unit, 4 * width),
        vm(total, width, kind=F32), vm(2, total, width), vm(2, total, 3 * width), vm(2, slots, HEADS, rows, rows),
        vm(2, total, width),
        vm(2, total, width), vm(2, total, width), vm(total, 6, kind=F32),
        vm(total, ff), vm(total, ff), vm(total, width), vm(total, width), vm(width, total),
    ]
    scratch += [vm(2, 2, n, r, width, kind=kind) for r, kind in tall]
    scratch += [vm(n, r, width, kind=kind) for r, kind in tall]
    plane = rest * rest - 1
    for g, (r, kind) in enumerate(tall):
        direct = g in (ATT, TAB)
        scratch.append(vm(*((plane, first) if direct else (rest - 1, rest * first)), r, width, kind=kind))
    scratch += [vm(2, rest - 1, first, *tall[g][:1], width) for g in (UP, DOWN)]
    scratch += [vm(2, first, r, width, kind=kind) for r, kind in tall]
    scratch += [dma(2, slots), dma(2, 2, slots), dma(2, slots), dma(4, slots), dma(4, slots), dma(4, slots)]
    scratch += [dma(4, 2, first), dma(8, first)] + [dma(8, rest - 1)] * 4 + [dma(8, rest)] * 2
    scratch += [dma(8)] * 2 + [dma(8, plane)] * 2 + [dma(8, rest - 1)] * 2 + [dma(8, first), dma(4, 2, first)]
    scratch += [pltpu.SemaphoreType.REGULAR((2, 4))]
    dims = (slots, length, rows, width, ff, head_dim, n)
    vmem = pl.BlockSpec(memory_space=pltpu.VMEM)
    hbm = pl.BlockSpec(memory_space=pltpu.HBM)
    acts, ings, f_a, f_u, f_d, f_t, *_ = pl.pallas_call(
        functools.partial(whole_kernel, dims),
        out_shape=[jax.ShapeDtypeStruct(*o) for o in outs],
        in_specs=[hbm, hbm, pl.BlockSpec(memory_space=pltpu.SMEM)] + [vmem] * 12,
        out_specs=[hbm, hbm] + [vmem] * 4 + [hbm] * 4,
        scratch_shapes=scratch,
        compiler_params=pltpu.CompilerParams(
            vmem_limit_bytes=(64 << 20) - (96 << 10), collective_id=0, has_side_effects=True
        ),
    )(
        images.transpose(1, 2, 0, 3), cotangent.transpose(1, 2, 0, 3), counts.T, ln1_gain, ln1_bias, b_out, ln2_gain, ln2_bias, b_down, b_qv, b_up,
        w_qkv, w_out, w_up, w_down,
    )

    params = (
        ln1_gain, ln1_bias, w_qkv, b_qv, w_out, b_out, ln2_gain, ln2_bias, w_up, b_up, w_down, b_down
    )
    acts, ings, *grads = pl.pallas_call(
        output_kernel,
        out_shape=[jax.ShapeDtypeStruct(v.shape, v.dtype) for v in (acts, ings)]
        + [jax.ShapeDtypeStruct(p.shape, F32) for p in params],
        in_specs=[hbm] * 2 + [vmem] * 4,
        out_specs=[hbm] * 2 + [vmem] * len(params),
        scratch_shapes=[dma(2, slots)],
    )(acts, ings, f_a, f_u, f_d, f_t)

    def as_given(value):
        return value.transpose(2, 0, 1, 3)[None]

    return (as_given(acts), as_given(ings), *grads)


def solution(mesh):
    split = P("section", "fsdp")
    cube = P("section", "fsdp", None)
    image = P(None, "fsdp", None, None)
    result = P("section", None, "fsdp", None, None)
    params = (split, split, cube, split, cube, split, split, split, cube, split, cube, split)
    return jax.shard_map(
        local,
        mesh=mesh,
        in_specs=(image, image, P(None, "fsdp")) + params,
        out_specs=(result, result) + params,
        check_vma=False,
    )
```

```python
import functools
import math

import jax
import jax.numpy as jnp
from jax import lax
from jax.experimental import pallas as pl
from jax.experimental.pallas import tpu as pltpu
from jax.sharding import PartitionSpec as P

HEADS = 6
EPS = 1e-06
F32 = jnp.float32
LOW = jnp.bfloat16

G1, S1, BO, G2, S2, BD, BQ, BV, BU = 0, 1, 2, 3, 4, 5, 6, 7, 8
TABLE = 16
TOGETHER, TOGETHER_ROWS = 2, 3
ATT, UP, DOWN, TAB = 0, 1, 2, 3


def radices(n):
    rest = max(r for r in range(1, n + 1) if r * r * r <= n and n % (r * r) == 0)
    return n // (rest * rest), rest


def mm(left, right):
    return jnp.dot(left, right, preferred_element_type=F32)


def mm_right(left, right):
    return lax.dot_general(left, right, (((1,), (1,)), ((), ())), preferred_element_type=F32)


def mm_left(left, right):
    return lax.dot_general(left, right, (((0,), (0,)), ((), ())), preferred_element_type=F32)


def normal_parts(pre):
    phi = 0.5 + 0.5 * lax.erf(pre * 0.7071067811865476)
    density = jnp.exp2(pre * pre * (-0.5 * 1.4426950408889634)) * 0.3989422804014327
    return phi, phi + pre * density


def normalize(value):
    mean = jnp.mean(value, axis=-1, keepdims=True)
    center = value - mean
    rstd = lax.rsqrt(jnp.mean(center * center, axis=-1, keepdims=True) + EPS)
    return center * rstd, rstd, mean


def normalize_back(d_hat, hat, rstd):
    mean_one = jnp.mean(d_hat, axis=-1, keepdims=True)
    mean_two = jnp.mean(d_hat * hat, axis=-1, keepdims=True)
    return rstd * (d_hat - mean_one - hat * mean_two)


def colsum(value):
    return jnp.sum(value, axis=0, keepdims=True)


def whole_kernel(dims, *refs):
    slots, length, rows, width, ff, head_dim, n = dims
    (
        images, cotangent, counts, v_g1, v_s1, v_bo, v_g2, v_s2, v_bd, v_qv, v_up, a_qkv, a_out, a_up, a_down,
        act_fin, ing_fin, f_a, f_u, f_d, f_t, hid_far, slope_far, act_out, ing_out,
        xs, raw, io_one, io_two, pack_a, pack_u, pack_d, pack_t,
        wqkv, wout, wup, wdown, table, gtable, rep_one, rep_two, rep_four,
        after_ref, nrm1, qkv, prob, overs, ctx, hat2, rstds, hid, slope, dal, low_g, left_t,
        s_a, s_u, s_d, s_t, r0_a, r0_u, r0_d, r0_t, r1_a, r1_u, r1_d, r1_t, r2_u, r2_d,
        r3_a, r3_u, r3_d, r3_t,
        in_s, weave_in, weave_out, ship_s, ship_r, far_s, ag1_s, ag1_r, ag2_s, ag2_r, ag3_s, ag3_r, ag4_s, ag4_r,
        rs0_s, rs0_r, rs1_s, rs1_r, rs2_s, rs2_r, rs3_s, rs3_r, credit,
    ) = refs
    groups = (ATT, UP, DOWN, TAB)
    pack = (pack_a, pack_u, pack_d, pack_t)
    stage = (s_a, s_u, s_d, s_t)
    r0, r1, r2 = (r0_a, r0_u, r0_d, r0_t), (r1_a, r1_u, r1_d, r1_t), (None, r2_u, r2_d, None)
    r3, final = (r3_a, r3_u, r3_d, r3_t), (f_a, f_u, f_d, f_t)

    first, rest = radices(n)
    unit = width // n
    core = lax.axis_index("section")
    me = lax.axis_index("fsdp")
    dig_a, dig_b, dig_c = me // (rest * rest), (me // rest) % rest, me % rest
    dig_three, dig_two = dig_c + core * (dig_b - dig_c), dig_b + core * (dig_c - dig_b)
    step_three, step_two = 1 + core * (rest - 1), rest - core * (rest - 1)
    pos = (dig_three * rest + dig_two) * first + dig_a
    pos_of = ((dig_c * rest + dig_b) * first + dig_a, (dig_b * rest + dig_c) * first + dig_a)
    sibling = {"section": 1 - core}

    def place(half, j):
        a, b, c = j // (rest * rest), (j // rest) % rest, j % rest
        return ((c * rest + b) if half == 0 else (b * rest + c)) * first + a

    def peer_first(t):
        return {"fsdp": me + ((dig_a + t) % first - dig_a) * (rest * rest)}

    def peer_two(t):
        return {"fsdp": me + ((dig_two + t) % rest - dig_two) * step_two}

    def peer_three(t):
        return {"fsdp": me + ((dig_three + t) % rest - dig_three) * step_three}

    def peer_plane(three, two):
        here = ((dig_three + three) % rest - dig_three) * step_three
        return {"fsdp": me + here + ((dig_two + two) % rest - dig_two) * step_two}

    plane = [(three, two) for three in range(rest) for two in range(rest) if three or two]

    def remote(src, dst, s_sem, r_sem, device):
        return pltpu.make_async_remote_copy(
            src_ref=src, dst_ref=dst, send_sem=s_sem, recv_sem=r_sem, device_id=device,
            device_id_type=pl.DeviceIdType.MESH,
        )

    def slab_two(three, two):
        return pl.ds((three * rest + two) * first, first)

    def slab_three(three):
        return pl.ds(three * rest * first, rest * first)

    def fill_repeats():
        for ref in (rep_one, rep_two, rep_four):
            part = ref.shape[0]
            lanes = lax.broadcasted_iota(jnp.int32, ref.shape, 1).astype(F32)
            line = lax.broadcasted_iota(jnp.int32, ref.shape, 0).astype(F32)
            rest_of = lanes - part * jnp.floor((lanes + 0.5) * (1.0 / part))
            ref[...] = jnp.where(jnp.abs(rest_of - line) < 0.5, 1.0, 0.0).astype(LOW)

    def own_lanes(part):
        shape = (n, part * n)
        lanes = lax.broadcasted_iota(jnp.int32, shape, 1)
        begin = lax.broadcasted_iota(jnp.int32, shape, 0) * part
        return (lanes >= begin) & (lanes < begin + part)

    shares = (
        ((G1, unit, rep_one), (S1, unit, rep_one), (BO, unit, rep_one), (G2, unit, rep_one), (S2, unit, rep_one),
         (BD, unit, rep_one), (BQ, 2 * unit, rep_two)),
        ((BU, 4 * unit, rep_four),),
    )

    def table_in(b):
        for half in range(2):
            lines = jnp.concatenate([s_t[b, half, place(half, j)] for j in range(n)], axis=0)
            begin = 0
            for row, part, ref in shares[half]:
                spread = mm(lines[:, begin : begin + part].astype(LOW), ref[...])
                line = colsum(jnp.where(own_lanes(part), spread, 0.0))
                for i in range(part * n // width):
                    table[b, row + i : row + i + 1, :] = line[:, width * i : width * (i + 1)]
                begin += part

    def table_out(b):
        for half in range(2):
            parts, begin = [], 0
            for row, part, ref in shares[half]:
                count = part * n // width
                line = jnp.concatenate([gtable[b, row + i : row + i + 1, :] for i in range(count)], axis=1)
                parts.append(mm_right(jnp.where(own_lanes(part), line, 0.0).astype(LOW), ref[...]))
                begin += part
            parts.append(jnp.zeros((n, width - begin), F32))
            lines = jnp.concatenate(parts, axis=1)
            for j in range(n):
                s_t[b, half, place(half, j)] = lines[j : j + 1]

    def pack_own():
        for half in range(2):
            vectors = ((v_g1, v_s1, v_bo, v_g2, v_s2, v_bd, v_qv), (v_up,))[half]
            lines = [vector[...].astype(F32) for vector in vectors]
            lines.append(jnp.zeros((1, width - sum(line.shape[1] for line in lines)), F32))
            pack_t[half] = jnp.concatenate(lines, axis=1)
            for ref in (pack_a, pack_u):
                both = []
                for part in (2 * half, 2 * half + 1):
                    if ref is pack_u:
                        both.append(a_up[0, :, part * width : (part + 1) * width])
                    elif part == 3:
                        both.append(a_out[0])
                    else:
                        both.append(a_qkv[0, :, part * width : (part + 1) * width])
                ref[half] = jnp.concatenate([value.astype(F32) for value in both], axis=0).astype(LOW)
            pack_d[half] = a_down[0, 2 * unit * half : 2 * unit * (half + 1), :]

    def at(b, g):
        return len(groups) * b + g

    def ag1_copy(b, g, half, t):
        device = {"section": half, **peer_first(t)} if t else sibling
        return remote(
            pack[g].at[half], stage[g].at[b, half, pos_of[half]],
            ag1_s.at[g, half, t], ag1_r.at[at(b, g), t], device,
        )

    def ag1_landing(b, g, t):
        ref = stage[g].at[b, core, (dig_three * rest + dig_two) * first + (dig_a + first - t) % first]
        return remote(ref, ref, ag1_s.at[g, 0, t], ag1_r.at[at(b, g), t], sibling)

    def ag2_copy(b, g, t):
        ref = stage[g].at[b, core, slab_two(dig_three, dig_two)]
        return remote(ref, ref, ag2_s.at[at(b, g), t - 1], ag2_r.at[at(b, g), t - 1], peer_two(t))

    def ag3_copy(b, g, t):
        ref = stage[g].at[b, core, slab_three(dig_three)]
        return remote(ref, ref, ag3_s.at[at(b, g), t - 1], ag3_r.at[at(b, g), t - 1], peer_three(t))

    def ag4_copy(b, g, t):
        ref = stage[g].at[b, core, slab_three((dig_three + rest - t) % rest)]
        return remote(ref, ref, ag4_s.at[at(b, g), t], ag4_r.at[at(b, g), t], sibling)

    def ag4_landing(b, g, t):
        ref = stage[g].at[b, 1 - core, slab_three((dig_two + rest - t) % rest)]
        return remote(ref, ref, ag4_s.at[at(b, g), t], ag4_r.at[at(b, g), t], sibling)

    def ag1(b, g):
        @pl.when(core == b)
        def _():
            for t in range(1, first):
                for half in range(2):
                    ag1_copy(b, g, half, t).start()
            ag1_copy(b, g, 1 - b, 0).start()
            stage[g][b, b, pos] = pack[g][b]

    def ag2(b, g):
        for t in range(1, first):
            ag1_landing(b, g, t).wait_recv()

        @pl.when(core != b)
        def _():
            ag1_landing(b, g, 0).wait_recv()

        for t in range(1, rest):
            ag2_copy(b, g, t).start()

    def ag3(b, g):
        for t in range(1, rest):
            ag2_copy(b, g, t).wait_recv()
        for t in range(1, rest):
            ag3_copy(b, g, t).start()
        ag4_copy(b, g, 0).start()

    def ag4(b, g):
        for t in range(1, rest):
            ag3_copy(b, g, t).wait_recv()
            ag4_copy(b, g, t).start()

    def ag5(b, g):
        for t in range(rest):
            ag4_landing(b, g, t).wait_recv()
        lay_out(b, g)

    def ag_sent(b, g):
        @pl.when(core == b)
        def _():
            for t in range(1, first):
                for half in range(2):
                    ag1_copy(b, g, half, t).wait_send()
            ag1_copy(b, g, 1 - b, 0).wait_send()

        for t in range(1, rest):
            ag2_copy(b, g, t).wait_send()
            ag3_copy(b, g, t).wait_send()
        for t in range(rest):
            ag4_copy(b, g, t).wait_send()

    def lay_out(b, g):
        if g == TAB:
            table_in(b)
            return
        if g == DOWN:
            for j in range(n):
                for half in range(2):
                    begin = 4 * unit * j + 2 * unit * half
                    wdown[b, begin : begin + 2 * unit, :] = s_d[b, half, place(half, j)]
            return
        together = 16 // math.gcd(unit, 16)
        for half in range(2):
            for j in range(0, n, together):
                pieces = [stage[g][b, half, place(half, j + i)].astype(F32) for i in range(together)]
                for sub in range(2):
                    low = sub * unit
                    block = jnp.concatenate([piece[low : low + unit] for piece in pieces], axis=0).astype(LOW)
                    part = 2 * half + sub
                    down = slice(unit * j, unit * (j + together))
                    if g == UP:
                        wup[b, down, part * width : (part + 1) * width] = block
                    elif part == 3:
                        wout[b, down, :] = block
                    else:
                        wqkv[b, down, part * width : (part + 1) * width] = block

    def rs0_copy(b, g):
        return remote(stage[g].at[b, 1 - core], r0[g], rs0_s.at[at(b, g)], rs0_r.at[at(b, g)], sibling)

    def rs1_copy(b, g, t):
        return remote(
            stage[g].at[b, core, slab_three((dig_three + t) % rest)], r1[g].at[t - 1],
            rs1_s.at[at(b, g), t - 1], rs1_r.at[at(b, g), t - 1], peer_three(t),
        )

    def rs2_copy(b, g, t):
        return remote(
            stage[g].at[b, core, slab_two(dig_three, (dig_two + t) % rest)], r2[g].at[b, t - 1],
            rs2_s.at[at(b, g), t - 1], rs2_r.at[at(b, g), t - 1], peer_two(t),
        )

    def rs3_copy(b, g, t):
        there = (dig_three * rest + dig_two) * first + (dig_a + t) % first
        device = {"section": b, **peer_first(t)} if t else sibling
        return remote(
            stage[g].at[b, core, there], r3[g].at[core, t], rs3_s.at[at(b, g), t], rs3_r.at[g, core, t], device
        )

    def plane_copy(b, g, t):
        three, two = plane[t]
        return remote(
            stage[g].at[b, core, slab_two((dig_three + three) % rest, (dig_two + two) % rest)], r1[g].at[t],
            rs1_s.at[at(b, g), t], rs1_r.at[at(b, g), t], peer_plane(three, two),
        )

    def rs0(b, g):
        @pl.when(b == 0)
        def _():
            pl.semaphore_wait(credit.at[0, g], 1)

        rs0_copy(b, g).start()

    def rs1(b, g):
        rs0_copy(b, g).wait_recv()

        @pl.loop(0, n)
        def _(p):
            stage[g][b, core, p] = stage[g][b, core, p] + r0[g][p]

        @pl.when(b == 1)
        def _():
            pl.semaphore_signal(credit.at[0, g], inc=1, device_id=sibling, device_id_type=pl.DeviceIdType.MESH)

        direct = g in (ATT, TAB)
        if rest > 1:
            @pl.when(b == 0)
            def _():
                pl.semaphore_wait(credit.at[1, g], len(plane) if direct else rest - 1)

        if direct:
            for t in range(len(plane)):
                plane_copy(b, g, t).start()
            return
        for t in range(1, rest):
            rs1_copy(b, g, t).start()

    def rs2(b, g):
        for t in range(1, rest):
            rs1_copy(b, g, t).wait_recv()

        @pl.loop(0, rest * first)
        def _(p):
            here = dig_three * rest * first + p
            total = stage[g][b, core, here].astype(F32)
            for t in range(1, rest):
                total = total + r1[g][t - 1, p].astype(F32)
            stage[g][b, core, here] = total.astype(stage[g].dtype)

        for t in range(1, rest):
            @pl.when(b == 1)
            def _():
                pl.semaphore_signal(
                    credit.at[1, g], inc=1, device_id=peer_three(t), device_id_type=pl.DeviceIdType.MESH
                )

            rs2_copy(b, g, t).start()

    def rs3(b, g):
        direct = g in (ATT, TAB)
        copies = [plane_copy(b, g, t) for t in range(len(plane))] if direct else [
            rs2_copy(b, g, t) for t in range(1, rest)
        ]
        landing = r1[g] if direct else r2[g].at[b]
        for copy in copies:
            copy.wait_recv()

        @pl.loop(0, first)
        def _(p):
            here = (dig_three * rest + dig_two) * first + p
            total = stage[g][b, core, here].astype(F32)
            for t in range(len(copies)):
                total = total + landing[t, p].astype(F32)
            stage[g][b, core, here] = total.astype(stage[g].dtype)

        if direct:
            @pl.when(b == 1)
            def _():
                for three, two in plane:
                    pl.semaphore_signal(
                        credit.at[1, g], inc=1, device_id=peer_plane(three, two),
                        device_id_type=pl.DeviceIdType.MESH,
                    )


        for t in range(1, first):
            rs3_copy(b, g, t).start()

        @pl.when(core != b)
        def _():
            rs3_copy(b, g, 0).start()

    def rs4(b, g):
        @pl.when(core == b)
        def _():
            for own in (True, False):
                half = core if own else 1 - core
                begin = int(own)
                for t in range(begin, first):
                    ref = r3[g].at[half, t]
                    remote(ref, ref, rs3_s.at[at(b, g), t], rs3_r.at[g, half, t], sibling).wait_recv()
                total = stage[g][b, core, pos].astype(F32) if own else None
                for t in range(begin, first):
                    value = r3[g][half, t].astype(F32)
                    total = value if total is None else total + value
                final[g][half] = total

    def rs_sent(b, g):
        rs0_copy(b, g).wait_send()
        if g in (ATT, TAB):
            for t in range(len(plane)):
                plane_copy(b, g, t).wait_send()
        else:
            for t in range(1, rest):
                rs1_copy(b, g, t).wait_send()
                rs2_copy(b, g, t).wait_send()
        for t in range(1, first):
            rs3_copy(b, g, t).wait_send()

        @pl.when(core != b)
        def _():
            rs3_copy(b, g, 0).wait_send()

    def rows_of(i, images_too=1):
        return pl.ds(pl.multiple_of(i * rows, 16), images_too * rows)

    few = TOGETHER if slots % TOGETHER == 0 else 1
    many = TOGETHER_ROWS if slots % TOGETHER_ROWS == 0 else 1

    def step_rows(i, count):
        return rows_of(i * count, count)

    def ship_parts(kind, b, i):
        src, out = ((io_one, act_out), (io_two, ing_out))[kind]
        q = 2 * kind + b
        near = pltpu.make_async_copy(src.at[i], out.at[core, i], ship_s.at[q, i])
        far = remote(src.at[i], out.at[core, i], ship_s.at[q, i], ship_r.at[q, i], sibling)
        return near, far

    def ship(kind, b, i):
        near, far = ship_parts(kind, b, i)

        @pl.when(core == b)
        def _():
            near.start()

        @pl.when(core != b)
        def _():
            far.start()

    def shipped(kind, b, i):
        near, far = ship_parts(kind, b, i)

        @pl.when(core == b)
        def _():
            near.wait()

        @pl.when(core != b)
        def _():
            far.wait_send()

    def landed(kind, b, i):
        out = (act_out, ing_out)[kind]
        q = 2 * kind + b
        ref = out.at[1 - core, i]

        @pl.when(core == b)
        def _():
            remote(ref, ref, ship_s.at[q, i], ship_r.at[q, i], sibling).wait_recv()

    def live(i):
        return jnp.where(i < counts[0, core], 1.0, 0.0).astype(F32)

    def only_live(i, value, count):
        parts = [value[rows * m : rows * (m + 1)] * live(i * count + m) for m in range(count)]
        return jnp.concatenate(parts, axis=0)

    def coming(which, i):
        slot = (which * slots + i) % raw.shape[0]
        return pltpu.make_async_copy((images, cotangent)[which].at[i], raw.at[slot], in_s.at[which, i])

    def take_in(which, i):
        coming(which, i).wait()
        both = raw[(which * slots + i) % raw.shape[0]].astype(F32)
        (io_one, io_two)[which][i] = jnp.where(core == 0, both[:, 0, :], both[:, 1, :]).astype(LOW)

    def weave(kind):
        source, target = ((act_out, act_fin), (ing_out, ing_fin))[kind]
        ring = raw.shape[0]

        def fetch(i, m):
            return pltpu.make_async_copy(source.at[m, i], io_one.at[2 * (i % ring) + m], weave_in.at[kind, m, i])

        def leave(i):
            return pltpu.make_async_copy(raw.at[i % ring], target.at[i], weave_out.at[kind, i])

        for i in range(min(ring - 1, slots)):
            for m in range(2):
                fetch(i, m).start()

        @pl.loop(0, slots)
        def _(i):
            @pl.when(i + ring - 1 < slots)
            def _():
                for m in range(2):
                    fetch(i + ring - 1, m).start()

            @pl.when(i >= ring)
            def _():
                leave(i - ring).wait()

            for m in range(2):
                fetch(i, m).wait()
                raw[i % ring, :, m, :] = io_one[2 * (i % ring) + m]
            leave(i).start()

        for i in range(max(slots - ring, 0), slots):
            leave(i).wait()

    def far_copy(which, i, back):
        near, far = ((hid, hid_far), (slope, slope_far))[which]
        near, far = near.at[rows_of(i)], far.at[rows_of(i)]
        src, dst = (far, near) if back else (near, far)
        return pltpu.make_async_copy(src, dst, far_s.at[2 * int(back) + which, i])

    pairs = width // 128
    scale = head_dim ** -0.5
    lane = lax.broadcasted_iota(jnp.int32, (1, 128), 1)
    half_low = [(lane < head_dim).astype(LOW), (lane >= head_dim).astype(LOW)]
    half_f = [(lane < head_dim).astype(F32), (lane >= head_dim).astype(F32)]
    token = lax.broadcasted_iota(jnp.int32, (rows, 128), 0) < length
    half_valid = [jnp.where(token, half_f[j], 0.0).astype(LOW) for j in range(2)]
    valid_lanes = jnp.where(lax.broadcasted_iota(jnp.int32, (1, rows), 1) < length, 1.0, 0.0).astype(F32)
    spare = -rows % 128
    chunk = 2 * width
    chunks = ff // chunk

    def vec(s, r):
        return table[s, r : r + 1, :]

    def up_bias(s, c):
        begin = c * chunk
        row, col = begin // width, begin % width
        if col + chunk <= width:
            return table[s, BU + row : BU + row + 1, col : col + chunk]
        a = table[s, BU + row : BU + row + 1, col:width]
        b = table[s, BU + row + 1 : BU + row + 2, 0 : chunk - (width - col)]
        return jnp.concatenate([a, b], axis=1)

    def add_vec(s, r, value):
        gtable[s, r : r + 1, :] += value

    def add_up_bias(s, c, value):
        begin = c * chunk
        row, col = begin // width, begin % width
        if col + chunk <= width:
            gtable[s, BU + row : BU + row + 1, col : col + chunk] += value
        else:
            cut = width - col
            gtable[s, BU + row : BU + row + 1, col:width] += value[:, :cut]
            gtable[s, BU + row + 1 : BU + row + 2, 0 : chunk - cut] += value[:, cut:]

    def attn_forward(s, x, hat, i):
        rd = step_rows(i, few)
        nrm_ref, qkv_ref, prob_ref, ctx_ref = nrm1.at[s], qkv.at[s], prob.at[s], ctx.at[s]
        nrm = (hat * vec(s, G1) + vec(s, S1)).astype(LOW)
        nrm_ref[rd, :] = nrm
        mixed = mm(nrm, wqkv[s])
        q = (mixed[:, 0:width] + vec(s, BQ)).astype(LOW)
        k = mixed[:, width : 2 * width].astype(LOW)
        v = (mixed[:, 2 * width :] + vec(s, BV)).astype(LOW)
        qkv_ref[rd, 0:width] = q
        qkv_ref[rd, width : 2 * width] = k
        qkv_ref[rd, 2 * width :] = v
        images_out = []
        for m in range(few):
            mine = slice(rows * m, rows * (m + 1))
            parts = []
            for p in range(pairs):
                cols = slice(128 * p, 128 * p + 128)
                weights, sides = [], []
                for j in range(2):
                    keys = k[mine, cols] * half_low[j]
                    keys = jnp.concatenate([keys, keys[rows - spare :]], axis=0)
                    scores = mm_right(q[mine, cols], keys)
                    top = jnp.max(scores, axis=-1, keepdims=True)
                    e = jnp.exp2((scores - top) * (scale * 1.4426950408889634)).astype(LOW)
                    prob_ref[i * few + m, 2 * p + j] = e[:, :rows]
                    weights.append(e)
                    sides.append(jnp.concatenate([v[mine, cols] * half_valid[j], half_valid[j]], axis=1))
                    sides.append(jnp.zeros((spare, 256), LOW))
                total = mm(jnp.concatenate(weights, axis=1), jnp.concatenate(sides, axis=0))
                over = 1.0 / total[:, 128:]
                overs[s, rows_of(i * few + m), cols] = over.astype(LOW)
                parts.append((total[:, :128] * over).astype(LOW))
            images_out.append(jnp.concatenate(parts, axis=1))
        context = jnp.concatenate(images_out, axis=0)
        ctx_ref[rd, :] = context
        return x + mm(context, wout[s]) + vec(s, BO)

    def ff_forward(s, after, rd):
        hat, rstd, _ = normalize(after)
        hat2[s, rd, :] = hat.astype(LOW)
        nrm = (hat * vec(s, G2) + vec(s, S2)).astype(LOW)
        total = after + vec(s, BD)
        for c in range(chunks):
            cols = slice(chunk * c, chunk * c + chunk)
            pre = mm(nrm, wup[s, :, cols]) + up_bias(s, c)
            phi, slo = normal_parts(pre)
            h = (pre * phi).astype(LOW)
            hid[rd, cols] = h
            slope[rd, cols] = slo.astype(LOW)
            total = total + mm(h, wdown[s, cols, :])
        return total, rstd

    def ff_backward(s, g, rd, rstd):
        g_low = g.astype(LOW)
        add_vec(s, BD, colsum(g_low.astype(F32)))
        d_nrm = None
        for c in range(chunks):
            cols = slice(chunk * c, chunk * c + chunk)
            d_hid = mm_right(g_low, wdown[s, cols, :])
            d_pre = (d_hid * slope[rd, cols].astype(F32)).astype(LOW)
            slope[rd, cols] = d_pre
            add_up_bias(s, c, colsum(d_pre.astype(F32)))
            part = mm_right(d_pre, wup[s, :, cols])
            d_nrm = part if d_nrm is None else d_nrm + part
        hat = hat2[s, rd, :].astype(F32)
        add_vec(s, G2, colsum(d_nrm * hat))
        add_vec(s, S2, colsum(d_nrm))
        d_after = g + normalize_back(d_nrm * vec(s, G2), hat, rstd)
        low = d_after.astype(LOW)
        dal[rd, :] = low
        add_vec(s, BO, colsum(low.astype(F32)))
        return d_after

    def attn_backward(s, i):
        qkv_ref, prob_ref, ctx_ref = qkv.at[s], prob.at[s], ctx.at[s]
        rd = step_rows(i, few)
        d_context = mm_right(dal[rd, :], wout[s])
        d_context = (d_context * overs[s, rd, :].astype(F32)).astype(LOW)
        for m in range(few):
            rd = rows_of(i * few + m)
            d_ctx = d_context[rows * m : rows * (m + 1)]
            dq, dk, dv = [], [], []
            for p in range(pairs):
                cols = slice(128 * p, 128 * p + 128)
                q = qkv_ref[rd, 128 * p : 128 * p + 128]
                k = qkv_ref[rd, width + 128 * p : width + 128 * p + 128]
                v = qkv_ref[rd, 2 * width + 128 * p : 2 * width + 128 * p + 128]
                dc = d_ctx[:, cols]
                both = dc.astype(F32) * ctx_ref[rd, cols].astype(F32)
                q_t, dc_t = q.T, dc.T
                to_q, to_k, to_v = None, [], []
                for j in range(2):
                    e = prob_ref[i * few + m, 2 * p + j]
                    delta = jnp.sum(both * half_f[j], axis=-1, keepdims=True)
                    d_prob = mm_right(dc, v * half_low[j])
                    ds = (e.astype(F32) * (d_prob - delta)).astype(LOW)
                    part = mm(ds, k * half_valid[j])
                    to_q = part if to_q is None else to_q + part
                    head = slice(head_dim * j, head_dim * (j + 1))
                    to_k.append(mm(q_t[head], ds))
                    to_v.append(mm(dc_t[head], e))
                dq.append((to_q * scale).astype(LOW))
                dk.append((jnp.concatenate(to_k, axis=0) * (valid_lanes * scale)).astype(LOW).T)
                dv.append((jnp.concatenate(to_v, axis=0) * valid_lanes).astype(LOW).T)
            d_mixed = jnp.concatenate(dq + dk + dv, axis=1)
            qkv_ref[rd, :] = d_mixed
            add_vec(s, BQ, colsum(d_mixed[:, 0:width].astype(F32)))
            add_vec(s, BV, colsum(d_mixed[:, 2 * width :].astype(F32)))

    def input_backward(s, d_after, rd, x, mean, rstd):
        d_nrm = mm_right(qkv[s, rd, :], wqkv[s])
        hat = (x - mean) * rstd
        add_vec(s, G1, colsum(d_nrm * hat))
        add_vec(s, S1, colsum(d_nrm))
        return d_after + normalize_back(d_nrm * vec(s, G1), hat, rstd)

    def grads_down(s):
        left_t[...] = low_g[...].T

        @pl.loop(0, 2)
        def _(c):
            cols = pl.ds(pl.multiple_of(c * 2 * width, 128), 2 * width)
            block = mm(left_t[...], hid[:, cols]).T
            for i in range(n // 2):
                for half in range(2):
                    begin = 4 * unit * i + 2 * unit * half
                    s_d[s, half, place(half, c * (n // 2) + i)] = block[begin : begin + 2 * unit].astype(LOW)

    def pair_out(ref, s, half, one, two):
        for j in range(n):
            down = slice(unit * j, unit * (j + 1))
            piece = jnp.concatenate([one[down], two[down]], axis=0).astype(LOW)
            ref[s, half, place(half, j)] = piece

    def grads_up(s):
        left_t[...] = (hat2[s].astype(F32) * vec(s, G2) + vec(s, S2)).astype(LOW).T
        for half in range(2):
            both = mm(left_t[...], slope[:, 2 * half * width : 2 * (half + 1) * width])
            pair_out(s_u, s, half, both[:, :width], both[:, width:])

    def grads_attn(s):
        mix_s = qkv.at[s]
        left_t[...] = ctx[s].T
        four = mm(left_t[...], dal[...])
        left_t[...] = nrm1[s].T
        three = mm(left_t[...], mix_s[:, 2 * width :])
        pair_out(s_a, s, 1, three, four)
        both = mm(left_t[...], mix_s[:, 0 : 2 * width])
        pair_out(s_a, s, 0, both[:, :width], both[:, width:])

    barrier = pltpu.get_barrier_semaphore()
    greeted = [sibling]
    greeted += [{"section": half, **peer_first(t)} for t in range(1, first) for half in range(2)]
    greeted += [peer_plane(three, two) for three, two in plane]
    for device in greeted:
        pl.semaphore_signal(barrier, inc=1, device_id=device, device_id_type=pl.DeviceIdType.MESH)
    pack_own()
    pl.semaphore_wait(barrier, len(greeted))

    def run(*todo):
        for f, b, g in todo:
            f(b, g)

    def events(i, table_of):
        for when, todo in table_of.items():
            @pl.when(i == when)
            def _():
                run(*todo)

    def both(f, b, g):
        return [(f, b, g), (f, b, TAB)]

    def take(i, m):
        return pl.ds(pl.multiple_of((i * many + m) * rows, 16), length)

    ahead = raw.shape[0]
    run(*both(ag1, 0, ATT))
    for i in range(ahead):
        coming(0, i).start()
    fill_repeats()
    gtable[...] = jnp.zeros_like(gtable)
    low_g[...] = jnp.zeros_like(low_g)
    xs[0] = jnp.zeros_like(low_g)

    @pl.loop(0, slots)
    def images_in(i):
        take_in(0, i)

        @pl.when(i + ahead < slots)
        def _():
            coming(0, i + ahead).start()

        @pl.when(i + ahead >= slots)
        def _():
            coming(1, i + ahead - slots).start()

        @pl.when(i == 3)
        def _():
            run(*both(ag2, 0, ATT), (ag1, 0, UP), (ag1, 0, DOWN))

    def statistic(s, rd, which):
        return jnp.where(s == 0, rstds[rd, which : which + 1], rstds[rd, 3 + which : 4 + which])

    def first_norm(s, rd, x):
        hat, rstd, mean = normalize(x)
        after_ref[rd, :] = hat
        rstds[rd, 3 * s : 3 * s + 1] = rstd
        rstds[rd, 3 * s + 2 : 3 * s + 3] = mean

    @pl.loop(0, slots // many)
    def norm_one(i):
        for m in range(many):
            xs[0, take(i, m), :] = io_one[i * many + m]
        rd = step_rows(i, many)
        x = xs[0, rd, :].astype(F32)
        token_rows = lax.broadcasted_iota(jnp.int32, (rows, width), 0) < length
        parts = [x[rows * m : rows * (m + 1)] for m in range(many)]
        x = jnp.concatenate([jnp.where(token_rows, part, part[0:1]) for part in parts], axis=0)
        xs[0, rd, :] = x.astype(LOW)
        first_norm(0, rd, x)

    run(*both(ag3, 0, ATT), (ag2, 0, UP), *both(ag1, 1, ATT), (ag2, 0, DOWN), (ag1, 1, UP), (ag1, 1, DOWN))

    @pl.loop(0, slots)
    def cotangents_in(i):
        take_in(1, i)

        @pl.when(i + ahead < slots)
        def _():
            coming(1, i + ahead).start()

    run(*both(ag4, 0, ATT), (ag3, 0, UP), *both(ag5, 0, ATT))

    @pl.loop(0, 2)
    def forward(s):
        @pl.loop(0, slots // few)
        def attention(i):
            @pl.when(s == 0)
            def _():
                events(i, {
                    0: [(ag3, 0, DOWN), *both(ag2, 1, ATT)],
                    1: [(ag4, 0, UP), (ag2, 1, UP)],
                    2: [(ag4, 0, DOWN)],
                })

            @pl.when(s == 1)
            def _():
                events(i, {2: [(ag4, 1, DOWN)]})

            rd = step_rows(i, few)
            after_ref[rd, :] = attn_forward(s, xs[s, rd, :].astype(F32), after_ref[rd, :], i)

        @pl.when(s == 0)
        def _():
            run(*both(ag3, 1, ATT), (ag5, 0, UP), (ag5, 0, DOWN))

        @pl.when(s == 1)
        def _():
            run((ag5, 1, UP), (ag5, 1, DOWN))

        @pl.loop(0, slots // many)
        def feed_forward(i):
            @pl.when(s == 0)
            def _():
                events(i, {0: [(ag3, 1, UP), (ag2, 1, DOWN)], 1: both(ag4, 1, ATT)})

            rd = step_rows(i, many)

            @pl.when(s == 1)
            def _():
                for m in range(many):
                    far_copy(0, i * many + m, False).wait()
                    far_copy(1, i * many + m, False).wait()
                    shipped(0, 0, i * many + m)

            out, rstd2 = ff_forward(s, after_ref[rd, :], rd)
            for block in range(2):
                @pl.when(s == block)
                def _():
                    rstds[rd, 3 * block + 1 : 3 * block + 2] = rstd2

            out = only_live(i, out, many)
            for m in range(many):
                io_one[i * many + m] = out[rows * m : rows * m + length].astype(LOW)
                ship(0, s, i * many + m)

            @pl.when(s == 0)
            def _():
                for m in range(many):
                    far_copy(0, i * many + m, False).start()
                    far_copy(1, i * many + m, False).start()
                low = out.astype(LOW)
                xs[1, rd, :] = low
                first_norm(1, rd, low.astype(F32))

        @pl.when(s == 0)
        def _():
            run((ag4, 1, UP), (ag3, 1, DOWN), *both(ag5, 1, ATT))

    for b in range(2):
        for g in groups:
            ag_sent(b, g)

    @pl.loop(0, 2)
    def backward(turn):
        s = 1 - turn

        @pl.loop(0, slots // many)
        def feed_forward(i):
            @pl.when(s == 0)
            def _():
                events(i, {1: [(rs1, 1, TAB), (rs4, 1, UP)]})
                for m in range(many):
                    far_copy(1, i * many + m, True).wait()

            rd = step_rows(i, many)
            for m in range(many):
                g = live(i * many + m) * io_two[i * many + m].astype(F32)
                low_g[take(i, m), :] = g.astype(LOW)
            after_ref[rd, :] = ff_backward(s, low_g[rd, :].astype(F32), rd, statistic(s, rd, 1))

        @pl.when(s == 0)
        def _():
            for i in range(slots):
                far_copy(0, i, True).wait()
            run((rs3, 1, ATT))

        grads_down(s)
        run((rs0, s, DOWN))

        @pl.when(s == 1)
        def _():
            for i in range(slots):
                far_copy(0, i, True).start()

        grads_up(s)
        run((rs0, s, UP), (rs1, s, DOWN))

        @pl.when(s == 1)
        def _():
            for i in range(slots):
                far_copy(1, i, True).start()

        @pl.when(s == 0)
        def _():
            run((rs3, 1, TAB))

        @pl.loop(0, slots // few)
        def attention(i):
            events(i, {1: [(rs1, s, UP), (rs2, s, DOWN)], 2: [(rs2, s, UP), (rs3, s, DOWN)]})

            @pl.when(s == 0)
            def _():
                events(i, {1: both(rs4, 1, ATT)})

            attn_backward(s, i)

        grads_attn(s)
        run((rs0, s, ATT), (rs3, s, UP))

        @pl.loop(0, slots // many)
        def to_input(i):
            events(i, {1: [(rs1, s, ATT), (rs4, s, DOWN)]})
            rd = step_rows(i, many)
            x = xs[s, rd, :].astype(F32)
            d_in = input_backward(s, after_ref[rd, :], rd, x, statistic(s, rd, 2), statistic(s, rd, 0))
            for m in range(many):
                @pl.when(s == 0)
                def _():
                    shipped(1, 1, i * many + m)

                io_two[i * many + m] = d_in[rows * m : rows * m + length].astype(LOW)
                ship(1, s, i * many + m)

        table_out(s)
        run((rs0, s, TAB))

    run((rs4, 0, UP), (rs1, 0, TAB))

    @pl.loop(0, slots)
    def acts_out(i):
        shipped(0, 1, i)
        for b in range(2):
            landed(0, b, i)

    weave(0)
    run((rs3, 0, ATT), (rs3, 0, TAB))

    @pl.loop(0, slots)
    def ings_out(i):
        shipped(1, 0, i)
        for b in range(2):
            landed(1, b, i)

    weave(1)
    run(*both(rs4, 0, ATT))
    for b in range(2):
        for g in groups:
            rs_sent(b, g)


def output_kernel(
    acts, ings, f_a, f_u, f_d, f_t, o_acts, o_ings, o_g1, o_s1, o_qkv, o_qv, o_out, o_bo, o_g2, o_s2, o_up, o_bu, o_down, o_bd, passing, sems
):
    arriving, leaving = [], []
    for which, (source, target) in enumerate(((acts, o_acts), (ings, o_ings))):
        for i in range(acts.shape[0]):
            arriving.append(pltpu.make_async_copy(source.at[i], passing.at[which, i], sems.at[0, which, i]))
            leaving.append(pltpu.make_async_copy(passing.at[which, i], target.at[i], sems.at[1, which, i]))
    for copy in arriving:
        copy.start()
    for one, two in zip(arriving, leaving):
        one.wait()
        two.start()
    unit, width = o_out.shape[1:]
    for half in range(2):
        o_down[0, 2 * unit * half : 2 * unit * (half + 1), :] = f_d[half]
        for sub in range(2):
            part = 2 * half + sub
            cols = slice(part * width, (part + 1) * width)
            o_up[0, :, cols] = f_u[half, unit * sub : unit * (sub + 1), :]
            piece = f_a[half, unit * sub : unit * (sub + 1), :]
            if part == 3:
                o_out[0] = piece
            else:
                o_qkv[0, :, cols] = piece
    begin = 0
    for out in (o_g1, o_s1, o_bo, o_g2, o_s2, o_bd, o_qv):
        part = out.shape[1]
        out[...] = f_t[0, :, begin : begin + part]
        begin += part
    o_bu[...] = f_t[1, :, 0 : o_bu.shape[1]]
    for copy in leaving:
        copy.wait()


def local(
    images, cotangent, counts,
    ln1_gain, ln1_bias, w_qkv, b_qv, w_out, b_out, ln2_gain, ln2_bias, w_up, b_up, w_down, b_down,
):
    micro_count, slots, length, width = images.shape
    ff = w_up.shape[2]
    rows = -(-length // 16) * 16
    n = lax.axis_size("fsdp")
    unit = width // n
    first, rest = radices(n)
    total = slots * rows
    head_dim = width // HEADS

    def vm(*shape, kind=LOW):
        return pltpu.VMEM(shape, kind)

    tall = [(2 * unit, LOW)] * 3 + [(1, F32)]
    dma = lambda *shape: pltpu.SemaphoreType.DMA(shape)
    outs = [((slots, length, 2, width), LOW)] * 2
    outs += [((2, r, width), F32) for r, _ in tall] + [((total, ff), LOW)] * 2 + [((2, slots, length, width), LOW)] * 2
    scratch = [
        vm(2, total, width), vm(3, length, 2, width), vm(slots, length, width), vm(slots, length, width),
        *[vm(2, r, width, kind=kind) for r, kind in tall],
        vm(2, width, 3 * width), vm(2, width, width), vm(2, width, ff), vm(2, ff, width),
        vm(2, TABLE, width, kind=F32), vm(2, TABLE, width, kind=F32),
        vm(unit, width), vm(2 * unit, 2 * width), vm(4 * unit, 4 * width),
        vm(total, width, kind=F32), vm(2, total, width), vm(2, total, 3 * width), vm(2, slots, HEADS, rows, rows),
        vm(2, total, width),
        vm(2, total, width), vm(2, total, width), vm(total, 6, kind=F32),
        vm(total, ff), vm(total, ff), vm(total, width), vm(total, width), vm(width, total),
    ]
    scratch += [vm(2, 2, n, r, width, kind=kind) for r, kind in tall]
    scratch += [vm(n, r, width, kind=kind) for r, kind in tall]
    plane = rest * rest - 1
    for g, (r, kind) in enumerate(tall):
        direct = g in (ATT, TAB)
        scratch.append(vm(*((plane, first) if direct else (rest - 1, rest * first)), r, width, kind=kind))
    scratch += [vm(2, rest - 1, first, *tall[g][:1], width) for g in (UP, DOWN)]
    scratch += [vm(2, first, r, width, kind=kind) for r, kind in tall]
    scratch += [dma(2, slots), dma(2, 2, slots), dma(2, slots), dma(4, slots), dma(4, slots), dma(4, slots)]
    scratch += [dma(4, 2, first), dma(8, first)] + [dma(8, rest - 1)] * 4 + [dma(8, rest)] * 2
    scratch += [dma(8)] * 2 + [dma(8, plane)] * 2 + [dma(8, rest - 1)] * 2 + [dma(8, first), dma(4, 2, first)]
    scratch += [pltpu.SemaphoreType.REGULAR((2, 4))]
    dims = (slots, length, rows, width, ff, head_dim, n)
    vmem = pl.BlockSpec(memory_space=pltpu.VMEM)
    hbm = pl.BlockSpec(memory_space=pltpu.HBM)
    acts, ings, f_a, f_u, f_d, f_t, *_ = pl.pallas_call(
        functools.partial(whole_kernel, dims),
        out_shape=[jax.ShapeDtypeStruct(*o) for o in outs],
        in_specs=[hbm, hbm, pl.BlockSpec(memory_space=pltpu.SMEM)] + [vmem] * 12,
        out_specs=[hbm, hbm] + [vmem] * 4 + [hbm] * 4,
        scratch_shapes=scratch,
        compiler_params=pltpu.CompilerParams(
            vmem_limit_bytes=(64 << 20) - (96 << 10), collective_id=0, has_side_effects=True
        ),
    )(
        images.transpose(1, 2, 0, 3), cotangent.transpose(1, 2, 0, 3), counts.T, ln1_gain, ln1_bias, b_out, ln2_gain, ln2_bias, b_down, b_qv, b_up,
        w_qkv, w_out, w_up, w_down,
    )

    params = (
        ln1_gain, ln1_bias, w_qkv, b_qv, w_out, b_out, ln2_gain, ln2_bias, w_up, b_up, w_down, b_down
    )
    acts, ings, *grads = pl.pallas_call(
        output_kernel,
        out_shape=[jax.ShapeDtypeStruct(v.shape, v.dtype) for v in (acts, ings)]
        + [jax.ShapeDtypeStruct(p.shape, F32) for p in params],
        in_specs=[hbm] * 2 + [vmem] * 4,
        out_specs=[hbm] * 2 + [vmem] * len(params),
        scratch_shapes=[vm(2, slots, length, 2, width), dma(2, 2, slots)],
        compiler_params=pltpu.CompilerParams(vmem_limit_bytes=24 << 20),
    )(acts, ings, f_a, f_u, f_d, f_t)

    def as_given(value):
        return value.transpose(2, 0, 1, 3)[None]

    return (as_given(acts), as_given(ings), *grads)


def solution(mesh):
    split = P("section", "fsdp")
    cube = P("section", "fsdp", None)
    image = P(None, "fsdp", None, None)
    result = P("section", None, "fsdp", None, None)
    params = (split, split, cube, split, cube, split, split, split, cube, split, cube, split)
    return jax.shard_map(
        local,
        mesh=mesh,
        in_specs=(image, image, P(None, "fsdp")) + params,
        out_specs=(result, result) + params,
        check_vma=False,
    )
```

```python
import functools
import math

import jax
import jax.numpy as jnp
from jax import lax
from jax.experimental import pallas as pl
from jax.experimental.pallas import tpu as pltpu
from jax.sharding import PartitionSpec as P

HEADS = 6
EPS = 1e-06
F32 = jnp.float32
LOW = jnp.bfloat16

G1, S1, BO, G2, S2, BD, BQ, BV, BU = 0, 1, 2, 3, 4, 5, 6, 7, 8
TABLE = 16
TOGETHER, TOGETHER_ROWS = 2, 3
ATT, UP, DOWN, TAB = 0, 1, 2, 3


def radices(n):
    rest = max(r for r in range(1, n + 1) if r * r * r <= n and n % (r * r) == 0)
    return n // (rest * rest), rest


def mm(left, right):
    return jnp.dot(left, right, preferred_element_type=F32)


def mm_right(left, right):
    return lax.dot_general(left, right, (((1,), (1,)), ((), ())), preferred_element_type=F32)


def mm_left(left, right):
    return lax.dot_general(left, right, (((0,), (0,)), ((), ())), preferred_element_type=F32)


def normal_parts(pre):
    phi = 0.5 + 0.5 * lax.erf(pre * 0.7071067811865476)
    density = jnp.exp2(pre * pre * (-0.5 * 1.4426950408889634)) * 0.3989422804014327
    return phi, phi + pre * density


def normalize(value):
    mean = jnp.mean(value, axis=-1, keepdims=True)
    center = value - mean
    rstd = lax.rsqrt(jnp.mean(center * center, axis=-1, keepdims=True) + EPS)
    return center * rstd, rstd, mean


def normalize_back(d_hat, hat, rstd):
    mean_one = jnp.mean(d_hat, axis=-1, keepdims=True)
    mean_two = jnp.mean(d_hat * hat, axis=-1, keepdims=True)
    return rstd * (d_hat - mean_one - hat * mean_two)


def colsum(value):
    return jnp.sum(value, axis=0, keepdims=True)


def whole_kernel(dims, *refs):
    slots, length, rows, width, ff, head_dim, n = dims
    (
        images, cotangent, counts, v_g1, v_s1, v_bo, v_g2, v_s2, v_bd, v_qv, v_up, a_qkv, a_out, a_up, a_down,
        woven, f_a, f_u, f_d, f_t, hid_far, slope_far, out_far,
        xs, raw, io_one, io_two, pack_a, pack_u, pack_d, pack_t,
        wqkv, wout, wup, wdown, table, gtable, rep_one, rep_two, rep_four,
        after_ref, nrm1, qkv, prob, overs, ctx, hat2, rstds, hid, slope, dal, low_g, left_t,
        s_a, s_u, s_d, s_t, r0_a, r0_u, r0_d, r0_t, r1_a, r1_u, r1_d, r1_t, r2_u, r2_d,
        r3_a, r3_u, r3_d, r3_t,
        in_s, weave_in, weave_out, ship_s, ship_r, far_s, ag1_s, ag1_r, ag2_s, ag2_r, ag3_s, ag3_r, ag4_s, ag4_r,
        rs0_s, rs0_r, rs1_s, rs1_r, rs2_s, rs2_r, rs3_s, rs3_r, credit,
    ) = refs
    groups = (ATT, UP, DOWN, TAB)
    pack = (pack_a, pack_u, pack_d, pack_t)
    stage = (s_a, s_u, s_d, s_t)
    r0, r1, r2 = (r0_a, r0_u, r0_d, r0_t), (r1_a, r1_u, r1_d, r1_t), (None, r2_u, r2_d, None)
    r3, final = (r3_a, r3_u, r3_d, r3_t), (f_a, f_u, f_d, f_t)

    first, rest = radices(n)
    unit = width // n
    core = lax.axis_index("section")
    me = lax.axis_index("fsdp")
    dig_a, dig_b, dig_c = me // (rest * rest), (me // rest) % rest, me % rest
    dig_three, dig_two = dig_c + core * (dig_b - dig_c), dig_b + core * (dig_c - dig_b)
    step_three, step_two = 1 + core * (rest - 1), rest - core * (rest - 1)
    pos = (dig_three * rest + dig_two) * first + dig_a
    pos_of = ((dig_c * rest + dig_b) * first + dig_a, (dig_b * rest + dig_c) * first + dig_a)
    sibling = {"section": 1 - core}

    def place(half, j):
        a, b, c = j // (rest * rest), (j // rest) % rest, j % rest
        return ((c * rest + b) if half == 0 else (b * rest + c)) * first + a

    def peer_first(t):
        return {"fsdp": me + ((dig_a + t) % first - dig_a) * (rest * rest)}

    def peer_two(t):
        return {"fsdp": me + ((dig_two + t) % rest - dig_two) * step_two}

    def peer_three(t):
        return {"fsdp": me + ((dig_three + t) % rest - dig_three) * step_three}

    def peer_plane(three, two):
        here = ((dig_three + three) % rest - dig_three) * step_three
        return {"fsdp": me + here + ((dig_two + two) % rest - dig_two) * step_two}

    plane = [(three, two) for three in range(rest) for two in range(rest) if three or two]

    def remote(src, dst, s_sem, r_sem, device):
        return pltpu.make_async_remote_copy(
            src_ref=src, dst_ref=dst, send_sem=s_sem, recv_sem=r_sem, device_id=device,
            device_id_type=pl.DeviceIdType.MESH,
        )

    def slab_two(three, two):
        return pl.ds((three * rest + two) * first, first)

    def slab_three(three):
        return pl.ds(three * rest * first, rest * first)

    def fill_repeats():
        for ref in (rep_one, rep_two, rep_four):
            part = ref.shape[0]
            lanes = lax.broadcasted_iota(jnp.int32, ref.shape, 1).astype(F32)
            line = lax.broadcasted_iota(jnp.int32, ref.shape, 0).astype(F32)
            rest_of = lanes - part * jnp.floor((lanes + 0.5) * (1.0 / part))
            ref[...] = jnp.where(jnp.abs(rest_of - line) < 0.5, 1.0, 0.0).astype(LOW)

    def own_lanes(part):
        shape = (n, part * n)
        lanes = lax.broadcasted_iota(jnp.int32, shape, 1)
        begin = lax.broadcasted_iota(jnp.int32, shape, 0) * part
        return (lanes >= begin) & (lanes < begin + part)

    shares = (
        ((G1, unit, rep_one), (S1, unit, rep_one), (BO, unit, rep_one), (G2, unit, rep_one), (S2, unit, rep_one),
         (BD, unit, rep_one), (BQ, 2 * unit, rep_two)),
        ((BU, 4 * unit, rep_four),),
    )

    def table_in(b):
        for half in range(2):
            lines = jnp.concatenate([s_t[b, half, place(half, j)] for j in range(n)], axis=0)
            begin = 0
            for row, part, ref in shares[half]:
                spread = mm(lines[:, begin : begin + part].astype(LOW), ref[...])
                line = colsum(jnp.where(own_lanes(part), spread, 0.0))
                for i in range(part * n // width):
                    table[b, row + i : row + i + 1, :] = line[:, width * i : width * (i + 1)]
                begin += part

    def table_out(b):
        for half in range(2):
            parts, begin = [], 0
            for row, part, ref in shares[half]:
                count = part * n // width
                line = jnp.concatenate([gtable[b, row + i : row + i + 1, :] for i in range(count)], axis=1)
                parts.append(mm_right(jnp.where(own_lanes(part), line, 0.0).astype(LOW), ref[...]))
                begin += part
            parts.append(jnp.zeros((n, width - begin), F32))
            lines = jnp.concatenate(parts, axis=1)
            for j in range(n):
                s_t[b, half, place(half, j)] = lines[j : j + 1]

    def pack_own():
        for half in range(2):
            vectors = ((v_g1, v_s1, v_bo, v_g2, v_s2, v_bd, v_qv), (v_up,))[half]
            lines = [vector[...].astype(F32) for vector in vectors]
            lines.append(jnp.zeros((1, width - sum(line.shape[1] for line in lines)), F32))
            pack_t[half] = jnp.concatenate(lines, axis=1)
            for ref in (pack_a, pack_u):
                both = []
                for part in (2 * half, 2 * half + 1):
                    if ref is pack_u:
                        both.append(a_up[0, :, part * width : (part + 1) * width])
                    elif part == 3:
                        both.append(a_out[0])
                    else:
                        both.append(a_qkv[0, :, part * width : (part + 1) * width])
                ref[half] = jnp.concatenate([value.astype(F32) for value in both], axis=0).astype(LOW)
            pack_d[half] = a_down[0, 2 * unit * half : 2 * unit * (half + 1), :]

    def at(b, g):
        return len(groups) * b + g

    def ag1_copy(b, g, half, t):
        device = {"section": half, **peer_first(t)} if t else sibling
        return remote(
            pack[g].at[half], stage[g].at[b, half, pos_of[half]],
            ag1_s.at[g, half, t], ag1_r.at[at(b, g), t], device,
        )

    def ag1_landing(b, g, t):
        ref = stage[g].at[b, core, (dig_three * rest + dig_two) * first + (dig_a + first - t) % first]
        return remote(ref, ref, ag1_s.at[g, 0, t], ag1_r.at[at(b, g), t], sibling)

    def ag2_copy(b, g, t):
        ref = stage[g].at[b, core, slab_two(dig_three, dig_two)]
        return remote(ref, ref, ag2_s.at[at(b, g), t - 1], ag2_r.at[at(b, g), t - 1], peer_two(t))

    def ag3_copy(b, g, t):
        ref = stage[g].at[b, core, slab_three(dig_three)]
        return remote(ref, ref, ag3_s.at[at(b, g), t - 1], ag3_r.at[at(b, g), t - 1], peer_three(t))

    def ag4_copy(b, g, t):
        ref = stage[g].at[b, core, slab_three((dig_three + rest - t) % rest)]
        return remote(ref, ref, ag4_s.at[at(b, g), t], ag4_r.at[at(b, g), t], sibling)

    def ag4_landing(b, g, t):
        ref = stage[g].at[b, 1 - core, slab_three((dig_two + rest - t) % rest)]
        return remote(ref, ref, ag4_s.at[at(b, g), t], ag4_r.at[at(b, g), t], sibling)

    def ag1(b, g):
        @pl.when(core == b)
        def _():
            for t in range(1, first):
                for half in range(2):
                    ag1_copy(b, g, half, t).start()
            ag1_copy(b, g, 1 - b, 0).start()
            stage[g][b, b, pos] = pack[g][b]

    def ag2(b, g):
        for t in range(1, first):
            ag1_landing(b, g, t).wait_recv()

        @pl.when(core != b)
        def _():
            ag1_landing(b, g, 0).wait_recv()

        for t in range(1, rest):
            ag2_copy(b, g, t).start()

    def ag3(b, g):
        for t in range(1, rest):
            ag2_copy(b, g, t).wait_recv()
        for t in range(1, rest):
            ag3_copy(b, g, t).start()
        ag4_copy(b, g, 0).start()

    def ag4(b, g):
        for t in range(1, rest):
            ag3_copy(b, g, t).wait_recv()
            ag4_copy(b, g, t).start()

    def ag5(b, g):
        for t in range(rest):
            ag4_landing(b, g, t).wait_recv()
        lay_out(b, g)

    def ag_sent(b, g):
        @pl.when(core == b)
        def _():
            for t in range(1, first):
                for half in range(2):
                    ag1_copy(b, g, half, t).wait_send()
            ag1_copy(b, g, 1 - b, 0).wait_send()

        for t in range(1, rest):
            ag2_copy(b, g, t).wait_send()
            ag3_copy(b, g, t).wait_send()
        for t in range(rest):
            ag4_copy(b, g, t).wait_send()

    def lay_out(b, g):
        if g == TAB:
            table_in(b)
            return
        if g == DOWN:
            for j in range(n):
                for half in range(2):
                    begin = 4 * unit * j + 2 * unit * half
                    wdown[b, begin : begin + 2 * unit, :] = s_d[b, half, place(half, j)]
            return
        together = 16 // math.gcd(unit, 16)
        for half in range(2):
            for j in range(0, n, together):
                pieces = [stage[g][b, half, place(half, j + i)].astype(F32) for i in range(together)]
                for sub in range(2):
                    low = sub * unit
                    block = jnp.concatenate([piece[low : low + unit] for piece in pieces], axis=0).astype(LOW)
                    part = 2 * half + sub
                    down = slice(unit * j, unit * (j + together))
                    if g == UP:
                        wup[b, down, part * width : (part + 1) * width] = block
                    elif part == 3:
                        wout[b, down, :] = block
                    else:
                        wqkv[b, down, part * width : (part + 1) * width] = block

    def rs0_copy(b, g):
        return remote(stage[g].at[b, 1 - core], r0[g], rs0_s.at[at(b, g)], rs0_r.at[at(b, g)], sibling)

    def rs1_copy(b, g, t):
        return remote(
            stage[g].at[b, core, slab_three((dig_three + t) % rest)], r1[g].at[t - 1],
            rs1_s.at[at(b, g), t - 1], rs1_r.at[at(b, g), t - 1], peer_three(t),
        )

    def rs2_copy(b, g, t):
        return remote(
            stage[g].at[b, core, slab_two(dig_three, (dig_two + t) % rest)], r2[g].at[b, t - 1],
            rs2_s.at[at(b, g), t - 1], rs2_r.at[at(b, g), t - 1], peer_two(t),
        )

    def rs3_copy(b, g, t):
        there = (dig_three * rest + dig_two) * first + (dig_a + t) % first
        device = {"section": b, **peer_first(t)} if t else sibling
        return remote(
            stage[g].at[b, core, there], r3[g].at[core, t], rs3_s.at[at(b, g), t], rs3_r.at[g, core, t], device
        )

    def plane_copy(b, g, t):
        three, two = plane[t]
        return remote(
            stage[g].at[b, core, slab_two((dig_three + three) % rest, (dig_two + two) % rest)], r1[g].at[t],
            rs1_s.at[at(b, g), t], rs1_r.at[at(b, g), t], peer_plane(three, two),
        )

    def rs0(b, g):
        @pl.when(b == 0)
        def _():
            pl.semaphore_wait(credit.at[0, g], 1)

        rs0_copy(b, g).start()

    def rs1(b, g):
        rs0_copy(b, g).wait_recv()

        @pl.loop(0, n)
        def _(p):
            stage[g][b, core, p] = stage[g][b, core, p] + r0[g][p]

        @pl.when(b == 1)
        def _():
            pl.semaphore_signal(credit.at[0, g], inc=1, device_id=sibling, device_id_type=pl.DeviceIdType.MESH)

        direct = g in (ATT, TAB)
        if rest > 1:
            @pl.when(b == 0)
            def _():
                pl.semaphore_wait(credit.at[1, g], len(plane) if direct else rest - 1)

        if direct:
            for t in range(len(plane)):
                plane_copy(b, g, t).start()
            return
        for t in range(1, rest):
            rs1_copy(b, g, t).start()

    def rs2(b, g):
        for t in range(1, rest):
            rs1_copy(b, g, t).wait_recv()

        @pl.loop(0, rest * first)
        def _(p):
            here = dig_three * rest * first + p
            total = stage[g][b, core, here].astype(F32)
            for t in range(1, rest):
                total = total + r1[g][t - 1, p].astype(F32)
            stage[g][b, core, here] = total.astype(stage[g].dtype)

        for t in range(1, rest):
            @pl.when(b == 1)
            def _():
                pl.semaphore_signal(
                    credit.at[1, g], inc=1, device_id=peer_three(t), device_id_type=pl.DeviceIdType.MESH
                )

            rs2_copy(b, g, t).start()

    def rs3(b, g):
        direct = g in (ATT, TAB)
        copies = [plane_copy(b, g, t) for t in range(len(plane))] if direct else [
            rs2_copy(b, g, t) for t in range(1, rest)
        ]
        landing = r1[g] if direct else r2[g].at[b]
        for copy in copies:
            copy.wait_recv()

        @pl.loop(0, first)
        def _(p):
            here = (dig_three * rest + dig_two) * first + p
            total = stage[g][b, core, here].astype(F32)
            for t in range(len(copies)):
                total = total + landing[t, p].astype(F32)
            stage[g][b, core, here] = total.astype(stage[g].dtype)

        if direct:
            @pl.when(b == 1)
            def _():
                for three, two in plane:
                    pl.semaphore_signal(
                        credit.at[1, g], inc=1, device_id=peer_plane(three, two),
                        device_id_type=pl.DeviceIdType.MESH,
                    )


        for t in range(1, first):
            rs3_copy(b, g, t).start()

        @pl.when(core != b)
        def _():
            rs3_copy(b, g, 0).start()

    def rs4(b, g):
        @pl.when(core == b)
        def _():
            for own in (True, False):
                half = core if own else 1 - core
                begin = int(own)
                for t in range(begin, first):
                    ref = r3[g].at[half, t]
                    remote(ref, ref, rs3_s.at[at(b, g), t], rs3_r.at[g, half, t], sibling).wait_recv()
                total = stage[g][b, core, pos].astype(F32) if own else None
                for t in range(begin, first):
                    value = r3[g][half, t].astype(F32)
                    total = value if total is None else total + value
                final[g][half] = total

    def rs_sent(b, g):
        rs0_copy(b, g).wait_send()
        if g in (ATT, TAB):
            for t in range(len(plane)):
                plane_copy(b, g, t).wait_send()
        else:
            for t in range(1, rest):
                rs1_copy(b, g, t).wait_send()
                rs2_copy(b, g, t).wait_send()
        for t in range(1, first):
            rs3_copy(b, g, t).wait_send()

        @pl.when(core != b)
        def _():
            rs3_copy(b, g, 0).wait_send()

    def rows_of(i, images_too=1):
        return pl.ds(pl.multiple_of(i * rows, 16), images_too * rows)

    few = TOGETHER if slots % TOGETHER == 0 else 1
    many = TOGETHER_ROWS if slots % TOGETHER_ROWS == 0 else 1

    def step_rows(i, count):
        return rows_of(i * count, count)

    def ship_parts(kind, b, i):
        src, out = (io_one, io_two)[kind].at[i], out_far.at[kind, core, i]
        q = 2 * kind + b
        near = pltpu.make_async_copy(src, out, ship_s.at[q, i])
        far = remote(src, out, ship_s.at[q, i], ship_r.at[q, i], sibling)
        return near, far

    def ship(kind, b, i):
        near, far = ship_parts(kind, b, i)

        @pl.when(core == b)
        def _():
            near.start()

        @pl.when(core != b)
        def _():
            far.start()

    def shipped(kind, b, i):
        near, far = ship_parts(kind, b, i)

        @pl.when(core == b)
        def _():
            near.wait()

        @pl.when(core != b)
        def _():
            far.wait_send()

    def landed(kind, b, i):
        q = 2 * kind + b
        ref = out_far.at[kind, 1 - core, i]

        @pl.when(core == b)
        def _():
            remote(ref, ref, ship_s.at[q, i], ship_r.at[q, i], sibling).wait_recv()

    def live(i):
        return jnp.where(i < counts[0, core], 1.0, 0.0).astype(F32)

    def only_live(i, value, count):
        parts = [value[rows * m : rows * (m + 1)] * live(i * count + m) for m in range(count)]
        return jnp.concatenate(parts, axis=0)

    def coming(which, i):
        slot = (which * slots + i) % raw.shape[0]
        return pltpu.make_async_copy((images, cotangent)[which].at[i], raw.at[slot], in_s.at[which, i])

    def take_in(which, i):
        coming(which, i).wait()
        both = raw[(which * slots + i) % raw.shape[0]].astype(F32)
        (io_one, io_two)[which][i] = jnp.where(core == 0, both[:, 0, :], both[:, 1, :]).astype(LOW)

    def weave(todo):
        ring = raw.shape[0]
        count = 2 * slots

        def fetch(t, m):
            source = out_far.at[t // slots, m, t % slots]
            return pltpu.make_async_copy(source, io_one.at[2 * (t % ring) + m], weave_in.at[m, t])

        def leave(t):
            return pltpu.make_async_copy(raw.at[t % ring], woven.at[t // slots, t % slots], weave_out.at[t])

        for t in range(ring - 1):
            for m in range(2):
                fetch(t, m).start()

        @pl.loop(0, count)
        def _(t):
            for when, act in todo.items():
                @pl.when(t == when)
                def _():
                    act()

            @pl.when(t + ring - 1 < count)
            def _():
                for m in range(2):
                    fetch(t + ring - 1, m).start()

            @pl.when(t >= ring)
            def _():
                leave(t - ring).wait()

            for m in range(2):
                fetch(t, m).wait()
                raw[t % ring, :, m, :] = io_one[2 * (t % ring) + m]
            leave(t).start()

        for t in range(count - ring, count):
            leave(t).wait()

    def far_copy(which, i, back):
        near, far = ((hid, hid_far), (slope, slope_far))[which]
        near, far = near.at[rows_of(i)], far.at[rows_of(i)]
        src, dst = (far, near) if back else (near, far)
        return pltpu.make_async_copy(src, dst, far_s.at[2 * int(back) + which, i])

    pairs = width // 128
    scale = head_dim ** -0.5
    lane = lax.broadcasted_iota(jnp.int32, (1, 128), 1)
    half_low = [(lane < head_dim).astype(LOW), (lane >= head_dim).astype(LOW)]
    half_f = [(lane < head_dim).astype(F32), (lane >= head_dim).astype(F32)]
    token = lax.broadcasted_iota(jnp.int32, (rows, 128), 0) < length
    half_valid = [jnp.where(token, half_f[j], 0.0).astype(LOW) for j in range(2)]
    valid_lanes = jnp.where(lax.broadcasted_iota(jnp.int32, (1, rows), 1) < length, 1.0, 0.0).astype(F32)
    spare = -rows % 128
    chunk = 2 * width
    chunks = ff // chunk

    def vec(s, r):
        return table[s, r : r + 1, :]

    def up_bias(s, c):
        begin = c * chunk
        row, col = begin // width, begin % width
        if col + chunk <= width:
            return table[s, BU + row : BU + row + 1, col : col + chunk]
        a = table[s, BU + row : BU + row + 1, col:width]
        b = table[s, BU + row + 1 : BU + row + 2, 0 : chunk - (width - col)]
        return jnp.concatenate([a, b], axis=1)

    def add_vec(s, r, value):
        gtable[s, r : r + 1, :] += value

    def add_up_bias(s, c, value):
        begin = c * chunk
        row, col = begin // width, begin % width
        if col + chunk <= width:
            gtable[s, BU + row : BU + row + 1, col : col + chunk] += value
        else:
            cut = width - col
            gtable[s, BU + row : BU + row + 1, col:width] += value[:, :cut]
            gtable[s, BU + row + 1 : BU + row + 2, 0 : chunk - cut] += value[:, cut:]

    def attn_forward(s, x, hat, i):
        rd = step_rows(i, few)
        nrm_ref, qkv_ref, prob_ref, ctx_ref = nrm1.at[s], qkv.at[s], prob.at[s], ctx.at[s]
        nrm = (hat * vec(s, G1) + vec(s, S1)).astype(LOW)
        nrm_ref[rd, :] = nrm
        mixed = mm(nrm, wqkv[s])
        q = (mixed[:, 0:width] + vec(s, BQ)).astype(LOW)
        k = mixed[:, width : 2 * width].astype(LOW)
        v = (mixed[:, 2 * width :] + vec(s, BV)).astype(LOW)
        qkv_ref[rd, 0:width] = q
        qkv_ref[rd, width : 2 * width] = k
        qkv_ref[rd, 2 * width :] = v
        images_out = []
        for m in range(few):
            mine = slice(rows * m, rows * (m + 1))
            parts = []
            for p in range(pairs):
                cols = slice(128 * p, 128 * p + 128)
                weights, sides = [], []
                for j in range(2):
                    keys = k[mine, cols] * half_low[j]
                    keys = jnp.concatenate([keys, keys[rows - spare :]], axis=0)
                    scores = mm_right(q[mine, cols], keys)
                    top = jnp.max(scores, axis=-1, keepdims=True)
                    e = jnp.exp2((scores - top) * (scale * 1.4426950408889634)).astype(LOW)
                    prob_ref[i * few + m, 2 * p + j] = e[:, :rows]
                    weights.append(e)
                    sides.append(jnp.concatenate([v[mine, cols] * half_valid[j], half_valid[j]], axis=1))
                    sides.append(jnp.zeros((spare, 256), LOW))
                total = mm(jnp.concatenate(weights, axis=1), jnp.concatenate(sides, axis=0))
                over = 1.0 / total[:, 128:]
                overs[s, rows_of(i * few + m), cols] = over.astype(LOW)
                parts.append((total[:, :128] * over).astype(LOW))
            images_out.append(jnp.concatenate(parts, axis=1))
        context = jnp.concatenate(images_out, axis=0)
        ctx_ref[rd, :] = context
        return x + mm(context, wout[s]) + vec(s, BO)

    def ff_forward(s, after, rd):
        hat, rstd, _ = normalize(after)
        hat2[s, rd, :] = hat.astype(LOW)
        nrm = (hat * vec(s, G2) + vec(s, S2)).astype(LOW)
        total = after + vec(s, BD)
        for c in range(chunks):
            cols = slice(chunk * c, chunk * c + chunk)
            pre = mm(nrm, wup[s, :, cols]) + up_bias(s, c)
            phi, slo = normal_parts(pre)
            h = (pre * phi).astype(LOW)
            hid[rd, cols] = h
            slope[rd, cols] = slo.astype(LOW)
            total = total + mm(h, wdown[s, cols, :])
        return total, rstd

    def ff_backward(s, g, rd, rstd):
        g_low = g.astype(LOW)
        add_vec(s, BD, colsum(g_low.astype(F32)))
        d_nrm = None
        for c in range(chunks):
            cols = slice(chunk * c, chunk * c + chunk)
            d_hid = mm_right(g_low, wdown[s, cols, :])
            d_pre = (d_hid * slope[rd, cols].astype(F32)).astype(LOW)
            slope[rd, cols] = d_pre
            add_up_bias(s, c, colsum(d_pre.astype(F32)))
            part = mm_right(d_pre, wup[s, :, cols])
            d_nrm = part if d_nrm is None else d_nrm + part
        hat = hat2[s, rd, :].astype(F32)
        add_vec(s, G2, colsum(d_nrm * hat))
        add_vec(s, S2, colsum(d_nrm))
        d_after = g + normalize_back(d_nrm * vec(s, G2), hat, rstd)
        low = d_after.astype(LOW)
        dal[rd, :] = low
        add_vec(s, BO, colsum(low.astype(F32)))
        return d_after

    def attn_backward(s, i):
        qkv_ref, prob_ref, ctx_ref = qkv.at[s], prob.at[s], ctx.at[s]
        rd = step_rows(i, few)
        d_context = mm_right(dal[rd, :], wout[s])
        d_context = (d_context * overs[s, rd, :].astype(F32)).astype(LOW)
        for m in range(few):
            rd = rows_of(i * few + m)
            d_ctx = d_context[rows * m : rows * (m + 1)]
            dq, dk, dv = [], [], []
            for p in range(pairs):
                cols = slice(128 * p, 128 * p + 128)
                q = qkv_ref[rd, 128 * p : 128 * p + 128]
                k = qkv_ref[rd, width + 128 * p : width + 128 * p + 128]
                v = qkv_ref[rd, 2 * width + 128 * p : 2 * width + 128 * p + 128]
                dc = d_ctx[:, cols]
                both = dc.astype(F32) * ctx_ref[rd, cols].astype(F32)
                q_t, dc_t = q.T, dc.T
                to_q, to_k, to_v = None, [], []
                for j in range(2):
                    e = prob_ref[i * few + m, 2 * p + j]
                    delta = jnp.sum(both * half_f[j], axis=-1, keepdims=True)
                    d_prob = mm_right(dc, v * half_low[j])
                    ds = (e.astype(F32) * (d_prob - delta)).astype(LOW)
                    part = mm(ds, k * half_valid[j])
                    to_q = part if to_q is None else to_q + part
                    head = slice(head_dim * j, head_dim * (j + 1))
                    to_k.append(mm(q_t[head], ds))
                    to_v.append(mm(dc_t[head], e))
                dq.append((to_q * scale).astype(LOW))
                dk.append((jnp.concatenate(to_k, axis=0) * (valid_lanes * scale)).astype(LOW).T)
                dv.append((jnp.concatenate(to_v, axis=0) * valid_lanes).astype(LOW).T)
            d_mixed = jnp.concatenate(dq + dk + dv, axis=1)
            qkv_ref[rd, :] = d_mixed
            add_vec(s, BQ, colsum(d_mixed[:, 0:width].astype(F32)))
            add_vec(s, BV, colsum(d_mixed[:, 2 * width :].astype(F32)))

    def input_backward(s, d_after, rd, x, mean, rstd):
        d_nrm = mm_right(qkv[s, rd, :], wqkv[s])
        hat = (x - mean) * rstd
        add_vec(s, G1, colsum(d_nrm * hat))
        add_vec(s, S1, colsum(d_nrm))
        return d_after + normalize_back(d_nrm * vec(s, G1), hat, rstd)

    def grads_down(s):
        left_t[...] = low_g[...].T

        @pl.loop(0, 2)
        def _(c):
            cols = pl.ds(pl.multiple_of(c * 2 * width, 128), 2 * width)
            block = mm(left_t[...], hid[:, cols]).T
            for i in range(n // 2):
                for half in range(2):
                    begin = 4 * unit * i + 2 * unit * half
                    s_d[s, half, place(half, c * (n // 2) + i)] = block[begin : begin + 2 * unit].astype(LOW)

    def pair_out(ref, s, half, one, two):
        for j in range(n):
            down = slice(unit * j, unit * (j + 1))
            piece = jnp.concatenate([one[down], two[down]], axis=0).astype(LOW)
            ref[s, half, place(half, j)] = piece

    def grads_up(s):
        left_t[...] = (hat2[s].astype(F32) * vec(s, G2) + vec(s, S2)).astype(LOW).T
        for half in range(2):
            both = mm(left_t[...], slope[:, 2 * half * width : 2 * (half + 1) * width])
            pair_out(s_u, s, half, both[:, :width], both[:, width:])

    def grads_attn(s):
        mix_s = qkv.at[s]
        left_t[...] = ctx[s].T
        four = mm(left_t[...], dal[...])
        left_t[...] = nrm1[s].T
        three = mm(left_t[...], mix_s[:, 2 * width :])
        pair_out(s_a, s, 1, three, four)
        both = mm(left_t[...], mix_s[:, 0 : 2 * width])
        pair_out(s_a, s, 0, both[:, :width], both[:, width:])

    barrier = pltpu.get_barrier_semaphore()
    greeted = [sibling]
    greeted += [{"section": half, **peer_first(t)} for t in range(1, first) for half in range(2)]
    greeted += [peer_plane(three, two) for three, two in plane]
    for device in greeted:
        pl.semaphore_signal(barrier, inc=1, device_id=device, device_id_type=pl.DeviceIdType.MESH)
    pack_own()
    pl.semaphore_wait(barrier, len(greeted))

    def run(*todo):
        for f, b, g in todo:
            f(b, g)

    def events(i, table_of):
        for when, todo in table_of.items():
            @pl.when(i == when)
            def _():
                run(*todo)

    def both(f, b, g):
        return [(f, b, g), (f, b, TAB)]

    def take(i, m):
        return pl.ds(pl.multiple_of((i * many + m) * rows, 16), length)

    ahead = raw.shape[0]
    run(*both(ag1, 0, ATT))
    for i in range(ahead):
        coming(0, i).start()
    fill_repeats()
    gtable[...] = jnp.zeros_like(gtable)
    low_g[...] = jnp.zeros_like(low_g)
    xs[0] = jnp.zeros_like(low_g)

    @pl.loop(0, slots)
    def images_in(i):
        take_in(0, i)

        @pl.when(i + ahead < slots)
        def _():
            coming(0, i + ahead).start()

        @pl.when(i + ahead >= slots)
        def _():
            coming(1, i + ahead - slots).start()

        @pl.when(i == 4)
        def _():
            run((ag1, 0, UP))

    run(*both(ag2, 0, ATT), (ag1, 0, DOWN), *both(ag1, 1, ATT))

    def statistic(s, rd, which):
        return jnp.where(s == 0, rstds[rd, which : which + 1], rstds[rd, 3 + which : 4 + which])

    def first_norm(s, rd, x):
        hat, rstd, mean = normalize(x)
        after_ref[rd, :] = hat
        rstds[rd, 3 * s : 3 * s + 1] = rstd
        rstds[rd, 3 * s + 2 : 3 * s + 3] = mean

    @pl.loop(0, slots // many)
    def norm_one(i):
        for m in range(many):
            xs[0, take(i, m), :] = io_one[i * many + m]
        rd = step_rows(i, many)
        x = xs[0, rd, :].astype(F32)
        token_rows = lax.broadcasted_iota(jnp.int32, (rows, width), 0) < length
        parts = [x[rows * m : rows * (m + 1)] for m in range(many)]
        x = jnp.concatenate([jnp.where(token_rows, part, part[0:1]) for part in parts], axis=0)
        xs[0, rd, :] = x.astype(LOW)
        first_norm(0, rd, x)

    run((ag2, 0, UP), *both(ag3, 0, ATT), (ag1, 1, UP), (ag1, 1, DOWN), (ag2, 0, DOWN), (ag3, 0, UP))

    @pl.loop(0, slots)
    def cotangents_in(i):
        take_in(1, i)

        @pl.when(i + ahead < slots)
        def _():
            coming(1, i + ahead).start()

    run(*both(ag4, 0, ATT), (ag3, 0, DOWN), *both(ag2, 1, ATT), *both(ag5, 0, ATT))

    @pl.loop(0, 2)
    def forward(s):
        @pl.loop(0, slots // few)
        def attention(i):
            @pl.when(s == 0)
            def _():
                events(i, {1: [(ag4, 0, UP), (ag2, 1, UP)], 2: [(ag4, 0, DOWN)]})

            @pl.when(s == 1)
            def _():
                events(i, {1: [(ag4, 1, UP)], 2: [(ag4, 1, DOWN)]})

            rd = step_rows(i, few)
            after_ref[rd, :] = attn_forward(s, xs[s, rd, :].astype(F32), after_ref[rd, :], i)

        @pl.when(s == 0)
        def _():
            run(*both(ag3, 1, ATT), (ag5, 0, UP), (ag5, 0, DOWN))

        @pl.when(s == 1)
        def _():
            run((ag5, 1, UP), (ag5, 1, DOWN))

        @pl.loop(0, slots // many)
        def feed_forward(i):
            @pl.when(s == 0)
            def _():
                events(i, {0: [(ag2, 1, DOWN), (ag3, 1, UP)], 1: both(ag4, 1, ATT)})

            rd = step_rows(i, many)

            @pl.when(s == 1)
            def _():
                for m in range(many):
                    far_copy(0, i * many + m, False).wait()
                    far_copy(1, i * many + m, False).wait()
                    shipped(0, 0, i * many + m)

            out, rstd2 = ff_forward(s, after_ref[rd, :], rd)
            for block in range(2):
                @pl.when(s == block)
                def _():
                    rstds[rd, 3 * block + 1 : 3 * block + 2] = rstd2

            out = only_live(i, out, many)
            for m in range(many):
                io_one[i * many + m] = out[rows * m : rows * m + length].astype(LOW)
                ship(0, s, i * many + m)

            @pl.when(s == 0)
            def _():
                for m in range(many):
                    far_copy(0, i * many + m, False).start()
                    far_copy(1, i * many + m, False).start()
                low = out.astype(LOW)
                xs[1, rd, :] = low
                first_norm(1, rd, low.astype(F32))

        @pl.when(s == 0)
        def _():
            run((ag3, 1, DOWN), *both(ag5, 1, ATT))

    for b in range(2):
        for g in groups:
            ag_sent(b, g)

    @pl.loop(0, 2)
    def backward(turn):
        s = 1 - turn

        @pl.when(s == 0)
        def _():
            run((rs3, 1, DOWN))

        @pl.loop(0, slots // many)
        def feed_forward(i):
            @pl.when(s == 0)
            def _():
                events(i, {1: [*both(rs1, 1, ATT), (rs3, 1, UP)]})
                for m in range(many):
                    far_copy(1, i * many + m, True).wait()

            rd = step_rows(i, many)
            for m in range(many):
                g = live(i * many + m) * io_two[i * many + m].astype(F32)
                low_g[take(i, m), :] = g.astype(LOW)
            after_ref[rd, :] = ff_backward(s, low_g[rd, :].astype(F32), rd, statistic(s, rd, 1))

        @pl.when(s == 0)
        def _():
            for i in range(slots):
                far_copy(0, i, True).wait()

        grads_down(s)
        run((rs0, s, DOWN))

        @pl.when(s == 1)
        def _():
            for i in range(slots):
                far_copy(0, i, True).start()

        grads_up(s)
        run((rs0, s, UP))

        @pl.when(s == 1)
        def _():
            for i in range(slots):
                far_copy(1, i, True).start()

        @pl.when(s == 0)
        def _():
            run((rs4, 1, DOWN), (rs4, 1, UP))

        @pl.loop(0, slots // few)
        def attention(i):
            @pl.when(s == 0)
            def _():
                events(i, {1: both(rs3, 1, ATT)})

            events(i, {1: [(rs1, s, DOWN), (rs1, s, UP)]})
            attn_backward(s, i)

        run((rs2, s, DOWN))

        @pl.when(s == 0)
        def _():
            run(*both(rs4, 1, ATT))

        grads_attn(s)
        run((rs0, s, ATT), (rs2, s, UP))

        @pl.loop(0, slots // many)
        def to_input(i):
            rd = step_rows(i, many)
            x = xs[s, rd, :].astype(F32)
            d_in = input_backward(s, after_ref[rd, :], rd, x, statistic(s, rd, 2), statistic(s, rd, 0))
            for m in range(many):
                @pl.when(s == 0)
                def _():
                    shipped(1, 1, i * many + m)

                io_two[i * many + m] = d_in[rows * m : rows * m + length].astype(LOW)
                ship(1, s, i * many + m)

        table_out(s)
        run((rs0, s, TAB))

    def sent_and_landed(kind):
        @pl.loop(0, slots)
        def _(i):
            shipped(kind, 1 - kind, i)
            for b in range(2):
                landed(kind, b, i)

    sent_and_landed(0)
    weave({
        1: lambda: run(*both(rs1, 0, ATT), (rs3, 0, DOWN), (rs3, 0, UP)),
        slots - raw.shape[0] + 1: lambda: sent_and_landed(1),
        slots + 3: lambda: run(*both(rs3, 0, ATT), (rs4, 0, DOWN), (rs4, 0, UP)),
    })
    run(*both(rs4, 0, ATT))
    for b in range(2):
        for g in groups:
            rs_sent(b, g)


def output_kernel(
    woven, f_a, f_u, f_d, f_t, o_acts, o_ings, o_g1, o_s1, o_qkv, o_qv, o_out, o_bo, o_g2, o_s2, o_up, o_bu, o_down, o_bd, passing, sems
):
    arriving, leaving = [], []
    for which, target in enumerate((o_acts, o_ings)):
        for i in range(target.shape[0]):
            arriving.append(pltpu.make_async_copy(woven.at[which, i], passing.at[which, i], sems.at[0, which, i]))
            leaving.append(pltpu.make_async_copy(passing.at[which, i], target.at[i], sems.at[1, which, i]))
    for copy in arriving:
        copy.start()
    for one, two in zip(arriving, leaving):
        one.wait()
        two.start()
    unit, width = o_out.shape[1:]
    for half in range(2):
        o_down[0, 2 * unit * half : 2 * unit * (half + 1), :] = f_d[half]
        for sub in range(2):
            part = 2 * half + sub
            cols = slice(part * width, (part + 1) * width)
            o_up[0, :, cols] = f_u[half, unit * sub : unit * (sub + 1), :]
            piece = f_a[half, unit * sub : unit * (sub + 1), :]
            if part == 3:
                o_out[0] = piece
            else:
                o_qkv[0, :, cols] = piece
    begin = 0
    for out in (o_g1, o_s1, o_bo, o_g2, o_s2, o_bd, o_qv):
        part = out.shape[1]
        out[...] = f_t[0, :, begin : begin + part]
        begin += part
    o_bu[...] = f_t[1, :, 0 : o_bu.shape[1]]
    for copy in leaving:
        copy.wait()


def local(
    images, cotangent, counts,
    ln1_gain, ln1_bias, w_qkv, b_qv, w_out, b_out, ln2_gain, ln2_bias, w_up, b_up, w_down, b_down,
):
    micro_count, slots, length, width = images.shape
    ff = w_up.shape[2]
    rows = -(-length // 16) * 16
    n = lax.axis_size("fsdp")
    unit = width // n
    first, rest = radices(n)
    total = slots * rows
    head_dim = width // HEADS

    def vm(*shape, kind=LOW):
        return pltpu.VMEM(shape, kind)

    tall = [(2 * unit, LOW)] * 3 + [(1, F32)]
    dma = lambda *shape: pltpu.SemaphoreType.DMA(shape)
    outs = [((2, slots, length, 2, width), LOW)]
    outs += [((2, r, width), F32) for r, _ in tall] + [((total, ff), LOW)] * 2 + [((2, 2, slots, length, width), LOW)]
    scratch = [
        vm(2, total, width), vm(3, length, 2, width), vm(slots, length, width), vm(slots, length, width),
        *[vm(2, r, width, kind=kind) for r, kind in tall],
        vm(2, width, 3 * width), vm(2, width, width), vm(2, width, ff), vm(2, ff, width),
        vm(2, TABLE, width, kind=F32), vm(2, TABLE, width, kind=F32),
        vm(unit, width), vm(2 * unit, 2 * width), vm(4 * unit, 4 * width),
        vm(total, width, kind=F32), vm(2, total, width), vm(2, total, 3 * width), vm(2, slots, HEADS, rows, rows),
        vm(2, total, width),
        vm(2, total, width), vm(2, total, width), vm(total, 6, kind=F32),
        vm(total, ff), vm(total, ff), vm(total, width), vm(total, width), vm(width, total),
    ]
    scratch += [vm(2, 2, n, r, width, kind=kind) for r, kind in tall]
    scratch += [vm(n, r, width, kind=kind) for r, kind in tall]
    plane = rest * rest - 1
    for g, (r, kind) in enumerate(tall):
        direct = g in (ATT, TAB)
        scratch.append(vm(*((plane, first) if direct else (rest - 1, rest * first)), r, width, kind=kind))
    scratch += [vm(2, rest - 1, first, *tall[g][:1], width) for g in (UP, DOWN)]
    scratch += [vm(2, first, r, width, kind=kind) for r, kind in tall]
    scratch += [dma(2, slots), dma(2, 2 * slots), dma(2 * slots), dma(4, slots), dma(4, slots), dma(4, slots)]
    scratch += [dma(4, 2, first), dma(8, first)] + [dma(8, rest - 1)] * 4 + [dma(8, rest)] * 2
    scratch += [dma(8)] * 2 + [dma(8, plane)] * 2 + [dma(8, rest - 1)] * 2 + [dma(8, first), dma(4, 2, first)]
    scratch += [pltpu.SemaphoreType.REGULAR((2, 4))]
    dims = (slots, length, rows, width, ff, head_dim, n)
    vmem = pl.BlockSpec(memory_space=pltpu.VMEM)
    hbm = pl.BlockSpec(memory_space=pltpu.HBM)
    woven, f_a, f_u, f_d, f_t, *_ = pl.pallas_call(
        functools.partial(whole_kernel, dims),
        out_shape=[jax.ShapeDtypeStruct(*o) for o in outs],
        in_specs=[hbm, hbm, pl.BlockSpec(memory_space=pltpu.SMEM)] + [vmem] * 12,
        out_specs=[hbm] + [vmem] * 4 + [hbm] * 3,
        scratch_shapes=scratch,
        compiler_params=pltpu.CompilerParams(
            vmem_limit_bytes=(64 << 20) - (96 << 10), collective_id=0, has_side_effects=True
        ),
    )(
        images.transpose(1, 2, 0, 3), cotangent.transpose(1, 2, 0, 3), counts.T, ln1_gain, ln1_bias, b_out, ln2_gain, ln2_bias, b_down, b_qv, b_up,
        w_qkv, w_out, w_up, w_down,
    )

    params = (
        ln1_gain, ln1_bias, w_qkv, b_qv, w_out, b_out, ln2_gain, ln2_bias, w_up, b_up, w_down, b_down
    )
    acts, ings, *grads = pl.pallas_call(
        output_kernel,
        out_shape=[jax.ShapeDtypeStruct(woven.shape[1:], LOW)] * 2
        + [jax.ShapeDtypeStruct(p.shape, F32) for p in params],
        in_specs=[hbm] + [vmem] * 4,
        out_specs=[hbm] * 2 + [vmem] * len(params),
        scratch_shapes=[vm(2, slots, length, 2, width), dma(2, 2, slots)],
        compiler_params=pltpu.CompilerParams(vmem_limit_bytes=(64 << 20) - (96 << 10)),
    )(woven, f_a, f_u, f_d, f_t)

    def as_given(value):
        return value.transpose(2, 0, 1, 3)[None]

    return (as_given(acts), as_given(ings), *grads)


def solution(mesh):
    split = P("section", "fsdp")
    cube = P("section", "fsdp", None)
    image = P(None, "fsdp", None, None)
    result = P("section", None, "fsdp", None, None)
    params = (split, split, cube, split, cube, split, split, split, cube, split, cube, split)
    return jax.shard_map(
        local,
        mesh=mesh,
        in_specs=(image, image, P(None, "fsdp")) + params,
        out_specs=(result, result) + params,
        check_vma=False,
    )
```

```python
import functools
import math

import jax
import jax.numpy as jnp
from jax import lax
from jax.experimental import pallas as pl
from jax.experimental.pallas import tpu as pltpu
from jax.sharding import PartitionSpec as P

HEADS = 6
EPS = 1e-06
F32 = jnp.float32
LOW = jnp.bfloat16

G1, S1, BO, G2, S2, BD, BQ, BV, BU = 0, 1, 2, 3, 4, 5, 6, 7, 8
TABLE = 16
TOGETHER, TOGETHER_ROWS = 3, 3
ATT, UP, DOWN, TAB = 0, 1, 2, 3


def radices(n):
    rest = max(r for r in range(1, n + 1) if r * r * r <= n and n % (r * r) == 0)
    return n // (rest * rest), rest


def mm(left, right):
    return jnp.dot(left, right, preferred_element_type=F32)


def mm_right(left, right):
    return lax.dot_general(left, right, (((1,), (1,)), ((), ())), preferred_element_type=F32)


def mm_left(left, right):
    return lax.dot_general(left, right, (((0,), (0,)), ((), ())), preferred_element_type=F32)


def normal_parts(pre):
    phi = 0.5 + 0.5 * lax.erf(pre * 0.7071067811865476)
    density = jnp.exp2(pre * pre * (-0.5 * 1.4426950408889634)) * 0.3989422804014327
    return phi, phi + pre * density


def normalize(value):
    mean = jnp.mean(value, axis=-1, keepdims=True)
    center = value - mean
    rstd = lax.rsqrt(jnp.mean(center * center, axis=-1, keepdims=True) + EPS)
    return center * rstd, rstd, mean


def normalize_back(d_hat, hat, rstd):
    mean_one = jnp.mean(d_hat, axis=-1, keepdims=True)
    mean_two = jnp.mean(d_hat * hat, axis=-1, keepdims=True)
    return rstd * (d_hat - mean_one - hat * mean_two)


def colsum(value):
    return jnp.sum(value, axis=0, keepdims=True)


def whole_kernel(dims, *refs):
    slots, length, rows, width, ff, head_dim, n = dims
    (
        images, cotangent, counts, v_g1, v_s1, v_bo, v_g2, v_s2, v_bd, v_qv, v_up, a_qkv, a_out, a_up, a_down,
        woven, f_a, f_u, f_d, f_t, hid_far, slope_far, out_far,
        xs, raw, io_one, io_two, pack_a, pack_u, pack_d, pack_t,
        wqkv, wout, wup, wdown, table, gtable, rep_one, rep_two, rep_four,
        after_ref, nrm1, qkv, prob, overs, ctx, hat2, rstds, hid, slope, dal, low_g, left_t,
        s_a, s_u, s_d, s_t, r0_a, r0_u, r0_d, r0_t, r1_a, r1_u, r1_d, r1_t, r2_u, r2_d,
        r3_a, r3_u, r3_d, r3_t,
        in_s, weave_in, weave_out, ship_s, ship_r, far_s, ag1_s, ag1_r, ag2_s, ag2_r, ag3_s, ag3_r, ag4_s, ag4_r,
        rs0_s, rs0_r, rs1_s, rs1_r, rs2_s, rs2_r, rs3_s, rs3_r, credit,
    ) = refs
    groups = (ATT, UP, DOWN, TAB)
    pack = (pack_a, pack_u, pack_d, pack_t)
    stage = (s_a, s_u, s_d, s_t)
    r0, r1, r2 = (r0_a, r0_u, r0_d, r0_t), (r1_a, r1_u, r1_d, r1_t), (None, r2_u, r2_d, None)
    r3, final = (r3_a, r3_u, r3_d, r3_t), (f_a, f_u, f_d, f_t)

    first, rest = radices(n)
    unit = width // n
    core = lax.axis_index("section")
    me = lax.axis_index("fsdp")
    dig_a, dig_b, dig_c = me // (rest * rest), (me // rest) % rest, me % rest
    dig_three, dig_two = dig_c + core * (dig_b - dig_c), dig_b + core * (dig_c - dig_b)
    step_three, step_two = 1 + core * (rest - 1), rest - core * (rest - 1)
    pos = (dig_three * rest + dig_two) * first + dig_a
    pos_of = ((dig_c * rest + dig_b) * first + dig_a, (dig_b * rest + dig_c) * first + dig_a)
    sibling = {"section": 1 - core}

    def place(half, j):
        a, b, c = j // (rest * rest), (j // rest) % rest, j % rest
        return ((c * rest + b) if half == 0 else (b * rest + c)) * first + a

    def peer_first(t):
        return {"fsdp": me + ((dig_a + t) % first - dig_a) * (rest * rest)}

    def peer_two(t):
        return {"fsdp": me + ((dig_two + t) % rest - dig_two) * step_two}

    def peer_three(t):
        return {"fsdp": me + ((dig_three + t) % rest - dig_three) * step_three}

    def peer_plane(three, two):
        here = ((dig_three + three) % rest - dig_three) * step_three
        return {"fsdp": me + here + ((dig_two + two) % rest - dig_two) * step_two}

    plane = [(three, two) for three in range(rest) for two in range(rest) if three or two]

    def remote(src, dst, s_sem, r_sem, device):
        return pltpu.make_async_remote_copy(
            src_ref=src, dst_ref=dst, send_sem=s_sem, recv_sem=r_sem, device_id=device,
            device_id_type=pl.DeviceIdType.MESH,
        )

    def slab_two(three, two):
        return pl.ds((three * rest + two) * first, first)

    def slab_three(three):
        return pl.ds(three * rest * first, rest * first)

    def fill_repeats():
        for ref in (rep_one, rep_two, rep_four):
            part = ref.shape[0]
            lanes = lax.broadcasted_iota(jnp.int32, ref.shape, 1).astype(F32)
            line = lax.broadcasted_iota(jnp.int32, ref.shape, 0).astype(F32)
            rest_of = lanes - part * jnp.floor((lanes + 0.5) * (1.0 / part))
            ref[...] = jnp.where(jnp.abs(rest_of - line) < 0.5, 1.0, 0.0).astype(LOW)

    def own_lanes(part):
        shape = (n, part * n)
        lanes = lax.broadcasted_iota(jnp.int32, shape, 1)
        begin = lax.broadcasted_iota(jnp.int32, shape, 0) * part
        return (lanes >= begin) & (lanes < begin + part)

    shares = (
        ((G1, unit, rep_one), (S1, unit, rep_one), (BO, unit, rep_one), (G2, unit, rep_one), (S2, unit, rep_one),
         (BD, unit, rep_one), (BQ, 2 * unit, rep_two)),
        ((BU, 4 * unit, rep_four),),
    )

    def table_in(b):
        for half in range(2):
            lines = jnp.concatenate([s_t[b, half, place(half, j)] for j in range(n)], axis=0)
            begin = 0
            for row, part, ref in shares[half]:
                spread = mm(lines[:, begin : begin + part].astype(LOW), ref[...])
                line = colsum(jnp.where(own_lanes(part), spread, 0.0))
                for i in range(part * n // width):
                    table[b, row + i : row + i + 1, :] = line[:, width * i : width * (i + 1)]
                begin += part

    def table_out(b):
        for half in range(2):
            parts, begin = [], 0
            for row, part, ref in shares[half]:
                count = part * n // width
                line = jnp.concatenate([gtable[b, row + i : row + i + 1, :] for i in range(count)], axis=1)
                parts.append(mm_right(jnp.where(own_lanes(part), line, 0.0).astype(LOW), ref[...]))
                begin += part
            parts.append(jnp.zeros((n, width - begin), F32))
            lines = jnp.concatenate(parts, axis=1)
            for j in range(n):
                s_t[b, half, place(half, j)] = lines[j : j + 1]

    def pack_own():
        for half in range(2):
            vectors = ((v_g1, v_s1, v_bo, v_g2, v_s2, v_bd, v_qv), (v_up,))[half]
            lines = [vector[...].astype(F32) for vector in vectors]
            lines.append(jnp.zeros((1, width - sum(line.shape[1] for line in lines)), F32))
            pack_t[half] = jnp.concatenate(lines, axis=1)
            for ref in (pack_a, pack_u):
                both = []
                for part in (2 * half, 2 * half + 1):
                    if ref is pack_u:
                        both.append(a_up[0, :, part * width : (part + 1) * width])
                    elif part == 3:
                        both.append(a_out[0])
                    else:
                        both.append(a_qkv[0, :, part * width : (part + 1) * width])
                ref[half] = jnp.concatenate([value.astype(F32) for value in both], axis=0).astype(LOW)
            pack_d[half] = a_down[0, 2 * unit * half : 2 * unit * (half + 1), :]

    def at(b, g):
        return len(groups) * b + g

    def ag1_copy(b, g, half, t):
        device = {"section": half, **peer_first(t)} if t else sibling
        return remote(
            pack[g].at[half], stage[g].at[b, half, pos_of[half]],
            ag1_s.at[g, half, t], ag1_r.at[at(b, g), t], device,
        )

    def ag1_landing(b, g, t):
        ref = stage[g].at[b, core, (dig_three * rest + dig_two) * first + (dig_a + first - t) % first]
        return remote(ref, ref, ag1_s.at[g, 0, t], ag1_r.at[at(b, g), t], sibling)

    def ag2_copy(b, g, t):
        ref = stage[g].at[b, core, slab_two(dig_three, dig_two)]
        return remote(ref, ref, ag2_s.at[at(b, g), t - 1], ag2_r.at[at(b, g), t - 1], peer_two(t))

    def ag3_copy(b, g, t):
        ref = stage[g].at[b, core, slab_three(dig_three)]
        return remote(ref, ref, ag3_s.at[at(b, g), t - 1], ag3_r.at[at(b, g), t - 1], peer_three(t))

    def ag4_copy(b, g, t):
        ref = stage[g].at[b, core, slab_three((dig_three + rest - t) % rest)]
        return remote(ref, ref, ag4_s.at[at(b, g), t], ag4_r.at[at(b, g), t], sibling)

    def ag4_landing(b, g, t):
        ref = stage[g].at[b, 1 - core, slab_three((dig_two + rest - t) % rest)]
        return remote(ref, ref, ag4_s.at[at(b, g), t], ag4_r.at[at(b, g), t], sibling)

    def ag1(b, g):
        @pl.when(core == b)
        def _():
            for t in range(1, first):
                for half in range(2):
                    ag1_copy(b, g, half, t).start()
            ag1_copy(b, g, 1 - b, 0).start()
            stage[g][b, b, pos] = pack[g][b]

    def ag2(b, g):
        for t in range(1, first):
            ag1_landing(b, g, t).wait_recv()

        @pl.when(core != b)
        def _():
            ag1_landing(b, g, 0).wait_recv()

        for t in range(1, rest):
            ag2_copy(b, g, t).start()

    def ag3(b, g):
        for t in range(1, rest):
            ag2_copy(b, g, t).wait_recv()
        for t in range(1, rest):
            ag3_copy(b, g, t).start()
        ag4_copy(b, g, 0).start()

    def ag4(b, g):
        for t in range(1, rest):
            ag3_copy(b, g, t).wait_recv()
            ag4_copy(b, g, t).start()

    def ag5(b, g):
        for t in range(rest):
            ag4_landing(b, g, t).wait_recv()
        lay_out(b, g)

    def ag_sent(b, g):
        @pl.when(core == b)
        def _():
            for t in range(1, first):
                for half in range(2):
                    ag1_copy(b, g, half, t).wait_send()
            ag1_copy(b, g, 1 - b, 0).wait_send()

        for t in range(1, rest):
            ag2_copy(b, g, t).wait_send()
            ag3_copy(b, g, t).wait_send()
        for t in range(rest):
            ag4_copy(b, g, t).wait_send()

    def lay_out(b, g):
        if g == TAB:
            table_in(b)
            return
        if g == DOWN:
            for j in range(n):
                for half in range(2):
                    begin = 4 * unit * j + 2 * unit * half
                    wdown[b, begin : begin + 2 * unit, :] = s_d[b, half, place(half, j)]
            return
        together = 16 // math.gcd(unit, 16)
        for half in range(2):
            for j in range(0, n, together):
                pieces = [stage[g][b, half, place(half, j + i)].astype(F32) for i in range(together)]
                for sub in range(2):
                    low = sub * unit
                    block = jnp.concatenate([piece[low : low + unit] for piece in pieces], axis=0).astype(LOW)
                    part = 2 * half + sub
                    down = slice(unit * j, unit * (j + together))
                    if g == UP:
                        wup[b, down, part * width : (part + 1) * width] = block
                    elif part == 3:
                        wout[b, down, :] = block
                    else:
                        wqkv[b, down, part * width : (part + 1) * width] = block

    def rs0_copy(b, g):
        return remote(stage[g].at[b, 1 - core], r0[g], rs0_s.at[at(b, g)], rs0_r.at[at(b, g)], sibling)

    def rs1_copy(b, g, t):
        return remote(
            stage[g].at[b, core, slab_three((dig_three + t) % rest)], r1[g].at[t - 1],
            rs1_s.at[at(b, g), t - 1, 0], rs1_r.at[at(b, g), t - 1, 0], peer_three(t),
        )

    def rs2_copy(b, g, t):
        return remote(
            stage[g].at[b, core, slab_two(dig_three, (dig_two + t) % rest)], r2[g].at[b, t - 1],
            rs2_s.at[at(b, g), t - 1], rs2_r.at[at(b, g), t - 1], peer_two(t),
        )

    def rs3_copy(b, g, t):
        there = (dig_three * rest + dig_two) * first + (dig_a + t) % first
        device = {"section": b, **peer_first(t)} if t else sibling
        return remote(
            stage[g].at[b, core, there], r3[g].at[core, t], rs3_s.at[at(b, g), t], rs3_r.at[g, core, t], device
        )

    chunk_count = 2 if first % 2 == 0 else 1
    chunk_size = first // chunk_count

    def plane_copy(b, g, t, part):
        three, two = plane[t]
        begin = (((dig_three + three) % rest) * rest + (dig_two + two) % rest) * first + chunk_size * part
        return remote(
            stage[g].at[b, core, pl.ds(begin, chunk_size)], r1[g].at[t, pl.ds(chunk_size * part, chunk_size)],
            rs1_s.at[at(b, g), t, part], rs1_r.at[at(b, g), t, part], peer_plane(three, two),
        )

    def rs0(b, g):
        @pl.when(b == 0)
        def _():
            pl.semaphore_wait(credit.at[0, g], 1)

        rs0_copy(b, g).start()

    def rs1(b, g):
        rs0_copy(b, g).wait_recv()

        @pl.loop(0, n)
        def _(p):
            stage[g][b, core, p] = stage[g][b, core, p] + r0[g][p]

        @pl.when(b == 1)
        def _():
            pl.semaphore_signal(credit.at[0, g], inc=1, device_id=sibling, device_id_type=pl.DeviceIdType.MESH)

        direct = g in (ATT, TAB)
        if rest > 1:
            @pl.when(b == 0)
            def _():
                pl.semaphore_wait(credit.at[1, g], len(plane) if direct else rest - 1)

        if direct:
            for part in range(chunk_count):
                for t in range(len(plane)):
                    plane_copy(b, g, t, part).start()
            return
        for t in range(1, rest):
            rs1_copy(b, g, t).start()

    def rs2(b, g):
        for t in range(1, rest):
            rs1_copy(b, g, t).wait_recv()

        @pl.loop(0, rest * first)
        def _(p):
            here = dig_three * rest * first + p
            total = stage[g][b, core, here].astype(F32)
            for t in range(1, rest):
                total = total + r1[g][t - 1, p].astype(F32)
            stage[g][b, core, here] = total.astype(stage[g].dtype)

        for t in range(1, rest):
            @pl.when(b == 1)
            def _():
                pl.semaphore_signal(
                    credit.at[1, g], inc=1, device_id=peer_three(t), device_id_type=pl.DeviceIdType.MESH
                )

            rs2_copy(b, g, t).start()

    def rs3_send(b, g, part):
        def here(digit):
            return (digit >= chunk_size * part) & (digit < chunk_size * (part + 1))

        for t in range(1, first):
            @pl.when(here((dig_a + t) % first))
            def _():
                rs3_copy(b, g, t).start()

        @pl.when(here(dig_a) & (core != b))
        def _():
            rs3_copy(b, g, 0).start()

    def rs3_part(b, g, part):
        for t in range(len(plane)):
            plane_copy(b, g, t, part).wait_recv()

        @pl.loop(chunk_size * part, chunk_size * (part + 1))
        def _(p):
            here = (dig_three * rest + dig_two) * first + p
            total = stage[g][b, core, here].astype(F32)
            for t in range(len(plane)):
                total = total + r1[g][t, p].astype(F32)
            stage[g][b, core, here] = total.astype(stage[g].dtype)

        rs3_send(b, g, part)

    def rs3_first(b, g):
        rs3_part(b, g, 0)

    def rs3_rest(b, g):
        for part in range(1, chunk_count):
            rs3_part(b, g, part)

    def rs3(b, g):
        if g in (ATT, TAB):
            for part in range(chunk_count):
                rs3_part(b, g, part)

            @pl.when(b == 1)
            def _():
                for three, two in plane:
                    pl.semaphore_signal(
                        credit.at[1, g], inc=1, device_id=peer_plane(three, two),
                        device_id_type=pl.DeviceIdType.MESH,
                    )

            return
        for t in range(1, rest):
            rs2_copy(b, g, t).wait_recv()

        @pl.loop(0, first)
        def _(p):
            here = (dig_three * rest + dig_two) * first + p
            total = stage[g][b, core, here].astype(F32)
            for t in range(1, rest):
                total = total + r2[g][b, t - 1, p].astype(F32)
            stage[g][b, core, here] = total.astype(stage[g].dtype)

        for part in range(chunk_count):
            rs3_send(b, g, part)

    def rs4(b, g):
        @pl.when(core == b)
        def _():
            for own in (True, False):
                half = core if own else 1 - core
                begin = int(own)
                for t in range(begin, first):
                    ref = r3[g].at[half, t]
                    remote(ref, ref, rs3_s.at[at(b, g), t], rs3_r.at[g, half, t], sibling).wait_recv()
                total = stage[g][b, core, pos].astype(F32) if own else None
                for t in range(begin, first):
                    value = r3[g][half, t].astype(F32)
                    total = value if total is None else total + value
                final[g][half] = total

    def rs_sent(b, g):
        rs0_copy(b, g).wait_send()
        if g in (ATT, TAB):
            for part in range(chunk_count):
                for t in range(len(plane)):
                    plane_copy(b, g, t, part).wait_send()
        else:
            for t in range(1, rest):
                rs1_copy(b, g, t).wait_send()
                rs2_copy(b, g, t).wait_send()
        for t in range(1, first):
            rs3_copy(b, g, t).wait_send()

        @pl.when(core != b)
        def _():
            rs3_copy(b, g, 0).wait_send()

    def rows_of(i, images_too=1):
        return pl.ds(pl.multiple_of(i * rows, 16), images_too * rows)

    few = TOGETHER if slots % TOGETHER == 0 else 1
    many = TOGETHER_ROWS if slots % TOGETHER_ROWS == 0 else 1

    def step_rows(i, count):
        return rows_of(i * count, count)

    def ship_parts(kind, b, i):
        src, out = (io_one, io_two)[kind].at[i], out_far.at[kind, core, i]
        q = 2 * kind + b
        near = pltpu.make_async_copy(src, out, ship_s.at[q, i])
        far = remote(src, out, ship_s.at[q, i], ship_r.at[q, i], sibling)
        return near, far

    def ship(kind, b, i):
        near, far = ship_parts(kind, b, i)

        @pl.when(core == b)
        def _():
            near.start()

        @pl.when(core != b)
        def _():
            far.start()

    def shipped(kind, b, i):
        near, far = ship_parts(kind, b, i)

        @pl.when(core == b)
        def _():
            near.wait()

        @pl.when(core != b)
        def _():
            far.wait_send()

    def landed(kind, b, i):
        q = 2 * kind + b
        ref = out_far.at[kind, 1 - core, i]

        @pl.when(core == b)
        def _():
            remote(ref, ref, ship_s.at[q, i], ship_r.at[q, i], sibling).wait_recv()

    def live(i):
        return jnp.where(i < counts[0, core], 1.0, 0.0).astype(F32)

    def only_live(i, value, count):
        parts = [value[rows * m : rows * (m + 1)] * live(i * count + m) for m in range(count)]
        return jnp.concatenate(parts, axis=0)

    def coming(which, i):
        slot = (which * slots + i) % raw.shape[0]
        return pltpu.make_async_copy((images, cotangent)[which].at[i], raw.at[slot], in_s.at[which, i])

    def take_in(which, i):
        coming(which, i).wait()
        both = raw[(which * slots + i) % raw.shape[0]].astype(F32)
        (io_one, io_two)[which][i] = jnp.where(core == 0, both[:, 0, :], both[:, 1, :]).astype(LOW)

    def weave(todo):
        ring = raw.shape[0]
        count = 2 * slots

        def fetch(t, m):
            source = out_far.at[t // slots, m, t % slots]
            return pltpu.make_async_copy(source, io_one.at[2 * (t % ring) + m], weave_in.at[m, t])

        def leave(t):
            return pltpu.make_async_copy(raw.at[t % ring], woven.at[t // slots, t % slots], weave_out.at[t])

        for t in range(ring - 1):
            for m in range(2):
                fetch(t, m).start()

        @pl.loop(0, count)
        def _(t):
            for when, act in todo.items():
                @pl.when(t == when)
                def _():
                    act()

            @pl.when(t + ring - 1 < count)
            def _():
                for m in range(2):
                    fetch(t + ring - 1, m).start()

            @pl.when(t >= ring)
            def _():
                leave(t - ring).wait()

            for m in range(2):
                fetch(t, m).wait()
                raw[t % ring, :, m, :] = io_one[2 * (t % ring) + m]
            leave(t).start()

        for t in range(count - ring, count):
            leave(t).wait()

    def far_copy(which, i, back):
        near, far = ((hid, hid_far), (slope, slope_far))[which]
        near, far = near.at[rows_of(i)], far.at[rows_of(i)]
        src, dst = (far, near) if back else (near, far)
        return pltpu.make_async_copy(src, dst, far_s.at[2 * int(back) + which, i])

    pairs = width // 128
    scale = head_dim ** -0.5
    lane = lax.broadcasted_iota(jnp.int32, (1, 128), 1)
    half_low = [(lane < head_dim).astype(LOW), (lane >= head_dim).astype(LOW)]
    half_f = [(lane < head_dim).astype(F32), (lane >= head_dim).astype(F32)]
    token = lax.broadcasted_iota(jnp.int32, (rows, 128), 0) < length
    half_valid = [jnp.where(token, half_f[j], 0.0).astype(LOW) for j in range(2)]
    valid_lanes = jnp.where(lax.broadcasted_iota(jnp.int32, (1, rows), 1) < length, 1.0, 0.0).astype(F32)
    spare = -rows % 128
    chunk = 2 * width
    chunks = ff // chunk

    def vec(s, r):
        return table[s, r : r + 1, :]

    def up_bias(s, c):
        begin = c * chunk
        row, col = begin // width, begin % width
        if col + chunk <= width:
            return table[s, BU + row : BU + row + 1, col : col + chunk]
        a = table[s, BU + row : BU + row + 1, col:width]
        b = table[s, BU + row + 1 : BU + row + 2, 0 : chunk - (width - col)]
        return jnp.concatenate([a, b], axis=1)

    def add_vec(s, r, value):
        gtable[s, r : r + 1, :] += value

    def add_up_bias(s, c, value):
        begin = c * chunk
        row, col = begin // width, begin % width
        if col + chunk <= width:
            gtable[s, BU + row : BU + row + 1, col : col + chunk] += value
        else:
            cut = width - col
            gtable[s, BU + row : BU + row + 1, col:width] += value[:, :cut]
            gtable[s, BU + row + 1 : BU + row + 2, 0 : chunk - cut] += value[:, cut:]

    def attn_forward(s, x, hat, i):
        rd = step_rows(i, few)
        nrm_ref, qkv_ref, prob_ref, ctx_ref = nrm1.at[s], qkv.at[s], prob.at[s], ctx.at[s]
        nrm = (hat * vec(s, G1) + vec(s, S1)).astype(LOW)
        nrm_ref[rd, :] = nrm
        mixed = mm(nrm, wqkv[s])
        q = (mixed[:, 0:width] + vec(s, BQ)).astype(LOW)
        k = mixed[:, width : 2 * width].astype(LOW)
        v = (mixed[:, 2 * width :] + vec(s, BV)).astype(LOW)
        qkv_ref[rd, 0:width] = q
        qkv_ref[rd, width : 2 * width] = k
        qkv_ref[rd, 2 * width :] = v
        images_out = []
        for m in range(few):
            mine = slice(rows * m, rows * (m + 1))
            parts = []
            for p in range(pairs):
                cols = slice(128 * p, 128 * p + 128)
                weights, sides = [], []
                for j in range(2):
                    keys = k[mine, cols] * half_low[j]
                    keys = jnp.concatenate([keys, keys[rows - spare :]], axis=0)
                    scores = mm_right(q[mine, cols], keys)
                    top = jnp.max(scores, axis=-1, keepdims=True)
                    e = jnp.exp2((scores - top) * (scale * 1.4426950408889634)).astype(LOW)
                    prob_ref[i * few + m, 2 * p + j] = e[:, :rows]
                    weights.append(e)
                    sides.append(jnp.concatenate([v[mine, cols] * half_valid[j], half_valid[j]], axis=1))
                    sides.append(jnp.zeros((spare, 256), LOW))
                total = mm(jnp.concatenate(weights, axis=1), jnp.concatenate(sides, axis=0))
                over = 1.0 / total[:, 128:]
                overs[s, rows_of(i * few + m), cols] = over.astype(LOW)
                parts.append((total[:, :128] * over).astype(LOW))
            images_out.append(jnp.concatenate(parts, axis=1))
        context = jnp.concatenate(images_out, axis=0)
        ctx_ref[rd, :] = context
        return x + mm(context, wout[s]) + vec(s, BO)

    def ff_forward(s, after, rd):
        hat, rstd, _ = normalize(after)
        hat2[s, rd, :] = hat.astype(LOW)
        nrm = (hat * vec(s, G2) + vec(s, S2)).astype(LOW)
        total = after + vec(s, BD)
        for c in range(chunks):
            cols = slice(chunk * c, chunk * c + chunk)
            pre = mm(nrm, wup[s, :, cols]) + up_bias(s, c)
            phi, slo = normal_parts(pre)
            h = (pre * phi).astype(LOW)
            hid[rd, cols] = h
            slope[rd, cols] = slo.astype(LOW)
            total = total + mm(h, wdown[s, cols, :])
        return total, rstd

    def ff_backward(s, g, rd, rstd):
        g_low = g.astype(LOW)
        add_vec(s, BD, colsum(g_low.astype(F32)))
        d_nrm = None
        for c in range(chunks):
            cols = slice(chunk * c, chunk * c + chunk)
            d_hid = mm_right(g_low, wdown[s, cols, :])
            d_pre = (d_hid * slope[rd, cols].astype(F32)).astype(LOW)
            slope[rd, cols] = d_pre
            add_up_bias(s, c, colsum(d_pre.astype(F32)))
            part = mm_right(d_pre, wup[s, :, cols])
            d_nrm = part if d_nrm is None else d_nrm + part
        hat = hat2[s, rd, :].astype(F32)
        add_vec(s, G2, colsum(d_nrm * hat))
        add_vec(s, S2, colsum(d_nrm))
        d_after = g + normalize_back(d_nrm * vec(s, G2), hat, rstd)
        low = d_after.astype(LOW)
        dal[rd, :] = low
        add_vec(s, BO, colsum(low.astype(F32)))
        return d_after

    def attn_backward(s, i):
        qkv_ref, prob_ref, ctx_ref = qkv.at[s], prob.at[s], ctx.at[s]
        rd = step_rows(i, few)
        d_context = mm_right(dal[rd, :], wout[s])
        d_context = (d_context * overs[s, rd, :].astype(F32)).astype(LOW)
        for m in range(few):
            rd = rows_of(i * few + m)
            d_ctx = d_context[rows * m : rows * (m + 1)]
            dq, dk, dv = [], [], []
            for p in range(pairs):
                cols = slice(128 * p, 128 * p + 128)
                q = qkv_ref[rd, 128 * p : 128 * p + 128]
                k = qkv_ref[rd, width + 128 * p : width + 128 * p + 128]
                v = qkv_ref[rd, 2 * width + 128 * p : 2 * width + 128 * p + 128]
                dc = d_ctx[:, cols]
                both = dc.astype(F32) * ctx_ref[rd, cols].astype(F32)
                q_t, dc_t = q.T, dc.T
                to_q, to_k, to_v = None, [], []
                for j in range(2):
                    e = prob_ref[i * few + m, 2 * p + j]
                    delta = jnp.sum(both * half_f[j], axis=-1, keepdims=True)
                    d_prob = mm_right(dc, v * half_low[j])
                    ds = (e.astype(F32) * (d_prob - delta)).astype(LOW)
                    part = mm(ds, k * half_valid[j])
                    to_q = part if to_q is None else to_q + part
                    head = slice(head_dim * j, head_dim * (j + 1))
                    to_k.append(mm(q_t[head], ds))
                    to_v.append(mm(dc_t[head], e))
                dq.append((to_q * scale).astype(LOW))
                dk.append((jnp.concatenate(to_k, axis=0) * (valid_lanes * scale)).astype(LOW).T)
                dv.append((jnp.concatenate(to_v, axis=0) * valid_lanes).astype(LOW).T)
            d_mixed = jnp.concatenate(dq + dk + dv, axis=1)
            qkv_ref[rd, :] = d_mixed
            add_vec(s, BQ, colsum(d_mixed[:, 0:width].astype(F32)))
            add_vec(s, BV, colsum(d_mixed[:, 2 * width :].astype(F32)))

    def input_backward(s, d_after, rd, x, mean, rstd):
        d_nrm = mm_right(qkv[s, rd, :], wqkv[s])
        hat = (x - mean) * rstd
        add_vec(s, G1, colsum(d_nrm * hat))
        add_vec(s, S1, colsum(d_nrm))
        return d_after + normalize_back(d_nrm * vec(s, G1), hat, rstd)

    def grads_down(s):
        left_t[...] = low_g[...].T

        @pl.loop(0, 2)
        def _(c):
            cols = pl.ds(pl.multiple_of(c * 2 * width, 128), 2 * width)
            block = mm(left_t[...], hid[:, cols]).T
            for i in range(n // 2):
                for half in range(2):
                    begin = 4 * unit * i + 2 * unit * half
                    s_d[s, half, place(half, c * (n // 2) + i)] = block[begin : begin + 2 * unit].astype(LOW)

    def pair_out(ref, s, half, one, two):
        for j in range(n):
            down = slice(unit * j, unit * (j + 1))
            piece = jnp.concatenate([one[down], two[down]], axis=0).astype(LOW)
            ref[s, half, place(half, j)] = piece

    def grads_up(s):
        left_t[...] = (hat2[s].astype(F32) * vec(s, G2) + vec(s, S2)).astype(LOW).T
        for half in range(2):
            both = mm(left_t[...], slope[:, 2 * half * width : 2 * (half + 1) * width])
            pair_out(s_u, s, half, both[:, :width], both[:, width:])

    def grads_attn(s):
        mix_s = qkv.at[s]
        left_t[...] = ctx[s].T
        four = mm(left_t[...], dal[...])
        left_t[...] = nrm1[s].T
        three = mm(left_t[...], mix_s[:, 2 * width :])
        pair_out(s_a, s, 1, three, four)
        both = mm(left_t[...], mix_s[:, 0 : 2 * width])
        pair_out(s_a, s, 0, both[:, :width], both[:, width:])

    barrier = pltpu.get_barrier_semaphore()
    greeted = [sibling]
    greeted += [{"section": half, **peer_first(t)} for t in range(1, first) for half in range(2)]
    greeted += [peer_plane(three, two) for three, two in plane]
    for device in greeted:
        pl.semaphore_signal(barrier, inc=1, device_id=device, device_id_type=pl.DeviceIdType.MESH)
    pack_own()
    pl.semaphore_wait(barrier, len(greeted))

    def run(*todo):
        for f, b, g in todo:
            f(b, g)

    def events(i, table_of):
        for when, todo in table_of.items():
            @pl.when(i == when)
            def _():
                run(*todo)

    def both(f, b, g):
        return [(f, b, g), (f, b, TAB)]

    def take(i, m):
        return pl.ds(pl.multiple_of((i * many + m) * rows, 16), length)

    ahead = raw.shape[0]
    run(*both(ag1, 0, ATT))
    for i in range(ahead):
        coming(0, i).start()
    fill_repeats()
    gtable[...] = jnp.zeros_like(gtable)
    low_g[...] = jnp.zeros_like(low_g)
    xs[0] = jnp.zeros_like(low_g)

    @pl.loop(0, slots)
    def images_in(i):
        take_in(0, i)

        @pl.when(i + ahead < slots)
        def _():
            coming(0, i + ahead).start()

        @pl.when(i + ahead >= slots)
        def _():
            coming(1, i + ahead - slots).start()

        @pl.when(i == 4)
        def _():
            run((ag1, 0, UP))

    run(*both(ag2, 0, ATT), (ag1, 0, DOWN), *both(ag1, 1, ATT))

    def statistic(s, rd, which):
        return jnp.where(s == 0, rstds[rd, which : which + 1], rstds[rd, 3 + which : 4 + which])

    def first_norm(s, rd, x):
        hat, rstd, mean = normalize(x)
        after_ref[rd, :] = hat
        rstds[rd, 3 * s : 3 * s + 1] = rstd
        rstds[rd, 3 * s + 2 : 3 * s + 3] = mean

    @pl.loop(0, slots // many)
    def norm_one(i):
        for m in range(many):
            xs[0, take(i, m), :] = io_one[i * many + m]
        rd = step_rows(i, many)
        x = xs[0, rd, :].astype(F32)
        token_rows = lax.broadcasted_iota(jnp.int32, (rows, width), 0) < length
        parts = [x[rows * m : rows * (m + 1)] for m in range(many)]
        x = jnp.concatenate([jnp.where(token_rows, part, part[0:1]) for part in parts], axis=0)
        xs[0, rd, :] = x.astype(LOW)
        first_norm(0, rd, x)

    run((ag2, 0, UP), *both(ag3, 0, ATT), (ag1, 1, UP), (ag1, 1, DOWN), (ag2, 0, DOWN), (ag3, 0, UP))

    @pl.loop(0, slots)
    def cotangents_in(i):
        take_in(1, i)

        @pl.when(i + ahead < slots)
        def _():
            coming(1, i + ahead).start()

    run(*both(ag4, 0, ATT), (ag3, 0, DOWN), *both(ag2, 1, ATT), *both(ag5, 0, ATT))

    @pl.loop(0, 2)
    def forward(s):
        @pl.loop(0, slots // few)
        def attention(i):
            @pl.when(s == 0)
            def _():
                events(i, {1: [(ag4, 0, UP), (ag2, 1, UP), (ag4, 0, DOWN)]})

            @pl.when(s == 1)
            def _():
                events(i, {1: [(ag4, 1, UP), (ag4, 1, DOWN)]})

            rd = step_rows(i, few)
            after_ref[rd, :] = attn_forward(s, xs[s, rd, :].astype(F32), after_ref[rd, :], i)

        @pl.when(s == 0)
        def _():
            run(*both(ag3, 1, ATT), (ag5, 0, UP), (ag5, 0, DOWN))

        @pl.when(s == 1)
        def _():
            run((ag5, 1, UP), (ag5, 1, DOWN))

        @pl.loop(0, slots // many)
        def feed_forward(i):
            @pl.when(s == 0)
            def _():
                events(i, {0: [(ag2, 1, DOWN), (ag3, 1, UP)], 1: both(ag4, 1, ATT)})

            rd = step_rows(i, many)

            @pl.when(s == 1)
            def _():
                for m in range(many):
                    far_copy(0, i * many + m, False).wait()
                    far_copy(1, i * many + m, False).wait()
                    shipped(0, 0, i * many + m)

            out, rstd2 = ff_forward(s, after_ref[rd, :], rd)
            for block in range(2):
                @pl.when(s == block)
                def _():
                    rstds[rd, 3 * block + 1 : 3 * block + 2] = rstd2

            out = only_live(i, out, many)
            for m in range(many):
                io_one[i * many + m] = out[rows * m : rows * m + length].astype(LOW)
                ship(0, s, i * many + m)

            @pl.when(s == 0)
            def _():
                for m in range(many):
                    far_copy(0, i * many + m, False).start()
                    far_copy(1, i * many + m, False).start()
                low = out.astype(LOW)
                xs[1, rd, :] = low
                first_norm(1, rd, low.astype(F32))

        @pl.when(s == 0)
        def _():
            run((ag3, 1, DOWN), *both(ag5, 1, ATT))

    for b in range(2):
        for g in groups:
            ag_sent(b, g)

    @pl.loop(0, 2)
    def backward(turn):
        s = 1 - turn

        @pl.when(s == 0)
        def _():
            run((rs3, 1, DOWN))

        @pl.loop(0, slots // many)
        def feed_forward(i):
            @pl.when(s == 0)
            def _():
                events(i, {1: [*both(rs1, 1, ATT), (rs3, 1, UP)]})
                for m in range(many):
                    far_copy(1, i * many + m, True).wait()

            rd = step_rows(i, many)
            for m in range(many):
                g = live(i * many + m) * io_two[i * many + m].astype(F32)
                low_g[take(i, m), :] = g.astype(LOW)
            after_ref[rd, :] = ff_backward(s, low_g[rd, :].astype(F32), rd, statistic(s, rd, 1))

        @pl.when(s == 0)
        def _():
            for i in range(slots):
                far_copy(0, i, True).wait()

        grads_down(s)
        run((rs0, s, DOWN))

        @pl.when(s == 1)
        def _():
            for i in range(slots):
                far_copy(0, i, True).start()

        grads_up(s)
        run((rs0, s, UP))

        @pl.when(s == 1)
        def _():
            for i in range(slots):
                far_copy(1, i, True).start()

        @pl.when(s == 0)
        def _():
            run((rs4, 1, DOWN), (rs4, 1, UP))

        @pl.loop(0, slots // few)
        def attention(i):
            @pl.when(s == 0)
            def _():
                events(i, {1: both(rs3, 1, ATT)})

            events(i, {1: [(rs1, s, DOWN), (rs1, s, UP)]})
            attn_backward(s, i)

        run((rs2, s, DOWN))

        @pl.when(s == 0)
        def _():
            run(*both(rs4, 1, ATT))

        grads_attn(s)
        run((rs0, s, ATT), (rs2, s, UP))

        @pl.loop(0, slots // many)
        def to_input(i):
            rd = step_rows(i, many)
            x = xs[s, rd, :].astype(F32)
            d_in = input_backward(s, after_ref[rd, :], rd, x, statistic(s, rd, 2), statistic(s, rd, 0))
            for m in range(many):
                @pl.when(s == 0)
                def _():
                    shipped(1, 1, i * many + m)

                io_two[i * many + m] = d_in[rows * m : rows * m + length].astype(LOW)
                ship(1, s, i * many + m)

        table_out(s)
        run((rs0, s, TAB))

    def sent_and_landed(kind):
        @pl.loop(0, slots)
        def _(i):
            shipped(kind, 1 - kind, i)
            for b in range(2):
                landed(kind, b, i)

    sent_and_landed(0)
    weave({
        1: lambda: run(*both(rs1, 0, ATT), (rs3, 0, DOWN), (rs3, 0, UP)),
        slots - raw.shape[0] + 1: lambda: sent_and_landed(1),
        slots + 2: lambda: run(*both(rs3_first, 0, ATT), (rs4, 0, DOWN), (rs4, 0, UP)),
    })
    run(*both(rs3_rest, 0, ATT))
    run(*both(rs4, 0, ATT))
    for b in range(2):
        for g in groups:
            rs_sent(b, g)


def output_kernel(
    woven, far_a, far_u, far_d, far_t, o_acts, o_ings, o_g1, o_s1, o_qkv, o_qv, o_out, o_bo, o_g2, o_s2, o_up, o_bu, o_down, o_bd,
    passing, f_a, f_u, f_d, f_t, sems, grad_sems
):
    coming = [
        pltpu.make_async_copy(source, target, grad_sems.at[i])
        for i, (source, target) in enumerate(((far_a, f_a), (far_u, f_u), (far_d, f_d), (far_t, f_t)))
    ]
    for copy in coming:
        copy.start()
    arriving, leaving = [], []
    for which, target in enumerate((o_acts, o_ings)):
        for i in range(target.shape[0]):
            arriving.append(pltpu.make_async_copy(woven.at[which, i], passing.at[which, i], sems.at[0, which, i]))
            leaving.append(pltpu.make_async_copy(passing.at[which, i], target.at[i], sems.at[1, which, i]))
    for copy in arriving:
        copy.start()
    for one, two in zip(arriving, leaving):
        one.wait()
        two.start()
    for copy in coming:
        copy.wait()
    unit, width = o_out.shape[1:]
    for half in range(2):
        o_down[0, 2 * unit * half : 2 * unit * (half + 1), :] = f_d[half]
        for sub in range(2):
            part = 2 * half + sub
            cols = slice(part * width, (part + 1) * width)
            o_up[0, :, cols] = f_u[half, unit * sub : unit * (sub + 1), :]
            piece = f_a[half, unit * sub : unit * (sub + 1), :]
            if part == 3:
                o_out[0] = piece
            else:
                o_qkv[0, :, cols] = piece
    begin = 0
    for out in (o_g1, o_s1, o_bo, o_g2, o_s2, o_bd, o_qv):
        part = out.shape[1]
        out[...] = f_t[0, :, begin : begin + part]
        begin += part
    o_bu[...] = f_t[1, :, 0 : o_bu.shape[1]]
    for copy in leaving:
        copy.wait()


def local(
    images, cotangent, counts,
    ln1_gain, ln1_bias, w_qkv, b_qv, w_out, b_out, ln2_gain, ln2_bias, w_up, b_up, w_down, b_down,
):
    micro_count, slots, length, width = images.shape
    ff = w_up.shape[2]
    rows = -(-length // 16) * 16
    n = lax.axis_size("fsdp")
    unit = width // n
    first, rest = radices(n)
    total = slots * rows
    head_dim = width // HEADS

    def vm(*shape, kind=LOW):
        return pltpu.VMEM(shape, kind)

    tall = [(2 * unit, LOW)] * 3 + [(1, F32)]
    dma = lambda *shape: pltpu.SemaphoreType.DMA(shape)
    outs = [((2, slots, length, 2, width), LOW)]
    outs += [((2, r, width), F32) for r, _ in tall] + [((total, ff), LOW)] * 2 + [((2, 2, slots, length, width), LOW)]
    scratch = [
        vm(2, total, width), vm(3, length, 2, width), vm(slots, length, width), vm(slots, length, width),
        *[vm(2, r, width, kind=kind) for r, kind in tall],
        vm(2, width, 3 * width), vm(2, width, width), vm(2, width, ff), vm(2, ff, width),
        vm(2, TABLE, width, kind=F32), vm(2, TABLE, width, kind=F32),
        vm(unit, width), vm(2 * unit, 2 * width), vm(4 * unit, 4 * width),
        vm(total, width, kind=F32), vm(2, total, width), vm(2, total, 3 * width), vm(2, slots, HEADS, rows, rows),
        vm(2, total, width),
        vm(2, total, width), vm(2, total, width), vm(total, 6, kind=F32),
        vm(total, ff), vm(total, ff), vm(total, width), vm(total, width), vm(width, total),
    ]
    scratch += [vm(2, 2, n, r, width, kind=kind) for r, kind in tall]
    scratch += [vm(n, r, width, kind=kind) for r, kind in tall]
    plane = rest * rest - 1
    for g, (r, kind) in enumerate(tall):
        direct = g in (ATT, TAB)
        scratch.append(vm(*((plane, first) if direct else (rest - 1, rest * first)), r, width, kind=kind))
    scratch += [vm(2, rest - 1, first, *tall[g][:1], width) for g in (UP, DOWN)]
    scratch += [vm(2, first, r, width, kind=kind) for r, kind in tall]
    scratch += [dma(2, slots), dma(2, 2 * slots), dma(2 * slots), dma(4, slots), dma(4, slots), dma(4, slots)]
    scratch += [dma(4, 2, first), dma(8, first)] + [dma(8, rest - 1)] * 4 + [dma(8, rest)] * 2
    scratch += [dma(8)] * 2 + [dma(8, plane, 2)] * 2 + [dma(8, rest - 1)] * 2 + [dma(8, first), dma(4, 2, first)]
    scratch += [pltpu.SemaphoreType.REGULAR((2, 4))]
    dims = (slots, length, rows, width, ff, head_dim, n)
    vmem = pl.BlockSpec(memory_space=pltpu.VMEM)
    hbm = pl.BlockSpec(memory_space=pltpu.HBM)
    woven, f_a, f_u, f_d, f_t, *_ = pl.pallas_call(
        functools.partial(whole_kernel, dims),
        out_shape=[jax.ShapeDtypeStruct(*o) for o in outs],
        in_specs=[hbm, hbm, pl.BlockSpec(memory_space=pltpu.SMEM)] + [vmem] * 12,
        out_specs=[hbm] + [vmem] * 4 + [hbm] * 3,
        scratch_shapes=scratch,
        compiler_params=pltpu.CompilerParams(
            vmem_limit_bytes=(64 << 20) - (96 << 10), collective_id=0, has_side_effects=True
        ),
    )(
        images.transpose(1, 2, 0, 3), cotangent.transpose(1, 2, 0, 3), counts.T, ln1_gain, ln1_bias, b_out, ln2_gain, ln2_bias, b_down, b_qv, b_up,
        w_qkv, w_out, w_up, w_down,
    )

    params = (
        ln1_gain, ln1_bias, w_qkv, b_qv, w_out, b_out, ln2_gain, ln2_bias, w_up, b_up, w_down, b_down
    )
    acts, ings, *grads = pl.pallas_call(
        output_kernel,
        out_shape=[jax.ShapeDtypeStruct(woven.shape[1:], LOW)] * 2
        + [jax.ShapeDtypeStruct(p.shape, F32) for p in params],
        in_specs=[hbm] * 5,
        out_specs=[hbm] * 2 + [vmem] * len(params),
        scratch_shapes=[
            vm(2, slots, length, 2, width), *[vm(2, r, width, kind=F32) for r, _ in tall], dma(2, 2, slots), dma(4)
        ],
        compiler_params=pltpu.CompilerParams(vmem_limit_bytes=(64 << 20) - (96 << 10)),
    )(woven, f_a, f_u, f_d, f_t)

    def as_given(value):
        return value.transpose(2, 0, 1, 3)[None]

    return (as_given(acts), as_given(ings), *grads)


def solution(mesh):
    split = P("section", "fsdp")
    cube = P("section", "fsdp", None)
    image = P(None, "fsdp", None, None)
    result = P("section", None, "fsdp", None, None)
    params = (split, split, cube, split, cube, split, split, split, cube, split, cube, split)
    return jax.shard_map(
        local,
        mesh=mesh,
        in_specs=(image, image, P(None, "fsdp")) + params,
        out_specs=(result, result) + params,
        check_vma=False,
    )
```

```python
import functools
import math

import jax
import jax.numpy as jnp
from jax import lax
from jax.experimental import pallas as pl
from jax.experimental.pallas import tpu as pltpu
from jax.sharding import PartitionSpec as P

HEADS = 6
EPS = 1e-06
F32 = jnp.float32
LOW = jnp.bfloat16

G1, S1, BO, G2, S2, BD, BQ, BV, BU = 0, 1, 2, 3, 4, 5, 6, 7, 8
TABLE = 16
TOGETHER, TOGETHER_ROWS = 2, 2
ATT, UP, DOWN, TAB = 0, 1, 2, 3


def radices(n):
    rest = max(r for r in range(1, n + 1) if r * r * r <= n and n % (r * r) == 0)
    return n // (rest * rest), rest


def mm(left, right):
    return jnp.dot(left, right, preferred_element_type=F32)


def mm_right(left, right):
    return lax.dot_general(left, right, (((1,), (1,)), ((), ())), preferred_element_type=F32)


def mm_left(left, right):
    return lax.dot_general(left, right, (((0,), (0,)), ((), ())), preferred_element_type=F32)


def normal_parts(pre):
    phi = 0.5 + 0.5 * lax.erf(pre * 0.7071067811865476)
    density = jnp.exp2(pre * pre * (-0.5 * 1.4426950408889634)) * 0.3989422804014327
    return phi, phi + pre * density


def normalize(value):
    mean = jnp.mean(value, axis=-1, keepdims=True)
    center = value - mean
    rstd = lax.rsqrt(jnp.mean(center * center, axis=-1, keepdims=True) + EPS)
    return center * rstd, rstd, mean


def normalize_back(d_hat, hat, rstd):
    mean_one = jnp.mean(d_hat, axis=-1, keepdims=True)
    mean_two = jnp.mean(d_hat * hat, axis=-1, keepdims=True)
    return rstd * (d_hat - mean_one - hat * mean_two)


def colsum(value):
    return jnp.sum(value, axis=0, keepdims=True)


def whole_kernel(dims, *refs):
    slots, length, rows, width, ff, head_dim, n = dims
    (
        images, cotangent, counts, v_g1, v_s1, v_bo, v_g2, v_s2, v_bd, v_qv, v_up, a_qkv, a_out, a_up, a_down,
        woven, f_a, f_u, f_d, f_t, hid_far, slope_far, out_far,
        xs, raw, io_one, io_two, pack_a, pack_u, pack_d, pack_t,
        wqkv, wout, wup, wdown, table, gtable, rep_one, rep_two, rep_four,
        after_ref, nrm1, qkv, prob, overs, ctx, hat2, rstds, hid, slope, dal, low_g, left_t,
        s_a, s_u, s_d, s_t, r0_a, r0_u, r0_d, r0_t, r1_a, r1_u, r1_d, r1_t, r2_u, r2_d,
        r3_a, r3_u, r3_d, r3_t,
        in_s, weave_in, weave_out, ship_s, ship_r, far_s, ag1_s, ag1_r, ag2_s, ag2_r, ag3_s, ag3_r, ag4_s, ag4_r,
        rs0_s, rs0_r, rs1_s, rs1_r, rs2_s, rs2_r, rs3_s, rs3_r, credit,
    ) = refs
    groups = (ATT, UP, DOWN, TAB)
    pack = (pack_a, pack_u, pack_d, pack_t)
    stage = (s_a, s_u, s_d, s_t)
    r0, r1, r2 = (r0_a, r0_u, r0_d, r0_t), (r1_a, r1_u, r1_d, r1_t), (None, r2_u, r2_d, None)
    r3, final = (r3_a, r3_u, r3_d, r3_t), (f_a, f_u, f_d, f_t)

    first, rest = radices(n)
    unit = width // n
    core = lax.axis_index("section")
    me = lax.axis_index("fsdp")
    dig_a, dig_b, dig_c = me // (rest * rest), (me // rest) % rest, me % rest
    dig_three, dig_two = dig_c + core * (dig_b - dig_c), dig_b + core * (dig_c - dig_b)
    step_three, step_two = 1 + core * (rest - 1), rest - core * (rest - 1)
    pos = (dig_three * rest + dig_two) * first + dig_a
    pos_of = ((dig_c * rest + dig_b) * first + dig_a, (dig_b * rest + dig_c) * first + dig_a)
    sibling = {"section": 1 - core}

    def place(half, j):
        a, b, c = j // (rest * rest), (j // rest) % rest, j % rest
        return ((c * rest + b) if half == 0 else (b * rest + c)) * first + a

    def peer_first(t):
        return {"fsdp": me + ((dig_a + t) % first - dig_a) * (rest * rest)}

    def peer_two(t):
        return {"fsdp": me + ((dig_two + t) % rest - dig_two) * step_two}

    def peer_three(t):
        return {"fsdp": me + ((dig_three + t) % rest - dig_three) * step_three}

    def peer_plane(three, two):
        here = ((dig_three + three) % rest - dig_three) * step_three
        return {"fsdp": me + here + ((dig_two + two) % rest - dig_two) * step_two}

    plane = [(three, two) for three in range(rest) for two in range(rest) if three or two]

    def remote(src, dst, s_sem, r_sem, device):
        return pltpu.make_async_remote_copy(
            src_ref=src, dst_ref=dst, send_sem=s_sem, recv_sem=r_sem, device_id=device,
            device_id_type=pl.DeviceIdType.MESH,
        )

    def slab_two(three, two):
        return pl.ds((three * rest + two) * first, first)

    def slab_three(three):
        return pl.ds(three * rest * first, rest * first)

    def fill_repeats():
        for ref in (rep_one, rep_two, rep_four):
            part = ref.shape[0]
            lanes = lax.broadcasted_iota(jnp.int32, ref.shape, 1).astype(F32)
            line = lax.broadcasted_iota(jnp.int32, ref.shape, 0).astype(F32)
            rest_of = lanes - part * jnp.floor((lanes + 0.5) * (1.0 / part))
            ref[...] = jnp.where(jnp.abs(rest_of - line) < 0.5, 1.0, 0.0).astype(LOW)

    def own_lanes(part):
        shape = (n, part * n)
        lanes = lax.broadcasted_iota(jnp.int32, shape, 1)
        begin = lax.broadcasted_iota(jnp.int32, shape, 0) * part
        return (lanes >= begin) & (lanes < begin + part)

    shares = (
        ((G1, unit, rep_one), (S1, unit, rep_one), (BO, unit, rep_one), (G2, unit, rep_one), (S2, unit, rep_one),
         (BD, unit, rep_one), (BQ, 2 * unit, rep_two)),
        ((BU, 4 * unit, rep_four),),
    )

    def table_in(b):
        for half in range(2):
            lines = jnp.concatenate([s_t[b, half, place(half, j)] for j in range(n)], axis=0)
            begin = 0
            for row, part, ref in shares[half]:
                spread = mm(lines[:, begin : begin + part].astype(LOW), ref[...])
                line = colsum(jnp.where(own_lanes(part), spread, 0.0))
                for i in range(part * n // width):
                    table[b, row + i : row + i + 1, :] = line[:, width * i : width * (i + 1)]
                begin += part

    def table_out(b):
        for half in range(2):
            parts, begin = [], 0
            for row, part, ref in shares[half]:
                count = part * n // width
                line = jnp.concatenate([gtable[b, row + i : row + i + 1, :] for i in range(count)], axis=1)
                parts.append(mm_right(jnp.where(own_lanes(part), line, 0.0).astype(LOW), ref[...]))
                begin += part
            parts.append(jnp.zeros((n, width - begin), F32))
            lines = jnp.concatenate(parts, axis=1)
            for j in range(n):
                s_t[b, half, place(half, j)] = lines[j : j + 1]

    def pack_own():
        for half in range(2):
            vectors = ((v_g1, v_s1, v_bo, v_g2, v_s2, v_bd, v_qv), (v_up,))[half]
            lines = [vector[...].astype(F32) for vector in vectors]
            lines.append(jnp.zeros((1, width - sum(line.shape[1] for line in lines)), F32))
            pack_t[half] = jnp.concatenate(lines, axis=1)
            for ref in (pack_a, pack_u):
                both = []
                for part in (2 * half, 2 * half + 1):
                    if ref is pack_u:
                        both.append(a_up[0, :, part * width : (part + 1) * width])
                    elif part == 3:
                        both.append(a_out[0])
                    else:
                        both.append(a_qkv[0, :, part * width : (part + 1) * width])
                ref[half] = jnp.concatenate([value.astype(F32) for value in both], axis=0).astype(LOW)
            pack_d[half] = a_down[0, 2 * unit * half : 2 * unit * (half + 1), :]

    def at(b, g):
        return len(groups) * b + g

    def ag1_copy(b, g, half, t):
        device = {"section": half, **peer_first(t)} if t else sibling
        return remote(
            pack[g].at[half], stage[g].at[b, half, pos_of[half]],
            ag1_s.at[g, half, t], ag1_r.at[at(b, g), t], device,
        )

    def ag1_landing(b, g, t):
        ref = stage[g].at[b, core, (dig_three * rest + dig_two) * first + (dig_a + first - t) % first]
        return remote(ref, ref, ag1_s.at[g, 0, t], ag1_r.at[at(b, g), t], sibling)

    def ag2_copy(b, g, t):
        ref = stage[g].at[b, core, slab_two(dig_three, dig_two)]
        return remote(ref, ref, ag2_s.at[at(b, g), t - 1], ag2_r.at[at(b, g), t - 1], peer_two(t))

    def ag3_copy(b, g, t):
        ref = stage[g].at[b, core, slab_three(dig_three)]
        return remote(ref, ref, ag3_s.at[at(b, g), t - 1], ag3_r.at[at(b, g), t - 1], peer_three(t))

    def ag4_copy(b, g, t):
        ref = stage[g].at[b, core, slab_three((dig_three + rest - t) % rest)]
        return remote(ref, ref, ag4_s.at[at(b, g), t], ag4_r.at[at(b, g), t], sibling)

    def ag4_landing(b, g, t):
        ref = stage[g].at[b, 1 - core, slab_three((dig_two + rest - t) % rest)]
        return remote(ref, ref, ag4_s.at[at(b, g), t], ag4_r.at[at(b, g), t], sibling)

    def ag1(b, g):
        @pl.when(core == b)
        def _():
            for t in range(1, first):
                for half in range(2):
                    ag1_copy(b, g, half, t).start()
            ag1_copy(b, g, 1 - b, 0).start()
            stage[g][b, b, pos] = pack[g][b]

    def ag2(b, g):
        for t in range(1, first):
            ag1_landing(b, g, t).wait_recv()

        @pl.when(core != b)
        def _():
            ag1_landing(b, g, 0).wait_recv()

        for t in range(1, rest):
            ag2_copy(b, g, t).start()

    def ag3(b, g):
        for t in range(1, rest):
            ag2_copy(b, g, t).wait_recv()
        for t in range(1, rest):
            ag3_copy(b, g, t).start()
        ag4_copy(b, g, 0).start()

    def ag4(b, g):
        for t in range(1, rest):
            ag3_copy(b, g, t).wait_recv()
            ag4_copy(b, g, t).start()

    def ag5(b, g):
        for t in range(rest):
            ag4_landing(b, g, t).wait_recv()
        lay_out(b, g)

    def ag_sent(b, g):
        @pl.when(core == b)
        def _():
            for t in range(1, first):
                for half in range(2):
                    ag1_copy(b, g, half, t).wait_send()
            ag1_copy(b, g, 1 - b, 0).wait_send()

        for t in range(1, rest):
            ag2_copy(b, g, t).wait_send()
            ag3_copy(b, g, t).wait_send()
        for t in range(rest):
            ag4_copy(b, g, t).wait_send()

    def lay_out(b, g):
        if g == TAB:
            table_in(b)
            return
        if g == DOWN:
            for j in range(n):
                for half in range(2):
                    begin = 4 * unit * j + 2 * unit * half
                    wdown[b, begin : begin + 2 * unit, :] = s_d[b, half, place(half, j)]
            return
        together = 16 // math.gcd(unit, 16)
        for half in range(2):
            for j in range(0, n, together):
                pieces = [stage[g][b, half, place(half, j + i)].astype(F32) for i in range(together)]
                for sub in range(2):
                    low = sub * unit
                    block = jnp.concatenate([piece[low : low + unit] for piece in pieces], axis=0).astype(LOW)
                    part = 2 * half + sub
                    down = slice(unit * j, unit * (j + together))
                    if g == UP:
                        wup[b, down, part * width : (part + 1) * width] = block
                    elif part == 3:
                        wout[b, down, :] = block
                    else:
                        wqkv[b, down, part * width : (part + 1) * width] = block

    def rs0_copy(b, g):
        return remote(stage[g].at[b, 1 - core], r0[g], rs0_s.at[at(b, g)], rs0_r.at[at(b, g)], sibling)

    def rs1_copy(b, g, t):
        return remote(
            stage[g].at[b, core, slab_three((dig_three + t) % rest)], r1[g].at[t - 1],
            rs1_s.at[at(b, g), t - 1, 0], rs1_r.at[at(b, g), t - 1, 0], peer_three(t),
        )

    def rs2_copy(b, g, t):
        return remote(
            stage[g].at[b, core, slab_two(dig_three, (dig_two + t) % rest)], r2[g].at[b, t - 1],
            rs2_s.at[at(b, g), t - 1], rs2_r.at[at(b, g), t - 1], peer_two(t),
        )

    def rs3_copy(b, g, t):
        there = (dig_three * rest + dig_two) * first + (dig_a + t) % first
        device = {"section": b, **peer_first(t)} if t else sibling
        return remote(
            stage[g].at[b, core, there], r3[g].at[core, t], rs3_s.at[at(b, g), t], rs3_r.at[g, core, t], device
        )

    chunk_count = 2 if first % 2 == 0 else 1
    chunk_size = first // chunk_count

    def plane_copy(b, g, t, part):
        three, two = plane[t]
        begin = (((dig_three + three) % rest) * rest + (dig_two + two) % rest) * first + chunk_size * part
        return remote(
            stage[g].at[b, core, pl.ds(begin, chunk_size)], r1[g].at[t, pl.ds(chunk_size * part, chunk_size)],
            rs1_s.at[at(b, g), t, part], rs1_r.at[at(b, g), t, part], peer_plane(three, two),
        )

    def rs0(b, g):
        @pl.when(b == 0)
        def _():
            pl.semaphore_wait(credit.at[0, g], 1)

        rs0_copy(b, g).start()

    def rs1(b, g):
        rs0_copy(b, g).wait_recv()

        @pl.loop(0, n)
        def _(p):
            stage[g][b, core, p] = stage[g][b, core, p] + r0[g][p]

        @pl.when(b == 1)
        def _():
            pl.semaphore_signal(credit.at[0, g], inc=1, device_id=sibling, device_id_type=pl.DeviceIdType.MESH)

        direct = g in (ATT, TAB)
        if rest > 1:
            @pl.when(b == 0)
            def _():
                pl.semaphore_wait(credit.at[1, g], len(plane) if direct else rest - 1)

        if direct:
            for part in range(chunk_count):
                for t in range(len(plane)):
                    plane_copy(b, g, t, part).start()
            return
        for t in range(1, rest):
            rs1_copy(b, g, t).start()

    def rs2(b, g):
        for t in range(1, rest):
            rs1_copy(b, g, t).wait_recv()

        @pl.loop(0, rest * first)
        def _(p):
            here = dig_three * rest * first + p
            total = stage[g][b, core, here].astype(F32)
            for t in range(1, rest):
                total = total + r1[g][t - 1, p].astype(F32)
            stage[g][b, core, here] = total.astype(stage[g].dtype)

        for t in range(1, rest):
            @pl.when(b == 1)
            def _():
                pl.semaphore_signal(
                    credit.at[1, g], inc=1, device_id=peer_three(t), device_id_type=pl.DeviceIdType.MESH
                )

            rs2_copy(b, g, t).start()

    def rs3_send(b, g, part):
        def here(digit):
            return (digit >= chunk_size * part) & (digit < chunk_size * (part + 1))

        for t in range(1, first):
            @pl.when(here((dig_a + t) % first))
            def _():
                rs3_copy(b, g, t).start()

        @pl.when(here(dig_a) & (core != b))
        def _():
            rs3_copy(b, g, 0).start()

    def rs3_part(b, g, part):
        for t in range(len(plane)):
            plane_copy(b, g, t, part).wait_recv()

        @pl.loop(chunk_size * part, chunk_size * (part + 1))
        def _(p):
            here = (dig_three * rest + dig_two) * first + p
            total = stage[g][b, core, here].astype(F32)
            for t in range(len(plane)):
                total = total + r1[g][t, p].astype(F32)
            stage[g][b, core, here] = total.astype(stage[g].dtype)

        rs3_send(b, g, part)

    def rs3_first(b, g):
        rs3_part(b, g, 0)

    def rs3_rest(b, g):
        for part in range(1, chunk_count):
            rs3_part(b, g, part)

    def rs3(b, g):
        if g in (ATT, TAB):
            for part in range(chunk_count):
                rs3_part(b, g, part)

            @pl.when(b == 1)
            def _():
                for three, two in plane:
                    pl.semaphore_signal(
                        credit.at[1, g], inc=1, device_id=peer_plane(three, two),
                        device_id_type=pl.DeviceIdType.MESH,
                    )

            return
        for t in range(1, rest):
            rs2_copy(b, g, t).wait_recv()

        @pl.loop(0, first)
        def _(p):
            here = (dig_three * rest + dig_two) * first + p
            total = stage[g][b, core, here].astype(F32)
            for t in range(1, rest):
                total = total + r2[g][b, t - 1, p].astype(F32)
            stage[g][b, core, here] = total.astype(stage[g].dtype)

        for part in range(chunk_count):
            rs3_send(b, g, part)

    def rs4(b, g):
        @pl.when(core == b)
        def _():
            for own in (True, False):
                half = core if own else 1 - core
                begin = int(own)
                for t in range(begin, first):
                    ref = r3[g].at[half, t]
                    remote(ref, ref, rs3_s.at[at(b, g), t], rs3_r.at[g, half, t], sibling).wait_recv()
                total = stage[g][b, core, pos].astype(F32) if own else None
                for t in range(begin, first):
                    value = r3[g][half, t].astype(F32)
                    total = value if total is None else total + value
                final[g][half] = total

    def rs_sent(b, g):
        rs0_copy(b, g).wait_send()
        if g in (ATT, TAB):
            for part in range(chunk_count):
                for t in range(len(plane)):
                    plane_copy(b, g, t, part).wait_send()
        else:
            for t in range(1, rest):
                rs1_copy(b, g, t).wait_send()
                rs2_copy(b, g, t).wait_send()
        for t in range(1, first):
            rs3_copy(b, g, t).wait_send()

        @pl.when(core != b)
        def _():
            rs3_copy(b, g, 0).wait_send()

    def rows_of(i, images_too=1):
        return pl.ds(pl.multiple_of(i * rows, 16), images_too * rows)

    few = TOGETHER if slots % TOGETHER == 0 else 1
    many = TOGETHER_ROWS if slots % TOGETHER_ROWS == 0 else 1

    def step_rows(i, count):
        return rows_of(i * count, count)

    def ship_parts(kind, b, i):
        src, out = (io_one, io_two)[kind].at[i], out_far.at[kind, core, i]
        q = 2 * kind + b
        near = pltpu.make_async_copy(src, out, ship_s.at[q, i])
        far = remote(src, out, ship_s.at[q, i], ship_r.at[q, i], sibling)
        return near, far

    def ship(kind, b, i):
        near, far = ship_parts(kind, b, i)

        @pl.when(core == b)
        def _():
            near.start()

        @pl.when(core != b)
        def _():
            far.start()

    def shipped(kind, b, i):
        near, far = ship_parts(kind, b, i)

        @pl.when(core == b)
        def _():
            near.wait()

        @pl.when(core != b)
        def _():
            far.wait_send()

    def landed(kind, b, i):
        q = 2 * kind + b
        ref = out_far.at[kind, 1 - core, i]

        @pl.when(core == b)
        def _():
            remote(ref, ref, ship_s.at[q, i], ship_r.at[q, i], sibling).wait_recv()

    def live(i):
        return jnp.where(i < counts[0, core], 1.0, 0.0).astype(F32)

    def only_live(i, value, count):
        parts = [value[rows * m : rows * (m + 1)] * live(i * count + m) for m in range(count)]
        return jnp.concatenate(parts, axis=0)

    def coming(which, i):
        slot = (which * slots + i) % raw.shape[0]
        return pltpu.make_async_copy((images, cotangent)[which].at[i], raw.at[slot], in_s.at[which, i])

    def take_in(which, i):
        coming(which, i).wait()
        both = raw[(which * slots + i) % raw.shape[0]].astype(F32)
        (io_one, io_two)[which][i] = jnp.where(core == 0, both[:, 0, :], both[:, 1, :]).astype(LOW)

    def weave(todo):
        ring = raw.shape[0]
        count = 2 * slots

        def fetch(t, m):
            source = out_far.at[t // slots, m, t % slots]
            return pltpu.make_async_copy(source, io_one.at[2 * (t % ring) + m], weave_in.at[m, t])

        def leave(t):
            return pltpu.make_async_copy(raw.at[t % ring], woven.at[t // slots, t % slots], weave_out.at[t])

        for t in range(ring - 1):
            for m in range(2):
                fetch(t, m).start()

        @pl.loop(0, count)
        def _(t):
            for when, act in todo.items():
                @pl.when(t == when)
                def _():
                    act()

            @pl.when(t + ring - 1 < count)
            def _():
                for m in range(2):
                    fetch(t + ring - 1, m).start()

            @pl.when(t >= ring)
            def _():
                leave(t - ring).wait()

            for m in range(2):
                fetch(t, m).wait()
                raw[t % ring, :, m, :] = io_one[2 * (t % ring) + m]
            leave(t).start()

        for t in range(count - ring, count):
            leave(t).wait()

    def far_copy(which, i, back):
        near, far = ((hid, hid_far), (slope, slope_far))[which]
        near, far = near.at[rows_of(i)], far.at[rows_of(i)]
        src, dst = (far, near) if back else (near, far)
        return pltpu.make_async_copy(src, dst, far_s.at[2 * int(back) + which, i])

    pairs = width // 128
    scale = head_dim ** -0.5
    lane = lax.broadcasted_iota(jnp.int32, (1, 128), 1)
    half_low = [(lane < head_dim).astype(LOW), (lane >= head_dim).astype(LOW)]
    half_f = [(lane < head_dim).astype(F32), (lane >= head_dim).astype(F32)]
    token = lax.broadcasted_iota(jnp.int32, (rows, 128), 0) < length
    half_valid = [jnp.where(token, half_f[j], 0.0).astype(LOW) for j in range(2)]
    valid_lanes = jnp.where(lax.broadcasted_iota(jnp.int32, (1, rows), 1) < length, 1.0, 0.0).astype(F32)
    spare = -rows % 128
    chunk = 2 * width
    chunks = ff // chunk

    def vec(s, r):
        return table[s, r : r + 1, :]

    def up_bias(s, c):
        begin = c * chunk
        row, col = begin // width, begin % width
        if col + chunk <= width:
            return table[s, BU + row : BU + row + 1, col : col + chunk]
        a = table[s, BU + row : BU + row + 1, col:width]
        b = table[s, BU + row + 1 : BU + row + 2, 0 : chunk - (width - col)]
        return jnp.concatenate([a, b], axis=1)

    def add_vec(s, r, value):
        gtable[s, r : r + 1, :] += value

    def add_up_bias(s, c, value):
        begin = c * chunk
        row, col = begin // width, begin % width
        if col + chunk <= width:
            gtable[s, BU + row : BU + row + 1, col : col + chunk] += value
        else:
            cut = width - col
            gtable[s, BU + row : BU + row + 1, col:width] += value[:, :cut]
            gtable[s, BU + row + 1 : BU + row + 2, 0 : chunk - cut] += value[:, cut:]

    def attn_forward(s, x, hat, i):
        rd = step_rows(i, few)
        nrm_ref, qkv_ref, prob_ref, ctx_ref = nrm1.at[s], qkv.at[s], prob.at[s], ctx.at[s]
        nrm = (hat * vec(s, G1) + vec(s, S1)).astype(LOW)
        nrm_ref[rd, :] = nrm
        mixed = mm(nrm, wqkv[s])
        q = (mixed[:, 0:width] + vec(s, BQ)).astype(LOW)
        k = mixed[:, width : 2 * width].astype(LOW)
        v = (mixed[:, 2 * width :] + vec(s, BV)).astype(LOW)
        qkv_ref[rd, 0:width] = q
        qkv_ref[rd, width : 2 * width] = k
        qkv_ref[rd, 2 * width :] = v
        images_out = []
        for m in range(few):
            mine = slice(rows * m, rows * (m + 1))
            parts = []
            for p in range(pairs):
                cols = slice(128 * p, 128 * p + 128)
                weights, sides = [], []
                for j in range(2):
                    keys = k[mine, cols] * half_low[j]
                    keys = jnp.concatenate([keys, keys[rows - spare :]], axis=0)
                    scores = mm_right(q[mine, cols], keys)
                    top = jnp.max(scores, axis=-1, keepdims=True)
                    e = jnp.exp2((scores - top) * (scale * 1.4426950408889634)).astype(LOW)
                    prob_ref[i * few + m, 2 * p + j] = e[:, :rows]
                    weights.append(e)
                    sides.append(jnp.concatenate([v[mine, cols] * half_valid[j], half_valid[j]], axis=1))
                    sides.append(jnp.zeros((spare, 256), LOW))
                total = mm(jnp.concatenate(weights, axis=1), jnp.concatenate(sides, axis=0))
                over = 1.0 / total[:, 128:]
                overs[s, rows_of(i * few + m), cols] = over.astype(LOW)
                parts.append((total[:, :128] * over).astype(LOW))
            images_out.append(jnp.concatenate(parts, axis=1))
        context = jnp.concatenate(images_out, axis=0)
        ctx_ref[rd, :] = context
        return x + mm(context, wout[s]) + vec(s, BO)

    def ff_forward(s, after, rd):
        hat, rstd, _ = normalize(after)
        hat2[s, rd, :] = hat.astype(LOW)
        nrm = (hat * vec(s, G2) + vec(s, S2)).astype(LOW)
        total = after + vec(s, BD)
        for c in range(chunks):
            cols = slice(chunk * c, chunk * c + chunk)
            pre = mm(nrm, wup[s, :, cols]) + up_bias(s, c)
            phi, slo = normal_parts(pre)
            h = (pre * phi).astype(LOW)
            hid[rd, cols] = h
            slope[rd, cols] = slo.astype(LOW)
            total = total + mm(h, wdown[s, cols, :])
        return total, rstd

    def ff_backward(s, g, rd, rstd):
        g_low = g.astype(LOW)
        add_vec(s, BD, colsum(g_low.astype(F32)))
        d_nrm = None
        for c in range(chunks):
            cols = slice(chunk * c, chunk * c + chunk)
            d_hid = mm_right(g_low, wdown[s, cols, :])
            d_pre = (d_hid * slope[rd, cols].astype(F32)).astype(LOW)
            slope[rd, cols] = d_pre
            add_up_bias(s, c, colsum(d_pre.astype(F32)))
            part = mm_right(d_pre, wup[s, :, cols])
            d_nrm = part if d_nrm is None else d_nrm + part
        hat = hat2[s, rd, :].astype(F32)
        add_vec(s, G2, colsum(d_nrm * hat))
        add_vec(s, S2, colsum(d_nrm))
        d_after = g + normalize_back(d_nrm * vec(s, G2), hat, rstd)
        low = d_after.astype(LOW)
        dal[rd, :] = low
        add_vec(s, BO, colsum(low.astype(F32)))
        return d_after

    def attn_backward(s, i):
        qkv_ref, prob_ref, ctx_ref = qkv.at[s], prob.at[s], ctx.at[s]
        rd = step_rows(i, few)
        d_context = mm_right(dal[rd, :], wout[s])
        d_context = (d_context * overs[s, rd, :].astype(F32)).astype(LOW)
        for m in range(few):
            rd = rows_of(i * few + m)
            d_ctx = d_context[rows * m : rows * (m + 1)]
            dq, dk, dv = [], [], []
            for p in range(pairs):
                cols = slice(128 * p, 128 * p + 128)
                q = qkv_ref[rd, 128 * p : 128 * p + 128]
                k = qkv_ref[rd, width + 128 * p : width + 128 * p + 128]
                v = qkv_ref[rd, 2 * width + 128 * p : 2 * width + 128 * p + 128]
                dc = d_ctx[:, cols]
                both = dc.astype(F32) * ctx_ref[rd, cols].astype(F32)
                q_t, dc_t = q.T, dc.T
                to_q, to_k, to_v = None, [], []
                for j in range(2):
                    e = prob_ref[i * few + m, 2 * p + j]
                    delta = jnp.sum(both * half_f[j], axis=-1, keepdims=True)
                    d_prob = mm_right(dc, v * half_low[j])
                    ds = (e.astype(F32) * (d_prob - delta)).astype(LOW)
                    part = mm(ds, k * half_valid[j])
                    to_q = part if to_q is None else to_q + part
                    head = slice(head_dim * j, head_dim * (j + 1))
                    to_k.append(mm(q_t[head], ds))
                    to_v.append(mm(dc_t[head], e))
                dq.append((to_q * scale).astype(LOW))
                dk.append((jnp.concatenate(to_k, axis=0) * (valid_lanes * scale)).astype(LOW).T)
                dv.append((jnp.concatenate(to_v, axis=0) * valid_lanes).astype(LOW).T)
            d_mixed = jnp.concatenate(dq + dk + dv, axis=1)
            qkv_ref[rd, :] = d_mixed
            add_vec(s, BQ, colsum(d_mixed[:, 0:width].astype(F32)))
            add_vec(s, BV, colsum(d_mixed[:, 2 * width :].astype(F32)))

    def input_backward(s, d_after, rd, x, mean, rstd):
        d_nrm = mm_right(qkv[s, rd, :], wqkv[s])
        hat = (x - mean) * rstd
        add_vec(s, G1, colsum(d_nrm * hat))
        add_vec(s, S1, colsum(d_nrm))
        return d_after + normalize_back(d_nrm * vec(s, G1), hat, rstd)

    def grads_down(s):
        left_t[...] = low_g[...].T

        @pl.loop(0, 2)
        def _(c):
            cols = pl.ds(pl.multiple_of(c * 2 * width, 128), 2 * width)
            block = mm(left_t[...], hid[:, cols]).T
            for i in range(n // 2):
                for half in range(2):
                    begin = 4 * unit * i + 2 * unit * half
                    s_d[s, half, place(half, c * (n // 2) + i)] = block[begin : begin + 2 * unit].astype(LOW)

    def pair_out(ref, s, half, one, two):
        for j in range(n):
            down = slice(unit * j, unit * (j + 1))
            piece = jnp.concatenate([one[down], two[down]], axis=0).astype(LOW)
            ref[s, half, place(half, j)] = piece

    def grads_up(s):
        left_t[...] = (hat2[s].astype(F32) * vec(s, G2) + vec(s, S2)).astype(LOW).T
        for half in range(2):
            both = mm(left_t[...], slope[:, 2 * half * width : 2 * (half + 1) * width])
            pair_out(s_u, s, half, both[:, :width], both[:, width:])

    def grads_attn(s):
        mix_s = qkv.at[s]
        left_t[...] = ctx[s].T
        four = mm(left_t[...], dal[...])
        left_t[...] = nrm1[s].T
        three = mm(left_t[...], mix_s[:, 2 * width :])
        pair_out(s_a, s, 1, three, four)
        both = mm(left_t[...], mix_s[:, 0 : 2 * width])
        pair_out(s_a, s, 0, both[:, :width], both[:, width:])

    barrier = pltpu.get_barrier_semaphore()
    greeted = [sibling]
    greeted += [{"section": half, **peer_first(t)} for t in range(1, first) for half in range(2)]
    greeted += [peer_plane(three, two) for three, two in plane]
    for device in greeted:
        pl.semaphore_signal(barrier, inc=1, device_id=device, device_id_type=pl.DeviceIdType.MESH)
    pack_own()
    pl.semaphore_wait(barrier, len(greeted))

    def run(*todo):
        for f, b, g in todo:
            f(b, g)

    def events(i, table_of):
        for when, todo in table_of.items():
            @pl.when(i == when)
            def _():
                run(*todo)

    def both(f, b, g):
        return [(f, b, g), (f, b, TAB)]

    def take(i, m):
        return pl.ds(pl.multiple_of((i * many + m) * rows, 16), length)

    ahead = raw.shape[0]
    run(*both(ag1, 0, ATT))
    for i in range(ahead):
        coming(0, i).start()
    fill_repeats()
    gtable[...] = jnp.zeros_like(gtable)
    low_g[...] = jnp.zeros_like(low_g)
    xs[0] = jnp.zeros_like(low_g)

    @pl.loop(0, slots)
    def images_in(i):
        take_in(0, i)

        @pl.when(i + ahead < slots)
        def _():
            coming(0, i + ahead).start()

        @pl.when(i + ahead >= slots)
        def _():
            coming(1, i + ahead - slots).start()

        @pl.when(i == 4)
        def _():
            run((ag1, 0, UP))

    run(*both(ag2, 0, ATT), (ag1, 0, DOWN), *both(ag1, 1, ATT))

    def statistic(s, rd, which):
        return jnp.where(s == 0, rstds[rd, which : which + 1], rstds[rd, 3 + which : 4 + which])

    def first_norm(s, rd, x):
        hat, rstd, mean = normalize(x)
        after_ref[rd, :] = hat
        rstds[rd, 3 * s : 3 * s + 1] = rstd
        rstds[rd, 3 * s + 2 : 3 * s + 3] = mean

    @pl.loop(0, slots // many)
    def norm_one(i):
        for m in range(many):
            xs[0, take(i, m), :] = io_one[i * many + m]
        rd = step_rows(i, many)
        x = xs[0, rd, :].astype(F32)
        token_rows = lax.broadcasted_iota(jnp.int32, (rows, width), 0) < length
        parts = [x[rows * m : rows * (m + 1)] for m in range(many)]
        x = jnp.concatenate([jnp.where(token_rows, part, part[0:1]) for part in parts], axis=0)
        xs[0, rd, :] = x.astype(LOW)
        first_norm(0, rd, x)

    run((ag2, 0, UP), *both(ag3, 0, ATT), (ag1, 1, UP), (ag1, 1, DOWN), (ag2, 0, DOWN), (ag3, 0, UP))

    @pl.loop(0, slots)
    def cotangents_in(i):
        take_in(1, i)

        @pl.when(i + ahead < slots)
        def _():
            coming(1, i + ahead).start()

    run(*both(ag4, 0, ATT), (ag3, 0, DOWN), *both(ag2, 1, ATT), *both(ag5, 0, ATT))

    @pl.loop(0, 2)
    def forward(s):
        @pl.loop(0, slots // few)
        def attention(i):
            @pl.when(s == 0)
            def _():
                events(i, {1: [(ag4, 0, UP), (ag2, 1, UP)], 2: [(ag4, 0, DOWN)]})

            @pl.when(s == 1)
            def _():
                events(i, {1: [(ag4, 1, UP)], 2: [(ag4, 1, DOWN)]})

            rd = step_rows(i, few)
            after_ref[rd, :] = attn_forward(s, xs[s, rd, :].astype(F32), after_ref[rd, :], i)

        @pl.when(s == 0)
        def _():
            run(*both(ag3, 1, ATT), (ag5, 0, UP), (ag5, 0, DOWN))

        @pl.when(s == 1)
        def _():
            run((ag5, 1, UP), (ag5, 1, DOWN))

        @pl.loop(0, slots // many)
        def feed_forward(i):
            @pl.when(s == 0)
            def _():
                events(i, {0: [(ag2, 1, DOWN), (ag3, 1, UP)], 2: both(ag4, 1, ATT)})

            rd = step_rows(i, many)

            @pl.when(s == 1)
            def _():
                for m in range(many):
                    far_copy(0, i * many + m, False).wait()
                    far_copy(1, i * many + m, False).wait()
                    shipped(0, 0, i * many + m)

            out, rstd2 = ff_forward(s, after_ref[rd, :], rd)
            for block in range(2):
                @pl.when(s == block)
                def _():
                    rstds[rd, 3 * block + 1 : 3 * block + 2] = rstd2

            out = only_live(i, out, many)
            for m in range(many):
                io_one[i * many + m] = out[rows * m : rows * m + length].astype(LOW)
                ship(0, s, i * many + m)

            @pl.when(s == 0)
            def _():
                for m in range(many):
                    far_copy(0, i * many + m, False).start()
                    far_copy(1, i * many + m, False).start()
                low = out.astype(LOW)
                xs[1, rd, :] = low
                first_norm(1, rd, low.astype(F32))

        @pl.when(s == 0)
        def _():
            run((ag3, 1, DOWN), *both(ag5, 1, ATT))

    for b in range(2):
        for g in groups:
            ag_sent(b, g)

    @pl.loop(0, 2)
    def backward(turn):
        s = 1 - turn

        @pl.when(s == 0)
        def _():
            run((rs3, 1, DOWN))

        @pl.loop(0, slots // many)
        def feed_forward(i):
            @pl.when(s == 0)
            def _():
                events(i, {1: [*both(rs1, 1, ATT), (rs3, 1, UP)]})
                for m in range(many):
                    far_copy(1, i * many + m, True).wait()

            rd = step_rows(i, many)
            for m in range(many):
                g = live(i * many + m) * io_two[i * many + m].astype(F32)
                low_g[take(i, m), :] = g.astype(LOW)
            after_ref[rd, :] = ff_backward(s, low_g[rd, :].astype(F32), rd, statistic(s, rd, 1))

        @pl.when(s == 0)
        def _():
            for i in range(slots):
                far_copy(0, i, True).wait()

        grads_down(s)
        run((rs0, s, DOWN))

        @pl.when(s == 1)
        def _():
            for i in range(slots):
                far_copy(0, i, True).start()

        grads_up(s)
        run((rs0, s, UP))

        @pl.when(s == 1)
        def _():
            for i in range(slots):
                far_copy(1, i, True).start()

        @pl.when(s == 0)
        def _():
            run((rs4, 1, DOWN), (rs4, 1, UP))

        @pl.loop(0, slots // few)
        def attention(i):
            @pl.when(s == 0)
            def _():
                events(i, {1: both(rs3, 1, ATT)})

            events(i, {1: [(rs1, s, DOWN), (rs1, s, UP)]})
            attn_backward(s, i)

        run((rs2, s, DOWN))

        @pl.when(s == 0)
        def _():
            run(*both(rs4, 1, ATT))

        grads_attn(s)
        run((rs0, s, ATT), (rs2, s, UP))

        @pl.loop(0, slots // many)
        def to_input(i):
            rd = step_rows(i, many)
            x = xs[s, rd, :].astype(F32)
            d_in = input_backward(s, after_ref[rd, :], rd, x, statistic(s, rd, 2), statistic(s, rd, 0))
            for m in range(many):
                @pl.when(s == 0)
                def _():
                    shipped(1, 1, i * many + m)

                io_two[i * many + m] = d_in[rows * m : rows * m + length].astype(LOW)
                ship(1, s, i * many + m)

        table_out(s)
        run((rs0, s, TAB))

    def sent_and_landed(kind):
        @pl.loop(0, slots)
        def _(i):
            shipped(kind, 1 - kind, i)
            for b in range(2):
                landed(kind, b, i)

    sent_and_landed(0)
    weave({
        1: lambda: run(*both(rs1, 0, ATT), (rs3, 0, DOWN), (rs3, 0, UP)),
        slots - raw.shape[0] + 1: lambda: sent_and_landed(1),
        slots + 2: lambda: run(*both(rs3_first, 0, ATT), (rs4, 0, DOWN), (rs4, 0, UP)),
    })
    run(*both(rs3_rest, 0, ATT))
    run(*both(rs4, 0, ATT))
    for b in range(2):
        for g in groups:
            rs_sent(b, g)


def output_kernel(
    woven, far_a, far_u, far_d, far_t, o_acts, o_ings, o_g1, o_s1, o_qkv, o_qv, o_out, o_bo, o_g2, o_s2, o_up, o_bu, o_down, o_bd,
    passing, f_a, f_u, f_d, f_t, sems, grad_sems
):
    coming = [
        pltpu.make_async_copy(source, target, grad_sems.at[i])
        for i, (source, target) in enumerate(((far_a, f_a), (far_u, f_u), (far_d, f_d), (far_t, f_t)))
    ]
    for copy in coming:
        copy.start()
    arriving, leaving = [], []
    for which, target in enumerate((o_acts, o_ings)):
        for i in range(target.shape[0]):
            arriving.append(pltpu.make_async_copy(woven.at[which, i], passing.at[which, i], sems.at[0, which, i]))
            leaving.append(pltpu.make_async_copy(passing.at[which, i], target.at[i], sems.at[1, which, i]))
    for copy in arriving:
        copy.start()
    for one, two in zip(arriving, leaving):
        one.wait()
        two.start()
    for copy in coming:
        copy.wait()
    unit, width = o_out.shape[1:]
    for half in range(2):
        o_down[0, 2 * unit * half : 2 * unit * (half + 1), :] = f_d[half]
        for sub in range(2):
            part = 2 * half + sub
            cols = slice(part * width, (part + 1) * width)
            o_up[0, :, cols] = f_u[half, unit * sub : unit * (sub + 1), :]
            piece = f_a[half, unit * sub : unit * (sub + 1), :]
            if part == 3:
                o_out[0] = piece
            else:
                o_qkv[0, :, cols] = piece
    begin = 0
    for out in (o_g1, o_s1, o_bo, o_g2, o_s2, o_bd, o_qv):
        part = out.shape[1]
        out[...] = f_t[0, :, begin : begin + part]
        begin += part
    o_bu[...] = f_t[1, :, 0 : o_bu.shape[1]]
    for copy in leaving:
        copy.wait()


def local(
    images, cotangent, counts,
    ln1_gain, ln1_bias, w_qkv, b_qv, w_out, b_out, ln2_gain, ln2_bias, w_up, b_up, w_down, b_down,
):
    micro_count, slots, length, width = images.shape
    ff = w_up.shape[2]
    rows = -(-length // 16) * 16
    n = lax.axis_size("fsdp")
    unit = width // n
    first, rest = radices(n)
    total = slots * rows
    head_dim = width // HEADS

    def vm(*shape, kind=LOW):
        return pltpu.VMEM(shape, kind)

    tall = [(2 * unit, LOW)] * 3 + [(1, F32)]
    dma = lambda *shape: pltpu.SemaphoreType.DMA(shape)
    outs = [((2, slots, length, 2, width), LOW)]
    outs += [((2, r, width), F32) for r, _ in tall] + [((total, ff), LOW)] * 2 + [((2, 2, slots, length, width), LOW)]
    scratch = [
        vm(2, total, width), vm(3, length, 2, width), vm(slots, length, width), vm(slots, length, width),
        *[vm(2, r, width, kind=kind) for r, kind in tall],
        vm(2, width, 3 * width), vm(2, width, width), vm(2, width, ff), vm(2, ff, width),
        vm(2, TABLE, width, kind=F32), vm(2, TABLE, width, kind=F32),
        vm(unit, width), vm(2 * unit, 2 * width), vm(4 * unit, 4 * width),
        vm(total, width, kind=F32), vm(2, total, width), vm(2, total, 3 * width), vm(2, slots, HEADS, rows, rows),
        vm(2, total, width),
        vm(2, total, width), vm(2, total, width), vm(total, 6, kind=F32),
        vm(total, ff), vm(total, ff), vm(total, width), vm(total, width), vm(width, total),
    ]
    scratch += [vm(2, 2, n, r, width, kind=kind) for r, kind in tall]
    scratch += [vm(n, r, width, kind=kind) for r, kind in tall]
    plane = rest * rest - 1
    for g, (r, kind) in enumerate(tall):
        direct = g in (ATT, TAB)
        scratch.append(vm(*((plane, first) if direct else (rest - 1, rest * first)), r, width, kind=kind))
    scratch += [vm(2, rest - 1, first, *tall[g][:1], width) for g in (UP, DOWN)]
    scratch += [vm(2, first, r, width, kind=kind) for r, kind in tall]
    scratch += [dma(2, slots), dma(2, 2 * slots), dma(2 * slots), dma(4, slots), dma(4, slots), dma(4, slots)]
    scratch += [dma(4, 2, first), dma(8, first)] + [dma(8, rest - 1)] * 4 + [dma(8, rest)] * 2
    scratch += [dma(8)] * 2 + [dma(8, plane, 2)] * 2 + [dma(8, rest - 1)] * 2 + [dma(8, first), dma(4, 2, first)]
    scratch += [pltpu.SemaphoreType.REGULAR((2, 4))]
    dims = (slots, length, rows, width, ff, head_dim, n)
    vmem = pl.BlockSpec(memory_space=pltpu.VMEM)
    hbm = pl.BlockSpec(memory_space=pltpu.HBM)
    woven, f_a, f_u, f_d, f_t, *_ = pl.pallas_call(
        functools.partial(whole_kernel, dims),
        out_shape=[jax.ShapeDtypeStruct(*o) for o in outs],
        in_specs=[hbm, hbm, pl.BlockSpec(memory_space=pltpu.SMEM)] + [vmem] * 12,
        out_specs=[hbm] + [vmem] * 4 + [hbm] * 3,
        scratch_shapes=scratch,
        compiler_params=pltpu.CompilerParams(
            vmem_limit_bytes=(64 << 20) - (96 << 10), collective_id=0, has_side_effects=True
        ),
    )(
        images.transpose(1, 2, 0, 3), cotangent.transpose(1, 2, 0, 3), counts.T, ln1_gain, ln1_bias, b_out, ln2_gain, ln2_bias, b_down, b_qv, b_up,
        w_qkv, w_out, w_up, w_down,
    )

    params = (
        ln1_gain, ln1_bias, w_qkv, b_qv, w_out, b_out, ln2_gain, ln2_bias, w_up, b_up, w_down, b_down
    )
    acts, ings, *grads = pl.pallas_call(
        output_kernel,
        out_shape=[jax.ShapeDtypeStruct(woven.shape[1:], LOW)] * 2
        + [jax.ShapeDtypeStruct(p.shape, F32) for p in params],
        in_specs=[hbm] * 5,
        out_specs=[hbm] * 2 + [vmem] * len(params),
        scratch_shapes=[
            vm(2, slots, length, 2, width), *[vm(2, r, width, kind=F32) for r, _ in tall], dma(2, 2, slots), dma(4)
        ],
        compiler_params=pltpu.CompilerParams(vmem_limit_bytes=(64 << 20) - (96 << 10)),
    )(woven, f_a, f_u, f_d, f_t)

    def as_given(value):
        return value.transpose(2, 0, 1, 3)[None]

    return (as_given(acts), as_given(ings), *grads)


def solution(mesh):
    split = P("section", "fsdp")
    cube = P("section", "fsdp", None)
    image = P(None, "fsdp", None, None)
    result = P("section", None, "fsdp", None, None)
    params = (split, split, cube, split, cube, split, split, split, cube, split, cube, split)
    return jax.shard_map(
        local,
        mesh=mesh,
        in_specs=(image, image, P(None, "fsdp")) + params,
        out_specs=(result, result) + params,
        check_vma=False,
    )
```

```python
import functools
import math

import jax
import jax.numpy as jnp
from jax import lax
from jax.experimental import pallas as pl
from jax.experimental.pallas import tpu as pltpu
from jax.sharding import PartitionSpec as P

HEADS = 6
EPS = 1e-06
F32 = jnp.float32
LOW = jnp.bfloat16

G1, S1, BO, G2, S2, BD, BQ, BV, BU = 0, 1, 2, 3, 4, 5, 6, 7, 8
TABLE = 16
TOGETHER, TOGETHER_ROWS = 1, 3
ATT, UP, DOWN, TAB = 0, 1, 2, 3


def radices(n):
    rest = max(r for r in range(1, n + 1) if r * r * r <= n and n % (r * r) == 0)
    return n // (rest * rest), rest


def mm(left, right):
    return jnp.dot(left, right, preferred_element_type=F32)


def mm_right(left, right):
    return lax.dot_general(left, right, (((1,), (1,)), ((), ())), preferred_element_type=F32)


def mm_left(left, right):
    return lax.dot_general(left, right, (((0,), (0,)), ((), ())), preferred_element_type=F32)


def normal_parts(pre):
    phi = 0.5 + 0.5 * lax.erf(pre * 0.7071067811865476)
    density = jnp.exp2(pre * pre * (-0.5 * 1.4426950408889634)) * 0.3989422804014327
    return phi, phi + pre * density


def normalize(value):
    mean = jnp.mean(value, axis=-1, keepdims=True)
    center = value - mean
    rstd = lax.rsqrt(jnp.mean(center * center, axis=-1, keepdims=True) + EPS)
    return center * rstd, rstd, mean


def normalize_back(d_hat, hat, rstd):
    mean_one = jnp.mean(d_hat, axis=-1, keepdims=True)
    mean_two = jnp.mean(d_hat * hat, axis=-1, keepdims=True)
    return rstd * (d_hat - mean_one - hat * mean_two)


def colsum(value):
    return jnp.sum(value, axis=0, keepdims=True)


def whole_kernel(dims, *refs):
    slots, length, rows, width, ff, head_dim, n = dims
    (
        images, cotangent, counts, v_g1, v_s1, v_bo, v_g2, v_s2, v_bd, v_qv, v_up, a_qkv, a_out, a_up, a_down,
        woven, f_a, f_u, f_d, f_t, hid_far, slope_far, out_far,
        xs, raw, io_one, io_two, pack_a, pack_u, pack_d, pack_t,
        wqkv, wout, wup, wdown, table, gtable, rep_one, rep_two, rep_four,
        after_ref, nrm1, qkv, prob, overs, ctx, hat2, rstds, hid, slope, dal, low_g, left_t,
        s_a, s_u, s_d, s_t, r0_a, r0_u, r0_d, r0_t, r1_a, r1_u, r1_d, r1_t, r2_u, r2_d,
        r3_a, r3_u, r3_d, r3_t,
        in_s, weave_in, weave_out, ship_s, ship_r, far_s, ag1_s, ag1_r, ag2_s, ag2_r, ag3_s, ag3_r, ag4_s, ag4_r,
        rs0_s, rs0_r, rs1_s, rs1_r, rs2_s, rs2_r, rs3_s, rs3_r, credit,
    ) = refs
    groups = (ATT, UP, DOWN, TAB)
    pack = (pack_a, pack_u, pack_d, pack_t)
    stage = (s_a, s_u, s_d, s_t)
    r0, r1, r2 = (r0_a, r0_u, r0_d, r0_t), (r1_a, r1_u, r1_d, r1_t), (None, r2_u, r2_d, None)
    r3, final = (r3_a, r3_u, r3_d, r3_t), (f_a, f_u, f_d, f_t)

    first, rest = radices(n)
    unit = width // n
    core = lax.axis_index("section")
    me = lax.axis_index("fsdp")
    dig_a, dig_b, dig_c = me // (rest * rest), (me // rest) % rest, me % rest
    dig_three, dig_two = dig_c + core * (dig_b - dig_c), dig_b + core * (dig_c - dig_b)
    step_three, step_two = 1 + core * (rest - 1), rest - core * (rest - 1)
    pos = (dig_three * rest + dig_two) * first + dig_a
    pos_of = ((dig_c * rest + dig_b) * first + dig_a, (dig_b * rest + dig_c) * first + dig_a)
    sibling = {"section": 1 - core}

    def place(half, j):
        a, b, c = j // (rest * rest), (j // rest) % rest, j % rest
        return ((c * rest + b) if half == 0 else (b * rest + c)) * first + a

    def peer_first(t):
        return {"fsdp": me + ((dig_a + t) % first - dig_a) * (rest * rest)}

    def peer_two(t):
        return {"fsdp": me + ((dig_two + t) % rest - dig_two) * step_two}

    def peer_three(t):
        return {"fsdp": me + ((dig_three + t) % rest - dig_three) * step_three}

    def peer_plane(three, two):
        here = ((dig_three + three) % rest - dig_three) * step_three
        return {"fsdp": me + here + ((dig_two + two) % rest - dig_two) * step_two}

    plane = [(three, two) for three in range(rest) for two in range(rest) if three or two]

    def remote(src, dst, s_sem, r_sem, device):
        return pltpu.make_async_remote_copy(
            src_ref=src, dst_ref=dst, send_sem=s_sem, recv_sem=r_sem, device_id=device,
            device_id_type=pl.DeviceIdType.MESH,
        )

    def slab_two(three, two):
        return pl.ds((three * rest + two) * first, first)

    def slab_three(three):
        return pl.ds(three * rest * first, rest * first)

    def fill_repeats():
        for ref in (rep_one, rep_two, rep_four):
            part = ref.shape[0]
            lanes = lax.broadcasted_iota(jnp.int32, ref.shape, 1).astype(F32)
            line = lax.broadcasted_iota(jnp.int32, ref.shape, 0).astype(F32)
            rest_of = lanes - part * jnp.floor((lanes + 0.5) * (1.0 / part))
            ref[...] = jnp.where(jnp.abs(rest_of - line) < 0.5, 1.0, 0.0).astype(LOW)

    def own_lanes(part):
        shape = (n, part * n)
        lanes = lax.broadcasted_iota(jnp.int32, shape, 1)
        begin = lax.broadcasted_iota(jnp.int32, shape, 0) * part
        return (lanes >= begin) & (lanes < begin + part)

    shares = (
        ((G1, unit, rep_one), (S1, unit, rep_one), (BO, unit, rep_one), (G2, unit, rep_one), (S2, unit, rep_one),
         (BD, unit, rep_one), (BQ, 2 * unit, rep_two)),
        ((BU, 4 * unit, rep_four),),
    )

    def table_in(b):
        for half in range(2):
            lines = jnp.concatenate([s_t[b, half, place(half, j)] for j in range(n)], axis=0)
            begin = 0
            for row, part, ref in shares[half]:
                spread = mm(lines[:, begin : begin + part].astype(LOW), ref[...])
                line = colsum(jnp.where(own_lanes(part), spread, 0.0))
                for i in range(part * n // width):
                    table[b, row + i : row + i + 1, :] = line[:, width * i : width * (i + 1)]
                begin += part

    def table_out(b):
        for half in range(2):
            parts, begin = [], 0
            for row, part, ref in shares[half]:
                count = part * n // width
                line = jnp.concatenate([gtable[b, row + i : row + i + 1, :] for i in range(count)], axis=1)
                parts.append(mm_right(jnp.where(own_lanes(part), line, 0.0).astype(LOW), ref[...]))
                begin += part
            parts.append(jnp.zeros((n, width - begin), F32))
            lines = jnp.concatenate(parts, axis=1)
            for j in range(n):
                s_t[b, half, place(half, j)] = lines[j : j + 1]

    def pack_own():
        for half in range(2):
            vectors = ((v_g1, v_s1, v_bo, v_g2, v_s2, v_bd, v_qv), (v_up,))[half]
            lines = [vector[...].astype(F32) for vector in vectors]
            lines.append(jnp.zeros((1, width - sum(line.shape[1] for line in lines)), F32))
            pack_t[half] = jnp.concatenate(lines, axis=1)
            for ref in (pack_a, pack_u):
                both = []
                for part in (2 * half, 2 * half + 1):
                    if ref is pack_u:
                        both.append(a_up[0, :, part * width : (part + 1) * width])
                    elif part == 3:
                        both.append(a_out[0])
                    else:
                        both.append(a_qkv[0, :, part * width : (part + 1) * width])
                ref[half] = jnp.concatenate([value.astype(F32) for value in both], axis=0).astype(LOW)
            pack_d[half] = a_down[0, 2 * unit * half : 2 * unit * (half + 1), :]

    def at(b, g):
        return len(groups) * b + g

    def ag1_copy(b, g, half, t):
        device = {"section": half, **peer_first(t)} if t else sibling
        return remote(
            pack[g].at[half], stage[g].at[b, half, pos_of[half]],
            ag1_s.at[g, half, t], ag1_r.at[at(b, g), t], device,
        )

    def ag1_landing(b, g, t):
        ref = stage[g].at[b, core, (dig_three * rest + dig_two) * first + (dig_a + first - t) % first]
        return remote(ref, ref, ag1_s.at[g, 0, t], ag1_r.at[at(b, g), t], sibling)

    def ag2_copy(b, g, t):
        ref = stage[g].at[b, core, slab_two(dig_three, dig_two)]
        return remote(ref, ref, ag2_s.at[at(b, g), t - 1], ag2_r.at[at(b, g), t - 1], peer_two(t))

    def ag3_copy(b, g, t):
        ref = stage[g].at[b, core, slab_three(dig_three)]
        return remote(ref, ref, ag3_s.at[at(b, g), t - 1], ag3_r.at[at(b, g), t - 1], peer_three(t))

    def ag4_copy(b, g, t):
        ref = stage[g].at[b, core, slab_three((dig_three + rest - t) % rest)]
        return remote(ref, ref, ag4_s.at[at(b, g), t], ag4_r.at[at(b, g), t], sibling)

    def ag4_landing(b, g, t):
        ref = stage[g].at[b, 1 - core, slab_three((dig_two + rest - t) % rest)]
        return remote(ref, ref, ag4_s.at[at(b, g), t], ag4_r.at[at(b, g), t], sibling)

    def ag1(b, g):
        @pl.when(core == b)
        def _():
            for t in range(1, first):
                for half in range(2):
                    ag1_copy(b, g, half, t).start()
            ag1_copy(b, g, 1 - b, 0).start()
            stage[g][b, b, pos] = pack[g][b]

    def ag2(b, g):
        for t in range(1, first):
            ag1_landing(b, g, t).wait_recv()

        @pl.when(core != b)
        def _():
            ag1_landing(b, g, 0).wait_recv()

        for t in range(1, rest):
            ag2_copy(b, g, t).start()

    def ag3(b, g):
        for t in range(1, rest):
            ag2_copy(b, g, t).wait_recv()
        for t in range(1, rest):
            ag3_copy(b, g, t).start()
        ag4_copy(b, g, 0).start()

    def ag4(b, g):
        for t in range(1, rest):
            ag3_copy(b, g, t).wait_recv()
            ag4_copy(b, g, t).start()

    def ag5(b, g):
        for t in range(rest):
            ag4_landing(b, g, t).wait_recv()
        lay_out(b, g)

    def ag_sent(b, g):
        @pl.when(core == b)
        def _():
            for t in range(1, first):
                for half in range(2):
                    ag1_copy(b, g, half, t).wait_send()
            ag1_copy(b, g, 1 - b, 0).wait_send()

        for t in range(1, rest):
            ag2_copy(b, g, t).wait_send()
            ag3_copy(b, g, t).wait_send()
        for t in range(rest):
            ag4_copy(b, g, t).wait_send()

    def lay_out(b, g):
        if g == TAB:
            table_in(b)
            return
        if g == DOWN:
            for j in range(n):
                for half in range(2):
                    begin = 4 * unit * j + 2 * unit * half
                    wdown[b, begin : begin + 2 * unit, :] = s_d[b, half, place(half, j)]
            return
        together = 16 // math.gcd(unit, 16)
        for half in range(2):
            for j in range(0, n, together):
                pieces = [stage[g][b, half, place(half, j + i)].astype(F32) for i in range(together)]
                for sub in range(2):
                    low = sub * unit
                    block = jnp.concatenate([piece[low : low + unit] for piece in pieces], axis=0).astype(LOW)
                    part = 2 * half + sub
                    down = slice(unit * j, unit * (j + together))
                    if g == UP:
                        wup[b, down, part * width : (part + 1) * width] = block
                    elif part == 3:
                        wout[b, down, :] = block
                    else:
                        wqkv[b, down, part * width : (part + 1) * width] = block

    def rs0_copy(b, g):
        return remote(stage[g].at[b, 1 - core], r0[g], rs0_s.at[at(b, g)], rs0_r.at[at(b, g)], sibling)

    def rs1_copy(b, g, t):
        return remote(
            stage[g].at[b, core, slab_three((dig_three + t) % rest)], r1[g].at[t - 1],
            rs1_s.at[at(b, g), t - 1, 0], rs1_r.at[at(b, g), t - 1, 0], peer_three(t),
        )

    def rs2_copy(b, g, t):
        return remote(
            stage[g].at[b, core, slab_two(dig_three, (dig_two + t) % rest)], r2[g].at[b, t - 1],
            rs2_s.at[at(b, g), t - 1], rs2_r.at[at(b, g), t - 1], peer_two(t),
        )

    def rs3_copy(b, g, t):
        there = (dig_three * rest + dig_two) * first + (dig_a + t) % first
        device = {"section": b, **peer_first(t)} if t else sibling
        return remote(
            stage[g].at[b, core, there], r3[g].at[core, t], rs3_s.at[at(b, g), t], rs3_r.at[g, core, t], device
        )

    chunk_count = 2 if first % 2 == 0 else 1
    chunk_size = first // chunk_count

    def plane_copy(b, g, t, part):
        three, two = plane[t]
        begin = (((dig_three + three) % rest) * rest + (dig_two + two) % rest) * first + chunk_size * part
        return remote(
            stage[g].at[b, core, pl.ds(begin, chunk_size)], r1[g].at[t, pl.ds(chunk_size * part, chunk_size)],
            rs1_s.at[at(b, g), t, part], rs1_r.at[at(b, g), t, part], peer_plane(three, two),
        )

    def rs0(b, g):
        @pl.when(b == 0)
        def _():
            pl.semaphore_wait(credit.at[0, g], 1)

        rs0_copy(b, g).start()

    def rs1(b, g):
        rs0_copy(b, g).wait_recv()

        @pl.loop(0, n)
        def _(p):
            stage[g][b, core, p] = stage[g][b, core, p] + r0[g][p]

        @pl.when(b == 1)
        def _():
            pl.semaphore_signal(credit.at[0, g], inc=1, device_id=sibling, device_id_type=pl.DeviceIdType.MESH)

        direct = g in (ATT, TAB)
        if rest > 1:
            @pl.when(b == 0)
            def _():
                pl.semaphore_wait(credit.at[1, g], len(plane) if direct else rest - 1)

        if direct:
            for part in range(chunk_count):
                for t in range(len(plane)):
                    plane_copy(b, g, t, part).start()
            return
        for t in range(1, rest):
            rs1_copy(b, g, t).start()

    def rs2(b, g):
        for t in range(1, rest):
            rs1_copy(b, g, t).wait_recv()

        @pl.loop(0, rest * first)
        def _(p):
            here = dig_three * rest * first + p
            total = stage[g][b, core, here].astype(F32)
            for t in range(1, rest):
                total = total + r1[g][t - 1, p].astype(F32)
            stage[g][b, core, here] = total.astype(stage[g].dtype)

        for t in range(1, rest):
            @pl.when(b == 1)
            def _():
                pl.semaphore_signal(
                    credit.at[1, g], inc=1, device_id=peer_three(t), device_id_type=pl.DeviceIdType.MESH
                )

            rs2_copy(b, g, t).start()

    def rs3_send(b, g, part):
        def here(digit):
            return (digit >= chunk_size * part) & (digit < chunk_size * (part + 1))

        for t in range(1, first):
            @pl.when(here((dig_a + t) % first))
            def _():
                rs3_copy(b, g, t).start()

        @pl.when(here(dig_a) & (core != b))
        def _():
            rs3_copy(b, g, 0).start()

    def rs3_part(b, g, part):
        for t in range(len(plane)):
            plane_copy(b, g, t, part).wait_recv()

        @pl.loop(chunk_size * part, chunk_size * (part + 1))
        def _(p):
            here = (dig_three * rest + dig_two) * first + p
            total = stage[g][b, core, here].astype(F32)
            for t in range(len(plane)):
                total = total + r1[g][t, p].astype(F32)
            stage[g][b, core, here] = total.astype(stage[g].dtype)

        rs3_send(b, g, part)

    def rs3_first(b, g):
        rs3_part(b, g, 0)

    def rs3_rest(b, g):
        for part in range(1, chunk_count):
            rs3_part(b, g, part)

    def rs3(b, g):
        if g in (ATT, TAB):
            for part in range(chunk_count):
                rs3_part(b, g, part)

            @pl.when(b == 1)
            def _():
                for three, two in plane:
                    pl.semaphore_signal(
                        credit.at[1, g], inc=1, device_id=peer_plane(three, two),
                        device_id_type=pl.DeviceIdType.MESH,
                    )

            return
        for t in range(1, rest):
            rs2_copy(b, g, t).wait_recv()

        @pl.loop(0, first)
        def _(p):
            here = (dig_three * rest + dig_two) * first + p
            total = stage[g][b, core, here].astype(F32)
            for t in range(1, rest):
                total = total + r2[g][b, t - 1, p].astype(F32)
            stage[g][b, core, here] = total.astype(stage[g].dtype)

        for part in range(chunk_count):
            rs3_send(b, g, part)

    def rs4(b, g):
        @pl.when(core == b)
        def _():
            for own in (True, False):
                half = core if own else 1 - core
                begin = int(own)
                for t in range(begin, first):
                    ref = r3[g].at[half, t]
                    remote(ref, ref, rs3_s.at[at(b, g), t], rs3_r.at[g, half, t], sibling).wait_recv()
                total = stage[g][b, core, pos].astype(F32) if own else None
                for t in range(begin, first):
                    value = r3[g][half, t].astype(F32)
                    total = value if total is None else total + value
                final[g][half] = total

    def rs_sent(b, g):
        rs0_copy(b, g).wait_send()
        if g in (ATT, TAB):
            for part in range(chunk_count):
                for t in range(len(plane)):
                    plane_copy(b, g, t, part).wait_send()
        else:
            for t in range(1, rest):
                rs1_copy(b, g, t).wait_send()
                rs2_copy(b, g, t).wait_send()
        for t in range(1, first):
            rs3_copy(b, g, t).wait_send()

        @pl.when(core != b)
        def _():
            rs3_copy(b, g, 0).wait_send()

    def rows_of(i, images_too=1):
        return pl.ds(pl.multiple_of(i * rows, 16), images_too * rows)

    few = TOGETHER if slots % TOGETHER == 0 else 1
    many = TOGETHER_ROWS if slots % TOGETHER_ROWS == 0 else 1

    def step_rows(i, count):
        return rows_of(i * count, count)

    def ship_parts(kind, b, i):
        src, out = (io_one, io_two)[kind].at[i], out_far.at[kind, core, i]
        q = 2 * kind + b
        near = pltpu.make_async_copy(src, out, ship_s.at[q, i])
        far = remote(src, out, ship_s.at[q, i], ship_r.at[q, i], sibling)
        return near, far

    def ship(kind, b, i):
        near, far = ship_parts(kind, b, i)

        @pl.when(core == b)
        def _():
            near.start()

        @pl.when(core != b)
        def _():
            far.start()

    def shipped(kind, b, i):
        near, far = ship_parts(kind, b, i)

        @pl.when(core == b)
        def _():
            near.wait()

        @pl.when(core != b)
        def _():
            far.wait_send()

    def landed(kind, b, i):
        q = 2 * kind + b
        ref = out_far.at[kind, 1 - core, i]

        @pl.when(core == b)
        def _():
            remote(ref, ref, ship_s.at[q, i], ship_r.at[q, i], sibling).wait_recv()

    def live(i):
        return jnp.where(i < counts[0, core], 1.0, 0.0).astype(F32)

    def only_live(i, value, count):
        parts = [value[rows * m : rows * (m + 1)] * live(i * count + m) for m in range(count)]
        return jnp.concatenate(parts, axis=0)

    def coming(which, i):
        slot = (which * slots + i) % raw.shape[0]
        return pltpu.make_async_copy((images, cotangent)[which].at[i], raw.at[slot], in_s.at[which, i])

    def take_in(which, i):
        coming(which, i).wait()
        both = raw[(which * slots + i) % raw.shape[0]].astype(F32)
        (io_one, io_two)[which][i] = jnp.where(core == 0, both[:, 0, :], both[:, 1, :]).astype(LOW)

    def weave(todo):
        ring = raw.shape[0]
        count = 2 * slots

        def fetch(t, m):
            source = out_far.at[t // slots, m, t % slots]
            return pltpu.make_async_copy(source, io_one.at[2 * (t % ring) + m], weave_in.at[m, t])

        def leave(t):
            return pltpu.make_async_copy(raw.at[t % ring], woven.at[t // slots, t % slots], weave_out.at[t])

        for t in range(ring - 1):
            for m in range(2):
                fetch(t, m).start()

        @pl.loop(0, count)
        def _(t):
            for when, act in todo.items():
                @pl.when(t == when)
                def _():
                    act()

            @pl.when(t + ring - 1 < count)
            def _():
                for m in range(2):
                    fetch(t + ring - 1, m).start()

            @pl.when(t >= ring)
            def _():
                leave(t - ring).wait()

            for m in range(2):
                fetch(t, m).wait()
                raw[t % ring, :, m, :] = io_one[2 * (t % ring) + m]
            leave(t).start()

        for t in range(count - ring, count):
            leave(t).wait()

    def far_copy(which, i, back):
        near, far = ((hid, hid_far), (slope, slope_far))[which]
        near, far = near.at[rows_of(i)], far.at[rows_of(i)]
        src, dst = (far, near) if back else (near, far)
        return pltpu.make_async_copy(src, dst, far_s.at[2 * int(back) + which, i])

    pairs = width // 128
    scale = head_dim ** -0.5
    lane = lax.broadcasted_iota(jnp.int32, (1, 128), 1)
    half_low = [(lane < head_dim).astype(LOW), (lane >= head_dim).astype(LOW)]
    half_f = [(lane < head_dim).astype(F32), (lane >= head_dim).astype(F32)]
    token = lax.broadcasted_iota(jnp.int32, (rows, 128), 0) < length
    half_valid = [jnp.where(token, half_f[j], 0.0).astype(LOW) for j in range(2)]
    valid_lanes = jnp.where(lax.broadcasted_iota(jnp.int32, (1, rows), 1) < length, 1.0, 0.0).astype(F32)
    spare = -rows % 128
    chunk = 2 * width
    chunks = ff // chunk

    def vec(s, r):
        return table[s, r : r + 1, :]

    def up_bias(s, c):
        begin = c * chunk
        row, col = begin // width, begin % width
        if col + chunk <= width:
            return table[s, BU + row : BU + row + 1, col : col + chunk]
        a = table[s, BU + row : BU + row + 1, col:width]
        b = table[s, BU + row + 1 : BU + row + 2, 0 : chunk - (width - col)]
        return jnp.concatenate([a, b], axis=1)

    def add_vec(s, r, value):
        gtable[s, r : r + 1, :] += value

    def add_up_bias(s, c, value):
        begin = c * chunk
        row, col = begin // width, begin % width
        if col + chunk <= width:
            gtable[s, BU + row : BU + row + 1, col : col + chunk] += value
        else:
            cut = width - col
            gtable[s, BU + row : BU + row + 1, col:width] += value[:, :cut]
            gtable[s, BU + row + 1 : BU + row + 2, 0 : chunk - cut] += value[:, cut:]

    def attn_forward(s, x, hat, i):
        rd = step_rows(i, few)
        nrm_ref, qkv_ref, prob_ref, ctx_ref = nrm1.at[s], qkv.at[s], prob.at[s], ctx.at[s]
        nrm = (hat * vec(s, G1) + vec(s, S1)).astype(LOW)
        nrm_ref[rd, :] = nrm
        mixed = mm(nrm, wqkv[s])
        q = (mixed[:, 0:width] + vec(s, BQ)).astype(LOW)
        k = mixed[:, width : 2 * width].astype(LOW)
        v = (mixed[:, 2 * width :] + vec(s, BV)).astype(LOW)
        qkv_ref[rd, 0:width] = q
        qkv_ref[rd, width : 2 * width] = k
        qkv_ref[rd, 2 * width :] = v
        images_out = []
        for m in range(few):
            mine = slice(rows * m, rows * (m + 1))
            parts = []
            for p in range(pairs):
                cols = slice(128 * p, 128 * p + 128)
                weights, sides = [], []
                for j in range(2):
                    keys = k[mine, cols] * half_low[j]
                    keys = jnp.concatenate([keys, keys[rows - spare :]], axis=0)
                    scores = mm_right(q[mine, cols], keys)
                    top = jnp.max(scores, axis=-1, keepdims=True)
                    e = jnp.exp2((scores - top) * (scale * 1.4426950408889634)).astype(LOW)
                    prob_ref[i * few + m, 2 * p + j] = e[:, :rows]
                    weights.append(e)
                    sides.append(jnp.concatenate([v[mine, cols] * half_valid[j], half_valid[j]], axis=1))
                    sides.append(jnp.zeros((spare, 256), LOW))
                total = mm(jnp.concatenate(weights, axis=1), jnp.concatenate(sides, axis=0))
                over = 1.0 / total[:, 128:]
                overs[s, rows_of(i * few + m), cols] = over.astype(LOW)
                parts.append((total[:, :128] * over).astype(LOW))
            images_out.append(jnp.concatenate(parts, axis=1))
        context = jnp.concatenate(images_out, axis=0)
        ctx_ref[rd, :] = context
        return x + mm(context, wout[s]) + vec(s, BO)

    def ff_forward(s, after, rd):
        hat, rstd, _ = normalize(after)
        hat2[s, rd, :] = hat.astype(LOW)
        nrm = (hat * vec(s, G2) + vec(s, S2)).astype(LOW)
        total = after + vec(s, BD)
        for c in range(chunks):
            cols = slice(chunk * c, chunk * c + chunk)
            pre = mm(nrm, wup[s, :, cols]) + up_bias(s, c)
            phi, slo = normal_parts(pre)
            h = (pre * phi).astype(LOW)
            hid[rd, cols] = h
            slope[rd, cols] = slo.astype(LOW)
            total = total + mm(h, wdown[s, cols, :])
        return total, rstd

    def ff_backward(s, g, rd, rstd):
        g_low = g.astype(LOW)
        add_vec(s, BD, colsum(g_low.astype(F32)))
        d_nrm = None
        for c in range(chunks):
            cols = slice(chunk * c, chunk * c + chunk)
            d_hid = mm_right(g_low, wdown[s, cols, :])
            d_pre = (d_hid * slope[rd, cols].astype(F32)).astype(LOW)
            slope[rd, cols] = d_pre
            add_up_bias(s, c, colsum(d_pre.astype(F32)))
            part = mm_right(d_pre, wup[s, :, cols])
            d_nrm = part if d_nrm is None else d_nrm + part
        hat = hat2[s, rd, :].astype(F32)
        add_vec(s, G2, colsum(d_nrm * hat))
        add_vec(s, S2, colsum(d_nrm))
        d_after = g + normalize_back(d_nrm * vec(s, G2), hat, rstd)
        low = d_after.astype(LOW)
        dal[rd, :] = low
        add_vec(s, BO, colsum(low.astype(F32)))
        return d_after

    def attn_backward(s, i):
        qkv_ref, prob_ref, ctx_ref = qkv.at[s], prob.at[s], ctx.at[s]
        rd = step_rows(i, few)
        d_context = mm_right(dal[rd, :], wout[s])
        d_context = (d_context * overs[s, rd, :].astype(F32)).astype(LOW)
        for m in range(few):
            rd = rows_of(i * few + m)
            d_ctx = d_context[rows * m : rows * (m + 1)]
            dq, dk, dv = [], [], []
            for p in range(pairs):
                cols = slice(128 * p, 128 * p + 128)
                q = qkv_ref[rd, 128 * p : 128 * p + 128]
                k = qkv_ref[rd, width + 128 * p : width + 128 * p + 128]
                v = qkv_ref[rd, 2 * width + 128 * p : 2 * width + 128 * p + 128]
                dc = d_ctx[:, cols]
                both = dc.astype(F32) * ctx_ref[rd, cols].astype(F32)
                q_t, dc_t = q.T, dc.T
                to_q, to_k, to_v = None, [], []
                for j in range(2):
                    e = prob_ref[i * few + m, 2 * p + j]
                    delta = jnp.sum(both * half_f[j], axis=-1, keepdims=True)
                    d_prob = mm_right(dc, v * half_low[j])
                    ds = (e.astype(F32) * (d_prob - delta)).astype(LOW)
                    part = mm(ds, k * half_valid[j])
                    to_q = part if to_q is None else to_q + part
                    head = slice(head_dim * j, head_dim * (j + 1))
                    to_k.append(mm(q_t[head], ds))
                    to_v.append(mm(dc_t[head], e))
                dq.append((to_q * scale).astype(LOW))
                dk.append((jnp.concatenate(to_k, axis=0) * (valid_lanes * scale)).astype(LOW).T)
                dv.append((jnp.concatenate(to_v, axis=0) * valid_lanes).astype(LOW).T)
            d_mixed = jnp.concatenate(dq + dk + dv, axis=1)
            qkv_ref[rd, :] = d_mixed
            add_vec(s, BQ, colsum(d_mixed[:, 0:width].astype(F32)))
            add_vec(s, BV, colsum(d_mixed[:, 2 * width :].astype(F32)))

    def input_backward(s, d_after, rd, x, mean, rstd):
        d_nrm = mm_right(qkv[s, rd, :], wqkv[s])
        hat = (x - mean) * rstd
        add_vec(s, G1, colsum(d_nrm * hat))
        add_vec(s, S1, colsum(d_nrm))
        return d_after + normalize_back(d_nrm * vec(s, G1), hat, rstd)

    def grads_down(s):
        left_t[...] = low_g[...].T

        @pl.loop(0, 2)
        def _(c):
            cols = pl.ds(pl.multiple_of(c * 2 * width, 128), 2 * width)
            block = mm(left_t[...], hid[:, cols]).T
            for i in range(n // 2):
                for half in range(2):
                    begin = 4 * unit * i + 2 * unit * half
                    s_d[s, half, place(half, c * (n // 2) + i)] = block[begin : begin + 2 * unit].astype(LOW)

    def pair_out(ref, s, half, one, two):
        for j in range(n):
            down = slice(unit * j, unit * (j + 1))
            piece = jnp.concatenate([one[down], two[down]], axis=0).astype(LOW)
            ref[s, half, place(half, j)] = piece

    def grads_up(s):
        left_t[...] = (hat2[s].astype(F32) * vec(s, G2) + vec(s, S2)).astype(LOW).T
        for half in range(2):
            both = mm(left_t[...], slope[:, 2 * half * width : 2 * (half + 1) * width])
            pair_out(s_u, s, half, both[:, :width], both[:, width:])

    def grads_attn(s):
        mix_s = qkv.at[s]
        left_t[...] = ctx[s].T
        four = mm(left_t[...], dal[...])
        left_t[...] = nrm1[s].T
        three = mm(left_t[...], mix_s[:, 2 * width :])
        pair_out(s_a, s, 1, three, four)
        both = mm(left_t[...], mix_s[:, 0 : 2 * width])
        pair_out(s_a, s, 0, both[:, :width], both[:, width:])

    barrier = pltpu.get_barrier_semaphore()
    greeted = [sibling]
    greeted += [{"section": half, **peer_first(t)} for t in range(1, first) for half in range(2)]
    greeted += [peer_plane(three, two) for three, two in plane]
    for device in greeted:
        pl.semaphore_signal(barrier, inc=1, device_id=device, device_id_type=pl.DeviceIdType.MESH)
    pack_own()
    pl.semaphore_wait(barrier, len(greeted))

    def run(*todo):
        for f, b, g in todo:
            f(b, g)

    def events(i, table_of):
        for when, todo in table_of.items():
            @pl.when(i == when)
            def _():
                run(*todo)

    def both(f, b, g):
        return [(f, b, g), (f, b, TAB)]

    def take(i, m):
        return pl.ds(pl.multiple_of((i * many + m) * rows, 16), length)

    ahead = raw.shape[0]
    run(*both(ag1, 0, ATT))
    for i in range(ahead):
        coming(0, i).start()
    fill_repeats()
    gtable[...] = jnp.zeros_like(gtable)
    low_g[...] = jnp.zeros_like(low_g)
    xs[0] = jnp.zeros_like(low_g)

    @pl.loop(0, slots)
    def images_in(i):
        take_in(0, i)

        @pl.when(i + ahead < slots)
        def _():
            coming(0, i + ahead).start()

        @pl.when(i + ahead >= slots)
        def _():
            coming(1, i + ahead - slots).start()

        @pl.when(i == 4)
        def _():
            run((ag1, 0, UP))

    run(*both(ag2, 0, ATT), (ag1, 0, DOWN), *both(ag1, 1, ATT))

    def statistic(s, rd, which):
        return jnp.where(s == 0, rstds[rd, which : which + 1], rstds[rd, 3 + which : 4 + which])

    def first_norm(s, rd, x):
        hat, rstd, mean = normalize(x)
        after_ref[rd, :] = hat
        rstds[rd, 3 * s : 3 * s + 1] = rstd
        rstds[rd, 3 * s + 2 : 3 * s + 3] = mean

    @pl.loop(0, slots // many)
    def norm_one(i):
        for m in range(many):
            xs[0, take(i, m), :] = io_one[i * many + m]
        rd = step_rows(i, many)
        x = xs[0, rd, :].astype(F32)
        token_rows = lax.broadcasted_iota(jnp.int32, (rows, width), 0) < length
        parts = [x[rows * m : rows * (m + 1)] for m in range(many)]
        x = jnp.concatenate([jnp.where(token_rows, part, part[0:1]) for part in parts], axis=0)
        xs[0, rd, :] = x.astype(LOW)
        first_norm(0, rd, x)

    run((ag2, 0, UP), *both(ag3, 0, ATT), (ag1, 1, UP), (ag1, 1, DOWN), (ag2, 0, DOWN), (ag3, 0, UP))

    @pl.loop(0, slots)
    def cotangents_in(i):
        take_in(1, i)

        @pl.when(i + ahead < slots)
        def _():
            coming(1, i + ahead).start()

    run(*both(ag4, 0, ATT), (ag3, 0, DOWN), *both(ag2, 1, ATT), *both(ag5, 0, ATT))

    @pl.loop(0, 2)
    def forward(s):
        @pl.loop(0, slots // few)
        def attention(i):
            @pl.when(s == 0)
            def _():
                events(i, {2: [(ag4, 0, UP), (ag2, 1, UP)], 4: [(ag4, 0, DOWN)]})

            @pl.when(s == 1)
            def _():
                events(i, {2: [(ag4, 1, UP)], 5: [(ag4, 1, DOWN)]})

            rd = step_rows(i, few)
            after_ref[rd, :] = attn_forward(s, xs[s, rd, :].astype(F32), after_ref[rd, :], i)

        @pl.when(s == 0)
        def _():
            run(*both(ag3, 1, ATT), (ag5, 0, UP), (ag5, 0, DOWN))

        @pl.when(s == 1)
        def _():
            run((ag5, 1, UP), (ag5, 1, DOWN))

        @pl.loop(0, slots // many)
        def feed_forward(i):
            @pl.when(s == 0)
            def _():
                events(i, {0: [(ag2, 1, DOWN), (ag3, 1, UP)], 1: both(ag4, 1, ATT)})

            rd = step_rows(i, many)

            @pl.when(s == 1)
            def _():
                for m in range(many):
                    far_copy(0, i * many + m, False).wait()
                    far_copy(1, i * many + m, False).wait()
                    shipped(0, 0, i * many + m)

            out, rstd2 = ff_forward(s, after_ref[rd, :], rd)
            for block in range(2):
                @pl.when(s == block)
                def _():
                    rstds[rd, 3 * block + 1 : 3 * block + 2] = rstd2

            out = only_live(i, out, many)
            for m in range(many):
                io_one[i * many + m] = out[rows * m : rows * m + length].astype(LOW)
                ship(0, s, i * many + m)

            @pl.when(s == 0)
            def _():
                for m in range(many):
                    far_copy(0, i * many + m, False).start()
                    far_copy(1, i * many + m, False).start()
                low = out.astype(LOW)
                xs[1, rd, :] = low
                first_norm(1, rd, low.astype(F32))

        @pl.when(s == 0)
        def _():
            run((ag3, 1, DOWN), *both(ag5, 1, ATT))

    for b in range(2):
        for g in groups:
            ag_sent(b, g)

    @pl.loop(0, 2)
    def backward(turn):
        s = 1 - turn

        @pl.when(s == 0)
        def _():
            run((rs3, 1, DOWN))

        @pl.loop(0, slots // many)
        def feed_forward(i):
            @pl.when(s == 0)
            def _():
                events(i, {1: [*both(rs1, 1, ATT), (rs3, 1, UP)]})
                for m in range(many):
                    far_copy(1, i * many + m, True).wait()

            rd = step_rows(i, many)
            for m in range(many):
                g = live(i * many + m) * io_two[i * many + m].astype(F32)
                low_g[take(i, m), :] = g.astype(LOW)
            after_ref[rd, :] = ff_backward(s, low_g[rd, :].astype(F32), rd, statistic(s, rd, 1))

        @pl.when(s == 0)
        def _():
            for i in range(slots):
                far_copy(0, i, True).wait()

        grads_down(s)
        run((rs0, s, DOWN))

        @pl.when(s == 1)
        def _():
            for i in range(slots):
                far_copy(0, i, True).start()

        grads_up(s)
        run((rs0, s, UP))

        @pl.when(s == 1)
        def _():
            for i in range(slots):
                far_copy(1, i, True).start()

        @pl.when(s == 0)
        def _():
            run((rs4, 1, DOWN), (rs4, 1, UP))

        @pl.loop(0, slots // few)
        def attention(i):
            @pl.when(s == 0)
            def _():
                events(i, {2: both(rs3, 1, ATT)})

            events(i, {2: [(rs1, s, DOWN), (rs1, s, UP)]})
            attn_backward(s, i)

        run((rs2, s, DOWN))

        @pl.when(s == 0)
        def _():
            run(*both(rs4, 1, ATT))

        grads_attn(s)
        run((rs0, s, ATT), (rs2, s, UP))

        @pl.loop(0, slots // many)
        def to_input(i):
            rd = step_rows(i, many)
            x = xs[s, rd, :].astype(F32)
            d_in = input_backward(s, after_ref[rd, :], rd, x, statistic(s, rd, 2), statistic(s, rd, 0))
            for m in range(many):
                @pl.when(s == 0)
                def _():
                    shipped(1, 1, i * many + m)

                io_two[i * many + m] = d_in[rows * m : rows * m + length].astype(LOW)
                ship(1, s, i * many + m)

        table_out(s)
        run((rs0, s, TAB))

    def sent_and_landed(kind):
        @pl.loop(0, slots)
        def _(i):
            shipped(kind, 1 - kind, i)
            for b in range(2):
                landed(kind, b, i)

    sent_and_landed(0)
    weave({
        1: lambda: run(*both(rs1, 0, ATT), (rs3, 0, DOWN), (rs3, 0, UP)),
        slots - raw.shape[0] + 1: lambda: sent_and_landed(1),
        slots + 2: lambda: run(*both(rs3_first, 0, ATT), (rs4, 0, DOWN), (rs4, 0, UP)),
    })
    run(*both(rs3_rest, 0, ATT))
    run(*both(rs4, 0, ATT))
    for b in range(2):
        for g in groups:
            rs_sent(b, g)


def output_kernel(
    woven, far_a, far_u, far_d, far_t, o_acts, o_ings, o_g1, o_s1, o_qkv, o_qv, o_out, o_bo, o_g2, o_s2, o_up, o_bu, o_down, o_bd,
    passing, f_a, f_u, f_d, f_t, sems, grad_sems
):
    coming = [
        pltpu.make_async_copy(source, target, grad_sems.at[i])
        for i, (source, target) in enumerate(((far_a, f_a), (far_u, f_u), (far_d, f_d), (far_t, f_t)))
    ]
    for copy in coming:
        copy.start()
    arriving, leaving = [], []
    for which, target in enumerate((o_acts, o_ings)):
        for i in range(target.shape[0]):
            arriving.append(pltpu.make_async_copy(woven.at[which, i], passing.at[which, i], sems.at[0, which, i]))
            leaving.append(pltpu.make_async_copy(passing.at[which, i], target.at[i], sems.at[1, which, i]))
    for copy in arriving:
        copy.start()
    for one, two in zip(arriving, leaving):
        one.wait()
        two.start()
    for copy in coming:
        copy.wait()
    unit, width = o_out.shape[1:]
    for half in range(2):
        o_down[0, 2 * unit * half : 2 * unit * (half + 1), :] = f_d[half]
        for sub in range(2):
            part = 2 * half + sub
            cols = slice(part * width, (part + 1) * width)
            o_up[0, :, cols] = f_u[half, unit * sub : unit * (sub + 1), :]
            piece = f_a[half, unit * sub : unit * (sub + 1), :]
            if part == 3:
                o_out[0] = piece
            else:
                o_qkv[0, :, cols] = piece
    begin = 0
    for out in (o_g1, o_s1, o_bo, o_g2, o_s2, o_bd, o_qv):
        part = out.shape[1]
        out[...] = f_t[0, :, begin : begin + part]
        begin += part
    o_bu[...] = f_t[1, :, 0 : o_bu.shape[1]]
    for copy in leaving:
        copy.wait()


def local(
    images, cotangent, counts,
    ln1_gain, ln1_bias, w_qkv, b_qv, w_out, b_out, ln2_gain, ln2_bias, w_up, b_up, w_down, b_down,
):
    micro_count, slots, length, width = images.shape
    ff = w_up.shape[2]
    rows = -(-length // 16) * 16
    n = lax.axis_size("fsdp")
    unit = width // n
    first, rest = radices(n)
    total = slots * rows
    head_dim = width // HEADS

    def vm(*shape, kind=LOW):
        return pltpu.VMEM(shape, kind)

    tall = [(2 * unit, LOW)] * 3 + [(1, F32)]
    dma = lambda *shape: pltpu.SemaphoreType.DMA(shape)
    outs = [((2, slots, length, 2, width), LOW)]
    outs += [((2, r, width), F32) for r, _ in tall] + [((total, ff), LOW)] * 2 + [((2, 2, slots, length, width), LOW)]
    scratch = [
        vm(2, total, width), vm(3, length, 2, width), vm(slots, length, width), vm(slots, length, width),
        *[vm(2, r, width, kind=kind) for r, kind in tall],
        vm(2, width, 3 * width), vm(2, width, width), vm(2, width, ff), vm(2, ff, width),
        vm(2, TABLE, width, kind=F32), vm(2, TABLE, width, kind=F32),
        vm(unit, width), vm(2 * unit, 2 * width), vm(4 * unit, 4 * width),
        vm(total, width, kind=F32), vm(2, total, width), vm(2, total, 3 * width), vm(2, slots, HEADS, rows, rows),
        vm(2, total, width),
        vm(2, total, width), vm(2, total, width), vm(total, 6, kind=F32),
        vm(total, ff), vm(total, ff), vm(total, width), vm(total, width), vm(width, total),
    ]
    scratch += [vm(2, 2, n, r, width, kind=kind) for r, kind in tall]
    scratch += [vm(n, r, width, kind=kind) for r, kind in tall]
    plane = rest * rest - 1
    for g, (r, kind) in enumerate(tall):
        direct = g in (ATT, TAB)
        scratch.append(vm(*((plane, first) if direct else (rest - 1, rest * first)), r, width, kind=kind))
    scratch += [vm(2, rest - 1, first, *tall[g][:1], width) for g in (UP, DOWN)]
    scratch += [vm(2, first, r, width, kind=kind) for r, kind in tall]
    scratch += [dma(2, slots), dma(2, 2 * slots), dma(2 * slots), dma(4, slots), dma(4, slots), dma(4, slots)]
    scratch += [dma(4, 2, first), dma(8, first)] + [dma(8, rest - 1)] * 4 + [dma(8, rest)] * 2
    scratch += [dma(8)] * 2 + [dma(8, plane, 2)] * 2 + [dma(8, rest - 1)] * 2 + [dma(8, first), dma(4, 2, first)]
    scratch += [pltpu.SemaphoreType.REGULAR((2, 4))]
    dims = (slots, length, rows, width, ff, head_dim, n)
    vmem = pl.BlockSpec(memory_space=pltpu.VMEM)
    hbm = pl.BlockSpec(memory_space=pltpu.HBM)
    woven, f_a, f_u, f_d, f_t, *_ = pl.pallas_call(
        functools.partial(whole_kernel, dims),
        out_shape=[jax.ShapeDtypeStruct(*o) for o in outs],
        in_specs=[hbm, hbm, pl.BlockSpec(memory_space=pltpu.SMEM)] + [vmem] * 12,
        out_specs=[hbm] + [vmem] * 4 + [hbm] * 3,
        scratch_shapes=scratch,
        compiler_params=pltpu.CompilerParams(
            vmem_limit_bytes=(64 << 20) - (96 << 10), collective_id=0, has_side_effects=True
        ),
    )(
        images.transpose(1, 2, 0, 3), cotangent.transpose(1, 2, 0, 3), counts.T, ln1_gain, ln1_bias, b_out, ln2_gain, ln2_bias, b_down, b_qv, b_up,
        w_qkv, w_out, w_up, w_down,
    )

    params = (
        ln1_gain, ln1_bias, w_qkv, b_qv, w_out, b_out, ln2_gain, ln2_bias, w_up, b_up, w_down, b_down
    )
    acts, ings, *grads = pl.pallas_call(
        output_kernel,
        out_shape=[jax.ShapeDtypeStruct(woven.shape[1:], LOW)] * 2
        + [jax.ShapeDtypeStruct(p.shape, F32) for p in params],
        in_specs=[hbm] * 5,
        out_specs=[hbm] * 2 + [vmem] * len(params),
        scratch_shapes=[
            vm(2, slots, length, 2, width), *[vm(2, r, width, kind=F32) for r, _ in tall], dma(2, 2, slots), dma(4)
        ],
        compiler_params=pltpu.CompilerParams(vmem_limit_bytes=(64 << 20) - (96 << 10)),
    )(woven, f_a, f_u, f_d, f_t)

    def as_given(value):
        return value.transpose(2, 0, 1, 3)[None]

    return (as_given(acts), as_given(ings), *grads)


def solution(mesh):
    split = P("section", "fsdp")
    cube = P("section", "fsdp", None)
    image = P(None, "fsdp", None, None)
    result = P("section", None, "fsdp", None, None)
    params = (split, split, cube, split, cube, split, split, split, cube, split, cube, split)
    return jax.shard_map(
        local,
        mesh=mesh,
        in_specs=(image, image, P(None, "fsdp")) + params,
        out_specs=(result, result) + params,
        check_vma=False,
    )
```

```python
import functools
import math

import jax
import jax.numpy as jnp
from jax import lax
from jax.experimental import pallas as pl
from jax.experimental.pallas import tpu as pltpu
from jax.sharding import PartitionSpec as P

HEADS = 6
EPS = 1e-06
F32 = jnp.float32
LOW = jnp.bfloat16

G1, S1, BO, G2, S2, BD, BQ, BV, BU = 0, 1, 2, 3, 4, 5, 6, 7, 8
TABLE = 16
TOGETHER, TOGETHER_ROWS = 2, 3
ATT, UP, DOWN, TAB = 0, 1, 2, 3


def radices(n):
    rest = max(r for r in range(1, n + 1) if r * r * r <= n and n % (r * r) == 0)
    return n // (rest * rest), rest


def mm(left, right):
    return jnp.dot(left, right, preferred_element_type=F32)


def mm_right(left, right):
    return lax.dot_general(left, right, (((1,), (1,)), ((), ())), preferred_element_type=F32)


def mm_left(left, right):
    return lax.dot_general(left, right, (((0,), (0,)), ((), ())), preferred_element_type=F32)


def normal_parts(pre):
    phi = 0.5 + 0.5 * lax.erf(pre * 0.7071067811865476)
    density = jnp.exp2(pre * pre * (-0.5 * 1.4426950408889634)) * 0.3989422804014327
    return phi, phi + pre * density


def normalize(value):
    mean = jnp.mean(value, axis=-1, keepdims=True)
    center = value - mean
    rstd = lax.rsqrt(jnp.mean(center * center, axis=-1, keepdims=True) + EPS)
    return center * rstd, rstd, mean


def normalize_back(d_hat, hat, rstd):
    mean_one = jnp.mean(d_hat, axis=-1, keepdims=True)
    mean_two = jnp.mean(d_hat * hat, axis=-1, keepdims=True)
    return rstd * (d_hat - mean_one - hat * mean_two)


def colsum(value):
    return jnp.sum(value, axis=0, keepdims=True)


def whole_kernel(dims, *refs):
    slots, length, rows, width, ff, head_dim, n = dims
    (
        images, cotangent, counts, v_g1, v_s1, v_bo, v_g2, v_s2, v_bd, v_qv, v_up, a_qkv, a_out, a_up, a_down,
        woven, f_a, f_u, f_d, f_t, hid_far, slope_far, out_far,
        xs, raw, io_one, io_two, pack_a, pack_u, pack_d, pack_t,
        wqkv, wout, wup, wdown, table, gtable, rep_one, rep_two, rep_four,
        after_ref, nrm1, qkv, prob, overs, ctx, hat2, rstds, hid, slope, dal, low_g, left_t,
        s_a, s_u, s_d, s_t, r0_a, r0_u, r0_d, r0_t, r1_a, r1_u, r1_d, r1_t, r2_u, r2_d,
        r3_a, r3_u, r3_d, r3_t,
        in_s, weave_in, weave_out, ship_s, ship_r, far_s, ag1_s, ag1_r, ag2_s, ag2_r, ag3_s, ag3_r, ag4_s, ag4_r, agp_s, agp_r,
        rs0_s, rs0_r, rs1_s, rs1_r, rs2_s, rs2_r, rs3_s, rs3_r, credit,
    ) = refs
    groups = (ATT, UP, DOWN, TAB)
    pack = (pack_a, pack_u, pack_d, pack_t)
    stage = (s_a, s_u, s_d, s_t)
    r0, r1, r2 = (r0_a, r0_u, r0_d, r0_t), (r1_a, r1_u, r1_d, r1_t), (None, r2_u, r2_d, None)
    r3, final = (r3_a, r3_u, r3_d, r3_t), (f_a, f_u, f_d, f_t)

    first, rest = radices(n)
    unit = width // n
    core = lax.axis_index("section")
    me = lax.axis_index("fsdp")
    dig_a, dig_b, dig_c = me // (rest * rest), (me // rest) % rest, me % rest
    dig_three, dig_two = dig_c + core * (dig_b - dig_c), dig_b + core * (dig_c - dig_b)
    step_three, step_two = 1 + core * (rest - 1), rest - core * (rest - 1)
    pos = (dig_three * rest + dig_two) * first + dig_a
    pos_of = ((dig_c * rest + dig_b) * first + dig_a, (dig_b * rest + dig_c) * first + dig_a)
    sibling = {"section": 1 - core}

    def place(half, j):
        a, b, c = j // (rest * rest), (j // rest) % rest, j % rest
        return ((c * rest + b) if half == 0 else (b * rest + c)) * first + a

    def peer_first(t):
        return {"fsdp": me + ((dig_a + t) % first - dig_a) * (rest * rest)}

    def peer_two(t):
        return {"fsdp": me + ((dig_two + t) % rest - dig_two) * step_two}

    def peer_three(t):
        return {"fsdp": me + ((dig_three + t) % rest - dig_three) * step_three}

    def peer_plane(three, two):
        here = ((dig_three + three) % rest - dig_three) * step_three
        return {"fsdp": me + here + ((dig_two + two) % rest - dig_two) * step_two}

    plane = [(three, two) for three in range(rest) for two in range(rest) if three or two]

    def remote(src, dst, s_sem, r_sem, device):
        return pltpu.make_async_remote_copy(
            src_ref=src, dst_ref=dst, send_sem=s_sem, recv_sem=r_sem, device_id=device,
            device_id_type=pl.DeviceIdType.MESH,
        )

    def slab_two(three, two):
        return pl.ds((three * rest + two) * first, first)

    def slab_three(three):
        return pl.ds(three * rest * first, rest * first)

    def fill_repeats():
        for ref in (rep_one, rep_two, rep_four):
            part = ref.shape[0]
            lanes = lax.broadcasted_iota(jnp.int32, ref.shape, 1).astype(F32)
            line = lax.broadcasted_iota(jnp.int32, ref.shape, 0).astype(F32)
            rest_of = lanes - part * jnp.floor((lanes + 0.5) * (1.0 / part))
            ref[...] = jnp.where(jnp.abs(rest_of - line) < 0.5, 1.0, 0.0).astype(LOW)

    def own_lanes(part):
        shape = (n, part * n)
        lanes = lax.broadcasted_iota(jnp.int32, shape, 1)
        begin = lax.broadcasted_iota(jnp.int32, shape, 0) * part
        return (lanes >= begin) & (lanes < begin + part)

    shares = (
        ((G1, unit, rep_one), (S1, unit, rep_one), (BO, unit, rep_one), (G2, unit, rep_one), (S2, unit, rep_one),
         (BD, unit, rep_one), (BQ, 2 * unit, rep_two)),
        ((BU, 4 * unit, rep_four),),
    )

    def table_in(b):
        for half in range(2):
            lines = jnp.concatenate([s_t[b, half, place(half, j)] for j in range(n)], axis=0)
            begin = 0
            for row, part, ref in shares[half]:
                spread = mm(lines[:, begin : begin + part].astype(LOW), ref[...])
                line = colsum(jnp.where(own_lanes(part), spread, 0.0))
                for i in range(part * n // width):
                    table[b, row + i : row + i + 1, :] = line[:, width * i : width * (i + 1)]
                begin += part

    def table_out(b):
        for half in range(2):
            parts, begin = [], 0
            for row, part, ref in shares[half]:
                count = part * n // width
                line = jnp.concatenate([gtable[b, row + i : row + i + 1, :] for i in range(count)], axis=1)
                parts.append(mm_right(jnp.where(own_lanes(part), line, 0.0).astype(LOW), ref[...]))
                begin += part
            parts.append(jnp.zeros((n, width - begin), F32))
            lines = jnp.concatenate(parts, axis=1)
            for j in range(n):
                s_t[b, half, place(half, j)] = lines[j : j + 1]

    def pack_own():
        for half in range(2):
            vectors = ((v_g1, v_s1, v_bo, v_g2, v_s2, v_bd, v_qv), (v_up,))[half]
            lines = [vector[...].astype(F32) for vector in vectors]
            lines.append(jnp.zeros((1, width - sum(line.shape[1] for line in lines)), F32))
            pack_t[half] = jnp.concatenate(lines, axis=1)
            for ref in (pack_a, pack_u):
                both = []
                for part in (2 * half, 2 * half + 1):
                    if ref is pack_u:
                        both.append(a_up[0, :, part * width : (part + 1) * width])
                    elif part == 3:
                        both.append(a_out[0])
                    else:
                        both.append(a_qkv[0, :, part * width : (part + 1) * width])
                ref[half] = jnp.concatenate([value.astype(F32) for value in both], axis=0).astype(LOW)
            pack_d[half] = a_down[0, 2 * unit * half : 2 * unit * (half + 1), :]

    def at(b, g):
        return len(groups) * b + g

    def ag1_copy(b, g, half, t):
        device = {"section": half, **peer_first(t)} if t else sibling
        return remote(
            pack[g].at[half], stage[g].at[b, half, pos_of[half]],
            ag1_s.at[g, half, t], ag1_r.at[at(b, g), t], device,
        )

    def ag1_landing(b, g, t):
        ref = stage[g].at[b, core, (dig_three * rest + dig_two) * first + (dig_a + first - t) % first]
        return remote(ref, ref, ag1_s.at[g, 0, t], ag1_r.at[at(b, g), t], sibling)

    def ag2_copy(b, g, t):
        ref = stage[g].at[b, core, slab_two(dig_three, dig_two)]
        return remote(ref, ref, ag2_s.at[at(b, g), t - 1], ag2_r.at[at(b, g), t - 1], peer_two(t))

    def ag3_copy(b, g, t):
        ref = stage[g].at[b, core, slab_three(dig_three)]
        return remote(ref, ref, ag3_s.at[at(b, g), t - 1], ag3_r.at[at(b, g), t - 1], peer_three(t))

    def ag4_copy(b, g, t):
        ref = stage[g].at[b, core, slab_three((dig_three + rest - t) % rest)]
        return remote(ref, ref, ag4_s.at[at(b, g), t], ag4_r.at[at(b, g), t], sibling)

    def ag4_landing(b, g, t):
        ref = stage[g].at[b, 1 - core, slab_three((dig_two + rest - t) % rest)]
        return remote(ref, ref, ag4_s.at[at(b, g), t], ag4_r.at[at(b, g), t], sibling)

    def ag1(b, g):
        @pl.when(core == b)
        def _():
            for t in range(1, first):
                for half in range(2):
                    ag1_copy(b, g, half, t).start()
            ag1_copy(b, g, 1 - b, 0).start()
            stage[g][b, b, pos] = pack[g][b]

    def ag2(b, g):
        for t in range(1, first):
            ag1_landing(b, g, t).wait_recv()

        @pl.when(core != b)
        def _():
            ag1_landing(b, g, 0).wait_recv()

        for t in range(1, rest):
            ag2_copy(b, g, t).start()

    def ag3(b, g):
        for t in range(1, rest):
            ag2_copy(b, g, t).wait_recv()
        for t in range(1, rest):
            ag3_copy(b, g, t).start()
        ag4_copy(b, g, 0).start()

    def ag4(b, g):
        for t in range(1, rest):
            ag3_copy(b, g, t).wait_recv()
            ag4_copy(b, g, t).start()

    def agp_copy(g, t, k):
        ref = stage[g].at[0, core, (dig_three * rest + dig_two) * first + (dig_a + first - t) % first]
        at_group = 0 if g == ATT else 1
        return remote(ref, ref, agp_s.at[at_group, t, k], agp_r.at[at_group, t, k], peer_plane(*plane[k]))

    def agp(b, g, t):
        if t == 0:
            @pl.when(core != b)
            def _():
                ag1_landing(b, g, 0).wait_recv()
        else:
            ag1_landing(b, g, t).wait_recv()
        for k in range(len(plane)):
            agp_copy(g, t, k).start()

    def agp_own(b, g):
        agp(b, g, 0)

    def agp_others(b, g):
        for t in range(1, first):
            agp(b, g, t)

    def agp_landed(b, g):
        for t in range(first):
            for k in range(len(plane)):
                agp_copy(g, t, k).wait_recv()
        for t in range(rest):
            ag4_copy(b, g, t).start()

    def ag5(b, g):
        for t in range(rest):
            ag4_landing(b, g, t).wait_recv()
        lay_out(b, g)

    def ag_sent(b, g):
        @pl.when(core == b)
        def _():
            for t in range(1, first):
                for half in range(2):
                    ag1_copy(b, g, half, t).wait_send()
            ag1_copy(b, g, 1 - b, 0).wait_send()

        if b == 0 and g in (ATT, TAB):
            for t in range(first):
                for k in range(len(plane)):
                    agp_copy(g, t, k).wait_send()
        else:
            for t in range(1, rest):
                ag2_copy(b, g, t).wait_send()
                ag3_copy(b, g, t).wait_send()
        for t in range(rest):
            ag4_copy(b, g, t).wait_send()

    def lay_out(b, g):
        if g == TAB:
            table_in(b)
            return
        if g == DOWN:
            for j in range(n):
                for half in range(2):
                    begin = 4 * unit * j + 2 * unit * half
                    wdown[b, begin : begin + 2 * unit, :] = s_d[b, half, place(half, j)]
            return
        together = 16 // math.gcd(unit, 16)
        for half in range(2):
            for j in range(0, n, together):
                pieces = [stage[g][b, half, place(half, j + i)].astype(F32) for i in range(together)]
                for sub in range(2):
                    low = sub * unit
                    block = jnp.concatenate([piece[low : low + unit] for piece in pieces], axis=0).astype(LOW)
                    part = 2 * half + sub
                    down = slice(unit * j, unit * (j + together))
                    if g == UP:
                        wup[b, down, part * width : (part + 1) * width] = block
                    elif part == 3:
                        wout[b, down, :] = block
                    else:
                        wqkv[b, down, part * width : (part + 1) * width] = block

    def rs0_copy(b, g):
        return remote(stage[g].at[b, 1 - core], r0[g], rs0_s.at[at(b, g)], rs0_r.at[at(b, g)], sibling)

    def rs1_copy(b, g, t):
        return remote(
            stage[g].at[b, core, slab_three((dig_three + t) % rest)], r1[g].at[t - 1],
            rs1_s.at[at(b, g), t - 1, 0], rs1_r.at[at(b, g), t - 1, 0], peer_three(t),
        )

    def rs2_copy(b, g, t):
        return remote(
            stage[g].at[b, core, slab_two(dig_three, (dig_two + t) % rest)], r2[g].at[b, t - 1],
            rs2_s.at[at(b, g), t - 1], rs2_r.at[at(b, g), t - 1], peer_two(t),
        )

    def rs3_copy(b, g, t):
        there = (dig_three * rest + dig_two) * first + (dig_a + t) % first
        device = {"section": b, **peer_first(t)} if t else sibling
        return remote(
            stage[g].at[b, core, there], r3[g].at[core, t], rs3_s.at[at(b, g), t], rs3_r.at[g, core, t], device
        )

    chunk_count = 2 if first % 2 == 0 else 1
    chunk_size = first // chunk_count

    def plane_copy(b, g, t, part):
        three, two = plane[t]
        begin = (((dig_three + three) % rest) * rest + (dig_two + two) % rest) * first + chunk_size * part
        return remote(
            stage[g].at[b, core, pl.ds(begin, chunk_size)], r1[g].at[t, pl.ds(chunk_size * part, chunk_size)],
            rs1_s.at[at(b, g), t, part], rs1_r.at[at(b, g), t, part], peer_plane(three, two),
        )

    def rs0(b, g):
        @pl.when(b == 0)
        def _():
            pl.semaphore_wait(credit.at[0, g], 1)

        rs0_copy(b, g).start()

    def rs1(b, g):
        rs0_copy(b, g).wait_recv()

        @pl.loop(0, n)
        def _(p):
            stage[g][b, core, p] = stage[g][b, core, p] + r0[g][p]

        @pl.when(b == 1)
        def _():
            pl.semaphore_signal(credit.at[0, g], inc=1, device_id=sibling, device_id_type=pl.DeviceIdType.MESH)

        direct = g in (ATT, TAB)
        if rest > 1:
            @pl.when(b == 0)
            def _():
                pl.semaphore_wait(credit.at[1, g], len(plane) if direct else rest - 1)

        if direct:
            for part in range(chunk_count):
                for t in range(len(plane)):
                    plane_copy(b, g, t, part).start()
            return
        for t in range(1, rest):
            rs1_copy(b, g, t).start()

    def rs2(b, g):
        for t in range(1, rest):
            rs1_copy(b, g, t).wait_recv()

        @pl.loop(0, rest * first)
        def _(p):
            here = dig_three * rest * first + p
            total = stage[g][b, core, here].astype(F32)
            for t in range(1, rest):
                total = total + r1[g][t - 1, p].astype(F32)
            stage[g][b, core, here] = total.astype(stage[g].dtype)

        for t in range(1, rest):
            @pl.when(b == 1)
            def _():
                pl.semaphore_signal(
                    credit.at[1, g], inc=1, device_id=peer_three(t), device_id_type=pl.DeviceIdType.MESH
                )

            rs2_copy(b, g, t).start()

    def rs3_send(b, g, part):
        def here(digit):
            return (digit >= chunk_size * part) & (digit < chunk_size * (part + 1))

        for t in range(1, first):
            @pl.when(here((dig_a + t) % first))
            def _():
                rs3_copy(b, g, t).start()

        @pl.when(here(dig_a) & (core != b))
        def _():
            rs3_copy(b, g, 0).start()

    def rs3_part(b, g, part):
        for t in range(len(plane)):
            plane_copy(b, g, t, part).wait_recv()

        @pl.loop(chunk_size * part, chunk_size * (part + 1))
        def _(p):
            here = (dig_three * rest + dig_two) * first + p
            total = stage[g][b, core, here].astype(F32)
            for t in range(len(plane)):
                total = total + r1[g][t, p].astype(F32)
            stage[g][b, core, here] = total.astype(stage[g].dtype)

        rs3_send(b, g, part)

    def rs3_first(b, g):
        rs3_part(b, g, 0)

    def rs3_rest(b, g):
        for part in range(1, chunk_count):
            rs3_part(b, g, part)

    def rs3(b, g):
        if g in (ATT, TAB):
            for part in range(chunk_count):
                rs3_part(b, g, part)

            @pl.when(b == 1)
            def _():
                for three, two in plane:
                    pl.semaphore_signal(
                        credit.at[1, g], inc=1, device_id=peer_plane(three, two),
                        device_id_type=pl.DeviceIdType.MESH,
                    )

            return
        for t in range(1, rest):
            rs2_copy(b, g, t).wait_recv()

        @pl.loop(0, first)
        def _(p):
            here = (dig_three * rest + dig_two) * first + p
            total = stage[g][b, core, here].astype(F32)
            for t in range(1, rest):
                total = total + r2[g][b, t - 1, p].astype(F32)
            stage[g][b, core, here] = total.astype(stage[g].dtype)

        for part in range(chunk_count):
            rs3_send(b, g, part)

    def rs4(b, g):
        @pl.when(core == b)
        def _():
            for own in (True, False):
                half = core if own else 1 - core
                begin = int(own)
                for t in range(begin, first):
                    ref = r3[g].at[half, t]
                    remote(ref, ref, rs3_s.at[at(b, g), t], rs3_r.at[g, half, t], sibling).wait_recv()
                total = stage[g][b, core, pos].astype(F32) if own else None
                for t in range(begin, first):
                    value = r3[g][half, t].astype(F32)
                    total = value if total is None else total + value
                final[g][half] = total

    def rs_sent(b, g):
        rs0_copy(b, g).wait_send()
        if g in (ATT, TAB):
            for part in range(chunk_count):
                for t in range(len(plane)):
                    plane_copy(b, g, t, part).wait_send()
        else:
            for t in range(1, rest):
                rs1_copy(b, g, t).wait_send()
                rs2_copy(b, g, t).wait_send()
        for t in range(1, first):
            rs3_copy(b, g, t).wait_send()

        @pl.when(core != b)
        def _():
            rs3_copy(b, g, 0).wait_send()

    def rows_of(i, images_too=1):
        return pl.ds(pl.multiple_of(i * rows, 16), images_too * rows)

    few = TOGETHER if slots % TOGETHER == 0 else 1
    many = TOGETHER_ROWS if slots % TOGETHER_ROWS == 0 else 1

    def step_rows(i, count):
        return rows_of(i * count, count)

    def ship_parts(kind, b, i):
        src, out = (io_one, io_two)[kind].at[i], out_far.at[kind, core, i]
        q = 2 * kind + b
        near = pltpu.make_async_copy(src, out, ship_s.at[q, i])
        far = remote(src, out, ship_s.at[q, i], ship_r.at[q, i], sibling)
        return near, far

    def ship(kind, b, i):
        near, far = ship_parts(kind, b, i)

        @pl.when(core == b)
        def _():
            near.start()

        @pl.when(core != b)
        def _():
            far.start()

    def shipped(kind, b, i):
        near, far = ship_parts(kind, b, i)

        @pl.when(core == b)
        def _():
            near.wait()

        @pl.when(core != b)
        def _():
            far.wait_send()

    def landed(kind, b, i):
        q = 2 * kind + b
        ref = out_far.at[kind, 1 - core, i]

        @pl.when(core == b)
        def _():
            remote(ref, ref, ship_s.at[q, i], ship_r.at[q, i], sibling).wait_recv()

    def live(i):
        return jnp.where(i < counts[0, core], 1.0, 0.0).astype(F32)

    def only_live(i, value, count):
        parts = [value[rows * m : rows * (m + 1)] * live(i * count + m) for m in range(count)]
        return jnp.concatenate(parts, axis=0)

    def coming(which, i):
        slot = (which * slots + i) % raw.shape[0]
        return pltpu.make_async_copy((images, cotangent)[which].at[i], raw.at[slot], in_s.at[which, i])

    def take_in(which, i):
        coming(which, i).wait()
        both = raw[(which * slots + i) % raw.shape[0]].astype(F32)
        (io_one, io_two)[which][i] = jnp.where(core == 0, both[:, 0, :], both[:, 1, :]).astype(LOW)

    def weave(todo):
        ring = raw.shape[0]
        count = 2 * slots

        def fetch(t, m):
            source = out_far.at[t // slots, m, t % slots]
            return pltpu.make_async_copy(source, io_one.at[2 * (t % ring) + m], weave_in.at[m, t])

        def leave(t):
            return pltpu.make_async_copy(raw.at[t % ring], woven.at[t // slots, t % slots], weave_out.at[t])

        for t in range(ring - 1):
            for m in range(2):
                fetch(t, m).start()

        @pl.loop(0, count)
        def _(t):
            for when, act in todo.items():
                @pl.when(t == when)
                def _():
                    act()

            @pl.when(t + ring - 1 < count)
            def _():
                for m in range(2):
                    fetch(t + ring - 1, m).start()

            @pl.when(t >= ring)
            def _():
                leave(t - ring).wait()

            for m in range(2):
                fetch(t, m).wait()
                raw[t % ring, :, m, :] = io_one[2 * (t % ring) + m]
            leave(t).start()

        for t in range(count - ring, count):
            leave(t).wait()

    def far_copy(which, i, back):
        near, far = ((hid, hid_far), (slope, slope_far))[which]
        near, far = near.at[rows_of(i)], far.at[rows_of(i)]
        src, dst = (far, near) if back else (near, far)
        return pltpu.make_async_copy(src, dst, far_s.at[2 * int(back) + which, i])

    pairs = width // 128
    scale = head_dim ** -0.5
    lane = lax.broadcasted_iota(jnp.int32, (1, 128), 1)
    half_low = [(lane < head_dim).astype(LOW), (lane >= head_dim).astype(LOW)]
    half_f = [(lane < head_dim).astype(F32), (lane >= head_dim).astype(F32)]
    token = lax.broadcasted_iota(jnp.int32, (rows, 128), 0) < length
    half_valid = [jnp.where(token, half_f[j], 0.0).astype(LOW) for j in range(2)]
    valid_lanes = jnp.where(lax.broadcasted_iota(jnp.int32, (1, rows), 1) < length, 1.0, 0.0).astype(F32)
    spare = -rows % 128
    chunk = 2 * width
    chunks = ff // chunk

    def vec(s, r):
        return table[s, r : r + 1, :]

    def up_bias(s, c):
        begin = c * chunk
        row, col = begin // width, begin % width
        if col + chunk <= width:
            return table[s, BU + row : BU + row + 1, col : col + chunk]
        a = table[s, BU + row : BU + row + 1, col:width]
        b = table[s, BU + row + 1 : BU + row + 2, 0 : chunk - (width - col)]
        return jnp.concatenate([a, b], axis=1)

    def add_vec(s, r, value):
        gtable[s, r : r + 1, :] += value

    def add_up_bias(s, c, value):
        begin = c * chunk
        row, col = begin // width, begin % width
        if col + chunk <= width:
            gtable[s, BU + row : BU + row + 1, col : col + chunk] += value
        else:
            cut = width - col
            gtable[s, BU + row : BU + row + 1, col:width] += value[:, :cut]
            gtable[s, BU + row + 1 : BU + row + 2, 0 : chunk - cut] += value[:, cut:]

    def attn_forward(s, x, hat, i):
        rd = step_rows(i, few)
        nrm_ref, qkv_ref, prob_ref, ctx_ref = nrm1.at[s], qkv.at[s], prob.at[s], ctx.at[s]
        nrm = (hat * vec(s, G1) + vec(s, S1)).astype(LOW)
        nrm_ref[rd, :] = nrm
        mixed = mm(nrm, wqkv[s])
        q = (mixed[:, 0:width] + vec(s, BQ)).astype(LOW)
        k = mixed[:, width : 2 * width].astype(LOW)
        v = (mixed[:, 2 * width :] + vec(s, BV)).astype(LOW)
        qkv_ref[rd, 0:width] = q
        qkv_ref[rd, width : 2 * width] = k
        qkv_ref[rd, 2 * width :] = v
        images_out = []
        for m in range(few):
            mine = slice(rows * m, rows * (m + 1))
            parts = []
            for p in range(pairs):
                cols = slice(128 * p, 128 * p + 128)
                weights, sides = [], []
                for j in range(2):
                    keys = k[mine, cols] * half_low[j]
                    keys = jnp.concatenate([keys, keys[rows - spare :]], axis=0)
                    scores = mm_right(q[mine, cols], keys)
                    top = jnp.max(scores, axis=-1, keepdims=True)
                    e = jnp.exp2((scores - top) * (scale * 1.4426950408889634)).astype(LOW)
                    prob_ref[i * few + m, 2 * p + j] = e[:, :rows]
                    weights.append(e)
                    sides.append(jnp.concatenate([v[mine, cols] * half_valid[j], half_valid[j]], axis=1))
                    sides.append(jnp.zeros((spare, 256), LOW))
                total = mm(jnp.concatenate(weights, axis=1), jnp.concatenate(sides, axis=0))
                over = 1.0 / total[:, 128:]
                overs[s, rows_of(i * few + m), cols] = over.astype(LOW)
                parts.append((total[:, :128] * over).astype(LOW))
            images_out.append(jnp.concatenate(parts, axis=1))
        context = jnp.concatenate(images_out, axis=0)
        ctx_ref[rd, :] = context
        return x + mm(context, wout[s]) + vec(s, BO)

    def ff_forward(s, after, rd):
        hat, rstd, _ = normalize(after)
        hat2[s, rd, :] = hat.astype(LOW)
        nrm = (hat * vec(s, G2) + vec(s, S2)).astype(LOW)
        total = after + vec(s, BD)
        for c in range(chunks):
            cols = slice(chunk * c, chunk * c + chunk)
            pre = mm(nrm, wup[s, :, cols]) + up_bias(s, c)
            phi, slo = normal_parts(pre)
            h = (pre * phi).astype(LOW)
            hid[rd, cols] = h
            slope[rd, cols] = slo.astype(LOW)
            total = total + mm(h, wdown[s, cols, :])
        return total, rstd

    def ff_backward(s, g, rd, rstd):
        g_low = g.astype(LOW)
        add_vec(s, BD, colsum(g_low.astype(F32)))
        d_nrm = None
        for c in range(chunks):
            cols = slice(chunk * c, chunk * c + chunk)
            d_hid = mm_right(g_low, wdown[s, cols, :])
            d_pre = (d_hid * slope[rd, cols].astype(F32)).astype(LOW)
            slope[rd, cols] = d_pre
            add_up_bias(s, c, colsum(d_pre.astype(F32)))
            part = mm_right(d_pre, wup[s, :, cols])
            d_nrm = part if d_nrm is None else d_nrm + part
        hat = hat2[s, rd, :].astype(F32)
        add_vec(s, G2, colsum(d_nrm * hat))
        add_vec(s, S2, colsum(d_nrm))
        d_after = g + normalize_back(d_nrm * vec(s, G2), hat, rstd)
        low = d_after.astype(LOW)
        dal[rd, :] = low
        add_vec(s, BO, colsum(low.astype(F32)))
        return d_after

    def attn_backward(s, i):
        qkv_ref, prob_ref, ctx_ref = qkv.at[s], prob.at[s], ctx.at[s]
        rd = step_rows(i, few)
        d_context = mm_right(dal[rd, :], wout[s])
        d_context = (d_context * overs[s, rd, :].astype(F32)).astype(LOW)
        for m in range(few):
            rd = rows_of(i * few + m)
            d_ctx = d_context[rows * m : rows * (m + 1)]
            dq, dk, dv = [], [], []
            for p in range(pairs):
                cols = slice(128 * p, 128 * p + 128)
                q = qkv_ref[rd, 128 * p : 128 * p + 128]
                k = qkv_ref[rd, width + 128 * p : width + 128 * p + 128]
                v = qkv_ref[rd, 2 * width + 128 * p : 2 * width + 128 * p + 128]
                dc = d_ctx[:, cols]
                both = dc.astype(F32) * ctx_ref[rd, cols].astype(F32)
                q_t, dc_t = q.T, dc.T
                to_q, to_k, to_v = None, [], []
                for j in range(2):
                    e = prob_ref[i * few + m, 2 * p + j]
                    delta = jnp.sum(both * half_f[j], axis=-1, keepdims=True)
                    d_prob = mm_right(dc, v * half_low[j])
                    ds = (e.astype(F32) * (d_prob - delta)).astype(LOW)
                    part = mm(ds, k * half_valid[j])
                    to_q = part if to_q is None else to_q + part
                    head = slice(head_dim * j, head_dim * (j + 1))
                    to_k.append(mm(q_t[head], ds))
                    to_v.append(mm(dc_t[head], e))
                dq.append((to_q * scale).astype(LOW))
                dk.append((jnp.concatenate(to_k, axis=0) * (valid_lanes * scale)).astype(LOW).T)
                dv.append((jnp.concatenate(to_v, axis=0) * valid_lanes).astype(LOW).T)
            d_mixed = jnp.concatenate(dq + dk + dv, axis=1)
            qkv_ref[rd, :] = d_mixed
            add_vec(s, BQ, colsum(d_mixed[:, 0:width].astype(F32)))
            add_vec(s, BV, colsum(d_mixed[:, 2 * width :].astype(F32)))

    def input_backward(s, d_after, rd, x, mean, rstd):
        d_nrm = mm_right(qkv[s, rd, :], wqkv[s])
        hat = (x - mean) * rstd
        add_vec(s, G1, colsum(d_nrm * hat))
        add_vec(s, S1, colsum(d_nrm))
        return d_after + normalize_back(d_nrm * vec(s, G1), hat, rstd)

    def grads_down(s):
        left_t[...] = low_g[...].T

        @pl.loop(0, 2)
        def _(c):
            cols = pl.ds(pl.multiple_of(c * 2 * width, 128), 2 * width)
            block = mm(left_t[...], hid[:, cols]).T
            for i in range(n // 2):
                for half in range(2):
                    begin = 4 * unit * i + 2 * unit * half
                    s_d[s, half, place(half, c * (n // 2) + i)] = block[begin : begin + 2 * unit].astype(LOW)

    def pair_out(ref, s, half, one, two):
        for j in range(n):
            down = slice(unit * j, unit * (j + 1))
            piece = jnp.concatenate([one[down], two[down]], axis=0).astype(LOW)
            ref[s, half, place(half, j)] = piece

    def grads_up(s):
        left_t[...] = (hat2[s].astype(F32) * vec(s, G2) + vec(s, S2)).astype(LOW).T
        for half in range(2):
            both = mm(left_t[...], slope[:, 2 * half * width : 2 * (half + 1) * width])
            pair_out(s_u, s, half, both[:, :width], both[:, width:])

    def grads_attn(s):
        mix_s = qkv.at[s]
        left_t[...] = ctx[s].T
        four = mm(left_t[...], dal[...])
        left_t[...] = nrm1[s].T
        three = mm(left_t[...], mix_s[:, 2 * width :])
        pair_out(s_a, s, 1, three, four)
        both = mm(left_t[...], mix_s[:, 0 : 2 * width])
        pair_out(s_a, s, 0, both[:, :width], both[:, width:])

    barrier = pltpu.get_barrier_semaphore()
    greeted = [sibling]
    greeted += [{"section": half, **peer_first(t)} for t in range(1, first) for half in range(2)]
    greeted += [peer_plane(three, two) for three, two in plane]
    for device in greeted:
        pl.semaphore_signal(barrier, inc=1, device_id=device, device_id_type=pl.DeviceIdType.MESH)
    pack_own()
    pl.semaphore_wait(barrier, len(greeted))

    def run(*todo):
        for f, b, g in todo:
            f(b, g)

    def events(i, table_of):
        for when, todo in table_of.items():
            @pl.when(i == when)
            def _():
                run(*todo)

    def both(f, b, g):
        return [(f, b, g), (f, b, TAB)]

    def take(i, m):
        return pl.ds(pl.multiple_of((i * many + m) * rows, 16), length)

    ahead = raw.shape[0]
    run(*both(ag1, 0, ATT))
    for i in range(ahead):
        coming(0, i).start()
    run(*both(agp_own, 0, ATT))
    fill_repeats()
    gtable[...] = jnp.zeros_like(gtable)
    low_g[...] = jnp.zeros_like(low_g)
    xs[0] = jnp.zeros_like(low_g)

    @pl.loop(0, slots)
    def images_in(i):
        take_in(0, i)

        @pl.when(i + ahead < slots)
        def _():
            coming(0, i + ahead).start()

        @pl.when(i + ahead >= slots)
        def _():
            coming(1, i + ahead - slots).start()

        @pl.when(i == 4)
        def _():
            run((ag1, 0, UP))

    run(*both(agp_others, 0, ATT), (ag1, 0, DOWN), *both(ag1, 1, ATT))

    def statistic(s, rd, which):
        return jnp.where(s == 0, rstds[rd, which : which + 1], rstds[rd, 3 + which : 4 + which])

    def first_norm(s, rd, x):
        hat, rstd, mean = normalize(x)
        after_ref[rd, :] = hat
        rstds[rd, 3 * s : 3 * s + 1] = rstd
        rstds[rd, 3 * s + 2 : 3 * s + 3] = mean

    @pl.loop(0, slots // many)
    def norm_one(i):
        for m in range(many):
            xs[0, take(i, m), :] = io_one[i * many + m]
        rd = step_rows(i, many)
        x = xs[0, rd, :].astype(F32)
        token_rows = lax.broadcasted_iota(jnp.int32, (rows, width), 0) < length
        parts = [x[rows * m : rows * (m + 1)] for m in range(many)]
        x = jnp.concatenate([jnp.where(token_rows, part, part[0:1]) for part in parts], axis=0)
        xs[0, rd, :] = x.astype(LOW)
        first_norm(0, rd, x)

    run((ag2, 0, UP), (ag1, 1, UP), (ag1, 1, DOWN), (ag2, 0, DOWN), (ag3, 0, UP))

    @pl.loop(0, slots)
    def cotangents_in(i):
        take_in(1, i)

        @pl.when(i + ahead < slots)
        def _():
            coming(1, i + ahead).start()

    run(*both(agp_landed, 0, ATT), (ag3, 0, DOWN), *both(ag2, 1, ATT), *both(ag5, 0, ATT))

    @pl.loop(0, 2)
    def forward(s):
        @pl.loop(0, slots // few)
        def attention(i):
            @pl.when(s == 0)
            def _():
                events(i, {1: [(ag4, 0, UP), (ag2, 1, UP)], 2: [(ag4, 0, DOWN)]})

            @pl.when(s == 1)
            def _():
                events(i, {1: [(ag4, 1, UP)], 2: [(ag4, 1, DOWN)]})

            rd = step_rows(i, few)
            after_ref[rd, :] = attn_forward(s, xs[s, rd, :].astype(F32), after_ref[rd, :], i)

        @pl.when(s == 0)
        def _():
            run(*both(ag3, 1, ATT), (ag5, 0, UP), (ag5, 0, DOWN))

        @pl.when(s == 1)
        def _():
            run((ag5, 1, UP), (ag5, 1, DOWN))

        @pl.loop(0, slots // many)
        def feed_forward(i):
            @pl.when(s == 0)
            def _():
                events(i, {0: [(ag2, 1, DOWN), (ag3, 1, UP)], 1: both(ag4, 1, ATT)})

            rd = step_rows(i, many)

            @pl.when(s == 1)
            def _():
                for m in range(many):
                    far_copy(0, i * many + m, False).wait()
                    far_copy(1, i * many + m, False).wait()
                    shipped(0, 0, i * many + m)

            out, rstd2 = ff_forward(s, after_ref[rd, :], rd)
            for block in range(2):
                @pl.when(s == block)
                def _():
                    rstds[rd, 3 * block + 1 : 3 * block + 2] = rstd2

            out = only_live(i, out, many)
            for m in range(many):
                io_one[i * many + m] = out[rows * m : rows * m + length].astype(LOW)
                ship(0, s, i * many + m)

            @pl.when(s == 0)
            def _():
                for m in range(many):
                    far_copy(0, i * many + m, False).start()
                    far_copy(1, i * many + m, False).start()
                low = out.astype(LOW)
                xs[1, rd, :] = low
                first_norm(1, rd, low.astype(F32))

        @pl.when(s == 0)
        def _():
            run((ag3, 1, DOWN), *both(ag5, 1, ATT))

    for b in range(2):
        for g in groups:
            ag_sent(b, g)

    @pl.loop(0, 2)
    def backward(turn):
        s = 1 - turn

        @pl.when(s == 0)
        def _():
            run((rs3, 1, DOWN))

        @pl.loop(0, slots // many)
        def feed_forward(i):
            @pl.when(s == 0)
            def _():
                events(i, {1: [*both(rs1, 1, ATT), (rs3, 1, UP)]})
                for m in range(many):
                    far_copy(1, i * many + m, True).wait()

            rd = step_rows(i, many)
            for m in range(many):
                g = live(i * many + m) * io_two[i * many + m].astype(F32)
                low_g[take(i, m), :] = g.astype(LOW)
            after_ref[rd, :] = ff_backward(s, low_g[rd, :].astype(F32), rd, statistic(s, rd, 1))

        @pl.when(s == 0)
        def _():
            for i in range(slots):
                far_copy(0, i, True).wait()

        grads_down(s)
        run((rs0, s, DOWN))

        @pl.when(s == 1)
        def _():
            for i in range(slots):
                far_copy(0, i, True).start()

        grads_up(s)
        run((rs0, s, UP))

        @pl.when(s == 1)
        def _():
            for i in range(slots):
                far_copy(1, i, True).start()

        @pl.when(s == 0)
        def _():
            run((rs4, 1, DOWN), (rs4, 1, UP))

        @pl.loop(0, slots // few)
        def attention(i):
            @pl.when(s == 0)
            def _():
                events(i, {1: both(rs3, 1, ATT)})

            events(i, {1: [(rs1, s, DOWN), (rs1, s, UP)]})
            attn_backward(s, i)

        run((rs2, s, DOWN))

        @pl.when(s == 0)
        def _():
            run(*both(rs4, 1, ATT))

        grads_attn(s)
        run((rs0, s, ATT), (rs2, s, UP))

        @pl.loop(0, slots // many)
        def to_input(i):
            rd = step_rows(i, many)
            x = xs[s, rd, :].astype(F32)
            d_in = input_backward(s, after_ref[rd, :], rd, x, statistic(s, rd, 2), statistic(s, rd, 0))
            for m in range(many):
                @pl.when(s == 0)
                def _():
                    shipped(1, 1, i * many + m)

                io_two[i * many + m] = d_in[rows * m : rows * m + length].astype(LOW)
                ship(1, s, i * many + m)

        table_out(s)
        run((rs0, s, TAB))

    def sent_and_landed(kind):
        @pl.loop(0, slots)
        def _(i):
            shipped(kind, 1 - kind, i)
            for b in range(2):
                landed(kind, b, i)

    sent_and_landed(0)
    weave({
        1: lambda: run(*both(rs1, 0, ATT), (rs3, 0, DOWN), (rs3, 0, UP)),
        slots - raw.shape[0] + 1: lambda: sent_and_landed(1),
        slots + 2: lambda: run(*both(rs3_first, 0, ATT), (rs4, 0, DOWN), (rs4, 0, UP)),
    })
    run(*both(rs3_rest, 0, ATT))
    run(*both(rs4, 0, ATT))
    for b in range(2):
        for g in groups:
            rs_sent(b, g)


def output_kernel(
    woven, far_a, far_u, far_d, far_t, o_acts, o_ings, o_g1, o_s1, o_qkv, o_qv, o_out, o_bo, o_g2, o_s2, o_up, o_bu, o_down, o_bd,
    passing, f_a, f_u, f_d, f_t, sems, grad_sems
):
    coming = [
        pltpu.make_async_copy(source, target, grad_sems.at[i])
        for i, (source, target) in enumerate(((far_a, f_a), (far_u, f_u), (far_d, f_d), (far_t, f_t)))
    ]
    for copy in coming:
        copy.start()
    arriving, leaving = [], []
    for which, target in enumerate((o_acts, o_ings)):
        for i in range(target.shape[0]):
            arriving.append(pltpu.make_async_copy(woven.at[which, i], passing.at[which, i], sems.at[0, which, i]))
            leaving.append(pltpu.make_async_copy(passing.at[which, i], target.at[i], sems.at[1, which, i]))
    for copy in arriving:
        copy.start()
    for one, two in zip(arriving, leaving):
        one.wait()
        two.start()
    for copy in coming:
        copy.wait()
    unit, width = o_out.shape[1:]
    for half in range(2):
        o_down[0, 2 * unit * half : 2 * unit * (half + 1), :] = f_d[half]
        for sub in range(2):
            part = 2 * half + sub
            cols = slice(part * width, (part + 1) * width)
            o_up[0, :, cols] = f_u[half, unit * sub : unit * (sub + 1), :]
            piece = f_a[half, unit * sub : unit * (sub + 1), :]
            if part == 3:
                o_out[0] = piece
            else:
                o_qkv[0, :, cols] = piece
    begin = 0
    for out in (o_g1, o_s1, o_bo, o_g2, o_s2, o_bd, o_qv):
        part = out.shape[1]
        out[...] = f_t[0, :, begin : begin + part]
        begin += part
    o_bu[...] = f_t[1, :, 0 : o_bu.shape[1]]
    for copy in leaving:
        copy.wait()


def local(
    images, cotangent, counts,
    ln1_gain, ln1_bias, w_qkv, b_qv, w_out, b_out, ln2_gain, ln2_bias, w_up, b_up, w_down, b_down,
):
    micro_count, slots, length, width = images.shape
    ff = w_up.shape[2]
    rows = -(-length // 16) * 16
    n = lax.axis_size("fsdp")
    unit = width // n
    first, rest = radices(n)
    total = slots * rows
    head_dim = width // HEADS

    def vm(*shape, kind=LOW):
        return pltpu.VMEM(shape, kind)

    tall = [(2 * unit, LOW)] * 3 + [(1, F32)]
    dma = lambda *shape: pltpu.SemaphoreType.DMA(shape)
    outs = [((2, slots, length, 2, width), LOW)]
    outs += [((2, r, width), F32) for r, _ in tall] + [((total, ff), LOW)] * 2 + [((2, 2, slots, length, width), LOW)]
    scratch = [
        vm(2, total, width), vm(3, length, 2, width), vm(slots, length, width), vm(slots, length, width),
        *[vm(2, r, width, kind=kind) for r, kind in tall],
        vm(2, width, 3 * width), vm(2, width, width), vm(2, width, ff), vm(2, ff, width),
        vm(2, TABLE, width, kind=F32), vm(2, TABLE, width, kind=F32),
        vm(unit, width), vm(2 * unit, 2 * width), vm(4 * unit, 4 * width),
        vm(total, width, kind=F32), vm(2, total, width), vm(2, total, 3 * width), vm(2, slots, HEADS, rows, rows),
        vm(2, total, width),
        vm(2, total, width), vm(2, total, width), vm(total, 6, kind=F32),
        vm(total, ff), vm(total, ff), vm(total, width), vm(total, width), vm(width, total),
    ]
    scratch += [vm(2, 2, n, r, width, kind=kind) for r, kind in tall]
    scratch += [vm(n, r, width, kind=kind) for r, kind in tall]
    plane = rest * rest - 1
    for g, (r, kind) in enumerate(tall):
        direct = g in (ATT, TAB)
        scratch.append(vm(*((plane, first) if direct else (rest - 1, rest * first)), r, width, kind=kind))
    scratch += [vm(2, rest - 1, first, *tall[g][:1], width) for g in (UP, DOWN)]
    scratch += [vm(2, first, r, width, kind=kind) for r, kind in tall]
    scratch += [dma(2, slots), dma(2, 2 * slots), dma(2 * slots), dma(4, slots), dma(4, slots), dma(4, slots)]
    scratch += [dma(4, 2, first), dma(8, first)] + [dma(8, rest - 1)] * 4 + [dma(8, rest)] * 2 + [dma(2, first, plane)] * 2
    scratch += [dma(8)] * 2 + [dma(8, plane, 2)] * 2 + [dma(8, rest - 1)] * 2 + [dma(8, first), dma(4, 2, first)]
    scratch += [pltpu.SemaphoreType.REGULAR((2, 4))]
    dims = (slots, length, rows, width, ff, head_dim, n)
    vmem = pl.BlockSpec(memory_space=pltpu.VMEM)
    hbm = pl.BlockSpec(memory_space=pltpu.HBM)
    woven, f_a, f_u, f_d, f_t, *_ = pl.pallas_call(
        functools.partial(whole_kernel, dims),
        out_shape=[jax.ShapeDtypeStruct(*o) for o in outs],
        in_specs=[hbm, hbm, pl.BlockSpec(memory_space=pltpu.SMEM)] + [vmem] * 12,
        out_specs=[hbm] + [vmem] * 4 + [hbm] * 3,
        scratch_shapes=scratch,
        compiler_params=pltpu.CompilerParams(
            vmem_limit_bytes=(64 << 20) - (96 << 10), collective_id=0, has_side_effects=True
        ),
    )(
        images.transpose(1, 2, 0, 3), cotangent.transpose(1, 2, 0, 3), counts.T, ln1_gain, ln1_bias, b_out, ln2_gain, ln2_bias, b_down, b_qv, b_up,
        w_qkv, w_out, w_up, w_down,
    )

    params = (
        ln1_gain, ln1_bias, w_qkv, b_qv, w_out, b_out, ln2_gain, ln2_bias, w_up, b_up, w_down, b_down
    )
    acts, ings, *grads = pl.pallas_call(
        output_kernel,
        out_shape=[jax.ShapeDtypeStruct(woven.shape[1:], LOW)] * 2
        + [jax.ShapeDtypeStruct(p.shape, F32) for p in params],
        in_specs=[hbm] * 5,
        out_specs=[hbm] * 2 + [vmem] * len(params),
        scratch_shapes=[
            vm(2, slots, length, 2, width), *[vm(2, r, width, kind=F32) for r, _ in tall], dma(2, 2, slots), dma(4)
        ],
        compiler_params=pltpu.CompilerParams(vmem_limit_bytes=(64 << 20) - (96 << 10)),
    )(woven, f_a, f_u, f_d, f_t)

    def as_given(value):
        return value.transpose(2, 0, 1, 3)[None]

    return (as_given(acts), as_given(ings), *grads)


def solution(mesh):
    split = P("section", "fsdp")
    cube = P("section", "fsdp", None)
    image = P(None, "fsdp", None, None)
    result = P("section", None, "fsdp", None, None)
    params = (split, split, cube, split, cube, split, split, split, cube, split, cube, split)
    return jax.shard_map(
        local,
        mesh=mesh,
        in_specs=(image, image, P(None, "fsdp")) + params,
        out_specs=(result, result) + params,
        check_vma=False,
    )
```

```python
import functools
import math

import jax
import jax.numpy as jnp
from jax import lax
from jax.experimental import pallas as pl
from jax.experimental.pallas import tpu as pltpu
from jax.sharding import PartitionSpec as P

HEADS = 6
EPS = 1e-06
F32 = jnp.float32
LOW = jnp.bfloat16

G1, S1, BO, G2, S2, BD, BQ, BV, BU = 0, 1, 2, 3, 4, 5, 6, 7, 8
TABLE = 16
TOGETHER, TOGETHER_ROWS = 2, 2
ATT, UP, DOWN, TAB = 0, 1, 2, 3


def radices(n):
    rest = max(r for r in range(1, n + 1) if r * r * r <= n and n % (r * r) == 0)
    return n // (rest * rest), rest


def mm(left, right):
    return jnp.dot(left, right, preferred_element_type=F32)


def mm_right(left, right):
    return lax.dot_general(left, right, (((1,), (1,)), ((), ())), preferred_element_type=F32)


def mm_left(left, right):
    return lax.dot_general(left, right, (((0,), (0,)), ((), ())), preferred_element_type=F32)


def normal_parts(pre):
    phi = 0.5 + 0.5 * lax.erf(pre * 0.7071067811865476)
    low = pre.astype(LOW)
    density = jnp.exp2(low * low * LOW(-0.5 * 1.4426950408889634)) * LOW(0.3989422804014327)
    return phi, phi.astype(LOW) + low * density


def normalize(value):
    mean = jnp.mean(value, axis=-1, keepdims=True)
    center = value - mean
    rstd = lax.rsqrt(jnp.mean(center * center, axis=-1, keepdims=True) + EPS)
    return center * rstd, rstd, mean


def normalize_back(d_hat, hat, rstd):
    mean_one = jnp.mean(d_hat, axis=-1, keepdims=True)
    mean_two = jnp.mean(d_hat * hat, axis=-1, keepdims=True)
    return rstd * (d_hat - mean_one - hat * mean_two)


def colsum(value):
    return jnp.sum(value, axis=0, keepdims=True)


def whole_kernel(dims, *refs):
    slots, length, rows, width, ff, head_dim, n = dims
    (
        images, cotangent, counts, v_g1, v_s1, v_bo, v_g2, v_s2, v_bd, v_qv, v_up, a_qkv, a_out, a_up, a_down,
        woven, f_a, f_u, f_d, f_t, hid_far, slope_far, out_far,
        xs, raw, io_one, io_two, pack_a, pack_u, pack_d, pack_t,
        wqkv, wout, wup, wdown, table, gtable, rep_one, rep_two, rep_four,
        after_ref, nrm1, qkv, prob, overs, ctx, hat2, rstds, hid, slope, dal, low_g, left_t,
        s_a, s_u, s_d, s_t, r0_a, r0_u, r0_d, r0_t, r1_a, r1_u, r1_d, r1_t, r2_u, r2_d,
        r3_a, r3_u, r3_d, r3_t,
        in_s, weave_in, weave_out, ship_s, ship_r, far_s, ag1_s, ag1_r, ag2_s, ag2_r, ag3_s, ag3_r, ag4_s, ag4_r,
        rs0_s, rs0_r, rs1_s, rs1_r, rs2_s, rs2_r, rs3_s, rs3_r, credit,
    ) = refs
    groups = (ATT, UP, DOWN, TAB)
    pack = (pack_a, pack_u, pack_d, pack_t)
    stage = (s_a, s_u, s_d, s_t)
    r0, r1, r2 = (r0_a, r0_u, r0_d, r0_t), (r1_a, r1_u, r1_d, r1_t), (None, r2_u, r2_d, None)
    r3, final = (r3_a, r3_u, r3_d, r3_t), (f_a, f_u, f_d, f_t)

    first, rest = radices(n)
    unit = width // n
    core = lax.axis_index("section")
    me = lax.axis_index("fsdp")
    dig_a, dig_b, dig_c = me // (rest * rest), (me // rest) % rest, me % rest
    dig_three, dig_two = dig_c + core * (dig_b - dig_c), dig_b + core * (dig_c - dig_b)
    step_three, step_two = 1 + core * (rest - 1), rest - core * (rest - 1)
    pos = (dig_three * rest + dig_two) * first + dig_a
    pos_of = ((dig_c * rest + dig_b) * first + dig_a, (dig_b * rest + dig_c) * first + dig_a)
    sibling = {"section": 1 - core}

    def place(half, j):
        a, b, c = j // (rest * rest), (j // rest) % rest, j % rest
        return ((c * rest + b) if half == 0 else (b * rest + c)) * first + a

    def peer_first(t):
        return {"fsdp": me + ((dig_a + t) % first - dig_a) * (rest * rest)}

    def peer_two(t):
        return {"fsdp": me + ((dig_two + t) % rest - dig_two) * step_two}

    def peer_three(t):
        return {"fsdp": me + ((dig_three + t) % rest - dig_three) * step_three}

    def peer_plane(three, two):
        here = ((dig_three + three) % rest - dig_three) * step_three
        return {"fsdp": me + here + ((dig_two + two) % rest - dig_two) * step_two}

    plane = [(three, two) for three in range(rest) for two in range(rest) if three or two]

    def remote(src, dst, s_sem, r_sem, device):
        return pltpu.make_async_remote_copy(
            src_ref=src, dst_ref=dst, send_sem=s_sem, recv_sem=r_sem, device_id=device,
            device_id_type=pl.DeviceIdType.MESH,
        )

    def slab_two(three, two):
        return pl.ds((three * rest + two) * first, first)

    def slab_three(three):
        return pl.ds(three * rest * first, rest * first)

    def fill_repeats():
        for ref in (rep_one, rep_two, rep_four):
            part = ref.shape[0]
            lanes = lax.broadcasted_iota(jnp.int32, ref.shape, 1).astype(F32)
            line = lax.broadcasted_iota(jnp.int32, ref.shape, 0).astype(F32)
            rest_of = lanes - part * jnp.floor((lanes + 0.5) * (1.0 / part))
            ref[...] = jnp.where(jnp.abs(rest_of - line) < 0.5, 1.0, 0.0).astype(LOW)

    def own_lanes(part):
        shape = (n, part * n)
        lanes = lax.broadcasted_iota(jnp.int32, shape, 1)
        begin = lax.broadcasted_iota(jnp.int32, shape, 0) * part
        return (lanes >= begin) & (lanes < begin + part)

    shares = (
        ((G1, unit, rep_one), (S1, unit, rep_one), (BO, unit, rep_one), (G2, unit, rep_one), (S2, unit, rep_one),
         (BD, unit, rep_one), (BQ, 2 * unit, rep_two)),
        ((BU, 4 * unit, rep_four),),
    )

    def table_in(b):
        for half in range(2):
            lines = jnp.concatenate([s_t[b, half, place(half, j)] for j in range(n)], axis=0)
            begin = 0
            for row, part, ref in shares[half]:
                spread = mm(lines[:, begin : begin + part].astype(LOW), ref[...])
                line = colsum(jnp.where(own_lanes(part), spread, 0.0))
                for i in range(part * n // width):
                    table[b, row + i : row + i + 1, :] = line[:, width * i : width * (i + 1)]
                begin += part

    def table_out(b):
        for half in range(2):
            parts, begin = [], 0
            for row, part, ref in shares[half]:
                count = part * n // width
                line = jnp.concatenate([gtable[b, row + i : row + i + 1, :] for i in range(count)], axis=1)
                parts.append(mm_right(jnp.where(own_lanes(part), line, 0.0).astype(LOW), ref[...]))
                begin += part
            parts.append(jnp.zeros((n, width - begin), F32))
            lines = jnp.concatenate(parts, axis=1)
            for j in range(n):
                s_t[b, half, place(half, j)] = lines[j : j + 1]

    def pack_own():
        for half in range(2):
            vectors = ((v_g1, v_s1, v_bo, v_g2, v_s2, v_bd, v_qv), (v_up,))[half]
            lines = [vector[...].astype(F32) for vector in vectors]
            lines.append(jnp.zeros((1, width - sum(line.shape[1] for line in lines)), F32))
            pack_t[half] = jnp.concatenate(lines, axis=1)
            for ref in (pack_a, pack_u):
                both = []
                for part in (2 * half, 2 * half + 1):
                    if ref is pack_u:
                        both.append(a_up[0, :, part * width : (part + 1) * width])
                    elif part == 3:
                        both.append(a_out[0])
                    else:
                        both.append(a_qkv[0, :, part * width : (part + 1) * width])
                ref[half] = jnp.concatenate([value.astype(F32) for value in both], axis=0).astype(LOW)
            pack_d[half] = a_down[0, 2 * unit * half : 2 * unit * (half + 1), :]

    def at(b, g):
        return len(groups) * b + g

    def ag1_copy(b, g, half, t):
        device = {"section": half, **peer_first(t)} if t else sibling
        return remote(
            pack[g].at[half], stage[g].at[b, half, pos_of[half]],
            ag1_s.at[g, half, t], ag1_r.at[at(b, g), t], device,
        )

    def ag1_landing(b, g, t):
        ref = stage[g].at[b, core, (dig_three * rest + dig_two) * first + (dig_a + first - t) % first]
        return remote(ref, ref, ag1_s.at[g, 0, t], ag1_r.at[at(b, g), t], sibling)

    def ag2_copy(b, g, t):
        ref = stage[g].at[b, core, slab_two(dig_three, dig_two)]
        return remote(ref, ref, ag2_s.at[at(b, g), t - 1], ag2_r.at[at(b, g), t - 1], peer_two(t))

    def ag3_copy(b, g, t):
        ref = stage[g].at[b, core, slab_three(dig_three)]
        return remote(ref, ref, ag3_s.at[at(b, g), t - 1], ag3_r.at[at(b, g), t - 1], peer_three(t))

    def ag4_copy(b, g, t):
        ref = stage[g].at[b, core, slab_three((dig_three + rest - t) % rest)]
        return remote(ref, ref, ag4_s.at[at(b, g), t], ag4_r.at[at(b, g), t], sibling)

    def ag4_landing(b, g, t):
        ref = stage[g].at[b, 1 - core, slab_three((dig_two + rest - t) % rest)]
        return remote(ref, ref, ag4_s.at[at(b, g), t], ag4_r.at[at(b, g), t], sibling)

    def ag1(b, g):
        @pl.when(core == b)
        def _():
            for t in range(1, first):
                for half in range(2):
                    ag1_copy(b, g, half, t).start()
            ag1_copy(b, g, 1 - b, 0).start()
            stage[g][b, b, pos] = pack[g][b]

    def ag2(b, g):
        for t in range(1, first):
            ag1_landing(b, g, t).wait_recv()

        @pl.when(core != b)
        def _():
            ag1_landing(b, g, 0).wait_recv()

        for t in range(1, rest):
            ag2_copy(b, g, t).start()

    def ag3(b, g):
        for t in range(1, rest):
            ag2_copy(b, g, t).wait_recv()
        for t in range(1, rest):
            ag3_copy(b, g, t).start()
        ag4_copy(b, g, 0).start()

    def ag4(b, g):
        for t in range(1, rest):
            ag3_copy(b, g, t).wait_recv()
            ag4_copy(b, g, t).start()

    def ag5(b, g):
        for t in range(rest):
            ag4_landing(b, g, t).wait_recv()
        lay_out(b, g)

    def ag_sent(b, g):
        @pl.when(core == b)
        def _():
            for t in range(1, first):
                for half in range(2):
                    ag1_copy(b, g, half, t).wait_send()
            ag1_copy(b, g, 1 - b, 0).wait_send()

        for t in range(1, rest):
            ag2_copy(b, g, t).wait_send()
            ag3_copy(b, g, t).wait_send()
        for t in range(rest):
            ag4_copy(b, g, t).wait_send()

    def lay_out(b, g):
        if g == TAB:
            table_in(b)
            return
        if g == DOWN:
            for j in range(n):
                for half in range(2):
                    begin = 4 * unit * j + 2 * unit * half
                    wdown[b, begin : begin + 2 * unit, :] = s_d[b, half, place(half, j)]
            return
        together = 16 // math.gcd(unit, 16)
        for half in range(2):
            for j in range(0, n, together):
                pieces = [stage[g][b, half, place(half, j + i)].astype(F32) for i in range(together)]
                for sub in range(2):
                    low = sub * unit
                    block = jnp.concatenate([piece[low : low + unit] for piece in pieces], axis=0).astype(LOW)
                    part = 2 * half + sub
                    down = slice(unit * j, unit * (j + together))
                    if g == UP:
                        wup[b, down, part * width : (part + 1) * width] = block
                    elif part == 3:
                        wout[b, down, :] = block
                    else:
                        wqkv[b, down, part * width : (part + 1) * width] = block

    def rs0_copy(b, g):
        return remote(stage[g].at[b, 1 - core], r0[g], rs0_s.at[at(b, g)], rs0_r.at[at(b, g)], sibling)

    def rs1_copy(b, g, t):
        return remote(
            stage[g].at[b, core, slab_three((dig_three + t) % rest)], r1[g].at[t - 1],
            rs1_s.at[at(b, g), t - 1, 0], rs1_r.at[at(b, g), t - 1, 0], peer_three(t),
        )

    def rs2_copy(b, g, t):
        return remote(
            stage[g].at[b, core, slab_two(dig_three, (dig_two + t) % rest)], r2[g].at[b, t - 1],
            rs2_s.at[at(b, g), t - 1], rs2_r.at[at(b, g), t - 1], peer_two(t),
        )

    def rs3_copy(b, g, t):
        there = (dig_three * rest + dig_two) * first + (dig_a + t) % first
        device = {"section": b, **peer_first(t)} if t else sibling
        return remote(
            stage[g].at[b, core, there], r3[g].at[core, t], rs3_s.at[at(b, g), t], rs3_r.at[g, core, t], device
        )

    chunk_count = 2 if first % 2 == 0 else 1
    chunk_size = first // chunk_count

    def plane_copy(b, g, t, part):
        three, two = plane[t]
        begin = (((dig_three + three) % rest) * rest + (dig_two + two) % rest) * first + chunk_size * part
        return remote(
            stage[g].at[b, core, pl.ds(begin, chunk_size)], r1[g].at[t, pl.ds(chunk_size * part, chunk_size)],
            rs1_s.at[at(b, g), t, part], rs1_r.at[at(b, g), t, part], peer_plane(three, two),
        )

    def rs0(b, g):
        @pl.when(b == 0)
        def _():
            pl.semaphore_wait(credit.at[0, g], 1)

        rs0_copy(b, g).start()

    def rs1(b, g):
        rs0_copy(b, g).wait_recv()

        @pl.loop(0, n)
        def _(p):
            stage[g][b, core, p] = stage[g][b, core, p] + r0[g][p]

        @pl.when(b == 1)
        def _():
            pl.semaphore_signal(credit.at[0, g], inc=1, device_id=sibling, device_id_type=pl.DeviceIdType.MESH)

        direct = g in (ATT, TAB)
        if rest > 1:
            @pl.when(b == 0)
            def _():
                pl.semaphore_wait(credit.at[1, g], len(plane) if direct else rest - 1)

        if direct:
            for part in range(chunk_count):
                for t in range(len(plane)):
                    plane_copy(b, g, t, part).start()
            return
        for t in range(1, rest):
            rs1_copy(b, g, t).start()

    def rs2(b, g):
        for t in range(1, rest):
            rs1_copy(b, g, t).wait_recv()

        @pl.loop(0, rest * first)
        def _(p):
            here = dig_three * rest * first + p
            total = stage[g][b, core, here].astype(F32)
            for t in range(1, rest):
                total = total + r1[g][t - 1, p].astype(F32)
            stage[g][b, core, here] = total.astype(stage[g].dtype)

        for t in range(1, rest):
            @pl.when(b == 1)
            def _():
                pl.semaphore_signal(
                    credit.at[1, g], inc=1, device_id=peer_three(t), device_id_type=pl.DeviceIdType.MESH
                )

            rs2_copy(b, g, t).start()

    def rs3_send(b, g, part):
        def here(digit):
            return (digit >= chunk_size * part) & (digit < chunk_size * (part + 1))

        for t in range(1, first):
            @pl.when(here((dig_a + t) % first))
            def _():
                rs3_copy(b, g, t).start()

        @pl.when(here(dig_a) & (core != b))
        def _():
            rs3_copy(b, g, 0).start()

    def rs3_part(b, g, part):
        for t in range(len(plane)):
            plane_copy(b, g, t, part).wait_recv()

        @pl.loop(chunk_size * part, chunk_size * (part + 1))
        def _(p):
            here = (dig_three * rest + dig_two) * first + p
            total = stage[g][b, core, here].astype(F32)
            for t in range(len(plane)):
                total = total + r1[g][t, p].astype(F32)
            stage[g][b, core, here] = total.astype(stage[g].dtype)

        rs3_send(b, g, part)

    def rs3_first(b, g):
        rs3_part(b, g, 0)

    def rs3_rest(b, g):
        for part in range(1, chunk_count):
            rs3_part(b, g, part)

    def rs3(b, g):
        if g in (ATT, TAB):
            for part in range(chunk_count):
                rs3_part(b, g, part)

            @pl.when(b == 1)
            def _():
                for three, two in plane:
                    pl.semaphore_signal(
                        credit.at[1, g], inc=1, device_id=peer_plane(three, two),
                        device_id_type=pl.DeviceIdType.MESH,
                    )

            return
        for t in range(1, rest):
            rs2_copy(b, g, t).wait_recv()

        @pl.loop(0, first)
        def _(p):
            here = (dig_three * rest + dig_two) * first + p
            total = stage[g][b, core, here].astype(F32)
            for t in range(1, rest):
                total = total + r2[g][b, t - 1, p].astype(F32)
            stage[g][b, core, here] = total.astype(stage[g].dtype)

        for part in range(chunk_count):
            rs3_send(b, g, part)

    def rs4(b, g):
        @pl.when(core == b)
        def _():
            for own in (True, False):
                half = core if own else 1 - core
                begin = int(own)
                for t in range(begin, first):
                    ref = r3[g].at[half, t]
                    remote(ref, ref, rs3_s.at[at(b, g), t], rs3_r.at[g, half, t], sibling).wait_recv()
                total = stage[g][b, core, pos].astype(F32) if own else None
                for t in range(begin, first):
                    value = r3[g][half, t].astype(F32)
                    total = value if total is None else total + value
                final[g][half] = total

    def rs_sent(b, g):
        rs0_copy(b, g).wait_send()
        if g in (ATT, TAB):
            for part in range(chunk_count):
                for t in range(len(plane)):
                    plane_copy(b, g, t, part).wait_send()
        else:
            for t in range(1, rest):
                rs1_copy(b, g, t).wait_send()
                rs2_copy(b, g, t).wait_send()
        for t in range(1, first):
            rs3_copy(b, g, t).wait_send()

        @pl.when(core != b)
        def _():
            rs3_copy(b, g, 0).wait_send()

    def rows_of(i, images_too=1):
        return pl.ds(pl.multiple_of(i * rows, 16), images_too * rows)

    few = TOGETHER if slots % TOGETHER == 0 else 1
    many = TOGETHER_ROWS if slots % TOGETHER_ROWS == 0 else 1

    def step_rows(i, count):
        return rows_of(i * count, count)

    def ship_parts(kind, b, i):
        src, out = (io_one, io_two)[kind].at[i], out_far.at[kind, core, i]
        q = 2 * kind + b
        near = pltpu.make_async_copy(src, out, ship_s.at[q, i])
        far = remote(src, out, ship_s.at[q, i], ship_r.at[q, i], sibling)
        return near, far

    def ship(kind, b, i):
        near, far = ship_parts(kind, b, i)

        @pl.when(core == b)
        def _():
            near.start()

        @pl.when(core != b)
        def _():
            far.start()

    def shipped(kind, b, i):
        near, far = ship_parts(kind, b, i)

        @pl.when(core == b)
        def _():
            near.wait()

        @pl.when(core != b)
        def _():
            far.wait_send()

    def landed(kind, b, i):
        q = 2 * kind + b
        ref = out_far.at[kind, 1 - core, i]

        @pl.when(core == b)
        def _():
            remote(ref, ref, ship_s.at[q, i], ship_r.at[q, i], sibling).wait_recv()

    def live(i):
        return jnp.where(i < counts[0, core], 1.0, 0.0).astype(F32)

    def only_live(i, value, count):
        parts = [value[rows * m : rows * (m + 1)] * live(i * count + m) for m in range(count)]
        return jnp.concatenate(parts, axis=0)

    def coming(which, i):
        slot = (which * slots + i) % raw.shape[0]
        return pltpu.make_async_copy((images, cotangent)[which].at[i], raw.at[slot], in_s.at[which, i])

    def take_in(which, i):
        coming(which, i).wait()
        both = raw[(which * slots + i) % raw.shape[0]].astype(F32)
        (io_one, io_two)[which][i] = jnp.where(core == 0, both[:, 0, :], both[:, 1, :]).astype(LOW)

    def weave(todo):
        ring = raw.shape[0]
        count = 2 * slots

        def fetch(t, m):
            source = out_far.at[t // slots, m, t % slots]
            return pltpu.make_async_copy(source, io_one.at[2 * (t % ring) + m], weave_in.at[m, t])

        def leave(t):
            return pltpu.make_async_copy(raw.at[t % ring], woven.at[t // slots, t % slots], weave_out.at[t])

        for t in range(ring - 1):
            for m in range(2):
                fetch(t, m).start()

        @pl.loop(0, count)
        def _(t):
            for when, act in todo.items():
                @pl.when(t == when)
                def _():
                    act()

            @pl.when(t + ring - 1 < count)
            def _():
                for m in range(2):
                    fetch(t + ring - 1, m).start()

            @pl.when(t >= ring)
            def _():
                leave(t - ring).wait()

            for m in range(2):
                fetch(t, m).wait()
                raw[t % ring, :, m, :] = io_one[2 * (t % ring) + m]
            leave(t).start()

        for t in range(count - ring, count):
            leave(t).wait()

    def far_copy(which, i, back):
        near, far = ((hid, hid_far), (slope, slope_far))[which]
        near, far = near.at[rows_of(i)], far.at[rows_of(i)]
        src, dst = (far, near) if back else (near, far)
        return pltpu.make_async_copy(src, dst, far_s.at[2 * int(back) + which, i])

    pairs = width // 128
    scale = head_dim ** -0.5
    lane = lax.broadcasted_iota(jnp.int32, (1, 128), 1)
    half_low = [(lane < head_dim).astype(LOW), (lane >= head_dim).astype(LOW)]
    half_f = [(lane < head_dim).astype(F32), (lane >= head_dim).astype(F32)]
    token = lax.broadcasted_iota(jnp.int32, (rows, 128), 0) < length
    half_valid = [jnp.where(token, half_f[j], 0.0).astype(LOW) for j in range(2)]
    valid_lanes = jnp.where(lax.broadcasted_iota(jnp.int32, (1, rows), 1) < length, 1.0, 0.0).astype(F32)
    spare = -rows % 128
    chunk = 2 * width
    chunks = ff // chunk

    def vec(s, r):
        return table[s, r : r + 1, :]

    def up_bias(s, c):
        begin = c * chunk
        row, col = begin // width, begin % width
        if col + chunk <= width:
            return table[s, BU + row : BU + row + 1, col : col + chunk]
        a = table[s, BU + row : BU + row + 1, col:width]
        b = table[s, BU + row + 1 : BU + row + 2, 0 : chunk - (width - col)]
        return jnp.concatenate([a, b], axis=1)

    def add_vec(s, r, value):
        gtable[s, r : r + 1, :] += value

    def add_up_bias(s, c, value):
        begin = c * chunk
        row, col = begin // width, begin % width
        if col + chunk <= width:
            gtable[s, BU + row : BU + row + 1, col : col + chunk] += value
        else:
            cut = width - col
            gtable[s, BU + row : BU + row + 1, col:width] += value[:, :cut]
            gtable[s, BU + row + 1 : BU + row + 2, 0 : chunk - cut] += value[:, cut:]

    def attn_forward(s, x, hat, i):
        rd = step_rows(i, few)
        nrm_ref, qkv_ref, prob_ref, ctx_ref = nrm1.at[s], qkv.at[s], prob.at[s], ctx.at[s]
        nrm = (hat * vec(s, G1) + vec(s, S1)).astype(LOW)
        nrm_ref[rd, :] = nrm
        mixed = mm(nrm, wqkv[s])
        q = (mixed[:, 0:width] + vec(s, BQ)).astype(LOW)
        k = mixed[:, width : 2 * width].astype(LOW)
        v = (mixed[:, 2 * width :] + vec(s, BV)).astype(LOW)
        qkv_ref[rd, 0:width] = q
        qkv_ref[rd, width : 2 * width] = k
        qkv_ref[rd, 2 * width :] = v
        images_out = []
        for m in range(few):
            mine = slice(rows * m, rows * (m + 1))
            parts = []
            for p in range(pairs):
                cols = slice(128 * p, 128 * p + 128)
                weights, sides = [], []
                for j in range(2):
                    keys = k[mine, cols] * half_low[j]
                    keys = jnp.concatenate([keys, keys[rows - spare :]], axis=0)
                    scores = mm_right(q[mine, cols], keys)
                    top = jnp.max(scores, axis=-1, keepdims=True)
                    e = jnp.exp2((scores - top) * (scale * 1.4426950408889634)).astype(LOW)
                    prob_ref[i * few + m, 2 * p + j] = e[:, :rows]
                    weights.append(e)
                    sides.append(jnp.concatenate([v[mine, cols] * half_valid[j], half_valid[j]], axis=1))
                    sides.append(jnp.zeros((spare, 256), LOW))
                total = mm(jnp.concatenate(weights, axis=1), jnp.concatenate(sides, axis=0))
                over = 1.0 / total[:, 128:]
                overs[s, rows_of(i * few + m), cols] = over.astype(LOW)
                parts.append((total[:, :128] * over).astype(LOW))
            images_out.append(jnp.concatenate(parts, axis=1))
        context = jnp.concatenate(images_out, axis=0)
        ctx_ref[rd, :] = context
        return x + mm(context, wout[s]) + vec(s, BO)

    def ff_forward(s, after, rd):
        hat, rstd, _ = normalize(after)
        hat2[s, rd, :] = hat.astype(LOW)
        nrm = (hat * vec(s, G2) + vec(s, S2)).astype(LOW)
        total = after + vec(s, BD)
        for c in range(chunks):
            cols = slice(chunk * c, chunk * c + chunk)
            pre = mm(nrm, wup[s, :, cols]) + up_bias(s, c)
            phi, slo = normal_parts(pre)
            h = (pre * phi).astype(LOW)
            hid[rd, cols] = h
            slope[rd, cols] = slo.astype(LOW)
            total = total + mm(h, wdown[s, cols, :])
        return total, rstd

    def ff_backward(s, g, rd, rstd):
        g_low = g.astype(LOW)
        add_vec(s, BD, colsum(g_low.astype(F32)))
        d_nrm = None
        for c in range(chunks):
            cols = slice(chunk * c, chunk * c + chunk)
            d_hid = mm_right(g_low, wdown[s, cols, :])
            d_pre = (d_hid * slope[rd, cols].astype(F32)).astype(LOW)
            slope[rd, cols] = d_pre
            add_up_bias(s, c, colsum(d_pre.astype(F32)))
            part = mm_right(d_pre, wup[s, :, cols])
            d_nrm = part if d_nrm is None else d_nrm + part
        hat = hat2[s, rd, :].astype(F32)
        add_vec(s, G2, colsum(d_nrm * hat))
        add_vec(s, S2, colsum(d_nrm))
        d_after = g + normalize_back(d_nrm * vec(s, G2), hat, rstd)
        low = d_after.astype(LOW)
        dal[rd, :] = low
        add_vec(s, BO, colsum(low.astype(F32)))
        return d_after

    def attn_backward(s, i):
        qkv_ref, prob_ref, ctx_ref = qkv.at[s], prob.at[s], ctx.at[s]
        rd = step_rows(i, few)
        d_context = mm_right(dal[rd, :], wout[s])
        d_context = (d_context * overs[s, rd, :].astype(F32)).astype(LOW)
        for m in range(few):
            rd = rows_of(i * few + m)
            d_ctx = d_context[rows * m : rows * (m + 1)]
            dq, dk, dv = [], [], []
            for p in range(pairs):
                cols = slice(128 * p, 128 * p + 128)
                q = qkv_ref[rd, 128 * p : 128 * p + 128]
                k = qkv_ref[rd, width + 128 * p : width + 128 * p + 128]
                v = qkv_ref[rd, 2 * width + 128 * p : 2 * width + 128 * p + 128]
                dc = d_ctx[:, cols]
                both = dc.astype(F32) * ctx_ref[rd, cols].astype(F32)
                q_t, dc_t = q.T, dc.T
                to_q, to_k, to_v = None, [], []
                for j in range(2):
                    e = prob_ref[i * few + m, 2 * p + j]
                    delta = jnp.sum(both * half_f[j], axis=-1, keepdims=True)
                    d_prob = mm_right(dc, v * half_low[j])
                    ds = (e.astype(F32) * (d_prob - delta)).astype(LOW)
                    part = mm(ds, k * half_valid[j])
                    to_q = part if to_q is None else to_q + part
                    head = slice(head_dim * j, head_dim * (j + 1))
                    to_k.append(mm(q_t[head], ds))
                    to_v.append(mm(dc_t[head], e))
                dq.append((to_q * scale).astype(LOW))
                dk.append((jnp.concatenate(to_k, axis=0) * (valid_lanes * scale)).astype(LOW).T)
                dv.append((jnp.concatenate(to_v, axis=0) * valid_lanes).astype(LOW).T)
            d_mixed = jnp.concatenate(dq + dk + dv, axis=1)
            qkv_ref[rd, :] = d_mixed
            add_vec(s, BQ, colsum(d_mixed[:, 0:width].astype(F32)))
            add_vec(s, BV, colsum(d_mixed[:, 2 * width :].astype(F32)))

    def input_backward(s, d_after, rd, x, mean, rstd):
        d_nrm = mm_right(qkv[s, rd, :], wqkv[s])
        hat = (x - mean) * rstd
        add_vec(s, G1, colsum(d_nrm * hat))
        add_vec(s, S1, colsum(d_nrm))
        return d_after + normalize_back(d_nrm * vec(s, G1), hat, rstd)

    def grads_down(s):
        left_t[...] = low_g[...].T

        @pl.loop(0, 2)
        def _(c):
            cols = pl.ds(pl.multiple_of(c * 2 * width, 128), 2 * width)
            block = mm(left_t[...], hid[:, cols]).T
            for i in range(n // 2):
                for half in range(2):
                    begin = 4 * unit * i + 2 * unit * half
                    s_d[s, half, place(half, c * (n // 2) + i)] = block[begin : begin + 2 * unit].astype(LOW)

    def pair_out(ref, s, half, one, two):
        for j in range(n):
            down = slice(unit * j, unit * (j + 1))
            piece = jnp.concatenate([one[down], two[down]], axis=0).astype(LOW)
            ref[s, half, place(half, j)] = piece

    def grads_up(s):
        left_t[...] = (hat2[s].astype(F32) * vec(s, G2) + vec(s, S2)).astype(LOW).T
        for half in range(2):
            both = mm(left_t[...], slope[:, 2 * half * width : 2 * (half + 1) * width])
            pair_out(s_u, s, half, both[:, :width], both[:, width:])

    def grads_attn(s):
        mix_s = qkv.at[s]
        left_t[...] = ctx[s].T
        four = mm(left_t[...], dal[...])
        left_t[...] = nrm1[s].T
        three = mm(left_t[...], mix_s[:, 2 * width :])
        pair_out(s_a, s, 1, three, four)
        both = mm(left_t[...], mix_s[:, 0 : 2 * width])
        pair_out(s_a, s, 0, both[:, :width], both[:, width:])

    barrier = pltpu.get_barrier_semaphore()
    greeted = [sibling]
    greeted += [{"section": half, **peer_first(t)} for t in range(1, first) for half in range(2)]
    greeted += [peer_plane(three, two) for three, two in plane]
    for device in greeted:
        pl.semaphore_signal(barrier, inc=1, device_id=device, device_id_type=pl.DeviceIdType.MESH)
    pack_own()
    pl.semaphore_wait(barrier, len(greeted))

    def run(*todo):
        for f, b, g in todo:
            f(b, g)

    def events(i, table_of):
        for when, todo in table_of.items():
            @pl.when(i == when)
            def _():
                run(*todo)

    def both(f, b, g):
        return [(f, b, g), (f, b, TAB)]

    def take(i, m):
        return pl.ds(pl.multiple_of((i * many + m) * rows, 16), length)

    ahead = raw.shape[0]
    run(*both(ag1, 0, ATT))
    for i in range(ahead):
        coming(0, i).start()
    fill_repeats()
    gtable[...] = jnp.zeros_like(gtable)
    low_g[...] = jnp.zeros_like(low_g)
    xs[0] = jnp.zeros_like(low_g)

    @pl.loop(0, slots)
    def images_in(i):
        take_in(0, i)

        @pl.when(i + ahead < slots)
        def _():
            coming(0, i + ahead).start()

        @pl.when(i + ahead >= slots)
        def _():
            coming(1, i + ahead - slots).start()

        @pl.when(i == 4)
        def _():
            run((ag1, 0, UP))

    run(*both(ag2, 0, ATT), (ag1, 0, DOWN), *both(ag1, 1, ATT))

    def statistic(s, rd, which):
        return jnp.where(s == 0, rstds[rd, which : which + 1], rstds[rd, 3 + which : 4 + which])

    def first_norm(s, rd, x):
        hat, rstd, mean = normalize(x)
        after_ref[rd, :] = hat
        rstds[rd, 3 * s : 3 * s + 1] = rstd
        rstds[rd, 3 * s + 2 : 3 * s + 3] = mean

    @pl.loop(0, slots // many)
    def norm_one(i):
        for m in range(many):
            xs[0, take(i, m), :] = io_one[i * many + m]
        rd = step_rows(i, many)
        x = xs[0, rd, :].astype(F32)
        token_rows = lax.broadcasted_iota(jnp.int32, (rows, width), 0) < length
        parts = [x[rows * m : rows * (m + 1)] for m in range(many)]
        x = jnp.concatenate([jnp.where(token_rows, part, part[0:1]) for part in parts], axis=0)
        xs[0, rd, :] = x.astype(LOW)
        first_norm(0, rd, x)

    run((ag2, 0, UP), *both(ag3, 0, ATT), (ag1, 1, UP), (ag1, 1, DOWN), (ag2, 0, DOWN), (ag3, 0, UP))

    @pl.loop(0, slots)
    def cotangents_in(i):
        take_in(1, i)

        @pl.when(i + ahead < slots)
        def _():
            coming(1, i + ahead).start()

    run(*both(ag4, 0, ATT), (ag3, 0, DOWN), *both(ag2, 1, ATT), *both(ag5, 0, ATT))

    @pl.loop(0, 2)
    def forward(s):
        @pl.loop(0, slots // few)
        def attention(i):
            @pl.when(s == 0)
            def _():
                events(i, {1: [(ag4, 0, UP), (ag2, 1, UP)], 2: [(ag4, 0, DOWN)]})

            @pl.when(s == 1)
            def _():
                events(i, {1: [(ag4, 1, UP)], 2: [(ag4, 1, DOWN)]})

            rd = step_rows(i, few)
            after_ref[rd, :] = attn_forward(s, xs[s, rd, :].astype(F32), after_ref[rd, :], i)

        @pl.when(s == 0)
        def _():
            run(*both(ag3, 1, ATT), (ag5, 0, UP), (ag5, 0, DOWN))

        @pl.when(s == 1)
        def _():
            run((ag5, 1, UP), (ag5, 1, DOWN))

        @pl.loop(0, slots // many)
        def feed_forward(i):
            @pl.when(s == 0)
            def _():
                events(i, {0: [(ag2, 1, DOWN), (ag3, 1, UP)], 2: both(ag4, 1, ATT)})

            rd = step_rows(i, many)

            @pl.when(s == 1)
            def _():
                for m in range(many):
                    far_copy(0, i * many + m, False).wait()
                    far_copy(1, i * many + m, False).wait()
                    shipped(0, 0, i * many + m)

            out, rstd2 = ff_forward(s, after_ref[rd, :], rd)
            for block in range(2):
                @pl.when(s == block)
                def _():
                    rstds[rd, 3 * block + 1 : 3 * block + 2] = rstd2

            out = only_live(i, out, many)
            for m in range(many):
                io_one[i * many + m] = out[rows * m : rows * m + length].astype(LOW)
                ship(0, s, i * many + m)

            @pl.when(s == 0)
            def _():
                for m in range(many):
                    far_copy(0, i * many + m, False).start()
                    far_copy(1, i * many + m, False).start()
                low = out.astype(LOW)
                xs[1, rd, :] = low
                first_norm(1, rd, low.astype(F32))

        @pl.when(s == 0)
        def _():
            run((ag3, 1, DOWN), *both(ag5, 1, ATT))

    for b in range(2):
        for g in groups:
            ag_sent(b, g)

    @pl.loop(0, 2)
    def backward(turn):
        s = 1 - turn

        @pl.when(s == 0)
        def _():
            run((rs3, 1, DOWN))

        @pl.loop(0, slots // many)
        def feed_forward(i):
            @pl.when(s == 0)
            def _():
                events(i, {1: [*both(rs1, 1, ATT), (rs3, 1, UP)]})
                for m in range(many):
                    far_copy(1, i * many + m, True).wait()

            rd = step_rows(i, many)
            for m in range(many):
                g = live(i * many + m) * io_two[i * many + m].astype(F32)
                low_g[take(i, m), :] = g.astype(LOW)
            after_ref[rd, :] = ff_backward(s, low_g[rd, :].astype(F32), rd, statistic(s, rd, 1))

        @pl.when(s == 0)
        def _():
            for i in range(slots):
                far_copy(0, i, True).wait()

        grads_down(s)
        run((rs0, s, DOWN))

        @pl.when(s == 1)
        def _():
            for i in range(slots):
                far_copy(0, i, True).start()

        grads_up(s)
        run((rs0, s, UP))

        @pl.when(s == 1)
        def _():
            for i in range(slots):
                far_copy(1, i, True).start()

        @pl.when(s == 0)
        def _():
            run((rs4, 1, DOWN), (rs4, 1, UP))

        @pl.loop(0, slots // few)
        def attention(i):
            @pl.when(s == 0)
            def _():
                events(i, {1: both(rs3, 1, ATT)})

            events(i, {1: [(rs1, s, DOWN), (rs1, s, UP)]})
            attn_backward(s, i)

        run((rs2, s, DOWN))

        @pl.when(s == 0)
        def _():
            run(*both(rs4, 1, ATT))

        grads_attn(s)
        run((rs0, s, ATT), (rs2, s, UP))

        @pl.loop(0, slots // many)
        def to_input(i):
            rd = step_rows(i, many)
            x = xs[s, rd, :].astype(F32)
            d_in = input_backward(s, after_ref[rd, :], rd, x, statistic(s, rd, 2), statistic(s, rd, 0))
            for m in range(many):
                @pl.when(s == 0)
                def _():
                    shipped(1, 1, i * many + m)

                io_two[i * many + m] = d_in[rows * m : rows * m + length].astype(LOW)
                ship(1, s, i * many + m)

        table_out(s)
        run((rs0, s, TAB))

    def sent_and_landed(kind):
        @pl.loop(0, slots)
        def _(i):
            shipped(kind, 1 - kind, i)
            for b in range(2):
                landed(kind, b, i)

    sent_and_landed(0)
    weave({
        1: lambda: run(*both(rs1, 0, ATT), (rs3, 0, DOWN), (rs3, 0, UP)),
        slots - raw.shape[0] + 1: lambda: sent_and_landed(1),
        slots: lambda: run(*both(rs3_first, 0, ATT)),
        slots + 3: lambda: run(*both(rs3_rest, 0, ATT), (rs4, 0, DOWN), (rs4, 0, UP)),
    })
    run(*both(rs4, 0, ATT))
    for b in range(2):
        for g in groups:
            rs_sent(b, g)


def output_kernel(
    woven, far_a, far_u, far_d, far_t, o_acts, o_ings, o_g1, o_s1, o_qkv, o_qv, o_out, o_bo, o_g2, o_s2, o_up, o_bu, o_down, o_bd,
    passing, f_a, f_u, f_d, f_t, sems, grad_sems
):
    coming = [
        pltpu.make_async_copy(source, target, grad_sems.at[i])
        for i, (source, target) in enumerate(((far_a, f_a), (far_u, f_u), (far_d, f_d), (far_t, f_t)))
    ]
    for copy in coming:
        copy.start()
    arriving, leaving = [], []
    for which, target in enumerate((o_acts, o_ings)):
        for i in range(target.shape[0]):
            arriving.append(pltpu.make_async_copy(woven.at[which, i], passing.at[which, i], sems.at[0, which, i]))
            leaving.append(pltpu.make_async_copy(passing.at[which, i], target.at[i], sems.at[1, which, i]))
    for copy in arriving:
        copy.start()
    for one, two in zip(arriving, leaving):
        one.wait()
        two.start()
    for copy in coming:
        copy.wait()
    unit, width = o_out.shape[1:]
    for half in range(2):
        o_down[0, 2 * unit * half : 2 * unit * (half + 1), :] = f_d[half]
        for sub in range(2):
            part = 2 * half + sub
            cols = slice(part * width, (part + 1) * width)
            o_up[0, :, cols] = f_u[half, unit * sub : unit * (sub + 1), :]
            piece = f_a[half, unit * sub : unit * (sub + 1), :]
            if part == 3:
                o_out[0] = piece
            else:
                o_qkv[0, :, cols] = piece
    begin = 0
    for out in (o_g1, o_s1, o_bo, o_g2, o_s2, o_bd, o_qv):
        part = out.shape[1]
        out[...] = f_t[0, :, begin : begin + part]
        begin += part
    o_bu[...] = f_t[1, :, 0 : o_bu.shape[1]]
    for copy in leaving:
        copy.wait()


def local(
    images, cotangent, counts,
    ln1_gain, ln1_bias, w_qkv, b_qv, w_out, b_out, ln2_gain, ln2_bias, w_up, b_up, w_down, b_down,
):
    micro_count, slots, length, width = images.shape
    ff = w_up.shape[2]
    rows = -(-length // 16) * 16
    n = lax.axis_size("fsdp")
    unit = width // n
    first, rest = radices(n)
    total = slots * rows
    head_dim = width // HEADS

    def vm(*shape, kind=LOW):
        return pltpu.VMEM(shape, kind)

    tall = [(2 * unit, LOW)] * 3 + [(1, F32)]
    dma = lambda *shape: pltpu.SemaphoreType.DMA(shape)
    outs = [((2, slots, length, 2, width), LOW)]
    outs += [((2, r, width), F32) for r, _ in tall] + [((total, ff), LOW)] * 2 + [((2, 2, slots, length, width), LOW)]
    scratch = [
        vm(2, total, width), vm(3, length, 2, width), vm(slots, length, width), vm(slots, length, width),
        *[vm(2, r, width, kind=kind) for r, kind in tall],
        vm(2, width, 3 * width), vm(2, width, width), vm(2, width, ff), vm(2, ff, width),
        vm(2, TABLE, width, kind=F32), vm(2, TABLE, width, kind=F32),
        vm(unit, width), vm(2 * unit, 2 * width), vm(4 * unit, 4 * width),
        vm(total, width, kind=F32), vm(2, total, width), vm(2, total, 3 * width), vm(2, slots, HEADS, rows, rows),
        vm(2, total, width),
        vm(2, total, width), vm(2, total, width), vm(total, 6, kind=F32),
        vm(total, ff), vm(total, ff), vm(total, width), vm(total, width), vm(width, total),
    ]
    scratch += [vm(2, 2, n, r, width, kind=kind) for r, kind in tall]
    scratch += [vm(n, r, width, kind=kind) for r, kind in tall]
    plane = rest * rest - 1
    for g, (r, kind) in enumerate(tall):
        direct = g in (ATT, TAB)
        scratch.append(vm(*((plane, first) if direct else (rest - 1, rest * first)), r, width, kind=kind))
    scratch += [vm(2, rest - 1, first, *tall[g][:1], width) for g in (UP, DOWN)]
    scratch += [vm(2, first, r, width, kind=kind) for r, kind in tall]
    scratch += [dma(2, slots), dma(2, 2 * slots), dma(2 * slots), dma(4, slots), dma(4, slots), dma(4, slots)]
    scratch += [dma(4, 2, first), dma(8, first)] + [dma(8, rest - 1)] * 4 + [dma(8, rest)] * 2
    scratch += [dma(8)] * 2 + [dma(8, plane, 2)] * 2 + [dma(8, rest - 1)] * 2 + [dma(8, first), dma(4, 2, first)]
    scratch += [pltpu.SemaphoreType.REGULAR((2, 4))]
    dims = (slots, length, rows, width, ff, head_dim, n)
    vmem = pl.BlockSpec(memory_space=pltpu.VMEM)
    hbm = pl.BlockSpec(memory_space=pltpu.HBM)
    woven, f_a, f_u, f_d, f_t, *_ = pl.pallas_call(
        functools.partial(whole_kernel, dims),
        out_shape=[jax.ShapeDtypeStruct(*o) for o in outs],
        in_specs=[hbm, hbm, pl.BlockSpec(memory_space=pltpu.SMEM)] + [vmem] * 12,
        out_specs=[hbm] + [vmem] * 4 + [hbm] * 3,
        scratch_shapes=scratch,
        compiler_params=pltpu.CompilerParams(
            vmem_limit_bytes=(64 << 20) - (96 << 10), collective_id=0, has_side_effects=True
        ),
    )(
        images.transpose(1, 2, 0, 3), cotangent.transpose(1, 2, 0, 3), counts.T, ln1_gain, ln1_bias, b_out, ln2_gain, ln2_bias, b_down, b_qv, b_up,
        w_qkv, w_out, w_up, w_down,
    )

    params = (
        ln1_gain, ln1_bias, w_qkv, b_qv, w_out, b_out, ln2_gain, ln2_bias, w_up, b_up, w_down, b_down
    )
    acts, ings, *grads = pl.pallas_call(
        output_kernel,
        out_shape=[jax.ShapeDtypeStruct(woven.shape[1:], LOW)] * 2
        + [jax.ShapeDtypeStruct(p.shape, F32) for p in params],
        in_specs=[hbm] * 5,
        out_specs=[hbm] * 2 + [vmem] * len(params),
        scratch_shapes=[
            vm(2, slots, length, 2, width), *[vm(2, r, width, kind=F32) for r, _ in tall], dma(2, 2, slots), dma(4)
        ],
        compiler_params=pltpu.CompilerParams(vmem_limit_bytes=(64 << 20) - (96 << 10)),
    )(woven, f_a, f_u, f_d, f_t)

    def as_given(value):
        return value.transpose(2, 0, 1, 3)[None]

    return (as_given(acts), as_given(ings), *grads)


def solution(mesh):
    split = P("section", "fsdp")
    cube = P("section", "fsdp", None)
    image = P(None, "fsdp", None, None)
    result = P("section", None, "fsdp", None, None)
    params = (split, split, cube, split, cube, split, split, split, cube, split, cube, split)
    return jax.shard_map(
        local,
        mesh=mesh,
        in_specs=(image, image, P(None, "fsdp")) + params,
        out_specs=(result, result) + params,
        check_vma=False,
    )
```

```python
import functools
import math

import jax
import jax.numpy as jnp
from jax import lax
from jax.experimental import pallas as pl
from jax.experimental.pallas import tpu as pltpu
from jax.sharding import PartitionSpec as P

HEADS = 6
EPS = 1e-06
F32 = jnp.float32
LOW = jnp.bfloat16

G1, S1, BO, G2, S2, BD, BQ, BV, BU = 0, 1, 2, 3, 4, 5, 6, 7, 8
TABLE = 16
TOGETHER, TOGETHER_ROWS = 2, 2
ATT, UP, DOWN, TAB = 0, 1, 2, 3


def radices(n):
    rest = max(r for r in range(1, n + 1) if r * r * r <= n and n % (r * r) == 0)
    return n // (rest * rest), rest


def mm(left, right):
    return jnp.dot(left, right, preferred_element_type=F32)


def mm_right(left, right):
    return lax.dot_general(left, right, (((1,), (1,)), ((), ())), preferred_element_type=F32)


def mm_left(left, right):
    return lax.dot_general(left, right, (((0,), (0,)), ((), ())), preferred_element_type=F32)


def normal_parts(pre):
    phi = 0.5 + 0.5 * lax.erf(pre * 0.7071067811865476)
    low = pre.astype(LOW)
    density = jnp.exp2(low * low * LOW(-0.5 * 1.4426950408889634)) * LOW(0.3989422804014327)
    return phi, phi.astype(LOW) + low * density


def normalize(value):
    mean = jnp.mean(value, axis=-1, keepdims=True)
    center = value - mean
    rstd = lax.rsqrt(jnp.mean(center * center, axis=-1, keepdims=True) + EPS)
    return center * rstd, rstd, mean


def normalize_back(d_hat, hat, rstd):
    mean_one = jnp.mean(d_hat, axis=-1, keepdims=True)
    mean_two = jnp.mean(d_hat * hat, axis=-1, keepdims=True)
    return rstd * (d_hat - mean_one - hat * mean_two)


def colsum(value):
    return jnp.sum(value, axis=0, keepdims=True)


def whole_kernel(dims, *refs):
    slots, length, rows, width, ff, head_dim, n = dims
    (
        images, cotangent, counts, v_g1, v_s1, v_bo, v_g2, v_s2, v_bd, v_qv, v_up, a_qkv, a_out, a_up, a_down,
        woven, f_a, f_u, f_d, f_t, hid_far, slope_far, out_far,
        xs, raw, io_one, io_two, pack_a, pack_u, pack_d, pack_t,
        wqkv, wout, wup, wdown, table, gtable, rep_one, rep_two, rep_four,
        after_ref, nrm1, qkv, prob, overs, ctx, hat2, rstds, hid, slope, dal, low_g, left_t,
        s_a, s_u, s_d, s_t, r0_a, r0_u, r0_d, r0_t, r1_a, r1_u, r1_d, r1_t, r2_u, r2_d,
        r3_a, r3_u, r3_d, r3_t,
        in_s, weave_in, weave_out, ship_s, ship_r, far_s, ag1_s, ag1_r, ag2_s, ag2_r, ag3_s, ag3_r, ag4_s, ag4_r,
        rs0_s, rs0_r, rs1_s, rs1_r, rs2_s, rs2_r, rs3_s, rs3_r, credit,
    ) = refs
    groups = (ATT, UP, DOWN, TAB)
    pack = (pack_a, pack_u, pack_d, pack_t)
    stage = (s_a, s_u, s_d, s_t)
    r0, r1, r2 = (r0_a, r0_u, r0_d, r0_t), (r1_a, r1_u, r1_d, r1_t), (None, r2_u, r2_d, None)
    r3, final = (r3_a, r3_u, r3_d, r3_t), (f_a, f_u, f_d, f_t)

    first, rest = radices(n)
    unit = width // n
    core = lax.axis_index("section")
    me = lax.axis_index("fsdp")
    dig_a, dig_b, dig_c = me // (rest * rest), (me // rest) % rest, me % rest
    dig_three, dig_two = dig_c + core * (dig_b - dig_c), dig_b + core * (dig_c - dig_b)
    step_three, step_two = 1 + core * (rest - 1), rest - core * (rest - 1)
    pos = (dig_three * rest + dig_two) * first + dig_a
    pos_of = ((dig_c * rest + dig_b) * first + dig_a, (dig_b * rest + dig_c) * first + dig_a)
    sibling = {"section": 1 - core}

    def place(half, j):
        a, b, c = j // (rest * rest), (j // rest) % rest, j % rest
        return ((c * rest + b) if half == 0 else (b * rest + c)) * first + a

    def peer_first(t):
        return {"fsdp": me + ((dig_a + t) % first - dig_a) * (rest * rest)}

    def peer_two(t):
        return {"fsdp": me + ((dig_two + t) % rest - dig_two) * step_two}

    def peer_three(t):
        return {"fsdp": me + ((dig_three + t) % rest - dig_three) * step_three}

    def peer_plane(three, two):
        here = ((dig_three + three) % rest - dig_three) * step_three
        return {"fsdp": me + here + ((dig_two + two) % rest - dig_two) * step_two}

    plane = [(three, two) for three in range(rest) for two in range(rest) if three or two]

    def remote(src, dst, s_sem, r_sem, device):
        return pltpu.make_async_remote_copy(
            src_ref=src, dst_ref=dst, send_sem=s_sem, recv_sem=r_sem, device_id=device,
            device_id_type=pl.DeviceIdType.MESH,
        )

    def slab_two(three, two):
        return pl.ds((three * rest + two) * first, first)

    def slab_three(three):
        return pl.ds(three * rest * first, rest * first)

    def fill_repeats():
        for ref in (rep_one, rep_two, rep_four):
            part = ref.shape[0]
            lanes = lax.broadcasted_iota(jnp.int32, ref.shape, 1).astype(F32)
            line = lax.broadcasted_iota(jnp.int32, ref.shape, 0).astype(F32)
            rest_of = lanes - part * jnp.floor((lanes + 0.5) * (1.0 / part))
            ref[...] = jnp.where(jnp.abs(rest_of - line) < 0.5, 1.0, 0.0).astype(LOW)

    def own_lanes(part):
        shape = (n, part * n)
        lanes = lax.broadcasted_iota(jnp.int32, shape, 1)
        begin = lax.broadcasted_iota(jnp.int32, shape, 0) * part
        return (lanes >= begin) & (lanes < begin + part)

    shares = (
        ((G1, unit, rep_one), (S1, unit, rep_one), (BO, unit, rep_one), (G2, unit, rep_one), (S2, unit, rep_one),
         (BD, unit, rep_one), (BQ, 2 * unit, rep_two)),
        ((BU, 4 * unit, rep_four),),
    )

    def table_in(b):
        for half in range(2):
            lines = jnp.concatenate([s_t[b, half, place(half, j)] for j in range(n)], axis=0)
            begin = 0
            for row, part, ref in shares[half]:
                spread = mm(lines[:, begin : begin + part].astype(LOW), ref[...])
                line = colsum(jnp.where(own_lanes(part), spread, 0.0))
                for i in range(part * n // width):
                    table[b, row + i : row + i + 1, :] = line[:, width * i : width * (i + 1)]
                begin += part

    def table_out(b):
        for half in range(2):
            parts, begin = [], 0
            for row, part, ref in shares[half]:
                count = part * n // width
                line = jnp.concatenate([gtable[b, row + i : row + i + 1, :] for i in range(count)], axis=1)
                parts.append(mm_right(jnp.where(own_lanes(part), line, 0.0).astype(LOW), ref[...]))
                begin += part
            parts.append(jnp.zeros((n, width - begin), F32))
            lines = jnp.concatenate(parts, axis=1)
            for j in range(n):
                s_t[b, half, place(half, j)] = lines[j : j + 1]

    def pack_own():
        for half in range(2):
            vectors = ((v_g1, v_s1, v_bo, v_g2, v_s2, v_bd, v_qv), (v_up,))[half]
            lines = [vector[...].astype(F32) for vector in vectors]
            lines.append(jnp.zeros((1, width - sum(line.shape[1] for line in lines)), F32))
            pack_t[half] = jnp.concatenate(lines, axis=1)
            for ref in (pack_a, pack_u):
                both = []
                for part in (2 * half, 2 * half + 1):
                    if ref is pack_u:
                        both.append(a_up[0, :, part * width : (part + 1) * width])
                    elif part == 3:
                        both.append(a_out[0])
                    else:
                        both.append(a_qkv[0, :, part * width : (part + 1) * width])
                ref[half] = jnp.concatenate([value.astype(F32) for value in both], axis=0).astype(LOW)
            pack_d[half] = a_down[0, 2 * unit * half : 2 * unit * (half + 1), :]

    def at(b, g):
        return len(groups) * b + g

    def ag1_copy(b, g, half, t):
        device = {"section": half, **peer_first(t)} if t else sibling
        return remote(
            pack[g].at[half], stage[g].at[b, half, pos_of[half]],
            ag1_s.at[g, half, t], ag1_r.at[at(b, g), t], device,
        )

    def ag1_landing(b, g, t):
        ref = stage[g].at[b, core, (dig_three * rest + dig_two) * first + (dig_a + first - t) % first]
        return remote(ref, ref, ag1_s.at[g, 0, t], ag1_r.at[at(b, g), t], sibling)

    def ag2_copy(b, g, t):
        ref = stage[g].at[b, core, slab_two(dig_three, dig_two)]
        return remote(ref, ref, ag2_s.at[at(b, g), t - 1], ag2_r.at[at(b, g), t - 1], peer_two(t))

    def ag3_copy(b, g, t):
        ref = stage[g].at[b, core, slab_three(dig_three)]
        return remote(ref, ref, ag3_s.at[at(b, g), t - 1], ag3_r.at[at(b, g), t - 1], peer_three(t))

    def ag4_copy(b, g, t):
        ref = stage[g].at[b, core, slab_three((dig_three + rest - t) % rest)]
        return remote(ref, ref, ag4_s.at[at(b, g), t], ag4_r.at[at(b, g), t], sibling)

    def ag4_landing(b, g, t):
        ref = stage[g].at[b, 1 - core, slab_three((dig_two + rest - t) % rest)]
        return remote(ref, ref, ag4_s.at[at(b, g), t], ag4_r.at[at(b, g), t], sibling)

    def ag1(b, g):
        @pl.when(core == b)
        def _():
            for t in range(1, first):
                for half in range(2):
                    ag1_copy(b, g, half, t).start()
            ag1_copy(b, g, 1 - b, 0).start()
            stage[g][b, b, pos] = pack[g][b]

    def ag2(b, g):
        for t in range(1, first):
            ag1_landing(b, g, t).wait_recv()

        @pl.when(core != b)
        def _():
            ag1_landing(b, g, 0).wait_recv()

        for t in range(1, rest):
            ag2_copy(b, g, t).start()

    def ag3(b, g):
        for t in range(1, rest):
            ag2_copy(b, g, t).wait_recv()
        for t in range(1, rest):
            ag3_copy(b, g, t).start()
        ag4_copy(b, g, 0).start()

    def ag4(b, g):
        for t in range(1, rest):
            ag3_copy(b, g, t).wait_recv()
            ag4_copy(b, g, t).start()

    def ag5(b, g):
        for t in range(rest):
            ag4_landing(b, g, t).wait_recv()
        lay_out(b, g)

    def ag_sent(b, g):
        @pl.when(core == b)
        def _():
            for t in range(1, first):
                for half in range(2):
                    ag1_copy(b, g, half, t).wait_send()
            ag1_copy(b, g, 1 - b, 0).wait_send()

        for t in range(1, rest):
            ag2_copy(b, g, t).wait_send()
            ag3_copy(b, g, t).wait_send()
        for t in range(rest):
            ag4_copy(b, g, t).wait_send()

    def lay_out(b, g):
        if g == TAB:
            table_in(b)
            return
        if g == DOWN:
            for j in range(n):
                for half in range(2):
                    begin = 4 * unit * j + 2 * unit * half
                    wdown[b, begin : begin + 2 * unit, :] = s_d[b, half, place(half, j)]
            return
        together = 16 // math.gcd(unit, 16)
        for half in range(2):
            for j in range(0, n, together):
                pieces = [stage[g][b, half, place(half, j + i)].astype(F32) for i in range(together)]
                for sub in range(2):
                    low = sub * unit
                    block = jnp.concatenate([piece[low : low + unit] for piece in pieces], axis=0).astype(LOW)
                    part = 2 * half + sub
                    down = slice(unit * j, unit * (j + together))
                    if g == UP:
                        wup[b, down, part * width : (part + 1) * width] = block
                    elif part == 3:
                        wout[b, down, :] = block
                    else:
                        wqkv[b, down, part * width : (part + 1) * width] = block

    def rs0_copy(b, g):
        return remote(stage[g].at[b, 1 - core], r0[g], rs0_s.at[at(b, g)], rs0_r.at[at(b, g)], sibling)

    def rs1_copy(b, g, t):
        return remote(
            stage[g].at[b, core, slab_three((dig_three + t) % rest)], r1[g].at[t - 1],
            rs1_s.at[at(b, g), t - 1, 0], rs1_r.at[at(b, g), t - 1, 0], peer_three(t),
        )

    def rs2_copy(b, g, t):
        return remote(
            stage[g].at[b, core, slab_two(dig_three, (dig_two + t) % rest)], r2[g].at[b, t - 1],
            rs2_s.at[at(b, g), t - 1], rs2_r.at[at(b, g), t - 1], peer_two(t),
        )

    def rs3_copy(b, g, t):
        there = (dig_three * rest + dig_two) * first + (dig_a + t) % first
        device = {"section": b, **peer_first(t)} if t else sibling
        return remote(
            stage[g].at[b, core, there], r3[g].at[core, t], rs3_s.at[at(b, g), t], rs3_r.at[g, core, t], device
        )

    chunk_count = 2 if first % 2 == 0 else 1
    chunk_size = first // chunk_count

    def plane_copy(b, g, t, part):
        three, two = plane[t]
        begin = (((dig_three + three) % rest) * rest + (dig_two + two) % rest) * first + chunk_size * part
        return remote(
            stage[g].at[b, core, pl.ds(begin, chunk_size)], r1[g].at[t, pl.ds(chunk_size * part, chunk_size)],
            rs1_s.at[at(b, g), t, part], rs1_r.at[at(b, g), t, part], peer_plane(three, two),
        )

    def rs0(b, g):
        @pl.when(b == 0)
        def _():
            pl.semaphore_wait(credit.at[0, g], 1)

        rs0_copy(b, g).start()

    def rs1(b, g):
        rs0_copy(b, g).wait_recv()

        @pl.loop(0, n)
        def _(p):
            stage[g][b, core, p] = stage[g][b, core, p] + r0[g][p]

        @pl.when(b == 1)
        def _():
            pl.semaphore_signal(credit.at[0, g], inc=1, device_id=sibling, device_id_type=pl.DeviceIdType.MESH)

        direct = g in (ATT, TAB)
        if rest > 1:
            @pl.when(b == 0)
            def _():
                pl.semaphore_wait(credit.at[1, g], len(plane) if direct else rest - 1)

        if direct:
            for part in range(chunk_count):
                for t in range(len(plane)):
                    plane_copy(b, g, t, part).start()
            return
        for t in range(1, rest):
            rs1_copy(b, g, t).start()

    def rs2(b, g):
        for t in range(1, rest):
            rs1_copy(b, g, t).wait_recv()

        @pl.loop(0, rest * first)
        def _(p):
            here = dig_three * rest * first + p
            total = stage[g][b, core, here].astype(F32)
            for t in range(1, rest):
                total = total + r1[g][t - 1, p].astype(F32)
            stage[g][b, core, here] = total.astype(stage[g].dtype)

        for t in range(1, rest):
            @pl.when(b == 1)
            def _():
                pl.semaphore_signal(
                    credit.at[1, g], inc=1, device_id=peer_three(t), device_id_type=pl.DeviceIdType.MESH
                )

            rs2_copy(b, g, t).start()

    def rs3_send(b, g, part):
        def here(digit):
            return (digit >= chunk_size * part) & (digit < chunk_size * (part + 1))

        for t in range(1, first):
            @pl.when(here((dig_a + t) % first))
            def _():
                rs3_copy(b, g, t).start()

        @pl.when(here(dig_a) & (core != b))
        def _():
            rs3_copy(b, g, 0).start()

    def rs3_part(b, g, part):
        for t in range(len(plane)):
            plane_copy(b, g, t, part).wait_recv()

        @pl.loop(chunk_size * part, chunk_size * (part + 1))
        def _(p):
            here = (dig_three * rest + dig_two) * first + p
            total = stage[g][b, core, here].astype(F32)
            for t in range(len(plane)):
                total = total + r1[g][t, p].astype(F32)
            stage[g][b, core, here] = total.astype(stage[g].dtype)

        rs3_send(b, g, part)

    def rs3_first(b, g):
        rs3_part(b, g, 0)

    def rs3_rest(b, g):
        for part in range(1, chunk_count):
            rs3_part(b, g, part)

    def rs3(b, g):
        if g in (ATT, TAB):
            for part in range(chunk_count):
                rs3_part(b, g, part)

            @pl.when(b == 1)
            def _():
                for three, two in plane:
                    pl.semaphore_signal(
                        credit.at[1, g], inc=1, device_id=peer_plane(three, two),
                        device_id_type=pl.DeviceIdType.MESH,
                    )

            return
        for t in range(1, rest):
            rs2_copy(b, g, t).wait_recv()

        @pl.loop(0, first)
        def _(p):
            here = (dig_three * rest + dig_two) * first + p
            total = stage[g][b, core, here].astype(F32)
            for t in range(1, rest):
                total = total + r2[g][b, t - 1, p].astype(F32)
            stage[g][b, core, here] = total.astype(stage[g].dtype)

        for part in range(chunk_count):
            rs3_send(b, g, part)

    def rs4(b, g):
        @pl.when(core == b)
        def _():
            for own in (True, False):
                half = core if own else 1 - core
                begin = int(own)
                for t in range(begin, first):
                    ref = r3[g].at[half, t]
                    remote(ref, ref, rs3_s.at[at(b, g), t], rs3_r.at[g, half, t], sibling).wait_recv()
                total = stage[g][b, core, pos].astype(F32) if own else None
                for t in range(begin, first):
                    value = r3[g][half, t].astype(F32)
                    total = value if total is None else total + value
                final[g][half] = total

    def rs_sent(b, g):
        rs0_copy(b, g).wait_send()
        if g in (ATT, TAB):
            for part in range(chunk_count):
                for t in range(len(plane)):
                    plane_copy(b, g, t, part).wait_send()
        else:
            for t in range(1, rest):
                rs1_copy(b, g, t).wait_send()
                rs2_copy(b, g, t).wait_send()
        for t in range(1, first):
            rs3_copy(b, g, t).wait_send()

        @pl.when(core != b)
        def _():
            rs3_copy(b, g, 0).wait_send()

    def rows_of(i, images_too=1):
        return pl.ds(pl.multiple_of(i * rows, 16), images_too * rows)

    few = TOGETHER if slots % TOGETHER == 0 else 1
    many = TOGETHER_ROWS if slots % TOGETHER_ROWS == 0 else 1

    def step_rows(i, count):
        return rows_of(i * count, count)

    def ship_parts(kind, b, i):
        src, out = (io_one, io_two)[kind].at[i], out_far.at[kind, core, i]
        q = 2 * kind + b
        near = pltpu.make_async_copy(src, out, ship_s.at[q, i])
        far = remote(src, out, ship_s.at[q, i], ship_r.at[q, i], sibling)
        return near, far

    def ship(kind, b, i):
        near, far = ship_parts(kind, b, i)

        @pl.when(core == b)
        def _():
            near.start()

        @pl.when(core != b)
        def _():
            far.start()

    def shipped(kind, b, i):
        near, far = ship_parts(kind, b, i)

        @pl.when(core == b)
        def _():
            near.wait()

        @pl.when(core != b)
        def _():
            far.wait_send()

    def landed(kind, b, i):
        q = 2 * kind + b
        ref = out_far.at[kind, 1 - core, i]

        @pl.when(core == b)
        def _():
            remote(ref, ref, ship_s.at[q, i], ship_r.at[q, i], sibling).wait_recv()

    def live(i):
        return jnp.where(i < counts[0, core], 1.0, 0.0).astype(F32)

    def only_live(i, value, count):
        parts = [value[rows * m : rows * (m + 1)] * live(i * count + m) for m in range(count)]
        return jnp.concatenate(parts, axis=0)

    def coming(which, i):
        slot = (which * slots + i) % raw.shape[0]
        return pltpu.make_async_copy((images, cotangent)[which].at[i], raw.at[slot], in_s.at[which, i])

    def take_in(which, i):
        coming(which, i).wait()
        both = raw[(which * slots + i) % raw.shape[0]].astype(F32)
        (io_one, io_two)[which][i] = jnp.where(core == 0, both[:, 0, :], both[:, 1, :]).astype(LOW)

    def weave(todo):
        ring = raw.shape[0]
        count = 2 * slots

        def fetch(t, m):
            source = out_far.at[t // slots, m, t % slots]
            return pltpu.make_async_copy(source, io_one.at[2 * (t % ring) + m], weave_in.at[m, t])

        def leave(t):
            return pltpu.make_async_copy(raw.at[t % ring], woven.at[t // slots, t % slots], weave_out.at[t])

        for t in range(ring - 1):
            for m in range(2):
                fetch(t, m).start()

        @pl.loop(0, count)
        def _(t):
            for when, act in todo.items():
                @pl.when(t == when)
                def _():
                    act()

            @pl.when(t + ring - 1 < count)
            def _():
                for m in range(2):
                    fetch(t + ring - 1, m).start()

            @pl.when(t >= ring)
            def _():
                leave(t - ring).wait()

            for m in range(2):
                fetch(t, m).wait()
                raw[t % ring, :, m, :] = io_one[2 * (t % ring) + m]
            leave(t).start()

        for t in range(count - ring, count):
            leave(t).wait()

    def far_copy(which, i, back):
        near, far = ((hid, hid_far), (slope, slope_far))[which]
        near, far = near.at[rows_of(i)], far.at[rows_of(i)]
        src, dst = (far, near) if back else (near, far)
        return pltpu.make_async_copy(src, dst, far_s.at[2 * int(back) + which, i])

    pairs = width // 128
    scale = head_dim ** -0.5
    lane = lax.broadcasted_iota(jnp.int32, (1, 128), 1)
    half_low = [(lane < head_dim).astype(LOW), (lane >= head_dim).astype(LOW)]
    half_f = [(lane < head_dim).astype(F32), (lane >= head_dim).astype(F32)]
    token = lax.broadcasted_iota(jnp.int32, (rows, 128), 0) < length
    half_valid = [jnp.where(token, half_f[j], 0.0).astype(LOW) for j in range(2)]
    valid_lanes = jnp.where(lax.broadcasted_iota(jnp.int32, (1, rows), 1) < length, 1.0, 0.0).astype(F32)
    spare = -rows % 128
    chunk = 2 * width
    chunks = ff // chunk

    def vec(s, r):
        return table[s, r : r + 1, :]

    def up_bias(s, c):
        begin = c * chunk
        row, col = begin // width, begin % width
        if col + chunk <= width:
            return table[s, BU + row : BU + row + 1, col : col + chunk]
        a = table[s, BU + row : BU + row + 1, col:width]
        b = table[s, BU + row + 1 : BU + row + 2, 0 : chunk - (width - col)]
        return jnp.concatenate([a, b], axis=1)

    def add_vec(s, r, value):
        gtable[s, r : r + 1, :] += value

    def attn_forward(s, x, hat, i):
        rd = step_rows(i, few)
        nrm_ref, qkv_ref, prob_ref, ctx_ref = nrm1.at[s], qkv.at[s], prob.at[s], ctx.at[s]
        nrm = (hat * vec(s, G1) + vec(s, S1)).astype(LOW)
        nrm_ref[rd, :] = nrm
        mixed = mm(nrm, wqkv[s])
        q = (mixed[:, 0:width] + vec(s, BQ)).astype(LOW)
        k = mixed[:, width : 2 * width].astype(LOW)
        v = (mixed[:, 2 * width :] + vec(s, BV)).astype(LOW)
        qkv_ref[rd, 0:width] = q
        qkv_ref[rd, width : 2 * width] = k
        qkv_ref[rd, 2 * width :] = v
        images_out = []
        for m in range(few):
            mine = slice(rows * m, rows * (m + 1))
            parts = []
            for p in range(pairs):
                cols = slice(128 * p, 128 * p + 128)
                weights, sides = [], []
                for j in range(2):
                    keys = k[mine, cols] * half_low[j]
                    keys = jnp.concatenate([keys, keys[rows - spare :]], axis=0)
                    scores = mm_right(q[mine, cols], keys)
                    top = jnp.max(scores, axis=-1, keepdims=True)
                    e = jnp.exp2((scores - top) * (scale * 1.4426950408889634)).astype(LOW)
                    prob_ref[i * few + m, 2 * p + j] = e[:, :rows]
                    weights.append(e)
                    sides.append(jnp.concatenate([v[mine, cols] * half_valid[j], half_valid[j]], axis=1))
                    sides.append(jnp.zeros((spare, 256), LOW))
                total = mm(jnp.concatenate(weights, axis=1), jnp.concatenate(sides, axis=0))
                over = 1.0 / total[:, 128:]
                overs[s, rows_of(i * few + m), cols] = over.astype(LOW)
                parts.append((total[:, :128] * over).astype(LOW))
            images_out.append(jnp.concatenate(parts, axis=1))
        context = jnp.concatenate(images_out, axis=0)
        ctx_ref[rd, :] = context
        return x + mm(context, wout[s]) + vec(s, BO)

    def ff_forward(s, after, rd):
        hat, rstd, _ = normalize(after)
        hat2[s, rd, :] = hat.astype(LOW)
        nrm = (hat * vec(s, G2) + vec(s, S2)).astype(LOW)
        total = after + vec(s, BD)
        for c in range(chunks):
            cols = slice(chunk * c, chunk * c + chunk)
            pre = mm(nrm, wup[s, :, cols]) + up_bias(s, c)
            phi, slo = normal_parts(pre)
            h = (pre * phi).astype(LOW)
            hid[rd, cols] = h
            slope[rd, cols] = slo.astype(LOW)
            total = total + mm(h, wdown[s, cols, :])
        return total, rstd

    def ff_backward(s, g, rd, rstd):
        g_low = g.astype(LOW)
        add_vec(s, BD, colsum(g_low.astype(F32)))
        d_nrm = None
        for c in range(chunks):
            cols = slice(chunk * c, chunk * c + chunk)
            d_hid = mm_right(g_low, wdown[s, cols, :])
            d_pre = (d_hid * slope[rd, cols].astype(F32)).astype(LOW)
            slope[rd, cols] = d_pre
            part = mm_right(d_pre, wup[s, :, cols])
            d_nrm = part if d_nrm is None else d_nrm + part
        hat = hat2[s, rd, :].astype(F32)
        add_vec(s, G2, colsum(d_nrm * hat))
        add_vec(s, S2, colsum(d_nrm))
        d_after = g + normalize_back(d_nrm * vec(s, G2), hat, rstd)
        low = d_after.astype(LOW)
        dal[rd, :] = low
        return d_after

    def attn_backward(s, i):
        qkv_ref, prob_ref, ctx_ref = qkv.at[s], prob.at[s], ctx.at[s]
        rd = step_rows(i, few)
        d_context = mm_right(dal[rd, :], wout[s])
        d_context = (d_context * overs[s, rd, :].astype(F32)).astype(LOW)
        for m in range(few):
            rd = rows_of(i * few + m)
            d_ctx = d_context[rows * m : rows * (m + 1)]
            dq, dk, dv = [], [], []
            for p in range(pairs):
                cols = slice(128 * p, 128 * p + 128)
                q = qkv_ref[rd, 128 * p : 128 * p + 128]
                k = qkv_ref[rd, width + 128 * p : width + 128 * p + 128]
                v = qkv_ref[rd, 2 * width + 128 * p : 2 * width + 128 * p + 128]
                dc = d_ctx[:, cols]
                both = dc.astype(F32) * ctx_ref[rd, cols].astype(F32)
                q_t, dc_t = q.T, dc.T
                to_q, to_k, to_v = None, [], []
                for j in range(2):
                    e = prob_ref[i * few + m, 2 * p + j]
                    delta = jnp.sum(both * half_f[j], axis=-1, keepdims=True)
                    d_prob = mm_right(dc, v * half_low[j])
                    ds = (e.astype(F32) * (d_prob - delta)).astype(LOW)
                    part = mm(ds, k * half_valid[j])
                    to_q = part if to_q is None else to_q + part
                    head = slice(head_dim * j, head_dim * (j + 1))
                    to_k.append(mm(q_t[head], ds))
                    to_v.append(mm(dc_t[head], e))
                dq.append((to_q * scale).astype(LOW))
                dk.append((jnp.concatenate(to_k, axis=0) * (valid_lanes * scale)).astype(LOW).T)
                dv.append((jnp.concatenate(to_v, axis=0) * valid_lanes).astype(LOW).T)
            d_mixed = jnp.concatenate(dq + dk + dv, axis=1)
            qkv_ref[rd, :] = d_mixed

    def input_backward(s, d_after, rd, x, mean, rstd):
        d_nrm = mm_right(qkv[s, rd, :], wqkv[s])
        hat = (x - mean) * rstd
        add_vec(s, G1, colsum(d_nrm * hat))
        add_vec(s, S1, colsum(d_nrm))
        return d_after + normalize_back(d_nrm * vec(s, G1), hat, rstd)

    def grads_down(s):
        left_t[0:width, :] = low_g[...].T

        @pl.loop(0, 2)
        def _(c):
            cols = pl.ds(pl.multiple_of(c * 2 * width, 128), 2 * width)
            block = mm(left_t[0:width, :], hid[:, cols]).T
            for i in range(n // 2):
                for half in range(2):
                    begin = 4 * unit * i + 2 * unit * half
                    s_d[s, half, place(half, c * (n // 2) + i)] = block[begin : begin + 2 * unit].astype(LOW)

    def pair_out(ref, s, half, one, two):
        for j in range(n):
            down = slice(unit * j, unit * (j + 1))
            piece = jnp.concatenate([one[down], two[down]], axis=0).astype(LOW)
            ref[s, half, place(half, j)] = piece

    def grads_up(s):
        left_t[0:width, :] = (hat2[s].astype(F32) * vec(s, G2) + vec(s, S2)).astype(LOW).T
        for half in range(2):
            both = mm(left_t[...], slope[:, 2 * half * width : 2 * (half + 1) * width])
            pair_out(s_u, s, half, both[:, :width], both[:, width:])
            gtable[s, BU + 2 * half : BU + 2 * half + 1, :] = both[width : width + 1, :width]
            gtable[s, BU + 2 * half + 1 : BU + 2 * half + 2, :] = both[width : width + 1, width:]

    def grads_attn(s):
        mix_s = qkv.at[s]
        left_t[0:width, :] = ctx[s].T
        four = mm(left_t[...], dal[...])
        left_t[0:width, :] = nrm1[s].T
        three = mm(left_t[...], mix_s[:, 2 * width :])
        pair_out(s_a, s, 1, three, four)
        both = mm(left_t[...], mix_s[:, 0 : 2 * width])
        pair_out(s_a, s, 0, both[:, :width], both[:, width:])
        for row, sums in ((BO, four), (BV, three), (BQ, both)):
            gtable[s, row : row + 1, :] = sums[width : width + 1, :width]

    barrier = pltpu.get_barrier_semaphore()
    greeted = [sibling]
    greeted += [{"section": half, **peer_first(t)} for t in range(1, first) for half in range(2)]
    greeted += [peer_plane(three, two) for three, two in plane]
    for device in greeted:
        pl.semaphore_signal(barrier, inc=1, device_id=device, device_id_type=pl.DeviceIdType.MESH)
    pack_own()
    pl.semaphore_wait(barrier, len(greeted))

    def run(*todo):
        for f, b, g in todo:
            f(b, g)

    def events(i, table_of):
        for when, todo in table_of.items():
            @pl.when(i == when)
            def _():
                run(*todo)

    def both(f, b, g):
        return [(f, b, g), (f, b, TAB)]

    def take(i, m):
        return pl.ds(pl.multiple_of((i * many + m) * rows, 16), length)

    ahead = raw.shape[0]
    run(*both(ag1, 0, ATT))
    for i in range(ahead):
        coming(0, i).start()
    fill_repeats()
    gtable[...] = jnp.zeros_like(gtable)
    left_t[width:, :] = jnp.ones((16, left_t.shape[1]), LOW)
    low_g[...] = jnp.zeros_like(low_g)
    xs[0] = jnp.zeros_like(low_g)

    @pl.loop(0, slots)
    def images_in(i):
        take_in(0, i)

        @pl.when(i + ahead < slots)
        def _():
            coming(0, i + ahead).start()

        @pl.when(i + ahead >= slots)
        def _():
            coming(1, i + ahead - slots).start()

        @pl.when(i == 4)
        def _():
            run((ag1, 0, UP))

    run(*both(ag2, 0, ATT), (ag1, 0, DOWN), *both(ag1, 1, ATT))

    def statistic(s, rd, which):
        return jnp.where(s == 0, rstds[rd, which : which + 1], rstds[rd, 3 + which : 4 + which])

    def first_norm(s, rd, x):
        hat, rstd, mean = normalize(x)
        after_ref[rd, :] = hat
        rstds[rd, 3 * s : 3 * s + 1] = rstd
        rstds[rd, 3 * s + 2 : 3 * s + 3] = mean

    @pl.loop(0, slots // many)
    def norm_one(i):
        for m in range(many):
            xs[0, take(i, m), :] = io_one[i * many + m]
        rd = step_rows(i, many)
        x = xs[0, rd, :].astype(F32)
        token_rows = lax.broadcasted_iota(jnp.int32, (rows, width), 0) < length
        parts = [x[rows * m : rows * (m + 1)] for m in range(many)]
        x = jnp.concatenate([jnp.where(token_rows, part, part[0:1]) for part in parts], axis=0)
        xs[0, rd, :] = x.astype(LOW)
        first_norm(0, rd, x)

    run((ag2, 0, UP), *both(ag3, 0, ATT), (ag1, 1, UP), (ag1, 1, DOWN), (ag2, 0, DOWN), (ag3, 0, UP))

    @pl.loop(0, slots)
    def cotangents_in(i):
        take_in(1, i)

        @pl.when(i + ahead < slots)
        def _():
            coming(1, i + ahead).start()

    run(*both(ag4, 0, ATT), (ag3, 0, DOWN), *both(ag2, 1, ATT), *both(ag5, 0, ATT))

    @pl.loop(0, 2)
    def forward(s):
        @pl.loop(0, slots // few)
        def attention(i):
            @pl.when(s == 0)
            def _():
                events(i, {1: [(ag4, 0, UP), (ag2, 1, UP)], 2: [(ag4, 0, DOWN)]})

            @pl.when(s == 1)
            def _():
                events(i, {1: [(ag4, 1, UP)], 2: [(ag4, 1, DOWN)]})

            rd = step_rows(i, few)
            after_ref[rd, :] = attn_forward(s, xs[s, rd, :].astype(F32), after_ref[rd, :], i)

        @pl.when(s == 0)
        def _():
            run(*both(ag3, 1, ATT), (ag5, 0, UP), (ag5, 0, DOWN))

        @pl.when(s == 1)
        def _():
            run((ag5, 1, UP), (ag5, 1, DOWN))

        @pl.loop(0, slots // many)
        def feed_forward(i):
            @pl.when(s == 0)
            def _():
                events(i, {0: [(ag2, 1, DOWN), (ag3, 1, UP)], 2: both(ag4, 1, ATT)})

            rd = step_rows(i, many)

            @pl.when(s == 1)
            def _():
                for m in range(many):
                    far_copy(0, i * many + m, False).wait()
                    far_copy(1, i * many + m, False).wait()
                    shipped(0, 0, i * many + m)

            out, rstd2 = ff_forward(s, after_ref[rd, :], rd)
            for block in range(2):
                @pl.when(s == block)
                def _():
                    rstds[rd, 3 * block + 1 : 3 * block + 2] = rstd2

            out = only_live(i, out, many)
            for m in range(many):
                io_one[i * many + m] = out[rows * m : rows * m + length].astype(LOW)
                ship(0, s, i * many + m)

            @pl.when(s == 0)
            def _():
                for m in range(many):
                    far_copy(0, i * many + m, False).start()
                    far_copy(1, i * many + m, False).start()
                low = out.astype(LOW)
                xs[1, rd, :] = low
                first_norm(1, rd, low.astype(F32))

        @pl.when(s == 0)
        def _():
            run((ag3, 1, DOWN), *both(ag5, 1, ATT))

    for b in range(2):
        for g in groups:
            ag_sent(b, g)

    @pl.loop(0, 2)
    def backward(turn):
        s = 1 - turn

        @pl.when(s == 0)
        def _():
            run((rs3, 1, DOWN))

        @pl.loop(0, slots // many)
        def feed_forward(i):
            @pl.when(s == 0)
            def _():
                events(i, {1: [*both(rs1, 1, ATT), (rs3, 1, UP)]})
                for m in range(many):
                    far_copy(1, i * many + m, True).wait()

            rd = step_rows(i, many)
            for m in range(many):
                g = live(i * many + m) * io_two[i * many + m].astype(F32)
                low_g[take(i, m), :] = g.astype(LOW)
            after_ref[rd, :] = ff_backward(s, low_g[rd, :].astype(F32), rd, statistic(s, rd, 1))

        @pl.when(s == 0)
        def _():
            for i in range(slots):
                far_copy(0, i, True).wait()

        grads_down(s)
        run((rs0, s, DOWN))

        @pl.when(s == 1)
        def _():
            for i in range(slots):
                far_copy(0, i, True).start()

        grads_up(s)
        run((rs0, s, UP))

        @pl.when(s == 1)
        def _():
            for i in range(slots):
                far_copy(1, i, True).start()

        @pl.when(s == 0)
        def _():
            run((rs4, 1, DOWN), (rs4, 1, UP))

        @pl.loop(0, slots // few)
        def attention(i):
            @pl.when(s == 0)
            def _():
                events(i, {1: both(rs3, 1, ATT)})

            events(i, {1: [(rs1, s, DOWN), (rs1, s, UP)]})
            attn_backward(s, i)

        run((rs2, s, DOWN))

        @pl.when(s == 0)
        def _():
            run(*both(rs4, 1, ATT))

        grads_attn(s)
        run((rs0, s, ATT), (rs2, s, UP))

        @pl.loop(0, slots // many)
        def to_input(i):
            rd = step_rows(i, many)
            x = xs[s, rd, :].astype(F32)
            d_in = input_backward(s, after_ref[rd, :], rd, x, statistic(s, rd, 2), statistic(s, rd, 0))
            for m in range(many):
                @pl.when(s == 0)
                def _():
                    shipped(1, 1, i * many + m)

                io_two[i * many + m] = d_in[rows * m : rows * m + length].astype(LOW)
                ship(1, s, i * many + m)

        table_out(s)
        run((rs0, s, TAB))

    def sent_and_landed(kind):
        @pl.loop(0, slots)
        def _(i):
            shipped(kind, 1 - kind, i)
            for b in range(2):
                landed(kind, b, i)

    sent_and_landed(0)
    weave({
        1: lambda: run(*both(rs1, 0, ATT), (rs3, 0, DOWN), (rs3, 0, UP)),
        slots - raw.shape[0] + 1: lambda: sent_and_landed(1),
        slots: lambda: run(*both(rs3_first, 0, ATT)),
        slots + 3: lambda: run(*both(rs3_rest, 0, ATT), (rs4, 0, DOWN), (rs4, 0, UP)),
    })
    run(*both(rs4, 0, ATT))
    for b in range(2):
        for g in groups:
            rs_sent(b, g)


def output_kernel(
    woven, far_a, far_u, far_d, far_t, o_acts, o_ings, o_g1, o_s1, o_qkv, o_qv, o_out, o_bo, o_g2, o_s2, o_up, o_bu, o_down, o_bd,
    passing, f_a, f_u, f_d, f_t, sems, grad_sems
):
    coming = [
        pltpu.make_async_copy(source, target, grad_sems.at[i])
        for i, (source, target) in enumerate(((far_a, f_a), (far_u, f_u), (far_d, f_d), (far_t, f_t)))
    ]
    for copy in coming:
        copy.start()
    arriving, leaving = [], []
    for which, target in enumerate((o_acts, o_ings)):
        for i in range(target.shape[0]):
            arriving.append(pltpu.make_async_copy(woven.at[which, i], passing.at[which, i], sems.at[0, which, i]))
            leaving.append(pltpu.make_async_copy(passing.at[which, i], target.at[i], sems.at[1, which, i]))
    for copy in arriving:
        copy.start()
    for one, two in zip(arriving, leaving):
        one.wait()
        two.start()
    for copy in coming:
        copy.wait()
    unit, width = o_out.shape[1:]
    for half in range(2):
        o_down[0, 2 * unit * half : 2 * unit * (half + 1), :] = f_d[half]
        for sub in range(2):
            part = 2 * half + sub
            cols = slice(part * width, (part + 1) * width)
            o_up[0, :, cols] = f_u[half, unit * sub : unit * (sub + 1), :]
            piece = f_a[half, unit * sub : unit * (sub + 1), :]
            if part == 3:
                o_out[0] = piece
            else:
                o_qkv[0, :, cols] = piece
    begin = 0
    for out in (o_g1, o_s1, o_bo, o_g2, o_s2, o_bd, o_qv):
        part = out.shape[1]
        out[...] = f_t[0, :, begin : begin + part]
        begin += part
    o_bu[...] = f_t[1, :, 0 : o_bu.shape[1]]
    for copy in leaving:
        copy.wait()


def local(
    images, cotangent, counts,
    ln1_gain, ln1_bias, w_qkv, b_qv, w_out, b_out, ln2_gain, ln2_bias, w_up, b_up, w_down, b_down,
):
    micro_count, slots, length, width = images.shape
    ff = w_up.shape[2]
    rows = -(-length // 16) * 16
    n = lax.axis_size("fsdp")
    unit = width // n
    first, rest = radices(n)
    total = slots * rows
    head_dim = width // HEADS

    def vm(*shape, kind=LOW):
        return pltpu.VMEM(shape, kind)

    tall = [(2 * unit, LOW)] * 3 + [(1, F32)]
    dma = lambda *shape: pltpu.SemaphoreType.DMA(shape)
    outs = [((2, slots, length, 2, width), LOW)]
    outs += [((2, r, width), F32) for r, _ in tall] + [((total, ff), LOW)] * 2 + [((2, 2, slots, length, width), LOW)]
    scratch = [
        vm(2, total, width), vm(3, length, 2, width), vm(slots, length, width), vm(slots, length, width),
        *[vm(2, r, width, kind=kind) for r, kind in tall],
        vm(2, width, 3 * width), vm(2, width, width), vm(2, width, ff), vm(2, ff, width),
        vm(2, TABLE, width, kind=F32), vm(2, TABLE, width, kind=F32),
        vm(unit, width), vm(2 * unit, 2 * width), vm(4 * unit, 4 * width),
        vm(total, width, kind=F32), vm(2, total, width), vm(2, total, 3 * width), vm(2, slots, HEADS, rows, rows),
        vm(2, total, width),
        vm(2, total, width), vm(2, total, width), vm(total, 6, kind=F32),
        vm(total, ff), vm(total, ff), vm(total, width), vm(total, width), vm(width + 16, total),
    ]
    scratch += [vm(2, 2, n, r, width, kind=kind) for r, kind in tall]
    scratch += [vm(n, r, width, kind=kind) for r, kind in tall]
    plane = rest * rest - 1
    for g, (r, kind) in enumerate(tall):
        direct = g in (ATT, TAB)
        scratch.append(vm(*((plane, first) if direct else (rest - 1, rest * first)), r, width, kind=kind))
    scratch += [vm(2, rest - 1, first, *tall[g][:1], width) for g in (UP, DOWN)]
    scratch += [vm(2, first, r, width, kind=kind) for r, kind in tall]
    scratch += [dma(2, slots), dma(2, 2 * slots), dma(2 * slots), dma(4, slots), dma(4, slots), dma(4, slots)]
    scratch += [dma(4, 2, first), dma(8, first)] + [dma(8, rest - 1)] * 4 + [dma(8, rest)] * 2
    scratch += [dma(8)] * 2 + [dma(8, plane, 2)] * 2 + [dma(8, rest - 1)] * 2 + [dma(8, first), dma(4, 2, first)]
    scratch += [pltpu.SemaphoreType.REGULAR((2, 4))]
    dims = (slots, length, rows, width, ff, head_dim, n)
    vmem = pl.BlockSpec(memory_space=pltpu.VMEM)
    hbm = pl.BlockSpec(memory_space=pltpu.HBM)
    woven, f_a, f_u, f_d, f_t, *_ = pl.pallas_call(
        functools.partial(whole_kernel, dims),
        out_shape=[jax.ShapeDtypeStruct(*o) for o in outs],
        in_specs=[hbm, hbm, pl.BlockSpec(memory_space=pltpu.SMEM)] + [vmem] * 12,
        out_specs=[hbm] + [vmem] * 4 + [hbm] * 3,
        scratch_shapes=scratch,
        compiler_params=pltpu.CompilerParams(
            vmem_limit_bytes=(64 << 20) - (96 << 10), collective_id=0, has_side_effects=True
        ),
    )(
        images.transpose(1, 2, 0, 3), cotangent.transpose(1, 2, 0, 3), counts.T, ln1_gain, ln1_bias, b_out, ln2_gain, ln2_bias, b_down, b_qv, b_up,
        w_qkv, w_out, w_up, w_down,
    )

    params = (
        ln1_gain, ln1_bias, w_qkv, b_qv, w_out, b_out, ln2_gain, ln2_bias, w_up, b_up, w_down, b_down
    )
    acts, ings, *grads = pl.pallas_call(
        output_kernel,
        out_shape=[jax.ShapeDtypeStruct(woven.shape[1:], LOW)] * 2
        + [jax.ShapeDtypeStruct(p.shape, F32) for p in params],
        in_specs=[hbm] * 5,
        out_specs=[hbm] * 2 + [vmem] * len(params),
        scratch_shapes=[
            vm(2, slots, length, 2, width), *[vm(2, r, width, kind=F32) for r, _ in tall], dma(2, 2, slots), dma(4)
        ],
        compiler_params=pltpu.CompilerParams(vmem_limit_bytes=(64 << 20) - (96 << 10)),
    )(woven, f_a, f_u, f_d, f_t)

    def as_given(value):
        return value.transpose(2, 0, 1, 3)[None]

    return (as_given(acts), as_given(ings), *grads)


def solution(mesh):
    split = P("section", "fsdp")
    cube = P("section", "fsdp", None)
    image = P(None, "fsdp", None, None)
    result = P("section", None, "fsdp", None, None)
    params = (split, split, cube, split, cube, split, split, split, cube, split, cube, split)
    return jax.shard_map(
        local,
        mesh=mesh,
        in_specs=(image, image, P(None, "fsdp")) + params,
        out_specs=(result, result) + params,
        check_vma=False,
    )
```

```python
import functools
import math

import jax
import jax.numpy as jnp
from jax import lax
from jax.experimental import pallas as pl
from jax.experimental.pallas import tpu as pltpu
from jax.sharding import PartitionSpec as P

HEADS = 6
EPS = 1e-06
F32 = jnp.float32
LOW = jnp.bfloat16

G1, S1, BO, G2, S2, BD, BQ, BV, BU = 0, 1, 2, 3, 4, 5, 6, 7, 8
TABLE = 16
TOGETHER, TOGETHER_ROWS = 2, 2
ATT, UP, DOWN, TAB = 0, 1, 2, 3


def radices(n):
    rest = max(r for r in range(1, n + 1) if r * r * r <= n and n % (r * r) == 0)
    return n // (rest * rest), rest


def mm(left, right):
    return jnp.dot(left, right, preferred_element_type=F32)


def mm_right(left, right):
    return lax.dot_general(left, right, (((1,), (1,)), ((), ())), preferred_element_type=F32)


def mm_left(left, right):
    return lax.dot_general(left, right, (((0,), (0,)), ((), ())), preferred_element_type=F32)


def normal_parts(pre):
    phi = 0.5 + 0.5 * lax.erf(pre * 0.7071067811865476)
    low = pre.astype(LOW)
    density = jnp.exp2(low * low * LOW(-0.5 * 1.4426950408889634)) * LOW(0.3989422804014327)
    return phi, phi.astype(LOW) + low * density


def normalize(value):
    mean = jnp.mean(value, axis=-1, keepdims=True)
    center = value - mean
    rstd = lax.rsqrt(jnp.mean(center * center, axis=-1, keepdims=True) + EPS)
    return center * rstd, rstd, mean


def normalize_back(d_hat, hat, rstd):
    mean_one = jnp.mean(d_hat, axis=-1, keepdims=True)
    mean_two = jnp.mean(d_hat * hat, axis=-1, keepdims=True)
    return rstd * (d_hat - mean_one - hat * mean_two)


def colsum(value):
    return jnp.sum(value, axis=0, keepdims=True)


def whole_kernel(dims, *refs):
    slots, length, rows, width, ff, head_dim, n = dims
    (
        images, cotangent, counts, v_g1, v_s1, v_bo, v_g2, v_s2, v_bd, v_qv, v_up, a_qkv, a_out, a_up, a_down,
        woven, f_a, f_u, f_d, f_t, hid_far, slope_far, out_far,
        xs, raw, io_one, io_two, pack_a, pack_u, pack_d, pack_t,
        wqkv, wout, wup, wdown, table, gtable, rep_one, rep_two, rep_four,
        after_ref, nrm1, qkv, prob, overs, ctx, hat2, rstds, hid, slope, dal, low_g, left_t,
        s_a, s_u, s_d, s_t, r0_a, r0_u, r0_d, r0_t, r1_a, r1_u, r1_d, r1_t, r2_u, r2_d,
        r3_a, r3_u, r3_d, r3_t,
        in_s, weave_in, weave_out, ship_s, ship_r, far_s, ag1_s, ag1_r, ag2_s, ag2_r, ag3_s, ag3_r, ag4_s, ag4_r,
        rs0_s, rs0_r, rs1_s, rs1_r, rs2_s, rs2_r, rs3_s, rs3_r, credit,
    ) = refs
    groups = (ATT, UP, DOWN, TAB)
    pack = (pack_a, pack_u, pack_d, pack_t)
    stage = (s_a, s_u, s_d, s_t)
    r0, r1, r2 = (r0_a, r0_u, r0_d, r0_t), (r1_a, r1_u, r1_d, r1_t), (None, r2_u, r2_d, None)
    r3, final = (r3_a, r3_u, r3_d, r3_t), (f_a, f_u, f_d, f_t)

    first, rest = radices(n)
    unit = width // n
    core = lax.axis_index("section")
    me = lax.axis_index("fsdp")
    dig_a, dig_b, dig_c = me // (rest * rest), (me // rest) % rest, me % rest
    dig_three, dig_two = dig_c + core * (dig_b - dig_c), dig_b + core * (dig_c - dig_b)
    step_three, step_two = 1 + core * (rest - 1), rest - core * (rest - 1)
    pos = (dig_three * rest + dig_two) * first + dig_a
    pos_of = ((dig_c * rest + dig_b) * first + dig_a, (dig_b * rest + dig_c) * first + dig_a)
    sibling = {"section": 1 - core}

    def place(half, j):
        a, b, c = j // (rest * rest), (j // rest) % rest, j % rest
        return ((c * rest + b) if half == 0 else (b * rest + c)) * first + a

    def peer_first(t):
        return {"fsdp": me + ((dig_a + t) % first - dig_a) * (rest * rest)}

    def peer_two(t):
        return {"fsdp": me + ((dig_two + t) % rest - dig_two) * step_two}

    def peer_three(t):
        return {"fsdp": me + ((dig_three + t) % rest - dig_three) * step_three}

    def peer_plane(three, two):
        here = ((dig_three + three) % rest - dig_three) * step_three
        return {"fsdp": me + here + ((dig_two + two) % rest - dig_two) * step_two}

    plane = [(three, two) for three in range(rest) for two in range(rest) if three or two]

    def remote(src, dst, s_sem, r_sem, device):
        return pltpu.make_async_remote_copy(
            src_ref=src, dst_ref=dst, send_sem=s_sem, recv_sem=r_sem, device_id=device,
            device_id_type=pl.DeviceIdType.MESH,
        )

    def slab_two(three, two):
        return pl.ds((three * rest + two) * first, first)

    def slab_three(three):
        return pl.ds(three * rest * first, rest * first)

    def fill_repeats():
        for ref in (rep_one, rep_two, rep_four):
            part = ref.shape[0]
            lanes = lax.broadcasted_iota(jnp.int32, ref.shape, 1).astype(F32)
            line = lax.broadcasted_iota(jnp.int32, ref.shape, 0).astype(F32)
            rest_of = lanes - part * jnp.floor((lanes + 0.5) * (1.0 / part))
            ref[...] = jnp.where(jnp.abs(rest_of - line) < 0.5, 1.0, 0.0).astype(LOW)

    def own_lanes(part):
        shape = (n, part * n)
        lanes = lax.broadcasted_iota(jnp.int32, shape, 1)
        begin = lax.broadcasted_iota(jnp.int32, shape, 0) * part
        return (lanes >= begin) & (lanes < begin + part)

    shares = (
        ((G1, unit, rep_one), (S1, unit, rep_one), (BO, unit, rep_one), (G2, unit, rep_one), (S2, unit, rep_one),
         (BD, unit, rep_one), (BQ, 2 * unit, rep_two)),
        ((BU, 4 * unit, rep_four),),
    )

    def table_in(b):
        for half in range(2):
            lines = jnp.concatenate([s_t[b, half, place(half, j)] for j in range(n)], axis=0)
            begin = 0
            for row, part, ref in shares[half]:
                spread = mm(lines[:, begin : begin + part].astype(LOW), ref[...])
                line = colsum(jnp.where(own_lanes(part), spread, 0.0))
                for i in range(part * n // width):
                    table[b, row + i : row + i + 1, :] = line[:, width * i : width * (i + 1)]
                begin += part

    def table_out(b):
        for half in range(2):
            parts, begin = [], 0
            for row, part, ref in shares[half]:
                count = part * n // width
                line = jnp.concatenate([gtable[b, row + i : row + i + 1, :] for i in range(count)], axis=1)
                parts.append(mm_right(jnp.where(own_lanes(part), line, 0.0).astype(LOW), ref[...]))
                begin += part
            parts.append(jnp.zeros((n, width - begin), F32))
            lines = jnp.concatenate(parts, axis=1)
            for j in range(n):
                s_t[b, half, place(half, j)] = lines[j : j + 1]

    def pack_own():
        for half in range(2):
            vectors = ((v_g1, v_s1, v_bo, v_g2, v_s2, v_bd, v_qv), (v_up,))[half]
            lines = [vector[...].astype(F32) for vector in vectors]
            lines.append(jnp.zeros((1, width - sum(line.shape[1] for line in lines)), F32))
            pack_t[half] = jnp.concatenate(lines, axis=1)
            for ref in (pack_a, pack_u):
                both = []
                for part in (2 * half, 2 * half + 1):
                    if ref is pack_u:
                        both.append(a_up[0, :, part * width : (part + 1) * width])
                    elif part == 3:
                        both.append(a_out[0])
                    else:
                        both.append(a_qkv[0, :, part * width : (part + 1) * width])
                ref[half] = jnp.concatenate([value.astype(F32) for value in both], axis=0).astype(LOW)
            pack_d[half] = a_down[0, 2 * unit * half : 2 * unit * (half + 1), :]

    def at(b, g):
        return len(groups) * b + g

    def ag1_copy(b, g, half, t):
        device = {"section": half, **peer_first(t)} if t else sibling
        return remote(
            pack[g].at[half], stage[g].at[b, half, pos_of[half]],
            ag1_s.at[g, half, t], ag1_r.at[at(b, g), t], device,
        )

    def ag1_landing(b, g, t):
        ref = stage[g].at[b, core, (dig_three * rest + dig_two) * first + (dig_a + first - t) % first]
        return remote(ref, ref, ag1_s.at[g, 0, t], ag1_r.at[at(b, g), t], sibling)

    def ag2_copy(b, g, t):
        ref = stage[g].at[b, core, slab_two(dig_three, dig_two)]
        return remote(ref, ref, ag2_s.at[at(b, g), t - 1], ag2_r.at[at(b, g), t - 1], peer_two(t))

    def ag3_copy(b, g, t):
        ref = stage[g].at[b, core, slab_three(dig_three)]
        return remote(ref, ref, ag3_s.at[at(b, g), t - 1], ag3_r.at[at(b, g), t - 1], peer_three(t))

    def ag4_copy(b, g, t):
        ref = stage[g].at[b, core, slab_three((dig_three + rest - t) % rest)]
        return remote(ref, ref, ag4_s.at[at(b, g), t], ag4_r.at[at(b, g), t], sibling)

    def ag4_landing(b, g, t):
        ref = stage[g].at[b, 1 - core, slab_three((dig_two + rest - t) % rest)]
        return remote(ref, ref, ag4_s.at[at(b, g), t], ag4_r.at[at(b, g), t], sibling)

    def ag1(b, g):
        @pl.when(core == b)
        def _():
            for t in range(1, first):
                for half in range(2):
                    ag1_copy(b, g, half, t).start()
            ag1_copy(b, g, 1 - b, 0).start()
            stage[g][b, b, pos] = pack[g][b]

    def ag2(b, g):
        for t in range(1, first):
            ag1_landing(b, g, t).wait_recv()

        @pl.when(core != b)
        def _():
            ag1_landing(b, g, 0).wait_recv()

        for t in range(1, rest):
            ag2_copy(b, g, t).start()

    def ag3(b, g):
        for t in range(1, rest):
            ag2_copy(b, g, t).wait_recv()
        for t in range(1, rest):
            ag3_copy(b, g, t).start()
        ag4_copy(b, g, 0).start()

    def ag4(b, g):
        for t in range(1, rest):
            ag3_copy(b, g, t).wait_recv()
            ag4_copy(b, g, t).start()

    def ag5(b, g):
        for t in range(rest):
            ag4_landing(b, g, t).wait_recv()
        lay_out(b, g)

    def ag_sent(b, g):
        @pl.when(core == b)
        def _():
            for t in range(1, first):
                for half in range(2):
                    ag1_copy(b, g, half, t).wait_send()
            ag1_copy(b, g, 1 - b, 0).wait_send()

        for t in range(1, rest):
            ag2_copy(b, g, t).wait_send()
            ag3_copy(b, g, t).wait_send()
        for t in range(rest):
            ag4_copy(b, g, t).wait_send()

    def lay_out(b, g):
        if g == TAB:
            table_in(b)
            return
        if g == DOWN:
            for j in range(n):
                for half in range(2):
                    begin = 4 * unit * j + 2 * unit * half
                    wdown[b, begin : begin + 2 * unit, :] = s_d[b, half, place(half, j)]
            return
        together = 16 // math.gcd(unit, 16)
        for half in range(2):
            for j in range(0, n, together):
                pieces = [stage[g][b, half, place(half, j + i)].astype(F32) for i in range(together)]
                for sub in range(2):
                    low = sub * unit
                    block = jnp.concatenate([piece[low : low + unit] for piece in pieces], axis=0).astype(LOW)
                    part = 2 * half + sub
                    down = slice(unit * j, unit * (j + together))
                    if g == UP:
                        wup[b, down, part * width : (part + 1) * width] = block
                    elif part == 3:
                        wout[b, down, :] = block
                    else:
                        wqkv[b, down, part * width : (part + 1) * width] = block

    def rs0_copy(b, g):
        return remote(stage[g].at[b, 1 - core], r0[g], rs0_s.at[at(b, g)], rs0_r.at[at(b, g)], sibling)

    def rs1_copy(b, g, t):
        return remote(
            stage[g].at[b, core, slab_three((dig_three + t) % rest)], r1[g].at[t - 1],
            rs1_s.at[at(b, g), t - 1, 0], rs1_r.at[at(b, g), t - 1, 0], peer_three(t),
        )

    def rs2_copy(b, g, t):
        return remote(
            stage[g].at[b, core, slab_two(dig_three, (dig_two + t) % rest)], r2[g].at[b, t - 1],
            rs2_s.at[at(b, g), t - 1], rs2_r.at[at(b, g), t - 1], peer_two(t),
        )

    def rs3_copy(b, g, t):
        there = (dig_three * rest + dig_two) * first + (dig_a + t) % first
        device = {"section": b, **peer_first(t)} if t else sibling
        return remote(
            stage[g].at[b, core, there], r3[g].at[core, t], rs3_s.at[at(b, g), t], rs3_r.at[g, core, t], device
        )

    chunk_count = 2 if first % 2 == 0 else 1
    chunk_size = first // chunk_count

    def plane_copy(b, g, t, part):
        three, two = plane[t]
        begin = (((dig_three + three) % rest) * rest + (dig_two + two) % rest) * first + chunk_size * part
        return remote(
            stage[g].at[b, core, pl.ds(begin, chunk_size)], r1[g].at[t, pl.ds(chunk_size * part, chunk_size)],
            rs1_s.at[at(b, g), t, part], rs1_r.at[at(b, g), t, part], peer_plane(three, two),
        )

    def rs0(b, g):
        @pl.when(b == 0)
        def _():
            pl.semaphore_wait(credit.at[0, g], 1)

        rs0_copy(b, g).start()

    def rs1(b, g):
        rs0_copy(b, g).wait_recv()

        @pl.loop(0, n)
        def _(p):
            stage[g][b, core, p] = stage[g][b, core, p] + r0[g][p]

        @pl.when(b == 1)
        def _():
            pl.semaphore_signal(credit.at[0, g], inc=1, device_id=sibling, device_id_type=pl.DeviceIdType.MESH)

        direct = g in (ATT, TAB)
        if rest > 1:
            @pl.when(b == 0)
            def _():
                pl.semaphore_wait(credit.at[1, g], len(plane) if direct else rest - 1)

        if direct:
            for part in range(chunk_count):
                for t in range(len(plane)):
                    plane_copy(b, g, t, part).start()
            return
        for t in range(1, rest):
            rs1_copy(b, g, t).start()

    def rs2(b, g):
        for t in range(1, rest):
            rs1_copy(b, g, t).wait_recv()

        @pl.loop(0, rest * first)
        def _(p):
            here = dig_three * rest * first + p
            total = stage[g][b, core, here].astype(F32)
            for t in range(1, rest):
                total = total + r1[g][t - 1, p].astype(F32)
            stage[g][b, core, here] = total.astype(stage[g].dtype)

        for t in range(1, rest):
            @pl.when(b == 1)
            def _():
                pl.semaphore_signal(
                    credit.at[1, g], inc=1, device_id=peer_three(t), device_id_type=pl.DeviceIdType.MESH
                )

            rs2_copy(b, g, t).start()

    def rs3_send(b, g, part):
        def here(digit):
            return (digit >= chunk_size * part) & (digit < chunk_size * (part + 1))

        for t in range(1, first):
            @pl.when(here((dig_a + t) % first))
            def _():
                rs3_copy(b, g, t).start()

        @pl.when(here(dig_a) & (core != b))
        def _():
            rs3_copy(b, g, 0).start()

    def rs3_part(b, g, part):
        for t in range(len(plane)):
            plane_copy(b, g, t, part).wait_recv()

        @pl.loop(chunk_size * part, chunk_size * (part + 1))
        def _(p):
            here = (dig_three * rest + dig_two) * first + p
            total = stage[g][b, core, here].astype(F32)
            for t in range(len(plane)):
                total = total + r1[g][t, p].astype(F32)
            stage[g][b, core, here] = total.astype(stage[g].dtype)

        rs3_send(b, g, part)

    def rs3_first(b, g):
        rs3_part(b, g, 0)

    def rs3_rest(b, g):
        for part in range(1, chunk_count):
            rs3_part(b, g, part)

    def rs3(b, g):
        if g in (ATT, TAB):
            for part in range(chunk_count):
                rs3_part(b, g, part)

            @pl.when(b == 1)
            def _():
                for three, two in plane:
                    pl.semaphore_signal(
                        credit.at[1, g], inc=1, device_id=peer_plane(three, two),
                        device_id_type=pl.DeviceIdType.MESH,
                    )

            return
        for t in range(1, rest):
            rs2_copy(b, g, t).wait_recv()

        @pl.loop(0, first)
        def _(p):
            here = (dig_three * rest + dig_two) * first + p
            total = stage[g][b, core, here].astype(F32)
            for t in range(1, rest):
                total = total + r2[g][b, t - 1, p].astype(F32)
            stage[g][b, core, here] = total.astype(stage[g].dtype)

        for part in range(chunk_count):
            rs3_send(b, g, part)

    def rs4(b, g):
        @pl.when(core == b)
        def _():
            for own in (True, False):
                half = core if own else 1 - core
                begin = int(own)
                for t in range(begin, first):
                    ref = r3[g].at[half, t]
                    remote(ref, ref, rs3_s.at[at(b, g), t], rs3_r.at[g, half, t], sibling).wait_recv()
                total = stage[g][b, core, pos].astype(F32) if own else None
                for t in range(begin, first):
                    value = r3[g][half, t].astype(F32)
                    total = value if total is None else total + value
                final[g][half] = total

    def rs_sent(b, g):
        rs0_copy(b, g).wait_send()
        if g in (ATT, TAB):
            for part in range(chunk_count):
                for t in range(len(plane)):
                    plane_copy(b, g, t, part).wait_send()
        else:
            for t in range(1, rest):
                rs1_copy(b, g, t).wait_send()
                rs2_copy(b, g, t).wait_send()
        for t in range(1, first):
            rs3_copy(b, g, t).wait_send()

        @pl.when(core != b)
        def _():
            rs3_copy(b, g, 0).wait_send()

    def rows_of(i, images_too=1):
        return pl.ds(pl.multiple_of(i * rows, 16), images_too * rows)

    few = TOGETHER if slots % TOGETHER == 0 else 1
    many = TOGETHER_ROWS if slots % TOGETHER_ROWS == 0 else 1

    def step_rows(i, count):
        return rows_of(i * count, count)

    def ship_parts(kind, b, i):
        src, out = (io_one, io_two)[kind].at[i], out_far.at[kind, core, i]
        q = 2 * kind + b
        near = pltpu.make_async_copy(src, out, ship_s.at[q, i])
        far = remote(src, out, ship_s.at[q, i], ship_r.at[q, i], sibling)
        return near, far

    def ship(kind, b, i):
        near, far = ship_parts(kind, b, i)

        @pl.when(core == b)
        def _():
            near.start()

        @pl.when(core != b)
        def _():
            far.start()

    def shipped(kind, b, i):
        near, far = ship_parts(kind, b, i)

        @pl.when(core == b)
        def _():
            near.wait()

        @pl.when(core != b)
        def _():
            far.wait_send()

    def landed(kind, b, i):
        q = 2 * kind + b
        ref = out_far.at[kind, 1 - core, i]

        @pl.when(core == b)
        def _():
            remote(ref, ref, ship_s.at[q, i], ship_r.at[q, i], sibling).wait_recv()

    def live(i):
        return jnp.where(i < counts[0, core], 1.0, 0.0).astype(F32)

    def only_live(i, value, count):
        parts = [value[rows * m : rows * (m + 1)] * live(i * count + m) for m in range(count)]
        return jnp.concatenate(parts, axis=0)

    def coming(which, i):
        slot = (which * slots + i) % raw.shape[0]
        return pltpu.make_async_copy((images, cotangent)[which].at[i], raw.at[slot], in_s.at[which, i])

    def take_in(which, i):
        coming(which, i).wait()
        both = raw[(which * slots + i) % raw.shape[0]].astype(F32)
        (io_one, io_two)[which][i] = jnp.where(core == 0, both[:, 0, :], both[:, 1, :]).astype(LOW)

    def weave(todo):
        ring = raw.shape[0]
        count = 2 * slots

        def fetch(t, m):
            source = out_far.at[t // slots, m, t % slots]
            return pltpu.make_async_copy(source, io_one.at[2 * (t % ring) + m], weave_in.at[m, t])

        def leave(t):
            return pltpu.make_async_copy(raw.at[t % ring], woven.at[t // slots, t % slots], weave_out.at[t])

        for t in range(ring - 1):
            for m in range(2):
                fetch(t, m).start()

        @pl.loop(0, count)
        def _(t):
            for when, act in todo.items():
                @pl.when(t == when)
                def _():
                    act()

            @pl.when(t + ring - 1 < count)
            def _():
                for m in range(2):
                    fetch(t + ring - 1, m).start()

            @pl.when(t >= ring)
            def _():
                leave(t - ring).wait()

            for m in range(2):
                fetch(t, m).wait()
                raw[t % ring, :, m, :] = io_one[2 * (t % ring) + m]
            leave(t).start()

        for t in range(count - ring, count):
            leave(t).wait()

    def far_copy(which, i, back):
        near, far = ((hid, hid_far), (slope, slope_far))[which]
        near, far = near.at[rows_of(i)], far.at[rows_of(i)]
        src, dst = (far, near) if back else (near, far)
        return pltpu.make_async_copy(src, dst, far_s.at[2 * int(back) + which, i])

    pairs = width // 128
    scale = head_dim ** -0.5
    lane = lax.broadcasted_iota(jnp.int32, (1, 128), 1)
    half_low = [(lane < head_dim).astype(LOW), (lane >= head_dim).astype(LOW)]
    half_f = [(lane < head_dim).astype(F32), (lane >= head_dim).astype(F32)]
    token = lax.broadcasted_iota(jnp.int32, (rows, 128), 0) < length
    half_valid = [jnp.where(token, half_f[j], 0.0).astype(LOW) for j in range(2)]
    valid_lanes = jnp.where(lax.broadcasted_iota(jnp.int32, (1, rows), 1) < length, 1.0, 0.0).astype(F32)
    spare = -rows % 128
    chunk = 2 * width
    chunks = ff // chunk

    def vec(s, r):
        return table[s, r : r + 1, :]

    def up_bias(s, c):
        begin = c * chunk
        row, col = begin // width, begin % width
        if col + chunk <= width:
            return table[s, BU + row : BU + row + 1, col : col + chunk]
        a = table[s, BU + row : BU + row + 1, col:width]
        b = table[s, BU + row + 1 : BU + row + 2, 0 : chunk - (width - col)]
        return jnp.concatenate([a, b], axis=1)

    def add_vec(s, r, value):
        gtable[s, r : r + 1, :] += value

    def attn_forward(s, x, hat, i):
        rd = step_rows(i, few)
        nrm_ref, qkv_ref, prob_ref, ctx_ref = nrm1.at[s], qkv.at[s], prob.at[s], ctx.at[s]
        nrm = (hat * vec(s, G1) + vec(s, S1)).astype(LOW)
        nrm_ref[rd, :] = nrm
        mixed = mm(nrm, wqkv[s])
        q = (mixed[:, 0:width] + vec(s, BQ)).astype(LOW)
        k = mixed[:, width : 2 * width].astype(LOW)
        v = (mixed[:, 2 * width :] + vec(s, BV)).astype(LOW)
        qkv_ref[rd, 0:width] = q
        qkv_ref[rd, width : 2 * width] = k
        qkv_ref[rd, 2 * width :] = v
        images_out = []
        for m in range(few):
            mine = slice(rows * m, rows * (m + 1))
            parts = []
            for p in range(pairs):
                cols = slice(128 * p, 128 * p + 128)
                weights, sides = [], []
                for j in range(2):
                    keys = k[mine, cols] * half_low[j]
                    keys = jnp.concatenate([keys, keys[rows - spare :]], axis=0)
                    scores = mm_right(q[mine, cols], keys)
                    top = jnp.max(scores, axis=-1, keepdims=True)
                    e = jnp.exp2((scores - top) * (scale * 1.4426950408889634)).astype(LOW)
                    prob_ref[i * few + m, 2 * p + j] = e[:, :rows]
                    weights.append(e)
                    sides.append(jnp.concatenate([v[mine, cols] * half_valid[j], half_valid[j]], axis=1))
                    sides.append(jnp.zeros((spare, 256), LOW))
                total = mm(jnp.concatenate(weights, axis=1), jnp.concatenate(sides, axis=0))
                over = 1.0 / total[:, 128:]
                overs[s, rows_of(i * few + m), cols] = over.astype(LOW)
                parts.append((total[:, :128] * over).astype(LOW))
            images_out.append(jnp.concatenate(parts, axis=1))
        context = jnp.concatenate(images_out, axis=0)
        ctx_ref[rd, :] = context
        return x + mm(context, wout[s]) + vec(s, BO)

    def ff_forward(s, after, rd):
        hat, rstd, _ = normalize(after)
        hat2[s, rd, :] = hat.astype(LOW)
        nrm = (hat * vec(s, G2) + vec(s, S2)).astype(LOW)
        total = after + vec(s, BD)
        for c in range(chunks):
            cols = slice(chunk * c, chunk * c + chunk)
            pre = mm(nrm, wup[s, :, cols]) + up_bias(s, c)
            phi, slo = normal_parts(pre)
            h = (pre * phi).astype(LOW)
            hid[rd, cols] = h
            slope[rd, cols] = slo.astype(LOW)
            total = total + mm(h, wdown[s, cols, :])
        return total, rstd

    def ff_backward(s, g, rd, rstd):
        g_low = g.astype(LOW)
        add_vec(s, BD, colsum(g_low.astype(F32)))
        d_nrm = None
        for c in range(chunks):
            cols = slice(chunk * c, chunk * c + chunk)
            d_hid = mm_right(g_low, wdown[s, cols, :])
            d_pre = (d_hid * slope[rd, cols].astype(F32)).astype(LOW)
            slope[rd, cols] = d_pre
            part = mm_right(d_pre, wup[s, :, cols])
            d_nrm = part if d_nrm is None else d_nrm + part
        hat = hat2[s, rd, :].astype(F32)
        add_vec(s, G2, colsum(d_nrm * hat))
        add_vec(s, S2, colsum(d_nrm))
        d_after = g + normalize_back(d_nrm * vec(s, G2), hat, rstd)
        low = d_after.astype(LOW)
        dal[rd, :] = low
        return d_after

    def attn_backward(s, i):
        qkv_ref, prob_ref, ctx_ref = qkv.at[s], prob.at[s], ctx.at[s]
        rd = step_rows(i, few)
        d_context = mm_right(dal[rd, :], wout[s])
        d_context = (d_context * overs[s, rd, :].astype(F32)).astype(LOW)
        for m in range(few):
            rd = rows_of(i * few + m)
            d_ctx = d_context[rows * m : rows * (m + 1)]
            dq, dk, dv = [], [], []
            for p in range(pairs):
                cols = slice(128 * p, 128 * p + 128)
                q = qkv_ref[rd, 128 * p : 128 * p + 128]
                k = qkv_ref[rd, width + 128 * p : width + 128 * p + 128]
                v = qkv_ref[rd, 2 * width + 128 * p : 2 * width + 128 * p + 128]
                dc = d_ctx[:, cols]
                both = dc.astype(F32) * ctx_ref[rd, cols].astype(F32)
                q_t, dc_t = q.T, dc.T
                to_q, to_k, to_v = None, [], []
                for j in range(2):
                    e = prob_ref[i * few + m, 2 * p + j]
                    delta = jnp.sum(both * half_f[j], axis=-1, keepdims=True)
                    d_prob = mm_right(dc, v * half_low[j])
                    ds = (e.astype(F32) * (d_prob - delta)).astype(LOW)
                    part = mm(ds, k * half_valid[j])
                    to_q = part if to_q is None else to_q + part
                    head = slice(head_dim * j, head_dim * (j + 1))
                    to_k.append(mm(q_t[head], ds))
                    to_v.append(mm(dc_t[head], e))
                dq.append((to_q * scale).astype(LOW))
                dk.append((jnp.concatenate(to_k, axis=0) * (valid_lanes * scale)).astype(LOW).T)
                dv.append((jnp.concatenate(to_v, axis=0) * valid_lanes).astype(LOW).T)
            d_mixed = jnp.concatenate(dq + dk + dv, axis=1)
            qkv_ref[rd, :] = d_mixed

    def input_backward(s, d_after, rd, x, mean, rstd):
        d_nrm = mm_right(qkv[s, rd, :], wqkv[s])
        hat = (x - mean) * rstd
        add_vec(s, G1, colsum(d_nrm * hat))
        add_vec(s, S1, colsum(d_nrm))
        return d_after + normalize_back(d_nrm * vec(s, G1), hat, rstd)

    def grads_down(s):
        left_t[0:width, :] = low_g[...].T

        @pl.loop(0, 2)
        def _(c):
            cols = pl.ds(pl.multiple_of(c * 2 * width, 128), 2 * width)
            block = mm(left_t[0:width, :], hid[:, cols]).T
            for i in range(n // 2):
                for half in range(2):
                    begin = 4 * unit * i + 2 * unit * half
                    s_d[s, half, place(half, c * (n // 2) + i)] = block[begin : begin + 2 * unit].astype(LOW)

    def pair_out(ref, s, half, one, two):
        for j in range(n):
            down = slice(unit * j, unit * (j + 1))
            piece = jnp.concatenate([one[down], two[down]], axis=0).astype(LOW)
            ref[s, half, place(half, j)] = piece

    def grads_up(s):
        left_t[0:width, :] = (hat2[s].astype(F32) * vec(s, G2) + vec(s, S2)).astype(LOW).T
        for half in range(2):
            both = mm(left_t[...], slope[:, 2 * half * width : 2 * (half + 1) * width])
            pair_out(s_u, s, half, both[:, :width], both[:, width:])
            gtable[s, BU + 2 * half : BU + 2 * half + 1, :] = both[width : width + 1, :width]
            gtable[s, BU + 2 * half + 1 : BU + 2 * half + 2, :] = both[width : width + 1, width:]

    def grads_attn(s):
        mix_s = qkv.at[s]
        left_t[0:width, :] = ctx[s].T
        four = mm(left_t[...], dal[...])
        left_t[0:width, :] = nrm1[s].T
        three = mm(left_t[...], mix_s[:, 2 * width :])
        pair_out(s_a, s, 1, three, four)
        both = mm(left_t[...], mix_s[:, 0 : 2 * width])
        pair_out(s_a, s, 0, both[:, :width], both[:, width:])
        for row, sums in ((BO, four), (BV, three), (BQ, both)):
            gtable[s, row : row + 1, :] = sums[width : width + 1, :width]

    barrier = pltpu.get_barrier_semaphore()
    greeted = [sibling]
    greeted += [{"section": half, **peer_first(t)} for t in range(1, first) for half in range(2)]
    greeted += [peer_plane(three, two) for three, two in plane]
    for device in greeted:
        pl.semaphore_signal(barrier, inc=1, device_id=device, device_id_type=pl.DeviceIdType.MESH)
    pack_own()
    pl.semaphore_wait(barrier, len(greeted))

    def run(*todo):
        for f, b, g in todo:
            f(b, g)

    def events(i, table_of):
        for when, todo in table_of.items():
            @pl.when(i == when)
            def _():
                run(*todo)

    def both(f, b, g):
        return [(f, b, g), (f, b, TAB)]

    def take(i, m):
        return pl.ds(pl.multiple_of((i * many + m) * rows, 16), length)

    ahead = raw.shape[0]
    run(*both(ag1, 0, ATT))
    for i in range(ahead):
        coming(0, i).start()
    fill_repeats()
    gtable[...] = jnp.zeros_like(gtable)
    left_t[width:, :] = jnp.ones((16, left_t.shape[1]), LOW)
    low_g[...] = jnp.zeros_like(low_g)
    xs[0] = jnp.zeros_like(low_g)

    @pl.loop(0, slots)
    def images_in(i):
        take_in(0, i)

        @pl.when(i + ahead < slots)
        def _():
            coming(0, i + ahead).start()

        @pl.when(i + ahead >= slots)
        def _():
            coming(1, i + ahead - slots).start()

        @pl.when(i == 4)
        def _():
            run((ag1, 0, UP))

    run(*both(ag2, 0, ATT), (ag1, 0, DOWN), *both(ag1, 1, ATT))

    def statistic(s, rd, which):
        return jnp.where(s == 0, rstds[rd, which : which + 1], rstds[rd, 3 + which : 4 + which])

    def first_norm(s, rd, x):
        hat, rstd, mean = normalize(x)
        after_ref[rd, :] = hat
        rstds[rd, 3 * s : 3 * s + 1] = rstd
        rstds[rd, 3 * s + 2 : 3 * s + 3] = mean

    @pl.loop(0, slots // many)
    def norm_one(i):
        for m in range(many):
            xs[0, take(i, m), :] = io_one[i * many + m]
        rd = step_rows(i, many)
        x = xs[0, rd, :].astype(F32)
        token_rows = lax.broadcasted_iota(jnp.int32, (rows, width), 0) < length
        parts = [x[rows * m : rows * (m + 1)] for m in range(many)]
        x = jnp.concatenate([jnp.where(token_rows, part, part[0:1]) for part in parts], axis=0)
        xs[0, rd, :] = x.astype(LOW)
        first_norm(0, rd, x)

    run((ag2, 0, UP), *both(ag3, 0, ATT), (ag1, 1, UP), (ag1, 1, DOWN), (ag2, 0, DOWN), (ag3, 0, UP))

    @pl.loop(0, slots)
    def cotangents_in(i):
        take_in(1, i)

        @pl.when(i + ahead < slots)
        def _():
            coming(1, i + ahead).start()

    run(*both(ag4, 0, ATT), (ag3, 0, DOWN), *both(ag2, 1, ATT), *both(ag5, 0, ATT))

    @pl.loop(0, 2)
    def forward(s):
        @pl.loop(0, slots // few)
        def attention(i):
            @pl.when(s == 0)
            def _():
                events(i, {1: [(ag4, 0, UP), (ag2, 1, UP)], 2: [(ag4, 0, DOWN)]})

            @pl.when(s == 1)
            def _():
                events(i, {1: [(ag4, 1, UP)], 2: [(ag4, 1, DOWN)]})

            rd = step_rows(i, few)
            after_ref[rd, :] = attn_forward(s, xs[s, rd, :].astype(F32), after_ref[rd, :], i)

        @pl.when(s == 0)
        def _():
            run(*both(ag3, 1, ATT), (ag5, 0, UP), (ag5, 0, DOWN))

        @pl.when(s == 1)
        def _():
            run((ag5, 1, UP), (ag5, 1, DOWN))

        @pl.loop(0, slots // many)
        def feed_forward(i):
            @pl.when(s == 0)
            def _():
                events(i, {0: [(ag2, 1, DOWN), (ag3, 1, UP)], 2: both(ag4, 1, ATT)})

            rd = step_rows(i, many)

            @pl.when(s == 1)
            def _():
                for m in range(many):
                    far_copy(0, i * many + m, False).wait()
                    far_copy(1, i * many + m, False).wait()
                    shipped(0, 0, i * many + m)

            out, rstd2 = ff_forward(s, after_ref[rd, :], rd)
            for block in range(2):
                @pl.when(s == block)
                def _():
                    rstds[rd, 3 * block + 1 : 3 * block + 2] = rstd2

            out = only_live(i, out, many)
            for m in range(many):
                io_one[i * many + m] = out[rows * m : rows * m + length].astype(LOW)
                ship(0, s, i * many + m)

            @pl.when(s == 0)
            def _():
                for m in range(many):
                    far_copy(0, i * many + m, False).start()
                    far_copy(1, i * many + m, False).start()
                low = out.astype(LOW)
                xs[1, rd, :] = low
                first_norm(1, rd, low.astype(F32))

        @pl.when(s == 0)
        def _():
            run((ag3, 1, DOWN), *both(ag5, 1, ATT))

    for b in range(2):
        for g in groups:
            ag_sent(b, g)

    @pl.loop(0, 2)
    def backward(turn):
        s = 1 - turn

        @pl.loop(0, slots // many)
        def feed_forward(i):
            @pl.when(s == 0)
            def _():
                events(i, {1: [*both(rs1, 1, ATT), (rs3, 1, DOWN)], 2: [(rs3, 1, UP)]})
                for m in range(many):
                    far_copy(1, i * many + m, True).wait()

            rd = step_rows(i, many)
            for m in range(many):
                g = live(i * many + m) * io_two[i * many + m].astype(F32)
                low_g[take(i, m), :] = g.astype(LOW)
            after_ref[rd, :] = ff_backward(s, low_g[rd, :].astype(F32), rd, statistic(s, rd, 1))

        @pl.when(s == 0)
        def _():
            for i in range(slots):
                far_copy(0, i, True).wait()

        grads_down(s)
        run((rs0, s, DOWN))

        @pl.when(s == 1)
        def _():
            for i in range(slots):
                far_copy(0, i, True).start()

        grads_up(s)
        run((rs0, s, UP))

        @pl.when(s == 1)
        def _():
            for i in range(slots):
                far_copy(1, i, True).start()

        @pl.loop(0, slots // few)
        def attention(i):
            @pl.when(s == 0)
            def _():
                events(i, {1: both(rs3, 1, ATT)})

            events(i, {0: [(rs1, s, DOWN)], 1: [(rs1, s, UP)]})
            attn_backward(s, i)

        run((rs2, s, DOWN))

        @pl.when(s == 0)
        def _():
            run(*both(rs4, 1, ATT), (rs4, 1, DOWN), (rs4, 1, UP))

        grads_attn(s)
        run((rs0, s, ATT))

        @pl.loop(0, slots // many)
        def to_input(i):
            rd = step_rows(i, many)
            x = xs[s, rd, :].astype(F32)
            d_in = input_backward(s, after_ref[rd, :], rd, x, statistic(s, rd, 2), statistic(s, rd, 0))
            for m in range(many):
                @pl.when(s == 0)
                def _():
                    shipped(1, 1, i * many + m)

                io_two[i * many + m] = d_in[rows * m : rows * m + length].astype(LOW)
                ship(1, s, i * many + m)

        table_out(s)
        run((rs0, s, TAB), (rs2, s, UP))

    def sent_and_landed(kind):
        @pl.loop(0, slots)
        def _(i):
            shipped(kind, 1 - kind, i)
            for b in range(2):
                landed(kind, b, i)

    sent_and_landed(0)
    weave({
        1: lambda: run(*both(rs1, 0, ATT), (rs3, 0, DOWN)),
        3: lambda: run((rs3, 0, UP)),
        slots - raw.shape[0] + 1: lambda: sent_and_landed(1),
        slots: lambda: run(*both(rs3_first, 0, ATT)),
        slots + 3: lambda: run(*both(rs3_rest, 0, ATT), (rs4, 0, DOWN), (rs4, 0, UP)),
    })
    run(*both(rs4, 0, ATT))
    for b in range(2):
        for g in groups:
            rs_sent(b, g)


def output_kernel(
    woven, far_a, far_u, far_d, far_t, o_acts, o_ings, o_g1, o_s1, o_qkv, o_qv, o_out, o_bo, o_g2, o_s2, o_up, o_bu, o_down, o_bd,
    passing, f_a, f_u, f_d, f_t, sems, grad_sems
):
    coming = [
        pltpu.make_async_copy(source, target, grad_sems.at[i])
        for i, (source, target) in enumerate(((far_a, f_a), (far_u, f_u), (far_d, f_d), (far_t, f_t)))
    ]
    for copy in coming:
        copy.start()
    arriving, leaving = [], []
    for which, target in enumerate((o_acts, o_ings)):
        for i in range(target.shape[0]):
            arriving.append(pltpu.make_async_copy(woven.at[which, i], passing.at[which, i], sems.at[0, which, i]))
            leaving.append(pltpu.make_async_copy(passing.at[which, i], target.at[i], sems.at[1, which, i]))
    for copy in arriving:
        copy.start()
    for one, two in zip(arriving, leaving):
        one.wait()
        two.start()
    for copy in coming:
        copy.wait()
    unit, width = o_out.shape[1:]
    for half in range(2):
        o_down[0, 2 * unit * half : 2 * unit * (half + 1), :] = f_d[half]
        for sub in range(2):
            part = 2 * half + sub
            cols = slice(part * width, (part + 1) * width)
            o_up[0, :, cols] = f_u[half, unit * sub : unit * (sub + 1), :]
            piece = f_a[half, unit * sub : unit * (sub + 1), :]
            if part == 3:
                o_out[0] = piece
            else:
                o_qkv[0, :, cols] = piece
    begin = 0
    for out in (o_g1, o_s1, o_bo, o_g2, o_s2, o_bd, o_qv):
        part = out.shape[1]
        out[...] = f_t[0, :, begin : begin + part]
        begin += part
    o_bu[...] = f_t[1, :, 0 : o_bu.shape[1]]
    for copy in leaving:
        copy.wait()


def local(
    images, cotangent, counts,
    ln1_gain, ln1_bias, w_qkv, b_qv, w_out, b_out, ln2_gain, ln2_bias, w_up, b_up, w_down, b_down,
):
    micro_count, slots, length, width = images.shape
    ff = w_up.shape[2]
    rows = -(-length // 16) * 16
    n = lax.axis_size("fsdp")
    unit = width // n
    first, rest = radices(n)
    total = slots * rows
    head_dim = width // HEADS

    def vm(*shape, kind=LOW):
        return pltpu.VMEM(shape, kind)

    tall = [(2 * unit, LOW)] * 3 + [(1, F32)]
    dma = lambda *shape: pltpu.SemaphoreType.DMA(shape)
    outs = [((2, slots, length, 2, width), LOW)]
    outs += [((2, r, width), F32) for r, _ in tall] + [((total, ff), LOW)] * 2 + [((2, 2, slots, length, width), LOW)]
    scratch = [
        vm(2, total, width), vm(3, length, 2, width), vm(slots, length, width), vm(slots, length, width),
        *[vm(2, r, width, kind=kind) for r, kind in tall],
        vm(2, width, 3 * width), vm(2, width, width), vm(2, width, ff), vm(2, ff, width),
        vm(2, TABLE, width, kind=F32), vm(2, TABLE, width, kind=F32),
        vm(unit, width), vm(2 * unit, 2 * width), vm(4 * unit, 4 * width),
        vm(total, width, kind=F32), vm(2, total, width), vm(2, total, 3 * width), vm(2, slots, HEADS, rows, rows),
        vm(2, total, width),
        vm(2, total, width), vm(2, total, width), vm(total, 6, kind=F32),
        vm(total, ff), vm(total, ff), vm(total, width), vm(total, width), vm(width + 16, total),
    ]
    scratch += [vm(2, 2, n, r, width, kind=kind) for r, kind in tall]
    scratch += [vm(n, r, width, kind=kind) for r, kind in tall]
    plane = rest * rest - 1
    for g, (r, kind) in enumerate(tall):
        direct = g in (ATT, TAB)
        scratch.append(vm(*((plane, first) if direct else (rest - 1, rest * first)), r, width, kind=kind))
    scratch += [vm(2, rest - 1, first, *tall[g][:1], width) for g in (UP, DOWN)]
    scratch += [vm(2, first, r, width, kind=kind) for r, kind in tall]
    scratch += [dma(2, slots), dma(2, 2 * slots), dma(2 * slots), dma(4, slots), dma(4, slots), dma(4, slots)]
    scratch += [dma(4, 2, first), dma(8, first)] + [dma(8, rest - 1)] * 4 + [dma(8, rest)] * 2
    scratch += [dma(8)] * 2 + [dma(8, plane, 2)] * 2 + [dma(8, rest - 1)] * 2 + [dma(8, first), dma(4, 2, first)]
    scratch += [pltpu.SemaphoreType.REGULAR((2, 4))]
    dims = (slots, length, rows, width, ff, head_dim, n)
    vmem = pl.BlockSpec(memory_space=pltpu.VMEM)
    hbm = pl.BlockSpec(memory_space=pltpu.HBM)
    woven, f_a, f_u, f_d, f_t, *_ = pl.pallas_call(
        functools.partial(whole_kernel, dims),
        out_shape=[jax.ShapeDtypeStruct(*o) for o in outs],
        in_specs=[hbm, hbm, pl.BlockSpec(memory_space=pltpu.SMEM)] + [vmem] * 12,
        out_specs=[hbm] + [vmem] * 4 + [hbm] * 3,
        scratch_shapes=scratch,
        compiler_params=pltpu.CompilerParams(
            vmem_limit_bytes=(64 << 20) - (96 << 10), collective_id=0, has_side_effects=True
        ),
    )(
        images.transpose(1, 2, 0, 3), cotangent.transpose(1, 2, 0, 3), counts.T, ln1_gain, ln1_bias, b_out, ln2_gain, ln2_bias, b_down, b_qv, b_up,
        w_qkv, w_out, w_up, w_down,
    )

    params = (
        ln1_gain, ln1_bias, w_qkv, b_qv, w_out, b_out, ln2_gain, ln2_bias, w_up, b_up, w_down, b_down
    )
    acts, ings, *grads = pl.pallas_call(
        output_kernel,
        out_shape=[jax.ShapeDtypeStruct(woven.shape[1:], LOW)] * 2
        + [jax.ShapeDtypeStruct(p.shape, F32) for p in params],
        in_specs=[hbm] * 5,
        out_specs=[hbm] * 2 + [vmem] * len(params),
        scratch_shapes=[
            vm(2, slots, length, 2, width), *[vm(2, r, width, kind=F32) for r, _ in tall], dma(2, 2, slots), dma(4)
        ],
        compiler_params=pltpu.CompilerParams(vmem_limit_bytes=(64 << 20) - (96 << 10)),
    )(woven, f_a, f_u, f_d, f_t)

    def as_given(value):
        return value.transpose(2, 0, 1, 3)[None]

    return (as_given(acts), as_given(ings), *grads)


def solution(mesh):
    split = P("section", "fsdp")
    cube = P("section", "fsdp", None)
    image = P(None, "fsdp", None, None)
    result = P("section", None, "fsdp", None, None)
    params = (split, split, cube, split, cube, split, split, split, cube, split, cube, split)
    return jax.shard_map(
        local,
        mesh=mesh,
        in_specs=(image, image, P(None, "fsdp")) + params,
        out_specs=(result, result) + params,
        check_vma=False,
    )
```

```python
import functools
import math

import jax
import jax.numpy as jnp
from jax import lax
from jax.experimental import pallas as pl
from jax.experimental.pallas import tpu as pltpu
from jax.sharding import PartitionSpec as P

HEADS = 6
EPS = 1e-06
F32 = jnp.float32
LOW = jnp.bfloat16

G1, S1, BO, G2, S2, BD, BQ, BV, BU = 0, 1, 2, 3, 4, 5, 6, 7, 8
TABLE = 16
TOGETHER, TOGETHER_ROWS = 2, 2
ATT, UP, DOWN, TAB = 0, 1, 2, 3


def radices(n):
    rest = max(r for r in range(1, n + 1) if r * r * r <= n and n % (r * r) == 0)
    return n // (rest * rest), rest


def mm(left, right):
    return jnp.dot(left, right, preferred_element_type=F32)


def mm_right(left, right):
    return lax.dot_general(left, right, (((1,), (1,)), ((), ())), preferred_element_type=F32)


def mm_left(left, right):
    return lax.dot_general(left, right, (((0,), (0,)), ((), ())), preferred_element_type=F32)


def normal_parts(pre):
    phi = 0.5 + 0.5 * lax.erf(pre * 0.7071067811865476)
    low = pre.astype(LOW)
    density = jnp.exp2(low * low * LOW(-0.5 * 1.4426950408889634)) * LOW(0.3989422804014327)
    return phi, phi.astype(LOW) + low * density


def normalize(value):
    mean = jnp.mean(value, axis=-1, keepdims=True)
    center = value - mean
    rstd = lax.rsqrt(jnp.mean(center * center, axis=-1, keepdims=True) + EPS)
    return center * rstd, rstd, mean


def normalize_back(d_hat, hat, rstd):
    mean_one = jnp.mean(d_hat, axis=-1, keepdims=True)
    mean_two = jnp.mean(d_hat * hat, axis=-1, keepdims=True)
    return rstd * (d_hat - mean_one - hat * mean_two)


def colsum(value):
    return jnp.sum(value, axis=0, keepdims=True)


def whole_kernel(dims, *refs):
    slots, length, rows, width, ff, head_dim, n = dims
    (
        images, cotangent, counts, v_g1, v_s1, v_bo, v_g2, v_s2, v_bd, v_qv, v_up, a_qkv, a_out, a_up, a_down,
        woven, f_a, f_u, f_d, f_t, hid_far, slope_far, out_far,
        xs, raw, io_one, io_two, pack_a, pack_u, pack_d, pack_t,
        wqkv, wout, wup, wdown, table, gtable, rep_one, rep_two, rep_four,
        after_ref, nrm1, qkv, prob, overs, ctx, hat2, rstds, hid, slope, dal, low_g, left_t,
        s_a, s_u, s_d, s_t, r0_a, r0_u, r0_d, r0_t, r1_a, r1_u, r1_d, r1_t, r2_u, r2_d,
        r3_a, r3_u, r3_d, r3_t,
        in_s, weave_in, weave_out, ship_s, ship_r, far_s, ag1_s, ag1_r, ag2_s, ag2_r, ag3_s, ag3_r, ag4_s, ag4_r,
        rs0_s, rs0_r, rs1_s, rs1_r, rs2_s, rs2_r, rs3_s, rs3_r, credit,
    ) = refs
    groups = (ATT, UP, DOWN, TAB)
    pack = (pack_a, pack_u, pack_d, pack_t)
    stage = (s_a, s_u, s_d, s_t)
    r0, r1, r2 = (r0_a, r0_u, r0_d, r0_t), (r1_a, r1_u, r1_d, r1_t), (None, r2_u, r2_d, None)
    r3, final = (r3_a, r3_u, r3_d, r3_t), (f_a, f_u, f_d, f_t)

    first, rest = radices(n)
    unit = width // n
    core = lax.axis_index("section")
    me = lax.axis_index("fsdp")
    dig_a, dig_b, dig_c = me // (rest * rest), (me // rest) % rest, me % rest
    dig_three, dig_two = dig_c + core * (dig_b - dig_c), dig_b + core * (dig_c - dig_b)
    step_three, step_two = 1 + core * (rest - 1), rest - core * (rest - 1)
    pos = (dig_three * rest + dig_two) * first + dig_a
    pos_of = ((dig_c * rest + dig_b) * first + dig_a, (dig_b * rest + dig_c) * first + dig_a)
    sibling = {"section": 1 - core}

    def place(half, j):
        a, b, c = j // (rest * rest), (j // rest) % rest, j % rest
        return ((c * rest + b) if half == 0 else (b * rest + c)) * first + a

    def peer_first(t):
        return {"fsdp": me + ((dig_a + t) % first - dig_a) * (rest * rest)}

    def peer_two(t):
        return {"fsdp": me + ((dig_two + t) % rest - dig_two) * step_two}

    def peer_three(t):
        return {"fsdp": me + ((dig_three + t) % rest - dig_three) * step_three}

    def peer_plane(three, two):
        here = ((dig_three + three) % rest - dig_three) * step_three
        return {"fsdp": me + here + ((dig_two + two) % rest - dig_two) * step_two}

    plane = [(three, two) for three in range(rest) for two in range(rest) if three or two]

    def remote(src, dst, s_sem, r_sem, device):
        return pltpu.make_async_remote_copy(
            src_ref=src, dst_ref=dst, send_sem=s_sem, recv_sem=r_sem, device_id=device,
            device_id_type=pl.DeviceIdType.MESH,
        )

    def slab_two(three, two):
        return pl.ds((three * rest + two) * first, first)

    def slab_three(three):
        return pl.ds(three * rest * first, rest * first)

    def fill_repeats():
        for ref in (rep_one, rep_two, rep_four):
            part = ref.shape[0]
            lanes = lax.broadcasted_iota(jnp.int32, ref.shape, 1).astype(F32)
            line = lax.broadcasted_iota(jnp.int32, ref.shape, 0).astype(F32)
            rest_of = lanes - part * jnp.floor((lanes + 0.5) * (1.0 / part))
            ref[...] = jnp.where(jnp.abs(rest_of - line) < 0.5, 1.0, 0.0).astype(LOW)

    def own_lanes(part):
        shape = (n, part * n)
        lanes = lax.broadcasted_iota(jnp.int32, shape, 1)
        begin = lax.broadcasted_iota(jnp.int32, shape, 0) * part
        return (lanes >= begin) & (lanes < begin + part)

    shares = (
        ((G1, unit, rep_one), (S1, unit, rep_one), (BO, unit, rep_one), (G2, unit, rep_one), (S2, unit, rep_one),
         (BD, unit, rep_one), (BQ, 2 * unit, rep_two)),
        ((BU, 4 * unit, rep_four),),
    )

    def table_in(b):
        for half in range(2):
            lines = jnp.concatenate([s_t[b, half, place(half, j)] for j in range(n)], axis=0)
            begin = 0
            for row, part, ref in shares[half]:
                spread = mm(lines[:, begin : begin + part].astype(LOW), ref[...])
                line = colsum(jnp.where(own_lanes(part), spread, 0.0))
                for i in range(part * n // width):
                    table[b, row + i : row + i + 1, :] = line[:, width * i : width * (i + 1)]
                begin += part

    def table_out(b):
        for half in range(2):
            parts, begin = [], 0
            for row, part, ref in shares[half]:
                count = part * n // width
                line = jnp.concatenate([gtable[b, row + i : row + i + 1, :] for i in range(count)], axis=1)
                parts.append(mm_right(jnp.where(own_lanes(part), line, 0.0).astype(LOW), ref[...]))
                begin += part
            parts.append(jnp.zeros((n, width - begin), F32))
            lines = jnp.concatenate(parts, axis=1)
            for j in range(n):
                s_t[b, half, place(half, j)] = lines[j : j + 1]

    def pack_own():
        for half in range(2):
            vectors = ((v_g1, v_s1, v_bo, v_g2, v_s2, v_bd, v_qv), (v_up,))[half]
            lines = [vector[...].astype(F32) for vector in vectors]
            lines.append(jnp.zeros((1, width - sum(line.shape[1] for line in lines)), F32))
            pack_t[half] = jnp.concatenate(lines, axis=1)
            for ref in (pack_a, pack_u):
                both = []
                for part in (2 * half, 2 * half + 1):
                    if ref is pack_u:
                        both.append(a_up[0, :, part * width : (part + 1) * width])
                    elif part == 3:
                        both.append(a_out[0])
                    else:
                        both.append(a_qkv[0, :, part * width : (part + 1) * width])
                ref[half] = jnp.concatenate([value.astype(F32) for value in both], axis=0).astype(LOW)
            pack_d[half] = a_down[0, 2 * unit * half : 2 * unit * (half + 1), :]

    def at(b, g):
        return len(groups) * b + g

    def ag1_copy(b, g, half, t):
        device = {"section": half, **peer_first(t)} if t else sibling
        return remote(
            pack[g].at[half], stage[g].at[b, half, pos_of[half]],
            ag1_s.at[g, half, t], ag1_r.at[at(b, g), t], device,
        )

    def ag1_landing(b, g, t):
        ref = stage[g].at[b, core, (dig_three * rest + dig_two) * first + (dig_a + first - t) % first]
        return remote(ref, ref, ag1_s.at[g, 0, t], ag1_r.at[at(b, g), t], sibling)

    def ag2_copy(b, g, t):
        ref = stage[g].at[b, core, slab_two(dig_three, dig_two)]
        return remote(ref, ref, ag2_s.at[at(b, g), t - 1], ag2_r.at[at(b, g), t - 1], peer_two(t))

    def ag3_copy(b, g, t):
        ref = stage[g].at[b, core, slab_three(dig_three)]
        return remote(ref, ref, ag3_s.at[at(b, g), t - 1], ag3_r.at[at(b, g), t - 1], peer_three(t))

    def ag4_copy(b, g, t):
        ref = stage[g].at[b, core, slab_three((dig_three + rest - t) % rest)]
        return remote(ref, ref, ag4_s.at[at(b, g), t], ag4_r.at[at(b, g), t], sibling)

    def ag4_landing(b, g, t):
        ref = stage[g].at[b, 1 - core, slab_three((dig_two + rest - t) % rest)]
        return remote(ref, ref, ag4_s.at[at(b, g), t], ag4_r.at[at(b, g), t], sibling)

    def ag1(b, g):
        @pl.when(core == b)
        def _():
            for t in range(1, first):
                for half in range(2):
                    ag1_copy(b, g, half, t).start()
            ag1_copy(b, g, 1 - b, 0).start()
            stage[g][b, b, pos] = pack[g][b]

    def ag2(b, g):
        for t in range(1, first):
            ag1_landing(b, g, t).wait_recv()

        @pl.when(core != b)
        def _():
            ag1_landing(b, g, 0).wait_recv()

        for t in range(1, rest):
            ag2_copy(b, g, t).start()

    def ag3(b, g):
        for t in range(1, rest):
            ag2_copy(b, g, t).wait_recv()
        for t in range(1, rest):
            ag3_copy(b, g, t).start()
        ag4_copy(b, g, 0).start()

    def ag4(b, g):
        for t in range(1, rest):
            ag3_copy(b, g, t).wait_recv()
            ag4_copy(b, g, t).start()

    def ag5(b, g):
        for t in range(rest):
            ag4_landing(b, g, t).wait_recv()
        lay_out(b, g)

    def ag_sent(b, g):
        @pl.when(core == b)
        def _():
            for t in range(1, first):
                for half in range(2):
                    ag1_copy(b, g, half, t).wait_send()
            ag1_copy(b, g, 1 - b, 0).wait_send()

        for t in range(1, rest):
            ag2_copy(b, g, t).wait_send()
            ag3_copy(b, g, t).wait_send()
        for t in range(rest):
            ag4_copy(b, g, t).wait_send()

    def lay_out(b, g):
        if g == TAB:
            table_in(b)
            return
        if g == DOWN:
            for j in range(n):
                for half in range(2):
                    begin = 4 * unit * j + 2 * unit * half
                    wdown[b, begin : begin + 2 * unit, :] = s_d[b, half, place(half, j)]
            return
        together = 16 // math.gcd(unit, 16)
        for half in range(2):
            for j in range(0, n, together):
                pieces = [stage[g][b, half, place(half, j + i)].astype(F32) for i in range(together)]
                for sub in range(2):
                    low = sub * unit
                    block = jnp.concatenate([piece[low : low + unit] for piece in pieces], axis=0).astype(LOW)
                    part = 2 * half + sub
                    down = slice(unit * j, unit * (j + together))
                    if g == UP:
                        wup[b, down, part * width : (part + 1) * width] = block
                    elif part == 3:
                        wout[b, down, :] = block
                    else:
                        wqkv[b, down, part * width : (part + 1) * width] = block

    def rs0_copy(b, g):
        return remote(stage[g].at[b, 1 - core], r0[g], rs0_s.at[at(b, g)], rs0_r.at[at(b, g)], sibling)

    def rs1_copy(b, g, t):
        return remote(
            stage[g].at[b, core, slab_three((dig_three + t) % rest)], r1[g].at[t - 1],
            rs1_s.at[at(b, g), t - 1, 0], rs1_r.at[at(b, g), t - 1, 0], peer_three(t),
        )

    def rs2_copy(b, g, t):
        return remote(
            stage[g].at[b, core, slab_two(dig_three, (dig_two + t) % rest)], r2[g].at[b, t - 1],
            rs2_s.at[at(b, g), t - 1], rs2_r.at[at(b, g), t - 1], peer_two(t),
        )

    def rs3_copy(b, g, t):
        there = (dig_three * rest + dig_two) * first + (dig_a + t) % first
        device = {"section": b, **peer_first(t)} if t else sibling
        return remote(
            stage[g].at[b, core, there], r3[g].at[core, t], rs3_s.at[at(b, g), t], rs3_r.at[g, core, t], device
        )

    chunk_count = 2 if first % 2 == 0 else 1
    chunk_size = first // chunk_count

    def plane_copy(b, g, t, part):
        three, two = plane[t]
        begin = (((dig_three + three) % rest) * rest + (dig_two + two) % rest) * first + chunk_size * part
        return remote(
            stage[g].at[b, core, pl.ds(begin, chunk_size)], r1[g].at[t, pl.ds(chunk_size * part, chunk_size)],
            rs1_s.at[at(b, g), t, part], rs1_r.at[at(b, g), t, part], peer_plane(three, two),
        )

    def rs0(b, g):
        @pl.when(b == 0)
        def _():
            pl.semaphore_wait(credit.at[0, g], 1)

        rs0_copy(b, g).start()

    def rs1(b, g):
        rs0_copy(b, g).wait_recv()

        @pl.loop(0, n)
        def _(p):
            stage[g][b, core, p] = stage[g][b, core, p] + r0[g][p]

        @pl.when(b == 1)
        def _():
            pl.semaphore_signal(credit.at[0, g], inc=1, device_id=sibling, device_id_type=pl.DeviceIdType.MESH)

        direct = g in (ATT, TAB)
        if rest > 1:
            @pl.when(b == 0)
            def _():
                pl.semaphore_wait(credit.at[1, g], len(plane) if direct else rest - 1)

        if direct:
            for part in range(chunk_count):
                for t in range(len(plane)):
                    plane_copy(b, g, t, part).start()
            return
        for t in range(1, rest):
            rs1_copy(b, g, t).start()

    def rs2(b, g):
        for t in range(1, rest):
            rs1_copy(b, g, t).wait_recv()

        @pl.loop(0, rest * first)
        def _(p):
            here = dig_three * rest * first + p
            total = stage[g][b, core, here].astype(F32)
            for t in range(1, rest):
                total = total + r1[g][t - 1, p].astype(F32)
            stage[g][b, core, here] = total.astype(stage[g].dtype)

        for t in range(1, rest):
            @pl.when(b == 1)
            def _():
                pl.semaphore_signal(
                    credit.at[1, g], inc=1, device_id=peer_three(t), device_id_type=pl.DeviceIdType.MESH
                )

            rs2_copy(b, g, t).start()

    def rs3_send(b, g, part):
        def here(digit):
            return (digit >= chunk_size * part) & (digit < chunk_size * (part + 1))

        for t in range(1, first):
            @pl.when(here((dig_a + t) % first))
            def _():
                rs3_copy(b, g, t).start()

        @pl.when(here(dig_a) & (core != b))
        def _():
            rs3_copy(b, g, 0).start()

    def rs3_part(b, g, part):
        for t in range(len(plane)):
            plane_copy(b, g, t, part).wait_recv()

        @pl.loop(chunk_size * part, chunk_size * (part + 1))
        def _(p):
            here = (dig_three * rest + dig_two) * first + p
            total = stage[g][b, core, here].astype(F32)
            for t in range(len(plane)):
                total = total + r1[g][t, p].astype(F32)
            stage[g][b, core, here] = total.astype(stage[g].dtype)

        rs3_send(b, g, part)

    def rs3_first(b, g):
        rs3_part(b, g, 0)

    def rs3_rest(b, g):
        for part in range(1, chunk_count):
            rs3_part(b, g, part)

    def rs3(b, g):
        if g in (ATT, TAB):
            for part in range(chunk_count):
                rs3_part(b, g, part)

            @pl.when(b == 1)
            def _():
                for three, two in plane:
                    pl.semaphore_signal(
                        credit.at[1, g], inc=1, device_id=peer_plane(three, two),
                        device_id_type=pl.DeviceIdType.MESH,
                    )

            return
        for t in range(1, rest):
            rs2_copy(b, g, t).wait_recv()

        @pl.loop(0, first)
        def _(p):
            here = (dig_three * rest + dig_two) * first + p
            total = stage[g][b, core, here].astype(F32)
            for t in range(1, rest):
                total = total + r2[g][b, t - 1, p].astype(F32)
            stage[g][b, core, here] = total.astype(stage[g].dtype)

        for part in range(chunk_count):
            rs3_send(b, g, part)

    def rs4(b, g):
        @pl.when(core == b)
        def _():
            for own in (True, False):
                half = core if own else 1 - core
                begin = int(own)
                for t in range(begin, first):
                    ref = r3[g].at[half, t]
                    remote(ref, ref, rs3_s.at[at(b, g), t], rs3_r.at[g, half, t], sibling).wait_recv()
                total = stage[g][b, core, pos].astype(F32) if own else None
                for t in range(begin, first):
                    value = r3[g][half, t].astype(F32)
                    total = value if total is None else total + value
                final[g][half] = total

    def rs_sent(b, g):
        rs0_copy(b, g).wait_send()
        if g in (ATT, TAB):
            for part in range(chunk_count):
                for t in range(len(plane)):
                    plane_copy(b, g, t, part).wait_send()
        else:
            for t in range(1, rest):
                rs1_copy(b, g, t).wait_send()
                rs2_copy(b, g, t).wait_send()
        for t in range(1, first):
            rs3_copy(b, g, t).wait_send()

        @pl.when(core != b)
        def _():
            rs3_copy(b, g, 0).wait_send()

    def rows_of(i, images_too=1):
        return pl.ds(pl.multiple_of(i * rows, 16), images_too * rows)

    few = TOGETHER if slots % TOGETHER == 0 else 1
    many = TOGETHER_ROWS if slots % TOGETHER_ROWS == 0 else 1

    def step_rows(i, count):
        return rows_of(i * count, count)

    def ship_parts(kind, b, i):
        src, out = (io_one, io_two)[kind].at[i], out_far.at[kind, core, i]
        q = 2 * kind + b
        near = pltpu.make_async_copy(src, out, ship_s.at[q, i])
        far = remote(src, out, ship_s.at[q, i], ship_r.at[q, i], sibling)
        return near, far

    def ship(kind, b, i):
        near, far = ship_parts(kind, b, i)

        @pl.when(core == b)
        def _():
            near.start()

        @pl.when(core != b)
        def _():
            far.start()

    def shipped(kind, b, i):
        near, far = ship_parts(kind, b, i)

        @pl.when(core == b)
        def _():
            near.wait()

        @pl.when(core != b)
        def _():
            far.wait_send()

    def landed(kind, b, i):
        q = 2 * kind + b
        ref = out_far.at[kind, 1 - core, i]

        @pl.when(core == b)
        def _():
            remote(ref, ref, ship_s.at[q, i], ship_r.at[q, i], sibling).wait_recv()

    def live(i):
        return jnp.where(i < counts[0, core], 1.0, 0.0).astype(F32)

    def only_live(i, value, count):
        parts = [value[rows * m : rows * (m + 1)] * live(i * count + m) for m in range(count)]
        return jnp.concatenate(parts, axis=0)

    def coming(which, i):
        slot = (which * slots + i) % raw.shape[0]
        return pltpu.make_async_copy((images, cotangent)[which].at[i], raw.at[slot], in_s.at[which, i])

    def take_in(which, i):
        coming(which, i).wait()
        both = raw[(which * slots + i) % raw.shape[0]].astype(F32)
        (io_one, io_two)[which][i] = jnp.where(core == 0, both[:, 0, :], both[:, 1, :]).astype(LOW)

    def weave(todo):
        ring = raw.shape[0]
        count = 2 * slots

        def fetch(t, m):
            source = out_far.at[t // slots, m, t % slots]
            return pltpu.make_async_copy(source, io_one.at[2 * (t % ring) + m], weave_in.at[m, t])

        def leave(t):
            return pltpu.make_async_copy(raw.at[t % ring], woven.at[t // slots, t % slots], weave_out.at[t])

        for t in range(ring - 1):
            for m in range(2):
                fetch(t, m).start()

        @pl.loop(0, count)
        def _(t):
            for when, act in todo.items():
                @pl.when(t == when)
                def _():
                    act()

            @pl.when(t + ring - 1 < count)
            def _():
                for m in range(2):
                    fetch(t + ring - 1, m).start()

            @pl.when(t >= ring)
            def _():
                leave(t - ring).wait()

            for m in range(2):
                fetch(t, m).wait()
                raw[t % ring, :, m, :] = io_one[2 * (t % ring) + m]
            leave(t).start()

        for t in range(count - ring, count):
            leave(t).wait()

    def far_copy(which, i, back):
        near, far = ((hid, hid_far), (slope, slope_far))[which]
        near, far = near.at[rows_of(i)], far.at[rows_of(i)]
        src, dst = (far, near) if back else (near, far)
        return pltpu.make_async_copy(src, dst, far_s.at[2 * int(back) + which, i])

    pairs = width // 128
    scale = head_dim ** -0.5
    lane = lax.broadcasted_iota(jnp.int32, (1, 128), 1)
    half_low = [(lane < head_dim).astype(LOW), (lane >= head_dim).astype(LOW)]
    half_f = [(lane < head_dim).astype(F32), (lane >= head_dim).astype(F32)]
    token = lax.broadcasted_iota(jnp.int32, (rows, 128), 0) < length
    half_valid = [jnp.where(token, half_f[j], 0.0).astype(LOW) for j in range(2)]
    valid_lanes = jnp.where(lax.broadcasted_iota(jnp.int32, (1, rows), 1) < length, 1.0, 0.0).astype(F32)
    spare = -rows % 128
    chunk = 2 * width
    chunks = ff // chunk

    def vec(s, r):
        return table[s, r : r + 1, :]

    def up_bias(s, c):
        begin = c * chunk
        row, col = begin // width, begin % width
        if col + chunk <= width:
            return table[s, BU + row : BU + row + 1, col : col + chunk]
        a = table[s, BU + row : BU + row + 1, col:width]
        b = table[s, BU + row + 1 : BU + row + 2, 0 : chunk - (width - col)]
        return jnp.concatenate([a, b], axis=1)

    def add_vec(s, r, value):
        gtable[s, r : r + 1, :] += value

    def attn_forward(s, x, hat, i):
        rd = step_rows(i, few)
        nrm_ref, qkv_ref, prob_ref, ctx_ref = nrm1.at[s], qkv.at[s], prob.at[s], ctx.at[s]
        nrm = (hat * vec(s, G1) + vec(s, S1)).astype(LOW)
        nrm_ref[rd, :] = nrm
        mixed = mm(nrm, wqkv[s])
        q = (mixed[:, 0:width] + vec(s, BQ)).astype(LOW)
        k = mixed[:, width : 2 * width].astype(LOW)
        v = (mixed[:, 2 * width :] + vec(s, BV)).astype(LOW)
        qkv_ref[rd, 0:width] = q
        qkv_ref[rd, width : 2 * width] = k
        qkv_ref[rd, 2 * width :] = v
        images_out = []
        for m in range(few):
            mine = slice(rows * m, rows * (m + 1))
            parts = []
            for p in range(pairs):
                cols = slice(128 * p, 128 * p + 128)
                weights, sides = [], []
                for j in range(2):
                    keys = k[mine, cols] * half_low[j]
                    keys = jnp.concatenate([keys, keys[rows - spare :]], axis=0)
                    scores = mm_right(q[mine, cols], keys)
                    top = jnp.max(scores, axis=-1, keepdims=True)
                    e = jnp.exp2((scores - top) * (scale * 1.4426950408889634)).astype(LOW)
                    prob_ref[i * few + m, 2 * p + j] = e[:, :rows]
                    weights.append(e)
                    sides.append(jnp.concatenate([v[mine, cols] * half_valid[j], half_valid[j]], axis=1))
                    sides.append(jnp.zeros((spare, 256), LOW))
                total = mm(jnp.concatenate(weights, axis=1), jnp.concatenate(sides, axis=0))
                over = 1.0 / total[:, 128:]
                overs[s, rows_of(i * few + m), cols] = over.astype(LOW)
                parts.append((total[:, :128] * over).astype(LOW))
            images_out.append(jnp.concatenate(parts, axis=1))
        context = jnp.concatenate(images_out, axis=0)
        ctx_ref[rd, :] = context
        return x + mm(context, wout[s]) + vec(s, BO)

    def ff_forward(s, after, rd):
        hat, rstd, _ = normalize(after)
        hat2[s, rd, :] = hat.astype(LOW)
        nrm = (hat * vec(s, G2) + vec(s, S2)).astype(LOW)
        total = after + vec(s, BD)
        for c in range(chunks):
            cols = slice(chunk * c, chunk * c + chunk)
            pre = mm(nrm, wup[s, :, cols]) + up_bias(s, c)
            phi, slo = normal_parts(pre)
            h = (pre * phi).astype(LOW)
            hid[rd, cols] = h
            slope[rd, cols] = slo.astype(LOW)
            total = total + mm(h, wdown[s, cols, :])
        return total, rstd

    def ff_backward(s, g, rd, rstd):
        g_low = g.astype(LOW)
        add_vec(s, BD, colsum(g_low.astype(F32)))
        d_nrm = None
        for c in range(chunks):
            cols = slice(chunk * c, chunk * c + chunk)
            d_hid = mm_right(g_low, wdown[s, cols, :])
            d_pre = (d_hid * slope[rd, cols].astype(F32)).astype(LOW)
            slope[rd, cols] = d_pre
            part = mm_right(d_pre, wup[s, :, cols])
            d_nrm = part if d_nrm is None else d_nrm + part
        hat = hat2[s, rd, :].astype(F32)
        add_vec(s, G2, colsum(d_nrm * hat))
        add_vec(s, S2, colsum(d_nrm))
        d_after = g + normalize_back(d_nrm * vec(s, G2), hat, rstd)
        low = d_after.astype(LOW)
        dal[rd, :] = low
        return d_after

    def attn_backward(s, i):
        qkv_ref, prob_ref, ctx_ref = qkv.at[s], prob.at[s], ctx.at[s]
        rd = step_rows(i, few)
        d_context = mm_right(dal[rd, :], wout[s])
        d_context = (d_context * overs[s, rd, :].astype(F32)).astype(LOW)
        for m in range(few):
            rd = rows_of(i * few + m)
            d_ctx = d_context[rows * m : rows * (m + 1)]
            dq, dk, dv = [], [], []
            for p in range(pairs):
                cols = slice(128 * p, 128 * p + 128)
                q = qkv_ref[rd, 128 * p : 128 * p + 128]
                k = qkv_ref[rd, width + 128 * p : width + 128 * p + 128]
                v = qkv_ref[rd, 2 * width + 128 * p : 2 * width + 128 * p + 128]
                dc = d_ctx[:, cols]
                both = dc.astype(F32) * ctx_ref[rd, cols].astype(F32)
                q_t, dc_t = q.T, dc.T
                to_q, to_k, to_v = None, [], []
                for j in range(2):
                    e = prob_ref[i * few + m, 2 * p + j]
                    delta = jnp.sum(both * half_f[j], axis=-1, keepdims=True)
                    d_prob = mm_right(dc, v * half_low[j])
                    ds = (e.astype(F32) * (d_prob - delta)).astype(LOW)
                    part = mm(ds, k * half_valid[j])
                    to_q = part if to_q is None else to_q + part
                    head = slice(head_dim * j, head_dim * (j + 1))
                    to_k.append(mm(q_t[head], ds))
                    to_v.append(mm(dc_t[head], e))
                dq.append((to_q * scale).astype(LOW))
                dk.append((jnp.concatenate(to_k, axis=0) * (valid_lanes * scale)).astype(LOW).T)
                dv.append((jnp.concatenate(to_v, axis=0) * valid_lanes).astype(LOW).T)
            d_mixed = jnp.concatenate(dq + dk + dv, axis=1)
            qkv_ref[rd, :] = d_mixed

    def input_backward(s, d_after, rd, x, mean, rstd):
        d_nrm = mm_right(qkv[s, rd, :], wqkv[s])
        hat = (x - mean) * rstd
        add_vec(s, G1, colsum(d_nrm * hat))
        add_vec(s, S1, colsum(d_nrm))
        return d_after + normalize_back(d_nrm * vec(s, G1), hat, rstd)

    def grads_down(s):
        left_t[0:width, :] = low_g[...].T

        @pl.loop(0, 2)
        def _(c):
            cols = pl.ds(pl.multiple_of(c * 2 * width, 128), 2 * width)
            block = mm(left_t[0:width, :], hid[:, cols]).T
            for i in range(n // 2):
                for half in range(2):
                    begin = 4 * unit * i + 2 * unit * half
                    s_d[s, half, place(half, c * (n // 2) + i)] = block[begin : begin + 2 * unit].astype(LOW)

    def pair_out(ref, s, half, one, two):
        for j in range(n):
            down = slice(unit * j, unit * (j + 1))
            piece = jnp.concatenate([one[down], two[down]], axis=0).astype(LOW)
            ref[s, half, place(half, j)] = piece

    def grads_up(s):
        left_t[0:width, :] = (hat2[s].astype(F32) * vec(s, G2) + vec(s, S2)).astype(LOW).T
        for half in range(2):
            both = mm(left_t[...], slope[:, 2 * half * width : 2 * (half + 1) * width])
            pair_out(s_u, s, half, both[:, :width], both[:, width:])
            gtable[s, BU + 2 * half : BU + 2 * half + 1, :] = both[width : width + 1, :width]
            gtable[s, BU + 2 * half + 1 : BU + 2 * half + 2, :] = both[width : width + 1, width:]

    def grads_attn(s):
        mix_s = qkv.at[s]
        left_t[0:width, :] = ctx[s].T
        four = mm(left_t[...], dal[...])
        left_t[0:width, :] = nrm1[s].T
        three = mm(left_t[...], mix_s[:, 2 * width :])
        pair_out(s_a, s, 1, three, four)
        both = mm(left_t[...], mix_s[:, 0 : 2 * width])
        pair_out(s_a, s, 0, both[:, :width], both[:, width:])
        for row, sums in ((BO, four), (BV, three), (BQ, both)):
            gtable[s, row : row + 1, :] = sums[width : width + 1, :width]

    barrier = pltpu.get_barrier_semaphore()
    greeted = [sibling]
    greeted += [{"section": half, **peer_first(t)} for t in range(1, first) for half in range(2)]
    greeted += [peer_plane(three, two) for three, two in plane]
    for device in greeted:
        pl.semaphore_signal(barrier, inc=1, device_id=device, device_id_type=pl.DeviceIdType.MESH)
    pack_own()
    pl.semaphore_wait(barrier, len(greeted))

    def run(*todo):
        for f, b, g in todo:
            f(b, g)

    def events(i, table_of):
        for when, todo in table_of.items():
            @pl.when(i == when)
            def _():
                run(*todo)

    def both(f, b, g):
        return [(f, b, g), (f, b, TAB)]

    def take(i, m):
        return pl.ds(pl.multiple_of((i * many + m) * rows, 16), length)

    ahead = raw.shape[0]
    run(*both(ag1, 0, ATT))
    for i in range(ahead):
        coming(0, i).start()
    fill_repeats()
    gtable[...] = jnp.zeros_like(gtable)
    left_t[width:, :] = jnp.ones((16, left_t.shape[1]), LOW)
    low_g[...] = jnp.zeros_like(low_g)
    xs[0] = jnp.zeros_like(low_g)

    @pl.loop(0, slots)
    def images_in(i):
        take_in(0, i)

        @pl.when(i + ahead < slots)
        def _():
            coming(0, i + ahead).start()

        @pl.when(i + ahead >= slots)
        def _():
            coming(1, i + ahead - slots).start()

        @pl.when(i == 4)
        def _():
            run((ag1, 0, UP))

    run(*both(ag2, 0, ATT), (ag1, 0, DOWN), *both(ag1, 1, ATT))

    def statistic(s, rd, which):
        return jnp.where(s == 0, rstds[rd, which : which + 1], rstds[rd, 3 + which : 4 + which])

    def first_norm(s, rd, x):
        hat, rstd, mean = normalize(x)
        after_ref[rd, :] = hat
        rstds[rd, 3 * s : 3 * s + 1] = rstd
        rstds[rd, 3 * s + 2 : 3 * s + 3] = mean

    @pl.loop(0, slots // many)
    def norm_one(i):
        for m in range(many):
            xs[0, take(i, m), :] = io_one[i * many + m]
        rd = step_rows(i, many)
        x = xs[0, rd, :].astype(F32)
        token_rows = lax.broadcasted_iota(jnp.int32, (rows, width), 0) < length
        parts = [x[rows * m : rows * (m + 1)] for m in range(many)]
        x = jnp.concatenate([jnp.where(token_rows, part, part[0:1]) for part in parts], axis=0)
        xs[0, rd, :] = x.astype(LOW)
        first_norm(0, rd, x)

    run(*both(ag3, 0, ATT), (ag2, 0, UP), (ag1, 1, UP), (ag1, 1, DOWN))

    @pl.loop(0, slots)
    def cotangents_in(i):
        take_in(1, i)

        @pl.when(i + ahead < slots)
        def _():
            coming(1, i + ahead).start()

    run(*both(ag4, 0, ATT), (ag2, 0, DOWN), (ag3, 0, UP), *both(ag5, 0, ATT))

    @pl.loop(0, 2)
    def forward(s):
        @pl.loop(0, slots // few)
        def attention(i):
            @pl.when(s == 0)
            def _():
                events(i, {
                    0: [(ag3, 0, DOWN), *both(ag2, 1, ATT)], 1: [(ag4, 0, UP), (ag2, 1, UP)], 2: [(ag4, 0, DOWN)],
                })

            @pl.when(s == 1)
            def _():
                events(i, {1: [(ag4, 1, UP)], 2: [(ag4, 1, DOWN)]})

            rd = step_rows(i, few)
            after_ref[rd, :] = attn_forward(s, xs[s, rd, :].astype(F32), after_ref[rd, :], i)

        @pl.when(s == 0)
        def _():
            run(*both(ag3, 1, ATT), (ag5, 0, UP), (ag5, 0, DOWN))

        @pl.when(s == 1)
        def _():
            run((ag5, 1, UP), (ag5, 1, DOWN))

        @pl.loop(0, slots // many)
        def feed_forward(i):
            @pl.when(s == 0)
            def _():
                events(i, {0: [(ag2, 1, DOWN), (ag3, 1, UP)], 2: both(ag4, 1, ATT)})

            rd = step_rows(i, many)

            @pl.when(s == 1)
            def _():
                for m in range(many):
                    far_copy(0, i * many + m, False).wait()
                    far_copy(1, i * many + m, False).wait()
                    shipped(0, 0, i * many + m)

            out, rstd2 = ff_forward(s, after_ref[rd, :], rd)
            for block in range(2):
                @pl.when(s == block)
                def _():
                    rstds[rd, 3 * block + 1 : 3 * block + 2] = rstd2

            out = only_live(i, out, many)
            for m in range(many):
                io_one[i * many + m] = out[rows * m : rows * m + length].astype(LOW)
                ship(0, s, i * many + m)

            @pl.when(s == 0)
            def _():
                for m in range(many):
                    far_copy(0, i * many + m, False).start()
                    far_copy(1, i * many + m, False).start()
                low = out.astype(LOW)
                xs[1, rd, :] = low
                first_norm(1, rd, low.astype(F32))

        @pl.when(s == 0)
        def _():
            run((ag3, 1, DOWN), *both(ag5, 1, ATT))

    for b in range(2):
        for g in groups:
            ag_sent(b, g)

    @pl.loop(0, 2)
    def backward(turn):
        s = 1 - turn

        @pl.loop(0, slots // many)
        def feed_forward(i):
            @pl.when(s == 0)
            def _():
                events(i, {1: [*both(rs1, 1, ATT), (rs3, 1, DOWN)], 2: [(rs3, 1, UP)]})
                for m in range(many):
                    far_copy(1, i * many + m, True).wait()

            rd = step_rows(i, many)
            for m in range(many):
                g = live(i * many + m) * io_two[i * many + m].astype(F32)
                low_g[take(i, m), :] = g.astype(LOW)
            after_ref[rd, :] = ff_backward(s, low_g[rd, :].astype(F32), rd, statistic(s, rd, 1))

        @pl.when(s == 0)
        def _():
            for i in range(slots):
                far_copy(0, i, True).wait()

        grads_down(s)
        run((rs0, s, DOWN))

        @pl.when(s == 1)
        def _():
            for i in range(slots):
                far_copy(0, i, True).start()

        grads_up(s)
        run((rs0, s, UP))

        @pl.when(s == 1)
        def _():
            for i in range(slots):
                far_copy(1, i, True).start()

        @pl.loop(0, slots // few)
        def attention(i):
            @pl.when(s == 0)
            def _():
                events(i, {1: both(rs3, 1, ATT)})

            events(i, {0: [(rs1, s, DOWN)], 1: [(rs1, s, UP)]})
            attn_backward(s, i)

        run((rs2, s, DOWN))

        @pl.when(s == 0)
        def _():
            run(*both(rs4, 1, ATT), (rs4, 1, DOWN), (rs4, 1, UP))

        grads_attn(s)
        run((rs0, s, ATT))

        @pl.loop(0, slots // many)
        def to_input(i):
            rd = step_rows(i, many)
            x = xs[s, rd, :].astype(F32)
            d_in = input_backward(s, after_ref[rd, :], rd, x, statistic(s, rd, 2), statistic(s, rd, 0))
            for m in range(many):
                @pl.when(s == 0)
                def _():
                    shipped(1, 1, i * many + m)

                io_two[i * many + m] = d_in[rows * m : rows * m + length].astype(LOW)
                ship(1, s, i * many + m)

        table_out(s)
        run((rs0, s, TAB), (rs2, s, UP))

    def sent_and_landed(kind):
        @pl.loop(0, slots)
        def _(i):
            shipped(kind, 1 - kind, i)
            for b in range(2):
                landed(kind, b, i)

    sent_and_landed(0)
    weave({
        1: lambda: run(*both(rs1, 0, ATT), (rs3, 0, DOWN)),
        3: lambda: run((rs3, 0, UP)),
        slots - raw.shape[0] + 1: lambda: sent_and_landed(1),
        slots: lambda: run(*both(rs3_first, 0, ATT)),
        slots + 3: lambda: run(*both(rs3_rest, 0, ATT), (rs4, 0, DOWN), (rs4, 0, UP)),
    })
    run(*both(rs4, 0, ATT))
    for b in range(2):
        for g in groups:
            rs_sent(b, g)


def output_kernel(
    woven, far_a, far_u, far_d, far_t, o_acts, o_ings, o_g1, o_s1, o_qkv, o_qv, o_out, o_bo, o_g2, o_s2, o_up, o_bu, o_down, o_bd,
    passing, f_a, f_u, f_d, f_t, sems, grad_sems
):
    coming = [
        pltpu.make_async_copy(source, target, grad_sems.at[i])
        for i, (source, target) in enumerate(((far_a, f_a), (far_u, f_u), (far_d, f_d), (far_t, f_t)))
    ]
    for copy in coming:
        copy.start()
    arriving, leaving = [], []
    for which, target in enumerate((o_acts, o_ings)):
        for i in range(target.shape[0]):
            arriving.append(pltpu.make_async_copy(woven.at[which, i], passing.at[which, i], sems.at[0, which, i]))
            leaving.append(pltpu.make_async_copy(passing.at[which, i], target.at[i], sems.at[1, which, i]))
    for copy in arriving:
        copy.start()
    for one, two in zip(arriving, leaving):
        one.wait()
        two.start()
    for copy in coming:
        copy.wait()
    unit, width = o_out.shape[1:]
    for half in range(2):
        o_down[0, 2 * unit * half : 2 * unit * (half + 1), :] = f_d[half]
        for sub in range(2):
            part = 2 * half + sub
            cols = slice(part * width, (part + 1) * width)
            o_up[0, :, cols] = f_u[half, unit * sub : unit * (sub + 1), :]
            piece = f_a[half, unit * sub : unit * (sub + 1), :]
            if part == 3:
                o_out[0] = piece
            else:
                o_qkv[0, :, cols] = piece
    begin = 0
    for out in (o_g1, o_s1, o_bo, o_g2, o_s2, o_bd, o_qv):
        part = out.shape[1]
        out[...] = f_t[0, :, begin : begin + part]
        begin += part
    o_bu[...] = f_t[1, :, 0 : o_bu.shape[1]]
    for copy in leaving:
        copy.wait()


def local(
    images, cotangent, counts,
    ln1_gain, ln1_bias, w_qkv, b_qv, w_out, b_out, ln2_gain, ln2_bias, w_up, b_up, w_down, b_down,
):
    micro_count, slots, length, width = images.shape
    ff = w_up.shape[2]
    rows = -(-length // 16) * 16
    n = lax.axis_size("fsdp")
    unit = width // n
    first, rest = radices(n)
    total = slots * rows
    head_dim = width // HEADS

    def vm(*shape, kind=LOW):
        return pltpu.VMEM(shape, kind)

    tall = [(2 * unit, LOW)] * 3 + [(1, F32)]
    dma = lambda *shape: pltpu.SemaphoreType.DMA(shape)
    outs = [((2, slots, length, 2, width), LOW)]
    outs += [((2, r, width), F32) for r, _ in tall] + [((total, ff), LOW)] * 2 + [((2, 2, slots, length, width), LOW)]
    scratch = [
        vm(2, total, width), vm(3, length, 2, width), vm(slots, length, width), vm(slots, length, width),
        *[vm(2, r, width, kind=kind) for r, kind in tall],
        vm(2, width, 3 * width), vm(2, width, width), vm(2, width, ff), vm(2, ff, width),
        vm(2, TABLE, width, kind=F32), vm(2, TABLE, width, kind=F32),
        vm(unit, width), vm(2 * unit, 2 * width), vm(4 * unit, 4 * width),
        vm(total, width, kind=F32), vm(2, total, width), vm(2, total, 3 * width), vm(2, slots, HEADS, rows, rows),
        vm(2, total, width),
        vm(2, total, width), vm(2, total, width), vm(total, 6, kind=F32),
        vm(total, ff), vm(total, ff), vm(total, width), vm(total, width), vm(width + 16, total),
    ]
    scratch += [vm(2, 2, n, r, width, kind=kind) for r, kind in tall]
    scratch += [vm(n, r, width, kind=kind) for r, kind in tall]
    plane = rest * rest - 1
    for g, (r, kind) in enumerate(tall):
        direct = g in (ATT, TAB)
        scratch.append(vm(*((plane, first) if direct else (rest - 1, rest * first)), r, width, kind=kind))
    scratch += [vm(2, rest - 1, first, *tall[g][:1], width) for g in (UP, DOWN)]
    scratch += [vm(2, first, r, width, kind=kind) for r, kind in tall]
    scratch += [dma(2, slots), dma(2, 2 * slots), dma(2 * slots), dma(4, slots), dma(4, slots), dma(4, slots)]
    scratch += [dma(4, 2, first), dma(8, first)] + [dma(8, rest - 1)] * 4 + [dma(8, rest)] * 2
    scratch += [dma(8)] * 2 + [dma(8, plane, 2)] * 2 + [dma(8, rest - 1)] * 2 + [dma(8, first), dma(4, 2, first)]
    scratch += [pltpu.SemaphoreType.REGULAR((2, 4))]
    dims = (slots, length, rows, width, ff, head_dim, n)
    vmem = pl.BlockSpec(memory_space=pltpu.VMEM)
    hbm = pl.BlockSpec(memory_space=pltpu.HBM)
    woven, f_a, f_u, f_d, f_t, *_ = pl.pallas_call(
        functools.partial(whole_kernel, dims),
        out_shape=[jax.ShapeDtypeStruct(*o) for o in outs],
        in_specs=[hbm, hbm, pl.BlockSpec(memory_space=pltpu.SMEM)] + [vmem] * 12,
        out_specs=[hbm] + [vmem] * 4 + [hbm] * 3,
        scratch_shapes=scratch,
        compiler_params=pltpu.CompilerParams(
            vmem_limit_bytes=(64 << 20) - (96 << 10), collective_id=0, has_side_effects=True
        ),
    )(
        images.transpose(1, 2, 0, 3), cotangent.transpose(1, 2, 0, 3), counts.T, ln1_gain, ln1_bias, b_out, ln2_gain, ln2_bias, b_down, b_qv, b_up,
        w_qkv, w_out, w_up, w_down,
    )

    params = (
        ln1_gain, ln1_bias, w_qkv, b_qv, w_out, b_out, ln2_gain, ln2_bias, w_up, b_up, w_down, b_down
    )
    acts, ings, *grads = pl.pallas_call(
        output_kernel,
        out_shape=[jax.ShapeDtypeStruct(woven.shape[1:], LOW)] * 2
        + [jax.ShapeDtypeStruct(p.shape, F32) for p in params],
        in_specs=[hbm] * 5,
        out_specs=[hbm] * 2 + [vmem] * len(params),
        scratch_shapes=[
            vm(2, slots, length, 2, width), *[vm(2, r, width, kind=F32) for r, _ in tall], dma(2, 2, slots), dma(4)
        ],
        compiler_params=pltpu.CompilerParams(vmem_limit_bytes=(64 << 20) - (96 << 10)),
    )(woven, f_a, f_u, f_d, f_t)

    def as_given(value):
        return value.transpose(2, 0, 1, 3)[None]

    return (as_given(acts), as_given(ings), *grads)


def solution(mesh):
    split = P("section", "fsdp")
    cube = P("section", "fsdp", None)
    image = P(None, "fsdp", None, None)
    result = P("section", None, "fsdp", None, None)
    params = (split, split, cube, split, cube, split, split, split, cube, split, cube, split)
    return jax.shard_map(
        local,
        mesh=mesh,
        in_specs=(image, image, P(None, "fsdp")) + params,
        out_specs=(result, result) + params,
        check_vma=False,
    )
```
